32 devices in a mesh: comp: 2 (over y), gx: 4 (over x, core), gy: 4 (over z).
Axes of the slice: x: 2, y: 2, z: 4, core: 2. Of those that a mesh axis runs over, the one named last changes fastest.
Arguments:
- fields: float32 [2, 32, 128, 1024], P('comp', 'gx', 'gy'), may hold values from -6 to 6
- wet_cells: int32 [32, 1024], P('gx'), may hold values 0 or 1
- flux_weight: float32 [128], replicated, may hold values from -0.5 to 0.5
- variable_sea_response: float32 [128], replicated, may hold values from 0.3 to 1
- diffusivity: float32 [128], replicated, may hold values from 0.05 to 500
- a2o_source: int32 [4, 4, 32, 128], P('gx', 'gy'), may hold values from 0 to 8191, as said below
- a2o_target: int32 [4, 4, 32, 128], P('gx', 'gy'), may hold values from 0 to 8191, as said below
- a2o_count: int32 [4, 4], P('gx', 'gy'), may hold values from 8 to 32, as said below
- a2o_weight: bfloat16 [4, 4, 32, 128, 128], P('gx', 'gy'), may hold values from -0.5 to 1.5
- marine_air_input_index: int32 [4, 4, 32, 128], P('gx', 'gy'), may hold values from 0 to 8191, as said below
- marine_air_output_index: int32 [4, 4, 32, 128], P('gx', 'gy'), may hold values from 0 to 8191, as said below
- marine_air_piece_tally: int32 [4, 4], P('gx', 'gy'), may hold values from 8 to 32, as said below
- marine_air_piece_factor: bfloat16 [4, 4, 32, 128, 128], P('gx', 'gy'), may hold values from -0.5 to 1.5
Outputs:
- new_fields: float32 [2, 32, 128, 1024], P('comp', 'gx', 'gy')
The draws below stay inside these ranges and needn't reach their ends.
Inputs may be any that keep to these rules, and one draw needn't show every extreme that they name: `a2o_source`: within a block the indices are distinct. `a2o_target`: within a block the indices are distinct. `a2o_count`: some block group uses all 32 blocks. `marine_air_input_index`: within a block the indices are distinct. `marine_air_output_index`: within a block the indices are distinct. `marine_air_piece_tally`: some block group uses all 32 blocks.
All inputs are finite; a program needn't handle non-finite values. No bound on the sum of `wet_cells` on one device may be relied on, other than what follows from the above.
Results may differ from the reference program's by a relative error of at most 0.0024.
Values may be sent and summed in bfloat16 or wider, within the bound.
No kernel may reach another device: no remote copies, remote signals or barrier semaphores. Data moves between devices by JAX's collectives and lax.ppermute only.
A program may use at most 128 MiB of HBM per device.

```python
import math
import jax
import jax.numpy as jnp
from jax import lax

LOCAL_LINE_SPAN = 8
CH_DEV = 32
MESH_MERIDIANS = 1024
NB = 32
BLK = 128
MESH_PARALLELS = 32
NCH = 128
N_GX = 4
N_GY = 4


def block_layout(key, flavour):
    key = jax.random.fold_in(key, flavour)
    tiles_x = MESH_PARALLELS // LOCAL_LINE_SPAN
    tiles_y = NCH // CH_DEV
    cells = LOCAL_LINE_SPAN * MESH_MERIDIANS
    score_limit = 2 ** 31 // cells - 1
    cell_ids = jnp.arange(cells, dtype=jnp.int32)

    def pick(sub_key):
        raw_score = jax.random.randint(sub_key, (tiles_y, NB, cells), 0, score_limit, dtype=jnp.int32)
        distinct_score = raw_score * cells + cell_ids
        return lax.top_k(distinct_score, BLK)[1].astype(jnp.int32)

    def one_tile(tile_key):
        key_one, key_two = jax.random.split(tile_key)
        return (pick(key_one), pick(key_two))
    tile_keys = jax.random.split(key, tiles_x)
    source, target = lax.map(one_tile, tile_keys)
    return (source.astype(jnp.int32), target.astype(jnp.int32))


def count_draw(key, flavour):
    key = jax.random.fold_in(key, flavour)
    tiles_x = MESH_PARALLELS // LOCAL_LINE_SPAN
    tiles_y = NCH // CH_DEV
    key_one, key_two = jax.random.split(key)
    counts = jax.random.randint(key_one, (tiles_x * tiles_y,), NB // 4, NB + 1)
    full_tile = jax.random.randint(key_two, (), 0, tiles_x * tiles_y)
    flat_counts = jnp.where(jnp.arange(tiles_x * tiles_y, dtype=jnp.int32) == full_tile, NB, counts)
    return flat_counts.reshape(tiles_x, tiles_y).astype(jnp.int32)


def weight_draw(key, flavour):
    key = jax.random.fold_in(key, flavour)
    tiles_x = MESH_PARALLELS // LOCAL_LINE_SPAN
    tiles_y = NCH // CH_DEV
    key_one, key_two = jax.random.split(key)
    grid_shape = (tiles_x, tiles_y, NB, BLK, BLK)
    identity = jnp.eye(BLK, dtype=jnp.float32)
    diagonal = jax.random.uniform(key_one, grid_shape[:-1], minval=0.4, maxval=0.8)
    spread_part = jnp.clip(jax.random.normal(key_two, grid_shape), -3.0, 3.0) * (0.45 / math.sqrt(BLK))
    return (diagonal[..., None] * identity + spread_part).astype(jnp.bfloat16)


def draw_a2o_source(key, part):
    return block_layout(key, 1)[0]


def draw_a2o_target(key, part):
    return block_layout(key, 1)[1]


def draw_a2o_count(key, part):
    return count_draw(key, 3)


def draw_a2o_weight(key, part):
    return weight_draw(key, 5)


def draw_marine_air_input_index(key, part):
    return block_layout(key, 2)[0]


def draw_marine_air_output_index(key, part):
    return block_layout(key, 2)[1]


def draw_marine_air_piece_tally(key, part):
    return count_draw(key, 4)


def draw_marine_air_piece_factor(key, part):
    return weight_draw(key, 6)


def set_ends(entries, rng, low, largest):
    place = [jax.random.randint(jax.random.fold_in(rng, axis), (), 0, length) for axis, length in enumerate(entries.shape)]
    main_axis = entries.shape.index(max(entries.shape))
    beside = place[:main_axis] + [(place[main_axis] + 1) % entries.shape[main_axis]] + place[main_axis + 1:]
    return entries.at[tuple(place)].set(low).at[tuple(beside)].set(largest)


def shard_levels(own_key, dims, shards, least, top_value):
    loudness = 1.0
    for position, shards_of in shards:
        heights = jax.random.uniform(jax.random.fold_in(jax.random.fold_in(own_key, 6), position), (shards_of,), jnp.float32, least / len(shards), top_value / len(shards))
        loudness = loudness * jnp.repeat(jnp.exp(heights), dims[position] // shards_of).reshape((-1,) + (1,) * (len(dims) - 1 - position))
    return loudness


def gaussian(own_key, extent, deviation, most, cuts=(), held_as=jnp.bfloat16):
    array = deviation * jax.random.normal(own_key, extent, jnp.float32)
    if cuts:
        array = array * shard_levels(own_key, extent, cuts, -0.22, 0.18)
    return jnp.clip(array, -most, most).astype(held_as)


def setup_inputs(seed: int = 0) -> dict:
    keys = jax.random.split(jax.random.key(seed), 14)
    return {
        "fields": gaussian(keys[0], (2, MESH_PARALLELS, NCH, MESH_MERIDIANS), 1.0, 6.0, ((0, 2), (1, 4), (2, 4)), jnp.float32),
        "wet_cells": set_ends((jax.random.randint(keys[1], (MESH_PARALLELS, MESH_MERIDIANS), 0, 4) < 3).astype(jnp.int32), jax.random.fold_in(keys[1], 1), 0, 1),
        "flux_weight": gaussian(keys[2], (NCH,), NCH ** -0.5, 0.5, (), jnp.float32),
        "variable_sea_response": jnp.clip(jax.random.uniform(keys[3], (NCH,), jnp.float32, 0.3, 1.0), 0.3, 1.0),
        "diffusivity": jnp.clip(jnp.exp(jax.random.uniform(keys[4], (NCH,), jnp.float32, math.log(0.05), math.log(500.0))), 0.05, 500.0),
        "a2o_source": draw_a2o_source(jax.random.fold_in(keys[13], 71), 0),
        "a2o_target": draw_a2o_target(jax.random.fold_in(keys[13], 71), 0),
        "a2o_count": draw_a2o_count(jax.random.fold_in(keys[13], 71), 0),
        "a2o_weight": draw_a2o_weight(jax.random.fold_in(keys[13], 71), 0),
        "marine_air_input_index": draw_marine_air_input_index(jax.random.fold_in(keys[13], 71), 0),
        "marine_air_output_index": draw_marine_air_output_index(jax.random.fold_in(keys[13], 71), 0),
        "marine_air_piece_tally": draw_marine_air_piece_tally(jax.random.fold_in(keys[13], 71), 0),
        "marine_air_piece_factor": draw_marine_air_piece_factor(jax.random.fold_in(keys[13], 71), 0),
    }


exact_mode = lax.Precision.HIGHEST
spread_rate = 0.2
mixing_rate = 0.1
heat_gain = 0.5
salt_gain = -0.25


def fourier_tables(columns, groups_x, groups_y):
    per_group = columns // 2 // groups_x
    per_sub = per_group // groups_y
    column_ids = jnp.arange(columns, dtype=jnp.int32)
    block_id = column_ids // (2 * per_group)
    inside = column_ids % (2 * per_group)
    sub_id = inside // (2 * per_sub)
    within = inside % (2 * per_sub)
    part_id = within // per_sub
    wave_ids = block_id * per_group + sub_id * per_sub + within % per_sub
    longitude = jnp.arange(columns, dtype=jnp.int32)
    phase_ids = (longitude[:, None] * wave_ids[None, :]) % columns
    angles = phase_ids.astype(jnp.float32) * (2.0 * math.pi / columns)
    forward = jnp.where(part_id[None, :] == 0, jnp.cos(angles), jnp.sin(angles))
    col_weight = jnp.where(wave_ids == 0, 1.0, 2.0) / columns
    inverse = forward.T * col_weight[:, None]
    return forward, inverse, wave_ids


def sine_table(count):
    ordinal = jnp.arange(1, count + 1, dtype=jnp.int32)
    phase_ids = (ordinal[:, None] * ordinal[None, :]) % (2 * (count + 1))
    return jnp.sin(phase_ids.astype(jnp.float32) * (math.pi / (count + 1)))


def meridional_rates(count):
    ordinal = jnp.arange(1, count + 1, dtype=jnp.int32).astype(jnp.float32)
    sines_half = jnp.sin(ordinal * (math.pi / (2 * (count + 1))))
    return 4.0 * sines_half * sines_half


def zonal_rates(wave_ids, columns):
    sines_half = jnp.sin(wave_ids.astype(jnp.float32) * (math.pi / columns))
    return 4.0 * sines_half * sines_half


def combine_matrix_pieces(surfaces, source, target, count, weight):
    def one_row(inputs):
        surface_row, source_row, target_row, count_row, weight_row = inputs

        def one_tile(surface, source_ids, target_ids, used_count, block_weight):
            gathered = surface.astype(jnp.bfloat16)[source_ids].astype(jnp.float32)
            block_terms = jnp.einsum('bkl,bl->bk', block_weight.astype(jnp.float32), gathered, precision=exact_mode)
            in_use = jnp.arange(source_ids.shape[0], dtype=jnp.int32)[:, None] < used_count
            block_terms = jnp.where(in_use, block_terms, 0.0)
            return jnp.zeros(surface.shape, jnp.float32).at[target_ids.reshape(-1)].add(block_terms.reshape(-1))

        return jax.vmap(one_tile)(surface_row, source_row, target_row, count_row, weight_row)

    return lax.map(one_row, (surfaces, source, target, count, weight))


def shift_rows(values, downward):
    blank = jnp.zeros_like(values[:1])
    if downward:
        return jnp.concatenate([blank, values[:-1]], axis=0)
    return jnp.concatenate([values[1:], blank], axis=0)


def reference(fields, wet_cells, flux_weight, variable_sea_response, diffusivity, a2o_source, a2o_target, a2o_count, a2o_weight, marine_air_input_index, marine_air_output_index, marine_air_piece_tally, marine_air_piece_factor):
    atmosphere = fields[0]
    half_dev = CH_DEV // 2
    heat_flux = jnp.einsum('rcl,c->rl', atmosphere, flux_weight, precision=exact_mode)
    marine_top_layer = fields[1][:, 0, :]
    heat_tiles = jnp.broadcast_to(heat_flux.reshape(N_GX, 1, LOCAL_LINE_SPAN * MESH_MERIDIANS), (N_GX, N_GY, LOCAL_LINE_SPAN * MESH_MERIDIANS))
    sea_heat_patches = jnp.broadcast_to(marine_top_layer.reshape(N_GX, 1, LOCAL_LINE_SPAN * MESH_MERIDIANS), (N_GX, N_GY, LOCAL_LINE_SPAN * MESH_MERIDIANS))
    to_ocean = combine_matrix_pieces(heat_tiles, a2o_source, a2o_target, a2o_count, a2o_weight)
    remap_onto_air_mesh = combine_matrix_pieces(sea_heat_patches, marine_air_input_index, marine_air_output_index, marine_air_piece_tally, marine_air_piece_factor)
    sea_heat_driver = jnp.sum(remap_onto_air_mesh, axis=1).reshape(MESH_PARALLELS, MESH_MERIDIANS)
    ocean_heat = jnp.sum(to_ocean, axis=1).reshape(MESH_PARALLELS, MESH_MERIDIANS)

    forward, inverse, wave_ids = fourier_tables(MESH_MERIDIANS, N_GX, N_GY)
    sine_matrix = sine_table(MESH_PARALLELS)
    coeffs = jnp.einsum('rcl,lj->rcj', atmosphere, forward, precision=exact_mode)
    mode_values = jnp.einsum('kr,rcj->kcj', sine_matrix, coeffs, precision=exact_mode)
    decay_rate = meridional_rates(MESH_PARALLELS)[:, None, None] + zonal_rates(wave_ids, MESH_MERIDIANS)[None, None, :]
    mode_values = mode_values / (1.0 + diffusivity[None, :, None] * decay_rate)
    coeffs = jnp.einsum('kr,kcj->rcj', sine_matrix, mode_values, precision=exact_mode) * (2.0 / (MESH_PARALLELS + 1))
    harmonic_damping = jnp.einsum('rcj,jl->rcl', coeffs, inverse, precision=exact_mode)
    advanced_air_state = harmonic_damping + variable_sea_response[None, :, None] * sea_heat_driver[:, None, :]

    all_levels = N_GY * half_dev
    ocean_grid = fields[1].reshape(MESH_PARALLELS, N_GY, 2, half_dev, MESH_MERIDIANS).transpose(0, 2, 1, 3, 4).reshape(MESH_PARALLELS, 2, all_levels, MESH_MERIDIANS)
    wet_here = wet_cells.astype(jnp.float32)
    level_ids = jnp.arange(all_levels, dtype=jnp.int32)
    tracer_gain = jnp.stack([jnp.where(level_ids == 0, heat_gain, 0.0), jnp.where(level_ids == 0, salt_gain, 0.0)])
    wet_north = shift_rows(wet_here, True)[:, None, None, :]
    wet_south = shift_rows(wet_here, False)[:, None, None, :]
    wet_west = jnp.roll(wet_here, 1, axis=1)[:, None, None, :]
    wet_east = jnp.roll(wet_here, -1, axis=1)[:, None, None, :]
    wet_full = wet_here[:, None, None, :]
    for ocean_step in range(2):
        from_north = shift_rows(ocean_grid, True)
        from_south = shift_rows(ocean_grid, False)
        from_west = jnp.roll(ocean_grid, 1, axis=3)
        from_east = jnp.roll(ocean_grid, -1, axis=3)
        inflow = wet_north * (from_north - ocean_grid) + wet_south * (from_south - ocean_grid)
        inflow = inflow + wet_west * (from_west - ocean_grid) + wet_east * (from_east - ocean_grid)
        upper = jnp.concatenate([ocean_grid[:, :, :1], ocean_grid[:, :, :-1]], axis=2)
        lower = jnp.concatenate([ocean_grid[:, :, 1:], ocean_grid[:, :, -1:]], axis=2)
        vertical = upper + lower - 2.0 * ocean_grid
        ocean_grid = wet_full * (ocean_grid + spread_rate * (wet_full * inflow) + mixing_rate * vertical + tracer_gain[None, :, :, None] * ocean_heat[:, None, None, :])
    ocean_new = ocean_grid.reshape(MESH_PARALLELS, 2, N_GY, half_dev, MESH_MERIDIANS).transpose(0, 2, 1, 3, 4).reshape(MESH_PARALLELS, NCH, MESH_MERIDIANS)
    return jnp.stack([advanced_air_state, ocean_new])
```

```python
import functools

import jax
import jax.numpy as jnp
import numpy as np
from jax import lax
from jax.experimental import pallas as pl
from jax.experimental.pallas import tpu as pltpu
from jax.sharding import PartitionSpec as P

spread_rate = 0.2
mixing_rate = 0.1
heat_gain = 0.5
salt_gain = -0.25
LANES = 128
f32 = jnp.float32
bf16 = jnp.bfloat16


def fourier_tables(columns):
    waves = np.arange(columns // 2)
    phase = np.arange(columns)[:, None] * waves[None, :] % columns
    angles = phase * (2.0 * np.pi / columns)
    forward = np.concatenate([np.cos(angles), np.sin(angles)], axis=1)
    weight = np.where(np.arange(columns) % (columns // 2) == 0, 1.0, 2.0) / columns
    inverse = forward.T * weight[:, None]
    half_rates = 2.0 * np.sin(np.pi * waves / columns) ** 2
    return (
        jnp.asarray(forward.astype(np.float32), bf16),
        jnp.asarray(inverse.astype(np.float32), bf16),
        jnp.asarray(half_rates[None, :].astype(np.float32)),
    )


def chain_pairs(count, odd):
    return [(low, low + 1) for low in range(odd, count - 1, 2)]


def both_ways(pairs):
    return [p for a, b in pairs for p in ((a, b), (b, a))]


def channel_column(row, channels, first):
    n = row.shape[1]
    lane = lax.broadcasted_iota(jnp.int32, (channels, n), 1)
    sub = lax.broadcasted_iota(jnp.int32, (channels, n), 0)
    return jnp.sum(jnp.where(lane == sub + first, row, 0.0), axis=1, keepdims=True)


def to_tiles(surface):
    cols = surface.shape[1]
    return jnp.concatenate(
        [surface[:, k : k + LANES] for k in range(0, cols, LANES)], axis=0
    )


def from_tiles(tiles, rows):
    return jnp.concatenate(
        [tiles[k : k + rows] for k in range(0, tiles.shape[0], rows)], axis=1
    )


def surface_kernel(x_ref, flux_ref, s_ref, row_ref):
    _, rows, channels, columns = x_ref.shape
    col_group = lax.axis_index("gy")
    is_atmos = lax.axis_index("comp") == 0

    @pl.when(is_atmos)
    def _():
        weight = channel_column(flux_ref[...], channels, col_group * channels)
        for r in range(rows):
            row_ref[r : r + 1, :] = jnp.sum(x_ref[0, r] * weight, axis=0, keepdims=True)
        s_ref[...] = to_tiles(row_ref[...]).astype(bf16)

    @pl.when(jnp.logical_not(is_atmos))
    def _():
        gain = jnp.where(col_group == 0, 1.0, 0.0)
        for r in range(rows):
            row_ref[r : r + 1, :] = x_ref[0, r, 0:1, :] * gain
        s_ref[...] = to_tiles(row_ref[...]).astype(bf16)


def decay_terms(diff_column, half_rates):
    half = 0.5 / diff_column + half_rates
    sinh = jnp.sqrt(half * (half + 2.0))
    grow = 1.0 + half + sinh
    return 1.0 / grow, jnp.log(grow), sinh


def forward_kernel(
    groups_x, x_ref, wet_ref, diff_ref, rates_ref, table_ref, *refs, xor_masks
):
    msgs = len(xor_masks)
    y_ref, e1_ref, e3_ref, e2_ref, e4_ref = refs[:5]
    pq_ref = refs[5] if not xor_masks else None
    edge_ref = refs[-1]
    _, rows, channels, columns = x_ref.shape
    waves = columns // 2
    row_group = lax.axis_index("gx")
    col_group = lax.axis_index("gy")
    is_atmos = lax.axis_index("comp") == 0

    @pl.when(is_atmos)
    def _():
        step = 256
        flat = x_ref[0].astype(bf16).reshape(rows * channels, columns)
        for n in range(0, columns, step):
            part = jnp.dot(flat, table_ref[:, n : n + step], preferred_element_type=f32)
            y_ref[:, :, n : n + step] = part.reshape(rows, channels, step)
        diff = channel_column(diff_ref[...], channels, col_group * channels)
        total = rows * groups_x
        base = (row_group * rows).astype(f32)
        for n in range(0, waves, LANES):
            lam, alpha, _ = decay_terms(diff, rates_ref[:, n : n + LANES])
            lam2 = lam * lam
            low = jnp.exp(-2.0 * base * alpha)
            high = jnp.exp(-2.0 * (total - rows - base) * alpha)
            for part in (n, n + waves):
                power = low
                p = jnp.zeros((channels, LANES), f32)
                for r in range(rows):
                    power = power * lam2
                    p = lam * p + (1.0 - power) * y_ref[r, :, part : part + LANES]
                power = high
                q = jnp.zeros((channels, LANES), f32)
                for r in reversed(range(rows)):
                    power = power * lam2
                    q = lam * q + (1.0 - power) * y_ref[r, :, part : part + LANES]
                if xor_masks:
                    for mask, out in zip((1, 2, 3), (e1_ref, e2_ref, e3_ref)):
                        if mask in xor_masks:
                            upward = row_group < (row_group ^ mask)
                            out[0:channels, part : part + LANES] = jnp.where(
                                upward, p, q
                            ).astype(bf16)
                else:
                    pq_ref[0, :, part : part + LANES] = p.astype(bf16)
                    pq_ref[1, :, part : part + LANES] = q.astype(bf16)

    @pl.when(jnp.logical_not(is_atmos))
    def _():
        levels = channels // 2
        even_x = row_group % 2 == 0
        even_y = col_group % 2 == 0
        wet = wet_ref[...].astype(f32)
        wet = jnp.concatenate([wet, wet], axis=0).astype(bf16)
        lines = 2 * channels

        def put(out, bottom):
            @pl.when(bottom)
            def _():
                out[0:lines, :] = x_ref[0, rows - 2 :].reshape(lines, columns).astype(bf16)

            @pl.when(jnp.logical_not(bottom))
            def _():
                out[0:lines, :] = x_ref[0, :2].reshape(lines, columns).astype(bf16)

            out[lines : lines + 16, :] = wet

        put(e1_ref, even_x)
        put(e3_ref, jnp.logical_not(even_x))

        def put_edges(out, bottom):
            @pl.when(bottom)
            def _():
                for r in range(rows):
                    for t in range(2):
                        at = (r * 2 + t) * 2
                        c = t * levels + levels - 2
                        edge_ref[at : at + 2, :] = x_ref[0, r, c : c + 2, :]

            @pl.when(jnp.logical_not(bottom))
            def _():
                for r in range(rows):
                    for t in range(2):
                        at = (r * 2 + t) * 2
                        c = t * levels
                        edge_ref[at : at + 2, :] = x_ref[0, r, c : c + 2, :]

            out[0 : rows * 4, :] = edge_ref[...].astype(bf16)

        put_edges(e2_ref, even_y)
        put_edges(e4_ref, jnp.logical_not(even_y))


def regrid_kernel(n_msgs, *refs):
    msgs = refs[:n_msgs]
    (
        a_src, a_dst, a_count, a_weight, m_src, m_dst, m_count, m_weight,
        e1_ref, e3_ref, e2_in, e4_in,
        land_ref, e2_ref, e4_ref,
        weight_ref, hot_ref, gath_ref, val_ref, tail_ref, sem,
    ) = refs[n_msgs:]
    is_atmos = lax.axis_index("comp") == 0
    blocks, points = val_ref.shape
    cells = msgs[0].shape[0]
    rows = 8

    @pl.when(is_atmos)
    def _():
        pltpu.make_async_copy(m_weight.at[0, 0], weight_ref, sem).start()

    @pl.when(jnp.logical_not(is_atmos))
    def _():
        pltpu.make_async_copy(a_weight.at[0, 0], weight_ref, sem).start()

    src = jnp.where(is_atmos, m_src[0, 0], a_src[0, 0])
    dst = jnp.where(is_atmos, m_dst[0, 0], a_dst[0, 0])
    count = jnp.where(is_atmos, m_count[0, 0], a_count[0, 0])
    tiles = cells // rows

    def split(index):
        row = index // (tiles * LANES)
        tile = (index // LANES) % tiles
        return tile * rows + row, index % LANES

    src_row, src_lane = split(src)
    dst_row, dst_lane = split(dst)
    lane_iota = lax.broadcasted_iota(jnp.int32, (LANES, points), 0)
    row_iota = lax.broadcasted_iota(jnp.int32, (cells, points), 0)
    table = msgs[0][...].astype(f32)
    for m in msgs[1:]:
        table = table + m[...].astype(f32)
    table = table.astype(bf16)
    for b in range(blocks):
        hot = jnp.where(lane_iota == src_lane[b : b + 1], 1.0, 0.0).astype(bf16)
        picked = jnp.dot(table, hot, preferred_element_type=f32)
        picked = jnp.where(row_iota == src_row[b : b + 1], picked, 0.0)
        gath_ref[b : b + 1, :] = jnp.sum(picked, axis=0, keepdims=True)
    gathered = gath_ref[...].astype(bf16)

    @pl.when(is_atmos)
    def _():
        pltpu.make_async_copy(m_weight.at[0, 0], weight_ref, sem).wait()

    @pl.when(jnp.logical_not(is_atmos))
    def _():
        pltpu.make_async_copy(a_weight.at[0, 0], weight_ref, sem).wait()

    block_iota = lax.broadcasted_iota(jnp.int32, (blocks, points), 0)
    values = jnp.zeros((blocks, points), f32)
    for b in range(blocks):
        term = lax.dot_general(
            gathered, weight_ref[b], (((1,), (1,)), ((), ())), preferred_element_type=f32
        )
        values = jnp.where(block_iota == b, term, values)
    val_ref[...] = jnp.where(block_iota < count, values, 0.0)
    land = jnp.zeros((2 * cells, LANES), f32)
    for b in range(blocks):
        value = val_ref[b : b + 1, :]
        coarse = value.astype(bf16).astype(f32)
        fine = value - coarse
        mine = row_iota == dst_row[b : b + 1]
        both = jnp.concatenate(
            [jnp.where(mine, coarse, 0.0), jnp.where(mine, fine, 0.0)], axis=0
        ).astype(bf16)
        hot = jnp.where(lane_iota == dst_lane[b : b + 1], 1.0, 0.0).astype(bf16)
        land = land + lax.dot_general(
            both, hot, (((1,), (1,)), ((), ())), preferred_element_type=f32
        )
    land_ref[...] = land[:cells] + land[cells:]

    @pl.when(is_atmos)
    def _():
        e2_ref[...] = e2_in[...]
        e4_ref[...] = e4_in[...]

    @pl.when(jnp.logical_not(is_atmos))
    def _():
        row_group = lax.axis_index("gx")
        col_group = lax.axis_index("gy")
        own = e2_in.shape[0] - 16
        channels = (e1_ref.shape[0] - 16) // 2
        levels = channels // 2
        even_x = row_group % 2 == 0
        lower = jnp.where(
            even_x, e3_ref[channels : 2 * channels, :].astype(f32),
            e1_ref[channels : 2 * channels, :].astype(f32),
        )
        upper = jnp.where(
            even_x, e1_ref[0:channels, :].astype(f32), e3_ref[0:channels, :].astype(f32)
        )
        even_y = col_group % 2 == 0

        def fill(out, inn, bottom):
            for line, values in enumerate((lower, upper)):
                for t in range(2):
                    at = (line * 2 + t) * 2
                    c = t * levels
                    tail_ref[at : at + 2, :] = jnp.where(
                        bottom, values[c + levels - 2 : c + levels], values[c : c + 2]
                    )
            out[0:own, :] = inn[0:own, :]
            tail = tail_ref[...]
            out[own : own + 16, :] = jnp.concatenate([tail, tail], axis=0).astype(bf16)

        fill(e2_ref, e2_in, even_y)
        fill(e4_ref, e4_in, jnp.logical_not(even_y))


def final_kernel(groups_x, groups_y, n_land, xor_masks, *refs):
    (
        x_ref, wet_ref, diff_ref, gain_ref, rates_ref, table_ref, y_ref,
        e1_ref, e3_ref, e2_ref, e4_ref, hsum_ref, ha_ref, hb_ref,
    ) = refs[:14]
    coupling = (e1_ref, e2_ref, e3_ref)
    at = 14
    if not xor_masks:
        pin_ref, qin_ref = refs[14:16]
        at = 16
    out_ref, z_ref, zb_ref, t0_ref, t1_ref, w_ref, c_ref, h_ref = refs[at:]
    _, rows, channels, columns = x_ref.shape
    waves = columns // 2
    row_group = lax.axis_index("gx")
    col_group = lax.axis_index("gy")
    is_atmos = lax.axis_index("comp") == 0

    @pl.when(is_atmos)
    def _():
        diff = channel_column(diff_ref[...], channels, col_group * channels)
        total = rows * groups_x
        base = (row_group * rows).astype(f32)
        for n in range(0, waves, LANES):
            lam, alpha, sinh = decay_terms(diff, rates_ref[:, n : n + LANES])
            lam2 = lam * lam
            low = jnp.exp(-2.0 * base * alpha)
            high = jnp.exp(-2.0 * (total - rows - base) * alpha)
            scale = 1.0 / (
                2.0 * diff * sinh * (1.0 - jnp.exp(-2.0 * (total + 1) * alpha))
            )
            lows, highs = [], []
            power = low
            for r in range(rows):
                power = power * lam2
                lows.append(1.0 - power)
            power = high
            for r in range(rows):
                power = power * lam2
                highs.append((1.0 - power))
            highs = highs[::-1]
            for part in (n, n + waves):
                lanes = slice(part, part + LANES)
                if xor_masks:
                    pin = jnp.zeros((channels, LANES), f32)
                    qin = jnp.zeros((channels, LANES), f32)
                    for mask in xor_masks:
                        other = row_group ^ mask
                        gap = (jnp.abs(row_group - other) - 1) * rows
                        term = jnp.exp(-gap.astype(f32) * alpha)
                        term = term * coupling[mask - 1][0:channels, lanes].astype(f32)
                        pin = pin + jnp.where(other < row_group, term, 0.0)
                        qin = qin + jnp.where(other > row_group, term, 0.0)
                else:
                    pin = pin_ref[:, lanes]
                    qin = qin_ref[:, lanes]
                f = pin
                for r in range(rows):
                    f = lam * f + lows[r] * y_ref[r, :, lanes]
                    z_ref[r, :, 0:LANES] = highs[r] * f
                g = lam * qin
                for r in reversed(range(rows)):
                    z = scale * (z_ref[r, :, 0:LANES] + lows[r] * g)
                    zb_ref[r * channels : (r + 1) * channels, lanes] = z.astype(bf16)
                    g = lam * (g + highs[r] * y_ref[r, :, lanes])
        response = channel_column(gain_ref[...], channels, col_group * channels)
        forcing = from_tiles(hsum_ref[...], rows)
        step = 256
        for n in range(0, columns, step):
            part = jnp.dot(
                zb_ref[...], table_ref[:, n : n + step], preferred_element_type=f32
            ).reshape(rows, channels, step)
            for r in range(rows):
                out_ref[0, r, :, n : n + step] = (
                    part[r] + response * forcing[r : r + 1, n : n + step]
                )

    @pl.when(jnp.logical_not(is_atmos))
    def _():
        levels = channels // 2
        ring = levels + 8
        lines = 2 * channels
        even_x = row_group % 2 == 0
        even_y = col_group % 2 == 0
        first_x = row_group == 0
        last_x = row_group == groups_x - 1
        top = col_group == 0
        bottom = col_group == groups_y - 1

        m1 = e1_ref[lines : lines + 16, :].astype(f32)
        m3 = e3_ref[lines : lines + 16, :].astype(f32)
        below = jnp.where(even_x, m3, m1)[rows - 2 : rows]
        above = jnp.where(even_x, m1, m3)[0:2]
        w_ref[0:2, :] = jnp.where(first_x, 0.0, below)
        w_ref[2 : rows + 2, :] = wet_ref[...].astype(f32)
        w_ref[rows + 2 : rows + 4, :] = jnp.where(last_x, 0.0, above)

        surface = jnp.where(top, 1.0, 0.0)
        own = from_tiles(hsum_ref[...], rows)
        ha = from_tiles(ha_ref[...].astype(f32), rows)
        hb = from_tiles(hb_ref[...].astype(f32), rows)
        h_ref[0:1, :] = jnp.where(even_x, hb, ha)[rows - 1 : rows]
        h_ref[1 : rows + 1, :] = own
        h_ref[rows + 1 : rows + 2, :] = jnp.where(even_x, ha, hb)[0:1]

        span = rows + 2
        north = w_ref[0:span, :]
        here = w_ref[1 : span + 1, :]
        south = w_ref[2 : span + 2, :]
        west = pltpu.roll(here, 1, 1)
        east = pltpu.roll(here, columns - 1, 1)
        c_ref[0, 0:span, :] = here * (
            1.0 - 2.0 * mixing_rate - spread_rate * (north + south + west + east)
        )
        c_ref[1, 0:span, :] = spread_rate * here * north
        c_ref[2, 0:span, :] = spread_rate * here * south
        c_ref[3, 0:span, :] = spread_rate * here * west
        c_ref[4, 0:span, :] = spread_rate * here * east
        c_ref[5, 0:span, :] = mixing_rate * here
        h_ref[0:span, :] = surface * here * h_ref[0:span, :]

        e1 = e1_ref[0:lines, :].astype(f32)
        e3 = e3_ref[0:lines, :].astype(f32)
        below = jnp.where(even_x, e3, e1)
        above = jnp.where(even_x, e1, e3)
        for k in range(2):
            for t in range(2):
                c = k * channels + t * levels
                t0_ref[k, t, 0:levels, :] = below[c : c + levels]
                t0_ref[rows + 2 + k, t, 0:levels, :] = above[c : c + levels]
                t0_ref[k, t, levels:ring, :] = jnp.zeros((8, columns), f32)
                t0_ref[rows + 2 + k, t, levels:ring, :] = jnp.zeros((8, columns), f32)
        for r in range(rows):
            for t in range(2):
                t0_ref[r + 2, t, 0:levels, :] = x_ref[0, r, t * levels : (t + 1) * levels, :]
                t0_ref[r + 2, t, levels:ring, :] = jnp.zeros((8, columns), f32)
        e2 = e2_ref[...].astype(f32)
        e4 = e4_ref[...].astype(f32)
        before = jnp.where(even_y, e4, e2)
        after = jnp.where(even_y, e2, e4)
        for r in range(-1, rows + 1):
            place = {-1: rows, rows: rows + 1}.get(r, r)
            for t in range(2):
                k = (place * 2 + t) * 2
                t0_ref[r + 2, t, levels : levels + 2, :] = after[k : k + 2]
                t0_ref[r + 2, t, ring - 2 : ring, :] = before[k : k + 2]

        def close(ref, r):
            for t in range(2):
                ref[r, t, ring - 1 : ring, :] = jnp.where(
                    top, ref[r, t, 0:1, :], ref[r, t, ring - 1 : ring, :]
                )
                ref[r, t, levels : levels + 1, :] = jnp.where(
                    bottom, ref[r, t, levels - 1 : levels, :], ref[r, t, levels : levels + 1, :]
                )

        gains = (heat_gain, salt_gain)

        def advance(ref, r, t, coefs, size):
            whole = ref[r, t]
            up = pltpu.roll(whole, 1, 0)[:size]
            down = pltpu.roll(whole, ring - 1, 0)[:size]
            mid = whole[:size]
            total = coefs[0] * mid + coefs[5] * (up + down)
            total = total + coefs[1] * ref[r - 1, t, 0:size, :]
            total = total + coefs[2] * ref[r + 1, t, 0:size, :]
            total = total + coefs[3] * pltpu.roll(mid, 1, 1)
            return total + coefs[4] * pltpu.roll(mid, columns - 1, 1)

        def first(r, carry):
            coefs = [c_ref[k, pl.ds(r, 1), :] for k in range(6)]
            close(t0_ref, r + 1)
            heat = h_ref[pl.ds(r, 1), :]
            for t in range(2):
                t1_ref[r, t] = advance(t0_ref, r + 1, t, coefs, ring)
                t1_ref[r, t, 0:1, :] = t1_ref[r, t, 0:1, :] + gains[t] * heat
            close(t1_ref, r)
            return carry

        lax.fori_loop(0, span, first, 0)

        def second(r, carry):
            coefs = [c_ref[k, pl.ds(r, 1), :] for k in range(6)]
            heat = h_ref[pl.ds(r, 1), :]
            for t in range(2):
                c = t * levels
                out_ref[0, r - 1, c : c + levels, :] = advance(t1_ref, r, t, coefs, levels)
                out_ref[0, r - 1, c : c + 1, :] = (
                    out_ref[0, r - 1, c : c + 1, :] + gains[t] * heat
                )
            return carry

        lax.fori_loop(1, span - 1, second, 0)


def local(
    fields,
    wet_cells,
    flux_weight,
    variable_sea_response,
    diffusivity,
    a2o_source,
    a2o_target,
    a2o_count,
    a2o_weight,
    marine_air_input_index,
    marine_air_output_index,
    marine_air_piece_tally,
    marine_air_piece_factor,
):
    _, rows, channels, columns = fields.shape
    groups_x = lax.axis_size("gx")
    groups_y = lax.axis_size("gy")
    blocks, points = a2o_source.shape[2:]
    cells = rows * columns // LANES
    waves = columns // 2
    forward, inverse, half_rates = fourier_tables(columns)
    flux_row = flux_weight[None, :]
    gain_row = variable_sea_response[None, :]
    diff_row = diffusivity[None, :]
    xor_masks = tuple(range(1, groups_x)) if groups_x in (2, 4) else ()
    params = functools.partial(pltpu.CompilerParams, vmem_limit_bytes=40 * 2**20)
    vmem = pl.BlockSpec(memory_space=pltpu.VMEM)
    smem = pl.BlockSpec(memory_space=pltpu.SMEM)
    anywhere = pl.BlockSpec(memory_space=pl.ANY)

    def shape(dims, dtype):
        return jax.ShapeDtypeStruct(dims, dtype)

    partial_surface = pl.pallas_call(
        surface_kernel,
        out_shape=shape((cells, LANES), bf16),
        in_specs=[vmem, vmem],
        out_specs=vmem,
        scratch_shapes=[pltpu.VMEM((rows, columns), f32)],
        compiler_params=params(),
        name="surface_partials",
    )(fields, flux_row)
    surfaces = []
    for mask in range(groups_y):
        route = []
        for j in range(groups_y):
            route += both_ways([(j, groups_y + (j ^ mask))])
        surfaces.append(lax.ppermute(partial_surface, ("comp", "gy"), route))

    lines = 2 * channels + 16
    edges = 4 * rows + 16
    shapes = [
        shape((rows, channels, columns), f32),
        shape((lines, columns), bf16),
        shape((lines, columns), bf16),
        shape((edges, columns), bf16),
        shape((edges, columns), bf16),
    ]
    if not xor_masks:
        shapes.append(shape((2, channels, columns), bf16))
    spectral = pl.pallas_call(
        functools.partial(forward_kernel, groups_x, xor_masks=xor_masks),
        out_shape=shapes,
        in_specs=[vmem] * 5,
        out_specs=[vmem] * len(shapes),
        scratch_shapes=[pltpu.VMEM((4 * rows, columns), f32)],
        compiler_params=params(),
        name="forward_and_halos",
    )(fields, wet_cells, diff_row, half_rates, forward)
    y, e1, e3, e2, e4 = spectral[:5]

    def gx_route(odd):
        pairs = [(groups_x + a, groups_x + b) for a, b in chain_pairs(groups_x, odd)]
        mask = 3 if odd else 1
        if mask in xor_masks:
            pairs += [(a, a ^ mask) for a in range(groups_x) if a < a ^ mask]
        return both_ways(pairs)

    e1 = lax.ppermute(e1, ("comp", "gx"), gx_route(0))
    e3 = lax.ppermute(e3, ("comp", "gx"), gx_route(1))

    landing, e2, e4 = pl.pallas_call(
        functools.partial(regrid_kernel, groups_y),
        out_shape=[
            shape((cells, LANES), f32),
            shape((edges, columns), bf16),
            shape((edges, columns), bf16),
        ],
        in_specs=[vmem] * groups_y
        + [vmem, vmem, smem, anywhere, vmem, vmem, smem, anywhere]
        + [vmem] * 4,
        out_specs=[vmem] * 3,
        scratch_shapes=[
            pltpu.VMEM((blocks, points, points), bf16),
            pltpu.VMEM((LANES, points), bf16),
            pltpu.VMEM((blocks, points), f32),
            pltpu.VMEM((blocks, points), f32),
            pltpu.VMEM((8, columns), f32),
            pltpu.SemaphoreType.DMA,
        ],
        compiler_params=params(),
        name="regrid_blocks",
    )(
        *surfaces,
        a2o_source, a2o_target, a2o_count, a2o_weight,
        marine_air_input_index, marine_air_output_index,
        marine_air_piece_tally, marine_air_piece_factor,
        e1, e3, e2, e4,
    )
    sent = landing.astype(bf16)
    parts = [
        lax.ppermute(sent, "gy", [(j, j ^ mask) for j in range(groups_y)])
        for mask in range(1, groups_y)
    ]
    surface_sum = landing
    for part in parts:
        surface_sum = surface_sum + part.astype(f32)

    axes = ("comp", "gx", "gy")

    def flat(comp, i, j):
        return (comp * groups_x + i) * groups_y + j

    def gy_route(odd):
        pairs = [
            (flat(1, i, a), flat(1, i, b))
            for i in range(groups_x)
            for a, b in chain_pairs(groups_y, odd)
        ]
        if not odd and 2 in xor_masks:
            pairs += [
                (flat(0, i, j), flat(0, i ^ 2, j))
                for i in range(groups_x)
                for j in range(groups_y)
                if i < i ^ 2
            ]
        return both_ways(pairs)

    e2 = lax.ppermute(e2, axes, gy_route(0))
    e4 = lax.ppermute(e4, axes, gy_route(1))

    short = surface_sum.astype(bf16)

    def heat_route(odd):
        return both_ways(
            [(groups_x + a, groups_x + b) for a, b in chain_pairs(groups_x, odd)]
        )

    heat_a = lax.ppermute(short, ("comp", "gx"), heat_route(0))
    heat_b = lax.ppermute(short, ("comp", "gx"), heat_route(1))

    extra = []
    if not xor_masks:
        sums = lax.all_gather(spectral[5], "gx").astype(f32)
        viscous = lax.dynamic_slice_in_dim(
            diffusivity, lax.axis_index("gy") * channels, channels
        )[:, None]
        _, alpha, _ = decay_terms(viscous, half_rates)
        alpha = jnp.concatenate([alpha, alpha], axis=1)
        gap = lax.axis_index("gx") - jnp.arange(groups_x)
        decay = jnp.exp(
            -(rows * jnp.maximum(jnp.abs(gap) - 1, 0))[:, None, None] * alpha[None]
        )
        extra = [
            jnp.sum(jnp.where((gap > 0)[:, None, None], decay * sums[:, 0], 0.0), axis=0),
            jnp.sum(jnp.where((gap < 0)[:, None, None], decay * sums[:, 1], 0.0), axis=0),
        ]

    ring = channels // 2 + 8
    return pl.pallas_call(
        functools.partial(final_kernel, groups_x, groups_y, groups_y, xor_masks),
        out_shape=shape(fields.shape, f32),
        in_specs=[vmem] * (14 + len(extra)),
        out_specs=vmem,
        scratch_shapes=[
            pltpu.VMEM((rows, channels, LANES), f32),
            pltpu.VMEM((rows * channels, columns), bf16),
            pltpu.VMEM((rows + 4, 2, ring, columns), f32),
            pltpu.VMEM((rows + 2, 2, ring, columns), f32),
            pltpu.VMEM((16, columns), f32),
            pltpu.VMEM((6, 16, columns), f32),
            pltpu.VMEM((16, columns), f32),
        ],
        compiler_params=params(),
        name="inverse_or_ocean_steps",
    )(
        fields, wet_cells, diff_row, gain_row, half_rates, inverse, y,
        e1, e3, e2, e4, surface_sum, heat_a, heat_b, *extra,
    )


def solution(mesh):
    in_specs = (
        P("comp", "gx", "gy", None),
        P("gx", None),
        P(),
        P(),
        P(),
        P("gx", "gy", None, None),
        P("gx", "gy", None, None),
        P("gx", "gy"),
        P("gx", "gy", None, None, None),
        P("gx", "gy", None, None),
        P("gx", "gy", None, None),
        P("gx", "gy"),
        P("gx", "gy", None, None, None),
    )
    out_specs = P("comp", "gx", "gy", None)
    return jax.shard_map(local, mesh=mesh, in_specs=in_specs, out_specs=out_specs, check_vma=False)
```

```python
import functools

import jax
import jax.numpy as jnp
import numpy as np
from jax import lax
from jax.experimental import pallas as pl
from jax.experimental.pallas import tpu as pltpu
from jax.sharding import PartitionSpec as P

spread_rate = 0.2
mixing_rate = 0.1
heat_gain = 0.5
salt_gain = -0.25
LANES = 128
f32 = jnp.float32
bf16 = jnp.bfloat16


def fourier_tables(columns):
    waves = np.arange(columns // 2)
    phase = np.arange(columns)[:, None] * waves[None, :] % columns
    angles = phase * (2.0 * np.pi / columns)
    forward = np.concatenate([np.cos(angles), np.sin(angles)], axis=1)
    weight = np.where(np.arange(columns) % (columns // 2) == 0, 1.0, 2.0) / columns
    inverse = forward.T * weight[:, None]
    half_rates = 2.0 * np.sin(np.pi * waves / columns) ** 2
    return (
        jnp.asarray(forward.astype(np.float32), bf16),
        jnp.asarray(inverse.astype(np.float32), bf16),
        jnp.asarray(half_rates[None, :].astype(np.float32)),
    )


def chain_pairs(count, odd):
    return [(low, low + 1) for low in range(odd, count - 1, 2)]


def both_ways(pairs):
    return [p for a, b in pairs for p in ((a, b), (b, a))]


def channel_column(row, channels, first):
    n = row.shape[1]
    lane = lax.broadcasted_iota(jnp.int32, (channels, n), 1)
    sub = lax.broadcasted_iota(jnp.int32, (channels, n), 0)
    return jnp.sum(jnp.where(lane == sub + first, row, 0.0), axis=1, keepdims=True)


def to_tiles(surface):
    cols = surface.shape[1]
    return jnp.concatenate(
        [surface[:, k : k + LANES] for k in range(0, cols, LANES)], axis=0
    )


def from_tiles(tiles, rows):
    return jnp.concatenate(
        [tiles[k : k + rows] for k in range(0, tiles.shape[0], rows)], axis=1
    )


def share(ref, block):
    for k in range(ref.shape[0]):
        ref[k] = block


def surface_kernel(x_ref, flux_ref, s_ref, row_ref):
    _, rows, channels, columns = x_ref.shape
    col_group = lax.axis_index("gy")
    is_atmos = lax.axis_index("comp") == 0

    @pl.when(is_atmos)
    def _():
        weight = channel_column(flux_ref[...], channels, col_group * channels)
        for r in range(rows):
            row_ref[r : r + 1, :] = jnp.sum(x_ref[0, r] * weight, axis=0, keepdims=True)
        share(s_ref, to_tiles(row_ref[...]).astype(bf16))

    @pl.when(jnp.logical_not(is_atmos))
    def _():
        gain = jnp.where(col_group == 0, 1.0, 0.0)
        for r in range(rows):
            row_ref[r : r + 1, :] = x_ref[0, r, 0:1, :] * gain
        share(s_ref, to_tiles(row_ref[...]).astype(bf16))


def decay_terms(diff_column, half_rates):
    half = 0.5 / diff_column + half_rates
    sinh = jnp.sqrt(half * (half + 2.0))
    grow = 1.0 + half + sinh
    return 1.0 / grow, jnp.log(grow), sinh


def forward_kernel(
    groups_x, x_ref, wet_ref, diff_ref, rates_ref, table_hbm, after_ref, *refs, xor_masks
):
    del after_ref
    y_ref, e1_ref, e3_ref, e2_ref, e4_ref = refs[:5]
    pq_ref = refs[5] if not xor_masks else None
    edge_ref, table_ref, sem = refs[-3:]
    _, rows, channels, columns = x_ref.shape
    waves = columns // 2
    row_group = lax.axis_index("gx")
    col_group = lax.axis_index("gy")
    is_atmos = lax.axis_index("comp") == 0

    @pl.when(is_atmos)
    def _():
        step = 256
        copies = []
        for k, n in enumerate(range(0, columns, step)):
            lanes = pl.ds(n, step)
            copies.append(
                pltpu.make_async_copy(
                    table_hbm.at[:, lanes], table_ref.at[:, lanes], sem.at[k]
                )
            )
            copies[-1].start()
        flat = x_ref[0].astype(bf16).reshape(rows * channels, columns)
        for k, n in enumerate(range(0, columns, step)):
            copies[k].wait()
            part = jnp.dot(flat, table_ref[:, n : n + step], preferred_element_type=f32)
            y_ref[:, :, n : n + step] = part.reshape(rows, channels, step)
        diff = channel_column(diff_ref[...], channels, col_group * channels)
        total = rows * groups_x
        base = (row_group * rows).astype(f32)
        for n in range(0, waves, LANES):
            lam, alpha, _ = decay_terms(diff, rates_ref[:, n : n + LANES])
            lam2 = lam * lam
            low = jnp.exp(-2.0 * base * alpha)
            high = jnp.exp(-2.0 * (total - rows - base) * alpha)
            for part in (n, n + waves):
                power = low
                p = jnp.zeros((channels, LANES), f32)
                for r in range(rows):
                    power = power * lam2
                    p = lam * p + (1.0 - power) * y_ref[r, :, part : part + LANES]
                power = high
                q = jnp.zeros((channels, LANES), f32)
                for r in reversed(range(rows)):
                    power = power * lam2
                    q = lam * q + (1.0 - power) * y_ref[r, :, part : part + LANES]
                if xor_masks:
                    for mask, out in zip((1, 2, 3), (e1_ref, e2_ref, e3_ref)):
                        if mask in xor_masks:
                            upward = row_group < (row_group ^ mask)
                            out[0:channels, part : part + LANES] = jnp.where(
                                upward, p, q
                            ).astype(bf16)
                else:
                    pq_ref[0, :, part : part + LANES] = p.astype(bf16)
                    pq_ref[1, :, part : part + LANES] = q.astype(bf16)

    @pl.when(jnp.logical_not(is_atmos))
    def _():
        levels = channels // 2
        even_x = row_group % 2 == 0
        even_y = col_group % 2 == 0
        wet = wet_ref[...].astype(f32)
        wet = jnp.concatenate([wet, wet], axis=0).astype(bf16)
        lines = 2 * channels

        def put(out, bottom):
            @pl.when(bottom)
            def _():
                out[0:lines, :] = x_ref[0, rows - 2 :].reshape(lines, columns).astype(bf16)

            @pl.when(jnp.logical_not(bottom))
            def _():
                out[0:lines, :] = x_ref[0, :2].reshape(lines, columns).astype(bf16)

            out[lines : lines + 16, :] = wet

        put(e1_ref, even_x)
        put(e3_ref, jnp.logical_not(even_x))

        def put_edges(out, bottom):
            @pl.when(bottom)
            def _():
                for r in range(rows):
                    for t in range(2):
                        at = (r * 2 + t) * 2
                        c = t * levels + levels - 2
                        edge_ref[at : at + 2, :] = x_ref[0, r, c : c + 2, :]

            @pl.when(jnp.logical_not(bottom))
            def _():
                for r in range(rows):
                    for t in range(2):
                        at = (r * 2 + t) * 2
                        c = t * levels
                        edge_ref[at : at + 2, :] = x_ref[0, r, c : c + 2, :]

            out[0 : rows * 4, :] = edge_ref[...].astype(bf16)

        put_edges(e2_ref, even_y)
        put_edges(e4_ref, jnp.logical_not(even_y))


def regrid_kernel(*refs):
    (
        surfaces_ref, a_src, a_dst, a_count, a_weight, m_src, m_dst, m_count, m_weight,
        e1_ref, e3_ref, e2_in, e4_in,
        land_ref, sent_ref, e2_ref, e4_ref,
        weight_ref, gath_ref, val_ref, tail_ref, sem,
    ) = refs
    is_atmos = lax.axis_index("comp") == 0
    blocks, points = val_ref.shape
    groups_y = surfaces_ref.shape[0] // 2
    cells = surfaces_ref.shape[1]
    rows = 8

    @pl.when(is_atmos)
    def _():
        pltpu.make_async_copy(m_weight.at[0, 0], weight_ref, sem).start()

    @pl.when(jnp.logical_not(is_atmos))
    def _():
        pltpu.make_async_copy(a_weight.at[0, 0], weight_ref, sem).start()

    src = jnp.where(is_atmos, m_src[0, 0], a_src[0, 0])
    dst = jnp.where(is_atmos, m_dst[0, 0], a_dst[0, 0])
    count = jnp.where(is_atmos, m_count[0, 0], a_count[0, 0])
    tiles = cells // rows

    def split(index):
        row = index // (tiles * LANES)
        tile = (index // LANES) % tiles
        return tile * rows + row, index % LANES

    src_row, src_lane = split(src)
    dst_row, dst_lane = split(dst)
    lane_iota = lax.broadcasted_iota(jnp.int32, (LANES, points), 0)
    row_iota = lax.broadcasted_iota(jnp.int32, (cells, points), 0)
    other = jnp.where(is_atmos, groups_y, 0)
    table = surfaces_ref[other].astype(f32)
    for k in range(1, groups_y):
        table = table + surfaces_ref[other + k].astype(f32)
    table = table.astype(bf16)
    for b in range(blocks):
        hot = jnp.where(lane_iota == src_lane[b : b + 1], 1.0, 0.0).astype(bf16)
        picked = jnp.dot(table, hot, preferred_element_type=f32)
        picked = jnp.where(row_iota == src_row[b : b + 1], picked, 0.0)
        gath_ref[b : b + 1, :] = jnp.sum(picked, axis=0, keepdims=True)
    gathered = gath_ref[...].astype(bf16)

    @pl.when(is_atmos)
    def _():
        pltpu.make_async_copy(m_weight.at[0, 0], weight_ref, sem).wait()

    @pl.when(jnp.logical_not(is_atmos))
    def _():
        pltpu.make_async_copy(a_weight.at[0, 0], weight_ref, sem).wait()

    block_iota = lax.broadcasted_iota(jnp.int32, (blocks, points), 0)
    values = jnp.zeros((blocks, points), f32)
    for b in range(blocks):
        term = lax.dot_general(
            gathered, weight_ref[b], (((1,), (1,)), ((), ())), preferred_element_type=f32
        )
        values = jnp.where(block_iota == b, term, values)
    val_ref[...] = jnp.where(block_iota < count, values, 0.0)
    land = jnp.zeros((2 * cells, LANES), f32)
    for b in range(blocks):
        value = val_ref[b : b + 1, :]
        coarse = value.astype(bf16).astype(f32)
        fine = value - coarse
        mine = row_iota == dst_row[b : b + 1]
        both = jnp.concatenate(
            [jnp.where(mine, coarse, 0.0), jnp.where(mine, fine, 0.0)], axis=0
        ).astype(bf16)
        hot = jnp.where(lane_iota == dst_lane[b : b + 1], 1.0, 0.0).astype(bf16)
        land = land + lax.dot_general(
            both, hot, (((1,), (1,)), ((), ())), preferred_element_type=f32
        )
    land = land[:cells] + land[cells:]
    land_ref[...] = land
    share(sent_ref, land.astype(bf16))

    @pl.when(is_atmos)
    def _():
        e2_ref[...] = e2_in[...]
        e4_ref[...] = e4_in[...]

    @pl.when(jnp.logical_not(is_atmos))
    def _():
        row_group = lax.axis_index("gx")
        col_group = lax.axis_index("gy")
        own = e2_in.shape[0] - 16
        channels = (e1_ref.shape[0] - 16) // 2
        levels = channels // 2
        even_x = row_group % 2 == 0
        lower = jnp.where(
            even_x, e3_ref[channels : 2 * channels, :].astype(f32),
            e1_ref[channels : 2 * channels, :].astype(f32),
        )
        upper = jnp.where(
            even_x, e1_ref[0:channels, :].astype(f32), e3_ref[0:channels, :].astype(f32)
        )
        even_y = col_group % 2 == 0

        def fill(out, inn, bottom):
            for line, values in enumerate((lower, upper)):
                for t in range(2):
                    at = (line * 2 + t) * 2
                    c = t * levels
                    tail_ref[at : at + 2, :] = jnp.where(
                        bottom, values[c + levels - 2 : c + levels], values[c : c + 2]
                    )
            out[0:own, :] = inn[0:own, :]
            tail = tail_ref[...]
            out[own : own + 16, :] = jnp.concatenate([tail, tail], axis=0).astype(bf16)

        fill(e2_ref, e2_in, even_y)
        fill(e4_ref, e4_in, jnp.logical_not(even_y))


def final_kernel(groups_x, groups_y, xor_masks, *refs):
    (
        x_ref, wet_ref, diff_ref, gain_ref, rates_ref, table_ref, y_ref,
        e1_ref, e3_ref, e2_ref, e4_ref, hsum_ref, heat_ref,
    ) = refs[:13]
    coupling = (e1_ref, e2_ref, e3_ref)
    at = 13
    if not xor_masks:
        pin_ref, qin_ref = refs[13:15]
        at = 15
    out_ref, z_ref, zb_ref, t0_ref, t1_ref, w_ref, c_ref, h_ref = refs[at:]
    _, rows, channels, columns = x_ref.shape
    waves = columns // 2
    row_group = lax.axis_index("gx")
    col_group = lax.axis_index("gy")
    is_atmos = lax.axis_index("comp") == 0

    @pl.when(is_atmos)
    def _():
        diff = channel_column(diff_ref[...], channels, col_group * channels)
        total = rows * groups_x
        base = (row_group * rows).astype(f32)
        for n in range(0, waves, LANES):
            lam, alpha, sinh = decay_terms(diff, rates_ref[:, n : n + LANES])
            lam2 = lam * lam
            low = jnp.exp(-2.0 * base * alpha)
            high = jnp.exp(-2.0 * (total - rows - base) * alpha)
            scale = 1.0 / (
                2.0 * diff * sinh * (1.0 - jnp.exp(-2.0 * (total + 1) * alpha))
            )
            lows, highs = [], []
            power = low
            for r in range(rows):
                power = power * lam2
                lows.append(1.0 - power)
            power = high
            for r in range(rows):
                power = power * lam2
                highs.append((1.0 - power))
            highs = highs[::-1]
            for part in (n, n + waves):
                lanes = slice(part, part + LANES)
                if xor_masks:
                    pin = jnp.zeros((channels, LANES), f32)
                    qin = jnp.zeros((channels, LANES), f32)
                    for mask in xor_masks:
                        other = row_group ^ mask
                        gap = (jnp.abs(row_group - other) - 1) * rows
                        term = jnp.exp(-gap.astype(f32) * alpha)
                        term = term * coupling[mask - 1][0:channels, lanes].astype(f32)
                        pin = pin + jnp.where(other < row_group, term, 0.0)
                        qin = qin + jnp.where(other > row_group, term, 0.0)
                else:
                    pin = pin_ref[:, lanes]
                    qin = qin_ref[:, lanes]
                f = pin
                for r in range(rows):
                    f = lam * f + lows[r] * y_ref[r, :, lanes]
                    z_ref[r, :, 0:LANES] = highs[r] * f
                g = lam * qin
                for r in reversed(range(rows)):
                    z = scale * (z_ref[r, :, 0:LANES] + lows[r] * g)
                    zb_ref[r * channels : (r + 1) * channels, lanes] = z.astype(bf16)
                    g = lam * (g + highs[r] * y_ref[r, :, lanes])
        response = channel_column(gain_ref[...], channels, col_group * channels)
        forcing = from_tiles(hsum_ref[...], rows)
        step = 256
        for n in range(0, columns, step):
            part = jnp.dot(
                zb_ref[...], table_ref[:, n : n + step], preferred_element_type=f32
            ).reshape(rows, channels, step)
            for r in range(rows):
                out_ref[0, r, :, n : n + step] = (
                    part[r] + response * forcing[r : r + 1, n : n + step]
                )

    @pl.when(jnp.logical_not(is_atmos))
    def _():
        levels = channels // 2
        ring = levels + 8
        lines = 2 * channels
        even_x = row_group % 2 == 0
        even_y = col_group % 2 == 0
        first_x = row_group == 0
        last_x = row_group == groups_x - 1
        top = col_group == 0
        bottom = col_group == groups_y - 1

        m1 = e1_ref[lines : lines + 16, :].astype(f32)
        m3 = e3_ref[lines : lines + 16, :].astype(f32)
        below = jnp.where(even_x, m3, m1)[rows - 2 : rows]
        above = jnp.where(even_x, m1, m3)[0:2]
        w_ref[0:2, :] = jnp.where(first_x, 0.0, below)
        w_ref[2 : rows + 2, :] = wet_ref[...].astype(f32)
        w_ref[rows + 2 : rows + 4, :] = jnp.where(last_x, 0.0, above)

        surface = jnp.where(top, 1.0, 0.0)
        own = from_tiles(hsum_ref[...], rows)
        below = heat_ref[jnp.maximum(row_group - 1, 0)].astype(f32)
        above = heat_ref[jnp.minimum(row_group + 1, groups_x - 1)].astype(f32)
        h_ref[0:1, :] = from_tiles(below, rows)[rows - 1 : rows]
        h_ref[1 : rows + 1, :] = own
        h_ref[rows + 1 : rows + 2, :] = from_tiles(above, rows)[0:1]

        span = rows + 2
        north = w_ref[0:span, :]
        here = w_ref[1 : span + 1, :]
        south = w_ref[2 : span + 2, :]
        west = pltpu.roll(here, 1, 1)
        east = pltpu.roll(here, columns - 1, 1)
        c_ref[0, 0:span, :] = here * (
            1.0 - 2.0 * mixing_rate - spread_rate * (north + south + west + east)
        )
        c_ref[1, 0:span, :] = spread_rate * here * north
        c_ref[2, 0:span, :] = spread_rate * here * south
        c_ref[3, 0:span, :] = spread_rate * here * west
        c_ref[4, 0:span, :] = spread_rate * here * east
        c_ref[5, 0:span, :] = mixing_rate * here
        h_ref[0:span, :] = surface * here * h_ref[0:span, :]

        e1 = e1_ref[0:lines, :].astype(f32)
        e3 = e3_ref[0:lines, :].astype(f32)
        below = jnp.where(even_x, e3, e1)
        above = jnp.where(even_x, e1, e3)
        for k in range(2):
            for t in range(2):
                c = k * channels + t * levels
                t0_ref[k, t, 0:levels, :] = below[c : c + levels]
                t0_ref[rows + 2 + k, t, 0:levels, :] = above[c : c + levels]
                t0_ref[k, t, levels:ring, :] = jnp.zeros((8, columns), f32)
                t0_ref[rows + 2 + k, t, levels:ring, :] = jnp.zeros((8, columns), f32)
        for r in range(rows):
            for t in range(2):
                t0_ref[r + 2, t, 0:levels, :] = x_ref[0, r, t * levels : (t + 1) * levels, :]
                t0_ref[r + 2, t, levels:ring, :] = jnp.zeros((8, columns), f32)
        e2 = e2_ref[...].astype(f32)
        e4 = e4_ref[...].astype(f32)
        before = jnp.where(even_y, e4, e2)
        after = jnp.where(even_y, e2, e4)
        for r in range(-1, rows + 1):
            place = {-1: rows, rows: rows + 1}.get(r, r)
            for t in range(2):
                k = (place * 2 + t) * 2
                t0_ref[r + 2, t, levels : levels + 2, :] = after[k : k + 2]
                t0_ref[r + 2, t, ring - 2 : ring, :] = before[k : k + 2]

        def close(ref, r):
            for t in range(2):
                ref[r, t, ring - 1 : ring, :] = jnp.where(
                    top, ref[r, t, 0:1, :], ref[r, t, ring - 1 : ring, :]
                )
                ref[r, t, levels : levels + 1, :] = jnp.where(
                    bottom, ref[r, t, levels - 1 : levels, :], ref[r, t, levels : levels + 1, :]
                )

        gains = (heat_gain, salt_gain)

        def advance(ref, r, t, coefs, size):
            whole = ref[r, t]
            up = pltpu.roll(whole, 1, 0)[:size]
            down = pltpu.roll(whole, ring - 1, 0)[:size]
            mid = whole[:size]
            total = coefs[0] * mid + coefs[5] * (up + down)
            total = total + coefs[1] * ref[r - 1, t, 0:size, :]
            total = total + coefs[2] * ref[r + 1, t, 0:size, :]
            total = total + coefs[3] * pltpu.roll(mid, 1, 1)
            return total + coefs[4] * pltpu.roll(mid, columns - 1, 1)

        def first(r, carry):
            coefs = [c_ref[k, pl.ds(r, 1), :] for k in range(6)]
            close(t0_ref, r + 1)
            heat = h_ref[pl.ds(r, 1), :]
            for t in range(2):
                t1_ref[r, t] = advance(t0_ref, r + 1, t, coefs, ring)
                t1_ref[r, t, 0:1, :] = t1_ref[r, t, 0:1, :] + gains[t] * heat
            close(t1_ref, r)
            return carry

        lax.fori_loop(0, span, first, 0)

        def second(r, carry):
            coefs = [c_ref[k, pl.ds(r, 1), :] for k in range(6)]
            heat = h_ref[pl.ds(r, 1), :]
            for t in range(2):
                c = t * levels
                out_ref[0, r - 1, c : c + levels, :] = advance(t1_ref, r, t, coefs, levels)
                out_ref[0, r - 1, c : c + 1, :] = (
                    out_ref[0, r - 1, c : c + 1, :] + gains[t] * heat
                )
            return carry

        lax.fori_loop(1, span - 1, second, 0)


def local(
    fields,
    wet_cells,
    flux_weight,
    variable_sea_response,
    diffusivity,
    a2o_source,
    a2o_target,
    a2o_count,
    a2o_weight,
    marine_air_input_index,
    marine_air_output_index,
    marine_air_piece_tally,
    marine_air_piece_factor,
):
    _, rows, channels, columns = fields.shape
    groups_x = lax.axis_size("gx")
    groups_y = lax.axis_size("gy")
    blocks, points = a2o_source.shape[2:]
    cells = rows * columns // LANES
    waves = columns // 2
    forward, inverse, half_rates = fourier_tables(columns)
    flux_row = flux_weight[None, :]
    gain_row = variable_sea_response[None, :]
    diff_row = diffusivity[None, :]
    xor_masks = tuple(range(1, groups_x)) if groups_x in (2, 4) else ()
    params = functools.partial(pltpu.CompilerParams, vmem_limit_bytes=40 * 2**20)
    vmem = pl.BlockSpec(memory_space=pltpu.VMEM)
    smem = pl.BlockSpec(memory_space=pltpu.SMEM)
    anywhere = pl.BlockSpec(memory_space=pl.ANY)

    def shape(dims, dtype):
        return jax.ShapeDtypeStruct(dims, dtype)

    partial_surface = pl.pallas_call(
        surface_kernel,
        out_shape=shape((2 * groups_y, cells, LANES), bf16),
        in_specs=[vmem, vmem],
        out_specs=vmem,
        scratch_shapes=[pltpu.VMEM((rows, columns), f32)],
        compiler_params=params(),
        name="surface_partials",
    )(fields, flux_row)
    surfaces = lax.all_to_all(partial_surface, ("comp", "gy"), 0, 0, tiled=True)

    lines = 2 * channels + 16
    edges = 4 * rows + 16
    shapes = [
        shape((rows, channels, columns), f32),
        shape((lines, columns), bf16),
        shape((lines, columns), bf16),
        shape((edges, columns), bf16),
        shape((edges, columns), bf16),
    ]
    if not xor_masks:
        shapes.append(shape((2, channels, columns), bf16))
    spectral = pl.pallas_call(
        functools.partial(forward_kernel, groups_x, xor_masks=xor_masks),
        out_shape=shapes,
        in_specs=[vmem] * 4 + [anywhere] * 2,
        out_specs=[vmem] * len(shapes),
        scratch_shapes=[
            pltpu.VMEM((4 * rows, columns), f32),
            pltpu.VMEM((columns, columns), bf16),
            pltpu.SemaphoreType.DMA((columns // 256,)),
        ],
        compiler_params=params(),
        name="forward_and_halos",
    )(fields, wet_cells, diff_row, half_rates, forward, partial_surface)
    y, e1, e3, e2, e4 = spectral[:5]

    def gx_route(odd):
        pairs = [(groups_x + a, groups_x + b) for a, b in chain_pairs(groups_x, odd)]
        mask = 3 if odd else 1
        if mask in xor_masks:
            pairs += [(a, a ^ mask) for a in range(groups_x) if a < a ^ mask]
        return both_ways(pairs)

    e1 = lax.ppermute(e1, ("comp", "gx"), gx_route(0))
    e3 = lax.ppermute(e3, ("comp", "gx"), gx_route(1))

    landing, sent, e2, e4 = pl.pallas_call(
        regrid_kernel,
        out_shape=[
            shape((cells, LANES), f32),
            shape((groups_y, cells, LANES), bf16),
            shape((edges, columns), bf16),
            shape((edges, columns), bf16),
        ],
        in_specs=[vmem]
        + [vmem, vmem, smem, anywhere, vmem, vmem, smem, anywhere]
        + [vmem] * 4,
        out_specs=[vmem] * 4,
        scratch_shapes=[
            pltpu.VMEM((blocks, points, points), bf16),
            pltpu.VMEM((blocks, points), f32),
            pltpu.VMEM((blocks, points), f32),
            pltpu.VMEM((8, columns), f32),
            pltpu.SemaphoreType.DMA,
        ],
        compiler_params=params(),
        name="regrid_blocks",
    )(
        surfaces,
        a2o_source, a2o_target, a2o_count, a2o_weight,
        marine_air_input_index, marine_air_output_index,
        marine_air_piece_tally, marine_air_piece_factor,
        e1, e3, e2, e4,
    )
    parts = lax.all_to_all(sent, "gy", 0, 0, tiled=True)
    mine = lax.axis_index("gy")
    surface_sum = landing
    for k in range(groups_y):
        surface_sum = surface_sum + jnp.where(k == mine, 0.0, parts[k].astype(f32))

    axes = ("comp", "gx", "gy")

    def flat(comp, i, j):
        return (comp * groups_x + i) * groups_y + j

    def gy_route(odd):
        pairs = [
            (flat(1, i, a), flat(1, i, b))
            for i in range(groups_x)
            for a, b in chain_pairs(groups_y, odd)
        ]
        if not odd and 2 in xor_masks:
            pairs += [
                (flat(0, i, j), flat(0, i ^ 2, j))
                for i in range(groups_x)
                for j in range(groups_y)
                if i < i ^ 2
            ]
        return both_ways(pairs)

    e2 = lax.ppermute(e2, axes, gy_route(0))
    e4 = lax.ppermute(e4, axes, gy_route(1))

    short = jnp.broadcast_to(surface_sum.astype(bf16), (groups_x, cells, LANES))
    heat = lax.all_to_all(short, "gx", 0, 0, tiled=True)

    extra = []
    if not xor_masks:
        sums = lax.all_gather(spectral[5], "gx").astype(f32)
        viscous = lax.dynamic_slice_in_dim(
            diffusivity, lax.axis_index("gy") * channels, channels
        )[:, None]
        _, alpha, _ = decay_terms(viscous, half_rates)
        alpha = jnp.concatenate([alpha, alpha], axis=1)
        gap = lax.axis_index("gx") - jnp.arange(groups_x)
        decay = jnp.exp(
            -(rows * jnp.maximum(jnp.abs(gap) - 1, 0))[:, None, None] * alpha[None]
        )
        extra = [
            jnp.sum(jnp.where((gap > 0)[:, None, None], decay * sums[:, 0], 0.0), axis=0),
            jnp.sum(jnp.where((gap < 0)[:, None, None], decay * sums[:, 1], 0.0), axis=0),
        ]

    ring = channels // 2 + 8
    return pl.pallas_call(
        functools.partial(final_kernel, groups_x, groups_y, xor_masks),
        out_shape=shape(fields.shape, f32),
        in_specs=[vmem] * (13 + len(extra)),
        out_specs=vmem,
        scratch_shapes=[
            pltpu.VMEM((rows, channels, LANES), f32),
            pltpu.VMEM((rows * channels, columns), bf16),
            pltpu.VMEM((rows + 4, 2, ring, columns), f32),
            pltpu.VMEM((rows + 2, 2, ring, columns), f32),
            pltpu.VMEM((16, columns), f32),
            pltpu.VMEM((6, 16, columns), f32),
            pltpu.VMEM((16, columns), f32),
        ],
        compiler_params=params(),
        name="inverse_or_ocean_steps",
    )(
        fields, wet_cells, diff_row, gain_row, half_rates, inverse, y,
        e1, e3, e2, e4, surface_sum, heat, *extra,
    )


def solution(mesh):
    in_specs = (
        P("comp", "gx", "gy", None),
        P("gx", None),
        P(),
        P(),
        P(),
        P("gx", "gy", None, None),
        P("gx", "gy", None, None),
        P("gx", "gy"),
        P("gx", "gy", None, None, None),
        P("gx", "gy", None, None),
        P("gx", "gy", None, None),
        P("gx", "gy"),
        P("gx", "gy", None, None, None),
    )
    out_specs = P("comp", "gx", "gy", None)
    return jax.shard_map(local, mesh=mesh, in_specs=in_specs, out_specs=out_specs, check_vma=False)
```

```python
import functools

import jax
import jax.numpy as jnp
import numpy as np
from jax import lax
from jax.experimental import pallas as pl
from jax.experimental.pallas import tpu as pltpu
from jax.sharding import PartitionSpec as P

spread_rate = 0.2
mixing_rate = 0.1
heat_gain = 0.5
salt_gain = -0.25
LANES = 128
f32 = jnp.float32
bf16 = jnp.bfloat16


def fourier_tables(columns):
    waves = np.arange(columns // 2)
    phase = np.arange(columns)[:, None] * waves[None, :] % columns
    angles = phase * (2.0 * np.pi / columns)
    forward = np.concatenate([np.cos(angles), np.sin(angles)], axis=1)
    weight = np.where(np.arange(columns) % (columns // 2) == 0, 1.0, 2.0) / columns
    inverse = forward.T * weight[:, None]
    half_rates = 2.0 * np.sin(np.pi * waves / columns) ** 2
    return (
        jnp.asarray(forward.astype(np.float32), bf16),
        jnp.asarray(inverse.astype(np.float32), bf16),
        jnp.asarray(half_rates[None, :].astype(np.float32)),
    )


def both_ways(pairs):
    return [p for a, b in pairs for p in ((a, b), (b, a))]


def channel_column(row, channels, first):
    n = row.shape[1]
    lane = lax.broadcasted_iota(jnp.int32, (channels, n), 1)
    sub = lax.broadcasted_iota(jnp.int32, (channels, n), 0)
    return jnp.sum(jnp.where(lane == sub + first, row, 0.0), axis=1, keepdims=True)


def to_tiles(surface):
    cols = surface.shape[1]
    return jnp.concatenate(
        [surface[:, k : k + LANES] for k in range(0, cols, LANES)], axis=0
    )


def from_tiles(tiles, rows):
    return jnp.concatenate(
        [tiles[k : k + rows] for k in range(0, tiles.shape[0], rows)], axis=1
    )


def surface_kernel(x_ref, flux_ref, s_ref, row_ref):
    _, rows, channels, columns = x_ref.shape
    col_group = lax.axis_index("gy")
    is_atmos = lax.axis_index("comp") == 0

    @pl.when(is_atmos)
    def _():
        weight = channel_column(flux_ref[...], channels, col_group * channels)
        for r in range(rows):
            row_ref[r : r + 1, :] = jnp.sum(x_ref[0, r] * weight, axis=0, keepdims=True)
        s_ref[...] = to_tiles(row_ref[...]).astype(bf16)

    @pl.when(jnp.logical_not(is_atmos))
    def _():
        gain = jnp.where(col_group == 0, 1.0, 0.0)
        for r in range(rows):
            row_ref[r : r + 1, :] = x_ref[0, r, 0:1, :] * gain
        s_ref[...] = to_tiles(row_ref[...]).astype(bf16)


def decay_terms(diff_column, half_rates):
    half = 0.5 / diff_column + half_rates
    sinh = jnp.sqrt(half * (half + 2.0))
    grow = 1.0 + half + sinh
    return 1.0 / grow, jnp.log(grow), sinh


def forward_kernel(
    groups_x, x_ref, wet_ref, diff_ref, rates_ref, table_ref, after_ref,
    y_ref, beside_ref, edges_ref, edge_ref,
):
    del after_ref
    _, rows, channels, columns = x_ref.shape
    waves = columns // 2
    row_group = lax.axis_index("gx")
    col_group = lax.axis_index("gy")
    is_atmos = lax.axis_index("comp") == 0

    @pl.when(is_atmos)
    def _():
        step = 256
        flat = x_ref[0].astype(bf16).reshape(rows * channels, columns)
        for n in range(0, columns, step):
            part = jnp.dot(flat, table_ref[:, n : n + step], preferred_element_type=f32)
            y_ref[:, :, n : n + step] = part.reshape(rows, channels, step)
        diff = channel_column(diff_ref[...], channels, col_group * channels)
        total = rows * groups_x
        base = (row_group * rows).astype(f32)
        for n in range(0, waves, LANES):
            lam, alpha, _ = decay_terms(diff, rates_ref[:, n : n + LANES])
            lam2 = lam * lam
            low = jnp.exp(-2.0 * base * alpha)
            high = jnp.exp(-2.0 * (total - rows - base) * alpha)
            for part in (n, n + waves):
                lanes = slice(part, part + LANES)
                power = low
                p = jnp.zeros((channels, LANES), f32)
                for r in range(rows):
                    power = power * lam2
                    p = lam * p + (1.0 - power) * y_ref[r, :, lanes]
                power = high
                q = jnp.zeros((channels, LANES), f32)
                for r in reversed(range(rows)):
                    power = power * lam2
                    q = lam * q + (1.0 - power) * y_ref[r, :, lanes]
                beside_ref[0:channels, lanes] = p.astype(bf16)
                beside_ref[channels : 2 * channels, lanes] = q.astype(bf16)

    @pl.when(jnp.logical_not(is_atmos))
    def _():
        levels = channels // 2
        lines = 2 * channels
        wet = wet_ref[...].astype(f32)
        beside_ref[0:lines, :] = x_ref[0, :2].reshape(lines, columns).astype(bf16)
        beside_ref[lines : 2 * lines, :] = (
            x_ref[0, rows - 2 :].reshape(lines, columns).astype(bf16)
        )
        beside_ref[2 * lines : 2 * lines + 16, :] = jnp.concatenate([wet, wet], axis=0).astype(
            bf16
        )
        for r in range(rows):
            for t in range(2):
                at = (r * 2 + t) * 4
                c = t * levels
                edge_ref[at : at + 2, :] = x_ref[0, r, c : c + 2, :]
                edge_ref[at + 2 : at + 4, :] = x_ref[0, r, c + levels - 2 : c + levels, :]
        edges_ref[...] = edge_ref[...].astype(bf16)


def regrid_kernel(n_msgs, *refs):
    msgs = refs[:n_msgs]
    (
        a_src, a_dst, a_count, a_weight, m_src, m_dst, m_count, m_weight,
        land_ref, sent_ref, weight_ref, gath_ref, val_ref, sem,
    ) = refs[n_msgs:]
    is_atmos = lax.axis_index("comp") == 0
    blocks, points = val_ref.shape
    cells = msgs[0].shape[0]
    rows = 8

    @pl.when(is_atmos)
    def _():
        pltpu.make_async_copy(m_weight.at[0, 0], weight_ref, sem).start()

    @pl.when(jnp.logical_not(is_atmos))
    def _():
        pltpu.make_async_copy(a_weight.at[0, 0], weight_ref, sem).start()

    src = jnp.where(is_atmos, m_src[0, 0], a_src[0, 0])
    dst = jnp.where(is_atmos, m_dst[0, 0], a_dst[0, 0])
    count = jnp.where(is_atmos, m_count[0, 0], a_count[0, 0])
    tiles = cells // rows

    def split(index):
        row = index // (tiles * LANES)
        tile = (index // LANES) % tiles
        return tile * rows + row, index % LANES

    src_row, src_lane = split(src)
    dst_row, dst_lane = split(dst)
    lane_iota = lax.broadcasted_iota(jnp.int32, (LANES, points), 0)
    row_iota = lax.broadcasted_iota(jnp.int32, (cells, points), 0)
    table = msgs[0][...].astype(f32)
    for m in msgs[1:]:
        table = table + m[...].astype(f32)
    table = table.astype(bf16)
    for b in range(blocks):
        hot = jnp.where(lane_iota == src_lane[b : b + 1], 1.0, 0.0).astype(bf16)
        picked = jnp.dot(table, hot, preferred_element_type=f32)
        picked = jnp.where(row_iota == src_row[b : b + 1], picked, 0.0)
        gath_ref[b : b + 1, :] = jnp.sum(picked, axis=0, keepdims=True)
    gathered = gath_ref[...].astype(bf16)

    @pl.when(is_atmos)
    def _():
        pltpu.make_async_copy(m_weight.at[0, 0], weight_ref, sem).wait()

    @pl.when(jnp.logical_not(is_atmos))
    def _():
        pltpu.make_async_copy(a_weight.at[0, 0], weight_ref, sem).wait()

    block_iota = lax.broadcasted_iota(jnp.int32, (blocks, points), 0)
    values = jnp.zeros((blocks, points), f32)
    for b in range(blocks):
        term = lax.dot_general(
            gathered, weight_ref[b], (((1,), (1,)), ((), ())), preferred_element_type=f32
        )
        values = jnp.where(block_iota == b, term, values)
    val_ref[...] = jnp.where(block_iota < count, values, 0.0)
    land = jnp.zeros((2 * cells, LANES), f32)
    for b in range(blocks):
        value = val_ref[b : b + 1, :]
        coarse = value.astype(bf16).astype(f32)
        fine = value - coarse
        mine = row_iota == dst_row[b : b + 1]
        both = jnp.concatenate(
            [jnp.where(mine, coarse, 0.0), jnp.where(mine, fine, 0.0)], axis=0
        ).astype(bf16)
        hot = jnp.where(lane_iota == dst_lane[b : b + 1], 1.0, 0.0).astype(bf16)
        land = land + lax.dot_general(
            both, hot, (((1,), (1,)), ((), ())), preferred_element_type=f32
        )
    land = land[:cells] + land[cells:]
    land_ref[...] = land
    sent_ref[...] = land.astype(bf16)


def heat_kernel(rows, levels_edges_ref, land_ref, *refs):
    parts = refs[:-3]
    sum_ref, near_ref, far_ref = refs[-3:]
    cells = land_ref.shape[0]
    columns = cells // rows * LANES
    groups_y = levels_edges_ref.shape[0]
    row_group = lax.axis_index("gx")
    col_group = lax.axis_index("gy")
    total = land_ref[...]
    for part in parts:
        total = total + part[...].astype(f32)
    sum_ref[...] = total
    before = jnp.maximum(col_group - 1, 0)
    after = jnp.minimum(col_group + 1, groups_y - 1)

    def corners(row):
        start = row * 8 // 16 * 16
        low = levels_edges_ref[before, start : start + 16, :].astype(f32)
        high = levels_edges_ref[after, start : start + 16, :].astype(f32)
        at = row * 8 - start
        lines = [low[at + 3 : at + 4], low[at + 7 : at + 8], high[at : at + 1], high[at + 4 : at + 5]]
        return to_tiles(jnp.concatenate(lines + [jnp.zeros((4, columns), f32)], axis=0))

    first, last = corners(0), corners(rows - 1)
    even = row_group % 2 == 0
    near_ref[0:cells, :] = total.astype(bf16)
    far_ref[0:cells, :] = total.astype(bf16)
    near_ref[cells:, :] = jnp.where(even, last, first).astype(bf16)
    far_ref[cells:, :] = jnp.where(even, first, last).astype(bf16)


def steps_kernel(
    groups_x, groups_y, summed, x_ref, wet_ref, diff_ref, rates_ref, y_ref, beside_ref,
    edges_ref, *refs,
):
    if summed:
        pin_ref, qin_ref = refs[:2]
    base_ref, zb_ref, c_ref, z_ref, t0_ref, t1_ref, w_ref = refs[-7:]
    _, rows, channels, columns = x_ref.shape
    waves = columns // 2
    row_group = lax.axis_index("gx")
    col_group = lax.axis_index("gy")
    is_atmos = lax.axis_index("comp") == 0

    @pl.when(is_atmos)
    def _():
        diff = channel_column(diff_ref[...], channels, col_group * channels)
        total = rows * groups_x
        base = (row_group * rows).astype(f32)
        for n in range(0, waves, LANES):
            lam, alpha, sinh = decay_terms(diff, rates_ref[:, n : n + LANES])
            lam2 = lam * lam
            low = jnp.exp(-2.0 * base * alpha)
            high = jnp.exp(-2.0 * (total - rows - base) * alpha)
            scale = 1.0 / (
                2.0 * diff * sinh * (1.0 - jnp.exp(-2.0 * (total + 1) * alpha))
            )
            lows, highs = [], []
            power = low
            for r in range(rows):
                power = power * lam2
                lows.append(1.0 - power)
            power = high
            for r in range(rows):
                power = power * lam2
                highs.append(1.0 - power)
            highs = highs[::-1]
            if not summed:
                decays = []
                for band in range(groups_x):
                    gap = (jnp.abs(row_group - band) - 1) * rows
                    decays.append(jnp.exp(-jnp.maximum(gap, 0).astype(f32) * alpha))
            for part in (n, n + waves):
                lanes = slice(part, part + LANES)
                if summed:
                    pin = pin_ref[:, lanes]
                    qin = qin_ref[:, lanes]
                else:
                    pin = jnp.zeros((channels, LANES), f32)
                    qin = jnp.zeros((channels, LANES), f32)
                    for band in range(groups_x):
                        p = beside_ref[band, 0:channels, lanes].astype(f32)
                        q = beside_ref[band, channels : 2 * channels, lanes].astype(f32)
                        pin = pin + jnp.where(band < row_group, decays[band] * p, 0.0)
                        qin = qin + jnp.where(band > row_group, decays[band] * q, 0.0)
                f = pin
                for r in range(rows):
                    f = lam * f + lows[r] * y_ref[r, :, lanes]
                    z_ref[r] = highs[r] * f
                g = lam * qin
                for r in reversed(range(rows)):
                    z = scale * (z_ref[r] + lows[r] * g)
                    zb_ref[r * channels : (r + 1) * channels, lanes] = z.astype(bf16)
                    g = lam * (g + highs[r] * y_ref[r, :, lanes])

    @pl.when(jnp.logical_not(is_atmos))
    def _():
        levels = channels // 2
        ring = levels + 8
        lines = 2 * channels
        first_x = row_group == 0
        last_x = row_group == groups_x - 1
        top = col_group == 0
        bottom = col_group == groups_y - 1
        if summed:
            under, over = 0, 1
        else:
            under = jnp.maximum(row_group - 1, 0)
            over = jnp.minimum(row_group + 1, groups_x - 1)

        below = beside_ref[under, 2 * lines : 2 * lines + 16, :].astype(f32)
        above = beside_ref[over, 2 * lines : 2 * lines + 16, :].astype(f32)
        w_ref[0:2, :] = jnp.where(first_x, 0.0, below[rows - 2 : rows])
        w_ref[2 : rows + 2, :] = wet_ref[...].astype(f32)
        w_ref[rows + 2 : rows + 4, :] = jnp.where(last_x, 0.0, above[0:2])

        span = rows + 2
        north = w_ref[0:span, :]
        here = w_ref[1 : span + 1, :]
        south = w_ref[2 : span + 2, :]
        west = pltpu.roll(here, 1, 1)
        east = pltpu.roll(here, columns - 1, 1)
        c_ref[0, 0:span, :] = here * (
            1.0 - 2.0 * mixing_rate - spread_rate * (north + south + west + east)
        )
        c_ref[1, 0:span, :] = spread_rate * here * north
        c_ref[2, 0:span, :] = spread_rate * here * south
        c_ref[3, 0:span, :] = spread_rate * here * west
        c_ref[4, 0:span, :] = spread_rate * here * east
        c_ref[5, 0:span, :] = mixing_rate * here
        c_ref[6, 0:span, :] = here

        below = beside_ref[under, lines : 2 * lines, :].astype(f32)
        above = beside_ref[over, 0:lines, :].astype(f32)
        blank = jnp.zeros((8, columns), f32)
        for k in range(2):
            for t in range(2):
                c = k * channels + t * levels
                t0_ref[k, t, 0:levels, :] = below[c : c + levels]
                t0_ref[rows + 2 + k, t, 0:levels, :] = above[c : c + levels]
                t0_ref[k, t, levels:ring, :] = blank
                t0_ref[rows + 2 + k, t, levels:ring, :] = blank
        before = edges_ref[jnp.maximum(col_group - 1, 0)].astype(f32)
        after = edges_ref[jnp.minimum(col_group + 1, groups_y - 1)].astype(f32)
        for r in range(rows):
            for t in range(2):
                k = (r * 2 + t) * 4
                t0_ref[r + 2, t, 0:levels, :] = x_ref[0, r, t * levels : (t + 1) * levels, :]
                t0_ref[r + 2, t, levels : levels + 2, :] = after[k : k + 2]
                t0_ref[r + 2, t, ring - 2 : ring, :] = before[k + 2 : k + 4]

        def close(ref, r):
            for t in range(2):
                ref[r, t, ring - 1 : ring, :] = jnp.where(
                    top, ref[r, t, 0:1, :], ref[r, t, ring - 1 : ring, :]
                )
                ref[r, t, levels : levels + 1, :] = jnp.where(
                    bottom, ref[r, t, levels - 1 : levels, :], ref[r, t, levels : levels + 1, :]
                )

        def advance(ref, r, t, coefs, size):
            whole = ref[r, t]
            up = pltpu.roll(whole, 1, 0)[:size]
            down = pltpu.roll(whole, ring - 1, 0)[:size]
            mid = whole[:size]
            total = coefs[0] * mid + coefs[5] * (up + down)
            total = total + coefs[1] * ref[r - 1, t, 0:size, :]
            total = total + coefs[2] * ref[r + 1, t, 0:size, :]
            total = total + coefs[3] * pltpu.roll(mid, 1, 1)
            return total + coefs[4] * pltpu.roll(mid, columns - 1, 1)

        def first(r, carry):
            coefs = [c_ref[k, pl.ds(r, 1), :] for k in range(6)]
            close(t0_ref, r + 1)
            for t in range(2):
                t1_ref[r, t] = advance(t0_ref, r + 1, t, coefs, ring)
            close(t1_ref, r)
            return carry

        lax.fori_loop(0, span, first, 0)

        def second(r, carry):
            coefs = [c_ref[k, pl.ds(r, 1), :] for k in range(6)]
            for t in range(2):
                c = t * levels
                base_ref[r - 1, c : c + levels, :] = advance(t1_ref, r, t, coefs, levels)
            return carry

        lax.fori_loop(1, span - 1, second, 0)


def last_kernel(
    groups_x, groups_y, gain_ref, table_ref, base_ref, zb_ref, c_ref, sum_ref, near_ref,
    far_ref, out_ref, e_ref,
):
    _, rows, channels, columns = out_ref.shape
    row_group = lax.axis_index("gx")
    col_group = lax.axis_index("gy")
    is_atmos = lax.axis_index("comp") == 0

    @pl.when(is_atmos)
    def _():
        response = channel_column(gain_ref[...], channels, col_group * channels)
        forcing = from_tiles(sum_ref[...], rows)
        step = 256
        for n in range(0, columns, step):
            part = jnp.dot(
                zb_ref[...], table_ref[:, n : n + step], preferred_element_type=f32
            ).reshape(rows, channels, step)
            for r in range(rows):
                out_ref[0, r, :, n : n + step] = (
                    part[r] + response * forcing[r : r + 1, n : n + step]
                )

    @pl.when(jnp.logical_not(is_atmos))
    def _():
        out_ref[0] = base_ref[...]
        levels = channels // 2
        cells = sum_ref.shape[0]
        even = row_group % 2 == 0
        below = jnp.where(even, far_ref[...].astype(f32), near_ref[...].astype(f32))
        above = jnp.where(even, near_ref[...].astype(f32), far_ref[...].astype(f32))

        low = from_tiles(below[cells:], 8)
        high = from_tiles(above[cells:], 8)
        by_low = c_ref[1, 1:2, :] * (c_ref[5, 0:1, :] + c_ref[5, 1:2, :])
        by_high = c_ref[2, rows : rows + 1, :] * (
            c_ref[5, rows : rows + 1, :] + c_ref[5, rows + 1 : rows + 2, :]
        )
        has_before = jnp.where(col_group > 0, 1.0, 0.0)
        has_after = jnp.where(col_group < groups_y - 1, 1.0, 0.0)
        for t in range(2):
            for r, factor, lines in ((0, by_low, low), (rows - 1, by_high, high)):
                c = t * levels
                out_ref[0, r, c : c + 1, :] = out_ref[0, r, c : c + 1, :] + (
                    has_before * factor * lines[t : t + 1]
                )
                c = c + levels - 1
                out_ref[0, r, c : c + 1, :] = out_ref[0, r, c : c + 1, :] + (
                    has_after * factor * lines[t + 2 : t + 3]
                )

        @pl.when(col_group == 0)
        def _():
            span = rows + 2
            e_ref[0:1, :] = from_tiles(below[:cells], rows)[rows - 1 : rows]
            e_ref[1 : rows + 1, :] = from_tiles(sum_ref[...], rows)
            e_ref[rows + 1 : span, :] = from_tiles(above[:cells], rows)[0:1]
            e_ref[0:span, :] = c_ref[6, 0:span, :] * e_ref[0:span, :]
            own = slice(1, rows + 1)
            heat = e_ref[own, :]
            second = c_ref[5, own, :] * heat
            first = (c_ref[0, own, :] + 1.0) * heat + second
            first = first + c_ref[1, own, :] * e_ref[0:rows, :]
            first = first + c_ref[2, own, :] * e_ref[2 : rows + 2, :]
            first = first + c_ref[3, own, :] * pltpu.roll(heat, 1, 1)
            first = first + c_ref[4, own, :] * pltpu.roll(heat, columns - 1, 1)
            for t, gain in enumerate((heat_gain, salt_gain)):
                c = t * levels
                for r in range(rows):
                    lines = jnp.concatenate([first[r : r + 1], second[r : r + 1]], axis=0)
                    out_ref[0, r, c : c + 2, :] = out_ref[0, r, c : c + 2, :] + gain * lines


def local(
    fields,
    wet_cells,
    flux_weight,
    variable_sea_response,
    diffusivity,
    a2o_source,
    a2o_target,
    a2o_count,
    a2o_weight,
    marine_air_input_index,
    marine_air_output_index,
    marine_air_piece_tally,
    marine_air_piece_factor,
):
    _, rows, channels, columns = fields.shape
    groups_x = lax.axis_size("gx")
    groups_y = lax.axis_size("gy")
    blocks, points = a2o_source.shape[2:]
    cells = rows * columns // LANES
    forward, inverse, half_rates = fourier_tables(columns)
    flux_row = flux_weight[None, :]
    gain_row = variable_sea_response[None, :]
    diff_row = diffusivity[None, :]
    params = functools.partial(pltpu.CompilerParams, vmem_limit_bytes=40 * 2**20)
    vmem = pl.BlockSpec(memory_space=pltpu.VMEM)
    smem = pl.BlockSpec(memory_space=pltpu.SMEM)
    anywhere = pl.BlockSpec(memory_space=pl.ANY)

    def shape(dims, dtype):
        return jax.ShapeDtypeStruct(dims, dtype)

    partial_surface = pl.pallas_call(
        surface_kernel,
        out_shape=shape((cells, LANES), bf16),
        in_specs=[vmem, vmem],
        out_specs=vmem,
        scratch_shapes=[pltpu.VMEM((rows, columns), f32)],
        compiler_params=params(),
        name="surface_partials",
    )(fields, flux_row)
    surfaces = []
    for mask in range(groups_y):
        route = []
        for j in range(groups_y):
            route += both_ways([(j, groups_y + (j ^ mask))])
        surfaces.append(lax.ppermute(partial_surface, ("comp", "gy"), route))

    lines = 4 * channels + 16
    y, beside, edges = pl.pallas_call(
        functools.partial(forward_kernel, groups_x),
        out_shape=[
            shape((rows, channels, columns), f32),
            shape((lines, columns), bf16),
            shape((8 * rows, columns), bf16),
        ],
        in_specs=[vmem] * 5 + [anywhere],
        out_specs=[vmem] * 3,
        scratch_shapes=[pltpu.VMEM((8 * rows, columns), f32)],
        compiler_params=params(),
        name="forward_and_halos",
    )(fields, wet_cells, diff_row, half_rates, forward, partial_surface)
    beside = lax.all_gather(beside, "gx")
    edges = lax.all_gather(edges, "gy")

    landing, sent = pl.pallas_call(
        functools.partial(regrid_kernel, groups_y),
        out_shape=[shape((cells, LANES), f32), shape((cells, LANES), bf16)],
        in_specs=[vmem] * groups_y
        + [vmem, vmem, smem, anywhere, vmem, vmem, smem, anywhere],
        out_specs=[vmem] * 2,
        scratch_shapes=[
            pltpu.VMEM((blocks, points, points), bf16),
            pltpu.VMEM((blocks, points), f32),
            pltpu.VMEM((blocks, points), f32),
            pltpu.SemaphoreType.DMA,
        ],
        compiler_params=params(),
        name="regrid_blocks",
    )(
        *surfaces,
        a2o_source, a2o_target, a2o_count, a2o_weight,
        marine_air_input_index, marine_air_output_index,
        marine_air_piece_tally, marine_air_piece_factor,
    )
    parts = [
        lax.ppermute(sent, "gy", [(j, j ^ mask) for j in range(groups_y)])
        for mask in range(1, groups_y)
    ]

    extra = []
    if groups_x > 8:
        mine = lax.axis_index("gx")
        viscous = lax.dynamic_slice_in_dim(
            diffusivity, lax.axis_index("gy") * channels, channels
        )[:, None]
        _, alpha, _ = decay_terms(viscous, half_rates)
        alpha = jnp.concatenate([alpha, alpha], axis=1)
        gap = mine - jnp.arange(groups_x)
        decay = jnp.exp(
            -(rows * jnp.maximum(jnp.abs(gap) - 1, 0))[:, None, None] * alpha[None]
        )
        p = beside[:, :channels].astype(f32)
        q = beside[:, channels : 2 * channels].astype(f32)
        extra = [
            jnp.sum(jnp.where((gap > 0)[:, None, None], decay * p, 0.0), axis=0),
            jnp.sum(jnp.where((gap < 0)[:, None, None], decay * q, 0.0), axis=0),
        ]
        near = jnp.stack([jnp.maximum(mine - 1, 0), jnp.minimum(mine + 1, groups_x - 1)])
        beside = jnp.take(beside, near, axis=0)
    ring = channels // 2 + 8
    base, damped, coefs = pl.pallas_call(
        functools.partial(steps_kernel, groups_x, groups_y, groups_x > 8),
        out_shape=[
            shape((rows, channels, columns), f32),
            shape((rows * channels, columns), bf16),
            shape((7, 16, columns), f32),
        ],
        in_specs=[vmem] * (7 + len(extra)),
        out_specs=[vmem] * 3,
        scratch_shapes=[
            pltpu.VMEM((rows, channels, LANES), f32),
            pltpu.VMEM((rows + 4, 2, ring, columns), f32),
            pltpu.VMEM((rows + 2, 2, ring, columns), f32),
            pltpu.VMEM((16, columns), f32),
        ],
        compiler_params=params(),
        name="damping_or_ocean_steps",
    )(fields, wet_cells, diff_row, half_rates, y, beside, edges, *extra)

    surface_sum, near, far = pl.pallas_call(
        functools.partial(heat_kernel, rows),
        out_shape=[
            shape((cells, LANES), f32),
            shape((cells + columns // 16, LANES), bf16),
            shape((cells + columns // 16, LANES), bf16),
        ],
        in_specs=[vmem] * (2 + len(parts)),
        out_specs=[vmem] * 3,
        compiler_params=params(),
        name="surface_sum",
    )(edges, landing, *parts)

    def ring_pairs(odd):
        pairs = [(a, (a + 1) % groups_x) for a in range(odd, groups_x, 2)]
        return both_ways(pairs)

    near = lax.ppermute(near, "gx", ring_pairs(0))
    far = lax.ppermute(far, "gx", ring_pairs(1))
    return pl.pallas_call(
        functools.partial(last_kernel, groups_x, groups_y),
        out_shape=shape(fields.shape, f32),
        in_specs=[vmem] * 8,
        out_specs=vmem,
        scratch_shapes=[pltpu.VMEM((16, columns), f32)],
        compiler_params=params(),
        name="inverse_or_heat",
    )(gain_row, inverse, base, damped, coefs, surface_sum, near, far)


def solution(mesh):
    in_specs = (
        P("comp", "gx", "gy", None),
        P("gx", None),
        P(),
        P(),
        P(),
        P("gx", "gy", None, None),
        P("gx", "gy", None, None),
        P("gx", "gy"),
        P("gx", "gy", None, None, None),
        P("gx", "gy", None, None),
        P("gx", "gy", None, None),
        P("gx", "gy"),
        P("gx", "gy", None, None, None),
    )
    out_specs = P("comp", "gx", "gy", None)
    return jax.shard_map(local, mesh=mesh, in_specs=in_specs, out_specs=out_specs, check_vma=False)
```

```python
import functools

import jax
import jax.numpy as jnp
import numpy as np
from jax import lax
from jax.experimental import pallas as pl
from jax.experimental.pallas import tpu as pltpu
from jax.sharding import PartitionSpec as P

spread_rate = 0.2
mixing_rate = 0.1
heat_gain = 0.5
salt_gain = -0.25
LANES = 128
f32 = jnp.float32
bf16 = jnp.bfloat16


def fourier_tables(columns):
    waves = np.arange(columns // 2)
    phase = np.arange(columns)[:, None] * waves[None, :] % columns
    angles = phase * (2.0 * np.pi / columns)
    forward = np.concatenate([np.cos(angles), np.sin(angles)], axis=1)
    weight = np.where(np.arange(columns) % (columns // 2) == 0, 1.0, 2.0) / columns
    inverse = forward.T * weight[:, None]
    half_rates = 2.0 * np.sin(np.pi * waves / columns) ** 2
    return (
        jnp.asarray(forward.astype(np.float32), bf16),
        jnp.asarray(inverse.astype(np.float32), bf16),
        jnp.asarray(half_rates[None, :].astype(np.float32)),
    )


def both_ways(pairs):
    return [p for a, b in pairs for p in ((a, b), (b, a))]


def channel_column(row, channels, first):
    n = row.shape[1]
    lane = lax.broadcasted_iota(jnp.int32, (channels, n), 1)
    sub = lax.broadcasted_iota(jnp.int32, (channels, n), 0)
    return jnp.sum(jnp.where(lane == sub + first, row, 0.0), axis=1, keepdims=True)


def to_tiles(surface):
    cols = surface.shape[1]
    return jnp.concatenate(
        [surface[:, k : k + LANES] for k in range(0, cols, LANES)], axis=0
    )


def from_tiles(tiles, rows):
    return jnp.concatenate(
        [tiles[k : k + rows] for k in range(0, tiles.shape[0], rows)], axis=1
    )


def decay_terms(diff_column, half_rates):
    half = 0.5 / diff_column + half_rates
    sinh = jnp.sqrt(half * (half + 2.0))
    grow = 1.0 + half + sinh
    return 1.0 / grow, jnp.log(grow), sinh


def start_kernel(
    groups_x, paired, x_hbm, wet_hbm, flux_hbm, diff_hbm, rates_hbm, table_hbm, *refs
):
    s_ref, y_ref, e1_ref, e3_ref, e2_ref, e4_ref = refs[:6]
    if not paired:
        pq_ref = refs[6]
    (
        x_ref, wet_ref, flux_ref, diff_ref, rates_ref, table_ref, flat_ref, row_ref,
        edge_ref, x_sem, table_sem, small_sem,
    ) = refs[-12:]
    rows, channels, columns = x_ref.shape
    waves = columns // 2
    row_group = lax.axis_index("gx")
    col_group = lax.axis_index("gy")
    is_atmos = lax.axis_index("comp") == 0
    x_copies = [
        pltpu.make_async_copy(x_hbm.at[0, r], x_ref.at[r], x_sem.at[r]) for r in range(rows)
    ]

    @pl.when(is_atmos)
    def _():
        step = 256
        small = [
            pltpu.make_async_copy(hbm, ref, small_sem.at[k])
            for k, (hbm, ref) in enumerate(
                ((flux_hbm, flux_ref), (diff_hbm, diff_ref), (rates_hbm, rates_ref))
            )
        ]
        table = [
            pltpu.make_async_copy(
                table_hbm.at[:, pl.ds(n, step)], table_ref.at[:, pl.ds(n, step)], table_sem.at[k]
            )
            for k, n in enumerate(range(0, columns, step))
        ]
        for copy in small + x_copies + table:
            copy.start()
        for copy in small:
            copy.wait()
        first = col_group * channels
        weight = channel_column(flux_ref[...], channels, first)
        for r in range(rows):
            x_copies[r].wait()
            row_ref[r : r + 1, :] = jnp.sum(x_ref[r] * weight, axis=0, keepdims=True)
            flat_ref[r * channels : (r + 1) * channels, :] = x_ref[r].astype(bf16)
        s_ref[...] = to_tiles(row_ref[...]).astype(bf16)
        for k, n in enumerate(range(0, columns, step)):
            table[k].wait()
            part = jnp.dot(
                flat_ref[...], table_ref[:, n : n + step], preferred_element_type=f32
            )
            y_ref[:, :, n : n + step] = part.reshape(rows, channels, step)
        diff = channel_column(diff_ref[...], channels, first)
        total = rows * groups_x
        base = (row_group * rows).astype(f32)
        for n in range(0, waves, LANES):
            lam, alpha, _ = decay_terms(diff, rates_ref[:, n : n + LANES])
            lam2 = lam * lam
            low = jnp.exp(-2.0 * base * alpha)
            high = jnp.exp(-2.0 * (total - rows - base) * alpha)
            for part in (n, n + waves):
                lanes = slice(part, part + LANES)
                power = low
                p = jnp.zeros((channels, LANES), f32)
                for r in range(rows):
                    power = power * lam2
                    p = lam * p + (1.0 - power) * y_ref[r, :, lanes]
                power = high
                q = jnp.zeros((channels, LANES), f32)
                for r in reversed(range(rows)):
                    power = power * lam2
                    q = lam * q + (1.0 - power) * y_ref[r, :, lanes]
                if paired:
                    for mask, out in ((1, e1_ref), (2, e2_ref), (3, e3_ref)):
                        upward = row_group < (row_group ^ mask)
                        out[0:channels, lanes] = jnp.where(upward, p, q).astype(bf16)
                else:
                    pq_ref[0, :, lanes] = p.astype(bf16)
                    pq_ref[1, :, lanes] = q.astype(bf16)

    @pl.when(jnp.logical_not(is_atmos))
    def _():
        wet_copy = pltpu.make_async_copy(wet_hbm, wet_ref, small_sem.at[0])
        for copy in x_copies:
            copy.start()
        wet_copy.start()
        for copy in x_copies:
            copy.wait()
        gain = jnp.where(col_group == 0, 1.0, 0.0)
        for r in range(rows):
            row_ref[r : r + 1, :] = x_ref[r, 0:1, :] * gain
        s_ref[...] = to_tiles(row_ref[...]).astype(bf16)
        levels = channels // 2
        lines = 2 * channels
        even_x = row_group % 2 == 0
        even_y = col_group % 2 == 0
        wet_copy.wait()
        wet = wet_ref[...].astype(f32)
        wet = jnp.concatenate([wet, wet], axis=0).astype(bf16)

        def put(out, last):
            @pl.when(last)
            def _():
                out[0:lines, :] = x_ref[rows - 2 :].reshape(lines, columns).astype(bf16)

            @pl.when(jnp.logical_not(last))
            def _():
                out[0:lines, :] = x_ref[:2].reshape(lines, columns).astype(bf16)

            out[lines : lines + 16, :] = wet

        put(e1_ref, even_x)
        put(e3_ref, jnp.logical_not(even_x))

        def put_edges(out, level):
            for r in range(rows):
                for t in range(2):
                    at = (r * 2 + t) * 2
                    c = t * levels + level
                    edge_ref[at : at + 2, :] = x_ref[r, c : c + 2, :]
            out[...] = edge_ref[...].astype(bf16)

        @pl.when(even_y)
        def _():
            put_edges(e2_ref, levels - 2)
            put_edges(e4_ref, 0)

        @pl.when(jnp.logical_not(even_y))
        def _():
            put_edges(e2_ref, 0)
            put_edges(e4_ref, levels - 2)


def regrid_kernel(n_msgs, *refs):
    msgs = refs[:n_msgs]
    (
        a_src, a_dst, a_count, a_weight, m_src, m_dst, m_count, m_weight,
        land_ref, sent_ref, weight_ref, gath_ref, val_ref, sem,
    ) = refs[n_msgs:]
    is_atmos = lax.axis_index("comp") == 0
    blocks, points = val_ref.shape
    cells = msgs[0].shape[0]
    rows = 8

    @pl.when(is_atmos)
    def _():
        pltpu.make_async_copy(m_weight.at[0, 0], weight_ref, sem).start()

    @pl.when(jnp.logical_not(is_atmos))
    def _():
        pltpu.make_async_copy(a_weight.at[0, 0], weight_ref, sem).start()

    src = jnp.where(is_atmos, m_src[0, 0], a_src[0, 0])
    dst = jnp.where(is_atmos, m_dst[0, 0], a_dst[0, 0])
    count = jnp.where(is_atmos, m_count[0, 0], a_count[0, 0])
    tiles = cells // rows

    def split(index):
        row = index // (tiles * LANES)
        tile = (index // LANES) % tiles
        return tile * rows + row, index % LANES

    src_row, src_lane = split(src)
    dst_row, dst_lane = split(dst)
    lane_iota = lax.broadcasted_iota(jnp.int32, (LANES, points), 0)
    row_iota = lax.broadcasted_iota(jnp.int32, (cells, points), 0)
    table = msgs[0][...].astype(f32)
    for m in msgs[1:]:
        table = table + m[...].astype(f32)
    table = table.astype(bf16)
    for b in range(blocks):
        hot = jnp.where(lane_iota == src_lane[b : b + 1], 1.0, 0.0).astype(bf16)
        picked = jnp.dot(table, hot, preferred_element_type=f32)
        picked = jnp.where(row_iota == src_row[b : b + 1], picked, 0.0)
        gath_ref[b : b + 1, :] = jnp.sum(picked, axis=0, keepdims=True)
    gathered = gath_ref[...].astype(bf16)

    @pl.when(is_atmos)
    def _():
        pltpu.make_async_copy(m_weight.at[0, 0], weight_ref, sem).wait()

    @pl.when(jnp.logical_not(is_atmos))
    def _():
        pltpu.make_async_copy(a_weight.at[0, 0], weight_ref, sem).wait()

    block_iota = lax.broadcasted_iota(jnp.int32, (blocks, points), 0)
    values = jnp.zeros((blocks, points), f32)
    for b in range(blocks):
        term = lax.dot_general(
            gathered, weight_ref[b], (((1,), (1,)), ((), ())), preferred_element_type=f32
        )
        values = jnp.where(block_iota == b, term, values)
    val_ref[...] = jnp.where(block_iota < count, values, 0.0)
    land = jnp.zeros((2 * cells, LANES), f32)
    for b in range(blocks):
        value = val_ref[b : b + 1, :]
        coarse = value.astype(bf16).astype(f32)
        fine = value - coarse
        mine = row_iota == dst_row[b : b + 1]
        both = jnp.concatenate(
            [jnp.where(mine, coarse, 0.0), jnp.where(mine, fine, 0.0)], axis=0
        ).astype(bf16)
        hot = jnp.where(lane_iota == dst_lane[b : b + 1], 1.0, 0.0).astype(bf16)
        land = land + lax.dot_general(
            both, hot, (((1,), (1,)), ((), ())), preferred_element_type=f32
        )
    land = land[:cells] + land[cells:]
    land_ref[...] = land
    sent_ref[...] = land.astype(bf16)


def heat_kernel(rows, e2_ref, e4_ref, land_ref, *refs):
    parts = refs[:-3]
    sum_ref, near_ref, far_ref = refs[-3:]
    cells = land_ref.shape[0]
    columns = cells // rows * LANES
    even_x = lax.axis_index("gx") % 2 == 0
    even_y = lax.axis_index("gy") % 2 == 0
    total = land_ref[...]
    for part in parts:
        total = total + part[...].astype(f32)
    sum_ref[...] = total

    def corners(row):
        start = row * 4 // 16 * 16
        one = e2_ref[start : start + 16, :].astype(f32)
        two = e4_ref[start : start + 16, :].astype(f32)
        low = jnp.where(even_y, two, one)
        high = jnp.where(even_y, one, two)
        at = row * 4 - start
        lines = [low[at + 1 : at + 2], low[at + 3 : at + 4], high[at : at + 1], high[at + 2 : at + 3]]
        return to_tiles(jnp.concatenate(lines + [jnp.zeros((4, columns), f32)], axis=0))

    first, last = corners(0), corners(rows - 1)
    near_ref[0:cells, :] = total.astype(bf16)
    far_ref[0:cells, :] = total.astype(bf16)
    near_ref[cells:, :] = jnp.where(even_x, last, first).astype(bf16)
    far_ref[cells:, :] = jnp.where(even_x, first, last).astype(bf16)


def steps_kernel(
    groups_x, groups_y, paired, x_ref, wet_ref, diff_ref, rates_ref, y_ref, e1_ref, e3_ref,
    e2_ref, e4_ref, *refs,
):
    if not paired:
        pin_ref, qin_ref = refs[:2]
    base_ref, zb_ref, c_ref, z_ref, t0_ref, t1_ref, w_ref = refs[-7:]
    _, rows, channels, columns = x_ref.shape
    waves = columns // 2
    row_group = lax.axis_index("gx")
    col_group = lax.axis_index("gy")
    is_atmos = lax.axis_index("comp") == 0

    @pl.when(is_atmos)
    def _():
        diff = channel_column(diff_ref[...], channels, col_group * channels)
        total = rows * groups_x
        base = (row_group * rows).astype(f32)
        for n in range(0, waves, LANES):
            lam, alpha, sinh = decay_terms(diff, rates_ref[:, n : n + LANES])
            lam2 = lam * lam
            low = jnp.exp(-2.0 * base * alpha)
            high = jnp.exp(-2.0 * (total - rows - base) * alpha)
            scale = 1.0 / (
                2.0 * diff * sinh * (1.0 - jnp.exp(-2.0 * (total + 1) * alpha))
            )
            lows, highs = [], []
            power = low
            for r in range(rows):
                power = power * lam2
                lows.append(1.0 - power)
            power = high
            for r in range(rows):
                power = power * lam2
                highs.append(1.0 - power)
            highs = highs[::-1]
            for part in (n, n + waves):
                lanes = slice(part, part + LANES)
                if paired:
                    pin = jnp.zeros((channels, LANES), f32)
                    qin = jnp.zeros((channels, LANES), f32)
                    for mask, msg in ((1, e1_ref), (2, e2_ref), (3, e3_ref)):
                        band = row_group ^ mask
                        gap = (jnp.abs(row_group - band) - 1) * rows
                        term = jnp.exp(-gap.astype(f32) * alpha)
                        term = term * msg[0:channels, lanes].astype(f32)
                        pin = pin + jnp.where(band < row_group, term, 0.0)
                        qin = qin + jnp.where(band > row_group, term, 0.0)
                else:
                    pin = pin_ref[:, lanes]
                    qin = qin_ref[:, lanes]
                f = pin
                for r in range(rows):
                    f = lam * f + lows[r] * y_ref[r, :, lanes]
                    z_ref[r] = highs[r] * f
                g = lam * qin
                for r in reversed(range(rows)):
                    z = scale * (z_ref[r] + lows[r] * g)
                    zb_ref[r * channels : (r + 1) * channels, lanes] = z.astype(bf16)
                    g = lam * (g + highs[r] * y_ref[r, :, lanes])

    @pl.when(jnp.logical_not(is_atmos))
    def _():
        levels = channels // 2
        ring = levels + 8
        lines = 2 * channels
        first_x = row_group == 0
        last_x = row_group == groups_x - 1
        top = col_group == 0
        bottom = col_group == groups_y - 1
        even_x = row_group % 2 == 0
        even_y = col_group % 2 == 0

        one = e1_ref[lines : lines + 16, :].astype(f32)
        three = e3_ref[lines : lines + 16, :].astype(f32)
        below = jnp.where(even_x, three, one)[rows - 2 : rows]
        above = jnp.where(even_x, one, three)[0:2]
        w_ref[0:2, :] = jnp.where(first_x, 0.0, below)
        w_ref[2 : rows + 2, :] = wet_ref[...].astype(f32)
        w_ref[rows + 2 : rows + 4, :] = jnp.where(last_x, 0.0, above)

        span = rows + 2
        north = w_ref[0:span, :]
        here = w_ref[1 : span + 1, :]
        south = w_ref[2 : span + 2, :]
        west = pltpu.roll(here, 1, 1)
        east = pltpu.roll(here, columns - 1, 1)
        c_ref[0, 0:span, :] = here * (
            1.0 - 2.0 * mixing_rate - spread_rate * (north + south + west + east)
        )
        c_ref[1, 0:span, :] = spread_rate * here * north
        c_ref[2, 0:span, :] = spread_rate * here * south
        c_ref[3, 0:span, :] = spread_rate * here * west
        c_ref[4, 0:span, :] = spread_rate * here * east
        c_ref[5, 0:span, :] = mixing_rate * here
        c_ref[6, 0:span, :] = here

        one = e1_ref[0:lines, :].astype(f32)
        three = e3_ref[0:lines, :].astype(f32)
        below = jnp.where(even_x, three, one)
        above = jnp.where(even_x, one, three)
        blank = jnp.zeros((8, columns), f32)
        for k in range(2):
            for t in range(2):
                c = k * channels + t * levels
                t0_ref[k, t, 0:levels, :] = below[c : c + levels]
                t0_ref[rows + 2 + k, t, 0:levels, :] = above[c : c + levels]
                t0_ref[k, t, levels:ring, :] = blank
                t0_ref[rows + 2 + k, t, levels:ring, :] = blank
        one = e2_ref[...].astype(f32)
        two = e4_ref[...].astype(f32)
        before = jnp.where(even_y, two, one)
        after = jnp.where(even_y, one, two)
        for r in range(rows):
            for t in range(2):
                k = (r * 2 + t) * 2
                t0_ref[r + 2, t, 0:levels, :] = x_ref[0, r, t * levels : (t + 1) * levels, :]
                t0_ref[r + 2, t, levels : levels + 2, :] = after[k : k + 2]
                t0_ref[r + 2, t, ring - 2 : ring, :] = before[k : k + 2]

        def close(ref, r):
            for t in range(2):
                ref[r, t, ring - 1 : ring, :] = jnp.where(
                    top, ref[r, t, 0:1, :], ref[r, t, ring - 1 : ring, :]
                )
                ref[r, t, levels : levels + 1, :] = jnp.where(
                    bottom, ref[r, t, levels - 1 : levels, :], ref[r, t, levels : levels + 1, :]
                )

        def advance(ref, r, t, coefs, size):
            whole = ref[r, t]
            up = pltpu.roll(whole, 1, 0)[:size]
            down = pltpu.roll(whole, ring - 1, 0)[:size]
            mid = whole[:size]
            total = coefs[0] * mid + coefs[5] * (up + down)
            total = total + coefs[1] * ref[r - 1, t, 0:size, :]
            total = total + coefs[2] * ref[r + 1, t, 0:size, :]
            total = total + coefs[3] * pltpu.roll(mid, 1, 1)
            return total + coefs[4] * pltpu.roll(mid, columns - 1, 1)

        def first(r, carry):
            coefs = [c_ref[k, pl.ds(r, 1), :] for k in range(6)]
            close(t0_ref, r + 1)
            for t in range(2):
                t1_ref[r, t] = advance(t0_ref, r + 1, t, coefs, ring)
            close(t1_ref, r)
            return carry

        lax.fori_loop(0, span, first, 0)

        def second(r, carry):
            coefs = [c_ref[k, pl.ds(r, 1), :] for k in range(6)]
            for t in range(2):
                c = t * levels
                base_ref[r - 1, c : c + levels, :] = advance(t1_ref, r, t, coefs, levels)
            return carry

        lax.fori_loop(1, span - 1, second, 0)


def last_kernel(
    groups_x, groups_y, gain_ref, table_ref, base_ref, zb_ref, c_ref, sum_ref, near_ref,
    far_ref, out_ref, e_ref,
):
    _, rows, channels, columns = out_ref.shape
    row_group = lax.axis_index("gx")
    col_group = lax.axis_index("gy")
    is_atmos = lax.axis_index("comp") == 0

    @pl.when(is_atmos)
    def _():
        response = channel_column(gain_ref[...], channels, col_group * channels)
        forcing = from_tiles(sum_ref[...], rows)
        step = 256
        for n in range(0, columns, step):
            part = jnp.dot(
                zb_ref[...], table_ref[:, n : n + step], preferred_element_type=f32
            ).reshape(rows, channels, step)
            for r in range(rows):
                out_ref[0, r, :, n : n + step] = (
                    part[r] + response * forcing[r : r + 1, n : n + step]
                )

    @pl.when(jnp.logical_not(is_atmos))
    def _():
        out_ref[0] = base_ref[...]
        levels = channels // 2
        cells = sum_ref.shape[0]
        even = row_group % 2 == 0
        below = jnp.where(even, far_ref[...].astype(f32), near_ref[...].astype(f32))
        above = jnp.where(even, near_ref[...].astype(f32), far_ref[...].astype(f32))

        low = from_tiles(below[cells:], 8)
        high = from_tiles(above[cells:], 8)
        by_low = c_ref[1, 1:2, :] * (c_ref[5, 0:1, :] + c_ref[5, 1:2, :])
        by_high = c_ref[2, rows : rows + 1, :] * (
            c_ref[5, rows : rows + 1, :] + c_ref[5, rows + 1 : rows + 2, :]
        )
        has_before = jnp.where(col_group > 0, 1.0, 0.0)
        has_after = jnp.where(col_group < groups_y - 1, 1.0, 0.0)
        for t in range(2):
            for r, factor, lines in ((0, by_low, low), (rows - 1, by_high, high)):
                c = t * levels
                out_ref[0, r, c : c + 1, :] = out_ref[0, r, c : c + 1, :] + (
                    has_before * factor * lines[t : t + 1]
                )
                c = c + levels - 1
                out_ref[0, r, c : c + 1, :] = out_ref[0, r, c : c + 1, :] + (
                    has_after * factor * lines[t + 2 : t + 3]
                )

        @pl.when(col_group == 0)
        def _():
            span = rows + 2
            e_ref[0:1, :] = from_tiles(below[:cells], rows)[rows - 1 : rows]
            e_ref[1 : rows + 1, :] = from_tiles(sum_ref[...], rows)
            e_ref[rows + 1 : span, :] = from_tiles(above[:cells], rows)[0:1]
            e_ref[0:span, :] = c_ref[6, 0:span, :] * e_ref[0:span, :]
            own = slice(1, rows + 1)
            heat = e_ref[own, :]
            second = c_ref[5, own, :] * heat
            first = (c_ref[0, own, :] + 1.0) * heat + second
            first = first + c_ref[1, own, :] * e_ref[0:rows, :]
            first = first + c_ref[2, own, :] * e_ref[2 : rows + 2, :]
            first = first + c_ref[3, own, :] * pltpu.roll(heat, 1, 1)
            first = first + c_ref[4, own, :] * pltpu.roll(heat, columns - 1, 1)
            for t, gain in enumerate((heat_gain, salt_gain)):
                c = t * levels
                for r in range(rows):
                    lines = jnp.concatenate([first[r : r + 1], second[r : r + 1]], axis=0)
                    out_ref[0, r, c : c + 2, :] = out_ref[0, r, c : c + 2, :] + gain * lines


def local(
    fields,
    wet_cells,
    flux_weight,
    variable_sea_response,
    diffusivity,
    a2o_source,
    a2o_target,
    a2o_count,
    a2o_weight,
    marine_air_input_index,
    marine_air_output_index,
    marine_air_piece_tally,
    marine_air_piece_factor,
):
    _, rows, channels, columns = fields.shape
    groups_x = lax.axis_size("gx")
    groups_y = lax.axis_size("gy")
    blocks, points = a2o_source.shape[2:]
    cells = rows * columns // LANES
    forward, inverse, half_rates = fourier_tables(columns)
    flux_row = flux_weight[None, :]
    gain_row = variable_sea_response[None, :]
    diff_row = diffusivity[None, :]
    paired = groups_x == 4
    params = functools.partial(pltpu.CompilerParams, vmem_limit_bytes=40 * 2**20)
    vmem = pl.BlockSpec(memory_space=pltpu.VMEM)
    smem = pl.BlockSpec(memory_space=pltpu.SMEM)
    anywhere = pl.BlockSpec(memory_space=pl.ANY)

    def shape(dims, dtype):
        return jax.ShapeDtypeStruct(dims, dtype)

    lines = 2 * channels + 16
    shapes = [
        shape((cells, LANES), bf16),
        shape((rows, channels, columns), f32),
        shape((lines, columns), bf16),
        shape((lines, columns), bf16),
        shape((4 * rows, columns), bf16),
        shape((4 * rows, columns), bf16),
    ]
    if not paired:
        shapes.append(shape((2, channels, columns), bf16))
    partial_surface, y, e1, e3, e2, e4, *sums = pl.pallas_call(
        functools.partial(start_kernel, groups_x, paired),
        out_shape=shapes,
        in_specs=[anywhere] * 6,
        out_specs=[vmem] * len(shapes),
        scratch_shapes=[
            pltpu.VMEM((rows, channels, columns), f32),
            pltpu.VMEM((rows, columns), jnp.int32),
            pltpu.VMEM(flux_row.shape, f32),
            pltpu.VMEM(diff_row.shape, f32),
            pltpu.VMEM(half_rates.shape, f32),
            pltpu.VMEM((columns, columns), bf16),
            pltpu.VMEM((rows * channels, columns), bf16),
            pltpu.VMEM((rows, columns), f32),
            pltpu.VMEM((4 * rows, columns), f32),
            pltpu.SemaphoreType.DMA((rows,)),
            pltpu.SemaphoreType.DMA((columns // 256,)),
            pltpu.SemaphoreType.DMA((3,)),
        ],
        compiler_params=params(),
        name="surface_and_forward_or_halos",
    )(fields, wet_cells, flux_row, diff_row, half_rates, forward)

    surfaces = []
    for mask in range(groups_y):
        route = []
        for j in range(groups_y):
            route += both_ways([(j, groups_y + (j ^ mask))])
        surfaces.append(lax.ppermute(partial_surface, ("comp", "gy"), route))

    def ring_pairs(count, odd):
        return [(a, (a + 1) % count) for a in range(odd, count, 2)]

    def flat(comp, i, j):
        return (comp * groups_x + i) * groups_y + j

    def level_route(odd):
        pairs = []
        for i in range(groups_x):
            for a, b in ring_pairs(groups_y, odd):
                pairs.append((flat(1, i, a), flat(1, i, b)))
                if odd or not paired:
                    pairs.append((flat(0, i, a), flat(0, i, b)))
            if paired and not odd and i < i ^ 2:
                pairs += [(flat(0, i, j), flat(0, i ^ 2, j)) for j in range(groups_y)]
        return both_ways(pairs)

    axes = ("comp", "gx", "gy")
    e1 = lax.ppermute(e1, "gx", both_ways(ring_pairs(groups_x, 0)))
    e3 = lax.ppermute(e3, "gx", both_ways(ring_pairs(groups_x, 1)))
    e2 = lax.ppermute(e2, axes, level_route(0))
    e4 = lax.ppermute(e4, axes, level_route(1))

    landing, sent = pl.pallas_call(
        functools.partial(regrid_kernel, groups_y),
        out_shape=[shape((cells, LANES), f32), shape((cells, LANES), bf16)],
        in_specs=[vmem] * groups_y
        + [vmem, vmem, smem, anywhere, vmem, vmem, smem, anywhere],
        out_specs=[vmem] * 2,
        scratch_shapes=[
            pltpu.VMEM((blocks, points, points), bf16),
            pltpu.VMEM((blocks, points), f32),
            pltpu.VMEM((blocks, points), f32),
            pltpu.SemaphoreType.DMA,
        ],
        compiler_params=params(),
        name="regrid_blocks",
    )(
        *surfaces,
        a2o_source, a2o_target, a2o_count, a2o_weight,
        marine_air_input_index, marine_air_output_index,
        marine_air_piece_tally, marine_air_piece_factor,
    )
    parts = [
        lax.ppermute(sent, "gy", [(j, j ^ mask) for j in range(groups_y)])
        for mask in range(1, groups_y)
    ]

    extra = []
    if not paired:
        p, q = jnp.moveaxis(lax.all_gather(sums[0], "gx").astype(f32), 1, 0)
        viscous = lax.dynamic_slice_in_dim(
            diffusivity, lax.axis_index("gy") * channels, channels
        )[:, None]
        _, alpha, _ = decay_terms(viscous, half_rates)
        alpha = jnp.concatenate([alpha, alpha], axis=1)
        gap = lax.axis_index("gx") - jnp.arange(groups_x)
        decay = jnp.exp(
            -(rows * jnp.maximum(jnp.abs(gap) - 1, 0))[:, None, None] * alpha[None]
        )
        extra = [
            jnp.sum(jnp.where((gap > 0)[:, None, None], decay * p, 0.0), axis=0),
            jnp.sum(jnp.where((gap < 0)[:, None, None], decay * q, 0.0), axis=0),
        ]
    ring = channels // 2 + 8
    base, damped, coefs = pl.pallas_call(
        functools.partial(steps_kernel, groups_x, groups_y, paired),
        out_shape=[
            shape((rows, channels, columns), f32),
            shape((rows * channels, columns), bf16),
            shape((7, 16, columns), f32),
        ],
        in_specs=[vmem] * (9 + len(extra)),
        out_specs=[vmem] * 3,
        scratch_shapes=[
            pltpu.VMEM((rows, channels, LANES), f32),
            pltpu.VMEM((rows + 4, 2, ring, columns), f32),
            pltpu.VMEM((rows + 2, 2, ring, columns), f32),
            pltpu.VMEM((16, columns), f32),
        ],
        compiler_params=params(),
        name="damping_or_ocean_steps",
    )(fields, wet_cells, diff_row, half_rates, y, e1, e3, e2, e4, *extra)

    surface_sum, near, far = pl.pallas_call(
        functools.partial(heat_kernel, rows),
        out_shape=[
            shape((cells, LANES), f32),
            shape((cells + columns // 16, LANES), bf16),
            shape((cells + columns // 16, LANES), bf16),
        ],
        in_specs=[vmem] * (3 + len(parts)),
        out_specs=[vmem] * 3,
        compiler_params=params(),
        name="surface_sum",
    )(e2, e4, landing, *parts)

    near = lax.ppermute(near, "gx", both_ways(ring_pairs(groups_x, 0)))
    far = lax.ppermute(far, "gx", both_ways(ring_pairs(groups_x, 1)))
    return pl.pallas_call(
        functools.partial(last_kernel, groups_x, groups_y),
        out_shape=shape(fields.shape, f32),
        in_specs=[vmem] * 8,
        out_specs=vmem,
        scratch_shapes=[pltpu.VMEM((16, columns), f32)],
        compiler_params=params(),
        name="inverse_or_heat",
    )(gain_row, inverse, base, damped, coefs, surface_sum, near, far)


def solution(mesh):
    in_specs = (
        P("comp", "gx", "gy", None),
        P("gx", None),
        P(),
        P(),
        P(),
        P("gx", "gy", None, None),
        P("gx", "gy", None, None),
        P("gx", "gy"),
        P("gx", "gy", None, None, None),
        P("gx", "gy", None, None),
        P("gx", "gy", None, None),
        P("gx", "gy"),
        P("gx", "gy", None, None, None),
    )
    out_specs = P("comp", "gx", "gy", None)
    return jax.shard_map(local, mesh=mesh, in_specs=in_specs, out_specs=out_specs, check_vma=False)
```

```python
import functools

import jax
import jax.numpy as jnp
import numpy as np
from jax import lax
from jax.experimental import pallas as pl
from jax.experimental.pallas import tpu as pltpu
from jax.sharding import PartitionSpec as P

spread_rate = 0.2
mixing_rate = 0.1
heat_gain = 0.5
salt_gain = -0.25
LANES = 128
f32 = jnp.float32
bf16 = jnp.bfloat16


def fourier_tables(columns):
    half = columns // 2
    forward, inverse, rates = [], [], []
    for first in (0, 1):
        waves = np.arange(first, half, 2)
        phase = np.arange(half)[:, None] * waves[None, :] % columns
        angles = phase * (2.0 * np.pi / columns)
        table = np.concatenate([np.cos(angles), np.sin(angles)], axis=1)
        weight = np.where(waves == 0, 1.0, 2.0) / columns
        forward.append(table)
        inverse.append(table.T * np.concatenate([weight, weight])[:, None])
        rates.append(2.0 * np.sin(np.pi * waves / columns) ** 2)
    return (
        jnp.asarray(np.stack(forward).astype(np.float32), bf16),
        jnp.asarray(np.stack(inverse).astype(np.float32), bf16),
        jnp.asarray(np.concatenate(rates)[None, :].astype(np.float32)),
    )


def wave_parts(columns):
    quarter = columns // 4
    return [
        (g * quarter + n, (g * 2 * quarter + n, (g * 2 + 1) * quarter + n))
        for g in (0, 1)
        for n in range(0, quarter, LANES)
    ]


def both_ways(pairs):
    return [p for a, b in pairs for p in ((a, b), (b, a))]


def channel_column(row, channels, first):
    n = row.shape[1]
    lane = lax.broadcasted_iota(jnp.int32, (channels, n), 1)
    sub = lax.broadcasted_iota(jnp.int32, (channels, n), 0)
    return jnp.sum(jnp.where(lane == sub + first, row, 0.0), axis=1, keepdims=True)


def to_tiles(surface):
    cols = surface.shape[1]
    return jnp.concatenate(
        [surface[:, k : k + LANES] for k in range(0, cols, LANES)], axis=0
    )


def from_tiles(tiles, rows):
    return jnp.concatenate(
        [tiles[k : k + rows] for k in range(0, tiles.shape[0], rows)], axis=1
    )


def decay_terms(diff_column, half_rates):
    half = 0.5 / diff_column + half_rates
    sinh = jnp.sqrt(half * (half + 2.0))
    grow = 1.0 + half + sinh
    return 1.0 / grow, jnp.log(grow), sinh


def start_kernel(
    groups_x, paired, x_hbm, wet_hbm, flux_hbm, diff_hbm, rates_hbm, table_hbm, *refs
):
    s_ref, y_ref, e1_ref, e3_ref, e2_ref, e4_ref = refs[:6]
    if not paired:
        pq_ref = refs[6]
    (
        x_ref, wet_ref, flux_ref, diff_ref, rates_ref, table_ref, flat_ref, row_ref,
        edge_ref, x_sem, table_sem, small_sem,
    ) = refs[-12:]
    rows, channels, columns = x_ref.shape
    half = columns // 2
    row_group = lax.axis_index("gx")
    col_group = lax.axis_index("gy")
    is_atmos = lax.axis_index("comp") == 0
    x_copies = [
        pltpu.make_async_copy(x_hbm.at[0, r], x_ref.at[r], x_sem.at[r]) for r in range(rows)
    ]

    @pl.when(is_atmos)
    def _():
        small = [
            pltpu.make_async_copy(hbm, ref, small_sem.at[k])
            for k, (hbm, ref) in enumerate(
                ((flux_hbm, flux_ref), (diff_hbm, diff_ref), (rates_hbm, rates_ref))
            )
        ]
        table = [
            pltpu.make_async_copy(table_hbm.at[k], table_ref.at[k], table_sem.at[k])
            for k in range(2)
        ]
        for copy in small + x_copies + table:
            copy.start()
        for copy in small:
            copy.wait()
        first = col_group * channels
        weight = channel_column(flux_ref[...], channels, first)
        for r in range(rows):
            x_copies[r].wait()
            row_ref[r : r + 1, :] = jnp.sum(x_ref[r] * weight, axis=0, keepdims=True)
            left, right = x_ref[r, :, :half], x_ref[r, :, half:]
            flat_ref[r * channels : (r + 1) * channels, :half] = (left + right).astype(bf16)
            flat_ref[r * channels : (r + 1) * channels, half:] = (left - right).astype(bf16)
        s_ref[...] = to_tiles(row_ref[...]).astype(bf16)
        for k in range(2):
            table[k].wait()
            lanes = slice(k * half, (k + 1) * half)
            part = jnp.dot(flat_ref[:, lanes], table_ref[k], preferred_element_type=f32)
            y_ref[:, :, lanes] = part.reshape(rows, channels, half)
        diff = channel_column(diff_ref[...], channels, first)
        total = rows * groups_x
        base = (row_group * rows).astype(f32)
        for n, parts in wave_parts(columns):
            lam, alpha, _ = decay_terms(diff, rates_ref[:, n : n + LANES])
            lam2 = lam * lam
            low = jnp.exp(-2.0 * base * alpha)
            high = jnp.exp(-2.0 * (total - rows - base) * alpha)
            for part in parts:
                lanes = slice(part, part + LANES)
                power = low
                p = jnp.zeros((channels, LANES), f32)
                for r in range(rows):
                    power = power * lam2
                    p = lam * p + (1.0 - power) * y_ref[r, :, lanes]
                power = high
                q = jnp.zeros((channels, LANES), f32)
                for r in reversed(range(rows)):
                    power = power * lam2
                    q = lam * q + (1.0 - power) * y_ref[r, :, lanes]
                if paired:
                    for mask, out in ((1, e1_ref), (2, e2_ref), (3, e3_ref)):
                        upward = row_group < (row_group ^ mask)
                        out[0:channels, lanes] = jnp.where(upward, p, q).astype(bf16)
                else:
                    pq_ref[0, :, lanes] = p.astype(bf16)
                    pq_ref[1, :, lanes] = q.astype(bf16)

    @pl.when(jnp.logical_not(is_atmos))
    def _():
        wet_copy = pltpu.make_async_copy(wet_hbm, wet_ref, small_sem.at[0])
        for copy in x_copies:
            copy.start()
        wet_copy.start()
        for copy in x_copies:
            copy.wait()
        gain = jnp.where(col_group == 0, 1.0, 0.0)
        for r in range(rows):
            row_ref[r : r + 1, :] = x_ref[r, 0:1, :] * gain
        s_ref[...] = to_tiles(row_ref[...]).astype(bf16)
        levels = channels // 2
        lines = 2 * channels
        even_x = row_group % 2 == 0
        even_y = col_group % 2 == 0
        wet_copy.wait()
        wet = wet_ref[...].astype(f32)
        wet = jnp.concatenate([wet, wet], axis=0).astype(bf16)

        def put(out, last):
            @pl.when(last)
            def _():
                out[0:lines, :] = x_ref[rows - 2 :].reshape(lines, columns).astype(bf16)

            @pl.when(jnp.logical_not(last))
            def _():
                out[0:lines, :] = x_ref[:2].reshape(lines, columns).astype(bf16)

            out[lines : lines + 16, :] = wet

        put(e1_ref, even_x)
        put(e3_ref, jnp.logical_not(even_x))

        def put_edges(out, level):
            for r in range(rows):
                for t in range(2):
                    at = (r * 2 + t) * 2
                    c = t * levels + level
                    edge_ref[at : at + 2, :] = x_ref[r, c : c + 2, :]
            out[...] = edge_ref[...].astype(bf16)

        @pl.when(even_y)
        def _():
            put_edges(e2_ref, levels - 2)
            put_edges(e4_ref, 0)

        @pl.when(jnp.logical_not(even_y))
        def _():
            put_edges(e2_ref, 0)
            put_edges(e4_ref, levels - 2)


def regrid_kernel(n_msgs, *refs):
    msgs = refs[:n_msgs]
    (
        a_src, a_dst, a_count, a_weight, m_src, m_dst, m_count, m_weight,
        _, _, e2_in, e4_in,
        land_ref, sent_ref, e2_ref, e4_ref, weight_ref, gath_ref, val_ref, sem,
    ) = refs[n_msgs:]
    e2_ref[...] = e2_in[...]
    e4_ref[...] = e4_in[...]
    is_atmos = lax.axis_index("comp") == 0
    blocks, points = val_ref.shape
    cells = msgs[0].shape[0]
    rows = 8

    @pl.when(is_atmos)
    def _():
        pltpu.make_async_copy(m_weight.at[0, 0], weight_ref, sem).start()

    @pl.when(jnp.logical_not(is_atmos))
    def _():
        pltpu.make_async_copy(a_weight.at[0, 0], weight_ref, sem).start()

    src = jnp.where(is_atmos, m_src[0, 0], a_src[0, 0])
    dst = jnp.where(is_atmos, m_dst[0, 0], a_dst[0, 0])
    count = jnp.where(is_atmos, m_count[0, 0], a_count[0, 0])
    tiles = cells // rows

    def split(index):
        row = index // (tiles * LANES)
        tile = (index // LANES) % tiles
        return tile * rows + row, index % LANES

    src_row, src_lane = split(src)
    dst_row, dst_lane = split(dst)
    lane_iota = lax.broadcasted_iota(jnp.int32, (LANES, points), 0)
    row_iota = lax.broadcasted_iota(jnp.int32, (cells, points), 0)
    table = msgs[0][...].astype(f32)
    for m in msgs[1:]:
        table = table + m[...].astype(f32)
    table = table.astype(bf16)
    for b in range(blocks):
        hot = jnp.where(lane_iota == src_lane[b : b + 1], 1.0, 0.0).astype(bf16)
        picked = jnp.dot(table, hot, preferred_element_type=f32)
        picked = jnp.where(row_iota == src_row[b : b + 1], picked, 0.0)
        gath_ref[b : b + 1, :] = jnp.sum(picked, axis=0, keepdims=True)
    gathered = gath_ref[...].astype(bf16)

    @pl.when(is_atmos)
    def _():
        pltpu.make_async_copy(m_weight.at[0, 0], weight_ref, sem).wait()

    @pl.when(jnp.logical_not(is_atmos))
    def _():
        pltpu.make_async_copy(a_weight.at[0, 0], weight_ref, sem).wait()

    block_iota = lax.broadcasted_iota(jnp.int32, (blocks, points), 0)
    values = jnp.zeros((blocks, points), f32)
    for b in range(blocks):
        term = lax.dot_general(
            gathered, weight_ref[b], (((1,), (1,)), ((), ())), preferred_element_type=f32
        )
        values = jnp.where(block_iota == b, term, values)
    val_ref[...] = jnp.where(block_iota < count, values, 0.0)
    land = jnp.zeros((2 * cells, LANES), f32)
    for b in range(blocks):
        value = val_ref[b : b + 1, :]
        coarse = value.astype(bf16).astype(f32)
        fine = value - coarse
        mine = row_iota == dst_row[b : b + 1]
        both = jnp.concatenate(
            [jnp.where(mine, coarse, 0.0), jnp.where(mine, fine, 0.0)], axis=0
        ).astype(bf16)
        hot = jnp.where(lane_iota == dst_lane[b : b + 1], 1.0, 0.0).astype(bf16)
        land = land + lax.dot_general(
            both, hot, (((1,), (1,)), ((), ())), preferred_element_type=f32
        )
    land = land[:cells] + land[cells:]
    land_ref[...] = land
    sent_ref[...] = land.astype(bf16)


def heat_kernel(rows, e2_ref, e4_ref, land_ref, *refs):
    parts = refs[:-3]
    sum_ref, near_ref, far_ref = refs[-3:]
    cells = land_ref.shape[0]
    columns = cells // rows * LANES
    even_x = lax.axis_index("gx") % 2 == 0
    even_y = lax.axis_index("gy") % 2 == 0
    total = land_ref[...]
    for part in parts:
        total = total + part[...].astype(f32)
    sum_ref[...] = total

    def corners(row):
        start = row * 4 // 16 * 16
        one = e2_ref[start : start + 16, :].astype(f32)
        two = e4_ref[start : start + 16, :].astype(f32)
        low = jnp.where(even_y, two, one)
        high = jnp.where(even_y, one, two)
        at = row * 4 - start
        lines = [low[at + 1 : at + 2], low[at + 3 : at + 4], high[at : at + 1], high[at + 2 : at + 3]]
        return to_tiles(jnp.concatenate(lines + [jnp.zeros((4, columns), f32)], axis=0))

    first, last = corners(0), corners(rows - 1)
    near_ref[0:cells, :] = total.astype(bf16)
    far_ref[0:cells, :] = total.astype(bf16)
    near_ref[cells:, :] = jnp.where(even_x, last, first).astype(bf16)
    far_ref[cells:, :] = jnp.where(even_x, first, last).astype(bf16)


def steps_kernel(
    groups_x, groups_y, paired, x_ref, wet_ref, diff_ref, rates_ref, y_ref, e1_ref, e3_ref,
    e2_ref, e4_ref, *refs,
):
    if not paired:
        pin_ref, qin_ref = refs[:2]
    base_ref, zb_ref, c_ref, z_ref, t0_ref, t1_ref, w_ref = refs[-7:]
    _, rows, channels, columns = x_ref.shape
    row_group = lax.axis_index("gx")
    col_group = lax.axis_index("gy")
    is_atmos = lax.axis_index("comp") == 0

    @pl.when(is_atmos)
    def _():
        diff = channel_column(diff_ref[...], channels, col_group * channels)
        total = rows * groups_x
        base = (row_group * rows).astype(f32)
        for n, parts in wave_parts(columns):
            lam, alpha, sinh = decay_terms(diff, rates_ref[:, n : n + LANES])
            lam2 = lam * lam
            low = jnp.exp(-2.0 * base * alpha)
            high = jnp.exp(-2.0 * (total - rows - base) * alpha)
            scale = 1.0 / (
                2.0 * diff * sinh * (1.0 - jnp.exp(-2.0 * (total + 1) * alpha))
            )
            lows, highs = [], []
            power = low
            for r in range(rows):
                power = power * lam2
                lows.append(1.0 - power)
            power = high
            for r in range(rows):
                power = power * lam2
                highs.append(1.0 - power)
            highs = highs[::-1]
            for part in parts:
                lanes = slice(part, part + LANES)
                if paired:
                    pin = jnp.zeros((channels, LANES), f32)
                    qin = jnp.zeros((channels, LANES), f32)
                    for mask, msg in ((1, e1_ref), (2, e2_ref), (3, e3_ref)):
                        band = row_group ^ mask
                        gap = (jnp.abs(row_group - band) - 1) * rows
                        term = jnp.exp(-gap.astype(f32) * alpha)
                        term = term * msg[0:channels, lanes].astype(f32)
                        pin = pin + jnp.where(band < row_group, term, 0.0)
                        qin = qin + jnp.where(band > row_group, term, 0.0)
                else:
                    pin = pin_ref[:, lanes]
                    qin = qin_ref[:, lanes]
                f = pin
                for r in range(rows):
                    f = lam * f + lows[r] * y_ref[r, :, lanes]
                    z_ref[r] = highs[r] * f
                g = lam * qin
                for r in reversed(range(rows)):
                    z = scale * (z_ref[r] + lows[r] * g)
                    zb_ref[r * channels : (r + 1) * channels, lanes] = z.astype(bf16)
                    g = lam * (g + highs[r] * y_ref[r, :, lanes])

    @pl.when(jnp.logical_not(is_atmos))
    def _():
        levels = channels // 2
        ring = levels + 8
        lines = 2 * channels
        first_x = row_group == 0
        last_x = row_group == groups_x - 1
        top = col_group == 0
        bottom = col_group == groups_y - 1
        even_x = row_group % 2 == 0
        even_y = col_group % 2 == 0

        one = e1_ref[lines : lines + 16, :].astype(f32)
        three = e3_ref[lines : lines + 16, :].astype(f32)
        below = jnp.where(even_x, three, one)[rows - 2 : rows]
        above = jnp.where(even_x, one, three)[0:2]
        w_ref[0:2, :] = jnp.where(first_x, 0.0, below)
        w_ref[2 : rows + 2, :] = wet_ref[...].astype(f32)
        w_ref[rows + 2 : rows + 4, :] = jnp.where(last_x, 0.0, above)

        span = rows + 2
        north = w_ref[0:span, :]
        here = w_ref[1 : span + 1, :]
        south = w_ref[2 : span + 2, :]
        west = pltpu.roll(here, 1, 1)
        east = pltpu.roll(here, columns - 1, 1)
        c_ref[0, 0:span, :] = here * (
            1.0 - 2.0 * mixing_rate - spread_rate * (north + south + west + east)
        )
        c_ref[1, 0:span, :] = spread_rate * here * north
        c_ref[2, 0:span, :] = spread_rate * here * south
        c_ref[3, 0:span, :] = spread_rate * here * west
        c_ref[4, 0:span, :] = spread_rate * here * east
        c_ref[5, 0:span, :] = mixing_rate * here
        c_ref[6, 0:span, :] = here

        one = e1_ref[0:lines, :].astype(f32)
        three = e3_ref[0:lines, :].astype(f32)
        below = jnp.where(even_x, three, one)
        above = jnp.where(even_x, one, three)
        blank = jnp.zeros((8, columns), f32)
        for k in range(2):
            for t in range(2):
                c = k * channels + t * levels
                t0_ref[k, t, 0:levels, :] = below[c : c + levels]
                t0_ref[rows + 2 + k, t, 0:levels, :] = above[c : c + levels]
                t0_ref[k, t, levels:ring, :] = blank
                t0_ref[rows + 2 + k, t, levels:ring, :] = blank
        one = e2_ref[...].astype(f32)
        two = e4_ref[...].astype(f32)
        before = jnp.where(even_y, two, one)
        after = jnp.where(even_y, one, two)
        for r in range(rows):
            for t in range(2):
                k = (r * 2 + t) * 2
                t0_ref[r + 2, t, 0:levels, :] = x_ref[0, r, t * levels : (t + 1) * levels, :]
                t0_ref[r + 2, t, levels : levels + 2, :] = after[k : k + 2]
                t0_ref[r + 2, t, ring - 2 : ring, :] = before[k : k + 2]

        def close(ref, r):
            for t in range(2):
                ref[r, t, ring - 1 : ring, :] = jnp.where(
                    top, ref[r, t, 0:1, :], ref[r, t, ring - 1 : ring, :]
                )
                ref[r, t, levels : levels + 1, :] = jnp.where(
                    bottom, ref[r, t, levels - 1 : levels, :], ref[r, t, levels : levels + 1, :]
                )

        def advance(ref, r, t, coefs, size):
            whole = ref[r, t]
            up = pltpu.roll(whole, 1, 0)[:size]
            down = pltpu.roll(whole, ring - 1, 0)[:size]
            mid = whole[:size]
            total = coefs[0] * mid + coefs[5] * (up + down)
            total = total + coefs[1] * ref[r - 1, t, 0:size, :]
            total = total + coefs[2] * ref[r + 1, t, 0:size, :]
            total = total + coefs[3] * pltpu.roll(mid, 1, 1)
            return total + coefs[4] * pltpu.roll(mid, columns - 1, 1)

        def first(r, carry):
            coefs = [c_ref[k, pl.ds(r, 1), :] for k in range(6)]
            close(t0_ref, r + 1)
            for t in range(2):
                t1_ref[r, t] = advance(t0_ref, r + 1, t, coefs, ring)
            close(t1_ref, r)
            return carry

        lax.fori_loop(0, span, first, 0)

        def second(r, carry):
            coefs = [c_ref[k, pl.ds(r, 1), :] for k in range(6)]
            for t in range(2):
                c = t * levels
                base_ref[r - 1, c : c + levels, :] = advance(t1_ref, r, t, coefs, levels)
            return carry

        lax.fori_loop(1, span - 1, second, 0)


def last_kernel(
    groups_x, groups_y, gain_ref, table_ref, base_ref, zb_ref, c_ref, sum_ref, near_ref,
    far_ref, out_ref, e_ref,
):
    _, rows, channels, columns = out_ref.shape
    row_group = lax.axis_index("gx")
    col_group = lax.axis_index("gy")
    is_atmos = lax.axis_index("comp") == 0

    @pl.when(is_atmos)
    def _():
        response = channel_column(gain_ref[...], channels, col_group * channels)
        forcing = from_tiles(sum_ref[...], rows)
        half = columns // 2
        step = 256
        for n in range(0, half, step):
            even, odd = [
                jnp.dot(
                    zb_ref[:, k * half : (k + 1) * half],
                    table_ref[k, :, n : n + step],
                    preferred_element_type=f32,
                ).reshape(rows, channels, step)
                for k in range(2)
            ]
            for r in range(rows):
                for lane, part in ((n, even[r] + odd[r]), (n + half, even[r] - odd[r])):
                    out_ref[0, r, :, lane : lane + step] = (
                        part + response * forcing[r : r + 1, lane : lane + step]
                    )

    @pl.when(jnp.logical_not(is_atmos))
    def _():
        out_ref[0] = base_ref[...]
        levels = channels // 2
        cells = sum_ref.shape[0]
        even = row_group % 2 == 0
        below = jnp.where(even, far_ref[...].astype(f32), near_ref[...].astype(f32))
        above = jnp.where(even, near_ref[...].astype(f32), far_ref[...].astype(f32))

        low = from_tiles(below[cells:], 8)
        high = from_tiles(above[cells:], 8)
        by_low = c_ref[1, 1:2, :] * (c_ref[5, 0:1, :] + c_ref[5, 1:2, :])
        by_high = c_ref[2, rows : rows + 1, :] * (
            c_ref[5, rows : rows + 1, :] + c_ref[5, rows + 1 : rows + 2, :]
        )
        has_before = jnp.where(col_group > 0, 1.0, 0.0)
        has_after = jnp.where(col_group < groups_y - 1, 1.0, 0.0)
        for t in range(2):
            for r, factor, lines in ((0, by_low, low), (rows - 1, by_high, high)):
                c = t * levels
                out_ref[0, r, c : c + 1, :] = out_ref[0, r, c : c + 1, :] + (
                    has_before * factor * lines[t : t + 1]
                )
                c = c + levels - 1
                out_ref[0, r, c : c + 1, :] = out_ref[0, r, c : c + 1, :] + (
                    has_after * factor * lines[t + 2 : t + 3]
                )

        @pl.when(col_group == 0)
        def _():
            span = rows + 2
            e_ref[0:1, :] = from_tiles(below[:cells], rows)[rows - 1 : rows]
            e_ref[1 : rows + 1, :] = from_tiles(sum_ref[...], rows)
            e_ref[rows + 1 : span, :] = from_tiles(above[:cells], rows)[0:1]
            e_ref[0:span, :] = c_ref[6, 0:span, :] * e_ref[0:span, :]
            own = slice(1, rows + 1)
            heat = e_ref[own, :]
            second = c_ref[5, own, :] * heat
            first = (c_ref[0, own, :] + 1.0) * heat + second
            first = first + c_ref[1, own, :] * e_ref[0:rows, :]
            first = first + c_ref[2, own, :] * e_ref[2 : rows + 2, :]
            first = first + c_ref[3, own, :] * pltpu.roll(heat, 1, 1)
            first = first + c_ref[4, own, :] * pltpu.roll(heat, columns - 1, 1)
            for t, gain in enumerate((heat_gain, salt_gain)):
                c = t * levels
                for r in range(rows):
                    lines = jnp.concatenate([first[r : r + 1], second[r : r + 1]], axis=0)
                    out_ref[0, r, c : c + 2, :] = out_ref[0, r, c : c + 2, :] + gain * lines


def local(
    fields,
    wet_cells,
    flux_weight,
    variable_sea_response,
    diffusivity,
    a2o_source,
    a2o_target,
    a2o_count,
    a2o_weight,
    marine_air_input_index,
    marine_air_output_index,
    marine_air_piece_tally,
    marine_air_piece_factor,
):
    _, rows, channels, columns = fields.shape
    groups_x = lax.axis_size("gx")
    groups_y = lax.axis_size("gy")
    blocks, points = a2o_source.shape[2:]
    cells = rows * columns // LANES
    forward, inverse, half_rates = fourier_tables(columns)
    flux_row = flux_weight[None, :]
    gain_row = variable_sea_response[None, :]
    diff_row = diffusivity[None, :]
    paired = groups_x == 4
    params = functools.partial(pltpu.CompilerParams, vmem_limit_bytes=40 * 2**20)
    vmem = pl.BlockSpec(memory_space=pltpu.VMEM)
    smem = pl.BlockSpec(memory_space=pltpu.SMEM)
    anywhere = pl.BlockSpec(memory_space=pl.ANY)
    hbm = pl.BlockSpec(memory_space=pltpu.HBM)

    def shape(dims, dtype):
        return jax.ShapeDtypeStruct(dims, dtype)

    lines = 2 * channels + 16
    shapes = [
        shape((cells, LANES), bf16),
        shape((rows, channels, columns), f32),
        shape((lines, columns), bf16),
        shape((lines, columns), bf16),
        shape((4 * rows, columns), bf16),
        shape((4 * rows, columns), bf16),
    ]
    if not paired:
        shapes.append(shape((2, channels, columns), bf16))
    partial_surface, y, e1, e3, e2, e4, *sums = pl.pallas_call(
        functools.partial(start_kernel, groups_x, paired),
        out_shape=shapes,
        in_specs=[hbm] * 6,
        out_specs=[vmem] * len(shapes),
        scratch_shapes=[
            pltpu.VMEM((rows, channels, columns), f32),
            pltpu.VMEM((rows, columns), jnp.int32),
            pltpu.VMEM(flux_row.shape, f32),
            pltpu.VMEM(diff_row.shape, f32),
            pltpu.VMEM(half_rates.shape, f32),
            pltpu.VMEM(forward.shape, bf16),
            pltpu.VMEM((rows * channels, columns), bf16),
            pltpu.VMEM((rows, columns), f32),
            pltpu.VMEM((4 * rows, columns), f32),
            pltpu.SemaphoreType.DMA((rows,)),
            pltpu.SemaphoreType.DMA((2,)),
            pltpu.SemaphoreType.DMA((3,)),
        ],
        compiler_params=params(),
        name="surface_and_forward_or_halos",
    )(fields, wet_cells, flux_row, diff_row, half_rates, forward)

    surfaces = []
    for mask in range(groups_y):
        route = []
        for j in range(groups_y):
            route += both_ways([(j, groups_y + (j ^ mask))])
        surfaces.append(lax.ppermute(partial_surface, ("comp", "gy"), route))

    def ring_pairs(count, odd):
        return [(a, (a + 1) % count) for a in range(odd, count, 2)]

    def flat(comp, i, j):
        return (comp * groups_x + i) * groups_y + j

    def level_route(odd):
        pairs = []
        for i in range(groups_x):
            for a, b in ring_pairs(groups_y, odd):
                pairs.append((flat(1, i, a), flat(1, i, b)))
                if odd or not paired:
                    pairs.append((flat(0, i, a), flat(0, i, b)))
            if paired and not odd and i < i ^ 2:
                pairs += [(flat(0, i, j), flat(0, i ^ 2, j)) for j in range(groups_y)]
        return both_ways(pairs)

    e1 = lax.ppermute(e1, "gx", both_ways(ring_pairs(groups_x, 0)))
    e3 = lax.ppermute(e3, "gx", both_ways(ring_pairs(groups_x, 1)))

    landing, sent, e2, e4 = pl.pallas_call(
        functools.partial(regrid_kernel, groups_y),
        out_shape=[
            shape((cells, LANES), f32),
            shape((cells, LANES), bf16),
            shape(e2.shape, bf16),
            shape(e4.shape, bf16),
        ],
        in_specs=[vmem] * groups_y
        + [vmem, vmem, smem, hbm, vmem, vmem, smem, hbm]
        + [anywhere, anywhere, vmem, vmem],
        out_specs=[vmem] * 4,
        scratch_shapes=[
            pltpu.VMEM((blocks, points, points), bf16),
            pltpu.VMEM((blocks, points), f32),
            pltpu.VMEM((blocks, points), f32),
            pltpu.SemaphoreType.DMA,
        ],
        compiler_params=params(),
        name="regrid_blocks",
    )(
        *surfaces,
        a2o_source, a2o_target, a2o_count, a2o_weight,
        marine_air_input_index, marine_air_output_index,
        marine_air_piece_tally, marine_air_piece_factor, e1, e3, e2, e4,
    )
    parts = [
        lax.ppermute(sent, "gy", [(j, j ^ mask) for j in range(groups_y)])
        for mask in range(1, groups_y)
    ]

    axes = ("comp", "gx", "gy")
    e2 = lax.ppermute(e2, axes, level_route(0))
    e4 = lax.ppermute(e4, axes, level_route(1))

    extra = []
    if not paired:
        p, q = jnp.moveaxis(lax.all_gather(sums[0], "gx").astype(f32), 1, 0)
        viscous = lax.dynamic_slice_in_dim(
            diffusivity, lax.axis_index("gy") * channels, channels
        )[:, None]
        _, alpha, _ = decay_terms(viscous, half_rates)
        alpha = jnp.concatenate([alpha, alpha], axis=1)
        gap = lax.axis_index("gx") - jnp.arange(groups_x)
        decay = jnp.exp(
            -(rows * jnp.maximum(jnp.abs(gap) - 1, 0))[:, None, None] * alpha[None]
        )
        extra = [
            jnp.sum(jnp.where((gap > 0)[:, None, None], decay * p, 0.0), axis=0),
            jnp.sum(jnp.where((gap < 0)[:, None, None], decay * q, 0.0), axis=0),
        ]
    ring = channels // 2 + 8
    base, damped, coefs = pl.pallas_call(
        functools.partial(steps_kernel, groups_x, groups_y, paired),
        out_shape=[
            shape((rows, channels, columns), f32),
            shape((rows * channels, columns), bf16),
            shape((7, 16, columns), f32),
        ],
        in_specs=[vmem] * (9 + len(extra)),
        out_specs=[vmem] * 3,
        scratch_shapes=[
            pltpu.VMEM((rows, channels, LANES), f32),
            pltpu.VMEM((rows + 4, 2, ring, columns), f32),
            pltpu.VMEM((rows + 2, 2, ring, columns), f32),
            pltpu.VMEM((16, columns), f32),
        ],
        compiler_params=params(),
        name="damping_or_ocean_steps",
    )(fields, wet_cells, diff_row, half_rates, y, e1, e3, e2, e4, *extra)

    surface_sum, near, far = pl.pallas_call(
        functools.partial(heat_kernel, rows),
        out_shape=[
            shape((cells, LANES), f32),
            shape((cells + columns // 16, LANES), bf16),
            shape((cells + columns // 16, LANES), bf16),
        ],
        in_specs=[vmem] * (3 + len(parts)),
        out_specs=[vmem] * 3,
        compiler_params=params(),
        name="surface_sum",
    )(e2, e4, landing, *parts)

    near = lax.ppermute(near, "gx", both_ways(ring_pairs(groups_x, 0)))
    far = lax.ppermute(far, "gx", both_ways(ring_pairs(groups_x, 1)))
    return pl.pallas_call(
        functools.partial(last_kernel, groups_x, groups_y),
        out_shape=shape(fields.shape, f32),
        in_specs=[vmem] * 8,
        out_specs=vmem,
        scratch_shapes=[pltpu.VMEM((16, columns), f32)],
        compiler_params=params(),
        name="inverse_or_heat",
    )(gain_row, inverse, base, damped, coefs, surface_sum, near, far)


def solution(mesh):
    in_specs = (
        P("comp", "gx", "gy", None),
        P("gx", None),
        P(),
        P(),
        P(),
        P("gx", "gy", None, None),
        P("gx", "gy", None, None),
        P("gx", "gy"),
        P("gx", "gy", None, None, None),
        P("gx", "gy", None, None),
        P("gx", "gy", None, None),
        P("gx", "gy"),
        P("gx", "gy", None, None, None),
    )
    out_specs = P("comp", "gx", "gy", None)
    return jax.shard_map(local, mesh=mesh, in_specs=in_specs, out_specs=out_specs, check_vma=False)
```

```python
import functools

import jax
import jax.numpy as jnp
import numpy as np
from jax import lax
from jax.experimental import pallas as pl
from jax.experimental.pallas import tpu as pltpu
from jax.sharding import PartitionSpec as P

spread_rate = 0.2
mixing_rate = 0.1
heat_gain = 0.5
salt_gain = -0.25
LANES = 128
f32 = jnp.float32
bf16 = jnp.bfloat16


def fourier_tables(columns):
    half = columns // 2
    forward, inverse = [], []
    for first in (0, 1):
        waves = np.arange(first, half, 2)
        phase = np.arange(half)[:, None] * waves[None, :] % columns
        angles = phase * (2.0 * np.pi / columns)
        table = np.concatenate([np.cos(angles), np.sin(angles)], axis=1)
        weight = np.where(waves == 0, 1.0, 2.0) / columns
        forward.append(table)
        inverse.append(table.T * np.concatenate([weight, weight])[:, None])
    return (
        jnp.asarray(np.concatenate(forward).astype(np.float32), bf16),
        jnp.asarray(np.concatenate(inverse).astype(np.float32), bf16),
    )


def wave_parts(columns):
    quarter = columns // 4
    return [
        (g, n, (g * 2 * quarter + n, (g * 2 + 1) * quarter + n))
        for g in (0, 1)
        for n in range(0, quarter, LANES)
    ]


def half_rates(group, first, count, columns):
    lane = lax.broadcasted_iota(jnp.int32, (1, count), 1) + first
    wave = (2 * lane + group).astype(f32)
    sine = jnp.sin(wave * (np.pi / columns))
    return 2.0 * sine * sine


def both_ways(pairs):
    return [p for a, b in pairs for p in ((a, b), (b, a))]


def channel_column(row, channels, first):
    n = row.shape[1]
    lane = lax.broadcasted_iota(jnp.int32, (channels, n), 1)
    sub = lax.broadcasted_iota(jnp.int32, (channels, n), 0)
    return jnp.sum(jnp.where(lane == sub + first, row, 0.0), axis=1, keepdims=True)


def to_tiles(surface):
    cols = surface.shape[1]
    return jnp.concatenate(
        [surface[:, k : k + LANES] for k in range(0, cols, LANES)], axis=0
    )


def from_tiles(tiles, rows):
    return jnp.concatenate(
        [tiles[k : k + rows] for k in range(0, tiles.shape[0], rows)], axis=1
    )


def decay_terms(diff_column, rates):
    half = 0.5 / diff_column + rates
    sinh = jnp.sqrt(half * (half + 2.0))
    grow = 1.0 + half + sinh
    return 1.0 / grow, jnp.log(grow), sinh


def surface_kernel(x_hbm, flux_hbm, s_ref, coarse_ref, x_ref, flux_ref, row_ref, x_sem, sem):
    rows, channels, columns = x_ref.shape
    col_group = lax.axis_index("gy")
    is_atmos = lax.axis_index("comp") == 0
    flux_copy = pltpu.make_async_copy(flux_hbm, flux_ref, sem)
    copies = [
        pltpu.make_async_copy(x_hbm.at[0, r], x_ref.at[r], x_sem.at[r]) for r in range(rows)
    ]

    @pl.when(is_atmos)
    def _():
        for copy in [flux_copy] + copies:
            copy.start()
        flux_copy.wait()
        weight = channel_column(flux_ref[...], channels, col_group * channels)
        for r in range(rows):
            copies[r].wait()
            row_ref[r : r + 1, :] = jnp.sum(x_ref[r] * weight, axis=0, keepdims=True)

    @pl.when(jnp.logical_not(is_atmos))
    def _():
        top = [
            pltpu.make_async_copy(
                x_hbm.at[0, r, pl.ds(0, 8)], x_ref.at[r, pl.ds(0, 8)], x_sem.at[r]
            )
            for r in range(rows)
        ]
        for copy in top:
            copy.start()
        gain = jnp.where(col_group == 0, 1.0, 0.0)
        for r in range(rows):
            top[r].wait()
            row_ref[r : r + 1, :] = x_ref[r, 0:1, :] * gain

    surface = to_tiles(row_ref[...])
    s_ref[...] = surface
    coarse_ref[...] = surface.astype(bf16)


def forward_kernel(
    groups_x, paired, x_ref, wet_ref, diff_ref, table_ref, s_ref, *refs
):
    kept_ref, y_ref, e1_ref, e3_ref, e2_ref, e4_ref = refs[:6]
    if not paired:
        pq_ref = refs[6]
    kept_ref[...] = s_ref[...]
    flat_ref, edge_ref = refs[-2:]
    _, rows, channels, columns = x_ref.shape
    half = columns // 2
    row_group = lax.axis_index("gx")
    col_group = lax.axis_index("gy")
    is_atmos = lax.axis_index("comp") == 0

    @pl.when(is_atmos)
    def _():
        first = col_group * channels
        for r in range(rows):
            left, right = x_ref[0, r, :, :half], x_ref[0, r, :, half:]
            flat_ref[r * channels : (r + 1) * channels, :half] = (left + right).astype(bf16)
            flat_ref[r * channels : (r + 1) * channels, half:] = (left - right).astype(bf16)
        for k in range(2):
            lanes = slice(k * half, (k + 1) * half)
            part = jnp.dot(
                flat_ref[:, lanes], table_ref[lanes, :], preferred_element_type=f32
            )
            y_ref[:, :, lanes] = part.reshape(rows, channels, half)
        diff = channel_column(diff_ref[...], channels, first)
        total = rows * groups_x
        base = (row_group * rows).astype(f32)
        for group, n, parts in wave_parts(columns):
            lam, alpha, _ = decay_terms(diff, half_rates(group, n, LANES, columns))
            lam2 = lam * lam
            low = jnp.exp(-2.0 * base * alpha)
            high = jnp.exp(-2.0 * (total - rows - base) * alpha)
            for part in parts:
                lanes = slice(part, part + LANES)
                power = low
                p = jnp.zeros((channels, LANES), f32)
                for r in range(rows):
                    power = power * lam2
                    p = lam * p + (1.0 - power) * y_ref[r, :, lanes]
                power = high
                q = jnp.zeros((channels, LANES), f32)
                for r in reversed(range(rows)):
                    power = power * lam2
                    q = lam * q + (1.0 - power) * y_ref[r, :, lanes]
                if paired:
                    for mask, out in ((1, e1_ref), (2, e2_ref), (3, e3_ref)):
                        upward = row_group < (row_group ^ mask)
                        out[0:channels, lanes] = jnp.where(upward, p, q).astype(bf16)
                else:
                    pq_ref[0, :, lanes] = p.astype(bf16)
                    pq_ref[1, :, lanes] = q.astype(bf16)

    @pl.when(jnp.logical_not(is_atmos))
    def _():
        levels = channels // 2
        lines = 2 * channels
        even_x = row_group % 2 == 0
        even_y = col_group % 2 == 0
        wet = wet_ref[...].astype(f32)
        wet = jnp.concatenate([wet, wet], axis=0).astype(bf16)

        def put(out, last):
            @pl.when(last)
            def _():
                out[0:lines, :] = x_ref[0, rows - 2 :].reshape(lines, columns).astype(bf16)

            @pl.when(jnp.logical_not(last))
            def _():
                out[0:lines, :] = x_ref[0, :2].reshape(lines, columns).astype(bf16)

            out[lines : lines + 16, :] = wet

        put(e1_ref, even_x)
        put(e3_ref, jnp.logical_not(even_x))

        def put_edges(out, level):
            for r in range(rows):
                for t in range(2):
                    at = (r * 2 + t) * 2
                    c = t * levels + level
                    edge_ref[at : at + 2, :] = x_ref[0, r, c : c + 2, :]
            out[...] = edge_ref[...].astype(bf16)

        @pl.when(even_y)
        def _():
            put_edges(e2_ref, levels - 2)
            put_edges(e4_ref, 0)

        @pl.when(jnp.logical_not(even_y))
        def _():
            put_edges(e2_ref, 0)
            put_edges(e4_ref, levels - 2)


def regrid_kernel(
    surface_ref, a_src, a_dst, a_count, a_weight, m_src, m_dst, m_count, m_weight,
    _, __,
    land_ref, sent_ref, weight_ref, gath_ref, val_ref, sem,
):
    is_atmos = lax.axis_index("comp") == 0
    blocks, points = val_ref.shape
    cells = surface_ref.shape[0]
    rows = 8

    @pl.when(is_atmos)
    def _():
        pltpu.make_async_copy(m_weight.at[0, 0], weight_ref, sem).start()

    @pl.when(jnp.logical_not(is_atmos))
    def _():
        pltpu.make_async_copy(a_weight.at[0, 0], weight_ref, sem).start()

    src = jnp.where(is_atmos, m_src[0, 0], a_src[0, 0])
    dst = jnp.where(is_atmos, m_dst[0, 0], a_dst[0, 0])
    count = jnp.where(is_atmos, m_count[0, 0], a_count[0, 0])
    tiles = cells // rows

    def split(index):
        row = index // (tiles * LANES)
        tile = (index // LANES) % tiles
        return tile * rows + row, index % LANES

    src_row, src_lane = split(src)
    dst_row, dst_lane = split(dst)
    lane_iota = lax.broadcasted_iota(jnp.int32, (LANES, points), 0)
    row_iota = lax.broadcasted_iota(jnp.int32, (cells, points), 0)
    table = surface_ref[...]
    for b in range(blocks):
        hot = jnp.where(lane_iota == src_lane[b : b + 1], 1.0, 0.0).astype(bf16)
        picked = jnp.dot(table, hot, preferred_element_type=f32)
        picked = jnp.where(row_iota == src_row[b : b + 1], picked, 0.0)
        gath_ref[b : b + 1, :] = jnp.sum(picked, axis=0, keepdims=True)
    gathered = gath_ref[...].astype(bf16)

    @pl.when(is_atmos)
    def _():
        pltpu.make_async_copy(m_weight.at[0, 0], weight_ref, sem).wait()

    @pl.when(jnp.logical_not(is_atmos))
    def _():
        pltpu.make_async_copy(a_weight.at[0, 0], weight_ref, sem).wait()

    block_iota = lax.broadcasted_iota(jnp.int32, (blocks, points), 0)
    values = jnp.zeros((blocks, points), f32)
    for b in range(blocks):
        term = lax.dot_general(
            gathered, weight_ref[b], (((1,), (1,)), ((), ())), preferred_element_type=f32
        )
        values = jnp.where(block_iota == b, term, values)
    val_ref[...] = jnp.where(block_iota < count, values, 0.0)
    land = jnp.zeros((2 * cells, LANES), f32)
    for b in range(blocks):
        value = val_ref[b : b + 1, :]
        coarse = value.astype(bf16).astype(f32)
        fine = value - coarse
        mine = row_iota == dst_row[b : b + 1]
        both = jnp.concatenate(
            [jnp.where(mine, coarse, 0.0), jnp.where(mine, fine, 0.0)], axis=0
        ).astype(bf16)
        hot = jnp.where(lane_iota == dst_lane[b : b + 1], 1.0, 0.0).astype(bf16)
        land = land + lax.dot_general(
            both, hot, (((1,), (1,)), ((), ())), preferred_element_type=f32
        )
    land = land[:cells] + land[cells:]
    land_ref[...] = land
    sent_ref[...] = land.astype(bf16)


def heat_kernel(rows, e2_ref, e4_ref, land_ref, part_ref, sum_ref, near_ref, far_ref):
    cells = land_ref.shape[0]
    columns = cells // rows * LANES
    even_x = lax.axis_index("gx") % 2 == 0
    even_y = lax.axis_index("gy") % 2 == 0
    total = land_ref[...] + part_ref[...].astype(f32)
    sum_ref[...] = total

    def corners(row):
        start = row * 4 // 16 * 16
        one = e2_ref[start : start + 16, :].astype(f32)
        two = e4_ref[start : start + 16, :].astype(f32)
        low = jnp.where(even_y, two, one)
        high = jnp.where(even_y, one, two)
        at = row * 4 - start
        lines = [low[at + 1 : at + 2], low[at + 3 : at + 4], high[at : at + 1], high[at + 2 : at + 3]]
        return to_tiles(jnp.concatenate(lines + [jnp.zeros((4, columns), f32)], axis=0))

    first, last = corners(0), corners(rows - 1)
    near_ref[0:cells, :] = total.astype(bf16)
    far_ref[0:cells, :] = total.astype(bf16)
    near_ref[cells:, :] = jnp.where(even_x, last, first).astype(bf16)
    far_ref[cells:, :] = jnp.where(even_x, first, last).astype(bf16)


def steps_kernel(
    groups_x, groups_y, paired, x_ref, wet_ref, diff_ref, y_ref, e1_ref, e3_ref,
    e2_ref, e4_ref, *refs,
):
    if not paired:
        pin_ref, qin_ref = refs[:2]
    base_ref, zb_ref, c_ref, z_ref, t0_ref, t1_ref, w_ref = refs[-7:]
    _, rows, channels, columns = x_ref.shape
    row_group = lax.axis_index("gx")
    col_group = lax.axis_index("gy")
    is_atmos = lax.axis_index("comp") == 0

    @pl.when(is_atmos)
    def _():
        diff = channel_column(diff_ref[...], channels, col_group * channels)
        total = rows * groups_x
        base = (row_group * rows).astype(f32)
        for group, n, parts in wave_parts(columns):
            lam, alpha, sinh = decay_terms(diff, half_rates(group, n, LANES, columns))
            lam2 = lam * lam
            low = jnp.exp(-2.0 * base * alpha)
            high = jnp.exp(-2.0 * (total - rows - base) * alpha)
            scale = 1.0 / (
                2.0 * diff * sinh * (1.0 - jnp.exp(-2.0 * (total + 1) * alpha))
            )
            lows, highs = [], []
            power = low
            for r in range(rows):
                power = power * lam2
                lows.append(1.0 - power)
            power = high
            for r in range(rows):
                power = power * lam2
                highs.append(1.0 - power)
            highs = highs[::-1]
            for part in parts:
                lanes = slice(part, part + LANES)
                if paired:
                    pin = jnp.zeros((channels, LANES), f32)
                    qin = jnp.zeros((channels, LANES), f32)
                    for mask, msg in ((1, e1_ref), (2, e2_ref), (3, e3_ref)):
                        band = row_group ^ mask
                        gap = (jnp.abs(row_group - band) - 1) * rows
                        term = jnp.exp(-gap.astype(f32) * alpha)
                        term = term * msg[0:channels, lanes].astype(f32)
                        pin = pin + jnp.where(band < row_group, term, 0.0)
                        qin = qin + jnp.where(band > row_group, term, 0.0)
                else:
                    pin = pin_ref[:, lanes]
                    qin = qin_ref[:, lanes]
                f = pin
                for r in range(rows):
                    f = lam * f + lows[r] * y_ref[r, :, lanes]
                    z_ref[r] = highs[r] * f
                g = lam * qin
                for r in reversed(range(rows)):
                    z = scale * (z_ref[r] + lows[r] * g)
                    zb_ref[r * channels : (r + 1) * channels, lanes] = z.astype(bf16)
                    g = lam * (g + highs[r] * y_ref[r, :, lanes])

    @pl.when(jnp.logical_not(is_atmos))
    def _():
        levels = channels // 2
        ring = levels + 8
        lines = 2 * channels
        first_x = row_group == 0
        last_x = row_group == groups_x - 1
        top = col_group == 0
        bottom = col_group == groups_y - 1
        even_x = row_group % 2 == 0
        even_y = col_group % 2 == 0

        one = e1_ref[lines : lines + 16, :].astype(f32)
        three = e3_ref[lines : lines + 16, :].astype(f32)
        below = jnp.where(even_x, three, one)[rows - 2 : rows]
        above = jnp.where(even_x, one, three)[0:2]
        w_ref[0:2, :] = jnp.where(first_x, 0.0, below)
        w_ref[2 : rows + 2, :] = wet_ref[...].astype(f32)
        w_ref[rows + 2 : rows + 4, :] = jnp.where(last_x, 0.0, above)

        span = rows + 2
        north = w_ref[0:span, :]
        here = w_ref[1 : span + 1, :]
        south = w_ref[2 : span + 2, :]
        west = pltpu.roll(here, 1, 1)
        east = pltpu.roll(here, columns - 1, 1)
        c_ref[0, 0:span, :] = here * (
            1.0 - 2.0 * mixing_rate - spread_rate * (north + south + west + east)
        )
        c_ref[1, 0:span, :] = spread_rate * here * north
        c_ref[2, 0:span, :] = spread_rate * here * south
        c_ref[3, 0:span, :] = spread_rate * here * west
        c_ref[4, 0:span, :] = spread_rate * here * east
        c_ref[5, 0:span, :] = mixing_rate * here
        c_ref[6, 0:span, :] = here

        one = e1_ref[0:lines, :].astype(f32)
        three = e3_ref[0:lines, :].astype(f32)
        below = jnp.where(even_x, three, one)
        above = jnp.where(even_x, one, three)
        blank = jnp.zeros((8, columns), f32)
        for k in range(2):
            for t in range(2):
                c = k * channels + t * levels
                t0_ref[k, t, 0:levels, :] = below[c : c + levels]
                t0_ref[rows + 2 + k, t, 0:levels, :] = above[c : c + levels]
                t0_ref[k, t, levels:ring, :] = blank
                t0_ref[rows + 2 + k, t, levels:ring, :] = blank
        one = e2_ref[...].astype(f32)
        two = e4_ref[...].astype(f32)
        before = jnp.where(even_y, two, one)
        after = jnp.where(even_y, one, two)
        for r in range(rows):
            for t in range(2):
                k = (r * 2 + t) * 2
                t0_ref[r + 2, t, 0:levels, :] = x_ref[0, r, t * levels : (t + 1) * levels, :]
                t0_ref[r + 2, t, levels : levels + 2, :] = after[k : k + 2]
                t0_ref[r + 2, t, ring - 2 : ring, :] = before[k : k + 2]

        def close(ref, r):
            for t in range(2):
                ref[r, t, ring - 1 : ring, :] = jnp.where(
                    top, ref[r, t, 0:1, :], ref[r, t, ring - 1 : ring, :]
                )
                ref[r, t, levels : levels + 1, :] = jnp.where(
                    bottom, ref[r, t, levels - 1 : levels, :], ref[r, t, levels : levels + 1, :]
                )

        def advance(ref, r, t, coefs, size):
            whole = ref[r, t]
            up = pltpu.roll(whole, 1, 0)[:size]
            down = pltpu.roll(whole, ring - 1, 0)[:size]
            mid = whole[:size]
            total = coefs[0] * mid + coefs[5] * (up + down)
            total = total + coefs[1] * ref[r - 1, t, 0:size, :]
            total = total + coefs[2] * ref[r + 1, t, 0:size, :]
            total = total + coefs[3] * pltpu.roll(mid, 1, 1)
            return total + coefs[4] * pltpu.roll(mid, columns - 1, 1)

        def first(r, carry):
            coefs = [c_ref[k, pl.ds(r, 1), :] for k in range(6)]
            close(t0_ref, r + 1)
            for t in range(2):
                t1_ref[r, t] = advance(t0_ref, r + 1, t, coefs, ring)
            close(t1_ref, r)
            return carry

        lax.fori_loop(0, span, first, 0)

        def second(r, carry):
            coefs = [c_ref[k, pl.ds(r, 1), :] for k in range(6)]
            for t in range(2):
                c = t * levels
                base_ref[r - 1, c : c + levels, :] = advance(t1_ref, r, t, coefs, levels)
            return carry

        lax.fori_loop(1, span - 1, second, 0)


def last_kernel(
    groups_x, groups_y, gain_ref, table_ref, base_ref, zb_ref, c_ref, sum_ref, near_ref,
    far_ref, out_ref, e_ref,
):
    _, rows, channels, columns = out_ref.shape
    row_group = lax.axis_index("gx")
    col_group = lax.axis_index("gy")
    is_atmos = lax.axis_index("comp") == 0

    @pl.when(is_atmos)
    def _():
        response = channel_column(gain_ref[...], channels, col_group * channels)
        forcing = from_tiles(sum_ref[...], rows)
        half = columns // 2
        step = 256
        for n in range(0, half, step):
            even, odd = [
                jnp.dot(
                    zb_ref[:, k * half : (k + 1) * half],
                    table_ref[k * half : (k + 1) * half, n : n + step],
                    preferred_element_type=f32,
                ).reshape(rows, channels, step)
                for k in range(2)
            ]
            for r in range(rows):
                for lane, part in ((n, even[r] + odd[r]), (n + half, even[r] - odd[r])):
                    out_ref[0, r, :, lane : lane + step] = (
                        part + response * forcing[r : r + 1, lane : lane + step]
                    )

    @pl.when(jnp.logical_not(is_atmos))
    def _():
        out_ref[0] = base_ref[...]
        levels = channels // 2
        cells = sum_ref.shape[0]
        even = row_group % 2 == 0
        below = jnp.where(even, far_ref[...].astype(f32), near_ref[...].astype(f32))
        above = jnp.where(even, near_ref[...].astype(f32), far_ref[...].astype(f32))

        low = from_tiles(below[cells:], 8)
        high = from_tiles(above[cells:], 8)
        by_low = c_ref[1, 1:2, :] * (c_ref[5, 0:1, :] + c_ref[5, 1:2, :])
        by_high = c_ref[2, rows : rows + 1, :] * (
            c_ref[5, rows : rows + 1, :] + c_ref[5, rows + 1 : rows + 2, :]
        )
        has_before = jnp.where(col_group > 0, 1.0, 0.0)
        has_after = jnp.where(col_group < groups_y - 1, 1.0, 0.0)
        for t in range(2):
            for r, factor, lines in ((0, by_low, low), (rows - 1, by_high, high)):
                c = t * levels
                out_ref[0, r, c : c + 1, :] = out_ref[0, r, c : c + 1, :] + (
                    has_before * factor * lines[t : t + 1]
                )
                c = c + levels - 1
                out_ref[0, r, c : c + 1, :] = out_ref[0, r, c : c + 1, :] + (
                    has_after * factor * lines[t + 2 : t + 3]
                )

        @pl.when(col_group == 0)
        def _():
            span = rows + 2
            e_ref[0:1, :] = from_tiles(below[:cells], rows)[rows - 1 : rows]
            e_ref[1 : rows + 1, :] = from_tiles(sum_ref[...], rows)
            e_ref[rows + 1 : span, :] = from_tiles(above[:cells], rows)[0:1]
            e_ref[0:span, :] = c_ref[6, 0:span, :] * e_ref[0:span, :]
            own = slice(1, rows + 1)
            heat = e_ref[own, :]
            second = c_ref[5, own, :] * heat
            first = (c_ref[0, own, :] + 1.0) * heat + second
            first = first + c_ref[1, own, :] * e_ref[0:rows, :]
            first = first + c_ref[2, own, :] * e_ref[2 : rows + 2, :]
            first = first + c_ref[3, own, :] * pltpu.roll(heat, 1, 1)
            first = first + c_ref[4, own, :] * pltpu.roll(heat, columns - 1, 1)
            for t, gain in enumerate((heat_gain, salt_gain)):
                c = t * levels
                for r in range(rows):
                    lines = jnp.concatenate([first[r : r + 1], second[r : r + 1]], axis=0)
                    out_ref[0, r, c : c + 2, :] = out_ref[0, r, c : c + 2, :] + gain * lines


def local(
    fields,
    wet_cells,
    flux_weight,
    variable_sea_response,
    diffusivity,
    a2o_source,
    a2o_target,
    a2o_count,
    a2o_weight,
    marine_air_input_index,
    marine_air_output_index,
    marine_air_piece_tally,
    marine_air_piece_factor,
):
    _, rows, channels, columns = fields.shape
    groups_x = lax.axis_size("gx")
    groups_y = lax.axis_size("gy")
    blocks, points = a2o_source.shape[2:]
    cells = rows * columns // LANES
    forward, inverse = fourier_tables(columns)
    flux_row = flux_weight[None, :]
    gain_row = variable_sea_response[None, :]
    diff_row = diffusivity[None, :]
    paired = groups_x == 4
    params = functools.partial(pltpu.CompilerParams, vmem_limit_bytes=40 * 2**20)
    vmem = pl.BlockSpec(memory_space=pltpu.VMEM)
    smem = pl.BlockSpec(memory_space=pltpu.SMEM)
    hbm = pl.BlockSpec(memory_space=pltpu.HBM)
    anywhere = pl.BlockSpec(memory_space=pl.ANY)

    def shape(dims, dtype):
        return jax.ShapeDtypeStruct(dims, dtype)

    partial_surface, coarse = pl.pallas_call(
        surface_kernel,
        out_shape=[shape((cells, LANES), f32), shape((cells, LANES), bf16)],
        in_specs=[hbm, hbm],
        out_specs=[vmem, vmem],
        scratch_shapes=[
            pltpu.VMEM((rows, channels, columns), f32),
            pltpu.VMEM(flux_row.shape, f32),
            pltpu.VMEM((rows, columns), f32),
            pltpu.SemaphoreType.DMA((rows,)),
            pltpu.SemaphoreType.DMA,
        ],
        compiler_params=pltpu.CompilerParams(vmem_limit_bytes=58 * 2**20),
        name="surface_partials",
    )(fields, flux_row)

    lines = 2 * channels + 16
    shapes = [
        shape((cells, LANES), f32),
        shape((rows, channels, columns), f32),
        shape((lines, columns), bf16),
        shape((lines, columns), bf16),
        shape((4 * rows, columns), bf16),
        shape((4 * rows, columns), bf16),
    ]
    if not paired:
        shapes.append(shape((2, channels, columns), bf16))
    partial_surface, y, e1, e3, e2, e4, *sums = pl.pallas_call(
        functools.partial(forward_kernel, groups_x, paired),
        out_shape=shapes,
        in_specs=[vmem] * 5,
        out_specs=[vmem] * len(shapes),
        scratch_shapes=[
            pltpu.VMEM((rows * channels, columns), bf16),
            pltpu.VMEM((4 * rows, columns), f32),
        ],
        compiler_params=params(),
        name="forward_or_halos",
    )(fields, wet_cells, diff_row, forward, partial_surface)

    def sum_masks():
        mask = 1
        while mask < groups_y:
            yield [(j, j ^ mask) for j in range(groups_y)]
            mask *= 2

    surface = partial_surface
    for route in sum_masks():
        surface = surface + lax.ppermute(coarse, "gy", route).astype(f32)
        coarse = surface.astype(bf16)
    surface = lax.ppermute(coarse, "comp", [(0, 1), (1, 0)])

    def ring_pairs(count, odd):
        return [(a, (a + 1) % count) for a in range(odd, count, 2)]

    def flat(comp, i, j):
        return (comp * groups_x + i) * groups_y + j

    def level_route(odd):
        pairs = []
        for i in range(groups_x):
            for a, b in ring_pairs(groups_y, odd):
                pairs.append((flat(1, i, a), flat(1, i, b)))
                if odd or not paired:
                    pairs.append((flat(0, i, a), flat(0, i, b)))
            if paired and not odd and i < i ^ 2:
                pairs += [(flat(0, i, j), flat(0, i ^ 2, j)) for j in range(groups_y)]
        return both_ways(pairs)

    e1 = lax.ppermute(e1, "gx", both_ways(ring_pairs(groups_x, 0)))
    e3 = lax.ppermute(e3, "gx", both_ways(ring_pairs(groups_x, 1)))
    axes = ("comp", "gx", "gy")
    e2 = lax.ppermute(e2, axes, level_route(0))
    e4 = lax.ppermute(e4, axes, level_route(1))

    landing, sent = pl.pallas_call(
        regrid_kernel,
        out_shape=[shape((cells, LANES), f32), shape((cells, LANES), bf16)],
        in_specs=[vmem, vmem, vmem, smem, hbm, vmem, vmem, smem, hbm, anywhere, anywhere],
        out_specs=[vmem] * 2,
        scratch_shapes=[
            pltpu.VMEM((blocks, points, points), bf16),
            pltpu.VMEM((blocks, points), f32),
            pltpu.VMEM((blocks, points), f32),
            pltpu.SemaphoreType.DMA,
        ],
        compiler_params=params(),
        name="regrid_blocks",
    )(
        surface,
        a2o_source, a2o_target, a2o_count, a2o_weight,
        marine_air_input_index, marine_air_output_index,
        marine_air_piece_tally, marine_air_piece_factor, e1, e3,
    )
    *early, final = sum_masks()
    for route in early:
        landing = landing + lax.ppermute(sent, "gy", route).astype(f32)
        sent = landing.astype(bf16)
    part = lax.ppermute(sent, "gy", final)

    extra = []
    if not paired:
        p, q = jnp.moveaxis(lax.all_gather(sums[0], "gx").astype(f32), 1, 0)
        viscous = lax.dynamic_slice_in_dim(
            diffusivity, lax.axis_index("gy") * channels, channels
        )[:, None]
        rates = [half_rates(g, 0, columns // 4, columns) for g in (0, 0, 1, 1)]
        _, alpha, _ = decay_terms(viscous, jnp.concatenate(rates, axis=1))
        gap = lax.axis_index("gx") - jnp.arange(groups_x)
        decay = jnp.exp(
            -(rows * jnp.maximum(jnp.abs(gap) - 1, 0))[:, None, None] * alpha[None]
        )
        extra = [
            jnp.sum(jnp.where((gap > 0)[:, None, None], decay * p, 0.0), axis=0),
            jnp.sum(jnp.where((gap < 0)[:, None, None], decay * q, 0.0), axis=0),
        ]
    ring = channels // 2 + 8
    base, damped, coefs = pl.pallas_call(
        functools.partial(steps_kernel, groups_x, groups_y, paired),
        out_shape=[
            shape((rows, channels, columns), f32),
            shape((rows * channels, columns), bf16),
            shape((7, 16, columns), f32),
        ],
        in_specs=[vmem] * (8 + len(extra)),
        out_specs=[vmem] * 3,
        scratch_shapes=[
            pltpu.VMEM((rows, channels, LANES), f32),
            pltpu.VMEM((rows + 4, 2, ring, columns), f32),
            pltpu.VMEM((rows + 2, 2, ring, columns), f32),
            pltpu.VMEM((16, columns), f32),
        ],
        compiler_params=params(),
        name="damping_or_ocean_steps",
    )(fields, wet_cells, diff_row, y, e1, e3, e2, e4, *extra)

    surface_sum, near, far = pl.pallas_call(
        functools.partial(heat_kernel, rows),
        out_shape=[
            shape((cells, LANES), f32),
            shape((cells + columns // 16, LANES), bf16),
            shape((cells + columns // 16, LANES), bf16),
        ],
        in_specs=[vmem] * 4,
        out_specs=[vmem] * 3,
        compiler_params=params(),
        name="surface_sum",
    )(e2, e4, landing, part)

    near = lax.ppermute(near, "gx", both_ways(ring_pairs(groups_x, 0)))
    far = lax.ppermute(far, "gx", both_ways(ring_pairs(groups_x, 1)))
    return pl.pallas_call(
        functools.partial(last_kernel, groups_x, groups_y),
        out_shape=shape(fields.shape, f32),
        in_specs=[vmem] * 8,
        out_specs=vmem,
        scratch_shapes=[pltpu.VMEM((16, columns), f32)],
        compiler_params=params(),
        name="inverse_or_heat",
    )(gain_row, inverse, base, damped, coefs, surface_sum, near, far)


def solution(mesh):
    in_specs = (
        P("comp", "gx", "gy", None),
        P("gx", None),
        P(),
        P(),
        P(),
        P("gx", "gy", None, None),
        P("gx", "gy", None, None),
        P("gx", "gy"),
        P("gx", "gy", None, None, None),
        P("gx", "gy", None, None),
        P("gx", "gy", None, None),
        P("gx", "gy"),
        P("gx", "gy", None, None, None),
    )
    out_specs = P("comp", "gx", "gy", None)
    return jax.shard_map(local, mesh=mesh, in_specs=in_specs, out_specs=out_specs, check_vma=False)
```

```python
import functools

import jax
import jax.numpy as jnp
import numpy as np
from jax import lax
from jax.experimental import pallas as pl
from jax.experimental.pallas import tpu as pltpu
from jax.sharding import PartitionSpec as P

spread_rate = 0.2
mixing_rate = 0.1
heat_gain = 0.5
salt_gain = -0.25
LANES = 128
f32 = jnp.float32
bf16 = jnp.bfloat16


def fourier_tables(columns):
    half = columns // 2
    forward, inverse = [], []
    for first in (0, 1):
        waves = np.arange(first, half, 2)
        phase = np.arange(half)[:, None] * waves[None, :] % columns
        angles = phase * (2.0 * np.pi / columns)
        table = np.concatenate([np.cos(angles), np.sin(angles)], axis=1)
        weight = np.where(waves == 0, 1.0, 2.0) / columns
        forward.append(table)
        inverse.append(table.T * np.concatenate([weight, weight])[:, None])
    return (
        jnp.asarray(np.concatenate(forward).astype(np.float32), bf16),
        jnp.asarray(np.concatenate(inverse).astype(np.float32), bf16),
    )


def wave_parts(columns):
    quarter = columns // 4
    return [
        (g, n, (g * 2 * quarter + n, (g * 2 + 1) * quarter + n))
        for g in (0, 1)
        for n in range(0, quarter, LANES)
    ]


def half_rates(group, first, count, columns):
    lane = lax.broadcasted_iota(jnp.int32, (1, count), 1) + first
    wave = (2 * lane + group).astype(f32)
    sine = jnp.sin(wave * (np.pi / columns))
    return 2.0 * sine * sine


def both_ways(pairs):
    return [p for a, b in pairs for p in ((a, b), (b, a))]


def channel_column(row, channels, first):
    n = row.shape[1]
    lane = lax.broadcasted_iota(jnp.int32, (channels, n), 1)
    sub = lax.broadcasted_iota(jnp.int32, (channels, n), 0)
    return jnp.sum(jnp.where(lane == sub + first, row, 0.0), axis=1, keepdims=True)


def to_tiles(surface):
    cols = surface.shape[1]
    return jnp.concatenate(
        [surface[:, k : k + LANES] for k in range(0, cols, LANES)], axis=0
    )


def from_tiles(tiles, rows):
    return jnp.concatenate(
        [tiles[k : k + rows] for k in range(0, tiles.shape[0], rows)], axis=1
    )


def decay_terms(diff_column, rates):
    half = 0.5 / diff_column + rates
    sinh = jnp.sqrt(half * (half + 2.0))
    grow = 1.0 + half + sinh
    return 1.0 / grow, jnp.log(grow), sinh


def surface_kernel(x_hbm, flux_hbm, s_ref, coarse_ref, x_ref, flux_ref, row_ref, x_sem, sem):
    rows, channels, columns = x_ref.shape
    col_group = lax.axis_index("gy")
    is_atmos = lax.axis_index("comp") == 0
    flux_copy = pltpu.make_async_copy(flux_hbm, flux_ref, sem)
    copies = [
        pltpu.make_async_copy(x_hbm.at[0, r], x_ref.at[r], x_sem.at[r]) for r in range(rows)
    ]

    @pl.when(is_atmos)
    def _():
        for copy in [flux_copy] + copies:
            copy.start()
        flux_copy.wait()
        weight = channel_column(flux_ref[...], channels, col_group * channels)
        for r in range(rows):
            copies[r].wait()
            row_ref[r : r + 1, :] = jnp.sum(x_ref[r] * weight, axis=0, keepdims=True)

    @pl.when(jnp.logical_not(is_atmos))
    def _():
        top = [
            pltpu.make_async_copy(
                x_hbm.at[0, r, pl.ds(0, 8)], x_ref.at[r, pl.ds(0, 8)], x_sem.at[r]
            )
            for r in range(rows)
        ]
        for copy in top:
            copy.start()
        gain = jnp.where(col_group == 0, 1.0, 0.0)
        for r in range(rows):
            top[r].wait()
            row_ref[r : r + 1, :] = x_ref[r, 0:1, :] * gain

    surface = to_tiles(row_ref[...])
    s_ref[...] = surface
    coarse_ref[...] = surface.astype(bf16)


def forward_kernel(
    groups_x, paired, x_hbm, wet_hbm, diff_hbm, table_hbm, s_hbm, kept_hbm, *refs
):
    del s_hbm, kept_hbm
    outs = 5 if paired else 6
    y_hbm, *message_hbm = refs[:outs]
    y_ref, *message_ref = refs[outs : 2 * outs]
    e1_ref, e3_ref, e2_ref, e4_ref = message_ref[:4]
    if not paired:
        pq_ref = message_ref[4]
    x_ref, wet_ref, diff_ref, table_ref, flat_ref, edge_ref, sem, out_sem = refs[2 * outs :]
    rows, channels, columns = x_ref.shape
    half = columns // 2
    row_group = lax.axis_index("gx")
    col_group = lax.axis_index("gy")
    is_atmos = lax.axis_index("comp") == 0

    x_copy = pltpu.make_async_copy(x_hbm.at[0], x_ref, sem.at[0])
    y_copies = [
        pltpu.make_async_copy(y_ref.at[r], y_hbm.at[r], out_sem.at[r]) for r in range(rows)
    ]
    message_copies = [
        pltpu.make_async_copy(ref, hbm, out_sem.at[rows + k])
        for k, (ref, hbm) in enumerate(zip(message_ref, message_hbm))
    ]

    @pl.when(is_atmos)
    def _():
        table_copy = pltpu.make_async_copy(table_hbm, table_ref, sem.at[1])
        diff_copy = pltpu.make_async_copy(diff_hbm, diff_ref, sem.at[2])
        for copy in (x_copy, table_copy, diff_copy):
            copy.start()
        x_copy.wait()
        first = col_group * channels
        for r in range(rows):
            left, right = x_ref[r, :, :half], x_ref[r, :, half:]
            flat_ref[r * channels : (r + 1) * channels, :half] = (left + right).astype(bf16)
            flat_ref[r * channels : (r + 1) * channels, half:] = (left - right).astype(bf16)
        table_copy.wait()
        for k in range(2):
            lanes = slice(k * half, (k + 1) * half)
            part = jnp.dot(
                flat_ref[:, lanes], table_ref[lanes, :], preferred_element_type=f32
            )
            y_ref[:, :, lanes] = part.reshape(rows, channels, half)
        for copy in y_copies:
            copy.start()
        diff_copy.wait()
        diff = channel_column(diff_ref[...], channels, first)
        total = rows * groups_x
        base = (row_group * rows).astype(f32)
        for group, n, parts in wave_parts(columns):
            lam, alpha, _ = decay_terms(diff, half_rates(group, n, LANES, columns))
            lam2 = lam * lam
            low = jnp.exp(-2.0 * base * alpha)
            high = jnp.exp(-2.0 * (total - rows - base) * alpha)
            for part in parts:
                lanes = slice(part, part + LANES)
                power = low
                p = jnp.zeros((channels, LANES), f32)
                for r in range(rows):
                    power = power * lam2
                    p = lam * p + (1.0 - power) * y_ref[r, :, lanes]
                power = high
                q = jnp.zeros((channels, LANES), f32)
                for r in reversed(range(rows)):
                    power = power * lam2
                    q = lam * q + (1.0 - power) * y_ref[r, :, lanes]
                if paired:
                    for mask, out in ((1, e1_ref), (2, e2_ref), (3, e3_ref)):
                        upward = row_group < (row_group ^ mask)
                        out[0:channels, lanes] = jnp.where(upward, p, q).astype(bf16)
                else:
                    pq_ref[0, :, lanes] = p.astype(bf16)
                    pq_ref[1, :, lanes] = q.astype(bf16)
        for copy in message_copies:
            copy.start()
        for copy in y_copies + message_copies:
            copy.wait()

    @pl.when(jnp.logical_not(is_atmos))
    def _():
        wet_copy = pltpu.make_async_copy(wet_hbm, wet_ref, sem.at[1])
        for copy in (x_copy, wet_copy):
            copy.start()
        x_copy.wait()
        wet_copy.wait()
        levels = channels // 2
        lines = 2 * channels
        even_x = row_group % 2 == 0
        even_y = col_group % 2 == 0
        wet = wet_ref[...].astype(f32)
        wet = jnp.concatenate([wet, wet], axis=0).astype(bf16)

        def put(out, last):
            @pl.when(last)
            def _():
                out[0:lines, :] = x_ref[rows - 2 :].reshape(lines, columns).astype(bf16)

            @pl.when(jnp.logical_not(last))
            def _():
                out[0:lines, :] = x_ref[:2].reshape(lines, columns).astype(bf16)

            out[lines : lines + 16, :] = wet

        put(e1_ref, even_x)
        put(e3_ref, jnp.logical_not(even_x))

        def put_edges(out, level):
            for r in range(rows):
                for t in range(2):
                    at = (r * 2 + t) * 2
                    c = t * levels + level
                    edge_ref[at : at + 2, :] = x_ref[r, c : c + 2, :]
            out[...] = edge_ref[...].astype(bf16)

        @pl.when(even_y)
        def _():
            put_edges(e2_ref, levels - 2)
            put_edges(e4_ref, 0)

        @pl.when(jnp.logical_not(even_y))
        def _():
            put_edges(e2_ref, 0)
            put_edges(e4_ref, levels - 2)

        for copy in message_copies:
            copy.start()
        for copy in message_copies:
            copy.wait()


def regrid_kernel(n_surfaces, *refs):
    surfaces = refs[:n_surfaces]
    (
        a_src, a_dst, a_count, a_weight, m_src, m_dst, m_count, m_weight,
        _, _,
        land_ref, sent_ref, weight_ref, gath_ref, val_ref, sem,
    ) = refs[n_surfaces:]
    is_atmos = lax.axis_index("comp") == 0
    blocks, points = val_ref.shape
    cells = surfaces[0].shape[0]
    rows = 8

    @pl.when(is_atmos)
    def _():
        pltpu.make_async_copy(m_weight.at[0, 0], weight_ref, sem).start()

    @pl.when(jnp.logical_not(is_atmos))
    def _():
        pltpu.make_async_copy(a_weight.at[0, 0], weight_ref, sem).start()

    src = jnp.where(is_atmos, m_src[0, 0], a_src[0, 0])
    dst = jnp.where(is_atmos, m_dst[0, 0], a_dst[0, 0])
    count = jnp.where(is_atmos, m_count[0, 0], a_count[0, 0])
    tiles = cells // rows

    def split(index):
        row = index // (tiles * LANES)
        tile = (index // LANES) % tiles
        return tile * rows + row, index % LANES

    src_row, src_lane = split(src)
    dst_row, dst_lane = split(dst)
    lane_iota = lax.broadcasted_iota(jnp.int32, (LANES, points), 0)
    row_iota = lax.broadcasted_iota(jnp.int32, (cells, points), 0)
    table = sum(surface[...].astype(f32) for surface in surfaces).astype(bf16)
    for b in range(blocks):
        hot = jnp.where(lane_iota == src_lane[b : b + 1], 1.0, 0.0).astype(bf16)
        picked = jnp.dot(table, hot, preferred_element_type=f32)
        picked = jnp.where(row_iota == src_row[b : b + 1], picked, 0.0)
        gath_ref[b : b + 1, :] = jnp.sum(picked, axis=0, keepdims=True)
    gathered = gath_ref[...].astype(bf16)

    @pl.when(is_atmos)
    def _():
        pltpu.make_async_copy(m_weight.at[0, 0], weight_ref, sem).wait()

    @pl.when(jnp.logical_not(is_atmos))
    def _():
        pltpu.make_async_copy(a_weight.at[0, 0], weight_ref, sem).wait()

    block_iota = lax.broadcasted_iota(jnp.int32, (blocks, points), 0)
    values = jnp.zeros((blocks, points), f32)
    for b in range(blocks):
        term = lax.dot_general(
            gathered, weight_ref[b], (((1,), (1,)), ((), ())), preferred_element_type=f32
        )
        values = jnp.where(block_iota == b, term, values)
    val_ref[...] = jnp.where(block_iota < count, values, 0.0)
    land = jnp.zeros((2 * cells, LANES), f32)
    for b in range(blocks):
        value = val_ref[b : b + 1, :]
        coarse = value.astype(bf16).astype(f32)
        fine = value - coarse
        mine = row_iota == dst_row[b : b + 1]
        both = jnp.concatenate(
            [jnp.where(mine, coarse, 0.0), jnp.where(mine, fine, 0.0)], axis=0
        ).astype(bf16)
        hot = jnp.where(lane_iota == dst_lane[b : b + 1], 1.0, 0.0).astype(bf16)
        land = land + lax.dot_general(
            both, hot, (((1,), (1,)), ((), ())), preferred_element_type=f32
        )
    land = land[:cells] + land[cells:]
    land_ref[...] = land
    sent_ref[...] = land.astype(bf16)


def heat_kernel(rows, e2_ref, e4_ref, land_ref, part_ref, _, sum_ref, near_ref, far_ref):
    cells = land_ref.shape[0]
    columns = cells // rows * LANES
    even_x = lax.axis_index("gx") % 2 == 0
    even_y = lax.axis_index("gy") % 2 == 0
    total = land_ref[...] + part_ref[...].astype(f32)
    sum_ref[...] = total

    def corners(row):
        start = row * 4 // 16 * 16
        one = e2_ref[start : start + 16, :].astype(f32)
        two = e4_ref[start : start + 16, :].astype(f32)
        low = jnp.where(even_y, two, one)
        high = jnp.where(even_y, one, two)
        at = row * 4 - start
        lines = [low[at + 1 : at + 2], low[at + 3 : at + 4], high[at : at + 1], high[at + 2 : at + 3]]
        return to_tiles(jnp.concatenate(lines + [jnp.zeros((4, columns), f32)], axis=0))

    first, last = corners(0), corners(rows - 1)
    near_ref[0:cells, :] = total.astype(bf16)
    far_ref[0:cells, :] = total.astype(bf16)
    near_ref[cells:, :] = jnp.where(even_x, last, first).astype(bf16)
    far_ref[cells:, :] = jnp.where(even_x, first, last).astype(bf16)


def advance(ref, r, t, coefs, size):
    ring, columns = ref.shape[2:]
    whole = ref[r, t]
    up = pltpu.roll(whole, 1, 0)[:size]
    down = pltpu.roll(whole, ring - 1, 0)[:size]
    mid = whole[:size]
    total = coefs[0] * mid + coefs[5] * (up + down)
    total = total + coefs[1] * ref[r - 1, t, 0:size, :]
    total = total + coefs[2] * ref[r + 1, t, 0:size, :]
    total = total + coefs[3] * pltpu.roll(mid, 1, 1)
    return total + coefs[4] * pltpu.roll(mid, columns - 1, 1)


def first_step_kernel(
    groups_x, groups_y, paired, x_ref, wet_ref, diff_ref, y_ref, e1_ref, e3_ref,
    e2_ref, e4_ref, *refs,
):
    if not paired:
        pin_ref, qin_ref = refs[:2]
    zb_ref, c_ref, t1_ref, z_ref, t0_ref, w_ref = refs[-6:]
    _, rows, channels, columns = x_ref.shape
    row_group = lax.axis_index("gx")
    col_group = lax.axis_index("gy")
    is_atmos = lax.axis_index("comp") == 0

    @pl.when(is_atmos)
    def _():
        diff = channel_column(diff_ref[...], channels, col_group * channels)
        total = rows * groups_x
        base = (row_group * rows).astype(f32)
        for group, n, parts in wave_parts(columns):
            lam, alpha, sinh = decay_terms(diff, half_rates(group, n, LANES, columns))
            lam2 = lam * lam
            low = jnp.exp(-2.0 * base * alpha)
            high = jnp.exp(-2.0 * (total - rows - base) * alpha)
            scale = 1.0 / (
                2.0 * diff * sinh * (1.0 - jnp.exp(-2.0 * (total + 1) * alpha))
            )
            lows, highs = [], []
            power = low
            for r in range(rows):
                power = power * lam2
                lows.append(1.0 - power)
            power = high
            for r in range(rows):
                power = power * lam2
                highs.append(1.0 - power)
            highs = highs[::-1]
            for part in parts:
                lanes = slice(part, part + LANES)
                if paired:
                    pin = jnp.zeros((channels, LANES), f32)
                    qin = jnp.zeros((channels, LANES), f32)
                    for mask, msg in ((1, e1_ref), (2, e2_ref), (3, e3_ref)):
                        band = row_group ^ mask
                        gap = (jnp.abs(row_group - band) - 1) * rows
                        term = jnp.exp(-gap.astype(f32) * alpha)
                        term = term * msg[0:channels, lanes].astype(f32)
                        pin = pin + jnp.where(band < row_group, term, 0.0)
                        qin = qin + jnp.where(band > row_group, term, 0.0)
                else:
                    pin = pin_ref[:, lanes]
                    qin = qin_ref[:, lanes]
                f = pin
                for r in range(rows):
                    f = lam * f + lows[r] * y_ref[r, :, lanes]
                    z_ref[r] = highs[r] * f
                g = lam * qin
                for r in reversed(range(rows)):
                    z = scale * (z_ref[r] + lows[r] * g)
                    zb_ref[r * channels : (r + 1) * channels, lanes] = z.astype(bf16)
                    g = lam * (g + highs[r] * y_ref[r, :, lanes])

    @pl.when(jnp.logical_not(is_atmos))
    def _():
        levels = channels // 2
        ring = levels + 8
        lines = 2 * channels
        first_x = row_group == 0
        last_x = row_group == groups_x - 1
        top = col_group == 0
        bottom = col_group == groups_y - 1
        even_x = row_group % 2 == 0
        even_y = col_group % 2 == 0

        one = e1_ref[lines : lines + 16, :].astype(f32)
        three = e3_ref[lines : lines + 16, :].astype(f32)
        below = jnp.where(even_x, three, one)[rows - 2 : rows]
        above = jnp.where(even_x, one, three)[0:2]
        w_ref[0:2, :] = jnp.where(first_x, 0.0, below)
        w_ref[2 : rows + 2, :] = wet_ref[...].astype(f32)
        w_ref[rows + 2 : rows + 4, :] = jnp.where(last_x, 0.0, above)

        span = rows + 2
        north = w_ref[0:span, :]
        here = w_ref[1 : span + 1, :]
        south = w_ref[2 : span + 2, :]
        west = pltpu.roll(here, 1, 1)
        east = pltpu.roll(here, columns - 1, 1)
        c_ref[0, 0:span, :] = here * (
            1.0 - 2.0 * mixing_rate - spread_rate * (north + south + west + east)
        )
        c_ref[1, 0:span, :] = spread_rate * here * north
        c_ref[2, 0:span, :] = spread_rate * here * south
        c_ref[3, 0:span, :] = spread_rate * here * west
        c_ref[4, 0:span, :] = spread_rate * here * east
        c_ref[5, 0:span, :] = mixing_rate * here
        c_ref[6, 0:span, :] = here

        one = e1_ref[0:lines, :].astype(f32)
        three = e3_ref[0:lines, :].astype(f32)
        below = jnp.where(even_x, three, one)
        above = jnp.where(even_x, one, three)
        blank = jnp.zeros((8, columns), f32)
        for k in range(2):
            for t in range(2):
                c = k * channels + t * levels
                t0_ref[k, t, 0:levels, :] = below[c : c + levels]
                t0_ref[rows + 2 + k, t, 0:levels, :] = above[c : c + levels]
                t0_ref[k, t, levels:ring, :] = blank
                t0_ref[rows + 2 + k, t, levels:ring, :] = blank
        one = e2_ref[...].astype(f32)
        two = e4_ref[...].astype(f32)
        before = jnp.where(even_y, two, one)
        after = jnp.where(even_y, one, two)
        for r in range(rows):
            for t in range(2):
                k = (r * 2 + t) * 2
                t0_ref[r + 2, t, 0:levels, :] = x_ref[0, r, t * levels : (t + 1) * levels, :]
                t0_ref[r + 2, t, levels : levels + 2, :] = after[k : k + 2]
                t0_ref[r + 2, t, ring - 2 : ring, :] = before[k : k + 2]

        def close(ref, r):
            for t in range(2):
                ref[r, t, ring - 1 : ring, :] = jnp.where(
                    top, ref[r, t, 0:1, :], ref[r, t, ring - 1 : ring, :]
                )
                ref[r, t, levels : levels + 1, :] = jnp.where(
                    bottom, ref[r, t, levels - 1 : levels, :], ref[r, t, levels : levels + 1, :]
                )

        def first(r, carry):
            coefs = [c_ref[k, pl.ds(r, 1), :] for k in range(6)]
            close(t0_ref, r + 1)
            for t in range(2):
                t1_ref[r, t] = advance(t0_ref, r + 1, t, coefs, ring)
            close(t1_ref, r)
            return carry

        lax.fori_loop(0, span, first, 0)


def second_step_kernel(gain_ref, table_ref, zb_ref, c_ref, t1_ref, base_ref, column_ref):
    rows, channels, columns = base_ref.shape
    is_atmos = lax.axis_index("comp") == 0

    @pl.when(is_atmos)
    def _():
        response = channel_column(gain_ref[...], channels, lax.axis_index("gy") * channels)
        column_ref[...] = jnp.broadcast_to(response, column_ref.shape)
        half = columns // 2
        step = 256
        for n in range(0, half, step):
            even, odd = [
                jnp.dot(
                    zb_ref[:, k * half : (k + 1) * half],
                    table_ref[k * half : (k + 1) * half, n : n + step],
                    preferred_element_type=f32,
                ).reshape(rows, channels, step)
                for k in range(2)
            ]
            base_ref[:, :, n : n + step] = even + odd
            base_ref[:, :, n + half : n + half + step] = even - odd

    @pl.when(jnp.logical_not(is_atmos))
    def _():
        levels = channels // 2

        def second(r, carry):
            coefs = [c_ref[k, pl.ds(r, 1), :] for k in range(6)]
            for t in range(2):
                c = t * levels
                base_ref[r - 1, c : c + levels, :] = advance(t1_ref, r, t, coefs, levels)
            return carry

        lax.fori_loop(1, rows + 1, second, 0)


def last_kernel(
    groups_x, groups_y, column_ref, base_ref, c_ref, sum_ref, near_ref, far_ref, out_ref, e_ref
):
    _, rows, channels, columns = out_ref.shape
    row_group = lax.axis_index("gx")
    col_group = lax.axis_index("gy")
    is_atmos = lax.axis_index("comp") == 0

    @pl.when(is_atmos)
    def _():
        for k in range(columns // LANES):
            lanes = slice(k * LANES, (k + 1) * LANES)
            for r in range(rows):
                at = k * rows + r
                out_ref[0, r, :, lanes] = (
                    base_ref[r, :, lanes] + column_ref[...] * sum_ref[at : at + 1, :]
                )

    @pl.when(jnp.logical_not(is_atmos))
    def _():
        out_ref[0] = base_ref[...]
        levels = channels // 2
        cells = sum_ref.shape[0]
        even = row_group % 2 == 0
        below = jnp.where(even, far_ref[...].astype(f32), near_ref[...].astype(f32))
        above = jnp.where(even, near_ref[...].astype(f32), far_ref[...].astype(f32))

        low = from_tiles(below[cells:], 8)
        high = from_tiles(above[cells:], 8)
        by_low = c_ref[1, 1:2, :] * (c_ref[5, 0:1, :] + c_ref[5, 1:2, :])
        by_high = c_ref[2, rows : rows + 1, :] * (
            c_ref[5, rows : rows + 1, :] + c_ref[5, rows + 1 : rows + 2, :]
        )
        has_before = jnp.where(col_group > 0, 1.0, 0.0)
        has_after = jnp.where(col_group < groups_y - 1, 1.0, 0.0)
        for t in range(2):
            for r, factor, lines in ((0, by_low, low), (rows - 1, by_high, high)):
                c = t * levels
                out_ref[0, r, c : c + 1, :] = out_ref[0, r, c : c + 1, :] + (
                    has_before * factor * lines[t : t + 1]
                )
                c = c + levels - 1
                out_ref[0, r, c : c + 1, :] = out_ref[0, r, c : c + 1, :] + (
                    has_after * factor * lines[t + 2 : t + 3]
                )

        @pl.when(col_group == 0)
        def _():
            span = rows + 2
            e_ref[0:1, :] = from_tiles(below[:cells], rows)[rows - 1 : rows]
            e_ref[1 : rows + 1, :] = from_tiles(sum_ref[...], rows)
            e_ref[rows + 1 : span, :] = from_tiles(above[:cells], rows)[0:1]
            e_ref[0:span, :] = c_ref[6, 0:span, :] * e_ref[0:span, :]
            own = slice(1, rows + 1)
            heat = e_ref[own, :]
            second = c_ref[5, own, :] * heat
            first = (c_ref[0, own, :] + 1.0) * heat + second
            first = first + c_ref[1, own, :] * e_ref[0:rows, :]
            first = first + c_ref[2, own, :] * e_ref[2 : rows + 2, :]
            first = first + c_ref[3, own, :] * pltpu.roll(heat, 1, 1)
            first = first + c_ref[4, own, :] * pltpu.roll(heat, columns - 1, 1)
            for t, gain in enumerate((heat_gain, salt_gain)):
                c = t * levels
                for r in range(rows):
                    lines = jnp.concatenate([first[r : r + 1], second[r : r + 1]], axis=0)
                    out_ref[0, r, c : c + 2, :] = out_ref[0, r, c : c + 2, :] + gain * lines


def local(
    fields,
    wet_cells,
    flux_weight,
    variable_sea_response,
    diffusivity,
    a2o_source,
    a2o_target,
    a2o_count,
    a2o_weight,
    marine_air_input_index,
    marine_air_output_index,
    marine_air_piece_tally,
    marine_air_piece_factor,
):
    _, rows, channels, columns = fields.shape
    groups_x = lax.axis_size("gx")
    groups_y = lax.axis_size("gy")
    blocks, points = a2o_source.shape[2:]
    cells = rows * columns // LANES
    forward, inverse = fourier_tables(columns)
    flux_row = flux_weight[None, :]
    gain_row = variable_sea_response[None, :]
    diff_row = diffusivity[None, :]
    paired = groups_x == 4
    params = functools.partial(pltpu.CompilerParams, vmem_limit_bytes=40 * 2**20)
    vmem = pl.BlockSpec(memory_space=pltpu.VMEM)
    smem = pl.BlockSpec(memory_space=pltpu.SMEM)
    hbm = pl.BlockSpec(memory_space=pltpu.HBM)
    anywhere = pl.BlockSpec(memory_space=pl.ANY)

    def shape(dims, dtype):
        return jax.ShapeDtypeStruct(dims, dtype)

    partial_surface, coarse = pl.pallas_call(
        surface_kernel,
        out_shape=[shape((cells, LANES), f32), shape((cells, LANES), bf16)],
        in_specs=[hbm, hbm],
        out_specs=[vmem, vmem],
        scratch_shapes=[
            pltpu.VMEM((rows, channels, columns), f32),
            pltpu.VMEM(flux_row.shape, f32),
            pltpu.VMEM((rows, columns), f32),
            pltpu.SemaphoreType.DMA((rows,)),
            pltpu.SemaphoreType.DMA,
        ],
        compiler_params=pltpu.CompilerParams(vmem_limit_bytes=58 * 2**20),
        name="surface_partials",
    )(fields, flux_row)

    lines = 2 * channels + 16
    shapes = [
        shape((cells, LANES), f32),
        shape((rows, channels, columns), f32),
        shape((lines, columns), bf16),
        shape((lines, columns), bf16),
        shape((4 * rows, columns), bf16),
        shape((4 * rows, columns), bf16),
    ]
    if not paired:
        shapes.append(shape((2, channels, columns), bf16))
    partial_surface, y, e1, e3, e2, e4, *sums = pl.pallas_call(
        functools.partial(forward_kernel, groups_x, paired),
        out_shape=shapes,
        in_specs=[hbm] * 4 + [anywhere],
        out_specs=[anywhere] + [hbm] * (len(shapes) - 1),
        scratch_shapes=[pltpu.VMEM(out.shape, out.dtype) for out in shapes[1:]]
        + [
            pltpu.VMEM((rows, channels, columns), f32),
            pltpu.VMEM((rows, columns), jnp.int32),
            pltpu.VMEM(diff_row.shape, f32),
            pltpu.VMEM(forward.shape, bf16),
            pltpu.VMEM((rows * channels, columns), bf16),
            pltpu.VMEM((4 * rows, columns), f32),
            pltpu.SemaphoreType.DMA((3,)),
            pltpu.SemaphoreType.DMA((rows + len(shapes) - 2,)),
        ],
        input_output_aliases={4: 0},
        compiler_params=pltpu.CompilerParams(vmem_limit_bytes=58 * 2**20),
        name="forward_or_halos",
    )(fields, wet_cells, diff_row, forward, partial_surface)

    masks = [1 << bit for bit in range(groups_y.bit_length() - 1)]

    def sum_route(mask):
        return [(j, j ^ mask) for j in range(groups_y)]

    def partner_route(mask):
        return both_ways([(j, groups_y + (j ^ mask)) for j in range(groups_y)])

    surface = partial_surface
    for mask in masks[:-1]:
        surface = surface + lax.ppermute(coarse, "gy", sum_route(mask)).astype(f32)
        coarse = surface.astype(bf16)
    surfaces = [
        lax.ppermute(coarse, ("comp", "gy"), partner_route(mask)) for mask in masks[-1:] + [0]
    ]

    def ring_pairs(count, odd):
        return [(a, (a + 1) % count) for a in range(odd, count, 2)]

    def flat(comp, i, j):
        return (comp * groups_x + i) * groups_y + j

    def level_route(odd):
        pairs = []
        for i in range(groups_x):
            for a, b in ring_pairs(groups_y, odd):
                pairs.append((flat(1, i, a), flat(1, i, b)))
                if odd or not paired:
                    pairs.append((flat(0, i, a), flat(0, i, b)))
            if paired and not odd and i < i ^ 2:
                pairs += [(flat(0, i, j), flat(0, i ^ 2, j)) for j in range(groups_y)]
        return both_ways(pairs)

    e1 = lax.ppermute(e1, "gx", both_ways(ring_pairs(groups_x, 0)))
    e3 = lax.ppermute(e3, "gx", both_ways(ring_pairs(groups_x, 1)))
    axes = ("comp", "gx", "gy")
    e2 = lax.ppermute(e2, axes, level_route(0))
    e4 = lax.ppermute(e4, axes, level_route(1))

    landing, sent = pl.pallas_call(
        functools.partial(regrid_kernel, len(surfaces)),
        out_shape=[shape((cells, LANES), f32), shape((cells, LANES), bf16)],
        in_specs=[vmem] * len(surfaces)
        + [vmem, vmem, smem, hbm, vmem, vmem, smem, hbm, anywhere, anywhere],
        out_specs=[vmem] * 2,
        scratch_shapes=[
            pltpu.VMEM((blocks, points, points), bf16),
            pltpu.VMEM((blocks, points), f32),
            pltpu.VMEM((blocks, points), f32),
            pltpu.SemaphoreType.DMA,
        ],
        compiler_params=params(),
        name="regrid_blocks",
    )(
        *surfaces,
        a2o_source, a2o_target, a2o_count, a2o_weight,
        marine_air_input_index, marine_air_output_index,
        marine_air_piece_tally, marine_air_piece_factor, e1, e3,
    )
    for mask in masks[:-1]:
        landing = landing + lax.ppermute(sent, "gy", sum_route(mask)).astype(f32)
        sent = landing.astype(bf16)
    part = lax.ppermute(sent, "gy", sum_route(masks[-1]))

    extra = []
    if not paired:
        p, q = jnp.moveaxis(lax.all_gather(sums[0], "gx").astype(f32), 1, 0)
        viscous = lax.dynamic_slice_in_dim(
            diffusivity, lax.axis_index("gy") * channels, channels
        )[:, None]
        rates = [half_rates(g, 0, columns // 4, columns) for g in (0, 0, 1, 1)]
        _, alpha, _ = decay_terms(viscous, jnp.concatenate(rates, axis=1))
        gap = lax.axis_index("gx") - jnp.arange(groups_x)
        decay = jnp.exp(
            -(rows * jnp.maximum(jnp.abs(gap) - 1, 0))[:, None, None] * alpha[None]
        )
        extra = [
            jnp.sum(jnp.where((gap > 0)[:, None, None], decay * p, 0.0), axis=0),
            jnp.sum(jnp.where((gap < 0)[:, None, None], decay * q, 0.0), axis=0),
        ]
    ring = channels // 2 + 8
    damped, coefs, stepped = pl.pallas_call(
        functools.partial(first_step_kernel, groups_x, groups_y, paired),
        out_shape=[
            shape((rows * channels, columns), bf16),
            shape((7, 16, columns), f32),
            shape((rows + 2, 2, ring, columns), f32),
        ],
        in_specs=[vmem] * (8 + len(extra)),
        out_specs=[vmem] * 3,
        scratch_shapes=[
            pltpu.VMEM((rows, channels, LANES), f32),
            pltpu.VMEM((rows + 4, 2, ring, columns), f32),
            pltpu.VMEM((16, columns), f32),
        ],
        compiler_params=params(),
        name="damping_or_first_step",
    )(fields, wet_cells, diff_row, y, e1, e3, e2, e4, *extra)

    surface_sum, near, far = pl.pallas_call(
        functools.partial(heat_kernel, rows),
        out_shape=[
            shape((cells, LANES), f32),
            shape((cells + columns // 16, LANES), bf16),
            shape((cells + columns // 16, LANES), bf16),
        ],
        in_specs=[vmem] * 4 + [anywhere],
        out_specs=[vmem] * 3,
        compiler_params=params(),
        name="surface_sum",
    )(e2, e4, landing, part, coefs)

    near = lax.ppermute(near, "gx", both_ways(ring_pairs(groups_x, 0)))
    far = lax.ppermute(far, "gx", both_ways(ring_pairs(groups_x, 1)))
    base, column = pl.pallas_call(
        second_step_kernel,
        out_shape=[shape((rows, channels, columns), f32), shape((channels, LANES), f32)],
        in_specs=[vmem] * 5,
        out_specs=[vmem] * 2,
        compiler_params=params(),
        name="inverse_or_second_step",
    )(gain_row, inverse, damped, coefs, stepped)
    return pl.pallas_call(
        functools.partial(last_kernel, groups_x, groups_y),
        out_shape=shape(fields.shape, f32),
        in_specs=[vmem] * 6,
        out_specs=vmem,
        scratch_shapes=[pltpu.VMEM((16, columns), f32)],
        compiler_params=params(),
        name="add_surface_terms",
    )(column, base, coefs, surface_sum, near, far)


def solution(mesh):
    in_specs = (
        P("comp", "gx", "gy", None),
        P("gx", None),
        P(),
        P(),
        P(),
        P("gx", "gy", None, None),
        P("gx", "gy", None, None),
        P("gx", "gy"),
        P("gx", "gy", None, None, None),
        P("gx", "gy", None, None),
        P("gx", "gy", None, None),
        P("gx", "gy"),
        P("gx", "gy", None, None, None),
    )
    out_specs = P("comp", "gx", "gy", None)
    return jax.shard_map(local, mesh=mesh, in_specs=in_specs, out_specs=out_specs, check_vma=False)
```

```python
import functools

import jax
import jax.numpy as jnp
import numpy as np
from jax import lax
from jax.experimental import pallas as pl
from jax.experimental.pallas import tpu as pltpu
from jax.sharding import PartitionSpec as P

spread_rate = 0.2
mixing_rate = 0.1
heat_gain = 0.5
salt_gain = -0.25
LANES = 128
f32 = jnp.float32
bf16 = jnp.bfloat16


def fourier_tables(columns):
    half = columns // 2
    forward, inverse = [], []
    for first in (0, 1):
        waves = np.arange(first, half, 2)
        phase = np.arange(half)[:, None] * waves[None, :] % columns
        angles = phase * (2.0 * np.pi / columns)
        table = np.concatenate([np.cos(angles), np.sin(angles)], axis=1)
        weight = np.where(waves == 0, 1.0, 2.0) / columns
        forward.append(table)
        inverse.append(table.T * np.concatenate([weight, weight])[:, None])
    return (
        jnp.asarray(np.concatenate(forward).astype(np.float32), bf16),
        jnp.asarray(np.concatenate(inverse).astype(np.float32), bf16),
    )


def wave_parts(columns):
    quarter = columns // 4
    return [
        (g, n, (g * 2 * quarter + n, (g * 2 + 1) * quarter + n))
        for g in (0, 1)
        for n in range(0, quarter, LANES)
    ]


def half_rates(group, first, count, columns):
    lane = lax.broadcasted_iota(jnp.int32, (1, count), 1) + first
    wave = (2 * lane + group).astype(f32)
    sine = jnp.sin(wave * (np.pi / columns))
    return 2.0 * sine * sine


def both_ways(pairs):
    return [p for a, b in pairs for p in ((a, b), (b, a))]


def channel_column(row, channels, first):
    n = row.shape[1]
    lane = lax.broadcasted_iota(jnp.int32, (channels, n), 1)
    sub = lax.broadcasted_iota(jnp.int32, (channels, n), 0)
    return jnp.sum(jnp.where(lane == sub + first, row, 0.0), axis=1, keepdims=True)


def to_tiles(surface):
    cols = surface.shape[1]
    return jnp.concatenate(
        [surface[:, k : k + LANES] for k in range(0, cols, LANES)], axis=0
    )


def from_tiles(tiles, rows):
    return jnp.concatenate(
        [tiles[k : k + rows] for k in range(0, tiles.shape[0], rows)], axis=1
    )


def decay_terms(diff_column, rates):
    half = 0.5 / diff_column + rates
    sinh = jnp.sqrt(half * (half + 2.0))
    grow = 1.0 + half + sinh
    return 1.0 / grow, jnp.log(grow), sinh


def surface_kernel(x_hbm, flux_hbm, s_ref, coarse_ref, x_ref, flux_ref, row_ref, x_sem, sem):
    rows, channels, columns = x_ref.shape
    col_group = lax.axis_index("gy")
    is_atmos = lax.axis_index("comp") == 0
    flux_copy = pltpu.make_async_copy(flux_hbm, flux_ref, sem)
    copies = [
        pltpu.make_async_copy(x_hbm.at[0, r], x_ref.at[r], x_sem.at[r]) for r in range(rows)
    ]

    @pl.when(is_atmos)
    def _():
        for copy in [flux_copy] + copies:
            copy.start()
        flux_copy.wait()
        weight = channel_column(flux_ref[...], channels, col_group * channels)
        for r in range(rows):
            copies[r].wait()
            row_ref[r : r + 1, :] = jnp.sum(x_ref[r] * weight, axis=0, keepdims=True)

    @pl.when(jnp.logical_not(is_atmos))
    def _():
        top = [
            pltpu.make_async_copy(
                x_hbm.at[0, r, pl.ds(0, 8)], x_ref.at[r, pl.ds(0, 8)], x_sem.at[r]
            )
            for r in range(rows)
        ]
        for copy in top:
            copy.start()
        gain = jnp.where(col_group == 0, 1.0, 0.0)
        for r in range(rows):
            top[r].wait()
            row_ref[r : r + 1, :] = x_ref[r, 0:1, :] * gain

    surface = to_tiles(row_ref[...])
    s_ref[...] = surface
    coarse_ref[...] = surface.astype(bf16)


def pair_kernel(surface_ref, part_ref, _, __, sum_ref, coarse_ref, ___, ____):
    total = surface_ref[...] + part_ref[...].astype(f32)
    sum_ref[...] = total
    coarse_ref[...] = total.astype(bf16)


def forward_kernel(
    groups_x, paired, x_hbm, wet_hbm, diff_hbm, table_hbm, s_hbm, kept_hbm, *refs
):
    del s_hbm, kept_hbm
    outs = 5 if paired else 6
    y_hbm, *message_hbm = refs[:outs]
    y_ref, *message_ref = refs[outs : 2 * outs]
    e1_ref, e3_ref, e2_ref, e4_ref = message_ref[:4]
    if not paired:
        pq_ref = message_ref[4]
    x_ref, wet_ref, diff_ref, table_ref, flat_ref, edge_ref, sem, out_sem = refs[2 * outs :]
    rows, channels, columns = x_ref.shape
    half = columns // 2
    row_group = lax.axis_index("gx")
    col_group = lax.axis_index("gy")
    is_atmos = lax.axis_index("comp") == 0

    x_copy = pltpu.make_async_copy(x_hbm.at[0], x_ref, sem.at[0])
    y_copies = [
        pltpu.make_async_copy(y_ref.at[r], y_hbm.at[r], out_sem.at[r]) for r in range(rows)
    ]
    message_copies = [
        pltpu.make_async_copy(ref, hbm, out_sem.at[rows + k])
        for k, (ref, hbm) in enumerate(zip(message_ref, message_hbm))
    ]

    @pl.when(is_atmos)
    def _():
        table_copy = pltpu.make_async_copy(table_hbm, table_ref, sem.at[1])
        diff_copy = pltpu.make_async_copy(diff_hbm, diff_ref, sem.at[2])
        for copy in (x_copy, table_copy, diff_copy):
            copy.start()
        x_copy.wait()
        first = col_group * channels
        for r in range(rows):
            left, right = x_ref[r, :, :half], x_ref[r, :, half:]
            flat_ref[r * channels : (r + 1) * channels, :half] = (left + right).astype(bf16)
            flat_ref[r * channels : (r + 1) * channels, half:] = (left - right).astype(bf16)
        table_copy.wait()
        for k in range(2):
            lanes = slice(k * half, (k + 1) * half)
            part = jnp.dot(
                flat_ref[:, lanes], table_ref[lanes, :], preferred_element_type=f32
            )
            y_ref[:, :, lanes] = part.reshape(rows, channels, half)
        for copy in y_copies:
            copy.start()
        diff_copy.wait()
        diff = channel_column(diff_ref[...], channels, first)
        total = rows * groups_x
        base = (row_group * rows).astype(f32)
        for group, n, parts in wave_parts(columns):
            lam, alpha, _ = decay_terms(diff, half_rates(group, n, LANES, columns))
            lam2 = lam * lam
            low = jnp.exp(-2.0 * base * alpha)
            high = jnp.exp(-2.0 * (total - rows - base) * alpha)
            for part in parts:
                lanes = slice(part, part + LANES)
                power = low
                p = jnp.zeros((channels, LANES), f32)
                for r in range(rows):
                    power = power * lam2
                    p = lam * p + (1.0 - power) * y_ref[r, :, lanes]
                power = high
                q = jnp.zeros((channels, LANES), f32)
                for r in reversed(range(rows)):
                    power = power * lam2
                    q = lam * q + (1.0 - power) * y_ref[r, :, lanes]
                if paired:
                    for mask, out in ((1, e1_ref), (2, e2_ref), (3, e3_ref)):
                        upward = row_group < (row_group ^ mask)
                        out[0:channels, lanes] = jnp.where(upward, p, q).astype(bf16)
                else:
                    pq_ref[0, :, lanes] = p.astype(bf16)
                    pq_ref[1, :, lanes] = q.astype(bf16)
        for copy in message_copies:
            copy.start()
        for copy in y_copies + message_copies:
            copy.wait()

    @pl.when(jnp.logical_not(is_atmos))
    def _():
        wet_copy = pltpu.make_async_copy(wet_hbm, wet_ref, sem.at[1])
        for copy in (x_copy, wet_copy):
            copy.start()
        x_copy.wait()
        wet_copy.wait()
        levels = channels // 2
        lines = 2 * channels
        even_x = row_group % 2 == 0
        even_y = col_group % 2 == 0
        wet = wet_ref[...].astype(f32)
        wet = jnp.concatenate([wet, wet], axis=0).astype(bf16)

        def put(out, last):
            @pl.when(last)
            def _():
                out[0:lines, :] = x_ref[rows - 2 :].reshape(lines, columns).astype(bf16)

            @pl.when(jnp.logical_not(last))
            def _():
                out[0:lines, :] = x_ref[:2].reshape(lines, columns).astype(bf16)

            out[lines : lines + 16, :] = wet

        put(e1_ref, even_x)
        put(e3_ref, jnp.logical_not(even_x))

        def put_edges(out, level):
            for r in range(rows):
                for t in range(2):
                    at = (r * 2 + t) * 2
                    c = t * levels + level
                    edge_ref[at : at + 2, :] = x_ref[r, c : c + 2, :]
            out[...] = edge_ref[...].astype(bf16)

        @pl.when(even_y)
        def _():
            put_edges(e2_ref, levels - 2)
            put_edges(e4_ref, 0)

        @pl.when(jnp.logical_not(even_y))
        def _():
            put_edges(e2_ref, 0)
            put_edges(e4_ref, levels - 2)

        for copy in message_copies:
            copy.start()
        for copy in message_copies:
            copy.wait()


def one_hot_kernel(
    rows, columns, a_src, a_dst, m_src, m_dst, _, src_hot_ref, dst_hot_ref, src_row_ref, dst_row_ref
):
    is_atmos = lax.axis_index("comp") == 0
    blocks, points = src_row_ref.shape
    lane_iota = lax.broadcasted_iota(jnp.int32, (LANES, points), 0)
    for a_ref, m_ref, hot_ref, row_ref in (
        (a_src, m_src, src_hot_ref, src_row_ref),
        (a_dst, m_dst, dst_hot_ref, dst_row_ref),
    ):
        index = jnp.where(is_atmos, m_ref[0, 0], a_ref[0, 0])
        row = index // columns
        tile = (index // LANES) % (columns // LANES)
        row_ref[...] = tile * rows + row
        lane = index % LANES
        for b in range(blocks):
            hot_ref[:, b * points : (b + 1) * points] = jnp.where(
                lane_iota == lane[b : b + 1], 1.0, 0.0
            ).astype(bf16)


def regrid_kernel(n_surfaces, *refs):
    surfaces = refs[:n_surfaces]
    (
        src_hot_ref, dst_hot_ref, src_row_ref, dst_row_ref, a_count, m_count, a_weight, m_weight,
        _, _,
        land_ref, sent_ref, weight_ref, gath_ref, val_ref, sem,
    ) = refs[n_surfaces:]
    is_atmos = lax.axis_index("comp") == 0
    blocks, points = val_ref.shape
    cells = surfaces[0].shape[0]

    @pl.when(is_atmos)
    def _():
        pltpu.make_async_copy(m_weight.at[0, 0], weight_ref, sem).start()

    @pl.when(jnp.logical_not(is_atmos))
    def _():
        pltpu.make_async_copy(a_weight.at[0, 0], weight_ref, sem).start()

    count = jnp.where(is_atmos, m_count[0, 0], a_count[0, 0])
    pair = 2 * points
    row_iota = lax.broadcasted_iota(jnp.int32, (cells, points), 0)
    table = sum(surface[...].astype(f32) for surface in surfaces).astype(bf16)
    for b in range(0, blocks, 2):
        picked = jnp.dot(
            table, src_hot_ref[:, b * points : b * points + pair], preferred_element_type=f32
        )
        for k in range(2):
            mine = row_iota == src_row_ref[b + k : b + k + 1, :]
            part = jnp.where(mine, picked[:, k * points : (k + 1) * points], 0.0)
            gath_ref[b + k : b + k + 1, :] = jnp.sum(part, axis=0, keepdims=True)
    gathered = gath_ref[...].astype(bf16)

    @pl.when(is_atmos)
    def _():
        pltpu.make_async_copy(m_weight.at[0, 0], weight_ref, sem).wait()

    @pl.when(jnp.logical_not(is_atmos))
    def _():
        pltpu.make_async_copy(a_weight.at[0, 0], weight_ref, sem).wait()

    block_iota = lax.broadcasted_iota(jnp.int32, (blocks, points), 0)
    values = jnp.zeros((blocks, points), f32)
    for b in range(0, blocks, 2):
        terms = lax.dot_general(
            gathered,
            weight_ref[b : b + 2].reshape(pair, points),
            (((1,), (1,)), ((), ())),
            preferred_element_type=f32,
        )
        for k in range(2):
            values = jnp.where(block_iota == b + k, terms[:, k * points : (k + 1) * points], values)
    val_ref[...] = jnp.where(block_iota < count, values, 0.0)
    land = jnp.zeros((2 * cells, LANES), f32)
    for b in range(0, blocks, 2):
        spread = []
        for k in range(b, b + 2):
            value = val_ref[k : k + 1, :]
            coarse = value.astype(bf16).astype(f32)
            fine = value - coarse
            mine = row_iota == dst_row_ref[k : k + 1, :]
            spread.append(
                jnp.concatenate(
                    [jnp.where(mine, coarse, 0.0), jnp.where(mine, fine, 0.0)], axis=0
                ).astype(bf16)
            )
        land = land + lax.dot_general(
            jnp.concatenate(spread, axis=1),
            dst_hot_ref[:, b * points : b * points + pair],
            (((1,), (1,)), ((), ())),
            preferred_element_type=f32,
        )
    land = land[:cells] + land[cells:]
    land_ref[...] = land
    sent_ref[...] = land.astype(bf16)


def heat_kernel(rows, e2_ref, e4_ref, land_ref, part_ref, _, sum_ref, near_ref, far_ref):
    cells = land_ref.shape[0]
    columns = cells // rows * LANES
    even_x = lax.axis_index("gx") % 2 == 0
    even_y = lax.axis_index("gy") % 2 == 0
    total = land_ref[...] + part_ref[...].astype(f32)
    sum_ref[...] = total

    def corners(row):
        start = row * 4 // 16 * 16
        one = e2_ref[start : start + 16, :].astype(f32)
        two = e4_ref[start : start + 16, :].astype(f32)
        low = jnp.where(even_y, two, one)
        high = jnp.where(even_y, one, two)
        at = row * 4 - start
        lines = [low[at + 1 : at + 2], low[at + 3 : at + 4], high[at : at + 1], high[at + 2 : at + 3]]
        return to_tiles(jnp.concatenate(lines + [jnp.zeros((4, columns), f32)], axis=0))

    first, last = corners(0), corners(rows - 1)
    near_ref[0:cells, :] = total.astype(bf16)
    far_ref[0:cells, :] = total.astype(bf16)
    near_ref[cells:, :] = jnp.where(even_x, last, first).astype(bf16)
    far_ref[cells:, :] = jnp.where(even_x, first, last).astype(bf16)


def advance(ref, r, t, coefs, size):
    ring, columns = ref.shape[2:]
    whole = ref[r, t]
    up = pltpu.roll(whole, 1, 0)[:size]
    down = pltpu.roll(whole, ring - 1, 0)[:size]
    mid = whole[:size]
    total = coefs[0] * mid + coefs[5] * (up + down)
    total = total + coefs[1] * ref[r - 1, t, 0:size, :]
    total = total + coefs[2] * ref[r + 1, t, 0:size, :]
    total = total + coefs[3] * pltpu.roll(mid, 1, 1)
    return total + coefs[4] * pltpu.roll(mid, columns - 1, 1)


def first_step_kernel(
    groups_x, groups_y, paired, x_ref, wet_ref, diff_ref, y_ref, e1_ref, e3_ref,
    e2_ref, e4_ref, *refs,
):
    if not paired:
        pin_ref, qin_ref = refs[:2]
    zb_ref, c_ref, t1_ref, z_ref, t0_ref, w_ref = refs[-6:]
    _, rows, channels, columns = x_ref.shape
    row_group = lax.axis_index("gx")
    col_group = lax.axis_index("gy")
    is_atmos = lax.axis_index("comp") == 0

    @pl.when(is_atmos)
    def _():
        diff = channel_column(diff_ref[...], channels, col_group * channels)
        total = rows * groups_x
        base = (row_group * rows).astype(f32)
        for group, n, parts in wave_parts(columns):
            lam, alpha, sinh = decay_terms(diff, half_rates(group, n, LANES, columns))
            lam2 = lam * lam
            low = jnp.exp(-2.0 * base * alpha)
            high = jnp.exp(-2.0 * (total - rows - base) * alpha)
            scale = 1.0 / (
                2.0 * diff * sinh * (1.0 - jnp.exp(-2.0 * (total + 1) * alpha))
            )
            lows, highs = [], []
            power = low
            for r in range(rows):
                power = power * lam2
                lows.append(1.0 - power)
            power = high
            for r in range(rows):
                power = power * lam2
                highs.append(1.0 - power)
            highs = highs[::-1]
            for part in parts:
                lanes = slice(part, part + LANES)
                if paired:
                    pin = jnp.zeros((channels, LANES), f32)
                    qin = jnp.zeros((channels, LANES), f32)
                    for mask, msg in ((1, e1_ref), (2, e2_ref), (3, e3_ref)):
                        band = row_group ^ mask
                        gap = (jnp.abs(row_group - band) - 1) * rows
                        term = jnp.exp(-gap.astype(f32) * alpha)
                        term = term * msg[0:channels, lanes].astype(f32)
                        pin = pin + jnp.where(band < row_group, term, 0.0)
                        qin = qin + jnp.where(band > row_group, term, 0.0)
                else:
                    pin = pin_ref[:, lanes]
                    qin = qin_ref[:, lanes]
                f = pin
                for r in range(rows):
                    f = lam * f + lows[r] * y_ref[r, :, lanes]
                    z_ref[r] = highs[r] * f
                g = lam * qin
                for r in reversed(range(rows)):
                    z = scale * (z_ref[r] + lows[r] * g)
                    zb_ref[r * channels : (r + 1) * channels, lanes] = z.astype(bf16)
                    g = lam * (g + highs[r] * y_ref[r, :, lanes])

    @pl.when(jnp.logical_not(is_atmos))
    def _():
        levels = channels // 2
        ring = levels + 8
        lines = 2 * channels
        first_x = row_group == 0
        last_x = row_group == groups_x - 1
        top = col_group == 0
        bottom = col_group == groups_y - 1
        even_x = row_group % 2 == 0
        even_y = col_group % 2 == 0

        one = e1_ref[lines : lines + 16, :].astype(f32)
        three = e3_ref[lines : lines + 16, :].astype(f32)
        below = jnp.where(even_x, three, one)[rows - 2 : rows]
        above = jnp.where(even_x, one, three)[0:2]
        w_ref[0:2, :] = jnp.where(first_x, 0.0, below)
        w_ref[2 : rows + 2, :] = wet_ref[...].astype(f32)
        w_ref[rows + 2 : rows + 4, :] = jnp.where(last_x, 0.0, above)

        span = rows + 2
        north = w_ref[0:span, :]
        here = w_ref[1 : span + 1, :]
        south = w_ref[2 : span + 2, :]
        west = pltpu.roll(here, 1, 1)
        east = pltpu.roll(here, columns - 1, 1)
        c_ref[0, 0:span, :] = here * (
            1.0 - 2.0 * mixing_rate - spread_rate * (north + south + west + east)
        )
        c_ref[1, 0:span, :] = spread_rate * here * north
        c_ref[2, 0:span, :] = spread_rate * here * south
        c_ref[3, 0:span, :] = spread_rate * here * west
        c_ref[4, 0:span, :] = spread_rate * here * east
        c_ref[5, 0:span, :] = mixing_rate * here
        c_ref[6, 0:span, :] = here

        one = e1_ref[0:lines, :].astype(f32)
        three = e3_ref[0:lines, :].astype(f32)
        below = jnp.where(even_x, three, one)
        above = jnp.where(even_x, one, three)
        blank = jnp.zeros((8, columns), f32)
        for k in range(2):
            for t in range(2):
                c = k * channels + t * levels
                t0_ref[k, t, 0:levels, :] = below[c : c + levels]
                t0_ref[rows + 2 + k, t, 0:levels, :] = above[c : c + levels]
                t0_ref[k, t, levels:ring, :] = blank
                t0_ref[rows + 2 + k, t, levels:ring, :] = blank
        one = e2_ref[...].astype(f32)
        two = e4_ref[...].astype(f32)
        before = jnp.where(even_y, two, one)
        after = jnp.where(even_y, one, two)
        for r in range(rows):
            for t in range(2):
                k = (r * 2 + t) * 2
                t0_ref[r + 2, t, 0:levels, :] = x_ref[0, r, t * levels : (t + 1) * levels, :]
                t0_ref[r + 2, t, levels : levels + 2, :] = after[k : k + 2]
                t0_ref[r + 2, t, ring - 2 : ring, :] = before[k : k + 2]

        def close(ref, r):
            for t in range(2):
                ref[r, t, ring - 1 : ring, :] = jnp.where(
                    top, ref[r, t, 0:1, :], ref[r, t, ring - 1 : ring, :]
                )
                ref[r, t, levels : levels + 1, :] = jnp.where(
                    bottom, ref[r, t, levels - 1 : levels, :], ref[r, t, levels : levels + 1, :]
                )

        def first(r, carry):
            coefs = [c_ref[k, pl.ds(r, 1), :] for k in range(6)]
            close(t0_ref, r + 1)
            for t in range(2):
                t1_ref[r, t] = advance(t0_ref, r + 1, t, coefs, ring)
            close(t1_ref, r)
            return carry

        lax.fori_loop(0, span, first, 0)


def second_step_kernel(gain_ref, table_ref, zb_ref, c_ref, t1_ref, base_ref, column_ref):
    rows, channels, columns = base_ref.shape
    is_atmos = lax.axis_index("comp") == 0

    @pl.when(is_atmos)
    def _():
        response = channel_column(gain_ref[...], channels, lax.axis_index("gy") * channels)
        column_ref[...] = jnp.broadcast_to(response, column_ref.shape)
        half = columns // 2
        step = 256
        for n in range(0, half, step):
            even, odd = [
                jnp.dot(
                    zb_ref[:, k * half : (k + 1) * half],
                    table_ref[k * half : (k + 1) * half, n : n + step],
                    preferred_element_type=f32,
                ).reshape(rows, channels, step)
                for k in range(2)
            ]
            base_ref[:, :, n : n + step] = even + odd
            base_ref[:, :, n + half : n + half + step] = even - odd

    @pl.when(jnp.logical_not(is_atmos))
    def _():
        levels = channels // 2

        def second(r, carry):
            coefs = [c_ref[k, pl.ds(r, 1), :] for k in range(6)]
            for t in range(2):
                c = t * levels
                base_ref[r - 1, c : c + levels, :] = advance(t1_ref, r, t, coefs, levels)
            return carry

        lax.fori_loop(1, rows + 1, second, 0)


def last_kernel(
    groups_x, groups_y, column_ref, base_ref, c_ref, sum_ref, near_ref, far_ref, out_ref, e_ref
):
    _, rows, channels, columns = out_ref.shape
    row_group = lax.axis_index("gx")
    col_group = lax.axis_index("gy")
    is_atmos = lax.axis_index("comp") == 0

    @pl.when(is_atmos)
    def _():
        for k in range(columns // LANES):
            lanes = slice(k * LANES, (k + 1) * LANES)
            for r in range(rows):
                at = k * rows + r
                out_ref[0, r, :, lanes] = (
                    base_ref[r, :, lanes] + column_ref[...] * sum_ref[at : at + 1, :]
                )

    @pl.when(jnp.logical_not(is_atmos))
    def _():
        out_ref[0] = base_ref[...]
        levels = channels // 2
        cells = sum_ref.shape[0]
        even = row_group % 2 == 0
        below = jnp.where(even, far_ref[...].astype(f32), near_ref[...].astype(f32))
        above = jnp.where(even, near_ref[...].astype(f32), far_ref[...].astype(f32))

        low = from_tiles(below[cells:], 8)
        high = from_tiles(above[cells:], 8)
        by_low = c_ref[1, 1:2, :] * (c_ref[5, 0:1, :] + c_ref[5, 1:2, :])
        by_high = c_ref[2, rows : rows + 1, :] * (
            c_ref[5, rows : rows + 1, :] + c_ref[5, rows + 1 : rows + 2, :]
        )
        has_before = jnp.where(col_group > 0, 1.0, 0.0)
        has_after = jnp.where(col_group < groups_y - 1, 1.0, 0.0)
        for t in range(2):
            for r, factor, lines in ((0, by_low, low), (rows - 1, by_high, high)):
                c = t * levels
                out_ref[0, r, c : c + 1, :] = out_ref[0, r, c : c + 1, :] + (
                    has_before * factor * lines[t : t + 1]
                )
                c = c + levels - 1
                out_ref[0, r, c : c + 1, :] = out_ref[0, r, c : c + 1, :] + (
                    has_after * factor * lines[t + 2 : t + 3]
                )

        @pl.when(col_group == 0)
        def _():
            span = rows + 2
            e_ref[0:1, :] = from_tiles(below[:cells], rows)[rows - 1 : rows]
            e_ref[1 : rows + 1, :] = from_tiles(sum_ref[...], rows)
            e_ref[rows + 1 : span, :] = from_tiles(above[:cells], rows)[0:1]
            e_ref[0:span, :] = c_ref[6, 0:span, :] * e_ref[0:span, :]
            own = slice(1, rows + 1)
            heat = e_ref[own, :]
            second = c_ref[5, own, :] * heat
            first = (c_ref[0, own, :] + 1.0) * heat + second
            first = first + c_ref[1, own, :] * e_ref[0:rows, :]
            first = first + c_ref[2, own, :] * e_ref[2 : rows + 2, :]
            first = first + c_ref[3, own, :] * pltpu.roll(heat, 1, 1)
            first = first + c_ref[4, own, :] * pltpu.roll(heat, columns - 1, 1)
            for t, gain in enumerate((heat_gain, salt_gain)):
                c = t * levels
                for r in range(rows):
                    lines = jnp.concatenate([first[r : r + 1], second[r : r + 1]], axis=0)
                    out_ref[0, r, c : c + 2, :] = out_ref[0, r, c : c + 2, :] + gain * lines


def local(
    fields,
    wet_cells,
    flux_weight,
    variable_sea_response,
    diffusivity,
    a2o_source,
    a2o_target,
    a2o_count,
    a2o_weight,
    marine_air_input_index,
    marine_air_output_index,
    marine_air_piece_tally,
    marine_air_piece_factor,
):
    _, rows, channels, columns = fields.shape
    groups_x = lax.axis_size("gx")
    groups_y = lax.axis_size("gy")
    blocks, points = a2o_source.shape[2:]
    cells = rows * columns // LANES
    forward, inverse = fourier_tables(columns)
    flux_row = flux_weight[None, :]
    gain_row = variable_sea_response[None, :]
    diff_row = diffusivity[None, :]
    paired = groups_x == 4
    params = functools.partial(pltpu.CompilerParams, vmem_limit_bytes=40 * 2**20)
    vmem = pl.BlockSpec(memory_space=pltpu.VMEM)
    smem = pl.BlockSpec(memory_space=pltpu.SMEM)
    hbm = pl.BlockSpec(memory_space=pltpu.HBM)
    anywhere = pl.BlockSpec(memory_space=pl.ANY)

    def shape(dims, dtype):
        return jax.ShapeDtypeStruct(dims, dtype)

    partial_surface, coarse = pl.pallas_call(
        surface_kernel,
        out_shape=[shape((cells, LANES), f32), shape((cells, LANES), bf16)],
        in_specs=[hbm, hbm],
        out_specs=[vmem, vmem],
        scratch_shapes=[
            pltpu.VMEM((rows, channels, columns), f32),
            pltpu.VMEM(flux_row.shape, f32),
            pltpu.VMEM((rows, columns), f32),
            pltpu.SemaphoreType.DMA((rows,)),
            pltpu.SemaphoreType.DMA,
        ],
        compiler_params=pltpu.CompilerParams(vmem_limit_bytes=58 * 2**20),
        name="surface_partials",
    )(fields, flux_row)

    lines = 2 * channels + 16
    shapes = [
        shape((cells, LANES), f32),
        shape((rows, channels, columns), f32),
        shape((lines, columns), bf16),
        shape((lines, columns), bf16),
        shape((4 * rows, columns), bf16),
        shape((4 * rows, columns), bf16),
    ]
    if not paired:
        shapes.append(shape((2, channels, columns), bf16))
    partial_surface, y, e1, e3, e2, e4, *sums = pl.pallas_call(
        functools.partial(forward_kernel, groups_x, paired),
        out_shape=shapes,
        in_specs=[hbm] * 4 + [anywhere],
        out_specs=[anywhere] + [hbm] * (len(shapes) - 1),
        scratch_shapes=[pltpu.VMEM(out.shape, out.dtype) for out in shapes[1:]]
        + [
            pltpu.VMEM((rows, channels, columns), f32),
            pltpu.VMEM((rows, columns), jnp.int32),
            pltpu.VMEM(diff_row.shape, f32),
            pltpu.VMEM(forward.shape, bf16),
            pltpu.VMEM((rows * channels, columns), bf16),
            pltpu.VMEM((4 * rows, columns), f32),
            pltpu.SemaphoreType.DMA((3,)),
            pltpu.SemaphoreType.DMA((rows + len(shapes) - 2,)),
        ],
        input_output_aliases={4: 0},
        compiler_params=pltpu.CompilerParams(vmem_limit_bytes=58 * 2**20),
        name="forward_or_halos",
    )(fields, wet_cells, diff_row, forward, partial_surface)

    masks = [1 << bit for bit in range(groups_y.bit_length() - 1)]

    def sum_route(mask):
        return [(j, j ^ mask) for j in range(groups_y)]

    def partner_route(mask):
        return both_ways([(j, groups_y + (j ^ mask)) for j in range(groups_y)])

    surface = partial_surface
    for mask in masks[:-1]:
        part = lax.ppermute(coarse, "gy", sum_route(mask))
        surface, coarse, e1, e3 = pl.pallas_call(
            pair_kernel,
            out_shape=[
                shape(surface.shape, f32),
                shape(surface.shape, bf16),
                shape(e1.shape, bf16),
                shape(e3.shape, bf16),
            ],
            in_specs=[vmem, vmem, anywhere, anywhere],
            out_specs=[vmem, vmem, anywhere, anywhere],
            input_output_aliases={2: 2, 3: 3},
            compiler_params=params(),
            name="pair_sum",
        )(surface, part, e1, e3)
    surfaces = [
        lax.ppermute(coarse, ("comp", "gy"), partner_route(mask)) for mask in masks[-1:] + [0]
    ]

    def ring_pairs(count, odd):
        return [(a, (a + 1) % count) for a in range(odd, count, 2)]

    def flat(comp, i, j):
        return (comp * groups_x + i) * groups_y + j

    def level_route(odd):
        pairs = []
        for i in range(groups_x):
            linked = [(a, a + 1) for a in range(odd, groups_y - 1, 2)]
            alone = set(range(groups_y)) - {j for pair in linked for j in pair}
            pairs += [(flat(1, i, a), flat(1, i, b)) for a, b in linked]
            if i % 2 == 0:
                pairs += [(flat(1, i, j), flat(1, i + 1, j)) for j in sorted(alone)]
                if odd or not paired:
                    pairs += [(flat(0, i, j), flat(0, i + 1, j)) for j in range(groups_y)]
            if paired and not odd and i < i ^ 2:
                pairs += [(flat(0, i, j), flat(0, i ^ 2, j)) for j in range(groups_y)]
        return both_ways(pairs)

    e1 = lax.ppermute(e1, "gx", both_ways(ring_pairs(groups_x, 0)))
    e3 = lax.ppermute(e3, "gx", both_ways(ring_pairs(groups_x, 1)))
    axes = ("comp", "gx", "gy")
    e2 = lax.ppermute(e2, axes, level_route(0))
    e4 = lax.ppermute(e4, axes, level_route(1))

    one_hots = pl.pallas_call(
        functools.partial(one_hot_kernel, rows, columns),
        out_shape=[
            shape((LANES, blocks * points), bf16),
            shape((LANES, blocks * points), bf16),
            shape((blocks, points), jnp.int32),
            shape((blocks, points), jnp.int32),
        ],
        in_specs=[vmem] * 4 + [anywhere],
        out_specs=[vmem] * 4,
        compiler_params=params(),
        name="one_hots",
    )(a2o_source, a2o_target, marine_air_input_index, marine_air_output_index, coarse)
    landing, sent = pl.pallas_call(
        functools.partial(regrid_kernel, len(surfaces)),
        out_shape=[shape((cells, LANES), f32), shape((cells, LANES), bf16)],
        in_specs=[vmem] * (len(surfaces) + 4) + [smem, smem, hbm, hbm, anywhere, anywhere],
        out_specs=[vmem] * 2,
        scratch_shapes=[
            pltpu.VMEM((blocks, points, points), bf16),
            pltpu.VMEM((blocks, points), f32),
            pltpu.VMEM((blocks, points), f32),
            pltpu.SemaphoreType.DMA,
        ],
        compiler_params=params(),
        name="regrid_blocks",
    )(
        *surfaces, *one_hots, a2o_count, marine_air_piece_tally,
        a2o_weight, marine_air_piece_factor, e1, e3,
    )
    for mask in masks[:-1]:
        landing = landing + lax.ppermute(sent, "gy", sum_route(mask)).astype(f32)
        sent = landing.astype(bf16)
    part = lax.ppermute(sent, "gy", sum_route(masks[-1]))

    extra = []
    if not paired:
        p, q = jnp.moveaxis(lax.all_gather(sums[0], "gx").astype(f32), 1, 0)
        viscous = lax.dynamic_slice_in_dim(
            diffusivity, lax.axis_index("gy") * channels, channels
        )[:, None]
        rates = [half_rates(g, 0, columns // 4, columns) for g in (0, 0, 1, 1)]
        _, alpha, _ = decay_terms(viscous, jnp.concatenate(rates, axis=1))
        gap = lax.axis_index("gx") - jnp.arange(groups_x)
        decay = jnp.exp(
            -(rows * jnp.maximum(jnp.abs(gap) - 1, 0))[:, None, None] * alpha[None]
        )
        extra = [
            jnp.sum(jnp.where((gap > 0)[:, None, None], decay * p, 0.0), axis=0),
            jnp.sum(jnp.where((gap < 0)[:, None, None], decay * q, 0.0), axis=0),
        ]
    ring = channels // 2 + 8
    damped, coefs, stepped = pl.pallas_call(
        functools.partial(first_step_kernel, groups_x, groups_y, paired),
        out_shape=[
            shape((rows * channels, columns), bf16),
            shape((7, 16, columns), f32),
            shape((rows + 2, 2, ring, columns), f32),
        ],
        in_specs=[vmem] * (8 + len(extra)),
        out_specs=[vmem] * 3,
        scratch_shapes=[
            pltpu.VMEM((rows, channels, LANES), f32),
            pltpu.VMEM((rows + 4, 2, ring, columns), f32),
            pltpu.VMEM((16, columns), f32),
        ],
        compiler_params=params(),
        name="damping_or_first_step",
    )(fields, wet_cells, diff_row, y, e1, e3, e2, e4, *extra)

    surface_sum, near, far = pl.pallas_call(
        functools.partial(heat_kernel, rows),
        out_shape=[
            shape((cells, LANES), f32),
            shape((cells + columns // 16, LANES), bf16),
            shape((cells + columns // 16, LANES), bf16),
        ],
        in_specs=[vmem] * 4 + [anywhere],
        out_specs=[vmem] * 3,
        compiler_params=params(),
        name="surface_sum",
    )(e2, e4, landing, part, coefs)

    near = lax.ppermute(near, "gx", both_ways(ring_pairs(groups_x, 0)))
    far = lax.ppermute(far, "gx", both_ways(ring_pairs(groups_x, 1)))
    base, column = pl.pallas_call(
        second_step_kernel,
        out_shape=[shape((rows, channels, columns), f32), shape((channels, LANES), f32)],
        in_specs=[vmem] * 5,
        out_specs=[vmem] * 2,
        compiler_params=params(),
        name="inverse_or_second_step",
    )(gain_row, inverse, damped, coefs, stepped)
    return pl.pallas_call(
        functools.partial(last_kernel, groups_x, groups_y),
        out_shape=shape(fields.shape, f32),
        in_specs=[vmem] * 6,
        out_specs=vmem,
        scratch_shapes=[pltpu.VMEM((16, columns), f32)],
        compiler_params=params(),
        name="add_surface_terms",
    )(column, base, coefs, surface_sum, near, far)


def solution(mesh):
    in_specs = (
        P("comp", "gx", "gy", None),
        P("gx", None),
        P(),
        P(),
        P(),
        P("gx", "gy", None, None),
        P("gx", "gy", None, None),
        P("gx", "gy"),
        P("gx", "gy", None, None, None),
        P("gx", "gy", None, None),
        P("gx", "gy", None, None),
        P("gx", "gy"),
        P("gx", "gy", None, None, None),
    )
    out_specs = P("comp", "gx", "gy", None)
    return jax.shard_map(local, mesh=mesh, in_specs=in_specs, out_specs=out_specs, check_vma=False)
```

```python
import functools

import jax
import jax.numpy as jnp
import numpy as np
from jax import lax
from jax.experimental import pallas as pl
from jax.experimental.pallas import tpu as pltpu
from jax.sharding import PartitionSpec as P

spread_rate = 0.2
mixing_rate = 0.1
heat_gain = 0.5
salt_gain = -0.25
LANES = 128
f32 = jnp.float32
bf16 = jnp.bfloat16


def fourier_tables(columns):
    half = columns // 2
    forward, inverse = [], []
    for first in (0, 1):
        waves = np.arange(first, half, 2)
        phase = np.arange(half)[:, None] * waves[None, :] % columns
        angles = phase * (2.0 * np.pi / columns)
        table = np.concatenate([np.cos(angles), np.sin(angles)], axis=1)
        weight = np.where(waves == 0, 1.0, 2.0) / columns
        forward.append(table)
        inverse.append(table.T * np.concatenate([weight, weight])[:, None])
    return (
        jnp.asarray(np.concatenate(forward).astype(np.float32), bf16),
        jnp.asarray(np.concatenate(inverse).astype(np.float32), bf16),
    )


def wave_parts(columns):
    quarter = columns // 4
    return [
        (g, n, (g * 2 * quarter + n, (g * 2 + 1) * quarter + n))
        for g in (0, 1)
        for n in range(0, quarter, LANES)
    ]


def half_rates(group, first, count, columns):
    lane = lax.broadcasted_iota(jnp.int32, (1, count), 1) + first
    wave = (2 * lane + group).astype(f32)
    sine = jnp.sin(wave * (np.pi / columns))
    return 2.0 * sine * sine


def both_ways(pairs):
    return [p for a, b in pairs for p in ((a, b), (b, a))]


def channel_column(row, channels, first):
    n = row.shape[1]
    lane = lax.broadcasted_iota(jnp.int32, (channels, n), 1)
    sub = lax.broadcasted_iota(jnp.int32, (channels, n), 0)
    return jnp.sum(jnp.where(lane == sub + first, row, 0.0), axis=1, keepdims=True)


def to_tiles(surface):
    cols = surface.shape[1]
    return jnp.concatenate(
        [surface[:, k : k + LANES] for k in range(0, cols, LANES)], axis=0
    )


def from_tiles(tiles, rows):
    return jnp.concatenate(
        [tiles[k : k + rows] for k in range(0, tiles.shape[0], rows)], axis=1
    )


def decay_terms(diff_column, rates):
    half = 0.5 / diff_column + rates
    sinh = jnp.sqrt(half * (half + 2.0))
    grow = 1.0 + half + sinh
    return 1.0 / grow, jnp.log(grow), sinh


def start_kernel(
    groups_x, paired, x_hbm, wet_hbm, flux_hbm, diff_hbm, table_hbm, *refs
):
    outs = 7 if paired else 8
    s_hbm, coarse_hbm, y_hbm, *message_hbm = refs[:outs]
    s_ref, coarse_ref, y_ref, *message_ref = refs[outs : 2 * outs]
    e1_ref, e3_ref, e2_ref, e4_ref = message_ref[:4]
    if not paired:
        pq_ref = message_ref[4]
    (
        x_ref, wet_ref, flux_ref, diff_ref, table_ref, flat_ref, row_ref, edge_ref,
        x_sem, sem, out_sem,
    ) = refs[2 * outs :]
    rows, channels, columns = x_ref.shape
    half = columns // 2
    row_group = lax.axis_index("gx")
    col_group = lax.axis_index("gy")
    is_atmos = lax.axis_index("comp") == 0

    x_copies = [
        pltpu.make_async_copy(x_hbm.at[0, r], x_ref.at[r], x_sem.at[r]) for r in range(rows)
    ]
    surface_copies = [
        pltpu.make_async_copy(s_ref, s_hbm, out_sem.at[0]),
        pltpu.make_async_copy(coarse_ref, coarse_hbm, out_sem.at[1]),
    ]
    y_copies = [
        pltpu.make_async_copy(y_ref.at[r], y_hbm.at[r], out_sem.at[2 + r]) for r in range(rows)
    ]
    message_copies = [
        pltpu.make_async_copy(ref, hbm, out_sem.at[2 + rows + k])
        for k, (ref, hbm) in enumerate(zip(message_ref, message_hbm))
    ]

    def send_surface():
        surface = to_tiles(row_ref[...])
        s_ref[...] = surface
        coarse_ref[...] = surface.astype(bf16)
        for copy in surface_copies:
            copy.start()

    @pl.when(is_atmos)
    def _():
        flux_copy = pltpu.make_async_copy(flux_hbm, flux_ref, sem.at[0])
        diff_copy = pltpu.make_async_copy(diff_hbm, diff_ref, sem.at[1])
        table_copy = pltpu.make_async_copy(table_hbm, table_ref, sem.at[2])
        for copy in [flux_copy, diff_copy] + x_copies + [table_copy]:
            copy.start()
        first = col_group * channels
        flux_copy.wait()
        weight = channel_column(flux_ref[...], channels, first)
        for r in range(rows):
            x_copies[r].wait()
            row_ref[r : r + 1, :] = jnp.sum(x_ref[r] * weight, axis=0, keepdims=True)
            left, right = x_ref[r, :, :half], x_ref[r, :, half:]
            flat_ref[r * channels : (r + 1) * channels, :half] = (left + right).astype(bf16)
            flat_ref[r * channels : (r + 1) * channels, half:] = (left - right).astype(bf16)
        send_surface()
        table_copy.wait()
        for k in range(2):
            lanes = slice(k * half, (k + 1) * half)
            part = jnp.dot(
                flat_ref[:, lanes], table_ref[lanes, :], preferred_element_type=f32
            )
            y_ref[:, :, lanes] = part.reshape(rows, channels, half)
        for copy in y_copies:
            copy.start()
        diff_copy.wait()
        diff = channel_column(diff_ref[...], channels, first)
        total = rows * groups_x
        base = (row_group * rows).astype(f32)
        for group, n, parts in wave_parts(columns):
            lam, alpha, _ = decay_terms(diff, half_rates(group, n, LANES, columns))
            lam2 = lam * lam
            low = jnp.exp(-2.0 * base * alpha)
            high = jnp.exp(-2.0 * (total - rows - base) * alpha)
            for part in parts:
                lanes = slice(part, part + LANES)
                power = low
                p = jnp.zeros((channels, LANES), f32)
                for r in range(rows):
                    power = power * lam2
                    p = lam * p + (1.0 - power) * y_ref[r, :, lanes]
                power = high
                q = jnp.zeros((channels, LANES), f32)
                for r in reversed(range(rows)):
                    power = power * lam2
                    q = lam * q + (1.0 - power) * y_ref[r, :, lanes]
                if paired:
                    for mask, out in ((1, e1_ref), (2, e2_ref), (3, e3_ref)):
                        upward = row_group < (row_group ^ mask)
                        out[0:channels, lanes] = jnp.where(upward, p, q).astype(bf16)
                else:
                    pq_ref[0, :, lanes] = p.astype(bf16)
                    pq_ref[1, :, lanes] = q.astype(bf16)
        for copy in message_copies:
            copy.start()
        for copy in surface_copies + y_copies + message_copies:
            copy.wait()

    @pl.when(jnp.logical_not(is_atmos))
    def _():
        wet_copy = pltpu.make_async_copy(wet_hbm, wet_ref, sem.at[0])
        for copy in x_copies + [wet_copy]:
            copy.start()
        gain = jnp.where(col_group == 0, 1.0, 0.0)
        for r in range(rows):
            x_copies[r].wait()
            row_ref[r : r + 1, :] = x_ref[r, 0:1, :] * gain
        send_surface()
        wet_copy.wait()
        levels = channels // 2
        lines = 2 * channels
        even_x = row_group % 2 == 0
        even_y = col_group % 2 == 0
        wet = wet_ref[...].astype(f32)
        wet = jnp.concatenate([wet, wet], axis=0).astype(bf16)

        def put(out, last):
            @pl.when(last)
            def _():
                out[0:lines, :] = x_ref[rows - 2 :].reshape(lines, columns).astype(bf16)

            @pl.when(jnp.logical_not(last))
            def _():
                out[0:lines, :] = x_ref[:2].reshape(lines, columns).astype(bf16)

            out[lines : lines + 16, :] = wet

        put(e1_ref, even_x)
        put(e3_ref, jnp.logical_not(even_x))

        def put_edges(out, level):
            for r in range(rows):
                for t in range(2):
                    at = (r * 2 + t) * 2
                    c = t * levels + level
                    edge_ref[at : at + 2, :] = x_ref[r, c : c + 2, :]
            out[...] = edge_ref[...].astype(bf16)

        @pl.when(even_y)
        def _():
            put_edges(e2_ref, levels - 2)
            put_edges(e4_ref, 0)

        @pl.when(jnp.logical_not(even_y))
        def _():
            put_edges(e2_ref, 0)
            put_edges(e4_ref, levels - 2)

        for copy in message_copies:
            copy.start()
        for copy in surface_copies + message_copies:
            copy.wait()


def one_hot_kernel(
    rows, columns, a_src, a_dst, m_src, m_dst, _, src_hot_ref, dst_hot_ref, src_row_ref, dst_row_ref
):
    is_atmos = lax.axis_index("comp") == 0
    blocks, points = src_row_ref.shape
    lane_iota = lax.broadcasted_iota(jnp.int32, (LANES, points), 0)
    for a_ref, m_ref, hot_ref, row_ref in (
        (a_src, m_src, src_hot_ref, src_row_ref),
        (a_dst, m_dst, dst_hot_ref, dst_row_ref),
    ):
        index = jnp.where(is_atmos, m_ref[0, 0], a_ref[0, 0])
        row = index // columns
        tile = (index // LANES) % (columns // LANES)
        row_ref[...] = tile * rows + row
        lane = index % LANES
        for b in range(blocks):
            hot_ref[:, b * points : (b + 1) * points] = jnp.where(
                lane_iota == lane[b : b + 1], 1.0, 0.0
            ).astype(bf16)


def regrid_kernel(n_surfaces, *refs):
    surfaces = refs[:n_surfaces]
    (
        src_hot_ref, dst_hot_ref, src_row_ref, dst_row_ref, a_count, m_count, a_weight, m_weight,
        _, _,
        land_ref, sent_ref, weight_ref, gath_ref, val_ref, sem,
    ) = refs[n_surfaces:]
    is_atmos = lax.axis_index("comp") == 0
    blocks, points = val_ref.shape
    cells = surfaces[0].shape[0]

    @pl.when(is_atmos)
    def _():
        pltpu.make_async_copy(m_weight.at[0, 0], weight_ref, sem).start()

    @pl.when(jnp.logical_not(is_atmos))
    def _():
        pltpu.make_async_copy(a_weight.at[0, 0], weight_ref, sem).start()

    count = jnp.where(is_atmos, m_count[0, 0], a_count[0, 0])
    pair = 2 * points
    row_iota = lax.broadcasted_iota(jnp.int32, (cells, points), 0)
    table = sum(surface[...].astype(f32) for surface in surfaces).astype(bf16)
    for b in range(0, blocks, 2):
        picked = jnp.dot(
            table, src_hot_ref[:, b * points : b * points + pair], preferred_element_type=f32
        )
        for k in range(2):
            mine = row_iota == src_row_ref[b + k : b + k + 1, :]
            part = jnp.where(mine, picked[:, k * points : (k + 1) * points], 0.0)
            gath_ref[b + k : b + k + 1, :] = jnp.sum(part, axis=0, keepdims=True)
    gathered = gath_ref[...].astype(bf16)

    @pl.when(is_atmos)
    def _():
        pltpu.make_async_copy(m_weight.at[0, 0], weight_ref, sem).wait()

    @pl.when(jnp.logical_not(is_atmos))
    def _():
        pltpu.make_async_copy(a_weight.at[0, 0], weight_ref, sem).wait()

    block_iota = lax.broadcasted_iota(jnp.int32, (blocks, points), 0)
    values = jnp.zeros((blocks, points), f32)
    for b in range(0, blocks, 2):
        terms = lax.dot_general(
            gathered,
            weight_ref[b : b + 2].reshape(pair, points),
            (((1,), (1,)), ((), ())),
            preferred_element_type=f32,
        )
        for k in range(2):
            values = jnp.where(block_iota == b + k, terms[:, k * points : (k + 1) * points], values)
    val_ref[...] = jnp.where(block_iota < count, values, 0.0)
    land = jnp.zeros((2 * cells, LANES), f32)
    for b in range(0, blocks, 2):
        spread = []
        for k in range(b, b + 2):
            value = val_ref[k : k + 1, :]
            coarse = value.astype(bf16).astype(f32)
            fine = value - coarse
            mine = row_iota == dst_row_ref[k : k + 1, :]
            spread.append(
                jnp.concatenate(
                    [jnp.where(mine, coarse, 0.0), jnp.where(mine, fine, 0.0)], axis=0
                ).astype(bf16)
            )
        land = land + lax.dot_general(
            jnp.concatenate(spread, axis=1),
            dst_hot_ref[:, b * points : b * points + pair],
            (((1,), (1,)), ((), ())),
            preferred_element_type=f32,
        )
    land = land[:cells] + land[cells:]
    land_ref[...] = land
    sent_ref[...] = land.astype(bf16)


def heat_kernel(rows, e2_ref, e4_ref, land_ref, part_ref, _, sum_ref, near_ref, far_ref):
    cells = land_ref.shape[0]
    columns = cells // rows * LANES
    even_x = lax.axis_index("gx") % 2 == 0
    even_y = lax.axis_index("gy") % 2 == 0
    total = land_ref[...] + part_ref[...].astype(f32)
    sum_ref[...] = total

    def corners(row):
        start = row * 4 // 16 * 16
        one = e2_ref[start : start + 16, :].astype(f32)
        two = e4_ref[start : start + 16, :].astype(f32)
        low = jnp.where(even_y, two, one)
        high = jnp.where(even_y, one, two)
        at = row * 4 - start
        lines = [low[at + 1 : at + 2], low[at + 3 : at + 4], high[at : at + 1], high[at + 2 : at + 3]]
        return to_tiles(jnp.concatenate(lines + [jnp.zeros((4, columns), f32)], axis=0))

    first, last = corners(0), corners(rows - 1)
    near_ref[0:cells, :] = total.astype(bf16)
    far_ref[0:cells, :] = total.astype(bf16)
    near_ref[cells:, :] = jnp.where(even_x, last, first).astype(bf16)
    far_ref[cells:, :] = jnp.where(even_x, first, last).astype(bf16)


def advance(ref, r, t, coefs, size):
    ring, columns = ref.shape[2:]
    whole = ref[r, t]
    up = pltpu.roll(whole, 1, 0)[:size]
    down = pltpu.roll(whole, ring - 1, 0)[:size]
    mid = whole[:size]
    total = coefs[0] * mid + coefs[5] * (up + down)
    total = total + coefs[1] * ref[r - 1, t, 0:size, :]
    total = total + coefs[2] * ref[r + 1, t, 0:size, :]
    total = total + coefs[3] * pltpu.roll(mid, 1, 1)
    return total + coefs[4] * pltpu.roll(mid, columns - 1, 1)


def first_step_kernel(
    groups_x, groups_y, paired, x_ref, wet_ref, diff_ref, y_ref, e1_ref, e3_ref,
    e2_ref, e4_ref, *refs,
):
    if not paired:
        pin_ref, qin_ref = refs[:2]
    zb_ref, c_ref, t1_ref, z_ref, t0_ref, w_ref = refs[-6:]
    _, rows, channels, columns = x_ref.shape
    row_group = lax.axis_index("gx")
    col_group = lax.axis_index("gy")
    is_atmos = lax.axis_index("comp") == 0

    @pl.when(is_atmos)
    def _():
        diff = channel_column(diff_ref[...], channels, col_group * channels)
        total = rows * groups_x
        base = (row_group * rows).astype(f32)
        for group, n, parts in wave_parts(columns):
            lam, alpha, sinh = decay_terms(diff, half_rates(group, n, LANES, columns))
            lam2 = lam * lam
            low = jnp.exp(-2.0 * base * alpha)
            high = jnp.exp(-2.0 * (total - rows - base) * alpha)
            scale = 1.0 / (
                2.0 * diff * sinh * (1.0 - jnp.exp(-2.0 * (total + 1) * alpha))
            )
            lows, highs = [], []
            power = low
            for r in range(rows):
                power = power * lam2
                lows.append(1.0 - power)
            power = high
            for r in range(rows):
                power = power * lam2
                highs.append(1.0 - power)
            highs = highs[::-1]
            for part in parts:
                lanes = slice(part, part + LANES)
                if paired:
                    pin = jnp.zeros((channels, LANES), f32)
                    qin = jnp.zeros((channels, LANES), f32)
                    for mask, msg in ((1, e1_ref), (2, e2_ref), (3, e3_ref)):
                        band = row_group ^ mask
                        gap = (jnp.abs(row_group - band) - 1) * rows
                        term = jnp.exp(-gap.astype(f32) * alpha)
                        term = term * msg[0:channels, lanes].astype(f32)
                        pin = pin + jnp.where(band < row_group, term, 0.0)
                        qin = qin + jnp.where(band > row_group, term, 0.0)
                else:
                    pin = pin_ref[:, lanes]
                    qin = qin_ref[:, lanes]
                f = pin
                for r in range(rows):
                    f = lam * f + lows[r] * y_ref[r, :, lanes]
                    z_ref[r] = highs[r] * f
                g = lam * qin
                for r in reversed(range(rows)):
                    z = scale * (z_ref[r] + lows[r] * g)
                    zb_ref[r * channels : (r + 1) * channels, lanes] = z.astype(bf16)
                    g = lam * (g + highs[r] * y_ref[r, :, lanes])

    @pl.when(jnp.logical_not(is_atmos))
    def _():
        levels = channels // 2
        ring = levels + 8
        lines = 2 * channels
        first_x = row_group == 0
        last_x = row_group == groups_x - 1
        top = col_group == 0
        bottom = col_group == groups_y - 1
        even_x = row_group % 2 == 0
        even_y = col_group % 2 == 0

        one = e1_ref[lines : lines + 16, :].astype(f32)
        three = e3_ref[lines : lines + 16, :].astype(f32)
        below = jnp.where(even_x, three, one)[rows - 2 : rows]
        above = jnp.where(even_x, one, three)[0:2]
        w_ref[0:2, :] = jnp.where(first_x, 0.0, below)
        w_ref[2 : rows + 2, :] = wet_ref[...].astype(f32)
        w_ref[rows + 2 : rows + 4, :] = jnp.where(last_x, 0.0, above)

        span = rows + 2
        north = w_ref[0:span, :]
        here = w_ref[1 : span + 1, :]
        south = w_ref[2 : span + 2, :]
        west = pltpu.roll(here, 1, 1)
        east = pltpu.roll(here, columns - 1, 1)
        c_ref[0, 0:span, :] = here * (
            1.0 - 2.0 * mixing_rate - spread_rate * (north + south + west + east)
        )
        c_ref[1, 0:span, :] = spread_rate * here * north
        c_ref[2, 0:span, :] = spread_rate * here * south
        c_ref[3, 0:span, :] = spread_rate * here * west
        c_ref[4, 0:span, :] = spread_rate * here * east
        c_ref[5, 0:span, :] = mixing_rate * here
        c_ref[6, 0:span, :] = here

        one = e1_ref[0:lines, :].astype(f32)
        three = e3_ref[0:lines, :].astype(f32)
        below = jnp.where(even_x, three, one)
        above = jnp.where(even_x, one, three)
        blank = jnp.zeros((8, columns), f32)
        for k in range(2):
            for t in range(2):
                c = k * channels + t * levels
                t0_ref[k, t, 0:levels, :] = below[c : c + levels]
                t0_ref[rows + 2 + k, t, 0:levels, :] = above[c : c + levels]
                t0_ref[k, t, levels:ring, :] = blank
                t0_ref[rows + 2 + k, t, levels:ring, :] = blank
        one = e2_ref[...].astype(f32)
        two = e4_ref[...].astype(f32)
        before = jnp.where(even_y, two, one)
        after = jnp.where(even_y, one, two)
        for r in range(rows):
            for t in range(2):
                k = (r * 2 + t) * 2
                t0_ref[r + 2, t, 0:levels, :] = x_ref[0, r, t * levels : (t + 1) * levels, :]
                t0_ref[r + 2, t, levels : levels + 2, :] = after[k : k + 2]
                t0_ref[r + 2, t, ring - 2 : ring, :] = before[k : k + 2]

        def close(ref, r):
            for t in range(2):
                ref[r, t, ring - 1 : ring, :] = jnp.where(
                    top, ref[r, t, 0:1, :], ref[r, t, ring - 1 : ring, :]
                )
                ref[r, t, levels : levels + 1, :] = jnp.where(
                    bottom, ref[r, t, levels - 1 : levels, :], ref[r, t, levels : levels + 1, :]
                )

        def first(r, carry):
            coefs = [c_ref[k, pl.ds(r, 1), :] for k in range(6)]
            close(t0_ref, r + 1)
            for t in range(2):
                t1_ref[r, t] = advance(t0_ref, r + 1, t, coefs, ring)
            close(t1_ref, r)
            return carry

        lax.fori_loop(0, span, first, 0)


def second_step_kernel(gain_ref, table_ref, zb_ref, c_ref, t1_ref, base_ref, column_ref):
    rows, channels, columns = base_ref.shape
    is_atmos = lax.axis_index("comp") == 0

    @pl.when(is_atmos)
    def _():
        response = channel_column(gain_ref[...], channels, lax.axis_index("gy") * channels)
        column_ref[...] = jnp.broadcast_to(response, column_ref.shape)
        half = columns // 2
        step = 256
        for n in range(0, half, step):
            even, odd = [
                jnp.dot(
                    zb_ref[:, k * half : (k + 1) * half],
                    table_ref[k * half : (k + 1) * half, n : n + step],
                    preferred_element_type=f32,
                ).reshape(rows, channels, step)
                for k in range(2)
            ]
            base_ref[:, :, n : n + step] = even + odd
            base_ref[:, :, n + half : n + half + step] = even - odd

    @pl.when(jnp.logical_not(is_atmos))
    def _():
        levels = channels // 2

        def second(r, carry):
            coefs = [c_ref[k, pl.ds(r, 1), :] for k in range(6)]
            for t in range(2):
                c = t * levels
                base_ref[r - 1, c : c + levels, :] = advance(t1_ref, r, t, coefs, levels)
            return carry

        lax.fori_loop(1, rows + 1, second, 0)


def last_kernel(
    groups_x, groups_y, column_ref, base_ref, c_ref, sum_ref, near_ref, far_ref, out_ref, e_ref
):
    _, rows, channels, columns = out_ref.shape
    row_group = lax.axis_index("gx")
    col_group = lax.axis_index("gy")
    is_atmos = lax.axis_index("comp") == 0

    @pl.when(is_atmos)
    def _():
        for k in range(columns // LANES):
            lanes = slice(k * LANES, (k + 1) * LANES)
            for r in range(rows):
                at = k * rows + r
                out_ref[0, r, :, lanes] = (
                    base_ref[r, :, lanes] + column_ref[...] * sum_ref[at : at + 1, :]
                )

    @pl.when(jnp.logical_not(is_atmos))
    def _():
        out_ref[0] = base_ref[...]
        levels = channels // 2
        cells = sum_ref.shape[0]
        even = row_group % 2 == 0
        below = jnp.where(even, far_ref[...].astype(f32), near_ref[...].astype(f32))
        above = jnp.where(even, near_ref[...].astype(f32), far_ref[...].astype(f32))

        low = from_tiles(below[cells:], 8)
        high = from_tiles(above[cells:], 8)
        by_low = c_ref[1, 1:2, :] * (c_ref[5, 0:1, :] + c_ref[5, 1:2, :])
        by_high = c_ref[2, rows : rows + 1, :] * (
            c_ref[5, rows : rows + 1, :] + c_ref[5, rows + 1 : rows + 2, :]
        )
        has_before = jnp.where(col_group > 0, 1.0, 0.0)
        has_after = jnp.where(col_group < groups_y - 1, 1.0, 0.0)
        for t in range(2):
            for r, factor, lines in ((0, by_low, low), (rows - 1, by_high, high)):
                c = t * levels
                out_ref[0, r, c : c + 1, :] = out_ref[0, r, c : c + 1, :] + (
                    has_before * factor * lines[t : t + 1]
                )
                c = c + levels - 1
                out_ref[0, r, c : c + 1, :] = out_ref[0, r, c : c + 1, :] + (
                    has_after * factor * lines[t + 2 : t + 3]
                )

        @pl.when(col_group == 0)
        def _():
            span = rows + 2
            e_ref[0:1, :] = from_tiles(below[:cells], rows)[rows - 1 : rows]
            e_ref[1 : rows + 1, :] = from_tiles(sum_ref[...], rows)
            e_ref[rows + 1 : span, :] = from_tiles(above[:cells], rows)[0:1]
            e_ref[0:span, :] = c_ref[6, 0:span, :] * e_ref[0:span, :]
            own = slice(1, rows + 1)
            heat = e_ref[own, :]
            second = c_ref[5, own, :] * heat
            first = (c_ref[0, own, :] + 1.0) * heat + second
            first = first + c_ref[1, own, :] * e_ref[0:rows, :]
            first = first + c_ref[2, own, :] * e_ref[2 : rows + 2, :]
            first = first + c_ref[3, own, :] * pltpu.roll(heat, 1, 1)
            first = first + c_ref[4, own, :] * pltpu.roll(heat, columns - 1, 1)
            for t, gain in enumerate((heat_gain, salt_gain)):
                c = t * levels
                for r in range(rows):
                    lines = jnp.concatenate([first[r : r + 1], second[r : r + 1]], axis=0)
                    out_ref[0, r, c : c + 2, :] = out_ref[0, r, c : c + 2, :] + gain * lines


def local(
    fields,
    wet_cells,
    flux_weight,
    variable_sea_response,
    diffusivity,
    a2o_source,
    a2o_target,
    a2o_count,
    a2o_weight,
    marine_air_input_index,
    marine_air_output_index,
    marine_air_piece_tally,
    marine_air_piece_factor,
):
    _, rows, channels, columns = fields.shape
    groups_x = lax.axis_size("gx")
    groups_y = lax.axis_size("gy")
    blocks, points = a2o_source.shape[2:]
    cells = rows * columns // LANES
    forward, inverse = fourier_tables(columns)
    flux_row = flux_weight[None, :]
    gain_row = variable_sea_response[None, :]
    diff_row = diffusivity[None, :]
    paired = groups_x == 4
    params = functools.partial(pltpu.CompilerParams, vmem_limit_bytes=40 * 2**20)
    vmem = pl.BlockSpec(memory_space=pltpu.VMEM)
    smem = pl.BlockSpec(memory_space=pltpu.SMEM)
    hbm = pl.BlockSpec(memory_space=pltpu.HBM)
    anywhere = pl.BlockSpec(memory_space=pl.ANY)

    def shape(dims, dtype):
        return jax.ShapeDtypeStruct(dims, dtype)

    lines = 2 * channels + 16
    shapes = [
        shape((cells, LANES), f32),
        shape((cells, LANES), bf16),
        shape((rows, channels, columns), f32),
        shape((lines, columns), bf16),
        shape((lines, columns), bf16),
        shape((4 * rows, columns), bf16),
        shape((4 * rows, columns), bf16),
    ]
    if not paired:
        shapes.append(shape((2, channels, columns), bf16))
    partial_surface, coarse, y, e1, e3, e2, e4, *sums = pl.pallas_call(
        functools.partial(start_kernel, groups_x, paired),
        out_shape=shapes,
        in_specs=[hbm] * 5,
        out_specs=[hbm] * len(shapes),
        scratch_shapes=[pltpu.VMEM(out.shape, out.dtype) for out in shapes]
        + [
            pltpu.VMEM((rows, channels, columns), f32),
            pltpu.VMEM((rows, columns), jnp.int32),
            pltpu.VMEM(flux_row.shape, f32),
            pltpu.VMEM(diff_row.shape, f32),
            pltpu.VMEM(forward.shape, bf16),
            pltpu.VMEM((rows * channels, columns), bf16),
            pltpu.VMEM((rows, columns), f32),
            pltpu.VMEM((4 * rows, columns), f32),
            pltpu.SemaphoreType.DMA((rows,)),
            pltpu.SemaphoreType.DMA((3,)),
            pltpu.SemaphoreType.DMA((rows + len(shapes) - 1,)),
        ],
        compiler_params=pltpu.CompilerParams(vmem_limit_bytes=58 * 2**20),
        name="surface_and_forward_or_halos",
    )(fields, wet_cells, flux_row, diff_row, forward)

    masks = [1 << bit for bit in range(groups_y.bit_length() - 1)]

    def sum_route(mask):
        return [(j, j ^ mask) for j in range(groups_y)]

    def partner_route(mask):
        return both_ways([(j, groups_y + (j ^ mask)) for j in range(groups_y)])

    surface = partial_surface
    for mask in masks[:-1]:
        surface = surface + lax.ppermute(coarse, "gy", sum_route(mask)).astype(f32)
        coarse = surface.astype(bf16)
    surfaces = [
        lax.ppermute(coarse, ("comp", "gy"), partner_route(mask)) for mask in masks[-1:] + [0]
    ]

    def ring_pairs(count, odd):
        return [(a, (a + 1) % count) for a in range(odd, count, 2)]

    def flat(comp, i, j):
        return (comp * groups_x + i) * groups_y + j

    def level_route(odd):
        pairs = []
        for i in range(groups_x):
            linked = [(a, a + 1) for a in range(odd, groups_y - 1, 2)]
            alone = set(range(groups_y)) - {j for pair in linked for j in pair}
            pairs += [(flat(1, i, a), flat(1, i, b)) for a, b in linked]
            if i % 2 == 0:
                pairs += [(flat(1, i, j), flat(1, i + 1, j)) for j in sorted(alone)]
                if odd or not paired:
                    pairs += [(flat(0, i, j), flat(0, i + 1, j)) for j in range(groups_y)]
            if paired and not odd and i < i ^ 2:
                pairs += [(flat(0, i, j), flat(0, i ^ 2, j)) for j in range(groups_y)]
        return both_ways(pairs)

    e1 = lax.ppermute(e1, "gx", both_ways(ring_pairs(groups_x, 0)))
    e3 = lax.ppermute(e3, "gx", both_ways(ring_pairs(groups_x, 1)))
    axes = ("comp", "gx", "gy")
    e2 = lax.ppermute(e2, axes, level_route(0))
    e4 = lax.ppermute(e4, axes, level_route(1))

    one_hots = pl.pallas_call(
        functools.partial(one_hot_kernel, rows, columns),
        out_shape=[
            shape((LANES, blocks * points), bf16),
            shape((LANES, blocks * points), bf16),
            shape((blocks, points), jnp.int32),
            shape((blocks, points), jnp.int32),
        ],
        in_specs=[vmem] * 4 + [anywhere],
        out_specs=[vmem] * 4,
        compiler_params=params(),
        name="one_hots",
    )(a2o_source, a2o_target, marine_air_input_index, marine_air_output_index, coarse)
    landing, sent = pl.pallas_call(
        functools.partial(regrid_kernel, len(surfaces)),
        out_shape=[shape((cells, LANES), f32), shape((cells, LANES), bf16)],
        in_specs=[vmem] * (len(surfaces) + 4) + [smem, smem, hbm, hbm, anywhere, anywhere],
        out_specs=[vmem] * 2,
        scratch_shapes=[
            pltpu.VMEM((blocks, points, points), bf16),
            pltpu.VMEM((blocks, points), f32),
            pltpu.VMEM((blocks, points), f32),
            pltpu.SemaphoreType.DMA,
        ],
        compiler_params=params(),
        name="regrid_blocks",
    )(
        *surfaces, *one_hots, a2o_count, marine_air_piece_tally,
        a2o_weight, marine_air_piece_factor, e1, e3,
    )
    for mask in masks[:-1]:
        landing = landing + lax.ppermute(sent, "gy", sum_route(mask)).astype(f32)
        sent = landing.astype(bf16)
    part = lax.ppermute(sent, "gy", sum_route(masks[-1]))

    extra = []
    if not paired:
        p, q = jnp.moveaxis(lax.all_gather(sums[0], "gx").astype(f32), 1, 0)
        viscous = lax.dynamic_slice_in_dim(
            diffusivity, lax.axis_index("gy") * channels, channels
        )[:, None]
        rates = [half_rates(g, 0, columns // 4, columns) for g in (0, 0, 1, 1)]
        _, alpha, _ = decay_terms(viscous, jnp.concatenate(rates, axis=1))
        gap = lax.axis_index("gx") - jnp.arange(groups_x)
        decay = jnp.exp(
            -(rows * jnp.maximum(jnp.abs(gap) - 1, 0))[:, None, None] * alpha[None]
        )
        extra = [
            jnp.sum(jnp.where((gap > 0)[:, None, None], decay * p, 0.0), axis=0),
            jnp.sum(jnp.where((gap < 0)[:, None, None], decay * q, 0.0), axis=0),
        ]
    ring = channels // 2 + 8
    damped, coefs, stepped = pl.pallas_call(
        functools.partial(first_step_kernel, groups_x, groups_y, paired),
        out_shape=[
            shape((rows * channels, columns), bf16),
            shape((7, 16, columns), f32),
            shape((rows + 2, 2, ring, columns), f32),
        ],
        in_specs=[vmem] * (8 + len(extra)),
        out_specs=[vmem] * 3,
        scratch_shapes=[
            pltpu.VMEM((rows, channels, LANES), f32),
            pltpu.VMEM((rows + 4, 2, ring, columns), f32),
            pltpu.VMEM((16, columns), f32),
        ],
        compiler_params=params(),
        name="damping_or_first_step",
    )(fields, wet_cells, diff_row, y, e1, e3, e2, e4, *extra)

    surface_sum, near, far = pl.pallas_call(
        functools.partial(heat_kernel, rows),
        out_shape=[
            shape((cells, LANES), f32),
            shape((cells + columns // 16, LANES), bf16),
            shape((cells + columns // 16, LANES), bf16),
        ],
        in_specs=[vmem] * 4 + [anywhere],
        out_specs=[vmem] * 3,
        compiler_params=params(),
        name="surface_sum",
    )(e2, e4, landing, part, coefs)

    near = lax.ppermute(near, "gx", both_ways(ring_pairs(groups_x, 0)))
    far = lax.ppermute(far, "gx", both_ways(ring_pairs(groups_x, 1)))
    base, column = pl.pallas_call(
        second_step_kernel,
        out_shape=[shape((rows, channels, columns), f32), shape((channels, LANES), f32)],
        in_specs=[vmem] * 5,
        out_specs=[vmem] * 2,
        compiler_params=params(),
        name="inverse_or_second_step",
    )(gain_row, inverse, damped, coefs, stepped)
    return pl.pallas_call(
        functools.partial(last_kernel, groups_x, groups_y),
        out_shape=shape(fields.shape, f32),
        in_specs=[vmem] * 6,
        out_specs=vmem,
        scratch_shapes=[pltpu.VMEM((16, columns), f32)],
        compiler_params=params(),
        name="add_surface_terms",
    )(column, base, coefs, surface_sum, near, far)


def solution(mesh):
    in_specs = (
        P("comp", "gx", "gy", None),
        P("gx", None),
        P(),
        P(),
        P(),
        P("gx", "gy", None, None),
        P("gx", "gy", None, None),
        P("gx", "gy"),
        P("gx", "gy", None, None, None),
        P("gx", "gy", None, None),
        P("gx", "gy", None, None),
        P("gx", "gy"),
        P("gx", "gy", None, None, None),
    )
    out_specs = P("comp", "gx", "gy", None)
    return jax.shard_map(local, mesh=mesh, in_specs=in_specs, out_specs=out_specs, check_vma=False)
```

```python
import functools

import jax
import jax.numpy as jnp
import numpy as np
from jax import lax
from jax.experimental import pallas as pl
from jax.experimental.pallas import tpu as pltpu
from jax.sharding import PartitionSpec as P

spread_rate = 0.2
mixing_rate = 0.1
heat_gain = 0.5
salt_gain = -0.25
LANES = 128
f32 = jnp.float32
bf16 = jnp.bfloat16


def fourier_tables(columns):
    half = columns // 2
    forward, inverse = [], []
    for first in (0, 1):
        waves = np.arange(first, half, 2)
        phase = np.arange(half)[:, None] * waves[None, :] % columns
        angles = phase * (2.0 * np.pi / columns)
        table = np.concatenate([np.cos(angles), np.sin(angles)], axis=1)
        weight = np.where(waves == 0, 1.0, 2.0) / columns
        forward.append(table)
        inverse.append(table.T * np.concatenate([weight, weight])[:, None])
    return (
        jnp.asarray(np.concatenate(forward).astype(np.float32), bf16),
        jnp.asarray(np.concatenate(inverse).astype(np.float32), bf16),
    )


def wave_parts(columns):
    quarter = columns // 4
    return [
        (g, n, (g * 2 * quarter + n, (g * 2 + 1) * quarter + n))
        for g in (0, 1)
        for n in range(0, quarter, LANES)
    ]


def half_rates(group, first, count, columns):
    lane = lax.broadcasted_iota(jnp.int32, (1, count), 1) + first
    wave = (2 * lane + group).astype(f32)
    sine = jnp.sin(wave * (np.pi / columns))
    return 2.0 * sine * sine


def both_ways(pairs):
    return [p for a, b in pairs for p in ((a, b), (b, a))]


def channel_column(row, channels, first):
    n = row.shape[1]
    lane = lax.broadcasted_iota(jnp.int32, (channels, n), 1)
    sub = lax.broadcasted_iota(jnp.int32, (channels, n), 0)
    return jnp.sum(jnp.where(lane == sub + first, row, 0.0), axis=1, keepdims=True)


def to_tiles(surface):
    cols = surface.shape[1]
    return jnp.concatenate(
        [surface[:, k : k + LANES] for k in range(0, cols, LANES)], axis=0
    )


def from_tiles(tiles, rows):
    return jnp.concatenate(
        [tiles[k : k + rows] for k in range(0, tiles.shape[0], rows)], axis=1
    )


def decay_terms(diff_column, rates):
    half = 0.5 / diff_column + rates
    sinh = jnp.sqrt(half * (half + 2.0))
    grow = 1.0 + half + sinh
    return 1.0 / grow, jnp.log(grow), sinh


def surface_kernel(x_hbm, flux_hbm, coarse_ref, x_ref, flux_ref, row_ref, x_sem, sem):
    rows, channels, columns = x_ref.shape
    col_group = lax.axis_index("gy")
    is_atmos = lax.axis_index("comp") == 0
    flux_copy = pltpu.make_async_copy(flux_hbm, flux_ref, sem)
    copies = [
        pltpu.make_async_copy(x_hbm.at[0, r], x_ref.at[r], x_sem.at[r]) for r in range(rows)
    ]

    @pl.when(is_atmos)
    def _():
        for copy in [flux_copy] + copies:
            copy.start()
        flux_copy.wait()
        weight = channel_column(flux_ref[...], channels, col_group * channels)
        for r in range(rows):
            copies[r].wait()
            row_ref[r : r + 1, :] = jnp.sum(x_ref[r] * weight, axis=0, keepdims=True)

    @pl.when(jnp.logical_not(is_atmos))
    def _():
        top = [
            pltpu.make_async_copy(
                x_hbm.at[0, r, pl.ds(0, 8)], x_ref.at[r, pl.ds(0, 8)], x_sem.at[r]
            )
            for r in range(rows)
        ]
        for copy in top:
            copy.start()
        gain = jnp.where(col_group == 0, 1.0, 0.0)
        for r in range(rows):
            top[r].wait()
            row_ref[r : r + 1, :] = x_ref[r, 0:1, :] * gain

    coarse_ref[...] = to_tiles(row_ref[...]).astype(bf16)


def forward_kernel(
    groups_x, paired, x_ref, wet_ref, diff_ref, table_ref, _, *refs
):
    y_ref, e1_ref, e3_ref, e2_ref, e4_ref = refs[:5]
    if not paired:
        pq_ref = refs[5]
    flat_ref, edge_ref = refs[-2:]
    _, rows, channels, columns = x_ref.shape
    half = columns // 2
    row_group = lax.axis_index("gx")
    col_group = lax.axis_index("gy")
    is_atmos = lax.axis_index("comp") == 0

    @pl.when(is_atmos)
    def _():
        first = col_group * channels
        for r in range(rows):
            left, right = x_ref[0, r, :, :half], x_ref[0, r, :, half:]
            flat_ref[r * channels : (r + 1) * channels, :half] = (left + right).astype(bf16)
            flat_ref[r * channels : (r + 1) * channels, half:] = (left - right).astype(bf16)
        for k in range(2):
            lanes = slice(k * half, (k + 1) * half)
            part = jnp.dot(
                flat_ref[:, lanes], table_ref[lanes, :], preferred_element_type=f32
            )
            y_ref[:, :, lanes] = part.reshape(rows, channels, half)
        diff = channel_column(diff_ref[...], channels, first)
        total = rows * groups_x
        base = (row_group * rows).astype(f32)
        for group, n, parts in wave_parts(columns):
            lam, alpha, _ = decay_terms(diff, half_rates(group, n, LANES, columns))
            lam2 = lam * lam
            low = jnp.exp(-2.0 * base * alpha)
            high = jnp.exp(-2.0 * (total - rows - base) * alpha)
            for part in parts:
                lanes = slice(part, part + LANES)
                power = low
                p = jnp.zeros((channels, LANES), f32)
                for r in range(rows):
                    power = power * lam2
                    p = lam * p + (1.0 - power) * y_ref[r, :, lanes]
                power = high
                q = jnp.zeros((channels, LANES), f32)
                for r in reversed(range(rows)):
                    power = power * lam2
                    q = lam * q + (1.0 - power) * y_ref[r, :, lanes]
                if paired:
                    for mask, out in ((1, e1_ref), (2, e2_ref), (3, e3_ref)):
                        upward = row_group < (row_group ^ mask)
                        out[0:channels, lanes] = jnp.where(upward, p, q).astype(bf16)
                else:
                    pq_ref[0, :, lanes] = p.astype(bf16)
                    pq_ref[1, :, lanes] = q.astype(bf16)

    @pl.when(jnp.logical_not(is_atmos))
    def _():
        levels = channels // 2
        lines = 2 * channels
        even_x = row_group % 2 == 0
        even_y = col_group % 2 == 0
        wet = wet_ref[...].astype(f32)
        wet = jnp.concatenate([wet, wet], axis=0).astype(bf16)

        def put(out, last):
            @pl.when(last)
            def _():
                out[0:lines, :] = x_ref[0, rows - 2 :].reshape(lines, columns).astype(bf16)

            @pl.when(jnp.logical_not(last))
            def _():
                out[0:lines, :] = x_ref[0, :2].reshape(lines, columns).astype(bf16)

            out[lines : lines + 16, :] = wet

        put(e1_ref, even_x)
        put(e3_ref, jnp.logical_not(even_x))

        def put_edges(out, level):
            for r in range(rows):
                for t in range(2):
                    at = (r * 2 + t) * 2
                    c = t * levels + level
                    edge_ref[at : at + 2, :] = x_ref[0, r, c : c + 2, :]
            out[...] = edge_ref[...].astype(bf16)

        @pl.when(even_y)
        def _():
            put_edges(e2_ref, levels - 2)
            put_edges(e4_ref, 0)

        @pl.when(jnp.logical_not(even_y))
        def _():
            put_edges(e2_ref, 0)
            put_edges(e4_ref, levels - 2)


def one_hot_kernel(
    rows, columns, a_src, a_dst, m_src, m_dst, _, src_hot_ref, dst_hot_ref, src_row_ref, dst_row_ref
):
    is_atmos = lax.axis_index("comp") == 0
    blocks, points = src_row_ref.shape
    lane_iota = lax.broadcasted_iota(jnp.int32, (LANES, points), 0)
    for a_ref, m_ref, hot_ref, row_ref in (
        (a_src, m_src, src_hot_ref, src_row_ref),
        (a_dst, m_dst, dst_hot_ref, dst_row_ref),
    ):
        index = jnp.where(is_atmos, m_ref[0, 0], a_ref[0, 0])
        row = index // columns
        tile = (index // LANES) % (columns // LANES)
        row_ref[...] = tile * rows + row
        lane = index % LANES
        for b in range(blocks):
            hot_ref[:, b * points : (b + 1) * points] = jnp.where(
                lane_iota == lane[b : b + 1], 1.0, 0.0
            ).astype(bf16)


def regrid_kernel(n_surfaces, *refs):
    surfaces = refs[:n_surfaces]
    (
        src_hot_ref, dst_hot_ref, src_row_ref, dst_row_ref, a_count, m_count, a_weight, m_weight,
        _,
        land_ref, sent_ref, weight_ref, gath_ref, val_ref, count_ref, sem,
    ) = refs[n_surfaces:]
    is_atmos = lax.axis_index("comp") == 0
    blocks, points = val_ref.shape
    cells = surfaces[0].shape[0]

    def operands(weight, count):
        return [
            pltpu.make_async_copy(count, count_ref, sem.at[0]),
            pltpu.make_async_copy(weight.at[0, 0], weight_ref, sem.at[1]),
        ]

    @pl.when(is_atmos)
    def _():
        for copy in operands(m_weight, m_count):
            copy.start()

    @pl.when(jnp.logical_not(is_atmos))
    def _():
        for copy in operands(a_weight, a_count):
            copy.start()

    pair = 2 * points
    row_iota = lax.broadcasted_iota(jnp.int32, (cells, points), 0)
    table = sum(surface[...].astype(f32) for surface in surfaces).astype(bf16)
    for b in range(0, blocks, 2):
        picked = jnp.dot(
            table, src_hot_ref[:, b * points : b * points + pair], preferred_element_type=f32
        )
        for k in range(2):
            mine = row_iota == src_row_ref[b + k : b + k + 1, :]
            part = jnp.where(mine, picked[:, k * points : (k + 1) * points], 0.0)
            gath_ref[b + k : b + k + 1, :] = jnp.sum(part, axis=0, keepdims=True)
    gathered = gath_ref[...].astype(bf16)

    for copy in operands(a_weight, a_count):
        copy.wait()
    count = count_ref[0, 0]
    block_iota = lax.broadcasted_iota(jnp.int32, (blocks, points), 0)
    values = jnp.zeros((blocks, points), f32)
    for b in range(0, blocks, 2):
        terms = lax.dot_general(
            gathered,
            weight_ref[b : b + 2].reshape(pair, points),
            (((1,), (1,)), ((), ())),
            preferred_element_type=f32,
        )
        for k in range(2):
            values = jnp.where(block_iota == b + k, terms[:, k * points : (k + 1) * points], values)
    val_ref[...] = jnp.where(block_iota < count, values, 0.0)
    land = jnp.zeros((2 * cells, LANES), f32)
    for b in range(0, blocks, 2):
        spread = []
        for k in range(b, b + 2):
            value = val_ref[k : k + 1, :]
            coarse = value.astype(bf16).astype(f32)
            fine = value - coarse
            mine = row_iota == dst_row_ref[k : k + 1, :]
            spread.append(
                jnp.concatenate(
                    [jnp.where(mine, coarse, 0.0), jnp.where(mine, fine, 0.0)], axis=0
                ).astype(bf16)
            )
        land = land + lax.dot_general(
            jnp.concatenate(spread, axis=1),
            dst_hot_ref[:, b * points : b * points + pair],
            (((1,), (1,)), ((), ())),
            preferred_element_type=f32,
        )
    land = land[:cells] + land[cells:]
    land_ref[...] = land
    sent_ref[...] = land.astype(bf16)


def heat_kernel(rows, e2_ref, e4_ref, land_ref, part_ref, _, sum_ref, near_ref, far_ref):
    cells = land_ref.shape[0]
    columns = cells // rows * LANES
    even_x = lax.axis_index("gx") % 2 == 0
    even_y = lax.axis_index("gy") % 2 == 0
    total = land_ref[...] + part_ref[...].astype(f32)
    sum_ref[...] = total

    def corners(row):
        start = row * 4 // 16 * 16
        one = e2_ref[start : start + 16, :].astype(f32)
        two = e4_ref[start : start + 16, :].astype(f32)
        low = jnp.where(even_y, two, one)
        high = jnp.where(even_y, one, two)
        at = row * 4 - start
        lines = [low[at + 1 : at + 2], low[at + 3 : at + 4], high[at : at + 1], high[at + 2 : at + 3]]
        return to_tiles(jnp.concatenate(lines + [jnp.zeros((4, columns), f32)], axis=0))

    first, last = corners(0), corners(rows - 1)
    near_ref[0:cells, :] = total.astype(bf16)
    far_ref[0:cells, :] = total.astype(bf16)
    near_ref[cells:, :] = jnp.where(even_x, last, first).astype(bf16)
    far_ref[cells:, :] = jnp.where(even_x, first, last).astype(bf16)


def advance(ref, r, t, coefs, size):
    ring, columns = ref.shape[2:]
    whole = ref[r, t]
    up = pltpu.roll(whole, 1, 0)[:size]
    down = pltpu.roll(whole, ring - 1, 0)[:size]
    mid = whole[:size]
    total = coefs[0] * mid + coefs[5] * (up + down)
    total = total + coefs[1] * ref[r - 1, t, 0:size, :]
    total = total + coefs[2] * ref[r + 1, t, 0:size, :]
    total = total + coefs[3] * pltpu.roll(mid, 1, 1)
    return total + coefs[4] * pltpu.roll(mid, columns - 1, 1)


def first_step_kernel(
    groups_x, groups_y, paired, x_ref, wet_ref, diff_ref, y_ref, e1_ref, e3_ref,
    e2_ref, e4_ref, *refs,
):
    if not paired:
        pin_ref, qin_ref = refs[:2]
    zb_ref, c_ref, t1_ref, z_ref, t0_ref, w_ref = refs[-6:]
    _, rows, channels, columns = x_ref.shape
    row_group = lax.axis_index("gx")
    col_group = lax.axis_index("gy")
    is_atmos = lax.axis_index("comp") == 0

    @pl.when(is_atmos)
    def _():
        diff = channel_column(diff_ref[...], channels, col_group * channels)
        total = rows * groups_x
        base = (row_group * rows).astype(f32)
        for group, n, parts in wave_parts(columns):
            lam, alpha, sinh = decay_terms(diff, half_rates(group, n, LANES, columns))
            lam2 = lam * lam
            low = jnp.exp(-2.0 * base * alpha)
            high = jnp.exp(-2.0 * (total - rows - base) * alpha)
            scale = 1.0 / (
                2.0 * diff * sinh * (1.0 - jnp.exp(-2.0 * (total + 1) * alpha))
            )
            lows, highs = [], []
            power = low
            for r in range(rows):
                power = power * lam2
                lows.append(1.0 - power)
            power = high
            for r in range(rows):
                power = power * lam2
                highs.append(1.0 - power)
            highs = highs[::-1]
            for part in parts:
                lanes = slice(part, part + LANES)
                if paired:
                    pin = jnp.zeros((channels, LANES), f32)
                    qin = jnp.zeros((channels, LANES), f32)
                    for mask, msg in ((1, e1_ref), (2, e2_ref), (3, e3_ref)):
                        band = row_group ^ mask
                        gap = (jnp.abs(row_group - band) - 1) * rows
                        term = jnp.exp(-gap.astype(f32) * alpha)
                        term = term * msg[0:channels, lanes].astype(f32)
                        pin = pin + jnp.where(band < row_group, term, 0.0)
                        qin = qin + jnp.where(band > row_group, term, 0.0)
                else:
                    pin = pin_ref[:, lanes]
                    qin = qin_ref[:, lanes]
                f = pin
                for r in range(rows):
                    f = lam * f + lows[r] * y_ref[r, :, lanes]
                    z_ref[r] = highs[r] * f
                g = lam * qin
                for r in reversed(range(rows)):
                    z = scale * (z_ref[r] + lows[r] * g)
                    zb_ref[r * channels : (r + 1) * channels, lanes] = z.astype(bf16)
                    g = lam * (g + highs[r] * y_ref[r, :, lanes])

    @pl.when(jnp.logical_not(is_atmos))
    def _():
        levels = channels // 2
        ring = levels + 8
        lines = 2 * channels
        first_x = row_group == 0
        last_x = row_group == groups_x - 1
        top = col_group == 0
        bottom = col_group == groups_y - 1
        even_x = row_group % 2 == 0
        even_y = col_group % 2 == 0

        one = e1_ref[lines : lines + 16, :].astype(f32)
        three = e3_ref[lines : lines + 16, :].astype(f32)
        below = jnp.where(even_x, three, one)[rows - 2 : rows]
        above = jnp.where(even_x, one, three)[0:2]
        w_ref[0:2, :] = jnp.where(first_x, 0.0, below)
        w_ref[2 : rows + 2, :] = wet_ref[...].astype(f32)
        w_ref[rows + 2 : rows + 4, :] = jnp.where(last_x, 0.0, above)

        span = rows + 2
        north = w_ref[0:span, :]
        here = w_ref[1 : span + 1, :]
        south = w_ref[2 : span + 2, :]
        west = pltpu.roll(here, 1, 1)
        east = pltpu.roll(here, columns - 1, 1)
        c_ref[0, 0:span, :] = here * (
            1.0 - 2.0 * mixing_rate - spread_rate * (north + south + west + east)
        )
        c_ref[1, 0:span, :] = spread_rate * here * north
        c_ref[2, 0:span, :] = spread_rate * here * south
        c_ref[3, 0:span, :] = spread_rate * here * west
        c_ref[4, 0:span, :] = spread_rate * here * east
        c_ref[5, 0:span, :] = mixing_rate * here
        c_ref[6, 0:span, :] = here

        one = e1_ref[0:lines, :].astype(f32)
        three = e3_ref[0:lines, :].astype(f32)
        below = jnp.where(even_x, three, one)
        above = jnp.where(even_x, one, three)
        blank = jnp.zeros((8, columns), f32)
        for k in range(2):
            for t in range(2):
                c = k * channels + t * levels
                t0_ref[k, t, 0:levels, :] = below[c : c + levels]
                t0_ref[rows + 2 + k, t, 0:levels, :] = above[c : c + levels]
                t0_ref[k, t, levels:ring, :] = blank
                t0_ref[rows + 2 + k, t, levels:ring, :] = blank
        one = e2_ref[...].astype(f32)
        two = e4_ref[...].astype(f32)
        before = jnp.where(even_y, two, one)
        after = jnp.where(even_y, one, two)
        for r in range(rows):
            for t in range(2):
                k = (r * 2 + t) * 2
                t0_ref[r + 2, t, 0:levels, :] = x_ref[0, r, t * levels : (t + 1) * levels, :]
                t0_ref[r + 2, t, levels : levels + 2, :] = after[k : k + 2]
                t0_ref[r + 2, t, ring - 2 : ring, :] = before[k : k + 2]

        def close(ref, r):
            for t in range(2):
                ref[r, t, ring - 1 : ring, :] = jnp.where(
                    top, ref[r, t, 0:1, :], ref[r, t, ring - 1 : ring, :]
                )
                ref[r, t, levels : levels + 1, :] = jnp.where(
                    bottom, ref[r, t, levels - 1 : levels, :], ref[r, t, levels : levels + 1, :]
                )

        def first(r, carry):
            coefs = [c_ref[k, pl.ds(r, 1), :] for k in range(6)]
            close(t0_ref, r + 1)
            for t in range(2):
                t1_ref[r, t] = advance(t0_ref, r + 1, t, coefs, ring)
            close(t1_ref, r)
            return carry

        lax.fori_loop(0, span, first, 0)


def second_step_kernel(gain_ref, table_ref, zb_ref, c_ref, t1_ref, base_ref, column_ref):
    rows, channels, columns = base_ref.shape
    is_atmos = lax.axis_index("comp") == 0

    @pl.when(is_atmos)
    def _():
        response = channel_column(gain_ref[...], channels, lax.axis_index("gy") * channels)
        column_ref[...] = jnp.broadcast_to(response, column_ref.shape)
        half = columns // 2
        step = 256
        for n in range(0, half, step):
            even, odd = [
                jnp.dot(
                    zb_ref[:, k * half : (k + 1) * half],
                    table_ref[k * half : (k + 1) * half, n : n + step],
                    preferred_element_type=f32,
                ).reshape(rows, channels, step)
                for k in range(2)
            ]
            base_ref[:, :, n : n + step] = even + odd
            base_ref[:, :, n + half : n + half + step] = even - odd

    @pl.when(jnp.logical_not(is_atmos))
    def _():
        levels = channels // 2

        def second(r, carry):
            coefs = [c_ref[k, pl.ds(r, 1), :] for k in range(6)]
            for t in range(2):
                c = t * levels
                base_ref[r - 1, c : c + levels, :] = advance(t1_ref, r, t, coefs, levels)
            return carry

        lax.fori_loop(1, rows + 1, second, 0)


def last_kernel(
    groups_x, groups_y, column_ref, base_ref, c_ref, sum_ref, near_ref, far_ref, out_ref, e_ref
):
    _, rows, channels, columns = out_ref.shape
    row_group = lax.axis_index("gx")
    col_group = lax.axis_index("gy")
    is_atmos = lax.axis_index("comp") == 0

    @pl.when(is_atmos)
    def _():
        for k in range(columns // LANES):
            lanes = slice(k * LANES, (k + 1) * LANES)
            for r in range(rows):
                at = k * rows + r
                out_ref[0, r, :, lanes] = (
                    base_ref[r, :, lanes] + column_ref[...] * sum_ref[at : at + 1, :]
                )

    @pl.when(jnp.logical_not(is_atmos))
    def _():
        out_ref[0] = base_ref[...]
        levels = channels // 2
        cells = sum_ref.shape[0]
        even = row_group % 2 == 0
        below = jnp.where(even, far_ref[...].astype(f32), near_ref[...].astype(f32))
        above = jnp.where(even, near_ref[...].astype(f32), far_ref[...].astype(f32))

        low = from_tiles(below[cells:], 8)
        high = from_tiles(above[cells:], 8)
        by_low = c_ref[1, 1:2, :] * (c_ref[5, 0:1, :] + c_ref[5, 1:2, :])
        by_high = c_ref[2, rows : rows + 1, :] * (
            c_ref[5, rows : rows + 1, :] + c_ref[5, rows + 1 : rows + 2, :]
        )
        has_before = jnp.where(col_group > 0, 1.0, 0.0)
        has_after = jnp.where(col_group < groups_y - 1, 1.0, 0.0)
        for t in range(2):
            for r, factor, lines in ((0, by_low, low), (rows - 1, by_high, high)):
                c = t * levels
                out_ref[0, r, c : c + 1, :] = out_ref[0, r, c : c + 1, :] + (
                    has_before * factor * lines[t : t + 1]
                )
                c = c + levels - 1
                out_ref[0, r, c : c + 1, :] = out_ref[0, r, c : c + 1, :] + (
                    has_after * factor * lines[t + 2 : t + 3]
                )

        @pl.when(col_group == 0)
        def _():
            span = rows + 2
            e_ref[0:1, :] = from_tiles(below[:cells], rows)[rows - 1 : rows]
            e_ref[1 : rows + 1, :] = from_tiles(sum_ref[...], rows)
            e_ref[rows + 1 : span, :] = from_tiles(above[:cells], rows)[0:1]
            e_ref[0:span, :] = c_ref[6, 0:span, :] * e_ref[0:span, :]
            own = slice(1, rows + 1)
            heat = e_ref[own, :]
            second = c_ref[5, own, :] * heat
            first = (c_ref[0, own, :] + 1.0) * heat + second
            first = first + c_ref[1, own, :] * e_ref[0:rows, :]
            first = first + c_ref[2, own, :] * e_ref[2 : rows + 2, :]
            first = first + c_ref[3, own, :] * pltpu.roll(heat, 1, 1)
            first = first + c_ref[4, own, :] * pltpu.roll(heat, columns - 1, 1)
            for t, gain in enumerate((heat_gain, salt_gain)):
                c = t * levels
                for r in range(rows):
                    lines = jnp.concatenate([first[r : r + 1], second[r : r + 1]], axis=0)
                    out_ref[0, r, c : c + 2, :] = out_ref[0, r, c : c + 2, :] + gain * lines


def local(
    fields,
    wet_cells,
    flux_weight,
    variable_sea_response,
    diffusivity,
    a2o_source,
    a2o_target,
    a2o_count,
    a2o_weight,
    marine_air_input_index,
    marine_air_output_index,
    marine_air_piece_tally,
    marine_air_piece_factor,
):
    _, rows, channels, columns = fields.shape
    groups_x = lax.axis_size("gx")
    groups_y = lax.axis_size("gy")
    blocks, points = a2o_source.shape[2:]
    cells = rows * columns // LANES
    forward, inverse = fourier_tables(columns)
    flux_row = flux_weight[None, :]
    gain_row = variable_sea_response[None, :]
    diff_row = diffusivity[None, :]
    paired = groups_x == 4
    params = functools.partial(pltpu.CompilerParams, vmem_limit_bytes=40 * 2**20)
    vmem = pl.BlockSpec(memory_space=pltpu.VMEM)
    hbm = pl.BlockSpec(memory_space=pltpu.HBM)
    anywhere = pl.BlockSpec(memory_space=pl.ANY)

    def shape(dims, dtype):
        return jax.ShapeDtypeStruct(dims, dtype)

    coarse = pl.pallas_call(
        surface_kernel,
        out_shape=shape((cells, LANES), bf16),
        in_specs=[hbm, hbm],
        out_specs=vmem,
        scratch_shapes=[
            pltpu.VMEM((rows, channels, columns), f32),
            pltpu.VMEM(flux_row.shape, f32),
            pltpu.VMEM((rows, columns), f32),
            pltpu.SemaphoreType.DMA((rows,)),
            pltpu.SemaphoreType.DMA,
        ],
        compiler_params=pltpu.CompilerParams(vmem_limit_bytes=58 * 2**20),
        name="surface_partials",
    )(fields, flux_row)
    surfaces = []
    for mask in reversed(range(groups_y)):
        route = both_ways([(j, groups_y + (j ^ mask)) for j in range(groups_y)])
        surfaces.append(lax.ppermute(coarse, ("comp", "gy"), route))

    lines = 2 * channels + 16
    shapes = [
        shape((rows, channels, columns), f32),
        shape((lines, columns), bf16),
        shape((lines, columns), bf16),
        shape((4 * rows, columns), bf16),
        shape((4 * rows, columns), bf16),
    ]
    if not paired:
        shapes.append(shape((2, channels, columns), bf16))
    y, e1, e3, e2, e4, *sums = pl.pallas_call(
        functools.partial(forward_kernel, groups_x, paired),
        out_shape=shapes,
        in_specs=[vmem] * 4 + [anywhere],
        out_specs=[vmem] * len(shapes),
        scratch_shapes=[
            pltpu.VMEM((rows * channels, columns), bf16),
            pltpu.VMEM((4 * rows, columns), f32),
        ],
        compiler_params=params(),
        name="forward_or_halos",
    )(fields, wet_cells, diff_row, forward, surfaces[0])
    masks = [1 << bit for bit in range(groups_y.bit_length() - 1)]

    def sum_route(mask):
        return [(j, j ^ mask) for j in range(groups_y)]

    def ring_pairs(count, odd):
        return [(a, (a + 1) % count) for a in range(odd, count, 2)]

    def flat(comp, i, j):
        return (comp * groups_x + i) * groups_y + j

    def level_route(odd):
        pairs = []
        for i in range(groups_x):
            linked = [(a, a + 1) for a in range(odd, groups_y - 1, 2)]
            alone = set(range(groups_y)) - {j for pair in linked for j in pair}
            pairs += [(flat(1, i, a), flat(1, i, b)) for a, b in linked]
            if i % 2 == 0:
                pairs += [(flat(1, i, j), flat(1, i + 1, j)) for j in sorted(alone)]
                if odd or not paired:
                    pairs += [(flat(0, i, j), flat(0, i + 1, j)) for j in range(groups_y)]
            if paired and not odd and i < i ^ 2:
                pairs += [(flat(0, i, j), flat(0, i ^ 2, j)) for j in range(groups_y)]
        return both_ways(pairs)

    e1 = lax.ppermute(e1, "gx", both_ways(ring_pairs(groups_x, 0)))
    e3 = lax.ppermute(e3, "gx", both_ways(ring_pairs(groups_x, 1)))
    axes = ("comp", "gx", "gy")
    e2 = lax.ppermute(e2, axes, level_route(0))
    e4 = lax.ppermute(e4, axes, level_route(1))

    one_hots = pl.pallas_call(
        functools.partial(one_hot_kernel, rows, columns),
        out_shape=[
            shape((LANES, blocks * points), bf16),
            shape((LANES, blocks * points), bf16),
            shape((blocks, points), jnp.int32),
            shape((blocks, points), jnp.int32),
        ],
        in_specs=[vmem] * 4 + [anywhere],
        out_specs=[vmem] * 4,
        compiler_params=params(),
        name="one_hots",
    )(a2o_source, a2o_target, marine_air_input_index, marine_air_output_index, coarse)
    landing, sent = pl.pallas_call(
        functools.partial(regrid_kernel, len(surfaces)),
        out_shape=[shape((cells, LANES), f32), shape((cells, LANES), bf16)],
        in_specs=[vmem] * (len(surfaces) + 4) + [hbm] * 4 + [anywhere],
        out_specs=[vmem] * 2,
        scratch_shapes=[
            pltpu.VMEM((blocks, points, points), bf16),
            pltpu.VMEM((blocks, points), f32),
            pltpu.VMEM((blocks, points), f32),
            pltpu.SMEM((1, 1), jnp.int32),
            pltpu.SemaphoreType.DMA((2,)),
        ],
        compiler_params=params(),
        name="regrid_blocks",
    )(
        *surfaces, *one_hots, a2o_count, marine_air_piece_tally,
        a2o_weight, marine_air_piece_factor, y,
    )
    for mask in masks[:-1]:
        landing = landing + lax.ppermute(sent, "gy", sum_route(mask)).astype(f32)
        sent = landing.astype(bf16)
    part = lax.ppermute(sent, "gy", sum_route(masks[-1]))

    extra = []
    if not paired:
        p, q = jnp.moveaxis(lax.all_gather(sums[0], "gx").astype(f32), 1, 0)
        viscous = lax.dynamic_slice_in_dim(
            diffusivity, lax.axis_index("gy") * channels, channels
        )[:, None]
        rates = [half_rates(g, 0, columns // 4, columns) for g in (0, 0, 1, 1)]
        _, alpha, _ = decay_terms(viscous, jnp.concatenate(rates, axis=1))
        gap = lax.axis_index("gx") - jnp.arange(groups_x)
        decay = jnp.exp(
            -(rows * jnp.maximum(jnp.abs(gap) - 1, 0))[:, None, None] * alpha[None]
        )
        extra = [
            jnp.sum(jnp.where((gap > 0)[:, None, None], decay * p, 0.0), axis=0),
            jnp.sum(jnp.where((gap < 0)[:, None, None], decay * q, 0.0), axis=0),
        ]
    ring = channels // 2 + 8
    damped, coefs, stepped = pl.pallas_call(
        functools.partial(first_step_kernel, groups_x, groups_y, paired),
        out_shape=[
            shape((rows * channels, columns), bf16),
            shape((7, 16, columns), f32),
            shape((rows + 2, 2, ring, columns), f32),
        ],
        in_specs=[vmem] * (8 + len(extra)),
        out_specs=[vmem] * 3,
        scratch_shapes=[
            pltpu.VMEM((rows, channels, LANES), f32),
            pltpu.VMEM((rows + 4, 2, ring, columns), f32),
            pltpu.VMEM((16, columns), f32),
        ],
        compiler_params=params(),
        name="damping_or_first_step",
    )(fields, wet_cells, diff_row, y, e1, e3, e2, e4, *extra)

    surface_sum, near, far = pl.pallas_call(
        functools.partial(heat_kernel, rows),
        out_shape=[
            shape((cells, LANES), f32),
            shape((cells + columns // 16, LANES), bf16),
            shape((cells + columns // 16, LANES), bf16),
        ],
        in_specs=[vmem] * 4 + [anywhere],
        out_specs=[vmem] * 3,
        compiler_params=params(),
        name="surface_sum",
    )(e2, e4, landing, part, coefs)

    near = lax.ppermute(near, "gx", both_ways(ring_pairs(groups_x, 0)))
    far = lax.ppermute(far, "gx", both_ways(ring_pairs(groups_x, 1)))
    base, column = pl.pallas_call(
        second_step_kernel,
        out_shape=[shape((rows, channels, columns), f32), shape((channels, LANES), f32)],
        in_specs=[vmem] * 5,
        out_specs=[vmem] * 2,
        compiler_params=params(),
        name="inverse_or_second_step",
    )(gain_row, inverse, damped, coefs, stepped)
    return pl.pallas_call(
        functools.partial(last_kernel, groups_x, groups_y),
        out_shape=shape(fields.shape, f32),
        in_specs=[vmem] * 6,
        out_specs=vmem,
        scratch_shapes=[pltpu.VMEM((16, columns), f32)],
        compiler_params=params(),
        name="add_surface_terms",
    )(column, base, coefs, surface_sum, near, far)


def solution(mesh):
    in_specs = (
        P("comp", "gx", "gy", None),
        P("gx", None),
        P(),
        P(),
        P(),
        P("gx", "gy", None, None),
        P("gx", "gy", None, None),
        P("gx", "gy"),
        P("gx", "gy", None, None, None),
        P("gx", "gy", None, None),
        P("gx", "gy", None, None),
        P("gx", "gy"),
        P("gx", "gy", None, None, None),
    )
    out_specs = P("comp", "gx", "gy", None)
    return jax.shard_map(local, mesh=mesh, in_specs=in_specs, out_specs=out_specs, check_vma=False)
```

```python
import functools

import jax
import jax.numpy as jnp
import numpy as np
from jax import lax
from jax.experimental import pallas as pl
from jax.experimental.pallas import tpu as pltpu
from jax.sharding import PartitionSpec as P

spread_rate = 0.2
mixing_rate = 0.1
heat_gain = 0.5
salt_gain = -0.25
LANES = 128
f32 = jnp.float32
bf16 = jnp.bfloat16


def fourier_tables(columns):
    half = columns // 2
    forward, inverse = [], []
    for first in (0, 1):
        waves = np.arange(first, half, 2)
        phase = np.arange(half)[:, None] * waves[None, :] % columns
        angles = phase * (2.0 * np.pi / columns)
        table = np.concatenate([np.cos(angles), np.sin(angles)], axis=1)
        weight = np.where(waves == 0, 1.0, 2.0) / columns
        forward.append(table)
        inverse.append(table.T * np.concatenate([weight, weight])[:, None])
    return (
        jnp.asarray(np.concatenate(forward).astype(np.float32), bf16),
        jnp.asarray(np.concatenate(inverse).astype(np.float32), bf16),
    )


def wave_parts(columns):
    quarter = columns // 4
    return [
        (g, n, (g * 2 * quarter + n, (g * 2 + 1) * quarter + n))
        for g in (0, 1)
        for n in range(0, quarter, LANES)
    ]


def half_rates(group, first, count, columns):
    lane = lax.broadcasted_iota(jnp.int32, (1, count), 1) + first
    wave = (2 * lane + group).astype(f32)
    sine = jnp.sin(wave * (np.pi / columns))
    return 2.0 * sine * sine


def both_ways(pairs):
    return [p for a, b in pairs for p in ((a, b), (b, a))]


def channel_column(row, channels, first):
    n = row.shape[1]
    lane = lax.broadcasted_iota(jnp.int32, (channels, n), 1)
    sub = lax.broadcasted_iota(jnp.int32, (channels, n), 0)
    return jnp.sum(jnp.where(lane == sub + first, row, 0.0), axis=1, keepdims=True)


def to_tiles(surface):
    cols = surface.shape[1]
    return jnp.concatenate(
        [surface[:, k : k + LANES] for k in range(0, cols, LANES)], axis=0
    )


def from_tiles(tiles, rows):
    return jnp.concatenate(
        [tiles[k : k + rows] for k in range(0, tiles.shape[0], rows)], axis=1
    )


def decay_terms(diff_column, rates):
    half = 0.5 / diff_column + rates
    sinh = jnp.sqrt(half * (half + 2.0))
    grow = 1.0 + half + sinh
    return 1.0 / grow, jnp.log(grow), sinh


def edge_factors(lam, alpha, base, total, rows):
    lam2 = lam * lam
    powers = [
        jnp.exp(-2.0 * base * alpha) * lam2,
        jnp.exp(-2.0 * (total - rows - base) * alpha) * lam2,
    ]
    lows, highs = [], []
    for _ in range(rows):
        lows.append(1.0 - powers[0])
        highs.insert(0, 1.0 - powers[1])
        powers = [power * lam2 for power in powers]
    return lows, highs


def start_kernel(
    groups_x, paired, x_hbm, wet_hbm, flux_hbm, diff_hbm, table_hbm, *refs
):
    outs = 6 if paired else 7
    coarse_hbm, y_hbm, *message_hbm = refs[:outs]
    coarse_ref, y_ref, *message_ref = refs[outs : 2 * outs]
    e1_ref, e3_ref, e2_ref, e4_ref = message_ref[:4]
    if not paired:
        pq_ref = message_ref[4]
    (
        x_ref, wet_ref, flux_ref, diff_ref, table_ref, flat_ref, row_ref, edge_ref,
        x_sem, sem, out_sem,
    ) = refs[2 * outs :]
    rows, channels, columns = x_ref.shape
    half = columns // 2
    row_group = lax.axis_index("gx")
    col_group = lax.axis_index("gy")
    is_atmos = lax.axis_index("comp") == 0

    x_copies = [
        pltpu.make_async_copy(x_hbm.at[0, r], x_ref.at[r], x_sem.at[r]) for r in range(rows)
    ]
    surface_copy = pltpu.make_async_copy(coarse_ref, coarse_hbm, out_sem.at[0])
    y_copies = [
        pltpu.make_async_copy(y_ref.at[r], y_hbm.at[r], out_sem.at[1 + r]) for r in range(rows)
    ]
    message_copies = [
        pltpu.make_async_copy(ref, hbm, out_sem.at[1 + rows + k])
        for k, (ref, hbm) in enumerate(zip(message_ref, message_hbm))
    ]

    def send_surface():
        coarse_ref[...] = to_tiles(row_ref[...]).astype(bf16)
        surface_copy.start()

    @pl.when(is_atmos)
    def _():
        flux_copy = pltpu.make_async_copy(flux_hbm, flux_ref, sem.at[0])
        diff_copy = pltpu.make_async_copy(diff_hbm, diff_ref, sem.at[1])
        table_copy = pltpu.make_async_copy(table_hbm, table_ref, sem.at[2])
        for copy in [flux_copy, diff_copy] + x_copies + [table_copy]:
            copy.start()
        first = col_group * channels
        flux_copy.wait()
        weight = channel_column(flux_ref[...], channels, first)
        for r in range(rows):
            x_copies[r].wait()
            row_ref[r : r + 1, :] = jnp.sum(x_ref[r] * weight, axis=0, keepdims=True)
            left, right = x_ref[r, :, :half], x_ref[r, :, half:]
            flat_ref[r * channels : (r + 1) * channels, :half] = (left + right).astype(bf16)
            flat_ref[r * channels : (r + 1) * channels, half:] = (left - right).astype(bf16)
        send_surface()
        table_copy.wait()
        for k in range(2):
            lanes = slice(k * half, (k + 1) * half)
            part = jnp.dot(
                flat_ref[:, lanes], table_ref[lanes, :], preferred_element_type=f32
            )
            y_ref[:, :, lanes] = part.reshape(rows, channels, half)
        for copy in y_copies:
            copy.start()
        diff_copy.wait()
        diff = channel_column(diff_ref[...], channels, first)
        total = rows * groups_x
        base = (row_group * rows).astype(f32)
        for group, n, parts in wave_parts(columns):
            lam, alpha, _ = decay_terms(diff, half_rates(group, n, LANES, columns))
            lows, highs = edge_factors(lam, alpha, base, total, rows)
            for part in parts:
                lanes = slice(part, part + LANES)
                p = lows[0] * y_ref[0, :, lanes]
                q = highs[-1] * y_ref[rows - 1, :, lanes]
                for r in range(1, rows):
                    p = lam * p + lows[r] * y_ref[r, :, lanes]
                    q = lam * q + highs[-1 - r] * y_ref[rows - 1 - r, :, lanes]
                if paired:
                    for mask, out in ((1, e1_ref), (2, e2_ref), (3, e3_ref)):
                        upward = row_group < (row_group ^ mask)
                        out[0:channels, lanes] = jnp.where(upward, p, q).astype(bf16)
                else:
                    pq_ref[0, :, lanes] = p.astype(bf16)
                    pq_ref[1, :, lanes] = q.astype(bf16)
        for copy in message_copies:
            copy.start()
        for copy in [surface_copy] + y_copies + message_copies:
            copy.wait()

    @pl.when(jnp.logical_not(is_atmos))
    def _():
        wet_copy = pltpu.make_async_copy(wet_hbm, wet_ref, sem.at[0])
        for copy in x_copies + [wet_copy]:
            copy.start()
        gain = jnp.where(col_group == 0, 1.0, 0.0)
        for r in range(rows):
            x_copies[r].wait()
            row_ref[r : r + 1, :] = x_ref[r, 0:1, :] * gain
        send_surface()
        wet_copy.wait()
        levels = channels // 2
        lines = 2 * channels
        even_x = row_group % 2 == 0
        even_y = col_group % 2 == 0
        wet = wet_ref[...].astype(f32)
        wet = jnp.concatenate([wet, wet], axis=0).astype(bf16)

        def put(out, last):
            @pl.when(last)
            def _():
                out[0:lines, :] = x_ref[rows - 2 :].reshape(lines, columns).astype(bf16)

            @pl.when(jnp.logical_not(last))
            def _():
                out[0:lines, :] = x_ref[:2].reshape(lines, columns).astype(bf16)

            out[lines : lines + 16, :] = wet

        put(e1_ref, even_x)
        put(e3_ref, jnp.logical_not(even_x))

        def put_edges(out, level):
            for r in range(rows):
                for t in range(2):
                    at = (r * 2 + t) * 2
                    c = t * levels + level
                    edge_ref[at : at + 2, :] = x_ref[r, c : c + 2, :]
            out[...] = edge_ref[...].astype(bf16)

        @pl.when(even_y)
        def _():
            put_edges(e2_ref, levels - 2)
            put_edges(e4_ref, 0)

        @pl.when(jnp.logical_not(even_y))
        def _():
            put_edges(e2_ref, 0)
            put_edges(e4_ref, levels - 2)

        for copy in message_copies:
            copy.start()
        for copy in [surface_copy] + message_copies:
            copy.wait()


def one_hot_kernel(
    rows, columns, a_src, a_dst, m_src, m_dst, _, src_hot_ref, dst_hot_ref, src_row_ref, dst_row_ref
):
    is_atmos = lax.axis_index("comp") == 0
    blocks, points = src_row_ref.shape
    lane_iota = lax.broadcasted_iota(jnp.int32, (LANES, points), 0)
    for a_ref, m_ref, hot_ref, row_ref in (
        (a_src, m_src, src_hot_ref, src_row_ref),
        (a_dst, m_dst, dst_hot_ref, dst_row_ref),
    ):
        index = jnp.where(is_atmos, m_ref[0, 0], a_ref[0, 0])
        row = index // columns
        tile = (index // LANES) % (columns // LANES)
        row_ref[...] = tile * rows + row
        lane = index % LANES
        for b in range(blocks):
            hot_ref[:, b * points : (b + 1) * points] = jnp.where(
                lane_iota == lane[b : b + 1], 1.0, 0.0
            ).astype(bf16)


def regrid_kernel(n_surfaces, *refs):
    surfaces = refs[:n_surfaces]
    (
        src_hot_ref, dst_hot_ref, src_row_ref, dst_row_ref, a_count, m_count, a_weight, m_weight,
        _, _,
        land_ref, sent_ref, weight_ref, gath_ref, val_ref, sem,
    ) = refs[n_surfaces:]
    is_atmos = lax.axis_index("comp") == 0
    blocks, points = val_ref.shape
    cells = surfaces[0].shape[0]

    @pl.when(is_atmos)
    def _():
        pltpu.make_async_copy(m_weight.at[0, 0], weight_ref, sem).start()

    @pl.when(jnp.logical_not(is_atmos))
    def _():
        pltpu.make_async_copy(a_weight.at[0, 0], weight_ref, sem).start()

    count = jnp.where(is_atmos, m_count[0, 0], a_count[0, 0])
    pair = 2 * points
    row_iota = lax.broadcasted_iota(jnp.int32, (cells, points), 0)
    table = sum(surface[...].astype(f32) for surface in surfaces).astype(bf16)
    for b in range(0, blocks, 2):
        picked = jnp.dot(
            table, src_hot_ref[:, b * points : b * points + pair], preferred_element_type=f32
        )
        for k in range(2):
            mine = row_iota == src_row_ref[b + k : b + k + 1, :]
            part = jnp.where(mine, picked[:, k * points : (k + 1) * points], 0.0)
            gath_ref[b + k : b + k + 1, :] = jnp.sum(part, axis=0, keepdims=True)
    gathered = gath_ref[...].astype(bf16)

    @pl.when(is_atmos)
    def _():
        pltpu.make_async_copy(m_weight.at[0, 0], weight_ref, sem).wait()

    @pl.when(jnp.logical_not(is_atmos))
    def _():
        pltpu.make_async_copy(a_weight.at[0, 0], weight_ref, sem).wait()

    block_iota = lax.broadcasted_iota(jnp.int32, (blocks, points), 0)
    values = jnp.zeros((blocks, points), f32)
    for b in range(0, blocks, 2):
        terms = lax.dot_general(
            gathered,
            weight_ref[b : b + 2].reshape(pair, points),
            (((1,), (1,)), ((), ())),
            preferred_element_type=f32,
        )
        for k in range(2):
            values = jnp.where(block_iota == b + k, terms[:, k * points : (k + 1) * points], values)
    val_ref[...] = jnp.where(block_iota < count, values, 0.0)
    land = jnp.zeros((2 * cells, LANES), f32)
    for b in range(0, blocks, 2):
        spread = []
        for k in range(b, b + 2):
            value = val_ref[k : k + 1, :]
            coarse = value.astype(bf16).astype(f32)
            fine = value - coarse
            mine = row_iota == dst_row_ref[k : k + 1, :]
            spread.append(
                jnp.concatenate(
                    [jnp.where(mine, coarse, 0.0), jnp.where(mine, fine, 0.0)], axis=0
                ).astype(bf16)
            )
        land = land + lax.dot_general(
            jnp.concatenate(spread, axis=1),
            dst_hot_ref[:, b * points : b * points + pair],
            (((1,), (1,)), ((), ())),
            preferred_element_type=f32,
        )
    land = land[:cells] + land[cells:]
    land_ref[...] = land
    sent_ref[...] = land.astype(bf16)


def heat_kernel(rows, e2_ref, e4_ref, land_ref, part_ref, _, sum_ref, near_ref, far_ref):
    cells = land_ref.shape[0]
    columns = cells // rows * LANES
    even_x = lax.axis_index("gx") % 2 == 0
    even_y = lax.axis_index("gy") % 2 == 0
    total = land_ref[...] + part_ref[...].astype(f32)
    sum_ref[...] = total

    def corners(row):
        start = row * 4 // 16 * 16
        one = e2_ref[start : start + 16, :].astype(f32)
        two = e4_ref[start : start + 16, :].astype(f32)
        low = jnp.where(even_y, two, one)
        high = jnp.where(even_y, one, two)
        at = row * 4 - start
        lines = [low[at + 1 : at + 2], low[at + 3 : at + 4], high[at : at + 1], high[at + 2 : at + 3]]
        return to_tiles(jnp.concatenate(lines + [jnp.zeros((4, columns), f32)], axis=0))

    first, last = corners(0), corners(rows - 1)
    near_ref[0:cells, :] = total.astype(bf16)
    far_ref[0:cells, :] = total.astype(bf16)
    near_ref[cells:, :] = jnp.where(even_x, last, first).astype(bf16)
    far_ref[cells:, :] = jnp.where(even_x, first, last).astype(bf16)


def advance(ref, r, t, coefs, size):
    ring, columns = ref.shape[2:]
    whole = ref[r, t]
    up = pltpu.roll(whole, 1, 0)[:size]
    down = pltpu.roll(whole, ring - 1, 0)[:size]
    mid = whole[:size]
    total = coefs[0] * mid + coefs[5] * (up + down)
    total = total + coefs[1] * ref[r - 1, t, 0:size, :]
    total = total + coefs[2] * ref[r + 1, t, 0:size, :]
    total = total + coefs[3] * pltpu.roll(mid, 1, 1)
    return total + coefs[4] * pltpu.roll(mid, columns - 1, 1)


def first_step_kernel(
    groups_x, groups_y, paired, x_ref, wet_ref, diff_ref, y_ref, e1_ref, e3_ref,
    e2_ref, e4_ref, *refs,
):
    if not paired:
        pin_ref, qin_ref = refs[:2]
    zb_ref, c_ref, t1_ref, z_ref, t0_ref, w_ref = refs[-6:]
    _, rows, channels, columns = x_ref.shape
    row_group = lax.axis_index("gx")
    col_group = lax.axis_index("gy")
    is_atmos = lax.axis_index("comp") == 0

    @pl.when(is_atmos)
    def _():
        diff = channel_column(diff_ref[...], channels, col_group * channels)
        total = rows * groups_x
        base = (row_group * rows).astype(f32)
        for group, n, parts in wave_parts(columns):
            lam, alpha, sinh = decay_terms(diff, half_rates(group, n, LANES, columns))
            scale = 1.0 / (
                2.0 * diff * sinh * (1.0 - jnp.exp(-2.0 * (total + 1) * alpha))
            )
            lows, highs = edge_factors(lam, alpha, base, total, rows)
            for part in parts:
                lanes = slice(part, part + LANES)
                if paired:
                    pin = jnp.zeros((channels, LANES), f32)
                    qin = jnp.zeros((channels, LANES), f32)
                    for mask, msg in ((1, e1_ref), (2, e2_ref), (3, e3_ref)):
                        band = row_group ^ mask
                        gap = (jnp.abs(row_group - band) - 1) * rows
                        term = jnp.exp(-gap.astype(f32) * alpha)
                        term = term * msg[0:channels, lanes].astype(f32)
                        pin = pin + jnp.where(band < row_group, term, 0.0)
                        qin = qin + jnp.where(band > row_group, term, 0.0)
                else:
                    pin = pin_ref[:, lanes]
                    qin = qin_ref[:, lanes]
                f = pin
                for r in range(rows):
                    f = lam * f + lows[r] * y_ref[r, :, lanes]
                    z_ref[r] = highs[r] * f
                g = lam * qin
                for r in reversed(range(rows)):
                    z = scale * (z_ref[r] + lows[r] * g)
                    zb_ref[r * channels : (r + 1) * channels, lanes] = z.astype(bf16)
                    g = lam * (g + highs[r] * y_ref[r, :, lanes])

    @pl.when(jnp.logical_not(is_atmos))
    def _():
        levels = channels // 2
        ring = levels + 8
        lines = 2 * channels
        first_x = row_group == 0
        last_x = row_group == groups_x - 1
        top = col_group == 0
        bottom = col_group == groups_y - 1
        even_x = row_group % 2 == 0
        even_y = col_group % 2 == 0

        one = e1_ref[lines : lines + 16, :].astype(f32)
        three = e3_ref[lines : lines + 16, :].astype(f32)
        below = jnp.where(even_x, three, one)[rows - 2 : rows]
        above = jnp.where(even_x, one, three)[0:2]
        w_ref[0:2, :] = jnp.where(first_x, 0.0, below)
        w_ref[2 : rows + 2, :] = wet_ref[...].astype(f32)
        w_ref[rows + 2 : rows + 4, :] = jnp.where(last_x, 0.0, above)

        span = rows + 2
        north = w_ref[0:span, :]
        here = w_ref[1 : span + 1, :]
        south = w_ref[2 : span + 2, :]
        west = pltpu.roll(here, 1, 1)
        east = pltpu.roll(here, columns - 1, 1)
        c_ref[0, 0:span, :] = here * (
            1.0 - 2.0 * mixing_rate - spread_rate * (north + south + west + east)
        )
        c_ref[1, 0:span, :] = spread_rate * here * north
        c_ref[2, 0:span, :] = spread_rate * here * south
        c_ref[3, 0:span, :] = spread_rate * here * west
        c_ref[4, 0:span, :] = spread_rate * here * east
        c_ref[5, 0:span, :] = mixing_rate * here
        c_ref[6, 0:span, :] = here

        one = e1_ref[0:lines, :].astype(f32)
        three = e3_ref[0:lines, :].astype(f32)
        below = jnp.where(even_x, three, one)
        above = jnp.where(even_x, one, three)
        blank = jnp.zeros((8, columns), f32)
        for k in range(2):
            for t in range(2):
                c = k * channels + t * levels
                t0_ref[k, t, 0:levels, :] = below[c : c + levels]
                t0_ref[rows + 2 + k, t, 0:levels, :] = above[c : c + levels]
                t0_ref[k, t, levels:ring, :] = blank
                t0_ref[rows + 2 + k, t, levels:ring, :] = blank
        one = e2_ref[...].astype(f32)
        two = e4_ref[...].astype(f32)
        before = jnp.where(even_y, two, one)
        after = jnp.where(even_y, one, two)
        for r in range(rows):
            for t in range(2):
                k = (r * 2 + t) * 2
                t0_ref[r + 2, t, 0:levels, :] = x_ref[0, r, t * levels : (t + 1) * levels, :]
                t0_ref[r + 2, t, levels : levels + 2, :] = after[k : k + 2]
                t0_ref[r + 2, t, ring - 2 : ring, :] = before[k : k + 2]

        def close(ref, r):
            for t in range(2):
                ref[r, t, ring - 1 : ring, :] = jnp.where(
                    top, ref[r, t, 0:1, :], ref[r, t, ring - 1 : ring, :]
                )
                ref[r, t, levels : levels + 1, :] = jnp.where(
                    bottom, ref[r, t, levels - 1 : levels, :], ref[r, t, levels : levels + 1, :]
                )

        def first(r, carry):
            coefs = [c_ref[k, pl.ds(r, 1), :] for k in range(6)]
            close(t0_ref, r + 1)
            for t in range(2):
                t1_ref[r, t] = advance(t0_ref, r + 1, t, coefs, ring)
            close(t1_ref, r)
            return carry

        lax.fori_loop(0, span, first, 0)


def second_step_kernel(gain_ref, table_ref, zb_ref, c_ref, t1_ref, base_ref, column_ref):
    rows, channels, columns = base_ref.shape
    is_atmos = lax.axis_index("comp") == 0

    @pl.when(is_atmos)
    def _():
        response = channel_column(gain_ref[...], channels, lax.axis_index("gy") * channels)
        column_ref[...] = jnp.broadcast_to(response, column_ref.shape)
        half = columns // 2
        step = 256
        for n in range(0, half, step):
            even, odd = [
                jnp.dot(
                    zb_ref[:, k * half : (k + 1) * half],
                    table_ref[k * half : (k + 1) * half, n : n + step],
                    preferred_element_type=f32,
                ).reshape(rows, channels, step)
                for k in range(2)
            ]
            base_ref[:, :, n : n + step] = even + odd
            base_ref[:, :, n + half : n + half + step] = even - odd

    @pl.when(jnp.logical_not(is_atmos))
    def _():
        levels = channels // 2

        def second(r, carry):
            coefs = [c_ref[k, pl.ds(r, 1), :] for k in range(6)]
            for t in range(2):
                c = t * levels
                base_ref[r - 1, c : c + levels, :] = advance(t1_ref, r, t, coefs, levels)
            return carry

        lax.fori_loop(1, rows + 1, second, 0)


def last_kernel(
    groups_x, groups_y, column_ref, base_ref, c_ref, sum_ref, near_ref, far_ref, out_hbm,
    out_ref, e_ref, heat_ref, sem,
):
    rows, channels, columns = out_ref.shape
    row_group = lax.axis_index("gx")
    col_group = lax.axis_index("gy")
    is_atmos = lax.axis_index("comp") == 0
    copies = [
        pltpu.make_async_copy(out_ref.at[r], out_hbm.at[0, r], sem.at[r]) for r in range(rows)
    ]

    @pl.when(is_atmos)
    def _():
        for r in range(rows):
            for k in range(columns // LANES):
                lanes = slice(k * LANES, (k + 1) * LANES)
                at = k * rows + r
                out_ref[r, :, lanes] = (
                    base_ref[r, :, lanes] + column_ref[...] * sum_ref[at : at + 1, :]
                )
            copies[r].start()

    @pl.when(jnp.logical_not(is_atmos))
    def _():
        levels = channels // 2
        cells = sum_ref.shape[0]
        even = row_group % 2 == 0
        below = jnp.where(even, far_ref[...].astype(f32), near_ref[...].astype(f32))
        above = jnp.where(even, near_ref[...].astype(f32), far_ref[...].astype(f32))

        low = from_tiles(below[cells:], 8)
        high = from_tiles(above[cells:], 8)
        by_low = c_ref[1, 1:2, :] * (c_ref[5, 0:1, :] + c_ref[5, 1:2, :])
        by_high = c_ref[2, rows : rows + 1, :] * (
            c_ref[5, rows : rows + 1, :] + c_ref[5, rows + 1 : rows + 2, :]
        )
        has_before = jnp.where(col_group > 0, 1.0, 0.0)
        has_after = jnp.where(col_group < groups_y - 1, 1.0, 0.0)

        @pl.when(col_group == 0)
        def _():
            span = rows + 2
            e_ref[0:1, :] = from_tiles(below[:cells], rows)[rows - 1 : rows]
            e_ref[1 : rows + 1, :] = from_tiles(sum_ref[...], rows)
            e_ref[rows + 1 : span, :] = from_tiles(above[:cells], rows)[0:1]
            e_ref[0:span, :] = c_ref[6, 0:span, :] * e_ref[0:span, :]
            own = slice(1, rows + 1)
            heat = e_ref[own, :]
            second = c_ref[5, own, :] * heat
            first = (c_ref[0, own, :] + 1.0) * heat + second
            first = first + c_ref[1, own, :] * e_ref[0:rows, :]
            first = first + c_ref[2, own, :] * e_ref[2 : rows + 2, :]
            first = first + c_ref[3, own, :] * pltpu.roll(heat, 1, 1)
            first = first + c_ref[4, own, :] * pltpu.roll(heat, columns - 1, 1)
            heat_ref[0] = first
            heat_ref[1] = second

        for r in [1, rows - 2] + list(range(2, rows - 2)) + [0, rows - 1]:
            out_ref[r] = base_ref[r]
            for t in range(2):
                c = t * levels
                for edge, factor, lines in ((0, by_low, low), (rows - 1, by_high, high)):
                    if r == edge:
                        out_ref[r, c : c + 1, :] = out_ref[r, c : c + 1, :] + (
                            has_before * factor * lines[t : t + 1]
                        )
                        d = c + levels - 1
                        out_ref[r, d : d + 1, :] = out_ref[r, d : d + 1, :] + (
                            has_after * factor * lines[t + 2 : t + 3]
                        )

            @pl.when(col_group == 0)
            def _():
                for t, gain in enumerate((heat_gain, salt_gain)):
                    c = t * levels
                    for k in range(2):
                        out_ref[r, c + k : c + k + 1, :] = (
                            out_ref[r, c + k : c + k + 1, :] + gain * heat_ref[k, r : r + 1, :]
                        )

            copies[r].start()

    for copy in copies:
        copy.wait()


def local(
    fields,
    wet_cells,
    flux_weight,
    variable_sea_response,
    diffusivity,
    a2o_source,
    a2o_target,
    a2o_count,
    a2o_weight,
    marine_air_input_index,
    marine_air_output_index,
    marine_air_piece_tally,
    marine_air_piece_factor,
):
    _, rows, channels, columns = fields.shape
    groups_x = lax.axis_size("gx")
    groups_y = lax.axis_size("gy")
    blocks, points = a2o_source.shape[2:]
    cells = rows * columns // LANES
    forward, inverse = fourier_tables(columns)
    flux_row = flux_weight[None, :]
    gain_row = variable_sea_response[None, :]
    diff_row = diffusivity[None, :]
    paired = groups_x == 4
    params = functools.partial(pltpu.CompilerParams, vmem_limit_bytes=40 * 2**20)
    vmem = pl.BlockSpec(memory_space=pltpu.VMEM)
    smem = pl.BlockSpec(memory_space=pltpu.SMEM)
    hbm = pl.BlockSpec(memory_space=pltpu.HBM)
    anywhere = pl.BlockSpec(memory_space=pl.ANY)

    def shape(dims, dtype):
        return jax.ShapeDtypeStruct(dims, dtype)

    lines = 2 * channels + 16
    shapes = [
        shape((cells, LANES), bf16),
        shape((rows, channels, columns), f32),
        shape((lines, columns), bf16),
        shape((lines, columns), bf16),
        shape((4 * rows, columns), bf16),
        shape((4 * rows, columns), bf16),
    ]
    if not paired:
        shapes.append(shape((2, channels, columns), bf16))
    coarse, y, e1, e3, e2, e4, *sums = pl.pallas_call(
        functools.partial(start_kernel, groups_x, paired),
        out_shape=shapes,
        in_specs=[hbm] * 5,
        out_specs=[hbm] * len(shapes),
        scratch_shapes=[pltpu.VMEM(out.shape, out.dtype) for out in shapes]
        + [
            pltpu.VMEM((rows, channels, columns), f32),
            pltpu.VMEM((rows, columns), jnp.int32),
            pltpu.VMEM(flux_row.shape, f32),
            pltpu.VMEM(diff_row.shape, f32),
            pltpu.VMEM(forward.shape, bf16),
            pltpu.VMEM((rows * channels, columns), bf16),
            pltpu.VMEM((rows, columns), f32),
            pltpu.VMEM((4 * rows, columns), f32),
            pltpu.SemaphoreType.DMA((rows,)),
            pltpu.SemaphoreType.DMA((3,)),
            pltpu.SemaphoreType.DMA((rows + len(shapes) - 1,)),
        ],
        compiler_params=pltpu.CompilerParams(vmem_limit_bytes=58 * 2**20),
        name="surface_and_forward_or_halos",
    )(fields, wet_cells, flux_row, diff_row, forward)

    masks = [1 << bit for bit in range(groups_y.bit_length() - 1)]

    def sum_route(mask):
        return [(j, j ^ mask) for j in range(groups_y)]

    def partner_route(mask):
        return both_ways([(j, groups_y + (j ^ mask)) for j in range(groups_y)])

    surface = sum(
        lax.ppermute(coarse, ("comp", "gy"), partner_route(mask)).astype(f32)
        for mask in masks[:1] + [0]
    )
    coarse = surface.astype(bf16)
    for mask in masks[1:-1]:
        surface = surface + lax.ppermute(coarse, "gy", sum_route(mask)).astype(f32)
        coarse = surface.astype(bf16)
    surfaces = [surface] + [
        lax.ppermute(coarse, "gy", sum_route(mask)) for mask in masks[1:][-1:]
    ]

    def ring_pairs(count, odd):
        return [(a, (a + 1) % count) for a in range(odd, count, 2)]

    def flat(comp, i, j):
        return (comp * groups_x + i) * groups_y + j

    def level_route(odd):
        pairs = []
        for i in range(groups_x):
            linked = [(a, a + 1) for a in range(odd, groups_y - 1, 2)]
            alone = set(range(groups_y)) - {j for pair in linked for j in pair}
            pairs += [(flat(1, i, a), flat(1, i, b)) for a, b in linked]
            if i % 2 == 0:
                pairs += [(flat(1, i, j), flat(1, i + 1, j)) for j in sorted(alone)]
                if odd or not paired:
                    pairs += [(flat(0, i, j), flat(0, i + 1, j)) for j in range(groups_y)]
            if paired and not odd and i < i ^ 2:
                pairs += [(flat(0, i, j), flat(0, i ^ 2, j)) for j in range(groups_y)]
        return both_ways(pairs)

    e1 = lax.ppermute(e1, "gx", both_ways(ring_pairs(groups_x, 0)))
    e3 = lax.ppermute(e3, "gx", both_ways(ring_pairs(groups_x, 1)))
    axes = ("comp", "gx", "gy")
    e2 = lax.ppermute(e2, axes, level_route(0))
    e4 = lax.ppermute(e4, axes, level_route(1))

    one_hots = pl.pallas_call(
        functools.partial(one_hot_kernel, rows, columns),
        out_shape=[
            shape((LANES, blocks * points), bf16),
            shape((LANES, blocks * points), bf16),
            shape((blocks, points), jnp.int32),
            shape((blocks, points), jnp.int32),
        ],
        in_specs=[vmem] * 4 + [anywhere],
        out_specs=[vmem] * 4,
        compiler_params=params(),
        name="one_hots",
    )(a2o_source, a2o_target, marine_air_input_index, marine_air_output_index, coarse)
    landing, sent = pl.pallas_call(
        functools.partial(regrid_kernel, len(surfaces)),
        out_shape=[shape((cells, LANES), f32), shape((cells, LANES), bf16)],
        in_specs=[vmem] * (len(surfaces) + 4) + [smem, smem, hbm, hbm, anywhere, anywhere],
        out_specs=[vmem] * 2,
        scratch_shapes=[
            pltpu.VMEM((blocks, points, points), bf16),
            pltpu.VMEM((blocks, points), f32),
            pltpu.VMEM((blocks, points), f32),
            pltpu.SemaphoreType.DMA,
        ],
        compiler_params=params(),
        name="regrid_blocks",
    )(
        *surfaces, *one_hots, a2o_count, marine_air_piece_tally,
        a2o_weight, marine_air_piece_factor, e1, e3,
    )
    for mask in masks[:-1]:
        landing = landing + lax.ppermute(sent, "gy", sum_route(mask)).astype(f32)
        sent = landing.astype(bf16)
    part = lax.ppermute(sent, "gy", sum_route(masks[-1]))

    extra = []
    if not paired:
        p, q = jnp.moveaxis(lax.all_gather(sums[0], "gx").astype(f32), 1, 0)
        viscous = lax.dynamic_slice_in_dim(
            diffusivity, lax.axis_index("gy") * channels, channels
        )[:, None]
        rates = [half_rates(g, 0, columns // 4, columns) for g in (0, 0, 1, 1)]
        _, alpha, _ = decay_terms(viscous, jnp.concatenate(rates, axis=1))
        gap = lax.axis_index("gx") - jnp.arange(groups_x)
        decay = jnp.exp(
            -(rows * jnp.maximum(jnp.abs(gap) - 1, 0))[:, None, None] * alpha[None]
        )
        extra = [
            jnp.sum(jnp.where((gap > 0)[:, None, None], decay * p, 0.0), axis=0),
            jnp.sum(jnp.where((gap < 0)[:, None, None], decay * q, 0.0), axis=0),
        ]
    ring = channels // 2 + 8
    damped, coefs, stepped = pl.pallas_call(
        functools.partial(first_step_kernel, groups_x, groups_y, paired),
        out_shape=[
            shape((rows * channels, columns), bf16),
            shape((7, 16, columns), f32),
            shape((rows + 2, 2, ring, columns), f32),
        ],
        in_specs=[vmem] * (8 + len(extra)),
        out_specs=[vmem] * 3,
        scratch_shapes=[
            pltpu.VMEM((rows, channels, LANES), f32),
            pltpu.VMEM((rows + 4, 2, ring, columns), f32),
            pltpu.VMEM((16, columns), f32),
        ],
        compiler_params=params(),
        name="damping_or_first_step",
    )(fields, wet_cells, diff_row, y, e1, e3, e2, e4, *extra)

    surface_sum, near, far = pl.pallas_call(
        functools.partial(heat_kernel, rows),
        out_shape=[
            shape((cells, LANES), f32),
            shape((cells + columns // 16, LANES), bf16),
            shape((cells + columns // 16, LANES), bf16),
        ],
        in_specs=[vmem] * 4 + [anywhere],
        out_specs=[vmem] * 3,
        compiler_params=params(),
        name="surface_sum",
    )(e2, e4, landing, part, coefs)

    near = lax.ppermute(near, "gx", both_ways(ring_pairs(groups_x, 0)))
    far = lax.ppermute(far, "gx", both_ways(ring_pairs(groups_x, 1)))
    base, column = pl.pallas_call(
        second_step_kernel,
        out_shape=[shape((rows, channels, columns), f32), shape((channels, LANES), f32)],
        in_specs=[vmem] * 5,
        out_specs=[vmem] * 2,
        compiler_params=params(),
        name="inverse_or_second_step",
    )(gain_row, inverse, damped, coefs, stepped)
    return pl.pallas_call(
        functools.partial(last_kernel, groups_x, groups_y),
        out_shape=shape(fields.shape, f32),
        in_specs=[vmem] * 6,
        out_specs=hbm,
        scratch_shapes=[
            pltpu.VMEM((rows, channels, columns), f32),
            pltpu.VMEM((16, columns), f32),
            pltpu.VMEM((2, rows, columns), f32),
            pltpu.SemaphoreType.DMA((rows,)),
        ],
        compiler_params=params(),
        name="add_surface_terms",
    )(column, base, coefs, surface_sum, near, far)


def solution(mesh):
    in_specs = (
        P("comp", "gx", "gy", None),
        P("gx", None),
        P(),
        P(),
        P(),
        P("gx", "gy", None, None),
        P("gx", "gy", None, None),
        P("gx", "gy"),
        P("gx", "gy", None, None, None),
        P("gx", "gy", None, None),
        P("gx", "gy", None, None),
        P("gx", "gy"),
        P("gx", "gy", None, None, None),
    )
    out_specs = P("comp", "gx", "gy", None)
    return jax.shard_map(local, mesh=mesh, in_specs=in_specs, out_specs=out_specs, check_vma=False)
```

```python
import functools

import jax
import jax.numpy as jnp
import numpy as np
from jax import lax
from jax.experimental import pallas as pl
from jax.experimental.pallas import tpu as pltpu
from jax.sharding import PartitionSpec as P

spread_rate = 0.2
mixing_rate = 0.1
heat_gain = 0.5
salt_gain = -0.25
LANES = 128
f32 = jnp.float32
bf16 = jnp.bfloat16


def fourier_tables(columns):
    half = columns // 2
    forward, inverse = [], []
    for first in (0, 1):
        waves = np.arange(first, half, 2)
        phase = np.arange(half)[:, None] * waves[None, :] % columns
        angles = phase * (2.0 * np.pi / columns)
        table = np.concatenate([np.cos(angles), np.sin(angles)], axis=1)
        weight = np.where(waves == 0, 1.0, 2.0) / columns
        forward.append(table)
        inverse.append(table.T * np.concatenate([weight, weight])[:, None])
    return (
        jnp.asarray(np.concatenate(forward).astype(np.float32), bf16),
        jnp.asarray(np.concatenate(inverse).astype(np.float32), bf16),
    )


def wave_parts(columns):
    quarter = columns // 4
    return [
        (g, n, (g * 2 * quarter + n, (g * 2 + 1) * quarter + n))
        for g in (0, 1)
        for n in range(0, quarter, LANES)
    ]


def half_rates(group, first, count, columns):
    lane = lax.broadcasted_iota(jnp.int32, (1, count), 1) + first
    wave = (2 * lane + group).astype(f32)
    sine = jnp.sin(wave * (np.pi / columns))
    return 2.0 * sine * sine


def both_ways(pairs):
    return [p for a, b in pairs for p in ((a, b), (b, a))]


def channel_column(row, channels, first):
    n = row.shape[1]
    lane = lax.broadcasted_iota(jnp.int32, (channels, n), 1)
    sub = lax.broadcasted_iota(jnp.int32, (channels, n), 0)
    return jnp.sum(jnp.where(lane == sub + first, row, 0.0), axis=1, keepdims=True)


def to_tiles(surface):
    cols = surface.shape[1]
    return jnp.concatenate(
        [surface[:, k : k + LANES] for k in range(0, cols, LANES)], axis=0
    )


def from_tiles(tiles, rows):
    return jnp.concatenate(
        [tiles[k : k + rows] for k in range(0, tiles.shape[0], rows)], axis=1
    )


def lengthen(ref, block):
    rows = block.shape[0]
    ref[0:rows, :] = block
    if ref.shape[0] > rows:
        ref[rows:, :] = block[: ref.shape[0] - rows]


def decay_terms(diff_column, rates):
    half = 0.5 / diff_column + rates
    sinh = jnp.sqrt(half * (half + 2.0))
    grow = 1.0 + half + sinh
    return 1.0 / grow, jnp.log(grow), sinh


def edge_factors(lam, alpha, base, total, rows):
    lam2 = lam * lam
    powers = [
        jnp.exp(-2.0 * base * alpha) * lam2,
        jnp.exp(-2.0 * (total - rows - base) * alpha) * lam2,
    ]
    lows, highs = [], []
    for _ in range(rows):
        lows.append(1.0 - powers[0])
        highs.insert(0, 1.0 - powers[1])
        powers = [power * lam2 for power in powers]
    return lows, highs


def start_kernel(
    groups_x, paired, x_hbm, wet_hbm, flux_hbm, diff_hbm, table_hbm, *refs
):
    outs = 7 if paired else 8
    coarse_hbm, wide_hbm, y_hbm, *message_hbm = refs[:outs]
    coarse_ref, wide_ref, y_ref, *message_ref = refs[outs : 2 * outs]
    e1_ref, e3_ref, e2_ref, e4_ref = message_ref[:4]
    if not paired:
        pq_ref = message_ref[4]
    (
        x_ref, wet_ref, flux_ref, diff_ref, table_ref, flat_ref, row_ref, edge_ref,
        x_sem, sem, out_sem,
    ) = refs[2 * outs :]
    rows, channels, columns = x_ref.shape
    half = columns // 2
    row_group = lax.axis_index("gx")
    col_group = lax.axis_index("gy")
    is_atmos = lax.axis_index("comp") == 0

    x_copies = [
        pltpu.make_async_copy(x_hbm.at[0, r], x_ref.at[r], x_sem.at[r]) for r in range(rows)
    ]
    surface_copies = [
        pltpu.make_async_copy(coarse_ref, coarse_hbm, out_sem.at[0]),
        pltpu.make_async_copy(wide_ref, wide_hbm, out_sem.at[1]),
    ]
    y_copies = [
        pltpu.make_async_copy(y_ref.at[r], y_hbm.at[r], out_sem.at[2 + r]) for r in range(rows)
    ]
    message_copies = [
        pltpu.make_async_copy(ref, hbm, out_sem.at[2 + rows + k])
        for k, (ref, hbm) in enumerate(zip(message_ref, message_hbm))
    ]

    def send_surface():
        coarse = to_tiles(row_ref[...]).astype(bf16)
        coarse_ref[...] = coarse
        lengthen(wide_ref, coarse)
        for copy in surface_copies:
            copy.start()

    @pl.when(is_atmos)
    def _():
        flux_copy = pltpu.make_async_copy(flux_hbm, flux_ref, sem.at[0])
        diff_copy = pltpu.make_async_copy(diff_hbm, diff_ref, sem.at[1])
        table_copy = pltpu.make_async_copy(table_hbm, table_ref, sem.at[2])
        for copy in [flux_copy, diff_copy] + x_copies + [table_copy]:
            copy.start()
        first = col_group * channels
        flux_copy.wait()
        weight = channel_column(flux_ref[...], channels, first)
        for r in range(rows):
            x_copies[r].wait()
            row_ref[r : r + 1, :] = jnp.sum(x_ref[r] * weight, axis=0, keepdims=True)
            left, right = x_ref[r, :, :half], x_ref[r, :, half:]
            flat_ref[r * channels : (r + 1) * channels, :half] = (left + right).astype(bf16)
            flat_ref[r * channels : (r + 1) * channels, half:] = (left - right).astype(bf16)
        send_surface()
        table_copy.wait()
        for k in range(2):
            lanes = slice(k * half, (k + 1) * half)
            part = jnp.dot(
                flat_ref[:, lanes], table_ref[lanes, :], preferred_element_type=f32
            )
            y_ref[:, :, lanes] = part.reshape(rows, channels, half)
        for copy in y_copies:
            copy.start()
        diff_copy.wait()
        diff = channel_column(diff_ref[...], channels, first)
        total = rows * groups_x
        base = (row_group * rows).astype(f32)
        for group, n, parts in wave_parts(columns):
            lam, alpha, _ = decay_terms(diff, half_rates(group, n, LANES, columns))
            lows, highs = edge_factors(lam, alpha, base, total, rows)
            for part in parts:
                lanes = slice(part, part + LANES)
                p = lows[0] * y_ref[0, :, lanes]
                q = highs[-1] * y_ref[rows - 1, :, lanes]
                for r in range(1, rows):
                    p = lam * p + lows[r] * y_ref[r, :, lanes]
                    q = lam * q + highs[-1 - r] * y_ref[rows - 1 - r, :, lanes]
                if paired:
                    for mask, out in ((1, e1_ref), (2, e2_ref), (3, e3_ref)):
                        upward = row_group < (row_group ^ mask)
                        out[0:channels, lanes] = jnp.where(upward, p, q).astype(bf16)
                else:
                    pq_ref[0, :, lanes] = p.astype(bf16)
                    pq_ref[1, :, lanes] = q.astype(bf16)
        for copy in message_copies:
            copy.start()
        for copy in surface_copies + y_copies + message_copies:
            copy.wait()

    @pl.when(jnp.logical_not(is_atmos))
    def _():
        wet_copy = pltpu.make_async_copy(wet_hbm, wet_ref, sem.at[0])
        for copy in x_copies + [wet_copy]:
            copy.start()
        gain = jnp.where(col_group == 0, 1.0, 0.0)
        for r in range(rows):
            x_copies[r].wait()
            row_ref[r : r + 1, :] = x_ref[r, 0:1, :] * gain
        send_surface()
        wet_copy.wait()
        levels = channels // 2
        lines = 2 * channels
        even_x = row_group % 2 == 0
        even_y = col_group % 2 == 0
        wet = wet_ref[...].astype(f32)
        wet = jnp.concatenate([wet, wet], axis=0).astype(bf16)

        def put(out, last):
            @pl.when(last)
            def _():
                out[0:lines, :] = x_ref[rows - 2 :].reshape(lines, columns).astype(bf16)

            @pl.when(jnp.logical_not(last))
            def _():
                out[0:lines, :] = x_ref[:2].reshape(lines, columns).astype(bf16)

            out[lines : lines + 16, :] = wet

        put(e1_ref, even_x)
        put(e3_ref, jnp.logical_not(even_x))

        def put_edges(out, level):
            for r in range(rows):
                for t in range(2):
                    at = (r * 2 + t) * 2
                    c = t * levels + level
                    edge_ref[at : at + 2, :] = x_ref[r, c : c + 2, :]
            out[...] = edge_ref[...].astype(bf16)

        @pl.when(even_y)
        def _():
            put_edges(e2_ref, levels - 2)
            put_edges(e4_ref, 0)

        @pl.when(jnp.logical_not(even_y))
        def _():
            put_edges(e2_ref, 0)
            put_edges(e4_ref, levels - 2)

        for copy in message_copies:
            copy.start()
        for copy in surface_copies + message_copies:
            copy.wait()


def one_hot_kernel(
    rows, columns, a_src, a_dst, m_src, m_dst, _, src_hot_ref, dst_hot_ref, src_row_ref, dst_row_ref
):
    is_atmos = lax.axis_index("comp") == 0
    blocks, points = src_row_ref.shape
    lane_iota = lax.broadcasted_iota(jnp.int32, (LANES, points), 0)
    for a_ref, m_ref, hot_ref, row_ref in (
        (a_src, m_src, src_hot_ref, src_row_ref),
        (a_dst, m_dst, dst_hot_ref, dst_row_ref),
    ):
        index = jnp.where(is_atmos, m_ref[0, 0], a_ref[0, 0])
        row = index // columns
        tile = (index // LANES) % (columns // LANES)
        row_ref[...] = tile * rows + row
        lane = index % LANES
        for b in range(blocks):
            hot_ref[:, b * points : (b + 1) * points] = jnp.where(
                lane_iota == lane[b : b + 1], 1.0, 0.0
            ).astype(bf16)


def regrid_kernel(n_surfaces, *refs):
    surfaces = refs[:n_surfaces]
    (
        src_hot_ref, dst_hot_ref, src_row_ref, dst_row_ref, a_count, m_count, a_weight, m_weight,
        _, _, _, _,
        *refs,
    ) = refs[n_surfaces:]
    land_ref, *sent_refs = refs[:-4]
    weight_ref, gath_ref, val_ref, sem = refs[-4:]
    is_atmos = lax.axis_index("comp") == 0
    blocks, points = val_ref.shape
    cells = surfaces[0].shape[0]

    @pl.when(is_atmos)
    def _():
        pltpu.make_async_copy(m_weight.at[0, 0], weight_ref, sem).start()

    @pl.when(jnp.logical_not(is_atmos))
    def _():
        pltpu.make_async_copy(a_weight.at[0, 0], weight_ref, sem).start()

    count = jnp.where(is_atmos, m_count[0, 0], a_count[0, 0])
    pair = 2 * points
    row_iota = lax.broadcasted_iota(jnp.int32, (cells, points), 0)
    table = sum(surface[...].astype(f32) for surface in surfaces).astype(bf16)
    for b in range(0, blocks, 2):
        picked = jnp.dot(
            table, src_hot_ref[:, b * points : b * points + pair], preferred_element_type=f32
        )
        for k in range(2):
            mine = row_iota == src_row_ref[b + k : b + k + 1, :]
            part = jnp.where(mine, picked[:, k * points : (k + 1) * points], 0.0)
            gath_ref[b + k : b + k + 1, :] = jnp.sum(part, axis=0, keepdims=True)
    gathered = gath_ref[...].astype(bf16)

    @pl.when(is_atmos)
    def _():
        pltpu.make_async_copy(m_weight.at[0, 0], weight_ref, sem).wait()

    @pl.when(jnp.logical_not(is_atmos))
    def _():
        pltpu.make_async_copy(a_weight.at[0, 0], weight_ref, sem).wait()

    block_iota = lax.broadcasted_iota(jnp.int32, (blocks, points), 0)
    values = jnp.zeros((blocks, points), f32)
    for b in range(0, blocks, 2):
        terms = lax.dot_general(
            gathered,
            weight_ref[b : b + 2].reshape(pair, points),
            (((1,), (1,)), ((), ())),
            preferred_element_type=f32,
        )
        for k in range(2):
            values = jnp.where(block_iota == b + k, terms[:, k * points : (k + 1) * points], values)
    val_ref[...] = jnp.where(block_iota < count, values, 0.0)
    land = jnp.zeros((2 * cells, LANES), f32)
    for b in range(0, blocks, 2):
        spread = []
        for k in range(b, b + 2):
            value = val_ref[k : k + 1, :]
            coarse = value.astype(bf16).astype(f32)
            fine = value - coarse
            mine = row_iota == dst_row_ref[k : k + 1, :]
            spread.append(
                jnp.concatenate(
                    [jnp.where(mine, coarse, 0.0), jnp.where(mine, fine, 0.0)], axis=0
                ).astype(bf16)
            )
        land = land + lax.dot_general(
            jnp.concatenate(spread, axis=1),
            dst_hot_ref[:, b * points : b * points + pair],
            (((1,), (1,)), ((), ())),
            preferred_element_type=f32,
        )
    land = land[:cells] + land[cells:]
    land_ref[...] = land
    for sent_ref in sent_refs:
        lengthen(sent_ref, land.astype(bf16))


def heat_kernel(rows, e2_ref, e4_ref, land_ref, _, *refs):
    parts = refs[:-3]
    sum_ref, near_ref, far_ref = refs[-3:]
    cells = land_ref.shape[0]
    columns = cells // rows * LANES
    even_x = lax.axis_index("gx") % 2 == 0
    even_y = lax.axis_index("gy") % 2 == 0
    total = land_ref[...]
    for part in parts:
        total = total + part[0:cells, :].astype(f32)
    sum_ref[...] = total

    def corners(row):
        start = row * 4 // 16 * 16
        one = e2_ref[start : start + 16, :].astype(f32)
        two = e4_ref[start : start + 16, :].astype(f32)
        low = jnp.where(even_y, two, one)
        high = jnp.where(even_y, one, two)
        at = row * 4 - start
        lines = [low[at + 1 : at + 2], low[at + 3 : at + 4], high[at : at + 1], high[at + 2 : at + 3]]
        return to_tiles(jnp.concatenate(lines + [jnp.zeros((4, columns), f32)], axis=0))

    first, last = corners(0), corners(rows - 1)
    near_ref[0:cells, :] = total.astype(bf16)
    far_ref[0:cells, :] = total.astype(bf16)
    near_ref[cells:, :] = jnp.where(even_x, last, first).astype(bf16)
    far_ref[cells:, :] = jnp.where(even_x, first, last).astype(bf16)


def advance(ref, r, t, coefs, size):
    ring, columns = ref.shape[2:]
    whole = ref[r, t]
    up = pltpu.roll(whole, 1, 0)[:size]
    down = pltpu.roll(whole, ring - 1, 0)[:size]
    mid = whole[:size]
    total = coefs[0] * mid + coefs[5] * (up + down)
    total = total + coefs[1] * ref[r - 1, t, 0:size, :]
    total = total + coefs[2] * ref[r + 1, t, 0:size, :]
    total = total + coefs[3] * pltpu.roll(mid, 1, 1)
    return total + coefs[4] * pltpu.roll(mid, columns - 1, 1)


def first_step_kernel(
    groups_x, groups_y, paired, x_ref, wet_ref, diff_ref, y_ref, e1_ref, e3_ref,
    e2_ref, e4_ref, *refs,
):
    if not paired:
        pin_ref, qin_ref = refs[:2]
    zb_ref, c_ref, t1_ref, z_ref, t0_ref, w_ref = refs[-6:]
    _, rows, channels, columns = x_ref.shape
    row_group = lax.axis_index("gx")
    col_group = lax.axis_index("gy")
    is_atmos = lax.axis_index("comp") == 0

    @pl.when(is_atmos)
    def _():
        diff = channel_column(diff_ref[...], channels, col_group * channels)
        total = rows * groups_x
        base = (row_group * rows).astype(f32)
        for group, n, parts in wave_parts(columns):
            lam, alpha, sinh = decay_terms(diff, half_rates(group, n, LANES, columns))
            scale = 1.0 / (
                2.0 * diff * sinh * (1.0 - jnp.exp(-2.0 * (total + 1) * alpha))
            )
            lows, highs = edge_factors(lam, alpha, base, total, rows)
            for part in parts:
                lanes = slice(part, part + LANES)
                if paired:
                    pin = jnp.zeros((channels, LANES), f32)
                    qin = jnp.zeros((channels, LANES), f32)
                    for mask, msg in ((1, e1_ref), (2, e2_ref), (3, e3_ref)):
                        band = row_group ^ mask
                        gap = (jnp.abs(row_group - band) - 1) * rows
                        term = jnp.exp(-gap.astype(f32) * alpha)
                        term = term * msg[0:channels, lanes].astype(f32)
                        pin = pin + jnp.where(band < row_group, term, 0.0)
                        qin = qin + jnp.where(band > row_group, term, 0.0)
                else:
                    pin = pin_ref[:, lanes]
                    qin = qin_ref[:, lanes]
                f = pin
                for r in range(rows):
                    f = lam * f + lows[r] * y_ref[r, :, lanes]
                    z_ref[r] = highs[r] * f
                g = lam * qin
                for r in reversed(range(rows)):
                    z = scale * (z_ref[r] + lows[r] * g)
                    zb_ref[r * channels : (r + 1) * channels, lanes] = z.astype(bf16)
                    g = lam * (g + highs[r] * y_ref[r, :, lanes])

    @pl.when(jnp.logical_not(is_atmos))
    def _():
        levels = channels // 2
        ring = levels + 8
        lines = 2 * channels
        first_x = row_group == 0
        last_x = row_group == groups_x - 1
        top = col_group == 0
        bottom = col_group == groups_y - 1
        even_x = row_group % 2 == 0
        even_y = col_group % 2 == 0

        one = e1_ref[lines : lines + 16, :].astype(f32)
        three = e3_ref[lines : lines + 16, :].astype(f32)
        below = jnp.where(even_x, three, one)[rows - 2 : rows]
        above = jnp.where(even_x, one, three)[0:2]
        w_ref[0:2, :] = jnp.where(first_x, 0.0, below)
        w_ref[2 : rows + 2, :] = wet_ref[...].astype(f32)
        w_ref[rows + 2 : rows + 4, :] = jnp.where(last_x, 0.0, above)

        span = rows + 2
        north = w_ref[0:span, :]
        here = w_ref[1 : span + 1, :]
        south = w_ref[2 : span + 2, :]
        west = pltpu.roll(here, 1, 1)
        east = pltpu.roll(here, columns - 1, 1)
        c_ref[0, 0:span, :] = here * (
            1.0 - 2.0 * mixing_rate - spread_rate * (north + south + west + east)
        )
        c_ref[1, 0:span, :] = spread_rate * here * north
        c_ref[2, 0:span, :] = spread_rate * here * south
        c_ref[3, 0:span, :] = spread_rate * here * west
        c_ref[4, 0:span, :] = spread_rate * here * east
        c_ref[5, 0:span, :] = mixing_rate * here
        c_ref[6, 0:span, :] = here

        one = e1_ref[0:lines, :].astype(f32)
        three = e3_ref[0:lines, :].astype(f32)
        below = jnp.where(even_x, three, one)
        above = jnp.where(even_x, one, three)
        blank = jnp.zeros((8, columns), f32)
        for k in range(2):
            for t in range(2):
                c = k * channels + t * levels
                t0_ref[k, t, 0:levels, :] = below[c : c + levels]
                t0_ref[rows + 2 + k, t, 0:levels, :] = above[c : c + levels]
                t0_ref[k, t, levels:ring, :] = blank
                t0_ref[rows + 2 + k, t, levels:ring, :] = blank
        one = e2_ref[...].astype(f32)
        two = e4_ref[...].astype(f32)
        before = jnp.where(even_y, two, one)
        after = jnp.where(even_y, one, two)
        for r in range(rows):
            for t in range(2):
                k = (r * 2 + t) * 2
                t0_ref[r + 2, t, 0:levels, :] = x_ref[0, r, t * levels : (t + 1) * levels, :]
                t0_ref[r + 2, t, levels : levels + 2, :] = after[k : k + 2]
                t0_ref[r + 2, t, ring - 2 : ring, :] = before[k : k + 2]

        def close(ref, r):
            for t in range(2):
                ref[r, t, ring - 1 : ring, :] = jnp.where(
                    top, ref[r, t, 0:1, :], ref[r, t, ring - 1 : ring, :]
                )
                ref[r, t, levels : levels + 1, :] = jnp.where(
                    bottom, ref[r, t, levels - 1 : levels, :], ref[r, t, levels : levels + 1, :]
                )

        def first(r, carry):
            coefs = [c_ref[k, pl.ds(r, 1), :] for k in range(6)]
            close(t0_ref, r + 1)
            for t in range(2):
                t1_ref[r, t] = advance(t0_ref, r + 1, t, coefs, ring)
            close(t1_ref, r)
            return carry

        lax.fori_loop(0, span, first, 0)


def second_step_kernel(gain_ref, table_ref, zb_ref, c_ref, t1_ref, base_ref, column_ref):
    rows, channels, columns = base_ref.shape
    is_atmos = lax.axis_index("comp") == 0

    @pl.when(is_atmos)
    def _():
        response = channel_column(gain_ref[...], channels, lax.axis_index("gy") * channels)
        column_ref[...] = jnp.broadcast_to(response, column_ref.shape)
        half = columns // 2
        step = 256
        for n in range(0, half, step):
            even, odd = [
                jnp.dot(
                    zb_ref[:, k * half : (k + 1) * half],
                    table_ref[k * half : (k + 1) * half, n : n + step],
                    preferred_element_type=f32,
                ).reshape(rows, channels, step)
                for k in range(2)
            ]
            base_ref[:, :, n : n + step] = even + odd
            base_ref[:, :, n + half : n + half + step] = even - odd

    @pl.when(jnp.logical_not(is_atmos))
    def _():
        levels = channels // 2

        def second(r, carry):
            coefs = [c_ref[k, pl.ds(r, 1), :] for k in range(6)]
            for t in range(2):
                c = t * levels
                base_ref[r - 1, c : c + levels, :] = advance(t1_ref, r, t, coefs, levels)
            return carry

        lax.fori_loop(1, rows + 1, second, 0)


def last_kernel(
    groups_x, groups_y, column_ref, base_ref, c_ref, sum_ref, near_ref, far_ref, out_hbm,
    out_ref, e_ref, heat_ref, sem,
):
    rows, channels, columns = out_ref.shape
    row_group = lax.axis_index("gx")
    col_group = lax.axis_index("gy")
    is_atmos = lax.axis_index("comp") == 0
    copies = [
        pltpu.make_async_copy(out_ref.at[r], out_hbm.at[0, r], sem.at[r]) for r in range(rows)
    ]

    @pl.when(is_atmos)
    def _():
        for r in range(rows):
            for k in range(columns // LANES):
                lanes = slice(k * LANES, (k + 1) * LANES)
                at = k * rows + r
                out_ref[r, :, lanes] = (
                    base_ref[r, :, lanes] + column_ref[...] * sum_ref[at : at + 1, :]
                )
            copies[r].start()

    @pl.when(jnp.logical_not(is_atmos))
    def _():
        levels = channels // 2
        cells = sum_ref.shape[0]
        even = row_group % 2 == 0
        below = jnp.where(even, far_ref[...].astype(f32), near_ref[...].astype(f32))
        above = jnp.where(even, near_ref[...].astype(f32), far_ref[...].astype(f32))

        low = from_tiles(below[cells:], 8)
        high = from_tiles(above[cells:], 8)
        by_low = c_ref[1, 1:2, :] * (c_ref[5, 0:1, :] + c_ref[5, 1:2, :])
        by_high = c_ref[2, rows : rows + 1, :] * (
            c_ref[5, rows : rows + 1, :] + c_ref[5, rows + 1 : rows + 2, :]
        )
        has_before = jnp.where(col_group > 0, 1.0, 0.0)
        has_after = jnp.where(col_group < groups_y - 1, 1.0, 0.0)

        @pl.when(col_group == 0)
        def _():
            span = rows + 2
            e_ref[0:1, :] = from_tiles(below[:cells], rows)[rows - 1 : rows]
            e_ref[1 : rows + 1, :] = from_tiles(sum_ref[...], rows)
            e_ref[rows + 1 : span, :] = from_tiles(above[:cells], rows)[0:1]
            e_ref[0:span, :] = c_ref[6, 0:span, :] * e_ref[0:span, :]
            own = slice(1, rows + 1)
            heat = e_ref[own, :]
            second = c_ref[5, own, :] * heat
            first = (c_ref[0, own, :] + 1.0) * heat + second
            first = first + c_ref[1, own, :] * e_ref[0:rows, :]
            first = first + c_ref[2, own, :] * e_ref[2 : rows + 2, :]
            first = first + c_ref[3, own, :] * pltpu.roll(heat, 1, 1)
            first = first + c_ref[4, own, :] * pltpu.roll(heat, columns - 1, 1)
            heat_ref[0] = first
            heat_ref[1] = second

        for r in [1, rows - 2] + list(range(2, rows - 2)) + [0, rows - 1]:
            out_ref[r] = base_ref[r]
            for t in range(2):
                c = t * levels
                for edge, factor, lines in ((0, by_low, low), (rows - 1, by_high, high)):
                    if r == edge:
                        out_ref[r, c : c + 1, :] = out_ref[r, c : c + 1, :] + (
                            has_before * factor * lines[t : t + 1]
                        )
                        d = c + levels - 1
                        out_ref[r, d : d + 1, :] = out_ref[r, d : d + 1, :] + (
                            has_after * factor * lines[t + 2 : t + 3]
                        )

            @pl.when(col_group == 0)
            def _():
                for t, gain in enumerate((heat_gain, salt_gain)):
                    c = t * levels
                    for k in range(2):
                        out_ref[r, c + k : c + k + 1, :] = (
                            out_ref[r, c + k : c + k + 1, :] + gain * heat_ref[k, r : r + 1, :]
                        )

            copies[r].start()

    for copy in copies:
        copy.wait()


def local(
    fields,
    wet_cells,
    flux_weight,
    variable_sea_response,
    diffusivity,
    a2o_source,
    a2o_target,
    a2o_count,
    a2o_weight,
    marine_air_input_index,
    marine_air_output_index,
    marine_air_piece_tally,
    marine_air_piece_factor,
):
    _, rows, channels, columns = fields.shape
    groups_x = lax.axis_size("gx")
    groups_y = lax.axis_size("gy")
    blocks, points = a2o_source.shape[2:]
    cells = rows * columns // LANES
    forward, inverse = fourier_tables(columns)
    flux_row = flux_weight[None, :]
    gain_row = variable_sea_response[None, :]
    diff_row = diffusivity[None, :]
    paired = groups_x == 4
    params = functools.partial(pltpu.CompilerParams, vmem_limit_bytes=40 * 2**20)
    vmem = pl.BlockSpec(memory_space=pltpu.VMEM)
    smem = pl.BlockSpec(memory_space=pltpu.SMEM)
    hbm = pl.BlockSpec(memory_space=pltpu.HBM)
    anywhere = pl.BlockSpec(memory_space=pl.ANY)

    def shape(dims, dtype):
        return jax.ShapeDtypeStruct(dims, dtype)

    lines = 2 * channels + 16
    shapes = [
        shape((cells, LANES), bf16),
        shape((cells + 16, LANES), bf16),
        shape((rows, channels, columns), f32),
        shape((lines, columns), bf16),
        shape((lines, columns), bf16),
        shape((4 * rows, columns), bf16),
        shape((4 * rows, columns), bf16),
    ]
    if not paired:
        shapes.append(shape((2, channels, columns), bf16))
    coarse, wide, y, e1, e3, e2, e4, *sums = pl.pallas_call(
        functools.partial(start_kernel, groups_x, paired),
        out_shape=shapes,
        in_specs=[hbm] * 5,
        out_specs=[hbm] * len(shapes),
        scratch_shapes=[pltpu.VMEM(out.shape, out.dtype) for out in shapes]
        + [
            pltpu.VMEM((rows, channels, columns), f32),
            pltpu.VMEM((rows, columns), jnp.int32),
            pltpu.VMEM(flux_row.shape, f32),
            pltpu.VMEM(diff_row.shape, f32),
            pltpu.VMEM(forward.shape, bf16),
            pltpu.VMEM((rows * channels, columns), bf16),
            pltpu.VMEM((rows, columns), f32),
            pltpu.VMEM((4 * rows, columns), f32),
            pltpu.SemaphoreType.DMA((rows,)),
            pltpu.SemaphoreType.DMA((3,)),
            pltpu.SemaphoreType.DMA((rows + len(shapes) - 1,)),
        ],
        compiler_params=pltpu.CompilerParams(vmem_limit_bytes=58 * 2**20),
        name="surface_and_forward_or_halos",
    )(fields, wet_cells, flux_row, diff_row, forward)

    masks = [1 << bit for bit in range(groups_y.bit_length() - 1)]

    def sum_route(mask):
        return [(j, j ^ mask) for j in range(groups_y)]

    def partner_route(mask):
        return both_ways([(j, groups_y + (j ^ mask)) for j in range(groups_y)])

    surface = lax.ppermute(coarse, ("comp", "gy"), partner_route(0)).astype(f32)
    for mask in masks[:1]:
        far = lax.ppermute(wide, ("comp", "gy"), partner_route(mask))
        surface = surface + far[:cells].astype(f32)
    coarse = surface.astype(bf16)
    for mask in masks[1:-1]:
        surface = surface + lax.ppermute(coarse, "gy", sum_route(mask)).astype(f32)
        coarse = surface.astype(bf16)
    surfaces = [surface] + [
        lax.ppermute(coarse, "gy", sum_route(mask)) for mask in masks[1:][-1:]
    ]

    def ring_pairs(count, odd):
        return [(a, (a + 1) % count) for a in range(odd, count, 2)]

    def flat(comp, i, j):
        return (comp * groups_x + i) * groups_y + j

    def level_route(odd):
        pairs = []
        for i in range(groups_x):
            linked = [(a, a + 1) for a in range(odd, groups_y - 1, 2)]
            alone = set(range(groups_y)) - {j for pair in linked for j in pair}
            pairs += [(flat(1, i, a), flat(1, i, b)) for a, b in linked]
            if i % 2 == 0:
                pairs += [(flat(1, i, j), flat(1, i + 1, j)) for j in sorted(alone)]
                if odd or not paired:
                    pairs += [(flat(0, i, j), flat(0, i + 1, j)) for j in range(groups_y)]
            if paired and not odd and i < i ^ 2:
                pairs += [(flat(0, i, j), flat(0, i ^ 2, j)) for j in range(groups_y)]
        return both_ways(pairs)

    e1 = lax.ppermute(e1, "gx", both_ways(ring_pairs(groups_x, 0)))
    e3 = lax.ppermute(e3, "gx", both_ways(ring_pairs(groups_x, 1)))
    axes = ("comp", "gx", "gy")
    e2 = lax.ppermute(e2, axes, level_route(0))
    e4 = lax.ppermute(e4, axes, level_route(1))

    one_hots = pl.pallas_call(
        functools.partial(one_hot_kernel, rows, columns),
        out_shape=[
            shape((LANES, blocks * points), bf16),
            shape((LANES, blocks * points), bf16),
            shape((blocks, points), jnp.int32),
            shape((blocks, points), jnp.int32),
        ],
        in_specs=[vmem] * 4 + [anywhere],
        out_specs=[vmem] * 4,
        compiler_params=params(),
        name="one_hots",
    )(a2o_source, a2o_target, marine_air_input_index, marine_air_output_index, coarse)
    landing, *sent = pl.pallas_call(
        functools.partial(regrid_kernel, len(surfaces)),
        out_shape=[shape((cells, LANES), f32)]
        + [shape((cells + 16 * (mask - 1), LANES), bf16) for mask in range(1, groups_y)],
        in_specs=[vmem] * (len(surfaces) + 4) + [smem, smem, hbm, hbm] + [anywhere] * 4,
        out_specs=[vmem] * groups_y,
        scratch_shapes=[
            pltpu.VMEM((blocks, points, points), bf16),
            pltpu.VMEM((blocks, points), f32),
            pltpu.VMEM((blocks, points), f32),
            pltpu.SemaphoreType.DMA,
        ],
        compiler_params=params(),
        name="regrid_blocks",
    )(
        *surfaces, *one_hots, a2o_count, marine_air_piece_tally,
        a2o_weight, marine_air_piece_factor, e1, e3, e2, e4,
    )
    parts = [
        lax.ppermute(block, "gy", sum_route(mask)) for mask, block in enumerate(sent, 1)
    ]

    extra = []
    if not paired:
        p, q = jnp.moveaxis(lax.all_gather(sums[0], "gx").astype(f32), 1, 0)
        viscous = lax.dynamic_slice_in_dim(
            diffusivity, lax.axis_index("gy") * channels, channels
        )[:, None]
        rates = [half_rates(g, 0, columns // 4, columns) for g in (0, 0, 1, 1)]
        _, alpha, _ = decay_terms(viscous, jnp.concatenate(rates, axis=1))
        gap = lax.axis_index("gx") - jnp.arange(groups_x)
        decay = jnp.exp(
            -(rows * jnp.maximum(jnp.abs(gap) - 1, 0))[:, None, None] * alpha[None]
        )
        extra = [
            jnp.sum(jnp.where((gap > 0)[:, None, None], decay * p, 0.0), axis=0),
            jnp.sum(jnp.where((gap < 0)[:, None, None], decay * q, 0.0), axis=0),
        ]
    ring = channels // 2 + 8
    damped, coefs, stepped = pl.pallas_call(
        functools.partial(first_step_kernel, groups_x, groups_y, paired),
        out_shape=[
            shape((rows * channels, columns), bf16),
            shape((7, 16, columns), f32),
            shape((rows + 2, 2, ring, columns), f32),
        ],
        in_specs=[vmem] * (8 + len(extra)),
        out_specs=[vmem] * 3,
        scratch_shapes=[
            pltpu.VMEM((rows, channels, LANES), f32),
            pltpu.VMEM((rows + 4, 2, ring, columns), f32),
            pltpu.VMEM((16, columns), f32),
        ],
        compiler_params=params(),
        name="damping_or_first_step",
    )(fields, wet_cells, diff_row, y, e1, e3, e2, e4, *extra)

    surface_sum, near, far = pl.pallas_call(
        functools.partial(heat_kernel, rows),
        out_shape=[
            shape((cells, LANES), f32),
            shape((cells + columns // 16, LANES), bf16),
            shape((cells + columns // 16, LANES), bf16),
        ],
        in_specs=[vmem] * 3 + [anywhere] + [vmem] * len(parts),
        out_specs=[vmem] * 3,
        compiler_params=params(),
        name="surface_sum",
    )(e2, e4, landing, coefs, *parts)

    near = lax.ppermute(near, "gx", both_ways(ring_pairs(groups_x, 0)))
    far = lax.ppermute(far, "gx", both_ways(ring_pairs(groups_x, 1)))
    base, column = pl.pallas_call(
        second_step_kernel,
        out_shape=[shape((rows, channels, columns), f32), shape((channels, LANES), f32)],
        in_specs=[vmem] * 5,
        out_specs=[vmem] * 2,
        compiler_params=params(),
        name="inverse_or_second_step",
    )(gain_row, inverse, damped, coefs, stepped)
    return pl.pallas_call(
        functools.partial(last_kernel, groups_x, groups_y),
        out_shape=shape(fields.shape, f32),
        in_specs=[vmem] * 6,
        out_specs=hbm,
        scratch_shapes=[
            pltpu.VMEM((rows, channels, columns), f32),
            pltpu.VMEM((16, columns), f32),
            pltpu.VMEM((2, rows, columns), f32),
            pltpu.SemaphoreType.DMA((rows,)),
        ],
        compiler_params=params(),
        name="add_surface_terms",
    )(column, base, coefs, surface_sum, near, far)


def solution(mesh):
    in_specs = (
        P("comp", "gx", "gy", None),
        P("gx", None),
        P(),
        P(),
        P(),
        P("gx", "gy", None, None),
        P("gx", "gy", None, None),
        P("gx", "gy"),
        P("gx", "gy", None, None, None),
        P("gx", "gy", None, None),
        P("gx", "gy", None, None),
        P("gx", "gy"),
        P("gx", "gy", None, None, None),
    )
    out_specs = P("comp", "gx", "gy", None)
    return jax.shard_map(local, mesh=mesh, in_specs=in_specs, out_specs=out_specs, check_vma=False)
```

```python
import functools

import jax
import jax.numpy as jnp
import numpy as np
from jax import lax
from jax.experimental import pallas as pl
from jax.experimental.pallas import tpu as pltpu
from jax.sharding import PartitionSpec as P

spread_rate = 0.2
mixing_rate = 0.1
heat_gain = 0.5
salt_gain = -0.25
LANES = 128
f32 = jnp.float32
bf16 = jnp.bfloat16


def fourier_tables(columns):
    half = columns // 2
    forward, inverse = [], []
    for first in (0, 1):
        waves = np.arange(first, half, 2)
        phase = np.arange(half)[:, None] * waves[None, :] % columns
        angles = phase * (2.0 * np.pi / columns)
        table = np.concatenate([np.cos(angles), np.sin(angles)], axis=1)
        weight = np.where(waves == 0, 1.0, 2.0) / columns
        forward.append(table)
        inverse.append(table.T * np.concatenate([weight, weight])[:, None])
    return (
        jnp.asarray(np.concatenate(forward).astype(np.float32), bf16),
        jnp.asarray(np.concatenate(inverse).astype(np.float32), bf16),
    )


def wave_parts(columns):
    quarter = columns // 4
    return [
        (g, n, (g * 2 * quarter + n, (g * 2 + 1) * quarter + n))
        for g in (0, 1)
        for n in range(0, quarter, LANES)
    ]


def half_rates(group, first, count, columns):
    lane = lax.broadcasted_iota(jnp.int32, (1, count), 1) + first
    wave = (2 * lane + group).astype(f32)
    sine = jnp.sin(wave * (np.pi / columns))
    return 2.0 * sine * sine


def both_ways(pairs):
    return [p for a, b in pairs for p in ((a, b), (b, a))]


def channel_column(row, channels, first):
    n = row.shape[1]
    lane = lax.broadcasted_iota(jnp.int32, (channels, n), 1)
    sub = lax.broadcasted_iota(jnp.int32, (channels, n), 0)
    return jnp.sum(jnp.where(lane == sub + first, row, 0.0), axis=1, keepdims=True)


def to_tiles(surface):
    cols = surface.shape[1]
    return jnp.concatenate(
        [surface[:, k : k + LANES] for k in range(0, cols, LANES)], axis=0
    )


def from_tiles(tiles, rows):
    return jnp.concatenate(
        [tiles[k : k + rows] for k in range(0, tiles.shape[0], rows)], axis=1
    )


def lengthen(ref, block):
    rows = block.shape[0]
    ref[0:rows, :] = block
    if ref.shape[0] > rows:
        ref[rows:, :] = block[: ref.shape[0] - rows]


def decay_terms(diff_column, rates):
    half = 0.5 / diff_column + rates
    sinh = jnp.sqrt(half * (half + 2.0))
    grow = 1.0 + half + sinh
    return 1.0 / grow, jnp.log(grow), sinh


def edge_factors(lam, alpha, base, total, rows):
    lam2 = lam * lam
    powers = [
        jnp.exp(-2.0 * base * alpha) * lam2,
        jnp.exp(-2.0 * (total - rows - base) * alpha) * lam2,
    ]
    lows, highs = [], []
    for _ in range(rows):
        lows.append(1.0 - powers[0])
        highs.insert(0, 1.0 - powers[1])
        powers = [power * lam2 for power in powers]
    return lows, highs


def start_kernel(
    groups_x, paired, x_hbm, wet_hbm, flux_hbm, diff_hbm, table_hbm, *refs
):
    outs = 7 if paired else 8
    coarse_hbm, wide_hbm, y_hbm, *message_hbm = refs[:outs]
    coarse_ref, wide_ref, y_ref, *message_ref = refs[outs : 2 * outs]
    e1_ref, e3_ref, e2_ref, e4_ref = message_ref[:4]
    if not paired:
        pq_ref = message_ref[4]
    (
        x_ref, wet_ref, flux_ref, diff_ref, table_ref, flat_ref, row_ref, edge_ref,
        factor_ref, x_sem, sem, out_sem,
    ) = refs[2 * outs :]
    rows, channels, columns = x_ref.shape
    half = columns // 2
    row_group = lax.axis_index("gx")
    col_group = lax.axis_index("gy")
    is_atmos = lax.axis_index("comp") == 0

    x_copies = [
        pltpu.make_async_copy(x_hbm.at[0, r], x_ref.at[r], x_sem.at[r]) for r in range(rows)
    ]
    surface_copies = [
        pltpu.make_async_copy(coarse_ref, coarse_hbm, out_sem.at[0]),
        pltpu.make_async_copy(wide_ref, wide_hbm, out_sem.at[1]),
    ]
    y_copies = [
        pltpu.make_async_copy(y_ref.at[r], y_hbm.at[r], out_sem.at[2 + r]) for r in range(rows)
    ]
    message_copies = [
        pltpu.make_async_copy(ref, hbm, out_sem.at[2 + rows + k])
        for k, (ref, hbm) in enumerate(zip(message_ref, message_hbm))
    ]

    def send_surface():
        coarse = to_tiles(row_ref[...]).astype(bf16)
        coarse_ref[...] = coarse
        lengthen(wide_ref, coarse)
        for copy in surface_copies:
            copy.start()

    @pl.when(is_atmos)
    def _():
        flux_copy = pltpu.make_async_copy(flux_hbm, flux_ref, sem.at[0])
        diff_copy = pltpu.make_async_copy(diff_hbm, diff_ref, sem.at[1])
        table_copy = pltpu.make_async_copy(table_hbm, table_ref, sem.at[2])
        for copy in [flux_copy, diff_copy] + x_copies + [table_copy]:
            copy.start()
        first = col_group * channels
        flux_copy.wait()
        weight = channel_column(flux_ref[...], channels, first)
        diff_copy.wait()
        diff = channel_column(diff_ref[...], channels, first)
        total = rows * groups_x
        base = (row_group * rows).astype(f32)
        tiles = wave_parts(columns)
        for k, (group, n, _) in enumerate(tiles):
            lam, alpha, _ = decay_terms(diff, half_rates(group, n, LANES, columns))
            factor_ref[k, 0] = lam
            lows, highs = edge_factors(lam, alpha, base, total, rows)
            for r in range(rows):
                factor_ref[k, 1 + r] = lows[r]
                factor_ref[k, 1 + rows + r] = highs[r]
        for r in range(rows):
            x_copies[r].wait()
            row_ref[r : r + 1, :] = jnp.sum(x_ref[r] * weight, axis=0, keepdims=True)
            left, right = x_ref[r, :, :half], x_ref[r, :, half:]
            flat_ref[r * channels : (r + 1) * channels, :half] = (left + right).astype(bf16)
            flat_ref[r * channels : (r + 1) * channels, half:] = (left - right).astype(bf16)
        send_surface()
        table_copy.wait()
        for k in range(2):
            lanes = slice(k * half, (k + 1) * half)
            part = jnp.dot(
                flat_ref[:, lanes], table_ref[lanes, :], preferred_element_type=f32
            )
            y_ref[:, :, lanes] = part.reshape(rows, channels, half)
            for tile, (group, _, parts) in enumerate(tiles):
                if group != k:
                    continue
                lam = factor_ref[tile, 0]
                for at in parts:
                    lanes = slice(at, at + LANES)
                    here = slice(at - k * half, at - k * half + LANES)
                    p = factor_ref[tile, 1] * part[0:channels, here]
                    q = factor_ref[tile, 2 * rows] * part[(rows - 1) * channels :, here]
                    for r in range(1, rows):
                        up = part[r * channels : (r + 1) * channels, here]
                        down = part[(rows - 1 - r) * channels : (rows - r) * channels, here]
                        p = lam * p + factor_ref[tile, 1 + r] * up
                        q = lam * q + factor_ref[tile, 2 * rows - r] * down
                    if paired:
                        for mask, out in ((1, e1_ref), (2, e2_ref), (3, e3_ref)):
                            upward = row_group < (row_group ^ mask)
                            out[0:channels, lanes] = jnp.where(upward, p, q).astype(bf16)
                    else:
                        pq_ref[0, :, lanes] = p.astype(bf16)
                        pq_ref[1, :, lanes] = q.astype(bf16)
        for copy in y_copies:
            copy.start()
        for copy in message_copies:
            copy.start()
        for copy in surface_copies + y_copies + message_copies:
            copy.wait()

    @pl.when(jnp.logical_not(is_atmos))
    def _():
        wet_copy = pltpu.make_async_copy(wet_hbm, wet_ref, sem.at[0])
        for copy in x_copies + [wet_copy]:
            copy.start()
        gain = jnp.where(col_group == 0, 1.0, 0.0)
        for r in range(rows):
            x_copies[r].wait()
            row_ref[r : r + 1, :] = x_ref[r, 0:1, :] * gain
        send_surface()
        wet_copy.wait()
        levels = channels // 2
        lines = 2 * channels
        even_x = row_group % 2 == 0
        even_y = col_group % 2 == 0
        wet = wet_ref[...].astype(f32)
        wet = jnp.concatenate([wet, wet], axis=0).astype(bf16)

        def put(out, last):
            @pl.when(last)
            def _():
                out[0:lines, :] = x_ref[rows - 2 :].reshape(lines, columns).astype(bf16)

            @pl.when(jnp.logical_not(last))
            def _():
                out[0:lines, :] = x_ref[:2].reshape(lines, columns).astype(bf16)

            out[lines : lines + 16, :] = wet

        put(e1_ref, even_x)
        put(e3_ref, jnp.logical_not(even_x))

        def put_edges(out, level):
            for r in range(rows):
                for t in range(2):
                    at = (r * 2 + t) * 2
                    c = t * levels + level
                    edge_ref[at : at + 2, :] = x_ref[r, c : c + 2, :]
            out[...] = edge_ref[...].astype(bf16)

        @pl.when(even_y)
        def _():
            put_edges(e2_ref, levels - 2)
            put_edges(e4_ref, 0)

        @pl.when(jnp.logical_not(even_y))
        def _():
            put_edges(e2_ref, 0)
            put_edges(e4_ref, levels - 2)

        for copy in message_copies:
            copy.start()
        for copy in surface_copies + message_copies:
            copy.wait()


def one_hot_kernel(
    rows, columns, a_src, a_dst, m_src, m_dst, _, src_hot_ref, dst_hot_ref, src_row_ref, dst_row_ref
):
    is_atmos = lax.axis_index("comp") == 0
    blocks, points = src_row_ref.shape
    lane_iota = lax.broadcasted_iota(jnp.int32, (LANES, points), 0)
    for a_ref, m_ref, hot_ref, row_ref in (
        (a_src, m_src, src_hot_ref, src_row_ref),
        (a_dst, m_dst, dst_hot_ref, dst_row_ref),
    ):
        index = jnp.where(is_atmos, m_ref[0, 0], a_ref[0, 0])
        row = index // columns
        tile = (index // LANES) % (columns // LANES)
        row_ref[...] = tile * rows + row
        lane = index % LANES
        for b in range(blocks):
            hot_ref[:, b * points : (b + 1) * points] = jnp.where(
                lane_iota == lane[b : b + 1], 1.0, 0.0
            ).astype(bf16)


def regrid_kernel(n_surfaces, *refs):
    surfaces = refs[:n_surfaces]
    (
        src_hot_ref, dst_hot_ref, src_row_ref, dst_row_ref, a_count, m_count, a_weight, m_weight,
        _, _, _, _,
        *refs,
    ) = refs[n_surfaces:]
    land_ref, *sent_refs = refs[:-4]
    weight_ref, gath_ref, val_ref, sem = refs[-4:]
    is_atmos = lax.axis_index("comp") == 0
    blocks, points = val_ref.shape
    cells = surfaces[0].shape[0]

    @pl.when(is_atmos)
    def _():
        pltpu.make_async_copy(m_weight.at[0, 0], weight_ref, sem).start()

    @pl.when(jnp.logical_not(is_atmos))
    def _():
        pltpu.make_async_copy(a_weight.at[0, 0], weight_ref, sem).start()

    count = jnp.where(is_atmos, m_count[0, 0], a_count[0, 0])
    pair = 2 * points
    row_iota = lax.broadcasted_iota(jnp.int32, (cells, points), 0)
    table = sum(surface[...].astype(f32) for surface in surfaces).astype(bf16)
    for b in range(0, blocks, 2):
        picked = jnp.dot(
            table, src_hot_ref[:, b * points : b * points + pair], preferred_element_type=f32
        )
        for k in range(2):
            mine = row_iota == src_row_ref[b + k : b + k + 1, :]
            part = jnp.where(mine, picked[:, k * points : (k + 1) * points], 0.0)
            gath_ref[b + k : b + k + 1, :] = jnp.sum(part, axis=0, keepdims=True)
    gathered = gath_ref[...].astype(bf16)

    @pl.when(is_atmos)
    def _():
        pltpu.make_async_copy(m_weight.at[0, 0], weight_ref, sem).wait()

    @pl.when(jnp.logical_not(is_atmos))
    def _():
        pltpu.make_async_copy(a_weight.at[0, 0], weight_ref, sem).wait()

    block_iota = lax.broadcasted_iota(jnp.int32, (blocks, points), 0)
    values = jnp.zeros((blocks, points), f32)
    for b in range(0, blocks, 2):
        terms = lax.dot_general(
            gathered,
            weight_ref[b : b + 2].reshape(pair, points),
            (((1,), (1,)), ((), ())),
            preferred_element_type=f32,
        )
        for k in range(2):
            values = jnp.where(block_iota == b + k, terms[:, k * points : (k + 1) * points], values)
    val_ref[...] = jnp.where(block_iota < count, values, 0.0)
    land = jnp.zeros((2 * cells, LANES), f32)
    for b in range(0, blocks, 2):
        spread = []
        for k in range(b, b + 2):
            value = val_ref[k : k + 1, :]
            coarse = value.astype(bf16).astype(f32)
            fine = value - coarse
            mine = row_iota == dst_row_ref[k : k + 1, :]
            spread.append(
                jnp.concatenate(
                    [jnp.where(mine, coarse, 0.0), jnp.where(mine, fine, 0.0)], axis=0
                ).astype(bf16)
            )
        land = land + lax.dot_general(
            jnp.concatenate(spread, axis=1),
            dst_hot_ref[:, b * points : b * points + pair],
            (((1,), (1,)), ((), ())),
            preferred_element_type=f32,
        )
    land = land[:cells] + land[cells:]
    land_ref[...] = land
    for sent_ref in sent_refs:
        lengthen(sent_ref, land.astype(bf16))


def heat_kernel(rows, e2_ref, e4_ref, land_ref, _, *refs):
    parts = refs[:-3]
    sum_ref, near_ref, far_ref = refs[-3:]
    cells = land_ref.shape[0]
    columns = cells // rows * LANES
    even_x = lax.axis_index("gx") % 2 == 0
    even_y = lax.axis_index("gy") % 2 == 0
    total = land_ref[...]
    for part in parts:
        total = total + part[0:cells, :].astype(f32)
    sum_ref[...] = total

    def corners(row):
        start = row * 4 // 16 * 16
        one = e2_ref[start : start + 16, :].astype(f32)
        two = e4_ref[start : start + 16, :].astype(f32)
        low = jnp.where(even_y, two, one)
        high = jnp.where(even_y, one, two)
        at = row * 4 - start
        lines = [low[at + 1 : at + 2], low[at + 3 : at + 4], high[at : at + 1], high[at + 2 : at + 3]]
        return to_tiles(jnp.concatenate(lines + [jnp.zeros((4, columns), f32)], axis=0))

    first, last = corners(0), corners(rows - 1)
    near_ref[0:cells, :] = total.astype(bf16)
    far_ref[0:cells, :] = total.astype(bf16)
    near_ref[cells:, :] = jnp.where(even_x, last, first).astype(bf16)
    far_ref[cells:, :] = jnp.where(even_x, first, last).astype(bf16)


def advance(ref, r, t, coefs, size):
    ring, columns = ref.shape[2:]
    whole = ref[r, t]
    up = pltpu.roll(whole, 1, 0)[:size]
    down = pltpu.roll(whole, ring - 1, 0)[:size]
    mid = whole[:size]
    total = coefs[0] * mid + coefs[5] * (up + down)
    total = total + coefs[1] * ref[r - 1, t, 0:size, :]
    total = total + coefs[2] * ref[r + 1, t, 0:size, :]
    total = total + coefs[3] * pltpu.roll(mid, 1, 1)
    return total + coefs[4] * pltpu.roll(mid, columns - 1, 1)


def first_step_kernel(
    groups_x, groups_y, paired, x_ref, wet_ref, diff_ref, y_ref, e1_ref, e3_ref,
    e2_ref, e4_ref, *refs,
):
    if not paired:
        pin_ref, qin_ref = refs[:2]
    zb_ref, c_ref, t1_ref, z_ref, t0_ref, w_ref = refs[-6:]
    _, rows, channels, columns = x_ref.shape
    row_group = lax.axis_index("gx")
    col_group = lax.axis_index("gy")
    is_atmos = lax.axis_index("comp") == 0

    @pl.when(is_atmos)
    def _():
        diff = channel_column(diff_ref[...], channels, col_group * channels)
        total = rows * groups_x
        base = (row_group * rows).astype(f32)
        for group, n, parts in wave_parts(columns):
            lam, alpha, sinh = decay_terms(diff, half_rates(group, n, LANES, columns))
            scale = 1.0 / (
                2.0 * diff * sinh * (1.0 - jnp.exp(-2.0 * (total + 1) * alpha))
            )
            lows, highs = edge_factors(lam, alpha, base, total, rows)
            for part in parts:
                lanes = slice(part, part + LANES)
                if paired:
                    pin = jnp.zeros((channels, LANES), f32)
                    qin = jnp.zeros((channels, LANES), f32)
                    for mask, msg in ((1, e1_ref), (2, e2_ref), (3, e3_ref)):
                        band = row_group ^ mask
                        gap = (jnp.abs(row_group - band) - 1) * rows
                        term = jnp.exp(-gap.astype(f32) * alpha)
                        term = term * msg[0:channels, lanes].astype(f32)
                        pin = pin + jnp.where(band < row_group, term, 0.0)
                        qin = qin + jnp.where(band > row_group, term, 0.0)
                else:
                    pin = pin_ref[:, lanes]
                    qin = qin_ref[:, lanes]
                f = pin
                for r in range(rows):
                    f = lam * f + lows[r] * y_ref[r, :, lanes]
                    z_ref[r] = highs[r] * f
                g = lam * qin
                for r in reversed(range(rows)):
                    z = scale * (z_ref[r] + lows[r] * g)
                    zb_ref[r * channels : (r + 1) * channels, lanes] = z.astype(bf16)
                    g = lam * (g + highs[r] * y_ref[r, :, lanes])

    @pl.when(jnp.logical_not(is_atmos))
    def _():
        levels = channels // 2
        ring = levels + 8
        lines = 2 * channels
        first_x = row_group == 0
        last_x = row_group == groups_x - 1
        top = col_group == 0
        bottom = col_group == groups_y - 1
        even_x = row_group % 2 == 0
        even_y = col_group % 2 == 0

        one = e1_ref[lines : lines + 16, :].astype(f32)
        three = e3_ref[lines : lines + 16, :].astype(f32)
        below = jnp.where(even_x, three, one)[rows - 2 : rows]
        above = jnp.where(even_x, one, three)[0:2]
        w_ref[0:2, :] = jnp.where(first_x, 0.0, below)
        w_ref[2 : rows + 2, :] = wet_ref[...].astype(f32)
        w_ref[rows + 2 : rows + 4, :] = jnp.where(last_x, 0.0, above)

        span = rows + 2
        north = w_ref[0:span, :]
        here = w_ref[1 : span + 1, :]
        south = w_ref[2 : span + 2, :]
        west = pltpu.roll(here, 1, 1)
        east = pltpu.roll(here, columns - 1, 1)
        c_ref[0, 0:span, :] = here * (
            1.0 - 2.0 * mixing_rate - spread_rate * (north + south + west + east)
        )
        c_ref[1, 0:span, :] = spread_rate * here * north
        c_ref[2, 0:span, :] = spread_rate * here * south
        c_ref[3, 0:span, :] = spread_rate * here * west
        c_ref[4, 0:span, :] = spread_rate * here * east
        c_ref[5, 0:span, :] = mixing_rate * here
        c_ref[6, 0:span, :] = here

        one = e1_ref[0:lines, :].astype(f32)
        three = e3_ref[0:lines, :].astype(f32)
        below = jnp.where(even_x, three, one)
        above = jnp.where(even_x, one, three)
        blank = jnp.zeros((8, columns), f32)
        for k in range(2):
            for t in range(2):
                c = k * channels + t * levels
                t0_ref[k, t, 0:levels, :] = below[c : c + levels]
                t0_ref[rows + 2 + k, t, 0:levels, :] = above[c : c + levels]
                t0_ref[k, t, levels:ring, :] = blank
                t0_ref[rows + 2 + k, t, levels:ring, :] = blank
        one = e2_ref[...].astype(f32)
        two = e4_ref[...].astype(f32)
        before = jnp.where(even_y, two, one)
        after = jnp.where(even_y, one, two)
        for r in range(rows):
            for t in range(2):
                k = (r * 2 + t) * 2
                t0_ref[r + 2, t, 0:levels, :] = x_ref[0, r, t * levels : (t + 1) * levels, :]
                t0_ref[r + 2, t, levels : levels + 2, :] = after[k : k + 2]
                t0_ref[r + 2, t, ring - 2 : ring, :] = before[k : k + 2]

        def close(ref, r):
            for t in range(2):
                ref[r, t, ring - 1 : ring, :] = jnp.where(
                    top, ref[r, t, 0:1, :], ref[r, t, ring - 1 : ring, :]
                )
                ref[r, t, levels : levels + 1, :] = jnp.where(
                    bottom, ref[r, t, levels - 1 : levels, :], ref[r, t, levels : levels + 1, :]
                )

        def first(r, carry):
            coefs = [c_ref[k, pl.ds(r, 1), :] for k in range(6)]
            close(t0_ref, r + 1)
            for t in range(2):
                t1_ref[r, t] = advance(t0_ref, r + 1, t, coefs, ring)
            close(t1_ref, r)
            return carry

        lax.fori_loop(0, span, first, 0)


def second_step_kernel(gain_ref, table_ref, zb_ref, c_ref, t1_ref, base_ref, column_ref):
    rows, channels, columns = base_ref.shape
    is_atmos = lax.axis_index("comp") == 0

    @pl.when(is_atmos)
    def _():
        response = channel_column(gain_ref[...], channels, lax.axis_index("gy") * channels)
        column_ref[...] = jnp.broadcast_to(response, column_ref.shape)
        half = columns // 2
        step = 256
        for n in range(0, half, step):
            even, odd = [
                jnp.dot(
                    zb_ref[:, k * half : (k + 1) * half],
                    table_ref[k * half : (k + 1) * half, n : n + step],
                    preferred_element_type=f32,
                ).reshape(rows, channels, step)
                for k in range(2)
            ]
            base_ref[:, :, n : n + step] = even + odd
            base_ref[:, :, n + half : n + half + step] = even - odd

    @pl.when(jnp.logical_not(is_atmos))
    def _():
        levels = channels // 2

        def second(r, carry):
            coefs = [c_ref[k, pl.ds(r, 1), :] for k in range(6)]
            for t in range(2):
                c = t * levels
                base_ref[r - 1, c : c + levels, :] = advance(t1_ref, r, t, coefs, levels)
            return carry

        lax.fori_loop(1, rows + 1, second, 0)


def last_kernel(
    groups_x, groups_y, column_ref, base_ref, c_ref, sum_ref, near_ref, far_ref, out_hbm,
    out_ref, e_ref, heat_ref, sem,
):
    rows, channels, columns = out_ref.shape
    row_group = lax.axis_index("gx")
    col_group = lax.axis_index("gy")
    is_atmos = lax.axis_index("comp") == 0
    copies = [
        pltpu.make_async_copy(out_ref.at[r], out_hbm.at[0, r], sem.at[r]) for r in range(rows)
    ]

    @pl.when(is_atmos)
    def _():
        for r in range(rows):
            for k in range(columns // LANES):
                lanes = slice(k * LANES, (k + 1) * LANES)
                at = k * rows + r
                out_ref[r, :, lanes] = (
                    base_ref[r, :, lanes] + column_ref[...] * sum_ref[at : at + 1, :]
                )
            copies[r].start()

    @pl.when(jnp.logical_not(is_atmos))
    def _():
        levels = channels // 2
        cells = sum_ref.shape[0]
        even = row_group % 2 == 0
        below = jnp.where(even, far_ref[...].astype(f32), near_ref[...].astype(f32))
        above = jnp.where(even, near_ref[...].astype(f32), far_ref[...].astype(f32))

        low = from_tiles(below[cells:], 8)
        high = from_tiles(above[cells:], 8)
        by_low = c_ref[1, 1:2, :] * (c_ref[5, 0:1, :] + c_ref[5, 1:2, :])
        by_high = c_ref[2, rows : rows + 1, :] * (
            c_ref[5, rows : rows + 1, :] + c_ref[5, rows + 1 : rows + 2, :]
        )
        has_before = jnp.where(col_group > 0, 1.0, 0.0)
        has_after = jnp.where(col_group < groups_y - 1, 1.0, 0.0)

        @pl.when(col_group == 0)
        def _():
            span = rows + 2
            e_ref[0:1, :] = from_tiles(below[:cells], rows)[rows - 1 : rows]
            e_ref[1 : rows + 1, :] = from_tiles(sum_ref[...], rows)
            e_ref[rows + 1 : span, :] = from_tiles(above[:cells], rows)[0:1]
            e_ref[0:span, :] = c_ref[6, 0:span, :] * e_ref[0:span, :]
            own = slice(1, rows + 1)
            heat = e_ref[own, :]
            second = c_ref[5, own, :] * heat
            first = (c_ref[0, own, :] + 1.0) * heat + second
            first = first + c_ref[1, own, :] * e_ref[0:rows, :]
            first = first + c_ref[2, own, :] * e_ref[2 : rows + 2, :]
            first = first + c_ref[3, own, :] * pltpu.roll(heat, 1, 1)
            first = first + c_ref[4, own, :] * pltpu.roll(heat, columns - 1, 1)
            heat_ref[0] = first
            heat_ref[1] = second

        for r in [1, rows - 2] + list(range(2, rows - 2)) + [0, rows - 1]:
            out_ref[r] = base_ref[r]
            for t in range(2):
                c = t * levels
                for edge, factor, lines in ((0, by_low, low), (rows - 1, by_high, high)):
                    if r == edge:
                        out_ref[r, c : c + 1, :] = out_ref[r, c : c + 1, :] + (
                            has_before * factor * lines[t : t + 1]
                        )
                        d = c + levels - 1
                        out_ref[r, d : d + 1, :] = out_ref[r, d : d + 1, :] + (
                            has_after * factor * lines[t + 2 : t + 3]
                        )

            @pl.when(col_group == 0)
            def _():
                for t, gain in enumerate((heat_gain, salt_gain)):
                    c = t * levels
                    for k in range(2):
                        out_ref[r, c + k : c + k + 1, :] = (
                            out_ref[r, c + k : c + k + 1, :] + gain * heat_ref[k, r : r + 1, :]
                        )

            copies[r].start()

    for copy in copies:
        copy.wait()


def local(
    fields,
    wet_cells,
    flux_weight,
    variable_sea_response,
    diffusivity,
    a2o_source,
    a2o_target,
    a2o_count,
    a2o_weight,
    marine_air_input_index,
    marine_air_output_index,
    marine_air_piece_tally,
    marine_air_piece_factor,
):
    _, rows, channels, columns = fields.shape
    groups_x = lax.axis_size("gx")
    groups_y = lax.axis_size("gy")
    blocks, points = a2o_source.shape[2:]
    cells = rows * columns // LANES
    forward, inverse = fourier_tables(columns)
    flux_row = flux_weight[None, :]
    gain_row = variable_sea_response[None, :]
    diff_row = diffusivity[None, :]
    paired = groups_x == 4
    params = functools.partial(pltpu.CompilerParams, vmem_limit_bytes=40 * 2**20)
    vmem = pl.BlockSpec(memory_space=pltpu.VMEM)
    smem = pl.BlockSpec(memory_space=pltpu.SMEM)
    hbm = pl.BlockSpec(memory_space=pltpu.HBM)
    anywhere = pl.BlockSpec(memory_space=pl.ANY)

    def shape(dims, dtype):
        return jax.ShapeDtypeStruct(dims, dtype)

    lines = 2 * channels + 16
    shapes = [
        shape((cells, LANES), bf16),
        shape((cells + 16, LANES), bf16),
        shape((rows, channels, columns), f32),
        shape((lines, columns), bf16),
        shape((lines, columns), bf16),
        shape((4 * rows, columns), bf16),
        shape((4 * rows, columns), bf16),
    ]
    if not paired:
        shapes.append(shape((2, channels, columns), bf16))
    coarse, wide, y, e1, e3, e2, e4, *sums = pl.pallas_call(
        functools.partial(start_kernel, groups_x, paired),
        out_shape=shapes,
        in_specs=[hbm] * 5,
        out_specs=[hbm] * len(shapes),
        scratch_shapes=[pltpu.VMEM(out.shape, out.dtype) for out in shapes]
        + [
            pltpu.VMEM((rows, channels, columns), f32),
            pltpu.VMEM((rows, columns), jnp.int32),
            pltpu.VMEM(flux_row.shape, f32),
            pltpu.VMEM(diff_row.shape, f32),
            pltpu.VMEM(forward.shape, bf16),
            pltpu.VMEM((rows * channels, columns), bf16),
            pltpu.VMEM((rows, columns), f32),
            pltpu.VMEM((4 * rows, columns), f32),
            pltpu.VMEM((columns // 2 // LANES, 2 * rows + 1, channels, LANES), f32),
            pltpu.SemaphoreType.DMA((rows,)),
            pltpu.SemaphoreType.DMA((3,)),
            pltpu.SemaphoreType.DMA((rows + len(shapes) - 1,)),
        ],
        compiler_params=pltpu.CompilerParams(vmem_limit_bytes=58 * 2**20),
        name="surface_and_forward_or_halos",
    )(fields, wet_cells, flux_row, diff_row, forward)

    masks = [1 << bit for bit in range(groups_y.bit_length() - 1)]

    def sum_route(mask):
        return [(j, j ^ mask) for j in range(groups_y)]

    def partner_route(mask):
        return both_ways([(j, groups_y + (j ^ mask)) for j in range(groups_y)])

    surface = lax.ppermute(coarse, ("comp", "gy"), partner_route(0)).astype(f32)
    for mask in masks[:1]:
        far = lax.ppermute(wide, ("comp", "gy"), partner_route(mask))
        surface = surface + far[:cells].astype(f32)
    coarse = surface.astype(bf16)
    for mask in masks[1:-1]:
        surface = surface + lax.ppermute(coarse, "gy", sum_route(mask)).astype(f32)
        coarse = surface.astype(bf16)
    surfaces = [surface] + [
        lax.ppermute(coarse, "gy", sum_route(mask)) for mask in masks[1:][-1:]
    ]

    def ring_pairs(count, odd):
        return [(a, (a + 1) % count) for a in range(odd, count, 2)]

    def flat(comp, i, j):
        return (comp * groups_x + i) * groups_y + j

    def level_route(odd):
        pairs = []
        for i in range(groups_x):
            linked = [(a, a + 1) for a in range(odd, groups_y - 1, 2)]
            alone = set(range(groups_y)) - {j for pair in linked for j in pair}
            pairs += [(flat(1, i, a), flat(1, i, b)) for a, b in linked]
            if i % 2 == 0:
                pairs += [(flat(1, i, j), flat(1, i + 1, j)) for j in sorted(alone)]
                if odd or not paired:
                    pairs += [(flat(0, i, j), flat(0, i + 1, j)) for j in range(groups_y)]
            if paired and not odd and i < i ^ 2:
                pairs += [(flat(0, i, j), flat(0, i ^ 2, j)) for j in range(groups_y)]
        return both_ways(pairs)

    e1 = lax.ppermute(e1, "gx", both_ways(ring_pairs(groups_x, 0)))
    e3 = lax.ppermute(e3, "gx", both_ways(ring_pairs(groups_x, 1)))
    axes = ("comp", "gx", "gy")
    e2 = lax.ppermute(e2, axes, level_route(0))
    e4 = lax.ppermute(e4, axes, level_route(1))

    one_hots = pl.pallas_call(
        functools.partial(one_hot_kernel, rows, columns),
        out_shape=[
            shape((LANES, blocks * points), bf16),
            shape((LANES, blocks * points), bf16),
            shape((blocks, points), jnp.int32),
            shape((blocks, points), jnp.int32),
        ],
        in_specs=[vmem] * 4 + [anywhere],
        out_specs=[vmem] * 4,
        compiler_params=params(),
        name="one_hots",
    )(a2o_source, a2o_target, marine_air_input_index, marine_air_output_index, coarse)
    landing, *sent = pl.pallas_call(
        functools.partial(regrid_kernel, len(surfaces)),
        out_shape=[shape((cells, LANES), f32)]
        + [shape((cells + 16 * (mask - 1), LANES), bf16) for mask in range(1, groups_y)],
        in_specs=[vmem] * (len(surfaces) + 4) + [smem, smem, hbm, hbm] + [anywhere] * 4,
        out_specs=[vmem] * groups_y,
        scratch_shapes=[
            pltpu.VMEM((blocks, points, points), bf16),
            pltpu.VMEM((blocks, points), f32),
            pltpu.VMEM((blocks, points), f32),
            pltpu.SemaphoreType.DMA,
        ],
        compiler_params=params(),
        name="regrid_blocks",
    )(
        *surfaces, *one_hots, a2o_count, marine_air_piece_tally,
        a2o_weight, marine_air_piece_factor, e1, e3, e2, e4,
    )
    parts = [
        lax.ppermute(block, "gy", sum_route(mask)) for mask, block in enumerate(sent, 1)
    ]

    extra = []
    if not paired:
        p, q = jnp.moveaxis(lax.all_gather(sums[0], "gx").astype(f32), 1, 0)
        viscous = lax.dynamic_slice_in_dim(
            diffusivity, lax.axis_index("gy") * channels, channels
        )[:, None]
        rates = [half_rates(g, 0, columns // 4, columns) for g in (0, 0, 1, 1)]
        _, alpha, _ = decay_terms(viscous, jnp.concatenate(rates, axis=1))
        gap = lax.axis_index("gx") - jnp.arange(groups_x)
        decay = jnp.exp(
            -(rows * jnp.maximum(jnp.abs(gap) - 1, 0))[:, None, None] * alpha[None]
        )
        extra = [
            jnp.sum(jnp.where((gap > 0)[:, None, None], decay * p, 0.0), axis=0),
            jnp.sum(jnp.where((gap < 0)[:, None, None], decay * q, 0.0), axis=0),
        ]
    ring = channels // 2 + 8
    damped, coefs, stepped = pl.pallas_call(
        functools.partial(first_step_kernel, groups_x, groups_y, paired),
        out_shape=[
            shape((rows * channels, columns), bf16),
            shape((7, 16, columns), f32),
            shape((rows + 2, 2, ring, columns), f32),
        ],
        in_specs=[vmem] * (8 + len(extra)),
        out_specs=[vmem] * 3,
        scratch_shapes=[
            pltpu.VMEM((rows, channels, LANES), f32),
            pltpu.VMEM((rows + 4, 2, ring, columns), f32),
            pltpu.VMEM((16, columns), f32),
        ],
        compiler_params=params(),
        name="damping_or_first_step",
    )(fields, wet_cells, diff_row, y, e1, e3, e2, e4, *extra)

    surface_sum, near, far = pl.pallas_call(
        functools.partial(heat_kernel, rows),
        out_shape=[
            shape((cells, LANES), f32),
            shape((cells + columns // 16, LANES), bf16),
            shape((cells + columns // 16, LANES), bf16),
        ],
        in_specs=[vmem] * 3 + [anywhere] + [vmem] * len(parts),
        out_specs=[vmem] * 3,
        compiler_params=params(),
        name="surface_sum",
    )(e2, e4, landing, coefs, *parts)

    near = lax.ppermute(near, "gx", both_ways(ring_pairs(groups_x, 0)))
    far = lax.ppermute(far, "gx", both_ways(ring_pairs(groups_x, 1)))
    base, column = pl.pallas_call(
        second_step_kernel,
        out_shape=[shape((rows, channels, columns), f32), shape((channels, LANES), f32)],
        in_specs=[vmem] * 5,
        out_specs=[vmem] * 2,
        compiler_params=params(),
        name="inverse_or_second_step",
    )(gain_row, inverse, damped, coefs, stepped)
    return pl.pallas_call(
        functools.partial(last_kernel, groups_x, groups_y),
        out_shape=shape(fields.shape, f32),
        in_specs=[vmem] * 6,
        out_specs=hbm,
        scratch_shapes=[
            pltpu.VMEM((rows, channels, columns), f32),
            pltpu.VMEM((16, columns), f32),
            pltpu.VMEM((2, rows, columns), f32),
            pltpu.SemaphoreType.DMA((rows,)),
        ],
        compiler_params=params(),
        name="add_surface_terms",
    )(column, base, coefs, surface_sum, near, far)


def solution(mesh):
    in_specs = (
        P("comp", "gx", "gy", None),
        P("gx", None),
        P(),
        P(),
        P(),
        P("gx", "gy", None, None),
        P("gx", "gy", None, None),
        P("gx", "gy"),
        P("gx", "gy", None, None, None),
        P("gx", "gy", None, None),
        P("gx", "gy", None, None),
        P("gx", "gy"),
        P("gx", "gy", None, None, None),
    )
    out_specs = P("comp", "gx", "gy", None)
    return jax.shard_map(local, mesh=mesh, in_specs=in_specs, out_specs=out_specs, check_vma=False)
```

```python
import functools

import jax
import jax.numpy as jnp
import numpy as np
from jax import lax
from jax.experimental import pallas as pl
from jax.experimental.pallas import tpu as pltpu
from jax.sharding import PartitionSpec as P

spread_rate = 0.2
mixing_rate = 0.1
heat_gain = 0.5
salt_gain = -0.25
LANES = 128
f32 = jnp.float32
bf16 = jnp.bfloat16


def fourier_tables(columns):
    half = columns // 2
    forward, inverse = [], []
    for first in (0, 1):
        waves = np.arange(first, half, 2)
        phase = np.arange(half)[:, None] * waves[None, :] % columns
        angles = phase * (2.0 * np.pi / columns)
        table = np.concatenate([np.cos(angles), np.sin(angles)], axis=1)
        weight = np.where(waves == 0, 1.0, 2.0) / columns
        forward.append(table)
        inverse.append(table.T * np.concatenate([weight, weight])[:, None])
    return (
        jnp.asarray(np.concatenate(forward).astype(np.float32), bf16),
        jnp.asarray(np.concatenate(inverse).astype(np.float32), bf16),
    )


def wave_parts(columns):
    quarter = columns // 4
    return [
        (g, n, (g * 2 * quarter + n, (g * 2 + 1) * quarter + n))
        for g in (0, 1)
        for n in range(0, quarter, LANES)
    ]


def half_rates(group, first, count, columns):
    lane = lax.broadcasted_iota(jnp.int32, (1, count), 1) + first
    wave = (2 * lane + group).astype(f32)
    sine = jnp.sin(wave * (np.pi / columns))
    return 2.0 * sine * sine


def both_ways(pairs):
    return [p for a, b in pairs for p in ((a, b), (b, a))]


def channel_column(row, channels, first):
    n = row.shape[1]
    lane = lax.broadcasted_iota(jnp.int32, (channels, n), 1)
    sub = lax.broadcasted_iota(jnp.int32, (channels, n), 0)
    return jnp.sum(jnp.where(lane == sub + first, row, 0.0), axis=1, keepdims=True)


def to_tiles(surface):
    cols = surface.shape[1]
    return jnp.concatenate(
        [surface[:, k : k + LANES] for k in range(0, cols, LANES)], axis=0
    )


def from_tiles(tiles, rows):
    return jnp.concatenate(
        [tiles[k : k + rows] for k in range(0, tiles.shape[0], rows)], axis=1
    )


def lengthen(ref, block):
    rows = block.shape[0]
    ref[0:rows, :] = block
    if ref.shape[0] > rows:
        ref[rows:, :] = block[: ref.shape[0] - rows]


def decay_terms(diff_column, rates):
    half = 0.5 / diff_column + rates
    sinh = jnp.sqrt(half * (half + 2.0))
    grow = 1.0 + half + sinh
    return 1.0 / grow, jnp.log(grow), sinh


def edge_factors(lam, alpha, base, total, rows):
    lam2 = lam * lam
    powers = [
        jnp.exp(-2.0 * base * alpha) * lam2,
        jnp.exp(-2.0 * (total - rows - base) * alpha) * lam2,
    ]
    lows, highs = [], []
    for _ in range(rows):
        lows.append(1.0 - powers[0])
        highs.insert(0, 1.0 - powers[1])
        powers = [power * lam2 for power in powers]
    return lows, highs


def start_kernel(
    groups_x, paired, x_hbm, wet_hbm, flux_hbm, diff_hbm, table_hbm, *refs
):
    outs = 7 if paired else 8
    coarse_hbm, wide_hbm, y_hbm, *message_hbm = refs[:outs]
    coarse_ref, wide_ref, y_ref, *message_ref = refs[outs : 2 * outs]
    e1_ref, e3_ref, e2_ref, e4_ref = message_ref[:4]
    if not paired:
        pq_ref = message_ref[4]
    (
        x_ref, wet_ref, flux_ref, diff_ref, table_ref, flat_ref, row_ref, edge_ref,
        factor_ref, x_sem, sem, out_sem,
    ) = refs[2 * outs :]
    rows, channels, columns = x_ref.shape
    half = columns // 2
    row_group = lax.axis_index("gx")
    col_group = lax.axis_index("gy")
    is_atmos = lax.axis_index("comp") == 0

    x_copies = [
        pltpu.make_async_copy(x_hbm.at[0, r], x_ref.at[r], x_sem.at[r]) for r in range(rows)
    ]
    surface_copies = [
        pltpu.make_async_copy(coarse_ref, coarse_hbm, out_sem.at[0]),
        pltpu.make_async_copy(wide_ref, wide_hbm, out_sem.at[1]),
    ]
    y_copies = [
        pltpu.make_async_copy(y_ref.at[r], y_hbm.at[r], out_sem.at[2 + r]) for r in range(rows)
    ]
    message_copies = [
        pltpu.make_async_copy(ref, hbm, out_sem.at[2 + rows + k])
        for k, (ref, hbm) in enumerate(zip(message_ref, message_hbm))
    ]

    def send_surface():
        coarse = to_tiles(row_ref[...]).astype(bf16)
        coarse_ref[...] = coarse
        lengthen(wide_ref, coarse)
        for copy in surface_copies:
            copy.start()

    @pl.when(is_atmos)
    def _():
        flux_copy = pltpu.make_async_copy(flux_hbm, flux_ref, sem.at[0])
        diff_copy = pltpu.make_async_copy(diff_hbm, diff_ref, sem.at[1])
        table_copy = pltpu.make_async_copy(table_hbm, table_ref, sem.at[2])
        for copy in [flux_copy, diff_copy] + x_copies + [table_copy]:
            copy.start()
        first = col_group * channels
        flux_copy.wait()
        weight = channel_column(flux_ref[...], channels, first)
        diff_copy.wait()
        diff = channel_column(diff_ref[...], channels, first)
        total = rows * groups_x
        base = (row_group * rows).astype(f32)
        tiles = wave_parts(columns)
        for k, (group, n, _) in enumerate(tiles):
            lam, alpha, _ = decay_terms(diff, half_rates(group, n, LANES, columns))
            factor_ref[k, 0] = lam
            lows, highs = edge_factors(lam, alpha, base, total, rows)
            for r in range(rows):
                factor_ref[k, 1 + r] = lows[r]
                factor_ref[k, 1 + rows + r] = highs[r]
        for r in range(rows):
            x_copies[r].wait()
            row_ref[r : r + 1, :] = jnp.sum(x_ref[r] * weight, axis=0, keepdims=True)
            left, right = x_ref[r, :, :half], x_ref[r, :, half:]
            flat_ref[r * channels : (r + 1) * channels, :half] = (left + right).astype(bf16)
            flat_ref[r * channels : (r + 1) * channels, half:] = (left - right).astype(bf16)
        send_surface()
        table_copy.wait()
        for k in range(2):
            lanes = slice(k * half, (k + 1) * half)
            part = jnp.dot(
                flat_ref[:, lanes], table_ref[lanes, :], preferred_element_type=f32
            )
            y_ref[:, :, lanes] = part.reshape(rows, channels, half)
            for tile, (group, _, parts) in enumerate(tiles):
                if group != k:
                    continue
                lam = factor_ref[tile, 0]
                for at in parts:
                    lanes = slice(at, at + LANES)
                    here = slice(at - k * half, at - k * half + LANES)
                    p = factor_ref[tile, 1] * part[0:channels, here]
                    q = factor_ref[tile, 2 * rows] * part[(rows - 1) * channels :, here]
                    for r in range(1, rows):
                        up = part[r * channels : (r + 1) * channels, here]
                        down = part[(rows - 1 - r) * channels : (rows - r) * channels, here]
                        p = lam * p + factor_ref[tile, 1 + r] * up
                        q = lam * q + factor_ref[tile, 2 * rows - r] * down
                    if paired:
                        for mask, out in ((1, e1_ref), (2, e2_ref), (3, e3_ref)):
                            upward = row_group < (row_group ^ mask)
                            out[0:channels, lanes] = jnp.where(upward, p, q).astype(bf16)
                    else:
                        pq_ref[0, :, lanes] = p.astype(bf16)
                        pq_ref[1, :, lanes] = q.astype(bf16)
        for copy in y_copies:
            copy.start()
        for copy in message_copies:
            copy.start()
        for copy in surface_copies + y_copies + message_copies:
            copy.wait()

    @pl.when(jnp.logical_not(is_atmos))
    def _():
        wet_copy = pltpu.make_async_copy(wet_hbm, wet_ref, sem.at[0])
        for copy in x_copies + [wet_copy]:
            copy.start()
        gain = jnp.where(col_group == 0, 1.0, 0.0)
        for r in range(rows):
            x_copies[r].wait()
            row_ref[r : r + 1, :] = x_ref[r, 0:1, :] * gain
        send_surface()
        wet_copy.wait()
        levels = channels // 2
        lines = 2 * channels
        even_x = row_group % 2 == 0
        even_y = col_group % 2 == 0
        wet = wet_ref[...].astype(f32)
        wet = jnp.concatenate([wet, wet], axis=0).astype(bf16)

        def put(out, last):
            @pl.when(last)
            def _():
                out[0:lines, :] = x_ref[rows - 2 :].reshape(lines, columns).astype(bf16)

            @pl.when(jnp.logical_not(last))
            def _():
                out[0:lines, :] = x_ref[:2].reshape(lines, columns).astype(bf16)

            out[lines : lines + 16, :] = wet

        put(e1_ref, even_x)
        put(e3_ref, jnp.logical_not(even_x))

        def put_edges(out, level):
            for r in range(rows):
                for t in range(2):
                    at = (r * 2 + t) * 2
                    c = t * levels + level
                    edge_ref[at : at + 2, :] = x_ref[r, c : c + 2, :]
            out[...] = edge_ref[...].astype(bf16)

        @pl.when(even_y)
        def _():
            put_edges(e2_ref, levels - 2)
            put_edges(e4_ref, 0)

        @pl.when(jnp.logical_not(even_y))
        def _():
            put_edges(e2_ref, 0)
            put_edges(e4_ref, levels - 2)

        for copy in message_copies:
            copy.start()
        for copy in surface_copies + message_copies:
            copy.wait()


def one_hot_kernel(
    rows, columns, a_src, a_dst, m_src, m_dst, _, src_hot_ref, dst_hot_ref, src_row_ref, dst_row_ref
):
    is_atmos = lax.axis_index("comp") == 0
    blocks, points = src_row_ref.shape
    lane_iota = lax.broadcasted_iota(jnp.int32, (LANES, points), 0)
    for a_ref, m_ref, hot_ref, row_ref in (
        (a_src, m_src, src_hot_ref, src_row_ref),
        (a_dst, m_dst, dst_hot_ref, dst_row_ref),
    ):
        index = jnp.where(is_atmos, m_ref[0, 0], a_ref[0, 0])
        row = index // columns
        tile = (index // LANES) % (columns // LANES)
        row_ref[...] = tile * rows + row
        lane = index % LANES
        for b in range(blocks):
            hot_ref[:, b * points : (b + 1) * points] = jnp.where(
                lane_iota == lane[b : b + 1], 1.0, 0.0
            ).astype(bf16)


def regrid_kernel(n_surfaces, *refs):
    surfaces = refs[:n_surfaces]
    (
        src_hot_ref, dst_hot_ref, src_row_ref, dst_row_ref, a_count, m_count, a_weight, m_weight,
        _, _, _,
        *refs,
    ) = refs[n_surfaces:]
    land_ref, *sent_refs = refs[:-4]
    weight_ref, gath_ref, val_ref, sem = refs[-4:]
    is_atmos = lax.axis_index("comp") == 0
    blocks, points = val_ref.shape
    cells = surfaces[0].shape[0]

    @pl.when(is_atmos)
    def _():
        pltpu.make_async_copy(m_weight.at[0, 0], weight_ref, sem).start()

    @pl.when(jnp.logical_not(is_atmos))
    def _():
        pltpu.make_async_copy(a_weight.at[0, 0], weight_ref, sem).start()

    count = jnp.where(is_atmos, m_count[0, 0], a_count[0, 0])
    pair = 2 * points
    row_iota = lax.broadcasted_iota(jnp.int32, (cells, points), 0)
    table = sum(surface[...].astype(f32) for surface in surfaces).astype(bf16)
    for b in range(0, blocks, 2):
        picked = jnp.dot(
            table, src_hot_ref[:, b * points : b * points + pair], preferred_element_type=f32
        )
        for k in range(2):
            mine = row_iota == src_row_ref[b + k : b + k + 1, :]
            part = jnp.where(mine, picked[:, k * points : (k + 1) * points], 0.0)
            gath_ref[b + k : b + k + 1, :] = jnp.sum(part, axis=0, keepdims=True)
    gathered = gath_ref[...].astype(bf16)

    @pl.when(is_atmos)
    def _():
        pltpu.make_async_copy(m_weight.at[0, 0], weight_ref, sem).wait()

    @pl.when(jnp.logical_not(is_atmos))
    def _():
        pltpu.make_async_copy(a_weight.at[0, 0], weight_ref, sem).wait()

    block_iota = lax.broadcasted_iota(jnp.int32, (blocks, points), 0)
    values = jnp.zeros((blocks, points), f32)
    for b in range(0, blocks, 2):
        terms = lax.dot_general(
            gathered,
            weight_ref[b : b + 2].reshape(pair, points),
            (((1,), (1,)), ((), ())),
            preferred_element_type=f32,
        )
        for k in range(2):
            values = jnp.where(block_iota == b + k, terms[:, k * points : (k + 1) * points], values)
    val_ref[...] = jnp.where(block_iota < count, values, 0.0)
    land = jnp.zeros((2 * cells, LANES), f32)
    for b in range(0, blocks, 2):
        spread = []
        for k in range(b, b + 2):
            value = val_ref[k : k + 1, :]
            coarse = value.astype(bf16).astype(f32)
            fine = value - coarse
            mine = row_iota == dst_row_ref[k : k + 1, :]
            spread.append(
                jnp.concatenate(
                    [jnp.where(mine, coarse, 0.0), jnp.where(mine, fine, 0.0)], axis=0
                ).astype(bf16)
            )
        land = land + lax.dot_general(
            jnp.concatenate(spread, axis=1),
            dst_hot_ref[:, b * points : b * points + pair],
            (((1,), (1,)), ((), ())),
            preferred_element_type=f32,
        )
    land = land[:cells] + land[cells:]
    land_ref[...] = land
    for sent_ref in sent_refs:
        lengthen(sent_ref, land.astype(bf16))


def heat_kernel(rows, e2_ref, e4_ref, land_ref, _, *refs):
    parts = refs[:-3]
    sum_ref, near_ref, far_ref = refs[-3:]
    cells = land_ref.shape[0]
    columns = cells // rows * LANES
    even_x = lax.axis_index("gx") % 2 == 0
    even_y = lax.axis_index("gy") % 2 == 0
    total = land_ref[...]
    for part in parts:
        total = total + part[0:cells, :].astype(f32)
    sum_ref[...] = total

    def corners(row):
        start = row * 4 // 16 * 16
        one = e2_ref[start : start + 16, :].astype(f32)
        two = e4_ref[start : start + 16, :].astype(f32)
        low = jnp.where(even_y, two, one)
        high = jnp.where(even_y, one, two)
        at = row * 4 - start
        lines = [low[at + 1 : at + 2], low[at + 3 : at + 4], high[at : at + 1], high[at + 2 : at + 3]]
        return to_tiles(jnp.concatenate(lines + [jnp.zeros((4, columns), f32)], axis=0))

    first, last = corners(0), corners(rows - 1)
    near_ref[0:cells, :] = total.astype(bf16)
    far_ref[0:cells, :] = total.astype(bf16)
    near_ref[cells:, :] = jnp.where(even_x, last, first).astype(bf16)
    far_ref[cells:, :] = jnp.where(even_x, first, last).astype(bf16)


def advance(ref, r, t, coefs, size):
    ring, columns = ref.shape[2:]
    whole = ref[r, t]
    up = pltpu.roll(whole, 1, 0)[:size]
    down = pltpu.roll(whole, ring - 1, 0)[:size]
    mid = whole[:size]
    total = coefs[0] * mid + coefs[5] * (up + down)
    total = total + coefs[1] * ref[r - 1, t, 0:size, :]
    total = total + coefs[2] * ref[r + 1, t, 0:size, :]
    total = total + coefs[3] * pltpu.roll(mid, 1, 1)
    return total + coefs[4] * pltpu.roll(mid, columns - 1, 1)


def first_step_kernel(
    groups_x, groups_y, paired, x_ref, wet_ref, diff_ref, y_ref, e1_ref, e3_ref,
    e2_ref, e4_ref, *refs,
):
    if not paired:
        pin_ref, qin_ref = refs[:2]
    zb_ref, c_ref, t1_ref, z_ref, t0_ref, w_ref = refs[-6:]
    _, rows, channels, columns = x_ref.shape
    row_group = lax.axis_index("gx")
    col_group = lax.axis_index("gy")
    is_atmos = lax.axis_index("comp") == 0

    @pl.when(is_atmos)
    def _():
        diff = channel_column(diff_ref[...], channels, col_group * channels)
        total = rows * groups_x
        base = (row_group * rows).astype(f32)
        for group, n, parts in wave_parts(columns):
            lam, alpha, sinh = decay_terms(diff, half_rates(group, n, LANES, columns))
            scale = 1.0 / (
                2.0 * diff * sinh * (1.0 - jnp.exp(-2.0 * (total + 1) * alpha))
            )
            lows, highs = edge_factors(lam, alpha, base, total, rows)
            for part in parts:
                lanes = slice(part, part + LANES)
                if paired:
                    pin = jnp.zeros((channels, LANES), f32)
                    qin = jnp.zeros((channels, LANES), f32)
                    for mask, msg in ((1, e1_ref), (2, e2_ref), (3, e3_ref)):
                        band = row_group ^ mask
                        gap = (jnp.abs(row_group - band) - 1) * rows
                        term = jnp.exp(-gap.astype(f32) * alpha)
                        term = term * msg[0:channels, lanes].astype(f32)
                        pin = pin + jnp.where(band < row_group, term, 0.0)
                        qin = qin + jnp.where(band > row_group, term, 0.0)
                else:
                    pin = pin_ref[:, lanes]
                    qin = qin_ref[:, lanes]
                f = pin
                for r in range(rows):
                    f = lam * f + lows[r] * y_ref[r, :, lanes]
                    z_ref[r] = highs[r] * f
                g = lam * qin
                for r in reversed(range(rows)):
                    z = scale * (z_ref[r] + lows[r] * g)
                    zb_ref[r * channels : (r + 1) * channels, lanes] = z.astype(bf16)
                    g = lam * (g + highs[r] * y_ref[r, :, lanes])

    @pl.when(jnp.logical_not(is_atmos))
    def _():
        levels = channels // 2
        ring = levels + 8
        lines = 2 * channels
        first_x = row_group == 0
        last_x = row_group == groups_x - 1
        top = col_group == 0
        bottom = col_group == groups_y - 1
        even_x = row_group % 2 == 0
        even_y = col_group % 2 == 0

        one = e1_ref[lines : lines + 16, :].astype(f32)
        three = e3_ref[lines : lines + 16, :].astype(f32)
        below = jnp.where(even_x, three, one)[rows - 2 : rows]
        above = jnp.where(even_x, one, three)[0:2]
        w_ref[0:2, :] = jnp.where(first_x, 0.0, below)
        w_ref[2 : rows + 2, :] = wet_ref[...].astype(f32)
        w_ref[rows + 2 : rows + 4, :] = jnp.where(last_x, 0.0, above)

        span = rows + 2
        north = w_ref[0:span, :]
        here = w_ref[1 : span + 1, :]
        south = w_ref[2 : span + 2, :]
        west = pltpu.roll(here, 1, 1)
        east = pltpu.roll(here, columns - 1, 1)
        c_ref[0, 0:span, :] = here * (
            1.0 - 2.0 * mixing_rate - spread_rate * (north + south + west + east)
        )
        c_ref[1, 0:span, :] = spread_rate * here * north
        c_ref[2, 0:span, :] = spread_rate * here * south
        c_ref[3, 0:span, :] = spread_rate * here * west
        c_ref[4, 0:span, :] = spread_rate * here * east
        c_ref[5, 0:span, :] = mixing_rate * here
        c_ref[6, 0:span, :] = here

        one = e1_ref[0:lines, :].astype(f32)
        three = e3_ref[0:lines, :].astype(f32)
        below = jnp.where(even_x, three, one)
        above = jnp.where(even_x, one, three)
        blank = jnp.zeros((8, columns), f32)
        for k in range(2):
            for t in range(2):
                c = k * channels + t * levels
                t0_ref[k, t, 0:levels, :] = below[c : c + levels]
                t0_ref[rows + 2 + k, t, 0:levels, :] = above[c : c + levels]
                t0_ref[k, t, levels:ring, :] = blank
                t0_ref[rows + 2 + k, t, levels:ring, :] = blank
        one = e2_ref[...].astype(f32)
        two = e4_ref[...].astype(f32)
        before = jnp.where(even_y, two, one)
        after = jnp.where(even_y, one, two)
        for r in range(rows):
            for t in range(2):
                k = (r * 2 + t) * 2
                t0_ref[r + 2, t, 0:levels, :] = x_ref[0, r, t * levels : (t + 1) * levels, :]
                t0_ref[r + 2, t, levels : levels + 2, :] = after[k : k + 2]
                t0_ref[r + 2, t, ring - 2 : ring, :] = before[k : k + 2]

        def close(ref, r):
            for t in range(2):
                ref[r, t, ring - 1 : ring, :] = jnp.where(
                    top, ref[r, t, 0:1, :], ref[r, t, ring - 1 : ring, :]
                )
                ref[r, t, levels : levels + 1, :] = jnp.where(
                    bottom, ref[r, t, levels - 1 : levels, :], ref[r, t, levels : levels + 1, :]
                )

        def first(r, carry):
            coefs = [c_ref[k, pl.ds(r, 1), :] for k in range(6)]
            close(t0_ref, r + 1)
            for t in range(2):
                t1_ref[r, t] = advance(t0_ref, r + 1, t, coefs, ring)
            close(t1_ref, r)
            return carry

        lax.fori_loop(0, span, first, 0)


def second_step_kernel(gain_ref, table_ref, zb_ref, c_ref, t1_ref, base_ref, column_ref):
    rows, channels, columns = base_ref.shape
    is_atmos = lax.axis_index("comp") == 0

    @pl.when(is_atmos)
    def _():
        response = channel_column(gain_ref[...], channels, lax.axis_index("gy") * channels)
        column_ref[...] = jnp.broadcast_to(response, column_ref.shape)
        half = columns // 2
        step = 256
        for n in range(0, half, step):
            even, odd = [
                jnp.dot(
                    zb_ref[:, k * half : (k + 1) * half],
                    table_ref[k * half : (k + 1) * half, n : n + step],
                    preferred_element_type=f32,
                ).reshape(rows, channels, step)
                for k in range(2)
            ]
            base_ref[:, :, n : n + step] = even + odd
            base_ref[:, :, n + half : n + half + step] = even - odd

    @pl.when(jnp.logical_not(is_atmos))
    def _():
        levels = channels // 2

        def second(r, carry):
            coefs = [c_ref[k, pl.ds(r, 1), :] for k in range(6)]
            for t in range(2):
                c = t * levels
                base_ref[r - 1, c : c + levels, :] = advance(t1_ref, r, t, coefs, levels)
            return carry

        lax.fori_loop(1, rows + 1, second, 0)


def last_kernel(
    groups_x, groups_y, column_ref, base_ref, c_ref, sum_ref, near_ref, far_ref, out_hbm,
    out_ref, e_ref, heat_ref, sem,
):
    rows, channels, columns = out_ref.shape
    row_group = lax.axis_index("gx")
    col_group = lax.axis_index("gy")
    is_atmos = lax.axis_index("comp") == 0
    copies = [
        pltpu.make_async_copy(out_ref.at[r], out_hbm.at[0, r], sem.at[r]) for r in range(rows)
    ]

    @pl.when(is_atmos)
    def _():
        for r in range(rows):
            for k in range(columns // LANES):
                lanes = slice(k * LANES, (k + 1) * LANES)
                at = k * rows + r
                out_ref[r, :, lanes] = (
                    base_ref[r, :, lanes] + column_ref[...] * sum_ref[at : at + 1, :]
                )
            copies[r].start()

    @pl.when(jnp.logical_not(is_atmos))
    def _():
        levels = channels // 2
        cells = sum_ref.shape[0]
        even = row_group % 2 == 0
        below = jnp.where(even, far_ref[...].astype(f32), near_ref[...].astype(f32))
        above = jnp.where(even, near_ref[...].astype(f32), far_ref[...].astype(f32))

        low = from_tiles(below[cells:], 8)
        high = from_tiles(above[cells:], 8)
        by_low = c_ref[1, 1:2, :] * (c_ref[5, 0:1, :] + c_ref[5, 1:2, :])
        by_high = c_ref[2, rows : rows + 1, :] * (
            c_ref[5, rows : rows + 1, :] + c_ref[5, rows + 1 : rows + 2, :]
        )
        has_before = jnp.where(col_group > 0, 1.0, 0.0)
        has_after = jnp.where(col_group < groups_y - 1, 1.0, 0.0)

        @pl.when(col_group == 0)
        def _():
            span = rows + 2
            e_ref[0:1, :] = from_tiles(below[:cells], rows)[rows - 1 : rows]
            e_ref[1 : rows + 1, :] = from_tiles(sum_ref[...], rows)
            e_ref[rows + 1 : span, :] = from_tiles(above[:cells], rows)[0:1]
            e_ref[0:span, :] = c_ref[6, 0:span, :] * e_ref[0:span, :]
            own = slice(1, rows + 1)
            heat = e_ref[own, :]
            second = c_ref[5, own, :] * heat
            first = (c_ref[0, own, :] + 1.0) * heat + second
            first = first + c_ref[1, own, :] * e_ref[0:rows, :]
            first = first + c_ref[2, own, :] * e_ref[2 : rows + 2, :]
            first = first + c_ref[3, own, :] * pltpu.roll(heat, 1, 1)
            first = first + c_ref[4, own, :] * pltpu.roll(heat, columns - 1, 1)
            heat_ref[0] = first
            heat_ref[1] = second

        for r in [1, rows - 2] + list(range(2, rows - 2)) + [0, rows - 1]:
            out_ref[r] = base_ref[r]
            for t in range(2):
                c = t * levels
                for edge, factor, lines in ((0, by_low, low), (rows - 1, by_high, high)):
                    if r == edge:
                        out_ref[r, c : c + 1, :] = out_ref[r, c : c + 1, :] + (
                            has_before * factor * lines[t : t + 1]
                        )
                        d = c + levels - 1
                        out_ref[r, d : d + 1, :] = out_ref[r, d : d + 1, :] + (
                            has_after * factor * lines[t + 2 : t + 3]
                        )

            @pl.when(col_group == 0)
            def _():
                for t, gain in enumerate((heat_gain, salt_gain)):
                    c = t * levels
                    for k in range(2):
                        out_ref[r, c + k : c + k + 1, :] = (
                            out_ref[r, c + k : c + k + 1, :] + gain * heat_ref[k, r : r + 1, :]
                        )

            copies[r].start()

    for copy in copies:
        copy.wait()


def local(
    fields,
    wet_cells,
    flux_weight,
    variable_sea_response,
    diffusivity,
    a2o_source,
    a2o_target,
    a2o_count,
    a2o_weight,
    marine_air_input_index,
    marine_air_output_index,
    marine_air_piece_tally,
    marine_air_piece_factor,
):
    _, rows, channels, columns = fields.shape
    groups_x = lax.axis_size("gx")
    groups_y = lax.axis_size("gy")
    blocks, points = a2o_source.shape[2:]
    cells = rows * columns // LANES
    forward, inverse = fourier_tables(columns)
    flux_row = flux_weight[None, :]
    gain_row = variable_sea_response[None, :]
    diff_row = diffusivity[None, :]
    paired = groups_x == 4
    params = functools.partial(pltpu.CompilerParams, vmem_limit_bytes=40 * 2**20)
    vmem = pl.BlockSpec(memory_space=pltpu.VMEM)
    smem = pl.BlockSpec(memory_space=pltpu.SMEM)
    hbm = pl.BlockSpec(memory_space=pltpu.HBM)
    anywhere = pl.BlockSpec(memory_space=pl.ANY)

    def shape(dims, dtype):
        return jax.ShapeDtypeStruct(dims, dtype)

    lines = 2 * channels + 16
    shapes = [
        shape((cells, LANES), bf16),
        shape((cells + 16, LANES), bf16),
        shape((rows, channels, columns), f32),
        shape((lines, columns), bf16),
        shape((lines, columns), bf16),
        shape((4 * rows, columns), bf16),
        shape((4 * rows, columns), bf16),
    ]
    if not paired:
        shapes.append(shape((2, channels, columns), bf16))
    coarse, wide, y, e1, e3, e2, e4, *sums = pl.pallas_call(
        functools.partial(start_kernel, groups_x, paired),
        out_shape=shapes,
        in_specs=[hbm] * 5,
        out_specs=[hbm] * len(shapes),
        scratch_shapes=[pltpu.VMEM(out.shape, out.dtype) for out in shapes]
        + [
            pltpu.VMEM((rows, channels, columns), f32),
            pltpu.VMEM((rows, columns), jnp.int32),
            pltpu.VMEM(flux_row.shape, f32),
            pltpu.VMEM(diff_row.shape, f32),
            pltpu.VMEM(forward.shape, bf16),
            pltpu.VMEM((rows * channels, columns), bf16),
            pltpu.VMEM((rows, columns), f32),
            pltpu.VMEM((4 * rows, columns), f32),
            pltpu.VMEM((columns // 2 // LANES, 2 * rows + 1, channels, LANES), f32),
            pltpu.SemaphoreType.DMA((rows,)),
            pltpu.SemaphoreType.DMA((3,)),
            pltpu.SemaphoreType.DMA((rows + len(shapes) - 1,)),
        ],
        compiler_params=pltpu.CompilerParams(vmem_limit_bytes=58 * 2**20),
        name="surface_and_forward_or_halos",
    )(fields, wet_cells, flux_row, diff_row, forward)

    masks = [1 << bit for bit in range(groups_y.bit_length() - 1)]

    def sum_route(mask):
        return [(j, j ^ mask) for j in range(groups_y)]

    def partner_route(mask):
        return both_ways([(j, groups_y + (j ^ mask)) for j in range(groups_y)])

    surface = lax.ppermute(coarse, ("comp", "gy"), partner_route(0)).astype(f32)
    for mask in masks[:1]:
        far = lax.ppermute(wide, ("comp", "gy"), partner_route(mask))
        surface = surface + far[:cells].astype(f32)
    coarse = surface.astype(bf16)
    for mask in masks[1:-1]:
        surface = surface + lax.ppermute(coarse, "gy", sum_route(mask)).astype(f32)
        coarse = surface.astype(bf16)
    surfaces = [surface] + [
        lax.ppermute(coarse, "gy", sum_route(mask)) for mask in masks[1:][-1:]
    ]

    def ring_pairs(count, odd):
        return [(a, (a + 1) % count) for a in range(odd, count, 2)]

    def flat(comp, i, j):
        return (comp * groups_x + i) * groups_y + j

    def level_route(odd):
        pairs = []
        for i in range(groups_x):
            linked = [(a, a + 1) for a in range(odd, groups_y - 1, 2)]
            alone = set(range(groups_y)) - {j for pair in linked for j in pair}
            pairs += [(flat(1, i, a), flat(1, i, b)) for a, b in linked]
            if i % 2 == 0:
                pairs += [(flat(1, i, j), flat(1, i + 1, j)) for j in sorted(alone)]
                if odd or not paired:
                    pairs += [(flat(0, i, j), flat(0, i + 1, j)) for j in range(groups_y)]
            if paired and not odd and i < i ^ 2:
                pairs += [(flat(0, i, j), flat(0, i ^ 2, j)) for j in range(groups_y)]
        return both_ways(pairs)

    e1 = lax.ppermute(e1, "gx", both_ways(ring_pairs(groups_x, 0)))
    e3 = lax.ppermute(e3, "gx", both_ways(ring_pairs(groups_x, 1)))
    axes = ("comp", "gx", "gy")
    e2 = lax.ppermute(e2, axes, level_route(0))

    *one_hots, dst_row = pl.pallas_call(
        functools.partial(one_hot_kernel, rows, columns),
        out_shape=[
            shape((LANES, blocks * points), bf16),
            shape((LANES, blocks * points), bf16),
            shape((blocks, points), jnp.int32),
            shape((blocks, points), jnp.int32),
        ],
        in_specs=[vmem] * 4 + [anywhere],
        out_specs=[vmem] * 4,
        compiler_params=params(),
        name="one_hots",
    )(a2o_source, a2o_target, marine_air_input_index, marine_air_output_index, coarse)
    e4, dst_row = lax.optimization_barrier((e4, dst_row))
    e4 = lax.ppermute(e4, axes, level_route(1))
    landing, *sent = pl.pallas_call(
        functools.partial(regrid_kernel, len(surfaces)),
        out_shape=[shape((cells, LANES), f32)]
        + [shape((cells + 16 * (mask - 1), LANES), bf16) for mask in range(1, groups_y)],
        in_specs=[vmem] * (len(surfaces) + 4) + [smem, smem, hbm, hbm] + [anywhere] * 3,
        out_specs=[vmem] * groups_y,
        scratch_shapes=[
            pltpu.VMEM((blocks, points, points), bf16),
            pltpu.VMEM((blocks, points), f32),
            pltpu.VMEM((blocks, points), f32),
            pltpu.SemaphoreType.DMA,
        ],
        compiler_params=params(),
        name="regrid_blocks",
    )(
        *surfaces, *one_hots, dst_row, a2o_count, marine_air_piece_tally,
        a2o_weight, marine_air_piece_factor, e1, e3, e2,
    )
    parts = [
        lax.ppermute(block, "gy", sum_route(mask)) for mask, block in enumerate(sent, 1)
    ]

    extra = []
    if not paired:
        p, q = jnp.moveaxis(lax.all_gather(sums[0], "gx").astype(f32), 1, 0)
        viscous = lax.dynamic_slice_in_dim(
            diffusivity, lax.axis_index("gy") * channels, channels
        )[:, None]
        rates = [half_rates(g, 0, columns // 4, columns) for g in (0, 0, 1, 1)]
        _, alpha, _ = decay_terms(viscous, jnp.concatenate(rates, axis=1))
        gap = lax.axis_index("gx") - jnp.arange(groups_x)
        decay = jnp.exp(
            -(rows * jnp.maximum(jnp.abs(gap) - 1, 0))[:, None, None] * alpha[None]
        )
        extra = [
            jnp.sum(jnp.where((gap > 0)[:, None, None], decay * p, 0.0), axis=0),
            jnp.sum(jnp.where((gap < 0)[:, None, None], decay * q, 0.0), axis=0),
        ]
    ring = channels // 2 + 8
    damped, coefs, stepped = pl.pallas_call(
        functools.partial(first_step_kernel, groups_x, groups_y, paired),
        out_shape=[
            shape((rows * channels, columns), bf16),
            shape((7, 16, columns), f32),
            shape((rows + 2, 2, ring, columns), f32),
        ],
        in_specs=[vmem] * (8 + len(extra)),
        out_specs=[vmem] * 3,
        scratch_shapes=[
            pltpu.VMEM((rows, channels, LANES), f32),
            pltpu.VMEM((rows + 4, 2, ring, columns), f32),
            pltpu.VMEM((16, columns), f32),
        ],
        compiler_params=params(),
        name="damping_or_first_step",
    )(fields, wet_cells, diff_row, y, e1, e3, e2, e4, *extra)

    surface_sum, near, far = pl.pallas_call(
        functools.partial(heat_kernel, rows),
        out_shape=[
            shape((cells, LANES), f32),
            shape((cells + columns // 16, LANES), bf16),
            shape((cells + columns // 16, LANES), bf16),
        ],
        in_specs=[vmem] * 3 + [anywhere] + [vmem] * len(parts),
        out_specs=[vmem] * 3,
        compiler_params=params(),
        name="surface_sum",
    )(e2, e4, landing, coefs, *parts)

    near = lax.ppermute(near, "gx", both_ways(ring_pairs(groups_x, 0)))
    far = lax.ppermute(far, "gx", both_ways(ring_pairs(groups_x, 1)))
    base, column = pl.pallas_call(
        second_step_kernel,
        out_shape=[shape((rows, channels, columns), f32), shape((channels, LANES), f32)],
        in_specs=[vmem] * 5,
        out_specs=[vmem] * 2,
        compiler_params=params(),
        name="inverse_or_second_step",
    )(gain_row, inverse, damped, coefs, stepped)
    return pl.pallas_call(
        functools.partial(last_kernel, groups_x, groups_y),
        out_shape=shape(fields.shape, f32),
        in_specs=[vmem] * 6,
        out_specs=hbm,
        scratch_shapes=[
            pltpu.VMEM((rows, channels, columns), f32),
            pltpu.VMEM((16, columns), f32),
            pltpu.VMEM((2, rows, columns), f32),
            pltpu.SemaphoreType.DMA((rows,)),
        ],
        compiler_params=params(),
        name="add_surface_terms",
    )(column, base, coefs, surface_sum, near, far)


def solution(mesh):
    in_specs = (
        P("comp", "gx", "gy", None),
        P("gx", None),
        P(),
        P(),
        P(),
        P("gx", "gy", None, None),
        P("gx", "gy", None, None),
        P("gx", "gy"),
        P("gx", "gy", None, None, None),
        P("gx", "gy", None, None),
        P("gx", "gy", None, None),
        P("gx", "gy"),
        P("gx", "gy", None, None, None),
    )
    out_specs = P("comp", "gx", "gy", None)
    return jax.shard_map(local, mesh=mesh, in_specs=in_specs, out_specs=out_specs, check_vma=False)
```

```python
import functools

import jax
import jax.numpy as jnp
import numpy as np
from jax import lax
from jax.experimental import pallas as pl
from jax.experimental.pallas import tpu as pltpu
from jax.sharding import PartitionSpec as P

spread_rate = 0.2
mixing_rate = 0.1
heat_gain = 0.5
salt_gain = -0.25
LANES = 128
f32 = jnp.float32
bf16 = jnp.bfloat16


def fourier_tables(columns):
    half = columns // 2
    forward, inverse = [], []
    for first in (0, 1):
        waves = np.arange(first, half, 2)
        phase = np.arange(half)[:, None] * waves[None, :] % columns
        angles = phase * (2.0 * np.pi / columns)
        table = np.concatenate([np.cos(angles), np.sin(angles)], axis=1)
        weight = np.where(waves == 0, 1.0, 2.0) / columns
        forward.append(table)
        inverse.append(table.T * np.concatenate([weight, weight])[:, None])
    return (
        jnp.asarray(np.concatenate(forward).astype(np.float32), bf16),
        jnp.asarray(np.concatenate(inverse).astype(np.float32), bf16),
    )


def wave_parts(columns):
    quarter = columns // 4
    return [
        (g, n, (g * 2 * quarter + n, (g * 2 + 1) * quarter + n))
        for g in (0, 1)
        for n in range(0, quarter, LANES)
    ]


def half_rates(group, first, count, columns):
    lane = lax.broadcasted_iota(jnp.int32, (1, count), 1) + first
    wave = (2 * lane + group).astype(f32)
    sine = jnp.sin(wave * (np.pi / columns))
    return 2.0 * sine * sine


def both_ways(pairs):
    return [p for a, b in pairs for p in ((a, b), (b, a))]


def channel_column(row, channels, first):
    n = row.shape[1]
    lane = lax.broadcasted_iota(jnp.int32, (channels, n), 1)
    sub = lax.broadcasted_iota(jnp.int32, (channels, n), 0)
    return jnp.sum(jnp.where(lane == sub + first, row, 0.0), axis=1, keepdims=True)


def to_tiles(surface):
    cols = surface.shape[1]
    return jnp.concatenate(
        [surface[:, k : k + LANES] for k in range(0, cols, LANES)], axis=0
    )


def from_tiles(tiles, rows):
    return jnp.concatenate(
        [tiles[k : k + rows] for k in range(0, tiles.shape[0], rows)], axis=1
    )


def lengthen(ref, block):
    rows = block.shape[0]
    ref[0:rows, :] = block
    if ref.shape[0] > rows:
        ref[rows:, :] = block[: ref.shape[0] - rows]


def decay_terms(diff_column, rates):
    half = 0.5 / diff_column + rates
    sinh = jnp.sqrt(half * (half + 2.0))
    grow = 1.0 + half + sinh
    return 1.0 / grow, jnp.log(grow), sinh


def edge_factors(lam, alpha, base, total, rows):
    lam2 = lam * lam
    powers = [
        jnp.exp(-2.0 * base * alpha) * lam2,
        jnp.exp(-2.0 * (total - rows - base) * alpha) * lam2,
    ]
    lows, highs = [], []
    for _ in range(rows):
        lows.append(1.0 - powers[0])
        highs.insert(0, 1.0 - powers[1])
        powers = [power * lam2 for power in powers]
    return lows, highs


def start_kernel(
    groups_x, paired, x_hbm, wet_hbm, flux_hbm, diff_hbm, table_hbm, *refs
):
    outs = 7 if paired else 8
    coarse_hbm, wide_hbm, y_hbm, *message_hbm = refs[:outs]
    coarse_ref, wide_ref, y_ref, *message_ref = refs[outs : 2 * outs]
    e1_ref, e3_ref, e2_ref, e4_ref = message_ref[:4]
    if not paired:
        pq_ref = message_ref[4]
    (
        x_ref, wet_ref, flux_ref, diff_ref, table_ref, flat_ref, row_ref, edge_ref,
        factor_ref, x_sem, sem, out_sem,
    ) = refs[2 * outs :]
    rows, channels, columns = x_ref.shape
    half = columns // 2
    row_group = lax.axis_index("gx")
    col_group = lax.axis_index("gy")
    is_atmos = lax.axis_index("comp") == 0

    x_copies = [
        pltpu.make_async_copy(x_hbm.at[0, r], x_ref.at[r], x_sem.at[r]) for r in range(rows)
    ]
    surface_copies = [
        pltpu.make_async_copy(coarse_ref, coarse_hbm, out_sem.at[0]),
        pltpu.make_async_copy(wide_ref, wide_hbm, out_sem.at[1]),
    ]
    y_copies = [
        pltpu.make_async_copy(y_ref.at[r], y_hbm.at[r], out_sem.at[2 + r]) for r in range(rows)
    ]
    message_copies = [
        pltpu.make_async_copy(ref, hbm, out_sem.at[2 + rows + k])
        for k, (ref, hbm) in enumerate(zip(message_ref, message_hbm))
    ]

    def send_surface():
        coarse = to_tiles(row_ref[...]).astype(bf16)
        coarse_ref[...] = coarse
        lengthen(wide_ref, coarse)
        for copy in surface_copies:
            copy.start()

    @pl.when(is_atmos)
    def _():
        flux_copy = pltpu.make_async_copy(flux_hbm, flux_ref, sem.at[0])
        diff_copy = pltpu.make_async_copy(diff_hbm, diff_ref, sem.at[1])
        table_copy = pltpu.make_async_copy(table_hbm, table_ref, sem.at[2])
        for copy in [flux_copy, diff_copy] + x_copies + [table_copy]:
            copy.start()
        first = col_group * channels
        flux_copy.wait()
        weight = channel_column(flux_ref[...], channels, first)
        diff_copy.wait()
        diff = channel_column(diff_ref[...], channels, first)
        total = rows * groups_x
        base = (row_group * rows).astype(f32)
        tiles = wave_parts(columns)
        for k, (group, n, _) in enumerate(tiles):
            lam, alpha, _ = decay_terms(diff, half_rates(group, n, LANES, columns))
            factor_ref[k, 0] = lam
            lows, highs = edge_factors(lam, alpha, base, total, rows)
            for r in range(rows):
                factor_ref[k, 1 + r] = lows[r]
                factor_ref[k, 1 + rows + r] = highs[r]
        for r in range(rows):
            x_copies[r].wait()
            row_ref[r : r + 1, :] = jnp.sum(x_ref[r] * weight, axis=0, keepdims=True)
            left, right = x_ref[r, :, :half], x_ref[r, :, half:]
            flat_ref[r * channels : (r + 1) * channels, :half] = (left + right).astype(bf16)
            flat_ref[r * channels : (r + 1) * channels, half:] = (left - right).astype(bf16)
        send_surface()
        table_copy.wait()
        for k in range(2):
            lanes = slice(k * half, (k + 1) * half)
            part = jnp.dot(
                flat_ref[:, lanes], table_ref[lanes, :], preferred_element_type=f32
            )
            y_ref[:, :, lanes] = part.reshape(rows, channels, half)
            for tile, (group, _, parts) in enumerate(tiles):
                if group != k:
                    continue
                lam = factor_ref[tile, 0]
                for at in parts:
                    lanes = slice(at, at + LANES)
                    here = slice(at - k * half, at - k * half + LANES)
                    p = factor_ref[tile, 1] * part[0:channels, here]
                    q = factor_ref[tile, 2 * rows] * part[(rows - 1) * channels :, here]
                    for r in range(1, rows):
                        up = part[r * channels : (r + 1) * channels, here]
                        down = part[(rows - 1 - r) * channels : (rows - r) * channels, here]
                        p = lam * p + factor_ref[tile, 1 + r] * up
                        q = lam * q + factor_ref[tile, 2 * rows - r] * down
                    if paired:
                        for mask, out in ((1, e1_ref), (2, e2_ref), (3, e3_ref)):
                            upward = row_group < (row_group ^ mask)
                            out[0:channels, lanes] = jnp.where(upward, p, q).astype(bf16)
                    else:
                        pq_ref[0, :, lanes] = p.astype(bf16)
                        pq_ref[1, :, lanes] = q.astype(bf16)
        for copy in y_copies:
            copy.start()
        for copy in message_copies:
            copy.start()
        for copy in surface_copies + y_copies + message_copies:
            copy.wait()

    @pl.when(jnp.logical_not(is_atmos))
    def _():
        wet_copy = pltpu.make_async_copy(wet_hbm, wet_ref, sem.at[0])
        for copy in x_copies + [wet_copy]:
            copy.start()
        gain = jnp.where(col_group == 0, 1.0, 0.0)
        for r in range(rows):
            x_copies[r].wait()
            row_ref[r : r + 1, :] = x_ref[r, 0:1, :] * gain
        send_surface()
        wet_copy.wait()
        levels = channels // 2
        lines = 2 * channels
        even_x = row_group % 2 == 0
        even_y = col_group % 2 == 0
        wet = wet_ref[...].astype(f32)
        wet = jnp.concatenate([wet, wet], axis=0).astype(bf16)

        def put(out, last):
            @pl.when(last)
            def _():
                out[0:lines, :] = x_ref[rows - 2 :].reshape(lines, columns).astype(bf16)

            @pl.when(jnp.logical_not(last))
            def _():
                out[0:lines, :] = x_ref[:2].reshape(lines, columns).astype(bf16)

            out[lines : lines + 16, :] = wet

        put(e1_ref, even_x)
        put(e3_ref, jnp.logical_not(even_x))

        def put_edges(out, level):
            for r in range(rows):
                for t in range(2):
                    at = (r * 2 + t) * 2
                    c = t * levels + level
                    edge_ref[at : at + 2, :] = x_ref[r, c : c + 2, :]
            out[0 : rows * 4, :] = edge_ref[...].astype(bf16)

        @pl.when(even_y)
        def _():
            put_edges(e2_ref, levels - 2)
            put_edges(e4_ref, 0)

        @pl.when(jnp.logical_not(even_y))
        def _():
            put_edges(e2_ref, 0)
            put_edges(e4_ref, levels - 2)

        for copy in message_copies:
            copy.start()
        for copy in surface_copies + message_copies:
            copy.wait()


def one_hot_kernel(
    rows, columns, a_src, a_dst, m_src, m_dst, _, src_hot_ref, dst_hot_ref, src_row_ref, dst_row_ref
):
    is_atmos = lax.axis_index("comp") == 0
    blocks, points = src_row_ref.shape
    lane_iota = lax.broadcasted_iota(jnp.int32, (LANES, points), 0)
    for a_ref, m_ref, hot_ref, row_ref in (
        (a_src, m_src, src_hot_ref, src_row_ref),
        (a_dst, m_dst, dst_hot_ref, dst_row_ref),
    ):
        index = jnp.where(is_atmos, m_ref[0, 0], a_ref[0, 0])
        row = index // columns
        tile = (index // LANES) % (columns // LANES)
        row_ref[...] = tile * rows + row
        lane = index % LANES
        for b in range(blocks):
            hot_ref[:, b * points : (b + 1) * points] = jnp.where(
                lane_iota == lane[b : b + 1], 1.0, 0.0
            ).astype(bf16)


def regrid_kernel(n_surfaces, *refs):
    surfaces = refs[:n_surfaces]
    (
        src_hot_ref, dst_hot_ref, src_row_ref, dst_row_ref, a_count, m_count, a_weight, m_weight,
        _, _, _, _,
        *refs,
    ) = refs[n_surfaces:]
    land_ref, *sent_refs = refs[:-4]
    weight_ref, gath_ref, val_ref, sem = refs[-4:]
    is_atmos = lax.axis_index("comp") == 0
    blocks, points = val_ref.shape
    cells = surfaces[0].shape[0]

    @pl.when(is_atmos)
    def _():
        pltpu.make_async_copy(m_weight.at[0, 0], weight_ref, sem).start()

    @pl.when(jnp.logical_not(is_atmos))
    def _():
        pltpu.make_async_copy(a_weight.at[0, 0], weight_ref, sem).start()

    count = jnp.where(is_atmos, m_count[0, 0], a_count[0, 0])
    pair = 2 * points
    row_iota = lax.broadcasted_iota(jnp.int32, (cells, points), 0)
    table = sum(surface[...].astype(f32) for surface in surfaces).astype(bf16)
    for b in range(0, blocks, 2):
        picked = jnp.dot(
            table, src_hot_ref[:, b * points : b * points + pair], preferred_element_type=f32
        )
        for k in range(2):
            mine = row_iota == src_row_ref[b + k : b + k + 1, :]
            part = jnp.where(mine, picked[:, k * points : (k + 1) * points], 0.0)
            gath_ref[b + k : b + k + 1, :] = jnp.sum(part, axis=0, keepdims=True)
    gathered = gath_ref[...].astype(bf16)

    @pl.when(is_atmos)
    def _():
        pltpu.make_async_copy(m_weight.at[0, 0], weight_ref, sem).wait()

    @pl.when(jnp.logical_not(is_atmos))
    def _():
        pltpu.make_async_copy(a_weight.at[0, 0], weight_ref, sem).wait()

    block_iota = lax.broadcasted_iota(jnp.int32, (blocks, points), 0)
    values = jnp.zeros((blocks, points), f32)
    for b in range(0, blocks, 2):
        terms = lax.dot_general(
            gathered,
            weight_ref[b : b + 2].reshape(pair, points),
            (((1,), (1,)), ((), ())),
            preferred_element_type=f32,
        )
        for k in range(2):
            values = jnp.where(block_iota == b + k, terms[:, k * points : (k + 1) * points], values)
    val_ref[...] = jnp.where(block_iota < count, values, 0.0)
    land = jnp.zeros((2 * cells, LANES), f32)
    for b in range(0, blocks, 2):
        spread = []
        for k in range(b, b + 2):
            value = val_ref[k : k + 1, :]
            coarse = value.astype(bf16).astype(f32)
            fine = value - coarse
            mine = row_iota == dst_row_ref[k : k + 1, :]
            spread.append(
                jnp.concatenate(
                    [jnp.where(mine, coarse, 0.0), jnp.where(mine, fine, 0.0)], axis=0
                ).astype(bf16)
            )
        land = land + lax.dot_general(
            jnp.concatenate(spread, axis=1),
            dst_hot_ref[:, b * points : b * points + pair],
            (((1,), (1,)), ((), ())),
            preferred_element_type=f32,
        )
    land = land[:cells] + land[cells:]
    land_ref[...] = land
    for sent_ref in sent_refs:
        lengthen(sent_ref, land.astype(bf16))


def heat_kernel(rows, e2_ref, e4_ref, land_ref, _, *refs):
    parts = refs[:-3]
    sum_ref, near_ref, far_ref = refs[-3:]
    cells = land_ref.shape[0]
    columns = cells // rows * LANES
    even_x = lax.axis_index("gx") % 2 == 0
    even_y = lax.axis_index("gy") % 2 == 0
    total = land_ref[...]
    for part in parts:
        total = total + part[0:cells, :].astype(f32)
    sum_ref[...] = total

    def corners(row):
        start = row * 4 // 16 * 16
        one = e2_ref[start : start + 16, :].astype(f32)
        two = e4_ref[start : start + 16, :].astype(f32)
        low = jnp.where(even_y, two, one)
        high = jnp.where(even_y, one, two)
        at = row * 4 - start
        lines = [low[at + 1 : at + 2], low[at + 3 : at + 4], high[at : at + 1], high[at + 2 : at + 3]]
        heat = from_tiles(total, rows)[row : row + 1]
        blank = jnp.zeros((3, columns), f32)
        return to_tiles(jnp.concatenate([heat] + lines + [blank], axis=0))

    first, last = corners(0), corners(rows - 1)
    near_ref[...] = jnp.where(even_x, last, first).astype(bf16)
    far_ref[...] = jnp.where(even_x, first, last).astype(bf16)


def advance(ref, r, t, coefs, size):
    ring, columns = ref.shape[2:]
    whole = ref[r, t]
    up = pltpu.roll(whole, 1, 0)[:size]
    down = pltpu.roll(whole, ring - 1, 0)[:size]
    mid = whole[:size]
    total = coefs[0] * mid + coefs[5] * (up + down)
    total = total + coefs[1] * ref[r - 1, t, 0:size, :]
    total = total + coefs[2] * ref[r + 1, t, 0:size, :]
    total = total + coefs[3] * pltpu.roll(mid, 1, 1)
    return total + coefs[4] * pltpu.roll(mid, columns - 1, 1)


def first_step_kernel(
    groups_x, groups_y, paired, x_ref, wet_ref, diff_ref, y_ref, e1_ref, e3_ref,
    e2_ref, e4_ref, *refs,
):
    if not paired:
        pin_ref, qin_ref = refs[:2]
    zb_ref, c_ref, t1_ref, z_ref, t0_ref, w_ref = refs[-6:]
    _, rows, channels, columns = x_ref.shape
    row_group = lax.axis_index("gx")
    col_group = lax.axis_index("gy")
    is_atmos = lax.axis_index("comp") == 0

    @pl.when(is_atmos)
    def _():
        diff = channel_column(diff_ref[...], channels, col_group * channels)
        total = rows * groups_x
        base = (row_group * rows).astype(f32)
        for group, n, parts in wave_parts(columns):
            lam, alpha, sinh = decay_terms(diff, half_rates(group, n, LANES, columns))
            scale = 1.0 / (
                2.0 * diff * sinh * (1.0 - jnp.exp(-2.0 * (total + 1) * alpha))
            )
            lows, highs = edge_factors(lam, alpha, base, total, rows)
            for part in parts:
                lanes = slice(part, part + LANES)
                if paired:
                    pin = jnp.zeros((channels, LANES), f32)
                    qin = jnp.zeros((channels, LANES), f32)
                    for mask, msg in ((1, e1_ref), (2, e2_ref), (3, e3_ref)):
                        band = row_group ^ mask
                        gap = (jnp.abs(row_group - band) - 1) * rows
                        term = jnp.exp(-gap.astype(f32) * alpha)
                        term = term * msg[0:channels, lanes].astype(f32)
                        pin = pin + jnp.where(band < row_group, term, 0.0)
                        qin = qin + jnp.where(band > row_group, term, 0.0)
                else:
                    pin = pin_ref[:, lanes]
                    qin = qin_ref[:, lanes]
                f = pin
                for r in range(rows):
                    f = lam * f + lows[r] * y_ref[r, :, lanes]
                    z_ref[r] = highs[r] * f
                g = lam * qin
                for r in reversed(range(rows)):
                    z = scale * (z_ref[r] + lows[r] * g)
                    zb_ref[r * channels : (r + 1) * channels, lanes] = z.astype(bf16)
                    g = lam * (g + highs[r] * y_ref[r, :, lanes])

    @pl.when(jnp.logical_not(is_atmos))
    def _():
        levels = channels // 2
        ring = levels + 8
        lines = 2 * channels
        first_x = row_group == 0
        last_x = row_group == groups_x - 1
        top = col_group == 0
        bottom = col_group == groups_y - 1
        even_x = row_group % 2 == 0
        even_y = col_group % 2 == 0

        one = e1_ref[lines : lines + 16, :].astype(f32)
        three = e3_ref[lines : lines + 16, :].astype(f32)
        below = jnp.where(even_x, three, one)[rows - 2 : rows]
        above = jnp.where(even_x, one, three)[0:2]
        w_ref[0:2, :] = jnp.where(first_x, 0.0, below)
        w_ref[2 : rows + 2, :] = wet_ref[...].astype(f32)
        w_ref[rows + 2 : rows + 4, :] = jnp.where(last_x, 0.0, above)

        span = rows + 2
        north = w_ref[0:span, :]
        here = w_ref[1 : span + 1, :]
        south = w_ref[2 : span + 2, :]
        west = pltpu.roll(here, 1, 1)
        east = pltpu.roll(here, columns - 1, 1)
        c_ref[0, 0:span, :] = here * (
            1.0 - 2.0 * mixing_rate - spread_rate * (north + south + west + east)
        )
        c_ref[1, 0:span, :] = spread_rate * here * north
        c_ref[2, 0:span, :] = spread_rate * here * south
        c_ref[3, 0:span, :] = spread_rate * here * west
        c_ref[4, 0:span, :] = spread_rate * here * east
        c_ref[5, 0:span, :] = mixing_rate * here
        c_ref[6, 0:span, :] = here

        one = e1_ref[0:lines, :].astype(f32)
        three = e3_ref[0:lines, :].astype(f32)
        below = jnp.where(even_x, three, one)
        above = jnp.where(even_x, one, three)
        blank = jnp.zeros((8, columns), f32)
        for k in range(2):
            for t in range(2):
                c = k * channels + t * levels
                t0_ref[k, t, 0:levels, :] = below[c : c + levels]
                t0_ref[rows + 2 + k, t, 0:levels, :] = above[c : c + levels]
                t0_ref[k, t, levels:ring, :] = blank
                t0_ref[rows + 2 + k, t, levels:ring, :] = blank
        one = e2_ref[...].astype(f32)
        two = e4_ref[0 : 4 * rows, :].astype(f32)
        before = jnp.where(even_y, two, one)
        after = jnp.where(even_y, one, two)
        for r in range(rows):
            for t in range(2):
                k = (r * 2 + t) * 2
                t0_ref[r + 2, t, 0:levels, :] = x_ref[0, r, t * levels : (t + 1) * levels, :]
                t0_ref[r + 2, t, levels : levels + 2, :] = after[k : k + 2]
                t0_ref[r + 2, t, ring - 2 : ring, :] = before[k : k + 2]

        def close(ref, r):
            for t in range(2):
                ref[r, t, ring - 1 : ring, :] = jnp.where(
                    top, ref[r, t, 0:1, :], ref[r, t, ring - 1 : ring, :]
                )
                ref[r, t, levels : levels + 1, :] = jnp.where(
                    bottom, ref[r, t, levels - 1 : levels, :], ref[r, t, levels : levels + 1, :]
                )

        def first(r, carry):
            coefs = [c_ref[k, pl.ds(r, 1), :] for k in range(6)]
            close(t0_ref, r + 1)
            for t in range(2):
                t1_ref[r, t] = advance(t0_ref, r + 1, t, coefs, ring)
            close(t1_ref, r)
            return carry

        lax.fori_loop(0, span, first, 0)


def second_step_kernel(gain_ref, table_ref, zb_ref, c_ref, t1_ref, base_ref, column_ref):
    rows, channels, columns = base_ref.shape
    is_atmos = lax.axis_index("comp") == 0

    @pl.when(is_atmos)
    def _():
        response = channel_column(gain_ref[...], channels, lax.axis_index("gy") * channels)
        column_ref[...] = jnp.broadcast_to(response, column_ref.shape)
        half = columns // 2
        step = 256
        for n in range(0, half, step):
            even, odd = [
                jnp.dot(
                    zb_ref[:, k * half : (k + 1) * half],
                    table_ref[k * half : (k + 1) * half, n : n + step],
                    preferred_element_type=f32,
                ).reshape(rows, channels, step)
                for k in range(2)
            ]
            base_ref[:, :, n : n + step] = even + odd
            base_ref[:, :, n + half : n + half + step] = even - odd

    @pl.when(jnp.logical_not(is_atmos))
    def _():
        levels = channels // 2

        def second(r, carry):
            coefs = [c_ref[k, pl.ds(r, 1), :] for k in range(6)]
            for t in range(2):
                c = t * levels
                base_ref[r - 1, c : c + levels, :] = advance(t1_ref, r, t, coefs, levels)
            return carry

        lax.fori_loop(1, rows + 1, second, 0)


def last_kernel(
    groups_x, groups_y, column_ref, base_ref, c_ref, sum_ref, near_ref, far_ref, out_hbm,
    out_ref, e_ref, heat_ref, sem,
):
    rows, channels, columns = out_ref.shape
    row_group = lax.axis_index("gx")
    col_group = lax.axis_index("gy")
    is_atmos = lax.axis_index("comp") == 0
    copies = [
        pltpu.make_async_copy(out_ref.at[r], out_hbm.at[0, r], sem.at[r]) for r in range(rows)
    ]

    @pl.when(is_atmos)
    def _():
        for r in range(rows):
            for k in range(columns // LANES):
                lanes = slice(k * LANES, (k + 1) * LANES)
                at = k * rows + r
                out_ref[r, :, lanes] = (
                    base_ref[r, :, lanes] + column_ref[...] * sum_ref[at : at + 1, :]
                )
            copies[r].start()

    @pl.when(jnp.logical_not(is_atmos))
    def _():
        levels = channels // 2
        even = row_group % 2 == 0
        below = jnp.where(even, far_ref[...].astype(f32), near_ref[...].astype(f32))
        above = jnp.where(even, near_ref[...].astype(f32), far_ref[...].astype(f32))

        low = from_tiles(below, 8)
        high = from_tiles(above, 8)
        by_low = c_ref[1, 1:2, :] * (c_ref[5, 0:1, :] + c_ref[5, 1:2, :])
        by_high = c_ref[2, rows : rows + 1, :] * (
            c_ref[5, rows : rows + 1, :] + c_ref[5, rows + 1 : rows + 2, :]
        )
        has_before = jnp.where(col_group > 0, 1.0, 0.0)
        has_after = jnp.where(col_group < groups_y - 1, 1.0, 0.0)

        @pl.when(col_group == 0)
        def _():
            span = rows + 2
            e_ref[0:1, :] = low[0:1]
            e_ref[1 : rows + 1, :] = from_tiles(sum_ref[...], rows)
            e_ref[rows + 1 : span, :] = high[0:1]
            e_ref[0:span, :] = c_ref[6, 0:span, :] * e_ref[0:span, :]
            own = slice(1, rows + 1)
            heat = e_ref[own, :]
            second = c_ref[5, own, :] * heat
            first = (c_ref[0, own, :] + 1.0) * heat + second
            first = first + c_ref[1, own, :] * e_ref[0:rows, :]
            first = first + c_ref[2, own, :] * e_ref[2 : rows + 2, :]
            first = first + c_ref[3, own, :] * pltpu.roll(heat, 1, 1)
            first = first + c_ref[4, own, :] * pltpu.roll(heat, columns - 1, 1)
            heat_ref[0] = first
            heat_ref[1] = second

        for r in [1, rows - 2] + list(range(2, rows - 2)) + [0, rows - 1]:
            out_ref[r] = base_ref[r]
            for t in range(2):
                c = t * levels
                for edge, factor, lines in ((0, by_low, low), (rows - 1, by_high, high)):
                    if r == edge:
                        out_ref[r, c : c + 1, :] = out_ref[r, c : c + 1, :] + (
                            has_before * factor * lines[t + 1 : t + 2]
                        )
                        d = c + levels - 1
                        out_ref[r, d : d + 1, :] = out_ref[r, d : d + 1, :] + (
                            has_after * factor * lines[t + 3 : t + 4]
                        )

            @pl.when(col_group == 0)
            def _():
                for t, gain in enumerate((heat_gain, salt_gain)):
                    c = t * levels
                    for k in range(2):
                        out_ref[r, c + k : c + k + 1, :] = (
                            out_ref[r, c + k : c + k + 1, :] + gain * heat_ref[k, r : r + 1, :]
                        )

            copies[r].start()

    for copy in copies:
        copy.wait()


def local(
    fields,
    wet_cells,
    flux_weight,
    variable_sea_response,
    diffusivity,
    a2o_source,
    a2o_target,
    a2o_count,
    a2o_weight,
    marine_air_input_index,
    marine_air_output_index,
    marine_air_piece_tally,
    marine_air_piece_factor,
):
    _, rows, channels, columns = fields.shape
    groups_x = lax.axis_size("gx")
    groups_y = lax.axis_size("gy")
    blocks, points = a2o_source.shape[2:]
    cells = rows * columns // LANES
    forward, inverse = fourier_tables(columns)
    flux_row = flux_weight[None, :]
    gain_row = variable_sea_response[None, :]
    diff_row = diffusivity[None, :]
    paired = groups_x == 4
    params = functools.partial(pltpu.CompilerParams, vmem_limit_bytes=40 * 2**20)
    vmem = pl.BlockSpec(memory_space=pltpu.VMEM)
    smem = pl.BlockSpec(memory_space=pltpu.SMEM)
    hbm = pl.BlockSpec(memory_space=pltpu.HBM)
    anywhere = pl.BlockSpec(memory_space=pl.ANY)

    def shape(dims, dtype):
        return jax.ShapeDtypeStruct(dims, dtype)

    lines = 2 * channels + 16
    shapes = [
        shape((cells, LANES), bf16),
        shape((cells + 16, LANES), bf16),
        shape((rows, channels, columns), f32),
        shape((lines, columns), bf16),
        shape((lines, columns), bf16),
        shape((4 * rows, columns), bf16),
        shape((4 * rows + 16, columns), bf16),
    ]
    if not paired:
        shapes.append(shape((2, channels, columns), bf16))
    coarse, wide, y, e1, e3, e2, e4, *sums = pl.pallas_call(
        functools.partial(start_kernel, groups_x, paired),
        out_shape=shapes,
        in_specs=[hbm] * 5,
        out_specs=[hbm] * len(shapes),
        scratch_shapes=[pltpu.VMEM(out.shape, out.dtype) for out in shapes]
        + [
            pltpu.VMEM((rows, channels, columns), f32),
            pltpu.VMEM((rows, columns), jnp.int32),
            pltpu.VMEM(flux_row.shape, f32),
            pltpu.VMEM(diff_row.shape, f32),
            pltpu.VMEM(forward.shape, bf16),
            pltpu.VMEM((rows * channels, columns), bf16),
            pltpu.VMEM((rows, columns), f32),
            pltpu.VMEM((4 * rows, columns), f32),
            pltpu.VMEM((columns // 2 // LANES, 2 * rows + 1, channels, LANES), f32),
            pltpu.SemaphoreType.DMA((rows,)),
            pltpu.SemaphoreType.DMA((3,)),
            pltpu.SemaphoreType.DMA((rows + len(shapes) - 1,)),
        ],
        compiler_params=pltpu.CompilerParams(vmem_limit_bytes=58 * 2**20),
        name="surface_and_forward_or_halos",
    )(fields, wet_cells, flux_row, diff_row, forward)

    masks = [1 << bit for bit in range(groups_y.bit_length() - 1)]

    def sum_route(mask):
        return [(j, j ^ mask) for j in range(groups_y)]

    def partner_route(mask):
        return both_ways([(j, groups_y + (j ^ mask)) for j in range(groups_y)])

    surface = lax.ppermute(coarse, ("comp", "gy"), partner_route(0)).astype(f32)
    for mask in masks[:1]:
        far = lax.ppermute(wide, ("comp", "gy"), partner_route(mask))
        surface = surface + far[:cells].astype(f32)
    coarse = surface.astype(bf16)
    for mask in masks[1:-1]:
        surface = surface + lax.ppermute(coarse, "gy", sum_route(mask)).astype(f32)
        coarse = surface.astype(bf16)
    surfaces = [surface] + [
        lax.ppermute(coarse, "gy", sum_route(mask)) for mask in masks[1:][-1:]
    ]

    def ring_pairs(count, odd):
        return [(a, (a + 1) % count) for a in range(odd, count, 2)]

    def flat(comp, i, j):
        return (comp * groups_x + i) * groups_y + j

    def level_route(odd):
        pairs = []
        for i in range(groups_x):
            linked = [(a, a + 1) for a in range(odd, groups_y - 1, 2)]
            alone = set(range(groups_y)) - {j for pair in linked for j in pair}
            pairs += [(flat(1, i, a), flat(1, i, b)) for a, b in linked]
            if i % 2 == 0:
                pairs += [(flat(1, i, j), flat(1, i + 1, j)) for j in sorted(alone)]
                if odd or not paired:
                    pairs += [(flat(0, i, j), flat(0, i + 1, j)) for j in range(groups_y)]
            if paired and not odd and i < i ^ 2:
                pairs += [(flat(0, i, j), flat(0, i ^ 2, j)) for j in range(groups_y)]
        return both_ways(pairs)

    e1 = lax.ppermute(e1, "gx", both_ways(ring_pairs(groups_x, 0)))
    e3 = lax.ppermute(e3, "gx", both_ways(ring_pairs(groups_x, 1)))
    axes = ("comp", "gx", "gy")
    e2 = lax.ppermute(e2, axes, level_route(0))
    e4 = lax.ppermute(e4, axes, level_route(1))

    one_hots = pl.pallas_call(
        functools.partial(one_hot_kernel, rows, columns),
        out_shape=[
            shape((LANES, blocks * points), bf16),
            shape((LANES, blocks * points), bf16),
            shape((blocks, points), jnp.int32),
            shape((blocks, points), jnp.int32),
        ],
        in_specs=[vmem] * 4 + [anywhere],
        out_specs=[vmem] * 4,
        compiler_params=params(),
        name="one_hots",
    )(a2o_source, a2o_target, marine_air_input_index, marine_air_output_index, coarse)
    landing, *sent = pl.pallas_call(
        functools.partial(regrid_kernel, len(surfaces)),
        out_shape=[shape((cells, LANES), f32)]
        + [shape((cells + 16 * (mask - 1), LANES), bf16) for mask in range(1, groups_y)],
        in_specs=[vmem] * (len(surfaces) + 4) + [smem, smem, hbm, hbm] + [anywhere] * 4,
        out_specs=[vmem] * groups_y,
        scratch_shapes=[
            pltpu.VMEM((blocks, points, points), bf16),
            pltpu.VMEM((blocks, points), f32),
            pltpu.VMEM((blocks, points), f32),
            pltpu.SemaphoreType.DMA,
        ],
        compiler_params=params(),
        name="regrid_blocks",
    )(
        *surfaces, *one_hots, a2o_count, marine_air_piece_tally,
        a2o_weight, marine_air_piece_factor, e1, e3, e2, e4,
    )

    def landing_route(mask):
        pairs = [
            (flat(0, i, j), flat(0, i, j ^ mask))
            for i in range(groups_x)
            for j in range(groups_y)
            if j < j ^ mask
        ]
        pairs += [(flat(1, i, 0), flat(1, i, mask)) for i in range(groups_x)]
        pairs += [
            (flat(1, i, j), flat(1, i + 1, j))
            for i in range(0, groups_x, 2)
            for j in range(groups_y)
            if j not in (0, mask)
        ]
        return both_ways(pairs)

    parts = [
        lax.ppermute(block, axes, landing_route(mask)) for mask, block in enumerate(sent, 1)
    ]

    extra = []
    if not paired:
        p, q = jnp.moveaxis(lax.all_gather(sums[0], "gx").astype(f32), 1, 0)
        viscous = lax.dynamic_slice_in_dim(
            diffusivity, lax.axis_index("gy") * channels, channels
        )[:, None]
        rates = [half_rates(g, 0, columns // 4, columns) for g in (0, 0, 1, 1)]
        _, alpha, _ = decay_terms(viscous, jnp.concatenate(rates, axis=1))
        gap = lax.axis_index("gx") - jnp.arange(groups_x)
        decay = jnp.exp(
            -(rows * jnp.maximum(jnp.abs(gap) - 1, 0))[:, None, None] * alpha[None]
        )
        extra = [
            jnp.sum(jnp.where((gap > 0)[:, None, None], decay * p, 0.0), axis=0),
            jnp.sum(jnp.where((gap < 0)[:, None, None], decay * q, 0.0), axis=0),
        ]
    ring = channels // 2 + 8
    damped, coefs, stepped = pl.pallas_call(
        functools.partial(first_step_kernel, groups_x, groups_y, paired),
        out_shape=[
            shape((rows * channels, columns), bf16),
            shape((7, 16, columns), f32),
            shape((rows + 2, 2, ring, columns), f32),
        ],
        in_specs=[vmem] * (8 + len(extra)),
        out_specs=[vmem] * 3,
        scratch_shapes=[
            pltpu.VMEM((rows, channels, LANES), f32),
            pltpu.VMEM((rows + 4, 2, ring, columns), f32),
            pltpu.VMEM((16, columns), f32),
        ],
        compiler_params=params(),
        name="damping_or_first_step",
    )(fields, wet_cells, diff_row, y, e1, e3, e2, e4, *extra)

    surface_sum, near, far = pl.pallas_call(
        functools.partial(heat_kernel, rows),
        out_shape=[
            shape((cells, LANES), f32),
            shape((columns // 16, LANES), bf16),
            shape((columns // 16, LANES), bf16),
        ],
        in_specs=[vmem] * 3 + [anywhere] + [vmem] * len(parts),
        out_specs=[vmem] * 3,
        compiler_params=params(),
        name="surface_sum",
    )(e2, e4, landing, coefs, *parts)

    near = lax.ppermute(near, "gx", both_ways(ring_pairs(groups_x, 0)))
    far = lax.ppermute(far, "gx", both_ways(ring_pairs(groups_x, 1)))
    base, column = pl.pallas_call(
        second_step_kernel,
        out_shape=[shape((rows, channels, columns), f32), shape((channels, LANES), f32)],
        in_specs=[vmem] * 5,
        out_specs=[vmem] * 2,
        compiler_params=params(),
        name="inverse_or_second_step",
    )(gain_row, inverse, damped, coefs, stepped)
    return pl.pallas_call(
        functools.partial(last_kernel, groups_x, groups_y),
        out_shape=shape(fields.shape, f32),
        in_specs=[vmem] * 6,
        out_specs=hbm,
        scratch_shapes=[
            pltpu.VMEM((rows, channels, columns), f32),
            pltpu.VMEM((16, columns), f32),
            pltpu.VMEM((2, rows, columns), f32),
            pltpu.SemaphoreType.DMA((rows,)),
        ],
        compiler_params=params(),
        name="add_surface_terms",
    )(column, base, coefs, surface_sum, near, far)


def solution(mesh):
    in_specs = (
        P("comp", "gx", "gy", None),
        P("gx", None),
        P(),
        P(),
        P(),
        P("gx", "gy", None, None),
        P("gx", "gy", None, None),
        P("gx", "gy"),
        P("gx", "gy", None, None, None),
        P("gx", "gy", None, None),
        P("gx", "gy", None, None),
        P("gx", "gy"),
        P("gx", "gy", None, None, None),
    )
    out_specs = P("comp", "gx", "gy", None)
    return jax.shard_map(local, mesh=mesh, in_specs=in_specs, out_specs=out_specs, check_vma=False)
```

```python
import functools

import jax
import jax.numpy as jnp
import numpy as np
from jax import lax
from jax.experimental import pallas as pl
from jax.experimental.pallas import tpu as pltpu
from jax.sharding import PartitionSpec as P

spread_rate = 0.2
mixing_rate = 0.1
heat_gain = 0.5
salt_gain = -0.25
LANES = 128
f32 = jnp.float32
bf16 = jnp.bfloat16


def fourier_tables(columns):
    half = columns // 2
    forward, inverse = [], []
    for first in (0, 1):
        waves = np.arange(first, half, 2)
        phase = np.arange(half)[:, None] * waves[None, :] % columns
        angles = phase * (2.0 * np.pi / columns)
        table = np.concatenate([np.cos(angles), np.sin(angles)], axis=1)
        weight = np.where(waves == 0, 1.0, 2.0) / columns
        forward.append(table)
        inverse.append(table.T * np.concatenate([weight, weight])[:, None])
    return (
        jnp.asarray(np.concatenate(forward).astype(np.float32), bf16),
        jnp.asarray(np.concatenate(inverse).astype(np.float32), bf16),
    )


def wave_parts(columns):
    quarter = columns // 4
    return [
        (g, n, (g * 2 * quarter + n, (g * 2 + 1) * quarter + n))
        for g in (0, 1)
        for n in range(0, quarter, LANES)
    ]


def half_rates(group, first, count, columns):
    lane = lax.broadcasted_iota(jnp.int32, (1, count), 1) + first
    wave = (2 * lane + group).astype(f32)
    sine = jnp.sin(wave * (np.pi / columns))
    return 2.0 * sine * sine


def both_ways(pairs):
    return [p for a, b in pairs for p in ((a, b), (b, a))]


def channel_column(row, channels, first):
    n = row.shape[1]
    lane = lax.broadcasted_iota(jnp.int32, (channels, n), 1)
    sub = lax.broadcasted_iota(jnp.int32, (channels, n), 0)
    return jnp.sum(jnp.where(lane == sub + first, row, 0.0), axis=1, keepdims=True)


def to_tiles(surface):
    cols = surface.shape[1]
    return jnp.concatenate(
        [surface[:, k : k + LANES] for k in range(0, cols, LANES)], axis=0
    )


def from_tiles(tiles, rows):
    return jnp.concatenate(
        [tiles[k : k + rows] for k in range(0, tiles.shape[0], rows)], axis=1
    )


def lengthen(ref, block):
    rows = block.shape[0]
    ref[0:rows, :] = block
    if ref.shape[0] > rows:
        ref[rows:, :] = block[: ref.shape[0] - rows]


def decay_terms(diff_column, rates):
    half = 0.5 / diff_column + rates
    sinh = jnp.sqrt(half * (half + 2.0))
    grow = 1.0 + half + sinh
    return 1.0 / grow, jnp.log(grow), sinh


def edge_factors(lam, alpha, base, total, rows):
    lam2 = lam * lam
    powers = [
        jnp.exp(-2.0 * base * alpha) * lam2,
        jnp.exp(-2.0 * (total - rows - base) * alpha) * lam2,
    ]
    lows, highs = [], []
    for _ in range(rows):
        lows.append(1.0 - powers[0])
        highs.insert(0, 1.0 - powers[1])
        powers = [power * lam2 for power in powers]
    return lows, highs


def start_kernel(
    groups_x, paired, x_hbm, wet_hbm, flux_hbm, diff_hbm, table_hbm, *refs
):
    outs = 7 if paired else 8
    coarse_hbm, wide_hbm, y_hbm, *message_hbm = refs[:outs]
    coarse_ref, wide_ref, y_ref, *message_ref = refs[outs : 2 * outs]
    e1_ref, e3_ref, e2_ref, e4_ref = message_ref[:4]
    if not paired:
        pq_ref = message_ref[4]
    (
        x_ref, wet_ref, flux_ref, diff_ref, table_ref, flat_ref, row_ref, edge_ref,
        factor_ref, x_sem, sem, out_sem,
    ) = refs[2 * outs :]
    rows, channels, columns = x_ref.shape
    half = columns // 2
    row_group = lax.axis_index("gx")
    col_group = lax.axis_index("gy")
    is_atmos = lax.axis_index("comp") == 0

    x_copies = [
        pltpu.make_async_copy(x_hbm.at[0, r], x_ref.at[r], x_sem.at[r]) for r in range(rows)
    ]
    surface_copies = [
        pltpu.make_async_copy(coarse_ref, coarse_hbm, out_sem.at[0]),
        pltpu.make_async_copy(wide_ref, wide_hbm, out_sem.at[1]),
    ]
    y_copies = [
        pltpu.make_async_copy(y_ref.at[r], y_hbm.at[r], out_sem.at[2 + r]) for r in range(rows)
    ]
    message_copies = [
        pltpu.make_async_copy(ref, hbm, out_sem.at[2 + rows + k])
        for k, (ref, hbm) in enumerate(zip(message_ref, message_hbm))
    ]

    def send_surface():
        coarse = to_tiles(row_ref[...]).astype(bf16)
        coarse_ref[...] = coarse
        lengthen(wide_ref, coarse)
        for copy in surface_copies:
            copy.start()

    @pl.when(is_atmos)
    def _():
        flux_copy = pltpu.make_async_copy(flux_hbm, flux_ref, sem.at[0])
        diff_copy = pltpu.make_async_copy(diff_hbm, diff_ref, sem.at[1])
        table_copy = pltpu.make_async_copy(table_hbm, table_ref, sem.at[2])
        for copy in [flux_copy, diff_copy] + x_copies + [table_copy]:
            copy.start()
        first = col_group * channels
        flux_copy.wait()
        weight = channel_column(flux_ref[...], channels, first)
        diff_copy.wait()
        diff = channel_column(diff_ref[...], channels, first)
        total = rows * groups_x
        base = (row_group * rows).astype(f32)
        tiles = wave_parts(columns)
        for k, (group, n, _) in enumerate(tiles):
            lam, alpha, _ = decay_terms(diff, half_rates(group, n, LANES, columns))
            factor_ref[k, 0] = lam
            lows, highs = edge_factors(lam, alpha, base, total, rows)
            for r in range(rows):
                factor_ref[k, 1 + r] = lows[r]
                factor_ref[k, 1 + rows + r] = highs[r]
        for r in range(rows):
            x_copies[r].wait()
            row_ref[r : r + 1, :] = jnp.sum(x_ref[r] * weight, axis=0, keepdims=True)
            left, right = x_ref[r, :, :half], x_ref[r, :, half:]
            flat_ref[r * channels : (r + 1) * channels, :half] = (left + right).astype(bf16)
            flat_ref[r * channels : (r + 1) * channels, half:] = (left - right).astype(bf16)
        send_surface()
        table_copy.wait()
        for k in range(2):
            lanes = slice(k * half, (k + 1) * half)
            part = jnp.dot(
                flat_ref[:, lanes], table_ref[lanes, :], preferred_element_type=f32
            )
            y_ref[:, :, lanes] = part.reshape(rows, channels, half)
            for tile, (group, _, parts) in enumerate(tiles):
                if group != k:
                    continue
                lam = factor_ref[tile, 0]
                for at in parts:
                    lanes = slice(at, at + LANES)
                    here = slice(at - k * half, at - k * half + LANES)
                    p = factor_ref[tile, 1] * part[0:channels, here]
                    q = factor_ref[tile, 2 * rows] * part[(rows - 1) * channels :, here]
                    for r in range(1, rows):
                        up = part[r * channels : (r + 1) * channels, here]
                        down = part[(rows - 1 - r) * channels : (rows - r) * channels, here]
                        p = lam * p + factor_ref[tile, 1 + r] * up
                        q = lam * q + factor_ref[tile, 2 * rows - r] * down
                    if paired:
                        for mask, out in ((1, e1_ref), (2, e2_ref), (3, e3_ref)):
                            upward = row_group < (row_group ^ mask)
                            out[0:channels, lanes] = jnp.where(upward, p, q).astype(bf16)
                    else:
                        pq_ref[0, :, lanes] = p.astype(bf16)
                        pq_ref[1, :, lanes] = q.astype(bf16)
        for copy in y_copies:
            copy.start()
        for copy in message_copies:
            copy.start()
        for copy in surface_copies + y_copies + message_copies:
            copy.wait()

    @pl.when(jnp.logical_not(is_atmos))
    def _():
        wet_copy = pltpu.make_async_copy(wet_hbm, wet_ref, sem.at[0])
        for copy in x_copies + [wet_copy]:
            copy.start()
        gain = jnp.where(col_group == 0, 1.0, 0.0)
        for r in range(rows):
            x_copies[r].wait()
            row_ref[r : r + 1, :] = x_ref[r, 0:1, :] * gain
        send_surface()
        wet_copy.wait()
        levels = channels // 2
        lines = 2 * channels
        even_x = row_group % 2 == 0
        even_y = col_group % 2 == 0
        wet = wet_ref[...].astype(f32)
        wet = jnp.concatenate([wet, wet], axis=0).astype(bf16)

        def put(out, last):
            @pl.when(last)
            def _():
                out[0:lines, :] = x_ref[rows - 2 :].reshape(lines, columns).astype(bf16)

            @pl.when(jnp.logical_not(last))
            def _():
                out[0:lines, :] = x_ref[:2].reshape(lines, columns).astype(bf16)

            out[lines : lines + 16, :] = wet

        put(e1_ref, even_x)
        put(e3_ref, jnp.logical_not(even_x))

        def put_edges(out, level):
            for r in range(rows):
                for t in range(2):
                    at = (r * 2 + t) * 2
                    c = t * levels + level
                    edge_ref[at : at + 2, :] = x_ref[r, c : c + 2, :]
            out[0 : rows * 4, :] = edge_ref[...].astype(bf16)

        @pl.when(even_y)
        def _():
            put_edges(e2_ref, levels - 2)
            put_edges(e4_ref, 0)

        @pl.when(jnp.logical_not(even_y))
        def _():
            put_edges(e2_ref, 0)
            put_edges(e4_ref, levels - 2)

        for copy in message_copies:
            copy.start()
        for copy in surface_copies + message_copies:
            copy.wait()


def one_hot_kernel(
    rows, columns, a_src, a_dst, m_src, m_dst, _, src_hot_ref, dst_hot_ref, src_row_ref, dst_row_ref
):
    is_atmos = lax.axis_index("comp") == 0
    blocks, points = src_row_ref.shape
    lane_iota = lax.broadcasted_iota(jnp.int32, (LANES, points), 0)
    for a_ref, m_ref, hot_ref, row_ref in (
        (a_src, m_src, src_hot_ref, src_row_ref),
        (a_dst, m_dst, dst_hot_ref, dst_row_ref),
    ):
        index = jnp.where(is_atmos, m_ref[0, 0], a_ref[0, 0])
        row = index // columns
        tile = (index // LANES) % (columns // LANES)
        row_ref[...] = tile * rows + row
        lane = index % LANES
        for b in range(blocks):
            hot_ref[:, b * points : (b + 1) * points] = jnp.where(
                lane_iota == lane[b : b + 1], 1.0, 0.0
            ).astype(bf16)


def regrid_kernel(n_surfaces, *refs):
    surfaces = refs[:n_surfaces]
    (
        src_hot_ref, dst_hot_ref, src_row_ref, dst_row_ref, a_count, m_count, a_weight, m_weight,
        _, _, _, _,
        *refs,
    ) = refs[n_surfaces:]
    land_ref, *sent_refs = refs[:-4]
    weight_ref, gath_ref, val_ref, sem = refs[-4:]
    is_atmos = lax.axis_index("comp") == 0
    blocks, points = val_ref.shape
    cells = surfaces[0].shape[0]

    @pl.when(is_atmos)
    def _():
        pltpu.make_async_copy(m_weight.at[0, 0], weight_ref, sem).start()

    @pl.when(jnp.logical_not(is_atmos))
    def _():
        pltpu.make_async_copy(a_weight.at[0, 0], weight_ref, sem).start()

    count = jnp.where(is_atmos, m_count[0, 0], a_count[0, 0])
    pair = 2 * points
    row_iota = lax.broadcasted_iota(jnp.int32, (cells, points), 0)
    table = sum(surface[...].astype(f32) for surface in surfaces).astype(bf16)
    for b in range(0, blocks, 2):
        picked = jnp.dot(
            table, src_hot_ref[:, b * points : b * points + pair], preferred_element_type=f32
        )
        for k in range(2):
            mine = row_iota == src_row_ref[b + k : b + k + 1, :]
            part = jnp.where(mine, picked[:, k * points : (k + 1) * points], 0.0)
            gath_ref[b + k : b + k + 1, :] = jnp.sum(part, axis=0, keepdims=True)
    gathered = gath_ref[...].astype(bf16)

    @pl.when(is_atmos)
    def _():
        pltpu.make_async_copy(m_weight.at[0, 0], weight_ref, sem).wait()

    @pl.when(jnp.logical_not(is_atmos))
    def _():
        pltpu.make_async_copy(a_weight.at[0, 0], weight_ref, sem).wait()

    block_iota = lax.broadcasted_iota(jnp.int32, (blocks, points), 0)
    values = jnp.zeros((blocks, points), f32)
    for b in range(0, blocks, 2):
        terms = lax.dot_general(
            gathered,
            weight_ref[b : b + 2].reshape(pair, points),
            (((1,), (1,)), ((), ())),
            preferred_element_type=f32,
        )
        for k in range(2):
            values = jnp.where(block_iota == b + k, terms[:, k * points : (k + 1) * points], values)
    val_ref[...] = jnp.where(block_iota < count, values, 0.0)
    land = jnp.zeros((2 * cells, LANES), f32)
    for b in range(0, blocks, 2):
        spread = []
        for k in range(b, b + 2):
            value = val_ref[k : k + 1, :]
            coarse = value.astype(bf16).astype(f32)
            fine = value - coarse
            mine = row_iota == dst_row_ref[k : k + 1, :]
            spread.append(
                jnp.concatenate(
                    [jnp.where(mine, coarse, 0.0), jnp.where(mine, fine, 0.0)], axis=0
                ).astype(bf16)
            )
        land = land + lax.dot_general(
            jnp.concatenate(spread, axis=1),
            dst_hot_ref[:, b * points : b * points + pair],
            (((1,), (1,)), ((), ())),
            preferred_element_type=f32,
        )
    land = land[:cells] + land[cells:]
    land_ref[...] = land
    for sent_ref in sent_refs:
        lengthen(sent_ref, land.astype(bf16))


def heat_kernel(rows, e2_ref, e4_ref, land_ref, _, *refs):
    parts = refs[:-3]
    sum_ref, near_ref, far_ref = refs[-3:]
    cells = land_ref.shape[0]
    columns = cells // rows * LANES
    even_x = lax.axis_index("gx") % 2 == 0
    even_y = lax.axis_index("gy") % 2 == 0
    total = land_ref[...]
    for part in parts:
        total = total + part[0:cells, :].astype(f32)
    sum_ref[...] = total

    def corners(row):
        start = row * 4 // 16 * 16
        one = e2_ref[start : start + 16, :].astype(f32)
        two = e4_ref[start : start + 16, :].astype(f32)
        low = jnp.where(even_y, two, one)
        high = jnp.where(even_y, one, two)
        at = row * 4 - start
        lines = [low[at + 1 : at + 2], low[at + 3 : at + 4], high[at : at + 1], high[at + 2 : at + 3]]
        heat = from_tiles(total, rows)[row : row + 1]
        blank = jnp.zeros((3, columns), f32)
        return to_tiles(jnp.concatenate([heat] + lines + [blank], axis=0))

    first, last = corners(0), corners(rows - 1)
    near_ref[...] = jnp.where(even_x, last, first).astype(bf16)
    far_ref[...] = jnp.where(even_x, first, last).astype(bf16)


def advance(ref, r, t, coefs, size):
    ring, columns = ref.shape[2:]
    whole = ref[r, t]
    up = pltpu.roll(whole, 1, 0)[:size]
    down = pltpu.roll(whole, ring - 1, 0)[:size]
    mid = whole[:size]
    total = coefs[0] * mid + coefs[5] * (up + down)
    total = total + coefs[1] * ref[r - 1, t, 0:size, :]
    total = total + coefs[2] * ref[r + 1, t, 0:size, :]
    total = total + coefs[3] * pltpu.roll(mid, 1, 1)
    return total + coefs[4] * pltpu.roll(mid, columns - 1, 1)


def first_step_kernel(
    groups_x, groups_y, paired, x_ref, wet_ref, diff_ref, y_ref, e1_ref, e3_ref,
    e2_ref, e4_ref, *refs,
):
    if not paired:
        pin_ref, qin_ref = refs[:2]
    zb_ref, c_ref, t1_ref, z_ref, t0_ref, w_ref = refs[-6:]
    _, rows, channels, columns = x_ref.shape
    row_group = lax.axis_index("gx")
    col_group = lax.axis_index("gy")
    is_atmos = lax.axis_index("comp") == 0

    @pl.when(is_atmos)
    def _():
        diff = channel_column(diff_ref[...], channels, col_group * channels)
        total = rows * groups_x
        base = (row_group * rows).astype(f32)
        for group, n, parts in wave_parts(columns):
            lam, alpha, sinh = decay_terms(diff, half_rates(group, n, LANES, columns))
            scale = 1.0 / (
                2.0 * diff * sinh * (1.0 - jnp.exp(-2.0 * (total + 1) * alpha))
            )
            lows, highs = edge_factors(lam, alpha, base, total, rows)
            for part in parts:
                lanes = slice(part, part + LANES)
                if paired:
                    pin = jnp.zeros((channels, LANES), f32)
                    qin = jnp.zeros((channels, LANES), f32)
                    for mask, msg in ((1, e1_ref), (2, e2_ref), (3, e3_ref)):
                        band = row_group ^ mask
                        gap = (jnp.abs(row_group - band) - 1) * rows
                        term = jnp.exp(-gap.astype(f32) * alpha)
                        term = term * msg[0:channels, lanes].astype(f32)
                        pin = pin + jnp.where(band < row_group, term, 0.0)
                        qin = qin + jnp.where(band > row_group, term, 0.0)
                else:
                    pin = pin_ref[:, lanes]
                    qin = qin_ref[:, lanes]
                f = pin
                for r in range(rows):
                    f = lam * f + lows[r] * y_ref[r, :, lanes]
                    z_ref[r] = highs[r] * f
                g = lam * qin
                for r in reversed(range(rows)):
                    z = scale * (z_ref[r] + lows[r] * g)
                    zb_ref[r * channels : (r + 1) * channels, lanes] = z.astype(bf16)
                    g = lam * (g + highs[r] * y_ref[r, :, lanes])

    @pl.when(jnp.logical_not(is_atmos))
    def _():
        levels = channels // 2
        ring = levels + 8
        lines = 2 * channels
        first_x = row_group == 0
        last_x = row_group == groups_x - 1
        top = col_group == 0
        bottom = col_group == groups_y - 1
        even_x = row_group % 2 == 0
        even_y = col_group % 2 == 0

        one = e1_ref[lines : lines + 16, :].astype(f32)
        three = e3_ref[lines : lines + 16, :].astype(f32)
        below = jnp.where(even_x, three, one)[rows - 2 : rows]
        above = jnp.where(even_x, one, three)[0:2]
        w_ref[0:2, :] = jnp.where(first_x, 0.0, below)
        w_ref[2 : rows + 2, :] = wet_ref[...].astype(f32)
        w_ref[rows + 2 : rows + 4, :] = jnp.where(last_x, 0.0, above)

        span = rows + 2
        north = w_ref[0:span, :]
        here = w_ref[1 : span + 1, :]
        south = w_ref[2 : span + 2, :]
        west = pltpu.roll(here, 1, 1)
        east = pltpu.roll(here, columns - 1, 1)
        c_ref[0, 0:span, :] = here * (
            1.0 - 2.0 * mixing_rate - spread_rate * (north + south + west + east)
        )
        c_ref[1, 0:span, :] = spread_rate * here * north
        c_ref[2, 0:span, :] = spread_rate * here * south
        c_ref[3, 0:span, :] = spread_rate * here * west
        c_ref[4, 0:span, :] = spread_rate * here * east
        c_ref[5, 0:span, :] = mixing_rate * here
        c_ref[6, 0:span, :] = here

        one = e1_ref[0:lines, :].astype(f32)
        three = e3_ref[0:lines, :].astype(f32)
        below = jnp.where(even_x, three, one)
        above = jnp.where(even_x, one, three)
        blank = jnp.zeros((8, columns), f32)
        for k in range(2):
            for t in range(2):
                c = k * channels + t * levels
                t0_ref[k, t, 0:levels, :] = below[c : c + levels]
                t0_ref[rows + 2 + k, t, 0:levels, :] = above[c : c + levels]
                t0_ref[k, t, levels:ring, :] = blank
                t0_ref[rows + 2 + k, t, levels:ring, :] = blank
        one = e2_ref[...].astype(f32)
        two = e4_ref[0 : 4 * rows, :].astype(f32)
        before = jnp.where(even_y, two, one)
        after = jnp.where(even_y, one, two)
        for r in range(rows):
            for t in range(2):
                k = (r * 2 + t) * 2
                t0_ref[r + 2, t, 0:levels, :] = x_ref[0, r, t * levels : (t + 1) * levels, :]
                t0_ref[r + 2, t, levels : levels + 2, :] = after[k : k + 2]
                t0_ref[r + 2, t, ring - 2 : ring, :] = before[k : k + 2]

        def close(ref, r):
            for t in range(2):
                ref[r, t, ring - 1 : ring, :] = jnp.where(
                    top, ref[r, t, 0:1, :], ref[r, t, ring - 1 : ring, :]
                )
                ref[r, t, levels : levels + 1, :] = jnp.where(
                    bottom, ref[r, t, levels - 1 : levels, :], ref[r, t, levels : levels + 1, :]
                )

        def first(r, carry):
            coefs = [c_ref[k, pl.ds(r, 1), :] for k in range(6)]
            close(t0_ref, r + 1)
            for t in range(2):
                t1_ref[r, t] = advance(t0_ref, r + 1, t, coefs, ring)
            close(t1_ref, r)
            return carry

        lax.fori_loop(0, span, first, 0)


def second_step_kernel(gain_ref, table_ref, zb_ref, c_ref, t1_ref, base_ref, column_ref):
    rows, channels, columns = base_ref.shape
    is_atmos = lax.axis_index("comp") == 0

    @pl.when(is_atmos)
    def _():
        response = channel_column(gain_ref[...], channels, lax.axis_index("gy") * channels)
        column_ref[...] = jnp.broadcast_to(response, column_ref.shape)
        half = columns // 2
        step = 256
        for n in range(0, half, step):
            even, odd = [
                jnp.dot(
                    zb_ref[:, k * half : (k + 1) * half],
                    table_ref[k * half : (k + 1) * half, n : n + step],
                    preferred_element_type=f32,
                ).reshape(rows, channels, step)
                for k in range(2)
            ]
            base_ref[:, :, n : n + step] = even + odd
            base_ref[:, :, n + half : n + half + step] = even - odd

    @pl.when(jnp.logical_not(is_atmos))
    def _():
        levels = channels // 2

        def second(r, carry):
            coefs = [c_ref[k, pl.ds(r, 1), :] for k in range(6)]
            for t in range(2):
                c = t * levels
                base_ref[r - 1, c : c + levels, :] = advance(t1_ref, r, t, coefs, levels)
            return carry

        lax.fori_loop(1, rows + 1, second, 0)


def last_kernel(
    groups_x, groups_y, column_ref, base_ref, c_ref, sum_ref, near_ref, far_ref, out_hbm,
    out_ref, e_ref, heat_ref, sem,
):
    rows, channels, columns = out_ref.shape
    row_group = lax.axis_index("gx")
    col_group = lax.axis_index("gy")
    is_atmos = lax.axis_index("comp") == 0
    copies = [
        pltpu.make_async_copy(out_ref.at[r], out_hbm.at[0, r], sem.at[r]) for r in range(rows)
    ]

    @pl.when(is_atmos)
    def _():
        for r in range(rows):
            for k in range(columns // LANES):
                lanes = slice(k * LANES, (k + 1) * LANES)
                at = k * rows + r
                out_ref[r, :, lanes] = (
                    base_ref[r, :, lanes] + column_ref[...] * sum_ref[at : at + 1, :]
                )
            copies[r].start()

    @pl.when(jnp.logical_not(is_atmos))
    def _():
        levels = channels // 2
        even = row_group % 2 == 0
        below = jnp.where(even, far_ref[...].astype(f32), near_ref[...].astype(f32))
        above = jnp.where(even, near_ref[...].astype(f32), far_ref[...].astype(f32))

        low = from_tiles(below, 8)
        high = from_tiles(above, 8)
        by_low = c_ref[1, 1:2, :] * (c_ref[5, 0:1, :] + c_ref[5, 1:2, :])
        by_high = c_ref[2, rows : rows + 1, :] * (
            c_ref[5, rows : rows + 1, :] + c_ref[5, rows + 1 : rows + 2, :]
        )
        has_before = jnp.where(col_group > 0, 1.0, 0.0)
        has_after = jnp.where(col_group < groups_y - 1, 1.0, 0.0)

        @pl.when(col_group == 0)
        def _():
            span = rows + 2
            e_ref[0:1, :] = low[0:1]
            e_ref[1 : rows + 1, :] = from_tiles(sum_ref[...], rows)
            e_ref[rows + 1 : span, :] = high[0:1]
            e_ref[0:span, :] = c_ref[6, 0:span, :] * e_ref[0:span, :]
            own = slice(1, rows + 1)
            heat = e_ref[own, :]
            second = c_ref[5, own, :] * heat
            first = (c_ref[0, own, :] + 1.0) * heat + second
            first = first + c_ref[1, own, :] * e_ref[0:rows, :]
            first = first + c_ref[2, own, :] * e_ref[2 : rows + 2, :]
            first = first + c_ref[3, own, :] * pltpu.roll(heat, 1, 1)
            first = first + c_ref[4, own, :] * pltpu.roll(heat, columns - 1, 1)
            heat_ref[0] = first
            heat_ref[1] = second

        for r in [1, rows - 2] + list(range(2, rows - 2)) + [0, rows - 1]:
            out_ref[r] = base_ref[r]
            for t in range(2):
                c = t * levels
                for edge, factor, lines in ((0, by_low, low), (rows - 1, by_high, high)):
                    if r == edge:
                        out_ref[r, c : c + 1, :] = out_ref[r, c : c + 1, :] + (
                            has_before * factor * lines[t + 1 : t + 2]
                        )
                        d = c + levels - 1
                        out_ref[r, d : d + 1, :] = out_ref[r, d : d + 1, :] + (
                            has_after * factor * lines[t + 3 : t + 4]
                        )

            @pl.when(col_group == 0)
            def _():
                for t, gain in enumerate((heat_gain, salt_gain)):
                    c = t * levels
                    for k in range(2):
                        out_ref[r, c + k : c + k + 1, :] = (
                            out_ref[r, c + k : c + k + 1, :] + gain * heat_ref[k, r : r + 1, :]
                        )

            copies[r].start()

    for copy in copies:
        copy.wait()


def local(
    fields,
    wet_cells,
    flux_weight,
    variable_sea_response,
    diffusivity,
    a2o_source,
    a2o_target,
    a2o_count,
    a2o_weight,
    marine_air_input_index,
    marine_air_output_index,
    marine_air_piece_tally,
    marine_air_piece_factor,
):
    _, rows, channels, columns = fields.shape
    groups_x = lax.axis_size("gx")
    groups_y = lax.axis_size("gy")
    blocks, points = a2o_source.shape[2:]
    cells = rows * columns // LANES
    forward, inverse = fourier_tables(columns)
    flux_row = flux_weight[None, :]
    gain_row = variable_sea_response[None, :]
    diff_row = diffusivity[None, :]
    paired = groups_x == 4
    params = functools.partial(pltpu.CompilerParams, vmem_limit_bytes=40 * 2**20)
    vmem = pl.BlockSpec(memory_space=pltpu.VMEM)
    smem = pl.BlockSpec(memory_space=pltpu.SMEM)
    hbm = pl.BlockSpec(memory_space=pltpu.HBM)
    anywhere = pl.BlockSpec(memory_space=pl.ANY)

    def shape(dims, dtype):
        return jax.ShapeDtypeStruct(dims, dtype)

    lines = 2 * channels + 16
    shapes = [
        shape((cells, LANES), bf16),
        shape((cells + 16, LANES), bf16),
        shape((rows, channels, columns), f32),
        shape((lines, columns), bf16),
        shape((lines, columns), bf16),
        shape((4 * rows, columns), bf16),
        shape((4 * rows, columns), bf16),
    ]
    if not paired:
        shapes.append(shape((2, channels, columns), bf16))
    coarse, wide, y, e1, e3, e2, e4, *sums = pl.pallas_call(
        functools.partial(start_kernel, groups_x, paired),
        out_shape=shapes,
        in_specs=[hbm] * 5,
        out_specs=[hbm] * len(shapes),
        scratch_shapes=[pltpu.VMEM(out.shape, out.dtype) for out in shapes]
        + [
            pltpu.VMEM((rows, channels, columns), f32),
            pltpu.VMEM((rows, columns), jnp.int32),
            pltpu.VMEM(flux_row.shape, f32),
            pltpu.VMEM(diff_row.shape, f32),
            pltpu.VMEM(forward.shape, bf16),
            pltpu.VMEM((rows * channels, columns), bf16),
            pltpu.VMEM((rows, columns), f32),
            pltpu.VMEM((4 * rows, columns), f32),
            pltpu.VMEM((columns // 2 // LANES, 2 * rows + 1, channels, LANES), f32),
            pltpu.SemaphoreType.DMA((rows,)),
            pltpu.SemaphoreType.DMA((3,)),
            pltpu.SemaphoreType.DMA((rows + len(shapes) - 1,)),
        ],
        compiler_params=pltpu.CompilerParams(vmem_limit_bytes=58 * 2**20),
        name="surface_and_forward_or_halos",
    )(fields, wet_cells, flux_row, diff_row, forward)

    masks = [1 << bit for bit in range(groups_y.bit_length() - 1)]

    def sum_route(mask):
        return [(j, j ^ mask) for j in range(groups_y)]

    def partner_route(mask):
        return both_ways([(j, groups_y + (j ^ mask)) for j in range(groups_y)])

    surface = lax.ppermute(coarse, ("comp", "gy"), partner_route(0)).astype(f32)
    for mask in masks[:1]:
        far = lax.ppermute(wide, ("comp", "gy"), partner_route(mask))
        surface = surface + far[:cells].astype(f32)
    coarse = surface.astype(bf16)
    for mask in masks[1:-1]:
        surface = surface + lax.ppermute(coarse, "gy", sum_route(mask)).astype(f32)
        coarse = surface.astype(bf16)
    surfaces = [surface] + [
        lax.ppermute(coarse, "gy", sum_route(mask)) for mask in masks[1:][-1:]
    ]

    def ring_pairs(count, odd):
        return [(a, (a + 1) % count) for a in range(odd, count, 2)]

    def flat(comp, i, j):
        return (comp * groups_x + i) * groups_y + j

    def level_route(odd):
        pairs = []
        for i in range(groups_x):
            linked = [(a, a + 1) for a in range(odd, groups_y - 1, 2)]
            alone = set(range(groups_y)) - {j for pair in linked for j in pair}
            pairs += [(flat(1, i, a), flat(1, i, b)) for a, b in linked]
            if i % 2 == 0:
                pairs += [(flat(1, i, j), flat(1, i + 1, j)) for j in sorted(alone)]
                if odd or not paired:
                    pairs += [(flat(0, i, j), flat(0, i + 1, j)) for j in range(groups_y)]
            if paired and not odd and i < i ^ 2:
                pairs += [(flat(0, i, j), flat(0, i ^ 2, j)) for j in range(groups_y)]
        return both_ways(pairs)

    e1, coarse = lax.optimization_barrier((e1, coarse))
    e1 = lax.ppermute(e1, "gx", both_ways(ring_pairs(groups_x, 0)))
    e3 = lax.ppermute(e3, "gx", both_ways(ring_pairs(groups_x, 1)))
    axes = ("comp", "gx", "gy")
    e2 = lax.ppermute(e2, axes, level_route(0))
    e4 = lax.ppermute(e4, axes, level_route(1))

    one_hots = pl.pallas_call(
        functools.partial(one_hot_kernel, rows, columns),
        out_shape=[
            shape((LANES, blocks * points), bf16),
            shape((LANES, blocks * points), bf16),
            shape((blocks, points), jnp.int32),
            shape((blocks, points), jnp.int32),
        ],
        in_specs=[vmem] * 4 + [anywhere],
        out_specs=[vmem] * 4,
        compiler_params=params(),
        name="one_hots",
    )(a2o_source, a2o_target, marine_air_input_index, marine_air_output_index, coarse)
    landing, *sent = pl.pallas_call(
        functools.partial(regrid_kernel, len(surfaces)),
        out_shape=[shape((cells, LANES), f32)]
        + [shape((cells + 16 * (mask - 1), LANES), bf16) for mask in range(1, groups_y)],
        in_specs=[vmem] * (len(surfaces) + 4) + [smem, smem, hbm, hbm] + [anywhere] * 4,
        out_specs=[vmem] * groups_y,
        scratch_shapes=[
            pltpu.VMEM((blocks, points, points), bf16),
            pltpu.VMEM((blocks, points), f32),
            pltpu.VMEM((blocks, points), f32),
            pltpu.SemaphoreType.DMA,
        ],
        compiler_params=params(),
        name="regrid_blocks",
    )(
        *surfaces, *one_hots, a2o_count, marine_air_piece_tally,
        a2o_weight, marine_air_piece_factor, e1, e3, e2, e4,
    )

    def landing_route(mask):
        pairs = [
            (flat(0, i, j), flat(0, i, j ^ mask))
            for i in range(groups_x)
            for j in range(groups_y)
            if j < j ^ mask
        ]
        pairs += [(flat(1, i, 0), flat(1, i, mask)) for i in range(groups_x)]
        pairs += [
            (flat(1, i, j), flat(1, i + 1, j))
            for i in range(0, groups_x, 2)
            for j in range(groups_y)
            if j not in (0, mask)
        ]
        return both_ways(pairs)

    parts = [
        lax.ppermute(block, axes, landing_route(mask)) for mask, block in enumerate(sent, 1)
    ]

    extra = []
    if not paired:
        p, q = jnp.moveaxis(lax.all_gather(sums[0], "gx").astype(f32), 1, 0)
        viscous = lax.dynamic_slice_in_dim(
            diffusivity, lax.axis_index("gy") * channels, channels
        )[:, None]
        rates = [half_rates(g, 0, columns // 4, columns) for g in (0, 0, 1, 1)]
        _, alpha, _ = decay_terms(viscous, jnp.concatenate(rates, axis=1))
        gap = lax.axis_index("gx") - jnp.arange(groups_x)
        decay = jnp.exp(
            -(rows * jnp.maximum(jnp.abs(gap) - 1, 0))[:, None, None] * alpha[None]
        )
        extra = [
            jnp.sum(jnp.where((gap > 0)[:, None, None], decay * p, 0.0), axis=0),
            jnp.sum(jnp.where((gap < 0)[:, None, None], decay * q, 0.0), axis=0),
        ]
    ring = channels // 2 + 8
    damped, coefs, stepped = pl.pallas_call(
        functools.partial(first_step_kernel, groups_x, groups_y, paired),
        out_shape=[
            shape((rows * channels, columns), bf16),
            shape((7, 16, columns), f32),
            shape((rows + 2, 2, ring, columns), f32),
        ],
        in_specs=[vmem] * (8 + len(extra)),
        out_specs=[vmem] * 3,
        scratch_shapes=[
            pltpu.VMEM((rows, channels, LANES), f32),
            pltpu.VMEM((rows + 4, 2, ring, columns), f32),
            pltpu.VMEM((16, columns), f32),
        ],
        compiler_params=params(),
        name="damping_or_first_step",
    )(fields, wet_cells, diff_row, y, e1, e3, e2, e4, *extra)

    surface_sum, near, far = pl.pallas_call(
        functools.partial(heat_kernel, rows),
        out_shape=[
            shape((cells, LANES), f32),
            shape((columns // 16, LANES), bf16),
            shape((columns // 16, LANES), bf16),
        ],
        in_specs=[vmem] * 3 + [anywhere] + [vmem] * len(parts),
        out_specs=[vmem] * 3,
        compiler_params=params(),
        name="surface_sum",
    )(e2, e4, landing, coefs, *parts)

    near = lax.ppermute(near, "gx", both_ways(ring_pairs(groups_x, 0)))
    far = lax.ppermute(far, "gx", both_ways(ring_pairs(groups_x, 1)))
    base, column = pl.pallas_call(
        second_step_kernel,
        out_shape=[shape((rows, channels, columns), f32), shape((channels, LANES), f32)],
        in_specs=[vmem] * 5,
        out_specs=[vmem] * 2,
        compiler_params=params(),
        name="inverse_or_second_step",
    )(gain_row, inverse, damped, coefs, stepped)
    return pl.pallas_call(
        functools.partial(last_kernel, groups_x, groups_y),
        out_shape=shape(fields.shape, f32),
        in_specs=[vmem] * 6,
        out_specs=hbm,
        scratch_shapes=[
            pltpu.VMEM((rows, channels, columns), f32),
            pltpu.VMEM((16, columns), f32),
            pltpu.VMEM((2, rows, columns), f32),
            pltpu.SemaphoreType.DMA((rows,)),
        ],
        compiler_params=params(),
        name="add_surface_terms",
    )(column, base, coefs, surface_sum, near, far)


def solution(mesh):
    in_specs = (
        P("comp", "gx", "gy", None),
        P("gx", None),
        P(),
        P(),
        P(),
        P("gx", "gy", None, None),
        P("gx", "gy", None, None),
        P("gx", "gy"),
        P("gx", "gy", None, None, None),
        P("gx", "gy", None, None),
        P("gx", "gy", None, None),
        P("gx", "gy"),
        P("gx", "gy", None, None, None),
    )
    out_specs = P("comp", "gx", "gy", None)
    return jax.shard_map(local, mesh=mesh, in_specs=in_specs, out_specs=out_specs, check_vma=False)
```

```python
import functools

import jax
import jax.numpy as jnp
import numpy as np
from jax import lax
from jax.experimental import pallas as pl
from jax.experimental.pallas import tpu as pltpu
from jax.sharding import PartitionSpec as P

spread_rate = 0.2
mixing_rate = 0.1
heat_gain = 0.5
salt_gain = -0.25
LANES = 128
f32 = jnp.float32
bf16 = jnp.bfloat16


def fourier_tables(columns):
    half = columns // 2
    forward, inverse = [], []
    for first in (0, 1):
        waves = np.arange(first, half, 2)
        phase = np.arange(half)[:, None] * waves[None, :] % columns
        angles = phase * (2.0 * np.pi / columns)
        table = np.concatenate([np.cos(angles), np.sin(angles)], axis=1)
        weight = np.where(waves == 0, 1.0, 2.0) / columns
        forward.append(table)
        inverse.append(table.T * np.concatenate([weight, weight])[:, None])
    return (
        jnp.asarray(np.concatenate(forward).astype(np.float32), bf16),
        jnp.asarray(np.concatenate(inverse).astype(np.float32), bf16),
    )


def wave_parts(columns):
    quarter = columns // 4
    return [
        (g, n, (g * 2 * quarter + n, (g * 2 + 1) * quarter + n))
        for g in (0, 1)
        for n in range(0, quarter, LANES)
    ]


def half_rates(group, first, count, columns):
    lane = lax.broadcasted_iota(jnp.int32, (1, count), 1) + first
    wave = (2 * lane + group).astype(f32)
    sine = jnp.sin(wave * (np.pi / columns))
    return 2.0 * sine * sine


def both_ways(pairs):
    return [p for a, b in pairs for p in ((a, b), (b, a))]


def channel_column(row, channels, first):
    n = row.shape[1]
    lane = lax.broadcasted_iota(jnp.int32, (channels, n), 1)
    sub = lax.broadcasted_iota(jnp.int32, (channels, n), 0)
    return jnp.sum(jnp.where(lane == sub + first, row, 0.0), axis=1, keepdims=True)


def to_tiles(surface):
    cols = surface.shape[1]
    return jnp.concatenate(
        [surface[:, k : k + LANES] for k in range(0, cols, LANES)], axis=0
    )


def from_tiles(tiles, rows):
    return jnp.concatenate(
        [tiles[k : k + rows] for k in range(0, tiles.shape[0], rows)], axis=1
    )


def lengthen(ref, block):
    rows = block.shape[0]
    ref[0:rows, :] = block
    if ref.shape[0] > rows:
        ref[rows:, :] = block[: ref.shape[0] - rows]


def decay_terms(diff_column, rates):
    half = 0.5 / diff_column + rates
    sinh = jnp.sqrt(half * (half + 2.0))
    grow = 1.0 + half + sinh
    return 1.0 / grow, jnp.log(grow), sinh


def edge_factors(lam, alpha, base, total, rows):
    lam2 = lam * lam
    powers = [
        jnp.exp(-2.0 * base * alpha) * lam2,
        jnp.exp(-2.0 * (total - rows - base) * alpha) * lam2,
    ]
    lows, highs = [], []
    for _ in range(rows):
        lows.append(1.0 - powers[0])
        highs.insert(0, 1.0 - powers[1])
        powers = [power * lam2 for power in powers]
    return lows, highs


def start_kernel(
    groups_x, paired, x_hbm, wet_hbm, flux_hbm, diff_hbm, table_hbm, *refs
):
    outs = 7 if paired else 8
    coarse_hbm, wide_hbm, y_hbm, *message_hbm = refs[:outs]
    coarse_ref, wide_ref, y_ref, *message_ref = refs[outs : 2 * outs]
    e1_ref, e3_ref, e2_ref, e4_ref = message_ref[:4]
    if not paired:
        pq_ref = message_ref[4]
    (
        x_ref, wet_ref, flux_ref, diff_ref, table_ref, flat_ref, row_ref, edge_ref,
        factor_ref, x_sem, sem, out_sem,
    ) = refs[2 * outs :]
    rows, channels, columns = x_ref.shape
    half = columns // 2
    row_group = lax.axis_index("gx")
    col_group = lax.axis_index("gy")
    is_atmos = lax.axis_index("comp") == 0

    x_copies = [
        pltpu.make_async_copy(x_hbm.at[0, r], x_ref.at[r], x_sem.at[r]) for r in range(rows)
    ]
    surface_copies = [
        pltpu.make_async_copy(coarse_ref, coarse_hbm, out_sem.at[0]),
        pltpu.make_async_copy(wide_ref, wide_hbm, out_sem.at[1]),
    ]
    y_copies = [
        pltpu.make_async_copy(y_ref.at[r], y_hbm.at[r], out_sem.at[2 + r]) for r in range(rows)
    ]
    message_copies = [
        pltpu.make_async_copy(ref, hbm, out_sem.at[2 + rows + k])
        for k, (ref, hbm) in enumerate(zip(message_ref, message_hbm))
    ]

    def send_surface():
        coarse = to_tiles(row_ref[...]).astype(bf16)
        coarse_ref[...] = coarse
        lengthen(wide_ref, coarse)
        for copy in surface_copies:
            copy.start()

    @pl.when(is_atmos)
    def _():
        flux_copy = pltpu.make_async_copy(flux_hbm, flux_ref, sem.at[0])
        diff_copy = pltpu.make_async_copy(diff_hbm, diff_ref, sem.at[1])
        table_copy = pltpu.make_async_copy(table_hbm, table_ref, sem.at[2])
        for copy in [flux_copy, diff_copy] + x_copies + [table_copy]:
            copy.start()
        first = col_group * channels
        flux_copy.wait()
        weight = channel_column(flux_ref[...], channels, first)
        diff_copy.wait()
        diff = channel_column(diff_ref[...], channels, first)
        total = rows * groups_x
        base = (row_group * rows).astype(f32)
        tiles = wave_parts(columns)
        for k, (group, n, _) in enumerate(tiles):
            lam, alpha, _ = decay_terms(diff, half_rates(group, n, LANES, columns))
            factor_ref[k, 0] = lam
            lows, highs = edge_factors(lam, alpha, base, total, rows)
            for r in range(rows):
                factor_ref[k, 1 + r] = lows[r]
                factor_ref[k, 1 + rows + r] = highs[r]
        for r in range(rows):
            x_copies[r].wait()
            row_ref[r : r + 1, :] = jnp.sum(x_ref[r] * weight, axis=0, keepdims=True)
            left, right = x_ref[r, :, :half], x_ref[r, :, half:]
            flat_ref[r * channels : (r + 1) * channels, :half] = (left + right).astype(bf16)
            flat_ref[r * channels : (r + 1) * channels, half:] = (left - right).astype(bf16)
        send_surface()
        table_copy.wait()
        for k in range(2):
            lanes = slice(k * half, (k + 1) * half)
            part = jnp.dot(
                flat_ref[:, lanes], table_ref[lanes, :], preferred_element_type=f32
            )
            y_ref[:, :, lanes] = part.reshape(rows, channels, half)
            for tile, (group, _, parts) in enumerate(tiles):
                if group != k:
                    continue
                lam = factor_ref[tile, 0]
                for at in parts:
                    lanes = slice(at, at + LANES)
                    here = slice(at - k * half, at - k * half + LANES)
                    p = factor_ref[tile, 1] * part[0:channels, here]
                    q = factor_ref[tile, 2 * rows] * part[(rows - 1) * channels :, here]
                    for r in range(1, rows):
                        up = part[r * channels : (r + 1) * channels, here]
                        down = part[(rows - 1 - r) * channels : (rows - r) * channels, here]
                        p = lam * p + factor_ref[tile, 1 + r] * up
                        q = lam * q + factor_ref[tile, 2 * rows - r] * down
                    if paired:
                        for mask, out in ((1, e1_ref), (2, e2_ref), (3, e3_ref)):
                            upward = row_group < (row_group ^ mask)
                            out[0:channels, lanes] = jnp.where(upward, p, q).astype(bf16)
                    else:
                        pq_ref[0, :, lanes] = p.astype(bf16)
                        pq_ref[1, :, lanes] = q.astype(bf16)
        for copy in y_copies:
            copy.start()
        for copy in message_copies:
            copy.start()
        for copy in surface_copies + y_copies + message_copies:
            copy.wait()

    @pl.when(jnp.logical_not(is_atmos))
    def _():
        wet_copy = pltpu.make_async_copy(wet_hbm, wet_ref, sem.at[0])
        for copy in x_copies + [wet_copy]:
            copy.start()
        gain = jnp.where(col_group == 0, 1.0, 0.0)
        for r in range(rows):
            x_copies[r].wait()
            row_ref[r : r + 1, :] = x_ref[r, 0:1, :] * gain
        send_surface()
        wet_copy.wait()
        levels = channels // 2
        lines = 2 * channels
        even_x = row_group % 2 == 0
        even_y = col_group % 2 == 0
        wet = wet_ref[...].astype(f32)
        wet = jnp.concatenate([wet, wet], axis=0).astype(bf16)

        def put(out, last):
            @pl.when(last)
            def _():
                out[0:lines, :] = x_ref[rows - 2 :].reshape(lines, columns).astype(bf16)

            @pl.when(jnp.logical_not(last))
            def _():
                out[0:lines, :] = x_ref[:2].reshape(lines, columns).astype(bf16)

            out[lines : lines + 16, :] = wet

        put(e1_ref, even_x)
        put(e3_ref, jnp.logical_not(even_x))

        def put_edges(out, level):
            for r in range(rows):
                for t in range(2):
                    at = (r * 2 + t) * 2
                    c = t * levels + level
                    edge_ref[at : at + 2, :] = x_ref[r, c : c + 2, :]
            out[0 : rows * 4, :] = edge_ref[...].astype(bf16)

        @pl.when(even_y)
        def _():
            put_edges(e2_ref, levels - 2)
            put_edges(e4_ref, 0)

        @pl.when(jnp.logical_not(even_y))
        def _():
            put_edges(e2_ref, 0)
            put_edges(e4_ref, levels - 2)

        for copy in message_copies:
            copy.start()
        for copy in surface_copies + message_copies:
            copy.wait()


def one_hot_kernel(
    rows, columns, a_src, a_dst, m_src, m_dst, _, src_hot_ref, dst_hot_ref, src_row_ref, dst_row_ref
):
    is_atmos = lax.axis_index("comp") == 0
    blocks, points = src_row_ref.shape
    lane_iota = lax.broadcasted_iota(jnp.int32, (LANES, points), 0)
    for a_ref, m_ref, hot_ref, row_ref in (
        (a_src, m_src, src_hot_ref, src_row_ref),
        (a_dst, m_dst, dst_hot_ref, dst_row_ref),
    ):
        index = jnp.where(is_atmos, m_ref[0, 0], a_ref[0, 0])
        row = index // columns
        tile = (index // LANES) % (columns // LANES)
        row_ref[...] = tile * rows + row
        lane = index % LANES
        for b in range(blocks):
            hot_ref[:, b * points : (b + 1) * points] = jnp.where(
                lane_iota == lane[b : b + 1], 1.0, 0.0
            ).astype(bf16)


def regrid_kernel(n_surfaces, *refs):
    surfaces = refs[:n_surfaces]
    (
        src_hot_ref, dst_hot_ref, src_row_ref, dst_row_ref, a_count, m_count, a_weight, m_weight,
        _,
        *refs,
    ) = refs[n_surfaces:]
    land_ref, *sent_refs = refs[:-4]
    weight_ref, gath_ref, val_ref, sem = refs[-4:]
    is_atmos = lax.axis_index("comp") == 0
    blocks, points = val_ref.shape
    cells = surfaces[0].shape[0]

    @pl.when(is_atmos)
    def _():
        pltpu.make_async_copy(m_weight.at[0, 0], weight_ref, sem).start()

    @pl.when(jnp.logical_not(is_atmos))
    def _():
        pltpu.make_async_copy(a_weight.at[0, 0], weight_ref, sem).start()

    count = jnp.where(is_atmos, m_count[0, 0], a_count[0, 0])
    pair = 2 * points
    row_iota = lax.broadcasted_iota(jnp.int32, (cells, points), 0)
    table = sum(surface[...].astype(f32) for surface in surfaces).astype(bf16)
    for b in range(0, blocks, 2):
        picked = jnp.dot(
            table, src_hot_ref[:, b * points : b * points + pair], preferred_element_type=f32
        )
        for k in range(2):
            mine = row_iota == src_row_ref[b + k : b + k + 1, :]
            part = jnp.where(mine, picked[:, k * points : (k + 1) * points], 0.0)
            gath_ref[b + k : b + k + 1, :] = jnp.sum(part, axis=0, keepdims=True)
    gathered = gath_ref[...].astype(bf16)

    @pl.when(is_atmos)
    def _():
        pltpu.make_async_copy(m_weight.at[0, 0], weight_ref, sem).wait()

    @pl.when(jnp.logical_not(is_atmos))
    def _():
        pltpu.make_async_copy(a_weight.at[0, 0], weight_ref, sem).wait()

    block_iota = lax.broadcasted_iota(jnp.int32, (blocks, points), 0)
    values = jnp.zeros((blocks, points), f32)
    for b in range(0, blocks, 2):
        terms = lax.dot_general(
            gathered,
            weight_ref[b : b + 2].reshape(pair, points),
            (((1,), (1,)), ((), ())),
            preferred_element_type=f32,
        )
        for k in range(2):
            values = jnp.where(block_iota == b + k, terms[:, k * points : (k + 1) * points], values)
    val_ref[...] = jnp.where(block_iota < count, values, 0.0)
    land = jnp.zeros((2 * cells, LANES), f32)
    for b in range(0, blocks, 2):
        spread = []
        for k in range(b, b + 2):
            value = val_ref[k : k + 1, :]
            coarse = value.astype(bf16).astype(f32)
            fine = value - coarse
            mine = row_iota == dst_row_ref[k : k + 1, :]
            spread.append(
                jnp.concatenate(
                    [jnp.where(mine, coarse, 0.0), jnp.where(mine, fine, 0.0)], axis=0
                ).astype(bf16)
            )
        land = land + lax.dot_general(
            jnp.concatenate(spread, axis=1),
            dst_hot_ref[:, b * points : b * points + pair],
            (((1,), (1,)), ((), ())),
            preferred_element_type=f32,
        )
    land = land[:cells] + land[cells:]
    land_ref[...] = land
    for sent_ref in sent_refs:
        lengthen(sent_ref, land.astype(bf16))


def heat_kernel(rows, e2_ref, e4_ref, land_ref, _, *refs):
    parts = refs[:-3]
    sum_ref, near_ref, far_ref = refs[-3:]
    cells = land_ref.shape[0]
    columns = cells // rows * LANES
    even_x = lax.axis_index("gx") % 2 == 0
    even_y = lax.axis_index("gy") % 2 == 0
    total = land_ref[...]
    for part in parts:
        total = total + part[0:cells, :].astype(f32)
    sum_ref[...] = total

    def corners(row):
        start = row * 4 // 16 * 16
        one = e2_ref[start : start + 16, :].astype(f32)
        two = e4_ref[start : start + 16, :].astype(f32)
        low = jnp.where(even_y, two, one)
        high = jnp.where(even_y, one, two)
        at = row * 4 - start
        lines = [low[at + 1 : at + 2], low[at + 3 : at + 4], high[at : at + 1], high[at + 2 : at + 3]]
        heat = from_tiles(total, rows)[row : row + 1]
        blank = jnp.zeros((3, columns), f32)
        return to_tiles(jnp.concatenate([heat] + lines + [blank], axis=0))

    first, last = corners(0), corners(rows - 1)
    near_ref[...] = jnp.where(even_x, last, first).astype(bf16)
    far_ref[...] = jnp.where(even_x, first, last).astype(bf16)


def advance(ref, r, t, coefs, size):
    ring, columns = ref.shape[2:]
    whole = ref[r, t]
    up = pltpu.roll(whole, 1, 0)[:size]
    down = pltpu.roll(whole, ring - 1, 0)[:size]
    mid = whole[:size]
    total = coefs[0] * mid + coefs[5] * (up + down)
    total = total + coefs[1] * ref[r - 1, t, 0:size, :]
    total = total + coefs[2] * ref[r + 1, t, 0:size, :]
    total = total + coefs[3] * pltpu.roll(mid, 1, 1)
    return total + coefs[4] * pltpu.roll(mid, columns - 1, 1)


def first_step_kernel(
    groups_x, groups_y, paired, x_ref, wet_ref, diff_ref, y_ref, e1_ref, e3_ref,
    e2_ref, e4_ref, *refs,
):
    if not paired:
        pin_ref, qin_ref = refs[:2]
    zb_ref, c_ref, t1_ref, z_ref, t0_ref, w_ref = refs[-6:]
    _, rows, channels, columns = x_ref.shape
    row_group = lax.axis_index("gx")
    col_group = lax.axis_index("gy")
    is_atmos = lax.axis_index("comp") == 0

    @pl.when(is_atmos)
    def _():
        diff = channel_column(diff_ref[...], channels, col_group * channels)
        total = rows * groups_x
        base = (row_group * rows).astype(f32)
        for group, n, parts in wave_parts(columns):
            lam, alpha, sinh = decay_terms(diff, half_rates(group, n, LANES, columns))
            scale = 1.0 / (
                2.0 * diff * sinh * (1.0 - jnp.exp(-2.0 * (total + 1) * alpha))
            )
            lows, highs = edge_factors(lam, alpha, base, total, rows)
            for part in parts:
                lanes = slice(part, part + LANES)
                if paired:
                    pin = jnp.zeros((channels, LANES), f32)
                    qin = jnp.zeros((channels, LANES), f32)
                    for mask, msg in ((1, e1_ref), (2, e2_ref), (3, e3_ref)):
                        band = row_group ^ mask
                        gap = (jnp.abs(row_group - band) - 1) * rows
                        term = jnp.exp(-gap.astype(f32) * alpha)
                        term = term * msg[0:channels, lanes].astype(f32)
                        pin = pin + jnp.where(band < row_group, term, 0.0)
                        qin = qin + jnp.where(band > row_group, term, 0.0)
                else:
                    pin = pin_ref[:, lanes]
                    qin = qin_ref[:, lanes]
                f = pin
                for r in range(rows):
                    f = lam * f + lows[r] * y_ref[r, :, lanes]
                    z_ref[r] = highs[r] * f
                g = lam * qin
                for r in reversed(range(rows)):
                    z = scale * (z_ref[r] + lows[r] * g)
                    zb_ref[r * channels : (r + 1) * channels, lanes] = z.astype(bf16)
                    g = lam * (g + highs[r] * y_ref[r, :, lanes])

    @pl.when(jnp.logical_not(is_atmos))
    def _():
        levels = channels // 2
        ring = levels + 8
        lines = 2 * channels
        first_x = row_group == 0
        last_x = row_group == groups_x - 1
        top = col_group == 0
        bottom = col_group == groups_y - 1
        even_x = row_group % 2 == 0
        even_y = col_group % 2 == 0

        one = e1_ref[lines : lines + 16, :].astype(f32)
        three = e3_ref[lines : lines + 16, :].astype(f32)
        below = jnp.where(even_x, three, one)[rows - 2 : rows]
        above = jnp.where(even_x, one, three)[0:2]
        w_ref[0:2, :] = jnp.where(first_x, 0.0, below)
        w_ref[2 : rows + 2, :] = wet_ref[...].astype(f32)
        w_ref[rows + 2 : rows + 4, :] = jnp.where(last_x, 0.0, above)

        span = rows + 2
        north = w_ref[0:span, :]
        here = w_ref[1 : span + 1, :]
        south = w_ref[2 : span + 2, :]
        west = pltpu.roll(here, 1, 1)
        east = pltpu.roll(here, columns - 1, 1)
        c_ref[0, 0:span, :] = here * (
            1.0 - 2.0 * mixing_rate - spread_rate * (north + south + west + east)
        )
        c_ref[1, 0:span, :] = spread_rate * here * north
        c_ref[2, 0:span, :] = spread_rate * here * south
        c_ref[3, 0:span, :] = spread_rate * here * west
        c_ref[4, 0:span, :] = spread_rate * here * east
        c_ref[5, 0:span, :] = mixing_rate * here
        c_ref[6, 0:span, :] = here

        one = e1_ref[0:lines, :].astype(f32)
        three = e3_ref[0:lines, :].astype(f32)
        below = jnp.where(even_x, three, one)
        above = jnp.where(even_x, one, three)
        blank = jnp.zeros((8, columns), f32)
        for k in range(2):
            for t in range(2):
                c = k * channels + t * levels
                t0_ref[k, t, 0:levels, :] = below[c : c + levels]
                t0_ref[rows + 2 + k, t, 0:levels, :] = above[c : c + levels]
                t0_ref[k, t, levels:ring, :] = blank
                t0_ref[rows + 2 + k, t, levels:ring, :] = blank
        one = e2_ref[...].astype(f32)
        two = e4_ref[0 : 4 * rows, :].astype(f32)
        before = jnp.where(even_y, two, one)
        after = jnp.where(even_y, one, two)
        for r in range(rows):
            for t in range(2):
                k = (r * 2 + t) * 2
                t0_ref[r + 2, t, 0:levels, :] = x_ref[0, r, t * levels : (t + 1) * levels, :]
                t0_ref[r + 2, t, levels : levels + 2, :] = after[k : k + 2]
                t0_ref[r + 2, t, ring - 2 : ring, :] = before[k : k + 2]

        def close(ref, r):
            for t in range(2):
                ref[r, t, ring - 1 : ring, :] = jnp.where(
                    top, ref[r, t, 0:1, :], ref[r, t, ring - 1 : ring, :]
                )
                ref[r, t, levels : levels + 1, :] = jnp.where(
                    bottom, ref[r, t, levels - 1 : levels, :], ref[r, t, levels : levels + 1, :]
                )

        def first(r, carry):
            coefs = [c_ref[k, pl.ds(r, 1), :] for k in range(6)]
            close(t0_ref, r + 1)
            for t in range(2):
                t1_ref[r, t] = advance(t0_ref, r + 1, t, coefs, ring)
            close(t1_ref, r)
            return carry

        lax.fori_loop(0, span, first, 0)


def second_step_kernel(gain_ref, table_ref, zb_ref, c_ref, t1_ref, base_ref, column_ref):
    rows, channels, columns = base_ref.shape
    is_atmos = lax.axis_index("comp") == 0

    @pl.when(is_atmos)
    def _():
        response = channel_column(gain_ref[...], channels, lax.axis_index("gy") * channels)
        column_ref[...] = jnp.broadcast_to(response, column_ref.shape)
        half = columns // 2
        step = 256
        for n in range(0, half, step):
            even, odd = [
                jnp.dot(
                    zb_ref[:, k * half : (k + 1) * half],
                    table_ref[k * half : (k + 1) * half, n : n + step],
                    preferred_element_type=f32,
                ).reshape(rows, channels, step)
                for k in range(2)
            ]
            base_ref[:, :, n : n + step] = even + odd
            base_ref[:, :, n + half : n + half + step] = even - odd

    @pl.when(jnp.logical_not(is_atmos))
    def _():
        levels = channels // 2

        def second(r, carry):
            coefs = [c_ref[k, pl.ds(r, 1), :] for k in range(6)]
            for t in range(2):
                c = t * levels
                base_ref[r - 1, c : c + levels, :] = advance(t1_ref, r, t, coefs, levels)
            return carry

        lax.fori_loop(1, rows + 1, second, 0)


def last_kernel(
    groups_x, groups_y, column_ref, base_ref, c_ref, sum_ref, near_ref, far_ref, out_hbm,
    out_ref, e_ref, heat_ref, sem,
):
    rows, channels, columns = out_ref.shape
    row_group = lax.axis_index("gx")
    col_group = lax.axis_index("gy")
    is_atmos = lax.axis_index("comp") == 0
    copies = [
        pltpu.make_async_copy(out_ref.at[r], out_hbm.at[0, r], sem.at[r]) for r in range(rows)
    ]

    @pl.when(is_atmos)
    def _():
        for r in range(rows):
            for k in range(columns // LANES):
                lanes = slice(k * LANES, (k + 1) * LANES)
                at = k * rows + r
                out_ref[r, :, lanes] = (
                    base_ref[r, :, lanes] + column_ref[...] * sum_ref[at : at + 1, :]
                )
            copies[r].start()

    @pl.when(jnp.logical_not(is_atmos))
    def _():
        levels = channels // 2
        even = row_group % 2 == 0
        below = jnp.where(even, far_ref[...].astype(f32), near_ref[...].astype(f32))
        above = jnp.where(even, near_ref[...].astype(f32), far_ref[...].astype(f32))

        low = from_tiles(below, 8)
        high = from_tiles(above, 8)
        by_low = c_ref[1, 1:2, :] * (c_ref[5, 0:1, :] + c_ref[5, 1:2, :])
        by_high = c_ref[2, rows : rows + 1, :] * (
            c_ref[5, rows : rows + 1, :] + c_ref[5, rows + 1 : rows + 2, :]
        )
        has_before = jnp.where(col_group > 0, 1.0, 0.0)
        has_after = jnp.where(col_group < groups_y - 1, 1.0, 0.0)

        @pl.when(col_group == 0)
        def _():
            span = rows + 2
            e_ref[0:1, :] = low[0:1]
            e_ref[1 : rows + 1, :] = from_tiles(sum_ref[...], rows)
            e_ref[rows + 1 : span, :] = high[0:1]
            e_ref[0:span, :] = c_ref[6, 0:span, :] * e_ref[0:span, :]
            own = slice(1, rows + 1)
            heat = e_ref[own, :]
            second = c_ref[5, own, :] * heat
            first = (c_ref[0, own, :] + 1.0) * heat + second
            first = first + c_ref[1, own, :] * e_ref[0:rows, :]
            first = first + c_ref[2, own, :] * e_ref[2 : rows + 2, :]
            first = first + c_ref[3, own, :] * pltpu.roll(heat, 1, 1)
            first = first + c_ref[4, own, :] * pltpu.roll(heat, columns - 1, 1)
            heat_ref[0] = first
            heat_ref[1] = second

        for r in [1, rows - 2] + list(range(2, rows - 2)) + [0, rows - 1]:
            out_ref[r] = base_ref[r]
            for t in range(2):
                c = t * levels
                for edge, factor, lines in ((0, by_low, low), (rows - 1, by_high, high)):
                    if r == edge:
                        out_ref[r, c : c + 1, :] = out_ref[r, c : c + 1, :] + (
                            has_before * factor * lines[t + 1 : t + 2]
                        )
                        d = c + levels - 1
                        out_ref[r, d : d + 1, :] = out_ref[r, d : d + 1, :] + (
                            has_after * factor * lines[t + 3 : t + 4]
                        )

            @pl.when(col_group == 0)
            def _():
                for t, gain in enumerate((heat_gain, salt_gain)):
                    c = t * levels
                    for k in range(2):
                        out_ref[r, c + k : c + k + 1, :] = (
                            out_ref[r, c + k : c + k + 1, :] + gain * heat_ref[k, r : r + 1, :]
                        )

            copies[r].start()

    for copy in copies:
        copy.wait()


def local(
    fields,
    wet_cells,
    flux_weight,
    variable_sea_response,
    diffusivity,
    a2o_source,
    a2o_target,
    a2o_count,
    a2o_weight,
    marine_air_input_index,
    marine_air_output_index,
    marine_air_piece_tally,
    marine_air_piece_factor,
):
    _, rows, channels, columns = fields.shape
    groups_x = lax.axis_size("gx")
    groups_y = lax.axis_size("gy")
    blocks, points = a2o_source.shape[2:]
    cells = rows * columns // LANES
    forward, inverse = fourier_tables(columns)
    flux_row = flux_weight[None, :]
    gain_row = variable_sea_response[None, :]
    diff_row = diffusivity[None, :]
    paired = groups_x == 4
    params = functools.partial(pltpu.CompilerParams, vmem_limit_bytes=40 * 2**20)
    vmem = pl.BlockSpec(memory_space=pltpu.VMEM)
    smem = pl.BlockSpec(memory_space=pltpu.SMEM)
    hbm = pl.BlockSpec(memory_space=pltpu.HBM)
    anywhere = pl.BlockSpec(memory_space=pl.ANY)

    def shape(dims, dtype):
        return jax.ShapeDtypeStruct(dims, dtype)

    lines = 2 * channels + 16
    shapes = [
        shape((cells, LANES), bf16),
        shape((cells + 16, LANES), bf16),
        shape((rows, channels, columns), f32),
        shape((lines, columns), bf16),
        shape((lines, columns), bf16),
        shape((4 * rows, columns), bf16),
        shape((4 * rows, columns), bf16),
    ]
    if not paired:
        shapes.append(shape((2, channels, columns), bf16))
    coarse, wide, y, e1, e3, e2, e4, *sums = pl.pallas_call(
        functools.partial(start_kernel, groups_x, paired),
        out_shape=shapes,
        in_specs=[hbm] * 5,
        out_specs=[hbm] * len(shapes),
        scratch_shapes=[pltpu.VMEM(out.shape, out.dtype) for out in shapes]
        + [
            pltpu.VMEM((rows, channels, columns), f32),
            pltpu.VMEM((rows, columns), jnp.int32),
            pltpu.VMEM(flux_row.shape, f32),
            pltpu.VMEM(diff_row.shape, f32),
            pltpu.VMEM(forward.shape, bf16),
            pltpu.VMEM((rows * channels, columns), bf16),
            pltpu.VMEM((rows, columns), f32),
            pltpu.VMEM((4 * rows, columns), f32),
            pltpu.VMEM((columns // 2 // LANES, 2 * rows + 1, channels, LANES), f32),
            pltpu.SemaphoreType.DMA((rows,)),
            pltpu.SemaphoreType.DMA((3,)),
            pltpu.SemaphoreType.DMA((rows + len(shapes) - 1,)),
        ],
        compiler_params=pltpu.CompilerParams(vmem_limit_bytes=58 * 2**20),
        name="surface_and_forward_or_halos",
    )(fields, wet_cells, flux_row, diff_row, forward)

    masks = [1 << bit for bit in range(groups_y.bit_length() - 1)]

    def sum_route(mask):
        return [(j, j ^ mask) for j in range(groups_y)]

    def partner_route(mask):
        return both_ways([(j, groups_y + (j ^ mask)) for j in range(groups_y)])

    surface = lax.ppermute(coarse, ("comp", "gy"), partner_route(0)).astype(f32)
    for mask in masks[:1]:
        far = lax.ppermute(wide, ("comp", "gy"), partner_route(mask))
        surface = surface + far[:cells].astype(f32)
    coarse = surface.astype(bf16)
    for mask in masks[1:-1]:
        surface = surface + lax.ppermute(coarse, "gy", sum_route(mask)).astype(f32)
        coarse = surface.astype(bf16)
    surfaces = [surface] + [
        lax.ppermute(coarse, "gy", sum_route(mask)) for mask in masks[1:][-1:]
    ]

    def ring_pairs(count, odd):
        return [(a, (a + 1) % count) for a in range(odd, count, 2)]

    def flat(comp, i, j):
        return (comp * groups_x + i) * groups_y + j

    def level_route(odd):
        pairs = []
        for i in range(groups_x):
            linked = [(a, a + 1) for a in range(odd, groups_y - 1, 2)]
            alone = set(range(groups_y)) - {j for pair in linked for j in pair}
            pairs += [(flat(1, i, a), flat(1, i, b)) for a, b in linked]
            if i % 2 == 0:
                pairs += [(flat(1, i, j), flat(1, i + 1, j)) for j in sorted(alone)]
                if odd or not paired:
                    pairs += [(flat(0, i, j), flat(0, i + 1, j)) for j in range(groups_y)]
            if paired and not odd and i < i ^ 2:
                pairs += [(flat(0, i, j), flat(0, i ^ 2, j)) for j in range(groups_y)]
        return both_ways(pairs)

    e1 = lax.ppermute(e1, "gx", both_ways(ring_pairs(groups_x, 0)))
    e3 = lax.ppermute(e3, "gx", both_ways(ring_pairs(groups_x, 1)))
    axes = ("comp", "gx", "gy")
    e2 = lax.ppermute(e2, axes, level_route(0))
    e4 = lax.ppermute(e4, axes, level_route(1))

    one_hots = pl.pallas_call(
        functools.partial(one_hot_kernel, rows, columns),
        out_shape=[
            shape((LANES, blocks * points), bf16),
            shape((LANES, blocks * points), bf16),
            shape((blocks, points), jnp.int32),
            shape((blocks, points), jnp.int32),
        ],
        in_specs=[vmem] * 4 + [anywhere],
        out_specs=[vmem] * 4,
        compiler_params=params(),
        name="one_hots",
    )(a2o_source, a2o_target, marine_air_input_index, marine_air_output_index, coarse)
    landing, *sent = pl.pallas_call(
        functools.partial(regrid_kernel, len(surfaces)),
        out_shape=[shape((cells, LANES), f32)]
        + [shape((cells + 16 * (mask - 1), LANES), bf16) for mask in range(1, groups_y)],
        in_specs=[vmem] * (len(surfaces) + 4) + [smem, smem, hbm, hbm] + [anywhere] * 1,
        out_specs=[vmem] * groups_y,
        scratch_shapes=[
            pltpu.VMEM((blocks, points, points), bf16),
            pltpu.VMEM((blocks, points), f32),
            pltpu.VMEM((blocks, points), f32),
            pltpu.SemaphoreType.DMA,
        ],
        compiler_params=params(),
        cost_estimate=pl.CostEstimate(flops=int(2.0 * 1.1e9), bytes_accessed=0, transcendentals=0),
        name="regrid_blocks",
    )(
        *surfaces, *one_hots, a2o_count, marine_air_piece_tally,
        a2o_weight, marine_air_piece_factor, e3,
    )

    def landing_route(mask):
        pairs = [
            (flat(0, i, j), flat(0, i, j ^ mask))
            for i in range(groups_x)
            for j in range(groups_y)
            if j < j ^ mask
        ]
        pairs += [(flat(1, i, 0), flat(1, i, mask)) for i in range(groups_x)]
        pairs += [
            (flat(1, i, j), flat(1, i + 1, j))
            for i in range(0, groups_x, 2)
            for j in range(groups_y)
            if j not in (0, mask)
        ]
        return both_ways(pairs)

    parts = [
        lax.ppermute(block, axes, landing_route(mask)) for mask, block in enumerate(sent, 1)
    ]

    extra = []
    if not paired:
        p, q = jnp.moveaxis(lax.all_gather(sums[0], "gx").astype(f32), 1, 0)
        viscous = lax.dynamic_slice_in_dim(
            diffusivity, lax.axis_index("gy") * channels, channels
        )[:, None]
        rates = [half_rates(g, 0, columns // 4, columns) for g in (0, 0, 1, 1)]
        _, alpha, _ = decay_terms(viscous, jnp.concatenate(rates, axis=1))
        gap = lax.axis_index("gx") - jnp.arange(groups_x)
        decay = jnp.exp(
            -(rows * jnp.maximum(jnp.abs(gap) - 1, 0))[:, None, None] * alpha[None]
        )
        extra = [
            jnp.sum(jnp.where((gap > 0)[:, None, None], decay * p, 0.0), axis=0),
            jnp.sum(jnp.where((gap < 0)[:, None, None], decay * q, 0.0), axis=0),
        ]
    ring = channels // 2 + 8
    damped, coefs, stepped = pl.pallas_call(
        functools.partial(first_step_kernel, groups_x, groups_y, paired),
        out_shape=[
            shape((rows * channels, columns), bf16),
            shape((7, 16, columns), f32),
            shape((rows + 2, 2, ring, columns), f32),
        ],
        in_specs=[vmem] * (8 + len(extra)),
        out_specs=[vmem] * 3,
        scratch_shapes=[
            pltpu.VMEM((rows, channels, LANES), f32),
            pltpu.VMEM((rows + 4, 2, ring, columns), f32),
            pltpu.VMEM((16, columns), f32),
        ],
        compiler_params=params(),
        name="damping_or_first_step",
    )(fields, wet_cells, diff_row, y, e1, e3, e2, e4, *extra)

    surface_sum, near, far = pl.pallas_call(
        functools.partial(heat_kernel, rows),
        out_shape=[
            shape((cells, LANES), f32),
            shape((columns // 16, LANES), bf16),
            shape((columns // 16, LANES), bf16),
        ],
        in_specs=[vmem] * 3 + [anywhere] + [vmem] * len(parts),
        out_specs=[vmem] * 3,
        compiler_params=params(),
        name="surface_sum",
    )(e2, e4, landing, coefs, *parts)

    near = lax.ppermute(near, "gx", both_ways(ring_pairs(groups_x, 0)))
    far = lax.ppermute(far, "gx", both_ways(ring_pairs(groups_x, 1)))
    base, column = pl.pallas_call(
        second_step_kernel,
        out_shape=[shape((rows, channels, columns), f32), shape((channels, LANES), f32)],
        in_specs=[vmem] * 5,
        out_specs=[vmem] * 2,
        compiler_params=params(),
        name="inverse_or_second_step",
    )(gain_row, inverse, damped, coefs, stepped)
    return pl.pallas_call(
        functools.partial(last_kernel, groups_x, groups_y),
        out_shape=shape(fields.shape, f32),
        in_specs=[vmem] * 6,
        out_specs=hbm,
        scratch_shapes=[
            pltpu.VMEM((rows, channels, columns), f32),
            pltpu.VMEM((16, columns), f32),
            pltpu.VMEM((2, rows, columns), f32),
            pltpu.SemaphoreType.DMA((rows,)),
        ],
        compiler_params=params(),
        name="add_surface_terms",
    )(column, base, coefs, surface_sum, near, far)


def solution(mesh):
    in_specs = (
        P("comp", "gx", "gy", None),
        P("gx", None),
        P(),
        P(),
        P(),
        P("gx", "gy", None, None),
        P("gx", "gy", None, None),
        P("gx", "gy"),
        P("gx", "gy", None, None, None),
        P("gx", "gy", None, None),
        P("gx", "gy", None, None),
        P("gx", "gy"),
        P("gx", "gy", None, None, None),
    )
    out_specs = P("comp", "gx", "gy", None)
    return jax.shard_map(local, mesh=mesh, in_specs=in_specs, out_specs=out_specs, check_vma=False)
```

```python
import functools

import jax
import jax.numpy as jnp
import numpy as np
from jax import lax
from jax.experimental import pallas as pl
from jax.experimental.pallas import tpu as pltpu
from jax.sharding import PartitionSpec as P

spread_rate = 0.2
mixing_rate = 0.1
heat_gain = 0.5
salt_gain = -0.25
LANES = 128
f32 = jnp.float32
bf16 = jnp.bfloat16


def fourier_tables(columns):
    half = columns // 2
    forward, inverse = [], []
    for first in (0, 1):
        waves = np.arange(first, half, 2)
        phase = np.arange(half)[:, None] * waves[None, :] % columns
        angles = phase * (2.0 * np.pi / columns)
        table = np.concatenate([np.cos(angles), np.sin(angles)], axis=1)
        weight = np.where(waves == 0, 1.0, 2.0) / columns
        forward.append(table)
        inverse.append(table.T * np.concatenate([weight, weight])[:, None])
    return (
        jnp.asarray(np.concatenate(forward).astype(np.float32), bf16),
        jnp.asarray(np.concatenate(inverse).astype(np.float32), bf16),
    )


def wave_parts(columns):
    quarter = columns // 4
    return [
        (g, n, (g * 2 * quarter + n, (g * 2 + 1) * quarter + n))
        for g in (0, 1)
        for n in range(0, quarter, LANES)
    ]


def half_rates(group, first, count, columns):
    lane = lax.broadcasted_iota(jnp.int32, (1, count), 1) + first
    wave = (2 * lane + group).astype(f32)
    sine = jnp.sin(wave * (np.pi / columns))
    return 2.0 * sine * sine


def both_ways(pairs):
    return [p for a, b in pairs for p in ((a, b), (b, a))]


def channel_column(row, channels, first):
    n = row.shape[1]
    lane = lax.broadcasted_iota(jnp.int32, (channels, n), 1)
    sub = lax.broadcasted_iota(jnp.int32, (channels, n), 0)
    return jnp.sum(jnp.where(lane == sub + first, row, 0.0), axis=1, keepdims=True)


def to_tiles(surface):
    cols = surface.shape[1]
    return jnp.concatenate(
        [surface[:, k : k + LANES] for k in range(0, cols, LANES)], axis=0
    )


def from_tiles(tiles, rows):
    return jnp.concatenate(
        [tiles[k : k + rows] for k in range(0, tiles.shape[0], rows)], axis=1
    )


def lengthen(ref, block):
    rows = block.shape[0]
    ref[0:rows, :] = block
    if ref.shape[0] > rows:
        ref[rows:, :] = block[: ref.shape[0] - rows]


def decay_terms(diff_column, rates):
    half = 0.5 / diff_column + rates
    sinh = jnp.sqrt(half * (half + 2.0))
    grow = 1.0 + half + sinh
    return 1.0 / grow, jnp.log(grow), sinh


def edge_factors(lam, alpha, base, total, rows):
    lam2 = lam * lam
    powers = [
        jnp.exp(-2.0 * base * alpha) * lam2,
        jnp.exp(-2.0 * (total - rows - base) * alpha) * lam2,
    ]
    lows, highs = [], []
    for _ in range(rows):
        lows.append(1.0 - powers[0])
        highs.insert(0, 1.0 - powers[1])
        powers = [power * lam2 for power in powers]
    return lows, highs


def start_kernel(
    groups_x, paired, x_hbm, wet_hbm, flux_hbm, diff_hbm, table_hbm, *refs
):
    outs = 7 if paired else 8
    coarse_hbm, wide_hbm, y_hbm, *message_hbm = refs[:outs]
    coarse_ref, wide_ref, y_ref, *message_ref = refs[outs : 2 * outs]
    e1_ref, e3_ref, e2_ref, e4_ref = message_ref[:4]
    if not paired:
        pq_ref = message_ref[4]
    (
        x_ref, wet_ref, flux_ref, diff_ref, table_ref, flat_ref, row_ref, edge_ref,
        factor_ref, x_sem, sem, out_sem,
    ) = refs[2 * outs :]
    rows, channels, columns = x_ref.shape
    half = columns // 2
    row_group = lax.axis_index("gx")
    col_group = lax.axis_index("gy")
    is_atmos = lax.axis_index("comp") == 0

    x_copies = [
        pltpu.make_async_copy(x_hbm.at[0, r], x_ref.at[r], x_sem.at[r]) for r in range(rows)
    ]
    surface_copies = [
        pltpu.make_async_copy(coarse_ref, coarse_hbm, out_sem.at[0]),
        pltpu.make_async_copy(wide_ref, wide_hbm, out_sem.at[1]),
    ]
    y_copies = [
        pltpu.make_async_copy(y_ref.at[r], y_hbm.at[r], out_sem.at[2 + r]) for r in range(rows)
    ]
    message_copies = [
        pltpu.make_async_copy(ref, hbm, out_sem.at[2 + rows + k])
        for k, (ref, hbm) in enumerate(zip(message_ref, message_hbm))
    ]

    def send_surface():
        coarse = to_tiles(row_ref[...]).astype(bf16)
        coarse_ref[...] = coarse
        lengthen(wide_ref, coarse)
        for copy in surface_copies:
            copy.start()

    @pl.when(is_atmos)
    def _():
        flux_copy = pltpu.make_async_copy(flux_hbm, flux_ref, sem.at[0])
        diff_copy = pltpu.make_async_copy(diff_hbm, diff_ref, sem.at[1])
        table_copy = pltpu.make_async_copy(table_hbm, table_ref, sem.at[2])
        for copy in [flux_copy, diff_copy] + x_copies + [table_copy]:
            copy.start()
        first = col_group * channels
        flux_copy.wait()
        weight = channel_column(flux_ref[...], channels, first)
        diff_copy.wait()
        diff = channel_column(diff_ref[...], channels, first)
        total = rows * groups_x
        base = (row_group * rows).astype(f32)
        tiles = wave_parts(columns)
        for k, (group, n, _) in enumerate(tiles):
            lam, alpha, _ = decay_terms(diff, half_rates(group, n, LANES, columns))
            factor_ref[k, 0] = lam
            lows, highs = edge_factors(lam, alpha, base, total, rows)
            for r in range(rows):
                factor_ref[k, 1 + r] = lows[r]
                factor_ref[k, 1 + rows + r] = highs[r]
        for r in range(rows):
            x_copies[r].wait()
            row_ref[r : r + 1, :] = jnp.sum(x_ref[r] * weight, axis=0, keepdims=True)
            left, right = x_ref[r, :, :half], x_ref[r, :, half:]
            flat_ref[r * channels : (r + 1) * channels, :half] = (left + right).astype(bf16)
            flat_ref[r * channels : (r + 1) * channels, half:] = (left - right).astype(bf16)
        send_surface()
        table_copy.wait()
        for k in range(2):
            lanes = slice(k * half, (k + 1) * half)
            part = jnp.dot(
                flat_ref[:, lanes], table_ref[lanes, :], preferred_element_type=f32
            )
            y_ref[:, :, lanes] = part.reshape(rows, channels, half)
            for tile, (group, _, parts) in enumerate(tiles):
                if group != k:
                    continue
                lam = factor_ref[tile, 0]
                for at in parts:
                    lanes = slice(at, at + LANES)
                    here = slice(at - k * half, at - k * half + LANES)
                    p = factor_ref[tile, 1] * part[0:channels, here]
                    q = factor_ref[tile, 2 * rows] * part[(rows - 1) * channels :, here]
                    for r in range(1, rows):
                        up = part[r * channels : (r + 1) * channels, here]
                        down = part[(rows - 1 - r) * channels : (rows - r) * channels, here]
                        p = lam * p + factor_ref[tile, 1 + r] * up
                        q = lam * q + factor_ref[tile, 2 * rows - r] * down
                    if paired:
                        for mask, out in ((1, e1_ref), (2, e2_ref), (3, e3_ref)):
                            upward = row_group < (row_group ^ mask)
                            out[0:channels, lanes] = jnp.where(upward, p, q).astype(bf16)
                    else:
                        pq_ref[0, :, lanes] = p.astype(bf16)
                        pq_ref[1, :, lanes] = q.astype(bf16)
        for copy in y_copies:
            copy.start()
        for copy in message_copies:
            copy.start()
        for copy in surface_copies + y_copies + message_copies:
            copy.wait()

    @pl.when(jnp.logical_not(is_atmos))
    def _():
        wet_copy = pltpu.make_async_copy(wet_hbm, wet_ref, sem.at[0])
        for copy in x_copies + [wet_copy]:
            copy.start()
        gain = jnp.where(col_group == 0, 1.0, 0.0)
        for r in range(rows):
            x_copies[r].wait()
            row_ref[r : r + 1, :] = x_ref[r, 0:1, :] * gain
        send_surface()
        wet_copy.wait()
        levels = channels // 2
        lines = 2 * channels
        even_x = row_group % 2 == 0
        even_y = col_group % 2 == 0
        wet = wet_ref[...].astype(f32)
        wet = jnp.concatenate([wet, wet], axis=0).astype(bf16)

        def put(out, last):
            @pl.when(last)
            def _():
                out[0:lines, :] = x_ref[rows - 2 :].reshape(lines, columns).astype(bf16)

            @pl.when(jnp.logical_not(last))
            def _():
                out[0:lines, :] = x_ref[:2].reshape(lines, columns).astype(bf16)

            out[lines : lines + 16, :] = wet

        put(e1_ref, even_x)
        put(e3_ref, jnp.logical_not(even_x))

        def put_edges(out, level):
            for r in range(rows):
                for t in range(2):
                    at = (r * 2 + t) * 2
                    c = t * levels + level
                    edge_ref[at : at + 2, :] = x_ref[r, c : c + 2, :]
            out[0 : rows * 4, :] = edge_ref[...].astype(bf16)

        @pl.when(even_y)
        def _():
            put_edges(e2_ref, levels - 2)
            put_edges(e4_ref, 0)

        @pl.when(jnp.logical_not(even_y))
        def _():
            put_edges(e2_ref, 0)
            put_edges(e4_ref, levels - 2)

        for copy in message_copies:
            copy.start()
        for copy in surface_copies + message_copies:
            copy.wait()


def one_hot_kernel(
    rows, columns, a_src, a_dst, a_count, m_src, m_dst, m_count, src_hot_ref, dst_hot_ref,
    src_row_ref, dst_row_ref, used_ref,
):
    is_atmos = lax.axis_index("comp") == 0
    blocks, points = src_row_ref.shape
    count = jnp.where(is_atmos, m_count[0, 0], a_count[0, 0])
    block_iota = lax.broadcasted_iota(jnp.int32, (blocks, points), 0)
    used_ref[...] = jnp.where(block_iota < count, 1, 0)
    lane_iota = lax.broadcasted_iota(jnp.int32, (LANES, points), 0)
    for a_ref, m_ref, hot_ref, row_ref in (
        (a_src, m_src, src_hot_ref, src_row_ref),
        (a_dst, m_dst, dst_hot_ref, dst_row_ref),
    ):
        index = jnp.where(is_atmos, m_ref[0, 0], a_ref[0, 0])
        row = index // columns
        tile = (index // LANES) % (columns // LANES)
        row_ref[...] = tile * rows + row
        lane = index % LANES
        for b in range(blocks):
            hot_ref[:, b * points : (b + 1) * points] = jnp.where(
                lane_iota == lane[b : b + 1], 1.0, 0.0
            ).astype(bf16)


def regrid_kernel(n_surfaces, *refs):
    surfaces = refs[:n_surfaces]
    (
        src_hot_ref, dst_hot_ref, src_row_ref, dst_row_ref, used_ref, a_weight, m_weight,
        _,
        *refs,
    ) = refs[n_surfaces:]
    land_ref, *sent_refs = refs[:-4]
    weight_ref, gath_ref, val_ref, sem = refs[-4:]
    is_atmos = lax.axis_index("comp") == 0
    blocks, points = val_ref.shape
    cells = surfaces[0].shape[0]

    @pl.when(is_atmos)
    def _():
        pltpu.make_async_copy(m_weight.at[0, 0], weight_ref, sem).start()

    @pl.when(jnp.logical_not(is_atmos))
    def _():
        pltpu.make_async_copy(a_weight.at[0, 0], weight_ref, sem).start()

    pair = 2 * points
    row_iota = lax.broadcasted_iota(jnp.int32, (cells, points), 0)
    table = sum(surface[...].astype(f32) for surface in surfaces).astype(bf16)
    for b in range(0, blocks, 2):
        picked = jnp.dot(
            table, src_hot_ref[:, b * points : b * points + pair], preferred_element_type=f32
        )
        for k in range(2):
            mine = row_iota == src_row_ref[b + k : b + k + 1, :]
            part = jnp.where(mine, picked[:, k * points : (k + 1) * points], 0.0)
            gath_ref[b + k : b + k + 1, :] = jnp.sum(part, axis=0, keepdims=True)
    gathered = gath_ref[...].astype(bf16)

    @pl.when(is_atmos)
    def _():
        pltpu.make_async_copy(m_weight.at[0, 0], weight_ref, sem).wait()

    @pl.when(jnp.logical_not(is_atmos))
    def _():
        pltpu.make_async_copy(a_weight.at[0, 0], weight_ref, sem).wait()

    block_iota = lax.broadcasted_iota(jnp.int32, (blocks, points), 0)
    values = jnp.zeros((blocks, points), f32)
    for b in range(0, blocks, 2):
        terms = lax.dot_general(
            gathered,
            weight_ref[b : b + 2].reshape(pair, points),
            (((1,), (1,)), ((), ())),
            preferred_element_type=f32,
        )
        for k in range(2):
            values = jnp.where(block_iota == b + k, terms[:, k * points : (k + 1) * points], values)
    val_ref[...] = jnp.where(used_ref[...] > 0, values, 0.0)
    land = jnp.zeros((2 * cells, LANES), f32)
    for b in range(0, blocks, 2):
        spread = []
        for k in range(b, b + 2):
            value = val_ref[k : k + 1, :]
            coarse = value.astype(bf16).astype(f32)
            fine = value - coarse
            mine = row_iota == dst_row_ref[k : k + 1, :]
            spread.append(
                jnp.concatenate(
                    [jnp.where(mine, coarse, 0.0), jnp.where(mine, fine, 0.0)], axis=0
                ).astype(bf16)
            )
        land = land + lax.dot_general(
            jnp.concatenate(spread, axis=1),
            dst_hot_ref[:, b * points : b * points + pair],
            (((1,), (1,)), ((), ())),
            preferred_element_type=f32,
        )
    land = land[:cells] + land[cells:]
    land_ref[...] = land
    for sent_ref in sent_refs:
        lengthen(sent_ref, land.astype(bf16))


def heat_kernel(rows, e2_ref, e4_ref, land_ref, _, *refs):
    parts = refs[:-3]
    sum_ref, near_ref, far_ref = refs[-3:]
    cells = land_ref.shape[0]
    columns = cells // rows * LANES
    even_x = lax.axis_index("gx") % 2 == 0
    even_y = lax.axis_index("gy") % 2 == 0
    total = land_ref[...]
    for part in parts:
        total = total + part[0:cells, :].astype(f32)
    sum_ref[...] = total

    def corners(row):
        start = row * 4 // 16 * 16
        one = e2_ref[start : start + 16, :].astype(f32)
        two = e4_ref[start : start + 16, :].astype(f32)
        low = jnp.where(even_y, two, one)
        high = jnp.where(even_y, one, two)
        at = row * 4 - start
        lines = [low[at + 1 : at + 2], low[at + 3 : at + 4], high[at : at + 1], high[at + 2 : at + 3]]
        heat = from_tiles(total, rows)[row : row + 1]
        blank = jnp.zeros((3, columns), f32)
        return to_tiles(jnp.concatenate([heat] + lines + [blank], axis=0))

    first, last = corners(0), corners(rows - 1)
    near_ref[...] = jnp.where(even_x, last, first).astype(bf16)
    far_ref[...] = jnp.where(even_x, first, last).astype(bf16)


def advance(ref, r, t, coefs, size):
    ring, columns = ref.shape[2:]
    whole = ref[r, t]
    up = pltpu.roll(whole, 1, 0)[:size]
    down = pltpu.roll(whole, ring - 1, 0)[:size]
    mid = whole[:size]
    total = coefs[0] * mid + coefs[5] * (up + down)
    total = total + coefs[1] * ref[r - 1, t, 0:size, :]
    total = total + coefs[2] * ref[r + 1, t, 0:size, :]
    total = total + coefs[3] * pltpu.roll(mid, 1, 1)
    return total + coefs[4] * pltpu.roll(mid, columns - 1, 1)


def first_step_kernel(
    groups_x, groups_y, paired, x_ref, wet_ref, diff_ref, y_ref, e1_ref, e3_ref,
    e2_ref, e4_ref, *refs,
):
    if not paired:
        pin_ref, qin_ref = refs[:2]
    zb_ref, c_ref, t1_ref, z_ref, t0_ref, w_ref = refs[-6:]
    _, rows, channels, columns = x_ref.shape
    row_group = lax.axis_index("gx")
    col_group = lax.axis_index("gy")
    is_atmos = lax.axis_index("comp") == 0

    @pl.when(is_atmos)
    def _():
        diff = channel_column(diff_ref[...], channels, col_group * channels)
        total = rows * groups_x
        base = (row_group * rows).astype(f32)
        for group, n, parts in wave_parts(columns):
            lam, alpha, sinh = decay_terms(diff, half_rates(group, n, LANES, columns))
            scale = 1.0 / (
                2.0 * diff * sinh * (1.0 - jnp.exp(-2.0 * (total + 1) * alpha))
            )
            lows, highs = edge_factors(lam, alpha, base, total, rows)
            for part in parts:
                lanes = slice(part, part + LANES)
                if paired:
                    pin = jnp.zeros((channels, LANES), f32)
                    qin = jnp.zeros((channels, LANES), f32)
                    for mask, msg in ((1, e1_ref), (2, e2_ref), (3, e3_ref)):
                        band = row_group ^ mask
                        gap = (jnp.abs(row_group - band) - 1) * rows
                        term = jnp.exp(-gap.astype(f32) * alpha)
                        term = term * msg[0:channels, lanes].astype(f32)
                        pin = pin + jnp.where(band < row_group, term, 0.0)
                        qin = qin + jnp.where(band > row_group, term, 0.0)
                else:
                    pin = pin_ref[:, lanes]
                    qin = qin_ref[:, lanes]
                f = pin
                for r in range(rows):
                    f = lam * f + lows[r] * y_ref[r, :, lanes]
                    z_ref[r] = highs[r] * f
                g = lam * qin
                for r in reversed(range(rows)):
                    z = scale * (z_ref[r] + lows[r] * g)
                    zb_ref[r * channels : (r + 1) * channels, lanes] = z.astype(bf16)
                    g = lam * (g + highs[r] * y_ref[r, :, lanes])

    @pl.when(jnp.logical_not(is_atmos))
    def _():
        levels = channels // 2
        ring = levels + 8
        lines = 2 * channels
        first_x = row_group == 0
        last_x = row_group == groups_x - 1
        top = col_group == 0
        bottom = col_group == groups_y - 1
        even_x = row_group % 2 == 0
        even_y = col_group % 2 == 0

        one = e1_ref[lines : lines + 16, :].astype(f32)
        three = e3_ref[lines : lines + 16, :].astype(f32)
        below = jnp.where(even_x, three, one)[rows - 2 : rows]
        above = jnp.where(even_x, one, three)[0:2]
        w_ref[0:2, :] = jnp.where(first_x, 0.0, below)
        w_ref[2 : rows + 2, :] = wet_ref[...].astype(f32)
        w_ref[rows + 2 : rows + 4, :] = jnp.where(last_x, 0.0, above)

        span = rows + 2
        north = w_ref[0:span, :]
        here = w_ref[1 : span + 1, :]
        south = w_ref[2 : span + 2, :]
        west = pltpu.roll(here, 1, 1)
        east = pltpu.roll(here, columns - 1, 1)
        c_ref[0, 0:span, :] = here * (
            1.0 - 2.0 * mixing_rate - spread_rate * (north + south + west + east)
        )
        c_ref[1, 0:span, :] = spread_rate * here * north
        c_ref[2, 0:span, :] = spread_rate * here * south
        c_ref[3, 0:span, :] = spread_rate * here * west
        c_ref[4, 0:span, :] = spread_rate * here * east
        c_ref[5, 0:span, :] = mixing_rate * here
        c_ref[6, 0:span, :] = here

        one = e1_ref[0:lines, :].astype(f32)
        three = e3_ref[0:lines, :].astype(f32)
        below = jnp.where(even_x, three, one)
        above = jnp.where(even_x, one, three)
        blank = jnp.zeros((8, columns), f32)
        for k in range(2):
            for t in range(2):
                c = k * channels + t * levels
                t0_ref[k, t, 0:levels, :] = below[c : c + levels]
                t0_ref[rows + 2 + k, t, 0:levels, :] = above[c : c + levels]
                t0_ref[k, t, levels:ring, :] = blank
                t0_ref[rows + 2 + k, t, levels:ring, :] = blank
        one = e2_ref[...].astype(f32)
        two = e4_ref[0 : 4 * rows, :].astype(f32)
        before = jnp.where(even_y, two, one)
        after = jnp.where(even_y, one, two)
        for r in range(rows):
            for t in range(2):
                k = (r * 2 + t) * 2
                t0_ref[r + 2, t, 0:levels, :] = x_ref[0, r, t * levels : (t + 1) * levels, :]
                t0_ref[r + 2, t, levels : levels + 2, :] = after[k : k + 2]
                t0_ref[r + 2, t, ring - 2 : ring, :] = before[k : k + 2]

        def close(ref, r):
            for t in range(2):
                ref[r, t, ring - 1 : ring, :] = jnp.where(
                    top, ref[r, t, 0:1, :], ref[r, t, ring - 1 : ring, :]
                )
                ref[r, t, levels : levels + 1, :] = jnp.where(
                    bottom, ref[r, t, levels - 1 : levels, :], ref[r, t, levels : levels + 1, :]
                )

        def first(r, carry):
            coefs = [c_ref[k, pl.ds(r, 1), :] for k in range(6)]
            close(t0_ref, r + 1)
            for t in range(2):
                t1_ref[r, t] = advance(t0_ref, r + 1, t, coefs, ring)
            close(t1_ref, r)
            return carry

        lax.fori_loop(0, span, first, 0)


def second_step_kernel(gain_ref, table_ref, zb_ref, c_ref, t1_ref, base_ref, column_ref):
    rows, channels, columns = base_ref.shape
    is_atmos = lax.axis_index("comp") == 0

    @pl.when(is_atmos)
    def _():
        response = channel_column(gain_ref[...], channels, lax.axis_index("gy") * channels)
        column_ref[...] = jnp.broadcast_to(response, column_ref.shape)
        half = columns // 2
        step = 256
        for n in range(0, half, step):
            even, odd = [
                jnp.dot(
                    zb_ref[:, k * half : (k + 1) * half],
                    table_ref[k * half : (k + 1) * half, n : n + step],
                    preferred_element_type=f32,
                ).reshape(rows, channels, step)
                for k in range(2)
            ]
            base_ref[:, :, n : n + step] = even + odd
            base_ref[:, :, n + half : n + half + step] = even - odd

    @pl.when(jnp.logical_not(is_atmos))
    def _():
        levels = channels // 2

        def second(r, carry):
            coefs = [c_ref[k, pl.ds(r, 1), :] for k in range(6)]
            for t in range(2):
                c = t * levels
                base_ref[r - 1, c : c + levels, :] = advance(t1_ref, r, t, coefs, levels)
            return carry

        lax.fori_loop(1, rows + 1, second, 0)


def last_kernel(
    groups_x, groups_y, column_ref, base_ref, c_ref, sum_ref, near_ref, far_ref, out_hbm,
    out_ref, e_ref, heat_ref, sem,
):
    rows, channels, columns = out_ref.shape
    row_group = lax.axis_index("gx")
    col_group = lax.axis_index("gy")
    is_atmos = lax.axis_index("comp") == 0
    copies = [
        pltpu.make_async_copy(out_ref.at[r], out_hbm.at[0, r], sem.at[r]) for r in range(rows)
    ]

    @pl.when(is_atmos)
    def _():
        for r in range(rows):
            for k in range(columns // LANES):
                lanes = slice(k * LANES, (k + 1) * LANES)
                at = k * rows + r
                out_ref[r, :, lanes] = (
                    base_ref[r, :, lanes] + column_ref[...] * sum_ref[at : at + 1, :]
                )
            copies[r].start()

    @pl.when(jnp.logical_not(is_atmos))
    def _():
        levels = channels // 2
        even = row_group % 2 == 0
        below = jnp.where(even, far_ref[...].astype(f32), near_ref[...].astype(f32))
        above = jnp.where(even, near_ref[...].astype(f32), far_ref[...].astype(f32))

        low = from_tiles(below, 8)
        high = from_tiles(above, 8)
        by_low = c_ref[1, 1:2, :] * (c_ref[5, 0:1, :] + c_ref[5, 1:2, :])
        by_high = c_ref[2, rows : rows + 1, :] * (
            c_ref[5, rows : rows + 1, :] + c_ref[5, rows + 1 : rows + 2, :]
        )
        has_before = jnp.where(col_group > 0, 1.0, 0.0)
        has_after = jnp.where(col_group < groups_y - 1, 1.0, 0.0)

        @pl.when(col_group == 0)
        def _():
            span = rows + 2
            e_ref[0:1, :] = low[0:1]
            e_ref[1 : rows + 1, :] = from_tiles(sum_ref[...], rows)
            e_ref[rows + 1 : span, :] = high[0:1]
            e_ref[0:span, :] = c_ref[6, 0:span, :] * e_ref[0:span, :]
            own = slice(1, rows + 1)
            heat = e_ref[own, :]
            second = c_ref[5, own, :] * heat
            first = (c_ref[0, own, :] + 1.0) * heat + second
            first = first + c_ref[1, own, :] * e_ref[0:rows, :]
            first = first + c_ref[2, own, :] * e_ref[2 : rows + 2, :]
            first = first + c_ref[3, own, :] * pltpu.roll(heat, 1, 1)
            first = first + c_ref[4, own, :] * pltpu.roll(heat, columns - 1, 1)
            heat_ref[0] = first
            heat_ref[1] = second

        for r in [1, rows - 2] + list(range(2, rows - 2)) + [0, rows - 1]:
            out_ref[r] = base_ref[r]
            for t in range(2):
                c = t * levels
                for edge, factor, lines in ((0, by_low, low), (rows - 1, by_high, high)):
                    if r == edge:
                        out_ref[r, c : c + 1, :] = out_ref[r, c : c + 1, :] + (
                            has_before * factor * lines[t + 1 : t + 2]
                        )
                        d = c + levels - 1
                        out_ref[r, d : d + 1, :] = out_ref[r, d : d + 1, :] + (
                            has_after * factor * lines[t + 3 : t + 4]
                        )

            @pl.when(col_group == 0)
            def _():
                for t, gain in enumerate((heat_gain, salt_gain)):
                    c = t * levels
                    for k in range(2):
                        out_ref[r, c + k : c + k + 1, :] = (
                            out_ref[r, c + k : c + k + 1, :] + gain * heat_ref[k, r : r + 1, :]
                        )

            copies[r].start()

    for copy in copies:
        copy.wait()


def local(
    fields,
    wet_cells,
    flux_weight,
    variable_sea_response,
    diffusivity,
    a2o_source,
    a2o_target,
    a2o_count,
    a2o_weight,
    marine_air_input_index,
    marine_air_output_index,
    marine_air_piece_tally,
    marine_air_piece_factor,
):
    _, rows, channels, columns = fields.shape
    groups_x = lax.axis_size("gx")
    groups_y = lax.axis_size("gy")
    blocks, points = a2o_source.shape[2:]
    cells = rows * columns // LANES
    forward, inverse = fourier_tables(columns)
    flux_row = flux_weight[None, :]
    gain_row = variable_sea_response[None, :]
    diff_row = diffusivity[None, :]
    paired = groups_x == 4
    params = functools.partial(pltpu.CompilerParams, vmem_limit_bytes=40 * 2**20)
    vmem = pl.BlockSpec(memory_space=pltpu.VMEM)
    smem = pl.BlockSpec(memory_space=pltpu.SMEM)
    hbm = pl.BlockSpec(memory_space=pltpu.HBM)
    anywhere = pl.BlockSpec(memory_space=pl.ANY)

    def shape(dims, dtype):
        return jax.ShapeDtypeStruct(dims, dtype)

    lines = 2 * channels + 16
    shapes = [
        shape((cells, LANES), bf16),
        shape((cells + 16, LANES), bf16),
        shape((rows, channels, columns), f32),
        shape((lines, columns), bf16),
        shape((lines, columns), bf16),
        shape((4 * rows, columns), bf16),
        shape((4 * rows, columns), bf16),
    ]
    if not paired:
        shapes.append(shape((2, channels, columns), bf16))
    coarse, wide, y, e1, e3, e2, e4, *sums = pl.pallas_call(
        functools.partial(start_kernel, groups_x, paired),
        out_shape=shapes,
        in_specs=[hbm] * 5,
        out_specs=[hbm] * len(shapes),
        scratch_shapes=[pltpu.VMEM(out.shape, out.dtype) for out in shapes]
        + [
            pltpu.VMEM((rows, channels, columns), f32),
            pltpu.VMEM((rows, columns), jnp.int32),
            pltpu.VMEM(flux_row.shape, f32),
            pltpu.VMEM(diff_row.shape, f32),
            pltpu.VMEM(forward.shape, bf16),
            pltpu.VMEM((rows * channels, columns), bf16),
            pltpu.VMEM((rows, columns), f32),
            pltpu.VMEM((4 * rows, columns), f32),
            pltpu.VMEM((columns // 2 // LANES, 2 * rows + 1, channels, LANES), f32),
            pltpu.SemaphoreType.DMA((rows,)),
            pltpu.SemaphoreType.DMA((3,)),
            pltpu.SemaphoreType.DMA((rows + len(shapes) - 1,)),
        ],
        compiler_params=pltpu.CompilerParams(vmem_limit_bytes=58 * 2**20),
        name="surface_and_forward_or_halos",
    )(fields, wet_cells, flux_row, diff_row, forward)

    one_hots = pl.pallas_call(
        functools.partial(one_hot_kernel, rows, columns),
        out_shape=[
            shape((LANES, blocks * points), bf16),
            shape((LANES, blocks * points), bf16),
            shape((blocks, points), jnp.int32),
            shape((blocks, points), jnp.int32),
            shape((blocks, points), jnp.int32),
        ],
        in_specs=[vmem, vmem, smem] * 2,
        out_specs=[vmem] * 5,
        compiler_params=params(),
        name="one_hots",
    )(
        a2o_source, a2o_target, a2o_count,
        marine_air_input_index, marine_air_output_index, marine_air_piece_tally,
    )

    masks = [1 << bit for bit in range(groups_y.bit_length() - 1)]

    def sum_route(mask):
        return [(j, j ^ mask) for j in range(groups_y)]

    def partner_route(mask):
        return both_ways([(j, groups_y + (j ^ mask)) for j in range(groups_y)])

    surface = lax.ppermute(coarse, ("comp", "gy"), partner_route(0)).astype(f32)
    for mask in masks[:1]:
        far = lax.ppermute(wide, ("comp", "gy"), partner_route(mask))
        surface = surface + far[:cells].astype(f32)
    coarse = surface.astype(bf16)
    *one_hots, used = one_hots
    coarse, used = lax.optimization_barrier((coarse, used))
    for mask in masks[1:-1]:
        surface = surface + lax.ppermute(coarse, "gy", sum_route(mask)).astype(f32)
        coarse = surface.astype(bf16)
    surfaces = [surface] + [
        lax.ppermute(coarse, "gy", sum_route(mask)) for mask in masks[1:][-1:]
    ]

    def ring_pairs(count, odd):
        return [(a, (a + 1) % count) for a in range(odd, count, 2)]

    def flat(comp, i, j):
        return (comp * groups_x + i) * groups_y + j

    def level_route(odd):
        pairs = []
        for i in range(groups_x):
            linked = [(a, a + 1) for a in range(odd, groups_y - 1, 2)]
            alone = set(range(groups_y)) - {j for pair in linked for j in pair}
            pairs += [(flat(1, i, a), flat(1, i, b)) for a, b in linked]
            if i % 2 == 0:
                pairs += [(flat(1, i, j), flat(1, i + 1, j)) for j in sorted(alone)]
                if odd or not paired:
                    pairs += [(flat(0, i, j), flat(0, i + 1, j)) for j in range(groups_y)]
            if paired and not odd and i < i ^ 2:
                pairs += [(flat(0, i, j), flat(0, i ^ 2, j)) for j in range(groups_y)]
        return both_ways(pairs)

    e1 = lax.ppermute(e1, "gx", both_ways(ring_pairs(groups_x, 0)))
    e3 = lax.ppermute(e3, "gx", both_ways(ring_pairs(groups_x, 1)))
    axes = ("comp", "gx", "gy")
    e2 = lax.ppermute(e2, axes, level_route(0))
    e4 = lax.ppermute(e4, axes, level_route(1))

    landing, *sent = pl.pallas_call(
        functools.partial(regrid_kernel, len(surfaces)),
        out_shape=[shape((cells, LANES), f32)]
        + [shape((cells + 16 * (mask - 1), LANES), bf16) for mask in range(1, groups_y)],
        in_specs=[vmem] * (len(surfaces) + 5) + [hbm, hbm] + [anywhere] * 1,
        out_specs=[vmem] * groups_y,
        scratch_shapes=[
            pltpu.VMEM((blocks, points, points), bf16),
            pltpu.VMEM((blocks, points), f32),
            pltpu.VMEM((blocks, points), f32),
            pltpu.SemaphoreType.DMA,
        ],
        compiler_params=params(),
        cost_estimate=pl.CostEstimate(flops=2_200_000_000, bytes_accessed=0, transcendentals=0),
        name="regrid_blocks",
    )(
        *surfaces, *one_hots, used, a2o_weight, marine_air_piece_factor, e3,
    )

    def landing_route(mask):
        pairs = [
            (flat(0, i, j), flat(0, i, j ^ mask))
            for i in range(groups_x)
            for j in range(groups_y)
            if j < j ^ mask
        ]
        pairs += [(flat(1, i, 0), flat(1, i, mask)) for i in range(groups_x)]
        pairs += [
            (flat(1, i, j), flat(1, i + 1, j))
            for i in range(0, groups_x, 2)
            for j in range(groups_y)
            if j not in (0, mask)
        ]
        return both_ways(pairs)

    parts = [
        lax.ppermute(block, axes, landing_route(mask)) for mask, block in enumerate(sent, 1)
    ]

    extra = []
    if not paired:
        p, q = jnp.moveaxis(lax.all_gather(sums[0], "gx").astype(f32), 1, 0)
        viscous = lax.dynamic_slice_in_dim(
            diffusivity, lax.axis_index("gy") * channels, channels
        )[:, None]
        rates = [half_rates(g, 0, columns // 4, columns) for g in (0, 0, 1, 1)]
        _, alpha, _ = decay_terms(viscous, jnp.concatenate(rates, axis=1))
        gap = lax.axis_index("gx") - jnp.arange(groups_x)
        decay = jnp.exp(
            -(rows * jnp.maximum(jnp.abs(gap) - 1, 0))[:, None, None] * alpha[None]
        )
        extra = [
            jnp.sum(jnp.where((gap > 0)[:, None, None], decay * p, 0.0), axis=0),
            jnp.sum(jnp.where((gap < 0)[:, None, None], decay * q, 0.0), axis=0),
        ]
    ring = channels // 2 + 8
    damped, coefs, stepped = pl.pallas_call(
        functools.partial(first_step_kernel, groups_x, groups_y, paired),
        out_shape=[
            shape((rows * channels, columns), bf16),
            shape((7, 16, columns), f32),
            shape((rows + 2, 2, ring, columns), f32),
        ],
        in_specs=[vmem] * (8 + len(extra)),
        out_specs=[vmem] * 3,
        scratch_shapes=[
            pltpu.VMEM((rows, channels, LANES), f32),
            pltpu.VMEM((rows + 4, 2, ring, columns), f32),
            pltpu.VMEM((16, columns), f32),
        ],
        compiler_params=params(),
        name="damping_or_first_step",
    )(fields, wet_cells, diff_row, y, e1, e3, e2, e4, *extra)

    surface_sum, near, far = pl.pallas_call(
        functools.partial(heat_kernel, rows),
        out_shape=[
            shape((cells, LANES), f32),
            shape((columns // 16, LANES), bf16),
            shape((columns // 16, LANES), bf16),
        ],
        in_specs=[vmem] * 3 + [anywhere] + [vmem] * len(parts),
        out_specs=[vmem] * 3,
        compiler_params=params(),
        name="surface_sum",
    )(e2, e4, landing, coefs, *parts)

    near = lax.ppermute(near, "gx", both_ways(ring_pairs(groups_x, 0)))
    far = lax.ppermute(far, "gx", both_ways(ring_pairs(groups_x, 1)))
    base, column = pl.pallas_call(
        second_step_kernel,
        out_shape=[shape((rows, channels, columns), f32), shape((channels, LANES), f32)],
        in_specs=[vmem] * 5,
        out_specs=[vmem] * 2,
        compiler_params=params(),
        name="inverse_or_second_step",
    )(gain_row, inverse, damped, coefs, stepped)
    return pl.pallas_call(
        functools.partial(last_kernel, groups_x, groups_y),
        out_shape=shape(fields.shape, f32),
        in_specs=[vmem] * 6,
        out_specs=hbm,
        scratch_shapes=[
            pltpu.VMEM((rows, channels, columns), f32),
            pltpu.VMEM((16, columns), f32),
            pltpu.VMEM((2, rows, columns), f32),
            pltpu.SemaphoreType.DMA((rows,)),
        ],
        compiler_params=params(),
        name="add_surface_terms",
    )(column, base, coefs, surface_sum, near, far)


def solution(mesh):
    in_specs = (
        P("comp", "gx", "gy", None),
        P("gx", None),
        P(),
        P(),
        P(),
        P("gx", "gy", None, None),
        P("gx", "gy", None, None),
        P("gx", "gy"),
        P("gx", "gy", None, None, None),
        P("gx", "gy", None, None),
        P("gx", "gy", None, None),
        P("gx", "gy"),
        P("gx", "gy", None, None, None),
    )
    out_specs = P("comp", "gx", "gy", None)
    return jax.shard_map(local, mesh=mesh, in_specs=in_specs, out_specs=out_specs, check_vma=False)
```

```python
import functools

import jax
import jax.numpy as jnp
import numpy as np
from jax import lax
from jax.experimental import pallas as pl
from jax.experimental.pallas import tpu as pltpu
from jax.sharding import PartitionSpec as P

spread_rate = 0.2
mixing_rate = 0.1
heat_gain = 0.5
salt_gain = -0.25
LANES = 128
f32 = jnp.float32
bf16 = jnp.bfloat16


def fourier_tables(columns):
    half = columns // 2
    forward, inverse = [], []
    for first in (0, 1):
        waves = np.arange(first, half, 2)
        phase = np.arange(half)[:, None] * waves[None, :] % columns
        angles = phase * (2.0 * np.pi / columns)
        table = np.concatenate([np.cos(angles), np.sin(angles)], axis=1)
        weight = np.where(waves == 0, 1.0, 2.0) / columns
        forward.append(table)
        inverse.append(table.T * np.concatenate([weight, weight])[:, None])
    return (
        jnp.asarray(np.concatenate(forward).astype(np.float32), bf16),
        jnp.asarray(np.concatenate(inverse).astype(np.float32), bf16),
    )


def wave_parts(columns):
    quarter = columns // 4
    return [
        (g, n, (g * 2 * quarter + n, (g * 2 + 1) * quarter + n))
        for g in (0, 1)
        for n in range(0, quarter, LANES)
    ]


def half_rates(group, first, count, columns):
    lane = lax.broadcasted_iota(jnp.int32, (1, count), 1) + first
    wave = (2 * lane + group).astype(f32)
    sine = jnp.sin(wave * (np.pi / columns))
    return 2.0 * sine * sine


def both_ways(pairs):
    return [p for a, b in pairs for p in ((a, b), (b, a))]


def channel_column(row, channels, first):
    n = row.shape[1]
    lane = lax.broadcasted_iota(jnp.int32, (channels, n), 1)
    sub = lax.broadcasted_iota(jnp.int32, (channels, n), 0)
    return jnp.sum(jnp.where(lane == sub + first, row, 0.0), axis=1, keepdims=True)


def to_tiles(surface):
    cols = surface.shape[1]
    return jnp.concatenate(
        [surface[:, k : k + LANES] for k in range(0, cols, LANES)], axis=0
    )


def from_tiles(tiles, rows):
    return jnp.concatenate(
        [tiles[k : k + rows] for k in range(0, tiles.shape[0], rows)], axis=1
    )


def lengthen(ref, block):
    rows = block.shape[0]
    ref[0:rows, :] = block
    if ref.shape[0] > rows:
        ref[rows:, :] = block[: ref.shape[0] - rows]


def decay_terms(diff_column, rates):
    half = 0.5 / diff_column + rates
    sinh = jnp.sqrt(half * (half + 2.0))
    grow = 1.0 + half + sinh
    return 1.0 / grow, jnp.log(grow), sinh


def edge_factors(lam, alpha, base, total, rows):
    lam2 = lam * lam
    powers = [
        jnp.exp(-2.0 * base * alpha) * lam2,
        jnp.exp(-2.0 * (total - rows - base) * alpha) * lam2,
    ]
    lows, highs = [], []
    for _ in range(rows):
        lows.append(1.0 - powers[0])
        highs.insert(0, 1.0 - powers[1])
        powers = [power * lam2 for power in powers]
    return lows, highs


def fold(values, flat_ref, r):
    channels, columns = values.shape
    half = columns // 2
    left, right = values[:, :half], values[:, half:]
    flat_ref[r * channels : (r + 1) * channels, :half] = (left + right).astype(bf16)
    flat_ref[r * channels : (r + 1) * channels, half:] = (left - right).astype(bf16)


def start_kernel(
    groups_x, paired, x_hbm, wet_hbm, flux_hbm, diff_hbm, table_hbm, *refs
):
    outs = 6 if paired else 7
    coarse_hbm, wide_hbm, *message_hbm = refs[:outs]
    coarse_ref, wide_ref, *message_ref = refs[outs : 2 * outs]
    e1_ref, e3_ref, e2_ref, e4_ref = message_ref[:4]
    if not paired:
        pq_ref = message_ref[4]
    (
        x_ref, wet_ref, flux_ref, diff_ref, table_ref, flat_ref, row_ref, edge_ref,
        factor_ref, x_sem, sem, out_sem,
    ) = refs[2 * outs :]
    rows, channels, columns = x_ref.shape
    half = columns // 2
    row_group = lax.axis_index("gx")
    col_group = lax.axis_index("gy")
    is_atmos = lax.axis_index("comp") == 0

    x_copies = [
        pltpu.make_async_copy(x_hbm.at[0, r], x_ref.at[r], x_sem.at[r]) for r in range(rows)
    ]
    surface_copies = [
        pltpu.make_async_copy(coarse_ref, coarse_hbm, out_sem.at[0]),
        pltpu.make_async_copy(wide_ref, wide_hbm, out_sem.at[1]),
    ]
    message_copies = [
        pltpu.make_async_copy(ref, hbm, out_sem.at[2 + k])
        for k, (ref, hbm) in enumerate(zip(message_ref, message_hbm))
    ]

    def send_surface():
        coarse = to_tiles(row_ref[...]).astype(bf16)
        coarse_ref[...] = coarse
        lengthen(wide_ref, coarse)
        for copy in surface_copies:
            copy.start()

    @pl.when(is_atmos)
    def _():
        flux_copy = pltpu.make_async_copy(flux_hbm, flux_ref, sem.at[0])
        diff_copy = pltpu.make_async_copy(diff_hbm, diff_ref, sem.at[1])
        table_copy = pltpu.make_async_copy(table_hbm, table_ref, sem.at[2])
        for copy in [flux_copy, diff_copy] + x_copies + [table_copy]:
            copy.start()
        first = col_group * channels
        flux_copy.wait()
        weight = channel_column(flux_ref[...], channels, first)
        diff_copy.wait()
        diff = channel_column(diff_ref[...], channels, first)
        total = rows * groups_x
        base = (row_group * rows).astype(f32)
        tiles = wave_parts(columns)
        for k, (group, n, _) in enumerate(tiles):
            lam, alpha, _ = decay_terms(diff, half_rates(group, n, LANES, columns))
            factor_ref[k, 0] = lam
            lows, highs = edge_factors(lam, alpha, base, total, rows)
            for r in range(rows):
                factor_ref[k, 1 + r] = lows[r]
                factor_ref[k, 1 + rows + r] = highs[r]
        for r in range(rows):
            x_copies[r].wait()
            row_ref[r : r + 1, :] = jnp.sum(x_ref[r] * weight, axis=0, keepdims=True)
            fold(x_ref[r], flat_ref, r)
        send_surface()
        table_copy.wait()
        for k in range(2):
            lanes = slice(k * half, (k + 1) * half)
            part = jnp.dot(
                flat_ref[:, lanes], table_ref[lanes, :], preferred_element_type=f32
            )
            for tile, (group, _, parts) in enumerate(tiles):
                if group != k:
                    continue
                lam = factor_ref[tile, 0]
                for at in parts:
                    lanes = slice(at, at + LANES)
                    here = slice(at - k * half, at - k * half + LANES)
                    p = factor_ref[tile, 1] * part[0:channels, here]
                    q = factor_ref[tile, 2 * rows] * part[(rows - 1) * channels :, here]
                    for r in range(1, rows):
                        up = part[r * channels : (r + 1) * channels, here]
                        down = part[(rows - 1 - r) * channels : (rows - r) * channels, here]
                        p = lam * p + factor_ref[tile, 1 + r] * up
                        q = lam * q + factor_ref[tile, 2 * rows - r] * down
                    if paired:
                        for mask, out in ((1, e1_ref), (2, e2_ref), (3, e3_ref)):
                            upward = row_group < (row_group ^ mask)
                            out[0:channels, lanes] = jnp.where(upward, p, q).astype(bf16)
                    else:
                        pq_ref[0, :, lanes] = p.astype(bf16)
                        pq_ref[1, :, lanes] = q.astype(bf16)
        sums_copies = [
            pltpu.make_async_copy(
                message_ref[k].at[pl.ds(0, channels)],
                message_hbm[k].at[pl.ds(0, channels)],
                out_sem.at[2 + k],
            )
            for k in range(3)
        ]
        if not paired:
            sums_copies = message_copies[4:]
        for copy in sums_copies:
            copy.start()
        for copy in surface_copies + sums_copies:
            copy.wait()

    @pl.when(jnp.logical_not(is_atmos))
    def _():
        wet_copy = pltpu.make_async_copy(wet_hbm, wet_ref, sem.at[0])
        for copy in x_copies + [wet_copy]:
            copy.start()
        gain = jnp.where(col_group == 0, 1.0, 0.0)
        for r in range(rows):
            x_copies[r].wait()
            row_ref[r : r + 1, :] = x_ref[r, 0:1, :] * gain
        send_surface()
        wet_copy.wait()
        levels = channels // 2
        lines = 2 * channels
        even_x = row_group % 2 == 0
        even_y = col_group % 2 == 0
        wet = wet_ref[...].astype(f32)
        wet = jnp.concatenate([wet, wet], axis=0).astype(bf16)

        def put(out, last):
            @pl.when(last)
            def _():
                out[0:lines, :] = x_ref[rows - 2 :].reshape(lines, columns).astype(bf16)

            @pl.when(jnp.logical_not(last))
            def _():
                out[0:lines, :] = x_ref[:2].reshape(lines, columns).astype(bf16)

            out[lines : lines + 16, :] = wet

        put(e1_ref, even_x)
        put(e3_ref, jnp.logical_not(even_x))

        def put_edges(out, level):
            for r in range(rows):
                for t in range(2):
                    at = (r * 2 + t) * 2
                    c = t * levels + level
                    edge_ref[at : at + 2, :] = x_ref[r, c : c + 2, :]
            out[0 : rows * 4, :] = edge_ref[...].astype(bf16)

        @pl.when(even_y)
        def _():
            put_edges(e2_ref, levels - 2)
            put_edges(e4_ref, 0)

        @pl.when(jnp.logical_not(even_y))
        def _():
            put_edges(e2_ref, 0)
            put_edges(e4_ref, levels - 2)

        for copy in message_copies:
            copy.start()
        for copy in surface_copies + message_copies:
            copy.wait()


def one_hot_kernel(
    rows, columns, a_src, a_dst, a_count, m_src, m_dst, m_count, src_hot_ref, dst_hot_ref,
    src_row_ref, dst_row_ref, used_ref,
):
    is_atmos = lax.axis_index("comp") == 0
    blocks, points = src_row_ref.shape
    count = jnp.where(is_atmos, m_count[0, 0], a_count[0, 0])
    block_iota = lax.broadcasted_iota(jnp.int32, (blocks, points), 0)
    used_ref[...] = jnp.where(block_iota < count, 1, 0)
    lane_iota = lax.broadcasted_iota(jnp.int32, (LANES, points), 0)
    for a_ref, m_ref, hot_ref, row_ref in (
        (a_src, m_src, src_hot_ref, src_row_ref),
        (a_dst, m_dst, dst_hot_ref, dst_row_ref),
    ):
        index = jnp.where(is_atmos, m_ref[0, 0], a_ref[0, 0])
        row = index // columns
        tile = (index // LANES) % (columns // LANES)
        row_ref[...] = tile * rows + row
        lane = index % LANES
        for b in range(blocks):
            hot_ref[:, b * points : (b + 1) * points] = jnp.where(
                lane_iota == lane[b : b + 1], 1.0, 0.0
            ).astype(bf16)


def regrid_kernel(n_surfaces, *refs):
    surfaces = refs[:n_surfaces]
    (
        src_hot_ref, dst_hot_ref, src_row_ref, dst_row_ref, used_ref, a_weight, m_weight,
        _,
        *refs,
    ) = refs[n_surfaces:]
    land_ref, *sent_refs = refs[:-4]
    weight_ref, gath_ref, val_ref, sem = refs[-4:]
    is_atmos = lax.axis_index("comp") == 0
    blocks, points = val_ref.shape
    cells = surfaces[0].shape[0]

    @pl.when(is_atmos)
    def _():
        pltpu.make_async_copy(m_weight.at[0, 0], weight_ref, sem).start()

    @pl.when(jnp.logical_not(is_atmos))
    def _():
        pltpu.make_async_copy(a_weight.at[0, 0], weight_ref, sem).start()

    pair = 2 * points
    row_iota = lax.broadcasted_iota(jnp.int32, (cells, points), 0)
    table = sum(surface[...].astype(f32) for surface in surfaces).astype(bf16)
    for b in range(0, blocks, 2):
        picked = jnp.dot(
            table, src_hot_ref[:, b * points : b * points + pair], preferred_element_type=f32
        )
        for k in range(2):
            mine = row_iota == src_row_ref[b + k : b + k + 1, :]
            part = jnp.where(mine, picked[:, k * points : (k + 1) * points], 0.0)
            gath_ref[b + k : b + k + 1, :] = jnp.sum(part, axis=0, keepdims=True)
    gathered = gath_ref[...].astype(bf16)

    @pl.when(is_atmos)
    def _():
        pltpu.make_async_copy(m_weight.at[0, 0], weight_ref, sem).wait()

    @pl.when(jnp.logical_not(is_atmos))
    def _():
        pltpu.make_async_copy(a_weight.at[0, 0], weight_ref, sem).wait()

    block_iota = lax.broadcasted_iota(jnp.int32, (blocks, points), 0)
    values = jnp.zeros((blocks, points), f32)
    for b in range(0, blocks, 2):
        terms = lax.dot_general(
            gathered,
            weight_ref[b : b + 2].reshape(pair, points),
            (((1,), (1,)), ((), ())),
            preferred_element_type=f32,
        )
        for k in range(2):
            values = jnp.where(block_iota == b + k, terms[:, k * points : (k + 1) * points], values)
    val_ref[...] = jnp.where(used_ref[...] > 0, values, 0.0)
    land = jnp.zeros((2 * cells, LANES), f32)
    for b in range(0, blocks, 2):
        spread = []
        for k in range(b, b + 2):
            value = val_ref[k : k + 1, :]
            coarse = value.astype(bf16).astype(f32)
            fine = value - coarse
            mine = row_iota == dst_row_ref[k : k + 1, :]
            spread.append(
                jnp.concatenate(
                    [jnp.where(mine, coarse, 0.0), jnp.where(mine, fine, 0.0)], axis=0
                ).astype(bf16)
            )
        land = land + lax.dot_general(
            jnp.concatenate(spread, axis=1),
            dst_hot_ref[:, b * points : b * points + pair],
            (((1,), (1,)), ((), ())),
            preferred_element_type=f32,
        )
    land = land[:cells] + land[cells:]
    land_ref[...] = land
    for sent_ref in sent_refs:
        lengthen(sent_ref, land.astype(bf16))


def heat_kernel(rows, e2_ref, e4_ref, land_ref, _, *refs):
    parts = refs[:-3]
    sum_ref, near_ref, far_ref = refs[-3:]
    cells = land_ref.shape[0]
    columns = cells // rows * LANES
    even_x = lax.axis_index("gx") % 2 == 0
    even_y = lax.axis_index("gy") % 2 == 0
    total = land_ref[...]
    for part in parts:
        total = total + part[0:cells, :].astype(f32)
    sum_ref[...] = total

    def corners(row):
        start = row * 4 // 16 * 16
        one = e2_ref[start : start + 16, :].astype(f32)
        two = e4_ref[start : start + 16, :].astype(f32)
        low = jnp.where(even_y, two, one)
        high = jnp.where(even_y, one, two)
        at = row * 4 - start
        lines = [low[at + 1 : at + 2], low[at + 3 : at + 4], high[at : at + 1], high[at + 2 : at + 3]]
        heat = from_tiles(total, rows)[row : row + 1]
        blank = jnp.zeros((3, columns), f32)
        return to_tiles(jnp.concatenate([heat] + lines + [blank], axis=0))

    first, last = corners(0), corners(rows - 1)
    near_ref[...] = jnp.where(even_x, last, first).astype(bf16)
    far_ref[...] = jnp.where(even_x, first, last).astype(bf16)


def advance(ref, r, t, coefs, size):
    ring, columns = ref.shape[2:]
    whole = ref[r, t]
    up = pltpu.roll(whole, 1, 0)[:size]
    down = pltpu.roll(whole, ring - 1, 0)[:size]
    mid = whole[:size]
    total = coefs[0] * mid + coefs[5] * (up + down)
    total = total + coefs[1] * ref[r - 1, t, 0:size, :]
    total = total + coefs[2] * ref[r + 1, t, 0:size, :]
    total = total + coefs[3] * pltpu.roll(mid, 1, 1)
    return total + coefs[4] * pltpu.roll(mid, columns - 1, 1)


def first_step_kernel(
    groups_x, groups_y, paired, x_ref, wet_ref, diff_ref, table_ref, e1_ref, e3_ref,
    e2_ref, e4_ref, *refs,
):
    if not paired:
        pin_ref, qin_ref = refs[:2]
    zb_ref, c_ref, t1_ref, y_ref, flat_ref, z_ref, t0_ref, w_ref = refs[-8:]
    _, rows, channels, columns = x_ref.shape
    row_group = lax.axis_index("gx")
    col_group = lax.axis_index("gy")
    is_atmos = lax.axis_index("comp") == 0

    @pl.when(is_atmos)
    def _():
        half = columns // 2
        for r in range(rows):
            fold(x_ref[0, r], flat_ref, r)
        for k in range(2):
            lanes = slice(k * half, (k + 1) * half)
            part = jnp.dot(
                flat_ref[:, lanes], table_ref[lanes, :], preferred_element_type=f32
            )
            y_ref[:, :, lanes] = part.reshape(rows, channels, half)
        diff = channel_column(diff_ref[...], channels, col_group * channels)
        total = rows * groups_x
        base = (row_group * rows).astype(f32)
        for group, n, parts in wave_parts(columns):
            lam, alpha, sinh = decay_terms(diff, half_rates(group, n, LANES, columns))
            scale = 1.0 / (
                2.0 * diff * sinh * (1.0 - jnp.exp(-2.0 * (total + 1) * alpha))
            )
            lows, highs = edge_factors(lam, alpha, base, total, rows)
            for part in parts:
                lanes = slice(part, part + LANES)
                if paired:
                    pin = jnp.zeros((channels, LANES), f32)
                    qin = jnp.zeros((channels, LANES), f32)
                    for mask, msg in ((1, e1_ref), (2, e2_ref), (3, e3_ref)):
                        band = row_group ^ mask
                        gap = (jnp.abs(row_group - band) - 1) * rows
                        term = jnp.exp(-gap.astype(f32) * alpha)
                        term = term * msg[0:channels, lanes].astype(f32)
                        pin = pin + jnp.where(band < row_group, term, 0.0)
                        qin = qin + jnp.where(band > row_group, term, 0.0)
                else:
                    pin = pin_ref[:, lanes]
                    qin = qin_ref[:, lanes]
                f = pin
                for r in range(rows):
                    f = lam * f + lows[r] * y_ref[r, :, lanes]
                    z_ref[r] = highs[r] * f
                g = lam * qin
                for r in reversed(range(rows)):
                    z = scale * (z_ref[r] + lows[r] * g)
                    zb_ref[r * channels : (r + 1) * channels, lanes] = z.astype(bf16)
                    g = lam * (g + highs[r] * y_ref[r, :, lanes])

    @pl.when(jnp.logical_not(is_atmos))
    def _():
        levels = channels // 2
        ring = levels + 8
        lines = 2 * channels
        first_x = row_group == 0
        last_x = row_group == groups_x - 1
        top = col_group == 0
        bottom = col_group == groups_y - 1
        even_x = row_group % 2 == 0
        even_y = col_group % 2 == 0

        one = e1_ref[lines : lines + 16, :].astype(f32)
        three = e3_ref[lines : lines + 16, :].astype(f32)
        below = jnp.where(even_x, three, one)[rows - 2 : rows]
        above = jnp.where(even_x, one, three)[0:2]
        w_ref[0:2, :] = jnp.where(first_x, 0.0, below)
        w_ref[2 : rows + 2, :] = wet_ref[...].astype(f32)
        w_ref[rows + 2 : rows + 4, :] = jnp.where(last_x, 0.0, above)

        span = rows + 2
        north = w_ref[0:span, :]
        here = w_ref[1 : span + 1, :]
        south = w_ref[2 : span + 2, :]
        west = pltpu.roll(here, 1, 1)
        east = pltpu.roll(here, columns - 1, 1)
        c_ref[0, 0:span, :] = here * (
            1.0 - 2.0 * mixing_rate - spread_rate * (north + south + west + east)
        )
        c_ref[1, 0:span, :] = spread_rate * here * north
        c_ref[2, 0:span, :] = spread_rate * here * south
        c_ref[3, 0:span, :] = spread_rate * here * west
        c_ref[4, 0:span, :] = spread_rate * here * east
        c_ref[5, 0:span, :] = mixing_rate * here
        c_ref[6, 0:span, :] = here

        one = e1_ref[0:lines, :].astype(f32)
        three = e3_ref[0:lines, :].astype(f32)
        below = jnp.where(even_x, three, one)
        above = jnp.where(even_x, one, three)
        blank = jnp.zeros((8, columns), f32)
        for k in range(2):
            for t in range(2):
                c = k * channels + t * levels
                t0_ref[k, t, 0:levels, :] = below[c : c + levels]
                t0_ref[rows + 2 + k, t, 0:levels, :] = above[c : c + levels]
                t0_ref[k, t, levels:ring, :] = blank
                t0_ref[rows + 2 + k, t, levels:ring, :] = blank
        one = e2_ref[...].astype(f32)
        two = e4_ref[0 : 4 * rows, :].astype(f32)
        before = jnp.where(even_y, two, one)
        after = jnp.where(even_y, one, two)
        for r in range(rows):
            for t in range(2):
                k = (r * 2 + t) * 2
                t0_ref[r + 2, t, 0:levels, :] = x_ref[0, r, t * levels : (t + 1) * levels, :]
                t0_ref[r + 2, t, levels : levels + 2, :] = after[k : k + 2]
                t0_ref[r + 2, t, ring - 2 : ring, :] = before[k : k + 2]

        def close(ref, r):
            for t in range(2):
                ref[r, t, ring - 1 : ring, :] = jnp.where(
                    top, ref[r, t, 0:1, :], ref[r, t, ring - 1 : ring, :]
                )
                ref[r, t, levels : levels + 1, :] = jnp.where(
                    bottom, ref[r, t, levels - 1 : levels, :], ref[r, t, levels : levels + 1, :]
                )

        def first(r, carry):
            coefs = [c_ref[k, pl.ds(r, 1), :] for k in range(6)]
            close(t0_ref, r + 1)
            for t in range(2):
                t1_ref[r, t] = advance(t0_ref, r + 1, t, coefs, ring)
            close(t1_ref, r)
            return carry

        lax.fori_loop(0, span, first, 0)


def second_step_kernel(gain_ref, table_ref, zb_ref, c_ref, t1_ref, base_ref, column_ref):
    rows, channels, columns = base_ref.shape
    is_atmos = lax.axis_index("comp") == 0

    @pl.when(is_atmos)
    def _():
        response = channel_column(gain_ref[...], channels, lax.axis_index("gy") * channels)
        column_ref[...] = jnp.broadcast_to(response, column_ref.shape)
        half = columns // 2
        step = 256
        for n in range(0, half, step):
            even, odd = [
                jnp.dot(
                    zb_ref[:, k * half : (k + 1) * half],
                    table_ref[k * half : (k + 1) * half, n : n + step],
                    preferred_element_type=f32,
                ).reshape(rows, channels, step)
                for k in range(2)
            ]
            base_ref[:, :, n : n + step] = even + odd
            base_ref[:, :, n + half : n + half + step] = even - odd

    @pl.when(jnp.logical_not(is_atmos))
    def _():
        levels = channels // 2

        def second(r, carry):
            coefs = [c_ref[k, pl.ds(r, 1), :] for k in range(6)]
            for t in range(2):
                c = t * levels
                base_ref[r - 1, c : c + levels, :] = advance(t1_ref, r, t, coefs, levels)
            return carry

        lax.fori_loop(1, rows + 1, second, 0)


def last_kernel(
    groups_x, groups_y, column_ref, base_ref, c_ref, sum_ref, near_ref, far_ref, out_hbm,
    out_ref, e_ref, heat_ref, sem,
):
    rows, channels, columns = out_ref.shape
    row_group = lax.axis_index("gx")
    col_group = lax.axis_index("gy")
    is_atmos = lax.axis_index("comp") == 0
    copies = [
        pltpu.make_async_copy(out_ref.at[r], out_hbm.at[0, r], sem.at[r]) for r in range(rows)
    ]

    @pl.when(is_atmos)
    def _():
        for r in range(rows):
            for k in range(columns // LANES):
                lanes = slice(k * LANES, (k + 1) * LANES)
                at = k * rows + r
                out_ref[r, :, lanes] = (
                    base_ref[r, :, lanes] + column_ref[...] * sum_ref[at : at + 1, :]
                )
            copies[r].start()

    @pl.when(jnp.logical_not(is_atmos))
    def _():
        levels = channels // 2
        even = row_group % 2 == 0
        below = jnp.where(even, far_ref[...].astype(f32), near_ref[...].astype(f32))
        above = jnp.where(even, near_ref[...].astype(f32), far_ref[...].astype(f32))

        low = from_tiles(below, 8)
        high = from_tiles(above, 8)
        by_low = c_ref[1, 1:2, :] * (c_ref[5, 0:1, :] + c_ref[5, 1:2, :])
        by_high = c_ref[2, rows : rows + 1, :] * (
            c_ref[5, rows : rows + 1, :] + c_ref[5, rows + 1 : rows + 2, :]
        )
        has_before = jnp.where(col_group > 0, 1.0, 0.0)
        has_after = jnp.where(col_group < groups_y - 1, 1.0, 0.0)

        @pl.when(col_group == 0)
        def _():
            span = rows + 2
            e_ref[0:1, :] = low[0:1]
            e_ref[1 : rows + 1, :] = from_tiles(sum_ref[...], rows)
            e_ref[rows + 1 : span, :] = high[0:1]
            e_ref[0:span, :] = c_ref[6, 0:span, :] * e_ref[0:span, :]
            own = slice(1, rows + 1)
            heat = e_ref[own, :]
            second = c_ref[5, own, :] * heat
            first = (c_ref[0, own, :] + 1.0) * heat + second
            first = first + c_ref[1, own, :] * e_ref[0:rows, :]
            first = first + c_ref[2, own, :] * e_ref[2 : rows + 2, :]
            first = first + c_ref[3, own, :] * pltpu.roll(heat, 1, 1)
            first = first + c_ref[4, own, :] * pltpu.roll(heat, columns - 1, 1)
            heat_ref[0] = first
            heat_ref[1] = second

        for r in [1, rows - 2] + list(range(2, rows - 2)) + [0, rows - 1]:
            out_ref[r] = base_ref[r]
            for t in range(2):
                c = t * levels
                for edge, factor, lines in ((0, by_low, low), (rows - 1, by_high, high)):
                    if r == edge:
                        out_ref[r, c : c + 1, :] = out_ref[r, c : c + 1, :] + (
                            has_before * factor * lines[t + 1 : t + 2]
                        )
                        d = c + levels - 1
                        out_ref[r, d : d + 1, :] = out_ref[r, d : d + 1, :] + (
                            has_after * factor * lines[t + 3 : t + 4]
                        )

            @pl.when(col_group == 0)
            def _():
                for t, gain in enumerate((heat_gain, salt_gain)):
                    c = t * levels
                    for k in range(2):
                        out_ref[r, c + k : c + k + 1, :] = (
                            out_ref[r, c + k : c + k + 1, :] + gain * heat_ref[k, r : r + 1, :]
                        )

            copies[r].start()

    for copy in copies:
        copy.wait()


def local(
    fields,
    wet_cells,
    flux_weight,
    variable_sea_response,
    diffusivity,
    a2o_source,
    a2o_target,
    a2o_count,
    a2o_weight,
    marine_air_input_index,
    marine_air_output_index,
    marine_air_piece_tally,
    marine_air_piece_factor,
):
    _, rows, channels, columns = fields.shape
    groups_x = lax.axis_size("gx")
    groups_y = lax.axis_size("gy")
    blocks, points = a2o_source.shape[2:]
    cells = rows * columns // LANES
    forward, inverse = fourier_tables(columns)
    flux_row = flux_weight[None, :]
    gain_row = variable_sea_response[None, :]
    diff_row = diffusivity[None, :]
    paired = groups_x == 4
    params = functools.partial(pltpu.CompilerParams, vmem_limit_bytes=40 * 2**20)
    vmem = pl.BlockSpec(memory_space=pltpu.VMEM)
    smem = pl.BlockSpec(memory_space=pltpu.SMEM)
    hbm = pl.BlockSpec(memory_space=pltpu.HBM)
    anywhere = pl.BlockSpec(memory_space=pl.ANY)

    def shape(dims, dtype):
        return jax.ShapeDtypeStruct(dims, dtype)

    lines = 2 * channels + 16
    shapes = [
        shape((cells, LANES), bf16),
        shape((cells + 16, LANES), bf16),
        shape((lines, columns), bf16),
        shape((lines, columns), bf16),
        shape((4 * rows, columns), bf16),
        shape((4 * rows, columns), bf16),
    ]
    if not paired:
        shapes.append(shape((2, channels, columns), bf16))
    coarse, wide, e1, e3, e2, e4, *sums = pl.pallas_call(
        functools.partial(start_kernel, groups_x, paired),
        out_shape=shapes,
        in_specs=[hbm] * 5,
        out_specs=[hbm] * len(shapes),
        scratch_shapes=[pltpu.VMEM(out.shape, out.dtype) for out in shapes]
        + [
            pltpu.VMEM((rows, channels, columns), f32),
            pltpu.VMEM((rows, columns), jnp.int32),
            pltpu.VMEM(flux_row.shape, f32),
            pltpu.VMEM(diff_row.shape, f32),
            pltpu.VMEM(forward.shape, bf16),
            pltpu.VMEM((rows * channels, columns), bf16),
            pltpu.VMEM((rows, columns), f32),
            pltpu.VMEM((4 * rows, columns), f32),
            pltpu.VMEM((columns // 2 // LANES, 2 * rows + 1, channels, LANES), f32),
            pltpu.SemaphoreType.DMA((rows,)),
            pltpu.SemaphoreType.DMA((3,)),
            pltpu.SemaphoreType.DMA((len(shapes),)),
        ],
        compiler_params=pltpu.CompilerParams(vmem_limit_bytes=58 * 2**20),
        name="surface_and_forward_or_halos",
    )(fields, wet_cells, flux_row, diff_row, forward)

    one_hots = pl.pallas_call(
        functools.partial(one_hot_kernel, rows, columns),
        out_shape=[
            shape((LANES, blocks * points), bf16),
            shape((LANES, blocks * points), bf16),
            shape((blocks, points), jnp.int32),
            shape((blocks, points), jnp.int32),
            shape((blocks, points), jnp.int32),
        ],
        in_specs=[vmem, vmem, smem] * 2,
        out_specs=[vmem] * 5,
        compiler_params=params(),
        name="one_hots",
    )(
        a2o_source, a2o_target, a2o_count,
        marine_air_input_index, marine_air_output_index, marine_air_piece_tally,
    )

    masks = [1 << bit for bit in range(groups_y.bit_length() - 1)]

    def sum_route(mask):
        return [(j, j ^ mask) for j in range(groups_y)]

    def partner_route(mask):
        return both_ways([(j, groups_y + (j ^ mask)) for j in range(groups_y)])

    surface = lax.ppermute(coarse, ("comp", "gy"), partner_route(0)).astype(f32)
    for mask in masks[:1]:
        far = lax.ppermute(wide, ("comp", "gy"), partner_route(mask))
        surface = surface + far[:cells].astype(f32)
    coarse = surface.astype(bf16)
    *one_hots, used = one_hots
    coarse, used = lax.optimization_barrier((coarse, used))
    for mask in masks[1:-1]:
        surface = surface + lax.ppermute(coarse, "gy", sum_route(mask)).astype(f32)
        coarse = surface.astype(bf16)
    surfaces = [surface] + [
        lax.ppermute(coarse, "gy", sum_route(mask)) for mask in masks[1:][-1:]
    ]

    def ring_pairs(count, odd):
        return [(a, (a + 1) % count) for a in range(odd, count, 2)]

    def flat(comp, i, j):
        return (comp * groups_x + i) * groups_y + j

    def level_route(odd):
        pairs = []
        for i in range(groups_x):
            linked = [(a, a + 1) for a in range(odd, groups_y - 1, 2)]
            alone = set(range(groups_y)) - {j for pair in linked for j in pair}
            pairs += [(flat(1, i, a), flat(1, i, b)) for a, b in linked]
            if i % 2 == 0:
                pairs += [(flat(1, i, j), flat(1, i + 1, j)) for j in sorted(alone)]
                if odd or not paired:
                    pairs += [(flat(0, i, j), flat(0, i + 1, j)) for j in range(groups_y)]
            if paired and not odd and i < i ^ 2:
                pairs += [(flat(0, i, j), flat(0, i ^ 2, j)) for j in range(groups_y)]
        return both_ways(pairs)

    e1 = lax.ppermute(e1, "gx", both_ways(ring_pairs(groups_x, 0)))
    e3 = lax.ppermute(e3, "gx", both_ways(ring_pairs(groups_x, 1)))
    axes = ("comp", "gx", "gy")
    e2 = lax.ppermute(e2, axes, level_route(0))
    e4 = lax.ppermute(e4, axes, level_route(1))

    landing, *sent = pl.pallas_call(
        functools.partial(regrid_kernel, len(surfaces)),
        out_shape=[shape((cells, LANES), f32)]
        + [shape((cells + 16 * (mask - 1), LANES), bf16) for mask in range(1, groups_y)],
        in_specs=[vmem] * (len(surfaces) + 5) + [hbm, hbm] + [anywhere] * 1,
        out_specs=[vmem] * groups_y,
        scratch_shapes=[
            pltpu.VMEM((blocks, points, points), bf16),
            pltpu.VMEM((blocks, points), f32),
            pltpu.VMEM((blocks, points), f32),
            pltpu.SemaphoreType.DMA,
        ],
        compiler_params=params(),
        cost_estimate=pl.CostEstimate(flops=2_200_000_000, bytes_accessed=0, transcendentals=0),
        name="regrid_blocks",
    )(
        *surfaces, *one_hots, used, a2o_weight, marine_air_piece_factor, e3,
    )

    def landing_route(mask):
        pairs = [
            (flat(0, i, j), flat(0, i, j ^ mask))
            for i in range(groups_x)
            for j in range(groups_y)
            if j < j ^ mask
        ]
        pairs += [(flat(1, i, 0), flat(1, i, mask)) for i in range(groups_x)]
        pairs += [
            (flat(1, i, j), flat(1, i + 1, j))
            for i in range(0, groups_x, 2)
            for j in range(groups_y)
            if j not in (0, mask)
        ]
        return both_ways(pairs)

    parts = [
        lax.ppermute(block, axes, landing_route(mask)) for mask, block in enumerate(sent, 1)
    ]

    extra = []
    if not paired:
        p, q = jnp.moveaxis(lax.all_gather(sums[0], "gx").astype(f32), 1, 0)
        viscous = lax.dynamic_slice_in_dim(
            diffusivity, lax.axis_index("gy") * channels, channels
        )[:, None]
        rates = [half_rates(g, 0, columns // 4, columns) for g in (0, 0, 1, 1)]
        _, alpha, _ = decay_terms(viscous, jnp.concatenate(rates, axis=1))
        gap = lax.axis_index("gx") - jnp.arange(groups_x)
        decay = jnp.exp(
            -(rows * jnp.maximum(jnp.abs(gap) - 1, 0))[:, None, None] * alpha[None]
        )
        extra = [
            jnp.sum(jnp.where((gap > 0)[:, None, None], decay * p, 0.0), axis=0),
            jnp.sum(jnp.where((gap < 0)[:, None, None], decay * q, 0.0), axis=0),
        ]
    ring = channels // 2 + 8
    damped, coefs, stepped = pl.pallas_call(
        functools.partial(first_step_kernel, groups_x, groups_y, paired),
        out_shape=[
            shape((rows * channels, columns), bf16),
            shape((7, 16, columns), f32),
            shape((rows + 2, 2, ring, columns), f32),
        ],
        in_specs=[vmem] * (8 + len(extra)),
        out_specs=[vmem] * 3,
        scratch_shapes=[
            pltpu.VMEM((rows, channels, columns), f32),
            pltpu.VMEM((rows * channels, columns), bf16),
            pltpu.VMEM((rows, channels, LANES), f32),
            pltpu.VMEM((rows + 4, 2, ring, columns), f32),
            pltpu.VMEM((16, columns), f32),
        ],
        compiler_params=params(),
        name="damping_or_first_step",
    )(fields, wet_cells, diff_row, forward, e1, e3, e2, e4, *extra)

    surface_sum, near, far = pl.pallas_call(
        functools.partial(heat_kernel, rows),
        out_shape=[
            shape((cells, LANES), f32),
            shape((columns // 16, LANES), bf16),
            shape((columns // 16, LANES), bf16),
        ],
        in_specs=[vmem] * 3 + [anywhere] + [vmem] * len(parts),
        out_specs=[vmem] * 3,
        compiler_params=params(),
        name="surface_sum",
    )(e2, e4, landing, coefs, *parts)

    near = lax.ppermute(near, "gx", both_ways(ring_pairs(groups_x, 0)))
    far = lax.ppermute(far, "gx", both_ways(ring_pairs(groups_x, 1)))
    base, column = pl.pallas_call(
        second_step_kernel,
        out_shape=[shape((rows, channels, columns), f32), shape((channels, LANES), f32)],
        in_specs=[vmem] * 5,
        out_specs=[vmem] * 2,
        compiler_params=params(),
        name="inverse_or_second_step",
    )(gain_row, inverse, damped, coefs, stepped)
    return pl.pallas_call(
        functools.partial(last_kernel, groups_x, groups_y),
        out_shape=shape(fields.shape, f32),
        in_specs=[vmem] * 6,
        out_specs=hbm,
        scratch_shapes=[
            pltpu.VMEM((rows, channels, columns), f32),
            pltpu.VMEM((16, columns), f32),
            pltpu.VMEM((2, rows, columns), f32),
            pltpu.SemaphoreType.DMA((rows,)),
        ],
        compiler_params=params(),
        name="add_surface_terms",
    )(column, base, coefs, surface_sum, near, far)


def solution(mesh):
    in_specs = (
        P("comp", "gx", "gy", None),
        P("gx", None),
        P(),
        P(),
        P(),
        P("gx", "gy", None, None),
        P("gx", "gy", None, None),
        P("gx", "gy"),
        P("gx", "gy", None, None, None),
        P("gx", "gy", None, None),
        P("gx", "gy", None, None),
        P("gx", "gy"),
        P("gx", "gy", None, None, None),
    )
    out_specs = P("comp", "gx", "gy", None)
    return jax.shard_map(local, mesh=mesh, in_specs=in_specs, out_specs=out_specs, check_vma=False)
```

```python
import functools

import jax
import jax.numpy as jnp
import numpy as np
from jax import lax
from jax.experimental import pallas as pl
from jax.experimental.pallas import tpu as pltpu
from jax.sharding import PartitionSpec as P

spread_rate = 0.2
mixing_rate = 0.1
heat_gain = 0.5
salt_gain = -0.25
LANES = 128
f32 = jnp.float32
bf16 = jnp.bfloat16


def fourier_tables(columns):
    half = columns // 2
    forward, inverse = [], []
    for first in (0, 1):
        waves = np.arange(first, half, 2)
        phase = np.arange(half)[:, None] * waves[None, :] % columns
        angles = phase * (2.0 * np.pi / columns)
        table = np.concatenate([np.cos(angles), np.sin(angles)], axis=1)
        weight = np.where(waves == 0, 1.0, 2.0) / columns
        forward.append(table)
        inverse.append(table.T * np.concatenate([weight, weight])[:, None])
    return (
        jnp.asarray(np.concatenate(forward).astype(np.float32), bf16),
        jnp.asarray(np.concatenate(inverse).astype(np.float32), bf16),
    )


def wave_parts(columns):
    quarter = columns // 4
    return [
        (g, n, (g * 2 * quarter + n, (g * 2 + 1) * quarter + n))
        for g in (0, 1)
        for n in range(0, quarter, LANES)
    ]


def half_rates(group, first, count, columns):
    lane = lax.broadcasted_iota(jnp.int32, (1, count), 1) + first
    wave = (2 * lane + group).astype(f32)
    sine = jnp.sin(wave * (np.pi / columns))
    return 2.0 * sine * sine


def both_ways(pairs):
    return [p for a, b in pairs for p in ((a, b), (b, a))]


def channel_column(row, channels, first):
    n = row.shape[1]
    lane = lax.broadcasted_iota(jnp.int32, (channels, n), 1)
    sub = lax.broadcasted_iota(jnp.int32, (channels, n), 0)
    return jnp.sum(jnp.where(lane == sub + first, row, 0.0), axis=1, keepdims=True)


def to_tiles(surface):
    cols = surface.shape[1]
    return jnp.concatenate(
        [surface[:, k : k + LANES] for k in range(0, cols, LANES)], axis=0
    )


def from_tiles(tiles, rows):
    return jnp.concatenate(
        [tiles[k : k + rows] for k in range(0, tiles.shape[0], rows)], axis=1
    )


def lengthen(ref, block):
    rows = block.shape[0]
    ref[0:rows, :] = block
    if ref.shape[0] > rows:
        ref[rows:, :] = block[: ref.shape[0] - rows]


def decay_terms(diff_column, rates):
    half = 0.5 / diff_column + rates
    sinh = jnp.sqrt(half * (half + 2.0))
    grow = 1.0 + half + sinh
    return 1.0 / grow, jnp.log(grow), sinh


def edge_factors(lam, alpha, base, total, rows):
    lam2 = lam * lam
    powers = [
        jnp.exp(-2.0 * base * alpha) * lam2,
        jnp.exp(-2.0 * (total - rows - base) * alpha) * lam2,
    ]
    lows, highs = [], []
    for _ in range(rows):
        lows.append(1.0 - powers[0])
        highs.insert(0, 1.0 - powers[1])
        powers = [power * lam2 for power in powers]
    return lows, highs


def fold(values, flat_ref, r):
    channels, columns = values.shape
    half = columns // 2
    left, right = values[:, :half], values[:, half:]
    flat_ref[r * channels : (r + 1) * channels, :half] = (left + right).astype(bf16)
    flat_ref[r * channels : (r + 1) * channels, half:] = (left - right).astype(bf16)


def start_kernel(
    groups_x, paired, x_hbm, wet_hbm, flux_hbm, diff_hbm, table_hbm, *refs
):
    outs = 6 if paired else 7
    coarse_hbm, wide_hbm, *message_hbm = refs[:outs]
    coarse_ref, wide_ref, *message_ref = refs[outs : 2 * outs]
    e1_ref, e3_ref, e2_ref, e4_ref = message_ref[:4]
    if not paired:
        pq_ref = message_ref[4]
    (
        x_ref, wet_ref, flux_ref, diff_ref, table_ref, flat_ref, row_ref, edge_ref,
        factor_ref, x_sem, sem, out_sem,
    ) = refs[2 * outs :]
    rows, channels, columns = x_ref.shape
    half = columns // 2
    row_group = lax.axis_index("gx")
    col_group = lax.axis_index("gy")
    is_atmos = lax.axis_index("comp") == 0

    x_copies = [
        pltpu.make_async_copy(x_hbm.at[0, r], x_ref.at[r], x_sem.at[r]) for r in range(rows)
    ]
    surface_copies = [
        pltpu.make_async_copy(coarse_ref, coarse_hbm, out_sem.at[0]),
        pltpu.make_async_copy(wide_ref, wide_hbm, out_sem.at[1]),
    ]
    message_copies = [
        pltpu.make_async_copy(ref, hbm, out_sem.at[2 + k])
        for k, (ref, hbm) in enumerate(zip(message_ref, message_hbm))
    ]

    def send_surface():
        coarse = to_tiles(row_ref[...]).astype(bf16)
        coarse_ref[...] = coarse
        lengthen(wide_ref, coarse)
        for copy in surface_copies:
            copy.start()

    @pl.when(is_atmos)
    def _():
        flux_copy = pltpu.make_async_copy(flux_hbm, flux_ref, sem.at[0])
        diff_copy = pltpu.make_async_copy(diff_hbm, diff_ref, sem.at[1])
        table_copies = [
            pltpu.make_async_copy(
                table_hbm.at[pl.ds(k * half, half)], table_ref.at[pl.ds(k * half, half)], sem.at[2 + k]
            )
            for k in range(2)
        ]
        for copy in [flux_copy, diff_copy] + x_copies + table_copies:
            copy.start()
        first = col_group * channels
        flux_copy.wait()
        weight = channel_column(flux_ref[...], channels, first)
        diff_copy.wait()
        diff = channel_column(diff_ref[...], channels, first)
        total = rows * groups_x
        base = (row_group * rows).astype(f32)
        tiles = wave_parts(columns)
        for k, (group, n, _) in enumerate(tiles):
            lam, alpha, _ = decay_terms(diff, half_rates(group, n, LANES, columns))
            factor_ref[k, 0] = lam
            lows, highs = edge_factors(lam, alpha, base, total, rows)
            for r in range(rows):
                factor_ref[k, 1 + r] = lows[r]
                factor_ref[k, 1 + rows + r] = highs[r]
        for r in range(rows):
            x_copies[r].wait()
            row_ref[r : r + 1, :] = jnp.sum(x_ref[r] * weight, axis=0, keepdims=True)
            fold(x_ref[r], flat_ref, r)
        send_surface()
        for k in range(2):
            table_copies[k].wait()
            lanes = slice(k * half, (k + 1) * half)
            part = jnp.dot(
                flat_ref[:, lanes], table_ref[lanes, :], preferred_element_type=f32
            )
            for tile, (group, _, parts) in enumerate(tiles):
                if group != k:
                    continue
                lam = factor_ref[tile, 0]
                for at in parts:
                    lanes = slice(at, at + LANES)
                    here = slice(at - k * half, at - k * half + LANES)
                    p = factor_ref[tile, 1] * part[0:channels, here]
                    q = factor_ref[tile, 2 * rows] * part[(rows - 1) * channels :, here]
                    for r in range(1, rows):
                        up = part[r * channels : (r + 1) * channels, here]
                        down = part[(rows - 1 - r) * channels : (rows - r) * channels, here]
                        p = lam * p + factor_ref[tile, 1 + r] * up
                        q = lam * q + factor_ref[tile, 2 * rows - r] * down
                    if paired:
                        for mask, out in ((1, e1_ref), (2, e2_ref), (3, e3_ref)):
                            upward = row_group < (row_group ^ mask)
                            out[0:channels, lanes] = jnp.where(upward, p, q).astype(bf16)
                    else:
                        pq_ref[0, :, lanes] = p.astype(bf16)
                        pq_ref[1, :, lanes] = q.astype(bf16)
        sums_copies = [
            pltpu.make_async_copy(
                message_ref[k].at[pl.ds(0, channels)],
                message_hbm[k].at[pl.ds(0, channels)],
                out_sem.at[2 + k],
            )
            for k in range(3)
        ]
        if not paired:
            sums_copies = message_copies[4:]
        for copy in sums_copies:
            copy.start()
        for copy in surface_copies + sums_copies:
            copy.wait()

    @pl.when(jnp.logical_not(is_atmos))
    def _():
        wet_copy = pltpu.make_async_copy(wet_hbm, wet_ref, sem.at[0])
        for copy in x_copies + [wet_copy]:
            copy.start()
        gain = jnp.where(col_group == 0, 1.0, 0.0)
        for r in range(rows):
            x_copies[r].wait()
            row_ref[r : r + 1, :] = x_ref[r, 0:1, :] * gain
        send_surface()
        wet_copy.wait()
        levels = channels // 2
        lines = 2 * channels
        even_x = row_group % 2 == 0
        even_y = col_group % 2 == 0
        wet = wet_ref[...].astype(f32)
        wet = jnp.concatenate([wet, wet], axis=0).astype(bf16)

        def put(out, last):
            @pl.when(last)
            def _():
                out[0:lines, :] = x_ref[rows - 2 :].reshape(lines, columns).astype(bf16)

            @pl.when(jnp.logical_not(last))
            def _():
                out[0:lines, :] = x_ref[:2].reshape(lines, columns).astype(bf16)

            out[lines : lines + 16, :] = wet

        put(e1_ref, even_x)
        put(e3_ref, jnp.logical_not(even_x))

        def put_edges(out, level):
            for r in range(rows):
                for t in range(2):
                    at = (r * 2 + t) * 2
                    c = t * levels + level
                    edge_ref[at : at + 2, :] = x_ref[r, c : c + 2, :]
            out[0 : rows * 4, :] = edge_ref[...].astype(bf16)

        @pl.when(even_y)
        def _():
            put_edges(e2_ref, levels - 2)
            put_edges(e4_ref, 0)

        @pl.when(jnp.logical_not(even_y))
        def _():
            put_edges(e2_ref, 0)
            put_edges(e4_ref, levels - 2)

        for copy in message_copies:
            copy.start()
        for copy in surface_copies + message_copies:
            copy.wait()


def one_hot_kernel(
    rows, columns, a_src, a_dst, a_count, m_src, m_dst, m_count, src_hot_ref, dst_hot_ref,
    src_row_ref, dst_row_ref, used_ref,
):
    is_atmos = lax.axis_index("comp") == 0
    blocks, points = src_row_ref.shape
    count = jnp.where(is_atmos, m_count[0, 0], a_count[0, 0])
    block_iota = lax.broadcasted_iota(jnp.int32, (blocks, points), 0)
    used_ref[...] = jnp.where(block_iota < count, 1, 0)
    lane_iota = lax.broadcasted_iota(jnp.int32, (LANES, points), 0)
    for a_ref, m_ref, hot_ref, row_ref in (
        (a_src, m_src, src_hot_ref, src_row_ref),
        (a_dst, m_dst, dst_hot_ref, dst_row_ref),
    ):
        index = jnp.where(is_atmos, m_ref[0, 0], a_ref[0, 0])
        row = index // columns
        tile = (index // LANES) % (columns // LANES)
        row_ref[...] = tile * rows + row
        lane = index % LANES
        for b in range(blocks):
            hot_ref[:, b * points : (b + 1) * points] = jnp.where(
                lane_iota == lane[b : b + 1], 1.0, 0.0
            ).astype(bf16)


def regrid_kernel(n_surfaces, *refs):
    surfaces = refs[:n_surfaces]
    (
        src_hot_ref, dst_hot_ref, src_row_ref, dst_row_ref, used_ref, a_weight, m_weight,
        _,
        *refs,
    ) = refs[n_surfaces:]
    land_ref, *sent_refs = refs[:-4]
    weight_ref, gath_ref, val_ref, sem = refs[-4:]
    is_atmos = lax.axis_index("comp") == 0
    blocks, points = val_ref.shape
    cells = surfaces[0].shape[0]

    @pl.when(is_atmos)
    def _():
        pltpu.make_async_copy(m_weight.at[0, 0], weight_ref, sem).start()

    @pl.when(jnp.logical_not(is_atmos))
    def _():
        pltpu.make_async_copy(a_weight.at[0, 0], weight_ref, sem).start()

    pair = 2 * points
    row_iota = lax.broadcasted_iota(jnp.int32, (cells, points), 0)
    table = sum(surface[...].astype(f32) for surface in surfaces).astype(bf16)
    for b in range(0, blocks, 2):
        picked = jnp.dot(
            table, src_hot_ref[:, b * points : b * points + pair], preferred_element_type=f32
        )
        for k in range(2):
            mine = row_iota == src_row_ref[b + k : b + k + 1, :]
            part = jnp.where(mine, picked[:, k * points : (k + 1) * points], 0.0)
            gath_ref[b + k : b + k + 1, :] = jnp.sum(part, axis=0, keepdims=True)
    gathered = gath_ref[...].astype(bf16)

    @pl.when(is_atmos)
    def _():
        pltpu.make_async_copy(m_weight.at[0, 0], weight_ref, sem).wait()

    @pl.when(jnp.logical_not(is_atmos))
    def _():
        pltpu.make_async_copy(a_weight.at[0, 0], weight_ref, sem).wait()

    block_iota = lax.broadcasted_iota(jnp.int32, (blocks, points), 0)
    values = jnp.zeros((blocks, points), f32)
    for b in range(0, blocks, 2):
        terms = lax.dot_general(
            gathered,
            weight_ref[b : b + 2].reshape(pair, points),
            (((1,), (1,)), ((), ())),
            preferred_element_type=f32,
        )
        for k in range(2):
            values = jnp.where(block_iota == b + k, terms[:, k * points : (k + 1) * points], values)
    val_ref[...] = jnp.where(used_ref[...] > 0, values, 0.0)
    land = jnp.zeros((2 * cells, LANES), f32)
    for b in range(0, blocks, 2):
        spread = []
        for k in range(b, b + 2):
            value = val_ref[k : k + 1, :]
            coarse = value.astype(bf16).astype(f32)
            fine = value - coarse
            mine = row_iota == dst_row_ref[k : k + 1, :]
            spread.append(
                jnp.concatenate(
                    [jnp.where(mine, coarse, 0.0), jnp.where(mine, fine, 0.0)], axis=0
                ).astype(bf16)
            )
        land = land + lax.dot_general(
            jnp.concatenate(spread, axis=1),
            dst_hot_ref[:, b * points : b * points + pair],
            (((1,), (1,)), ((), ())),
            preferred_element_type=f32,
        )
    land = land[:cells] + land[cells:]
    land_ref[...] = land
    for sent_ref in sent_refs:
        lengthen(sent_ref, land.astype(bf16))


def heat_kernel(rows, e2_ref, e4_ref, land_ref, _, *refs):
    parts = refs[:-3]
    sum_ref, near_ref, far_ref = refs[-3:]
    cells = land_ref.shape[0]
    columns = cells // rows * LANES
    even_x = lax.axis_index("gx") % 2 == 0
    even_y = lax.axis_index("gy") % 2 == 0
    total = land_ref[...]
    for part in parts:
        total = total + part[0:cells, :].astype(f32)
    sum_ref[...] = total

    def corners(row):
        start = row * 4 // 16 * 16
        one = e2_ref[start : start + 16, :].astype(f32)
        two = e4_ref[start : start + 16, :].astype(f32)
        low = jnp.where(even_y, two, one)
        high = jnp.where(even_y, one, two)
        at = row * 4 - start
        lines = [low[at + 1 : at + 2], low[at + 3 : at + 4], high[at : at + 1], high[at + 2 : at + 3]]
        heat = from_tiles(total, rows)[row : row + 1]
        blank = jnp.zeros((3, columns), f32)
        return to_tiles(jnp.concatenate([heat] + lines + [blank], axis=0))

    first, last = corners(0), corners(rows - 1)
    near_ref[...] = jnp.where(even_x, last, first).astype(bf16)
    far_ref[...] = jnp.where(even_x, first, last).astype(bf16)


def advance(ref, r, t, coefs, size):
    ring, columns = ref.shape[2:]
    whole = ref[r, t]
    up = pltpu.roll(whole, 1, 0)[:size]
    down = pltpu.roll(whole, ring - 1, 0)[:size]
    mid = whole[:size]
    total = coefs[0] * mid + coefs[5] * (up + down)
    total = total + coefs[1] * ref[r - 1, t, 0:size, :]
    total = total + coefs[2] * ref[r + 1, t, 0:size, :]
    total = total + coefs[3] * pltpu.roll(mid, 1, 1)
    return total + coefs[4] * pltpu.roll(mid, columns - 1, 1)


def first_step_kernel(
    groups_x, groups_y, paired, x_ref, wet_ref, diff_ref, table_ref, e1_ref, e3_ref,
    e2_ref, e4_ref, *refs,
):
    if not paired:
        pin_ref, qin_ref = refs[:2]
    zb_ref, c_ref, t1_ref, y_ref, flat_ref, z_ref, t0_ref, w_ref = refs[-8:]
    _, rows, channels, columns = x_ref.shape
    row_group = lax.axis_index("gx")
    col_group = lax.axis_index("gy")
    is_atmos = lax.axis_index("comp") == 0

    @pl.when(is_atmos)
    def _():
        half = columns // 2
        for r in range(rows):
            fold(x_ref[0, r], flat_ref, r)
        for k in range(2):
            lanes = slice(k * half, (k + 1) * half)
            part = jnp.dot(
                flat_ref[:, lanes], table_ref[lanes, :], preferred_element_type=f32
            )
            y_ref[:, :, lanes] = part.reshape(rows, channels, half)
        diff = channel_column(diff_ref[...], channels, col_group * channels)
        total = rows * groups_x
        base = (row_group * rows).astype(f32)
        for group, n, parts in wave_parts(columns):
            lam, alpha, sinh = decay_terms(diff, half_rates(group, n, LANES, columns))
            scale = 1.0 / (
                2.0 * diff * sinh * (1.0 - jnp.exp(-2.0 * (total + 1) * alpha))
            )
            lows, highs = edge_factors(lam, alpha, base, total, rows)
            for part in parts:
                lanes = slice(part, part + LANES)
                if paired:
                    pin = jnp.zeros((channels, LANES), f32)
                    qin = jnp.zeros((channels, LANES), f32)
                    for mask, msg in ((1, e1_ref), (2, e2_ref), (3, e3_ref)):
                        band = row_group ^ mask
                        gap = (jnp.abs(row_group - band) - 1) * rows
                        term = jnp.exp(-gap.astype(f32) * alpha)
                        term = term * msg[0:channels, lanes].astype(f32)
                        pin = pin + jnp.where(band < row_group, term, 0.0)
                        qin = qin + jnp.where(band > row_group, term, 0.0)
                else:
                    pin = pin_ref[:, lanes]
                    qin = qin_ref[:, lanes]
                f = pin
                for r in range(rows):
                    f = lam * f + lows[r] * y_ref[r, :, lanes]
                    z_ref[r] = highs[r] * f
                g = lam * qin
                for r in reversed(range(rows)):
                    z = scale * (z_ref[r] + lows[r] * g)
                    zb_ref[r * channels : (r + 1) * channels, lanes] = z.astype(bf16)
                    g = lam * (g + highs[r] * y_ref[r, :, lanes])

    @pl.when(jnp.logical_not(is_atmos))
    def _():
        levels = channels // 2
        ring = levels + 8
        lines = 2 * channels
        first_x = row_group == 0
        last_x = row_group == groups_x - 1
        top = col_group == 0
        bottom = col_group == groups_y - 1
        even_x = row_group % 2 == 0
        even_y = col_group % 2 == 0

        one = e1_ref[lines : lines + 16, :].astype(f32)
        three = e3_ref[lines : lines + 16, :].astype(f32)
        below = jnp.where(even_x, three, one)[rows - 2 : rows]
        above = jnp.where(even_x, one, three)[0:2]
        w_ref[0:2, :] = jnp.where(first_x, 0.0, below)
        w_ref[2 : rows + 2, :] = wet_ref[...].astype(f32)
        w_ref[rows + 2 : rows + 4, :] = jnp.where(last_x, 0.0, above)

        span = rows + 2
        north = w_ref[0:span, :]
        here = w_ref[1 : span + 1, :]
        south = w_ref[2 : span + 2, :]
        west = pltpu.roll(here, 1, 1)
        east = pltpu.roll(here, columns - 1, 1)
        c_ref[0, 0:span, :] = here * (
            1.0 - 2.0 * mixing_rate - spread_rate * (north + south + west + east)
        )
        c_ref[1, 0:span, :] = spread_rate * here * north
        c_ref[2, 0:span, :] = spread_rate * here * south
        c_ref[3, 0:span, :] = spread_rate * here * west
        c_ref[4, 0:span, :] = spread_rate * here * east
        c_ref[5, 0:span, :] = mixing_rate * here
        c_ref[6, 0:span, :] = here

        one = e1_ref[0:lines, :].astype(f32)
        three = e3_ref[0:lines, :].astype(f32)
        below = jnp.where(even_x, three, one)
        above = jnp.where(even_x, one, three)
        blank = jnp.zeros((8, columns), f32)
        for k in range(2):
            for t in range(2):
                c = k * channels + t * levels
                t0_ref[k, t, 0:levels, :] = below[c : c + levels]
                t0_ref[rows + 2 + k, t, 0:levels, :] = above[c : c + levels]
                t0_ref[k, t, levels:ring, :] = blank
                t0_ref[rows + 2 + k, t, levels:ring, :] = blank
        one = e2_ref[...].astype(f32)
        two = e4_ref[0 : 4 * rows, :].astype(f32)
        before = jnp.where(even_y, two, one)
        after = jnp.where(even_y, one, two)
        for r in range(rows):
            for t in range(2):
                k = (r * 2 + t) * 2
                t0_ref[r + 2, t, 0:levels, :] = x_ref[0, r, t * levels : (t + 1) * levels, :]
                t0_ref[r + 2, t, levels : levels + 2, :] = after[k : k + 2]
                t0_ref[r + 2, t, ring - 2 : ring, :] = before[k : k + 2]

        def close(ref, r):
            for t in range(2):
                ref[r, t, ring - 1 : ring, :] = jnp.where(
                    top, ref[r, t, 0:1, :], ref[r, t, ring - 1 : ring, :]
                )
                ref[r, t, levels : levels + 1, :] = jnp.where(
                    bottom, ref[r, t, levels - 1 : levels, :], ref[r, t, levels : levels + 1, :]
                )

        def first(r, carry):
            coefs = [c_ref[k, pl.ds(r, 1), :] for k in range(6)]
            close(t0_ref, r + 1)
            for t in range(2):
                t1_ref[r, t] = advance(t0_ref, r + 1, t, coefs, ring)
            close(t1_ref, r)
            return carry

        lax.fori_loop(0, span, first, 0)


def second_step_kernel(gain_ref, table_ref, zb_ref, c_ref, t1_ref, base_ref, column_ref):
    rows, channels, columns = base_ref.shape
    is_atmos = lax.axis_index("comp") == 0

    @pl.when(is_atmos)
    def _():
        response = channel_column(gain_ref[...], channels, lax.axis_index("gy") * channels)
        column_ref[...] = jnp.broadcast_to(response, column_ref.shape)
        half = columns // 2
        step = 256
        for n in range(0, half, step):
            even, odd = [
                jnp.dot(
                    zb_ref[:, k * half : (k + 1) * half],
                    table_ref[k * half : (k + 1) * half, n : n + step],
                    preferred_element_type=f32,
                ).reshape(rows, channels, step)
                for k in range(2)
            ]
            base_ref[:, :, n : n + step] = even + odd
            base_ref[:, :, n + half : n + half + step] = even - odd

    @pl.when(jnp.logical_not(is_atmos))
    def _():
        levels = channels // 2

        def second(r, carry):
            coefs = [c_ref[k, pl.ds(r, 1), :] for k in range(6)]
            for t in range(2):
                c = t * levels
                base_ref[r - 1, c : c + levels, :] = advance(t1_ref, r, t, coefs, levels)
            return carry

        lax.fori_loop(1, rows + 1, second, 0)


def last_kernel(
    groups_x, groups_y, column_ref, base_ref, c_ref, sum_ref, near_ref, far_ref, out_hbm,
    out_ref, e_ref, heat_ref, sem,
):
    rows, channels, columns = out_ref.shape
    row_group = lax.axis_index("gx")
    col_group = lax.axis_index("gy")
    is_atmos = lax.axis_index("comp") == 0
    copies = [
        pltpu.make_async_copy(out_ref.at[r], out_hbm.at[0, r], sem.at[r]) for r in range(rows)
    ]

    @pl.when(is_atmos)
    def _():
        for r in range(rows):
            for k in range(columns // LANES):
                lanes = slice(k * LANES, (k + 1) * LANES)
                at = k * rows + r
                out_ref[r, :, lanes] = (
                    base_ref[r, :, lanes] + column_ref[...] * sum_ref[at : at + 1, :]
                )
            copies[r].start()

    @pl.when(jnp.logical_not(is_atmos))
    def _():
        levels = channels // 2
        even = row_group % 2 == 0
        below = jnp.where(even, far_ref[...].astype(f32), near_ref[...].astype(f32))
        above = jnp.where(even, near_ref[...].astype(f32), far_ref[...].astype(f32))

        low = from_tiles(below, 8)
        high = from_tiles(above, 8)
        by_low = c_ref[1, 1:2, :] * (c_ref[5, 0:1, :] + c_ref[5, 1:2, :])
        by_high = c_ref[2, rows : rows + 1, :] * (
            c_ref[5, rows : rows + 1, :] + c_ref[5, rows + 1 : rows + 2, :]
        )
        has_before = jnp.where(col_group > 0, 1.0, 0.0)
        has_after = jnp.where(col_group < groups_y - 1, 1.0, 0.0)

        @pl.when(col_group == 0)
        def _():
            span = rows + 2
            e_ref[0:1, :] = low[0:1]
            e_ref[1 : rows + 1, :] = from_tiles(sum_ref[...], rows)
            e_ref[rows + 1 : span, :] = high[0:1]
            e_ref[0:span, :] = c_ref[6, 0:span, :] * e_ref[0:span, :]
            own = slice(1, rows + 1)
            heat = e_ref[own, :]
            second = c_ref[5, own, :] * heat
            first = (c_ref[0, own, :] + 1.0) * heat + second
            first = first + c_ref[1, own, :] * e_ref[0:rows, :]
            first = first + c_ref[2, own, :] * e_ref[2 : rows + 2, :]
            first = first + c_ref[3, own, :] * pltpu.roll(heat, 1, 1)
            first = first + c_ref[4, own, :] * pltpu.roll(heat, columns - 1, 1)
            heat_ref[0] = first
            heat_ref[1] = second

        for r in [1, rows - 2] + list(range(2, rows - 2)) + [0, rows - 1]:
            out_ref[r] = base_ref[r]
            for t in range(2):
                c = t * levels
                for edge, factor, lines in ((0, by_low, low), (rows - 1, by_high, high)):
                    if r == edge:
                        out_ref[r, c : c + 1, :] = out_ref[r, c : c + 1, :] + (
                            has_before * factor * lines[t + 1 : t + 2]
                        )
                        d = c + levels - 1
                        out_ref[r, d : d + 1, :] = out_ref[r, d : d + 1, :] + (
                            has_after * factor * lines[t + 3 : t + 4]
                        )

            @pl.when(col_group == 0)
            def _():
                for t, gain in enumerate((heat_gain, salt_gain)):
                    c = t * levels
                    for k in range(2):
                        out_ref[r, c + k : c + k + 1, :] = (
                            out_ref[r, c + k : c + k + 1, :] + gain * heat_ref[k, r : r + 1, :]
                        )

            copies[r].start()

    for copy in copies:
        copy.wait()


def local(
    fields,
    wet_cells,
    flux_weight,
    variable_sea_response,
    diffusivity,
    a2o_source,
    a2o_target,
    a2o_count,
    a2o_weight,
    marine_air_input_index,
    marine_air_output_index,
    marine_air_piece_tally,
    marine_air_piece_factor,
):
    _, rows, channels, columns = fields.shape
    groups_x = lax.axis_size("gx")
    groups_y = lax.axis_size("gy")
    blocks, points = a2o_source.shape[2:]
    cells = rows * columns // LANES
    forward, inverse = fourier_tables(columns)
    flux_row = flux_weight[None, :]
    gain_row = variable_sea_response[None, :]
    diff_row = diffusivity[None, :]
    paired = groups_x == 4
    params = functools.partial(pltpu.CompilerParams, vmem_limit_bytes=40 * 2**20)
    vmem = pl.BlockSpec(memory_space=pltpu.VMEM)
    smem = pl.BlockSpec(memory_space=pltpu.SMEM)
    hbm = pl.BlockSpec(memory_space=pltpu.HBM)
    anywhere = pl.BlockSpec(memory_space=pl.ANY)

    def shape(dims, dtype):
        return jax.ShapeDtypeStruct(dims, dtype)

    lines = 2 * channels + 16
    shapes = [
        shape((cells, LANES), bf16),
        shape((cells + 16, LANES), bf16),
        shape((lines, columns), bf16),
        shape((lines, columns), bf16),
        shape((4 * rows, columns), bf16),
        shape((4 * rows, columns), bf16),
    ]
    if not paired:
        shapes.append(shape((2, channels, columns), bf16))
    coarse, wide, e1, e3, e2, e4, *sums = pl.pallas_call(
        functools.partial(start_kernel, groups_x, paired),
        out_shape=shapes,
        in_specs=[hbm] * 5,
        out_specs=[hbm] * len(shapes),
        scratch_shapes=[pltpu.VMEM(out.shape, out.dtype) for out in shapes]
        + [
            pltpu.VMEM((rows, channels, columns), f32),
            pltpu.VMEM((rows, columns), jnp.int32),
            pltpu.VMEM(flux_row.shape, f32),
            pltpu.VMEM(diff_row.shape, f32),
            pltpu.VMEM(forward.shape, bf16),
            pltpu.VMEM((rows * channels, columns), bf16),
            pltpu.VMEM((rows, columns), f32),
            pltpu.VMEM((4 * rows, columns), f32),
            pltpu.VMEM((columns // 2 // LANES, 2 * rows + 1, channels, LANES), f32),
            pltpu.SemaphoreType.DMA((rows,)),
            pltpu.SemaphoreType.DMA((4,)),
            pltpu.SemaphoreType.DMA((len(shapes),)),
        ],
        compiler_params=pltpu.CompilerParams(vmem_limit_bytes=58 * 2**20),
        name="surface_and_forward_or_halos",
    )(fields, wet_cells, flux_row, diff_row, forward)

    one_hots = pl.pallas_call(
        functools.partial(one_hot_kernel, rows, columns),
        out_shape=[
            shape((LANES, blocks * points), bf16),
            shape((LANES, blocks * points), bf16),
            shape((blocks, points), jnp.int32),
            shape((blocks, points), jnp.int32),
            shape((blocks, points), jnp.int32),
        ],
        in_specs=[vmem, vmem, smem] * 2,
        out_specs=[vmem] * 5,
        compiler_params=params(),
        name="one_hots",
    )(
        a2o_source, a2o_target, a2o_count,
        marine_air_input_index, marine_air_output_index, marine_air_piece_tally,
    )

    masks = [1 << bit for bit in reversed(range(groups_y.bit_length() - 1))]

    def sum_route(mask):
        return [(j, j ^ mask) for j in range(groups_y)]

    def partner_route(mask):
        return both_ways([(j, groups_y + (j ^ mask)) for j in range(groups_y)])

    surface = lax.ppermute(coarse, ("comp", "gy"), partner_route(0)).astype(f32)
    for mask in masks[:1]:
        far = lax.ppermute(wide, ("comp", "gy"), partner_route(mask))
        surface = surface + far[:cells].astype(f32)
    coarse = surface.astype(bf16)
    *one_hots, used = one_hots
    coarse, used = lax.optimization_barrier((coarse, used))
    for mask in masks[1:-1]:
        surface = surface + lax.ppermute(coarse, "gy", sum_route(mask)).astype(f32)
        coarse = surface.astype(bf16)
    surfaces = [surface] + [
        lax.ppermute(coarse, "gy", sum_route(mask)) for mask in masks[1:][-1:]
    ]

    def ring_pairs(count, odd):
        return [(a, (a + 1) % count) for a in range(odd, count, 2)]

    def flat(comp, i, j):
        return (comp * groups_x + i) * groups_y + j

    def level_route(odd):
        pairs = []
        for i in range(groups_x):
            linked = [(a, a + 1) for a in range(odd, groups_y - 1, 2)]
            alone = set(range(groups_y)) - {j for pair in linked for j in pair}
            pairs += [(flat(1, i, a), flat(1, i, b)) for a, b in linked]
            if i % 2 == 0:
                pairs += [(flat(1, i, j), flat(1, i + 1, j)) for j in sorted(alone)]
                if odd or not paired:
                    pairs += [(flat(0, i, j), flat(0, i + 1, j)) for j in range(groups_y)]
            if paired and not odd and i < i ^ 2:
                pairs += [(flat(0, i, j), flat(0, i ^ 2, j)) for j in range(groups_y)]
        return both_ways(pairs)

    e1 = lax.ppermute(e1, "gx", both_ways(ring_pairs(groups_x, 0)))
    e3 = lax.ppermute(e3, "gx", both_ways(ring_pairs(groups_x, 1)))
    axes = ("comp", "gx", "gy")
    e2 = lax.ppermute(e2, axes, level_route(0))
    e4 = lax.ppermute(e4, axes, level_route(1))

    landing, *sent = pl.pallas_call(
        functools.partial(regrid_kernel, len(surfaces)),
        out_shape=[shape((cells, LANES), f32)]
        + [shape((cells + 16 * (mask - 1), LANES), bf16) for mask in range(1, groups_y)],
        in_specs=[vmem] * (len(surfaces) + 5) + [hbm, hbm] + [anywhere] * 1,
        out_specs=[vmem] * groups_y,
        scratch_shapes=[
            pltpu.VMEM((blocks, points, points), bf16),
            pltpu.VMEM((blocks, points), f32),
            pltpu.VMEM((blocks, points), f32),
            pltpu.SemaphoreType.DMA,
        ],
        compiler_params=params(),
        cost_estimate=pl.CostEstimate(flops=2_200_000_000, bytes_accessed=0, transcendentals=0),
        name="regrid_blocks",
    )(
        *surfaces, *one_hots, used, a2o_weight, marine_air_piece_factor, e3,
    )

    def landing_route(mask):
        pairs = [
            (flat(0, i, j), flat(0, i, j ^ mask))
            for i in range(groups_x)
            for j in range(groups_y)
            if j < j ^ mask
        ]
        pairs += [(flat(1, i, 0), flat(1, i, mask)) for i in range(groups_x)]
        pairs += [
            (flat(1, i, j), flat(1, i + 1, j))
            for i in range(0, groups_x, 2)
            for j in range(groups_y)
            if j not in (0, mask)
        ]
        return both_ways(pairs)

    parts = [
        lax.ppermute(block, axes, landing_route(mask)) for mask, block in enumerate(sent, 1)
    ]

    extra = []
    if not paired:
        p, q = jnp.moveaxis(lax.all_gather(sums[0], "gx").astype(f32), 1, 0)
        viscous = lax.dynamic_slice_in_dim(
            diffusivity, lax.axis_index("gy") * channels, channels
        )[:, None]
        rates = [half_rates(g, 0, columns // 4, columns) for g in (0, 0, 1, 1)]
        _, alpha, _ = decay_terms(viscous, jnp.concatenate(rates, axis=1))
        gap = lax.axis_index("gx") - jnp.arange(groups_x)
        decay = jnp.exp(
            -(rows * jnp.maximum(jnp.abs(gap) - 1, 0))[:, None, None] * alpha[None]
        )
        extra = [
            jnp.sum(jnp.where((gap > 0)[:, None, None], decay * p, 0.0), axis=0),
            jnp.sum(jnp.where((gap < 0)[:, None, None], decay * q, 0.0), axis=0),
        ]
    ring = channels // 2 + 8
    damped, coefs, stepped = pl.pallas_call(
        functools.partial(first_step_kernel, groups_x, groups_y, paired),
        out_shape=[
            shape((rows * channels, columns), bf16),
            shape((7, 16, columns), f32),
            shape((rows + 2, 2, ring, columns), f32),
        ],
        in_specs=[vmem] * (8 + len(extra)),
        out_specs=[vmem] * 3,
        scratch_shapes=[
            pltpu.VMEM((rows, channels, columns), f32),
            pltpu.VMEM((rows * channels, columns), bf16),
            pltpu.VMEM((rows, channels, LANES), f32),
            pltpu.VMEM((rows + 4, 2, ring, columns), f32),
            pltpu.VMEM((16, columns), f32),
        ],
        compiler_params=params(),
        name="damping_or_first_step",
    )(fields, wet_cells, diff_row, forward, e1, e3, e2, e4, *extra)

    surface_sum, near, far = pl.pallas_call(
        functools.partial(heat_kernel, rows),
        out_shape=[
            shape((cells, LANES), f32),
            shape((columns // 16, LANES), bf16),
            shape((columns // 16, LANES), bf16),
        ],
        in_specs=[vmem] * 3 + [anywhere] + [vmem] * len(parts),
        out_specs=[vmem] * 3,
        compiler_params=params(),
        name="surface_sum",
    )(e2, e4, landing, coefs, *parts)

    near = lax.ppermute(near, "gx", both_ways(ring_pairs(groups_x, 0)))
    far = lax.ppermute(far, "gx", both_ways(ring_pairs(groups_x, 1)))
    base, column = pl.pallas_call(
        second_step_kernel,
        out_shape=[shape((rows, channels, columns), f32), shape((channels, LANES), f32)],
        in_specs=[vmem] * 5,
        out_specs=[vmem] * 2,
        compiler_params=params(),
        name="inverse_or_second_step",
    )(gain_row, inverse, damped, coefs, stepped)
    return pl.pallas_call(
        functools.partial(last_kernel, groups_x, groups_y),
        out_shape=shape(fields.shape, f32),
        in_specs=[vmem] * 6,
        out_specs=hbm,
        scratch_shapes=[
            pltpu.VMEM((rows, channels, columns), f32),
            pltpu.VMEM((16, columns), f32),
            pltpu.VMEM((2, rows, columns), f32),
            pltpu.SemaphoreType.DMA((rows,)),
        ],
        compiler_params=params(),
        name="add_surface_terms",
    )(column, base, coefs, surface_sum, near, far)


def solution(mesh):
    in_specs = (
        P("comp", "gx", "gy", None),
        P("gx", None),
        P(),
        P(),
        P(),
        P("gx", "gy", None, None),
        P("gx", "gy", None, None),
        P("gx", "gy"),
        P("gx", "gy", None, None, None),
        P("gx", "gy", None, None),
        P("gx", "gy", None, None),
        P("gx", "gy"),
        P("gx", "gy", None, None, None),
    )
    out_specs = P("comp", "gx", "gy", None)
    return jax.shard_map(local, mesh=mesh, in_specs=in_specs, out_specs=out_specs, check_vma=False)
```

```python
import functools

import jax
import jax.numpy as jnp
import numpy as np
from jax import lax
from jax.experimental import pallas as pl
from jax.experimental.pallas import tpu as pltpu
from jax.sharding import PartitionSpec as P

spread_rate = 0.2
mixing_rate = 0.1
heat_gain = 0.5
salt_gain = -0.25
LANES = 128
f32 = jnp.float32
bf16 = jnp.bfloat16


def fourier_tables(columns):
    half = columns // 2
    forward, inverse = [], []
    for first in (0, 1):
        waves = np.arange(first, half, 2)
        phase = np.arange(half)[:, None] * waves[None, :] % columns
        angles = phase * (2.0 * np.pi / columns)
        table = np.concatenate([np.cos(angles), np.sin(angles)], axis=1)
        weight = np.where(waves == 0, 1.0, 2.0) / columns
        forward.append(table)
        inverse.append(table.T * np.concatenate([weight, weight])[:, None])
    return (
        jnp.asarray(np.concatenate(forward).astype(np.float32), bf16),
        jnp.asarray(np.concatenate(inverse).astype(np.float32), bf16),
    )


def wave_parts(columns):
    quarter = columns // 4
    return [
        (g, n, (g * 2 * quarter + n, (g * 2 + 1) * quarter + n))
        for g in (0, 1)
        for n in range(0, quarter, LANES)
    ]


def half_rates(group, first, count, columns):
    lane = lax.broadcasted_iota(jnp.int32, (1, count), 1) + first
    wave = (2 * lane + group).astype(f32)
    sine = jnp.sin(wave * (np.pi / columns))
    return 2.0 * sine * sine


def both_ways(pairs):
    return [p for a, b in pairs for p in ((a, b), (b, a))]


def channel_column(row, channels, first):
    n = row.shape[1]
    lane = lax.broadcasted_iota(jnp.int32, (channels, n), 1)
    sub = lax.broadcasted_iota(jnp.int32, (channels, n), 0)
    return jnp.sum(jnp.where(lane == sub + first, row, 0.0), axis=1, keepdims=True)


def to_tiles(surface):
    cols = surface.shape[1]
    return jnp.concatenate(
        [surface[:, k : k + LANES] for k in range(0, cols, LANES)], axis=0
    )


def from_tiles(tiles, rows):
    return jnp.concatenate(
        [tiles[k : k + rows] for k in range(0, tiles.shape[0], rows)], axis=1
    )


def lengthen(ref, block):
    rows = block.shape[0]
    ref[0:rows, :] = block
    if ref.shape[0] > rows:
        ref[rows:, :] = block[: ref.shape[0] - rows]


def decay_terms(diff_column, rates):
    half = 0.5 / diff_column + rates
    sinh = jnp.sqrt(half * (half + 2.0))
    grow = 1.0 + half + sinh
    return 1.0 / grow, jnp.log(grow), sinh


def edge_factors(lam, alpha, base, total, rows):
    lam2 = lam * lam
    powers = [
        jnp.exp(-2.0 * base * alpha) * lam2,
        jnp.exp(-2.0 * (total - rows - base) * alpha) * lam2,
    ]
    lows, highs = [], []
    for _ in range(rows):
        lows.append(1.0 - powers[0])
        highs.insert(0, 1.0 - powers[1])
        powers = [power * lam2 for power in powers]
    return lows, highs


def fold(values, flat_ref, r):
    channels, columns = values.shape
    half = columns // 2
    left, right = values[:, :half], values[:, half:]
    flat_ref[r * channels : (r + 1) * channels, :half] = (left + right).astype(bf16)
    flat_ref[r * channels : (r + 1) * channels, half:] = (left - right).astype(bf16)


def start_kernel(
    groups_x, paired, x_hbm, wet_hbm, flux_hbm, diff_hbm, table_hbm, *refs
):
    outs = 6 if paired else 7
    coarse_hbm, wide_hbm, *message_hbm = refs[:outs]
    coarse_ref, wide_ref, *message_ref = refs[outs : 2 * outs]
    e1_ref, e3_ref, e2_ref, e4_ref = message_ref[:4]
    if not paired:
        pq_ref = message_ref[4]
    (
        x_ref, wet_ref, flux_ref, diff_ref, table_ref, flat_ref, row_ref, edge_ref,
        factor_ref, x_sem, sem, out_sem,
    ) = refs[2 * outs :]
    rows, channels, columns = x_ref.shape
    half = columns // 2
    row_group = lax.axis_index("gx")
    col_group = lax.axis_index("gy")
    is_atmos = lax.axis_index("comp") == 0

    x_copies = [
        pltpu.make_async_copy(x_hbm.at[0, r], x_ref.at[r], x_sem.at[r]) for r in range(rows)
    ]
    surface_copies = [
        pltpu.make_async_copy(coarse_ref, coarse_hbm, out_sem.at[0]),
        pltpu.make_async_copy(wide_ref, wide_hbm, out_sem.at[1]),
    ]
    message_copies = [
        pltpu.make_async_copy(ref, hbm, out_sem.at[2 + k])
        for k, (ref, hbm) in enumerate(zip(message_ref, message_hbm))
    ]

    def send_surface():
        coarse = to_tiles(row_ref[...]).astype(bf16)
        coarse_ref[...] = coarse
        lengthen(wide_ref, coarse)
        for copy in surface_copies:
            copy.start()

    @pl.when(is_atmos)
    def _():
        flux_copy = pltpu.make_async_copy(flux_hbm, flux_ref, sem.at[0])
        diff_copy = pltpu.make_async_copy(diff_hbm, diff_ref, sem.at[1])
        table_copies = [
            pltpu.make_async_copy(
                table_hbm.at[pl.ds(k * half, half)], table_ref.at[pl.ds(k * half, half)], sem.at[2 + k]
            )
            for k in range(2)
        ]
        for copy in [flux_copy, diff_copy] + x_copies + table_copies:
            copy.start()
        first = col_group * channels
        flux_copy.wait()
        weight = channel_column(flux_ref[...], channels, first)
        diff_copy.wait()
        diff = channel_column(diff_ref[...], channels, first)
        total = rows * groups_x
        base = (row_group * rows).astype(f32)
        tiles = wave_parts(columns)
        for k, (group, n, _) in enumerate(tiles):
            lam, alpha, _ = decay_terms(diff, half_rates(group, n, LANES, columns))
            factor_ref[k, 0] = lam
            lows, highs = edge_factors(lam, alpha, base, total, rows)
            for r in range(rows):
                factor_ref[k, 1 + r] = lows[r]
                factor_ref[k, 1 + rows + r] = highs[r]
        for r in range(rows):
            x_copies[r].wait()
            row_ref[r : r + 1, :] = jnp.sum(x_ref[r] * weight, axis=0, keepdims=True)
            fold(x_ref[r], flat_ref, r)
        send_surface()
        for k in range(2):
            table_copies[k].wait()
            lanes = slice(k * half, (k + 1) * half)
            part = jnp.dot(
                flat_ref[:, lanes], table_ref[lanes, :], preferred_element_type=f32
            )
            for tile, (group, _, parts) in enumerate(tiles):
                if group != k:
                    continue
                lam = factor_ref[tile, 0]
                for at in parts:
                    lanes = slice(at, at + LANES)
                    here = slice(at - k * half, at - k * half + LANES)
                    p = factor_ref[tile, 1] * part[0:channels, here]
                    q = factor_ref[tile, 2 * rows] * part[(rows - 1) * channels :, here]
                    for r in range(1, rows):
                        up = part[r * channels : (r + 1) * channels, here]
                        down = part[(rows - 1 - r) * channels : (rows - r) * channels, here]
                        p = lam * p + factor_ref[tile, 1 + r] * up
                        q = lam * q + factor_ref[tile, 2 * rows - r] * down
                    if paired:
                        for mask, out in ((1, e1_ref), (2, e2_ref), (3, e3_ref)):
                            upward = row_group < (row_group ^ mask)
                            out[0:channels, lanes] = jnp.where(upward, p, q).astype(bf16)
                    else:
                        pq_ref[0, :, lanes] = p.astype(bf16)
                        pq_ref[1, :, lanes] = q.astype(bf16)
        sums_copies = [
            pltpu.make_async_copy(
                message_ref[k].at[pl.ds(0, channels)],
                message_hbm[k].at[pl.ds(0, channels)],
                out_sem.at[2 + k],
            )
            for k in range(3)
        ]
        if not paired:
            sums_copies = message_copies[4:]
        for copy in sums_copies:
            copy.start()
        for copy in surface_copies + sums_copies:
            copy.wait()

    @pl.when(jnp.logical_not(is_atmos))
    def _():
        wet_copy = pltpu.make_async_copy(wet_hbm, wet_ref, sem.at[0])
        for copy in x_copies + [wet_copy]:
            copy.start()
        gain = jnp.where(col_group == 0, 1.0, 0.0)
        for r in range(rows):
            x_copies[r].wait()
            row_ref[r : r + 1, :] = x_ref[r, 0:1, :] * gain
        send_surface()
        wet_copy.wait()
        levels = channels // 2
        lines = 2 * channels
        even_x = row_group % 2 == 0
        even_y = col_group % 2 == 0
        wet = wet_ref[...].astype(f32)
        wet = jnp.concatenate([wet, wet], axis=0).astype(bf16)

        def put(out, last):
            @pl.when(last)
            def _():
                out[0:lines, :] = x_ref[rows - 2 :].reshape(lines, columns).astype(bf16)

            @pl.when(jnp.logical_not(last))
            def _():
                out[0:lines, :] = x_ref[:2].reshape(lines, columns).astype(bf16)

            out[lines : lines + 16, :] = wet

        put(e1_ref, even_x)
        put(e3_ref, jnp.logical_not(even_x))

        def put_edges(out, level):
            for r in range(rows):
                for t in range(2):
                    at = (r * 2 + t) * 2
                    c = t * levels + level
                    edge_ref[at : at + 2, :] = x_ref[r, c : c + 2, :]
            out[0 : rows * 4, :] = edge_ref[...].astype(bf16)

        @pl.when(even_y)
        def _():
            put_edges(e2_ref, levels - 2)
            put_edges(e4_ref, 0)

        @pl.when(jnp.logical_not(even_y))
        def _():
            put_edges(e2_ref, 0)
            put_edges(e4_ref, levels - 2)

        for copy in message_copies:
            copy.start()
        for copy in surface_copies + message_copies:
            copy.wait()


def one_hot_kernel(
    rows, columns, a_src, a_dst, a_count, m_src, m_dst, m_count, src_hot_ref, dst_hot_ref,
    src_row_ref, dst_row_ref, used_ref,
):
    is_atmos = lax.axis_index("comp") == 0
    blocks, points = src_row_ref.shape
    count = jnp.where(is_atmos, m_count[0, 0], a_count[0, 0])
    block_iota = lax.broadcasted_iota(jnp.int32, (blocks, points), 0)
    used_ref[...] = jnp.where(block_iota < count, 1, 0)
    lane_iota = lax.broadcasted_iota(jnp.int32, (LANES, points), 0)
    for a_ref, m_ref, hot_ref, row_ref in (
        (a_src, m_src, src_hot_ref, src_row_ref),
        (a_dst, m_dst, dst_hot_ref, dst_row_ref),
    ):
        index = jnp.where(is_atmos, m_ref[0, 0], a_ref[0, 0])
        row = index // columns
        tile = (index // LANES) % (columns // LANES)
        row_ref[...] = tile * rows + row
        lane = index % LANES
        for b in range(blocks):
            hot_ref[:, b * points : (b + 1) * points] = jnp.where(
                lane_iota == lane[b : b + 1], 1.0, 0.0
            ).astype(bf16)


def regrid_kernel(n_surfaces, *refs):
    surfaces = refs[:n_surfaces]
    (
        src_hot_ref, dst_hot_ref, src_row_ref, dst_row_ref, used_ref, a_weight, m_weight,
        _,
        *refs,
    ) = refs[n_surfaces:]
    land_ref, *sent_refs = refs[:-4]
    weight_ref, gath_ref, val_ref, sem = refs[-4:]
    is_atmos = lax.axis_index("comp") == 0
    blocks, points = val_ref.shape
    cells = surfaces[0].shape[0]

    @pl.when(is_atmos)
    def _():
        pltpu.make_async_copy(m_weight.at[0, 0], weight_ref, sem).start()

    @pl.when(jnp.logical_not(is_atmos))
    def _():
        pltpu.make_async_copy(a_weight.at[0, 0], weight_ref, sem).start()

    pair = 2 * points
    row_iota = lax.broadcasted_iota(jnp.int32, (cells, points), 0)
    table = sum(surface[...].astype(f32) for surface in surfaces).astype(bf16)
    for b in range(0, blocks, 2):
        picked = jnp.dot(
            table, src_hot_ref[:, b * points : b * points + pair], preferred_element_type=f32
        )
        for k in range(2):
            mine = row_iota == src_row_ref[b + k : b + k + 1, :]
            part = jnp.where(mine, picked[:, k * points : (k + 1) * points], 0.0)
            gath_ref[b + k : b + k + 1, :] = jnp.sum(part, axis=0, keepdims=True)
    gathered = gath_ref[...].astype(bf16)

    @pl.when(is_atmos)
    def _():
        pltpu.make_async_copy(m_weight.at[0, 0], weight_ref, sem).wait()

    @pl.when(jnp.logical_not(is_atmos))
    def _():
        pltpu.make_async_copy(a_weight.at[0, 0], weight_ref, sem).wait()

    block_iota = lax.broadcasted_iota(jnp.int32, (blocks, points), 0)
    values = jnp.zeros((blocks, points), f32)
    for b in range(0, blocks, 2):
        terms = lax.dot_general(
            gathered,
            weight_ref[b : b + 2].reshape(pair, points),
            (((1,), (1,)), ((), ())),
            preferred_element_type=f32,
        )
        for k in range(2):
            values = jnp.where(block_iota == b + k, terms[:, k * points : (k + 1) * points], values)
    val_ref[...] = jnp.where(used_ref[...] > 0, values, 0.0)
    land = jnp.zeros((2 * cells, LANES), f32)
    for b in range(0, blocks, 2):
        spread = []
        for k in range(b, b + 2):
            value = val_ref[k : k + 1, :]
            coarse = value.astype(bf16).astype(f32)
            fine = value - coarse
            mine = row_iota == dst_row_ref[k : k + 1, :]
            spread.append(
                jnp.concatenate(
                    [jnp.where(mine, coarse, 0.0), jnp.where(mine, fine, 0.0)], axis=0
                ).astype(bf16)
            )
        land = land + lax.dot_general(
            jnp.concatenate(spread, axis=1),
            dst_hot_ref[:, b * points : b * points + pair],
            (((1,), (1,)), ((), ())),
            preferred_element_type=f32,
        )
    land = land[:cells] + land[cells:]
    land_ref[...] = land
    for sent_ref in sent_refs:
        lengthen(sent_ref, land.astype(bf16))


def heat_kernel(rows, e2_ref, e4_ref, land_ref, _, *refs):
    parts = refs[:-3]
    sum_ref, near_ref, far_ref = refs[-3:]
    cells = land_ref.shape[0]
    columns = cells // rows * LANES
    even_x = lax.axis_index("gx") % 2 == 0
    even_y = lax.axis_index("gy") % 2 == 0
    total = land_ref[...]
    for part in parts:
        total = total + part[0:cells, :].astype(f32)
    sum_ref[...] = total

    def corners(row):
        start = row * 4 // 16 * 16
        one = e2_ref[start : start + 16, :].astype(f32)
        two = e4_ref[start : start + 16, :].astype(f32)
        low = jnp.where(even_y, two, one)
        high = jnp.where(even_y, one, two)
        at = row * 4 - start
        lines = [low[at + 1 : at + 2], low[at + 3 : at + 4], high[at : at + 1], high[at + 2 : at + 3]]
        heat = from_tiles(total, rows)[row : row + 1]
        blank = jnp.zeros((3, columns), f32)
        return to_tiles(jnp.concatenate([heat] + lines + [blank], axis=0))

    first, last = corners(0), corners(rows - 1)
    near_ref[...] = jnp.where(even_x, last, first).astype(bf16)
    far_ref[...] = jnp.where(even_x, first, last).astype(bf16)


def advance(ref, r, t, coefs, size):
    ring, columns = ref.shape[2:]
    whole = ref[r, t]
    up = pltpu.roll(whole, 1, 0)[:size]
    down = pltpu.roll(whole, ring - 1, 0)[:size]
    mid = whole[:size]
    total = coefs[0] * mid + coefs[5] * (up + down)
    total = total + coefs[1] * ref[r - 1, t, 0:size, :]
    total = total + coefs[2] * ref[r + 1, t, 0:size, :]
    total = total + coefs[3] * pltpu.roll(mid, 1, 1)
    return total + coefs[4] * pltpu.roll(mid, columns - 1, 1)


def first_step_kernel(
    groups_x, groups_y, paired, x_ref, wet_ref, diff_ref, table_ref, e1_ref, e3_ref,
    e2_ref, e4_ref, *refs,
):
    if not paired:
        pin_ref, qin_ref = refs[:2]
    zb_ref, c_ref, t1_ref, y_ref, flat_ref, z_ref, t0_ref, w_ref = refs[-8:]
    _, rows, channels, columns = x_ref.shape
    row_group = lax.axis_index("gx")
    col_group = lax.axis_index("gy")
    is_atmos = lax.axis_index("comp") == 0

    @pl.when(is_atmos)
    def _():
        half = columns // 2
        for r in range(rows):
            fold(x_ref[0, r], flat_ref, r)
        for k in range(2):
            lanes = slice(k * half, (k + 1) * half)
            part = jnp.dot(
                flat_ref[:, lanes], table_ref[lanes, :], preferred_element_type=f32
            )
            y_ref[:, :, lanes] = part.reshape(rows, channels, half)
        diff = channel_column(diff_ref[...], channels, col_group * channels)
        total = rows * groups_x
        base = (row_group * rows).astype(f32)
        for group, n, parts in wave_parts(columns):
            lam, alpha, sinh = decay_terms(diff, half_rates(group, n, LANES, columns))
            scale = 1.0 / (
                2.0 * diff * sinh * (1.0 - jnp.exp(-2.0 * (total + 1) * alpha))
            )
            lows, highs = edge_factors(lam, alpha, base, total, rows)
            for part in parts:
                lanes = slice(part, part + LANES)
                if paired:
                    pin = jnp.zeros((channels, LANES), f32)
                    qin = jnp.zeros((channels, LANES), f32)
                    for mask, msg in ((1, e1_ref), (2, e2_ref), (3, e3_ref)):
                        band = row_group ^ mask
                        gap = (jnp.abs(row_group - band) - 1) * rows
                        term = jnp.exp(-gap.astype(f32) * alpha)
                        term = term * msg[0:channels, lanes].astype(f32)
                        pin = pin + jnp.where(band < row_group, term, 0.0)
                        qin = qin + jnp.where(band > row_group, term, 0.0)
                else:
                    pin = pin_ref[:, lanes]
                    qin = qin_ref[:, lanes]
                f = pin
                for r in range(rows):
                    f = lam * f + lows[r] * y_ref[r, :, lanes]
                    z_ref[r] = highs[r] * f
                g = lam * qin
                for r in reversed(range(rows)):
                    z = scale * (z_ref[r] + lows[r] * g)
                    zb_ref[r * channels : (r + 1) * channels, lanes] = z.astype(bf16)
                    g = lam * (g + highs[r] * y_ref[r, :, lanes])

    @pl.when(jnp.logical_not(is_atmos))
    def _():
        levels = channels // 2
        ring = levels + 8
        lines = 2 * channels
        first_x = row_group == 0
        last_x = row_group == groups_x - 1
        top = col_group == 0
        bottom = col_group == groups_y - 1
        even_x = row_group % 2 == 0
        even_y = col_group % 2 == 0

        one = e1_ref[lines : lines + 16, :].astype(f32)
        three = e3_ref[lines : lines + 16, :].astype(f32)
        below = jnp.where(even_x, three, one)[rows - 2 : rows]
        above = jnp.where(even_x, one, three)[0:2]
        w_ref[0:2, :] = jnp.where(first_x, 0.0, below)
        w_ref[2 : rows + 2, :] = wet_ref[...].astype(f32)
        w_ref[rows + 2 : rows + 4, :] = jnp.where(last_x, 0.0, above)

        span = rows + 2
        north = w_ref[0:span, :]
        here = w_ref[1 : span + 1, :]
        south = w_ref[2 : span + 2, :]
        west = pltpu.roll(here, 1, 1)
        east = pltpu.roll(here, columns - 1, 1)
        c_ref[0, 0:span, :] = here * (
            1.0 - 2.0 * mixing_rate - spread_rate * (north + south + west + east)
        )
        c_ref[1, 0:span, :] = spread_rate * here * north
        c_ref[2, 0:span, :] = spread_rate * here * south
        c_ref[3, 0:span, :] = spread_rate * here * west
        c_ref[4, 0:span, :] = spread_rate * here * east
        c_ref[5, 0:span, :] = mixing_rate * here
        c_ref[6, 0:span, :] = here

        one = e1_ref[0:lines, :].astype(f32)
        three = e3_ref[0:lines, :].astype(f32)
        below = jnp.where(even_x, three, one)
        above = jnp.where(even_x, one, three)
        blank = jnp.zeros((8, columns), f32)
        for k in range(2):
            for t in range(2):
                c = k * channels + t * levels
                t0_ref[k, t, 0:levels, :] = below[c : c + levels]
                t0_ref[rows + 2 + k, t, 0:levels, :] = above[c : c + levels]
                t0_ref[k, t, levels:ring, :] = blank
                t0_ref[rows + 2 + k, t, levels:ring, :] = blank
        one = e2_ref[...].astype(f32)
        two = e4_ref[0 : 4 * rows, :].astype(f32)
        before = jnp.where(even_y, two, one)
        after = jnp.where(even_y, one, two)
        for r in range(rows):
            for t in range(2):
                k = (r * 2 + t) * 2
                t0_ref[r + 2, t, 0:levels, :] = x_ref[0, r, t * levels : (t + 1) * levels, :]
                t0_ref[r + 2, t, levels : levels + 2, :] = after[k : k + 2]
                t0_ref[r + 2, t, ring - 2 : ring, :] = before[k : k + 2]

        def close(ref, r):
            for t in range(2):
                ref[r, t, ring - 1 : ring, :] = jnp.where(
                    top, ref[r, t, 0:1, :], ref[r, t, ring - 1 : ring, :]
                )
                ref[r, t, levels : levels + 1, :] = jnp.where(
                    bottom, ref[r, t, levels - 1 : levels, :], ref[r, t, levels : levels + 1, :]
                )

        def first(r, carry):
            coefs = [c_ref[k, pl.ds(r, 1), :] for k in range(6)]
            close(t0_ref, r + 1)
            for t in range(2):
                t1_ref[r, t] = advance(t0_ref, r + 1, t, coefs, ring)
            close(t1_ref, r)
            return carry

        lax.fori_loop(0, span, first, 0)


def second_step_kernel(gain_ref, table_ref, zb_ref, c_ref, t1_ref, base_ref, column_ref):
    rows, channels, columns = base_ref.shape
    is_atmos = lax.axis_index("comp") == 0

    @pl.when(is_atmos)
    def _():
        response = channel_column(gain_ref[...], channels, lax.axis_index("gy") * channels)
        column_ref[...] = jnp.broadcast_to(response, column_ref.shape)
        half = columns // 2
        step = 256
        for n in range(0, half, step):
            even, odd = [
                jnp.dot(
                    zb_ref[:, k * half : (k + 1) * half],
                    table_ref[k * half : (k + 1) * half, n : n + step],
                    preferred_element_type=f32,
                ).reshape(rows, channels, step)
                for k in range(2)
            ]
            base_ref[:, :, n : n + step] = even + odd
            base_ref[:, :, n + half : n + half + step] = even - odd

    @pl.when(jnp.logical_not(is_atmos))
    def _():
        levels = channels // 2

        def second(r, carry):
            coefs = [c_ref[k, pl.ds(r, 1), :] for k in range(6)]
            for t in range(2):
                c = t * levels
                base_ref[r - 1, c : c + levels, :] = advance(t1_ref, r, t, coefs, levels)
            return carry

        lax.fori_loop(1, rows + 1, second, 0)


def last_kernel(
    groups_x, groups_y, column_ref, base_ref, c_ref, sum_ref, near_ref, far_ref, out_hbm,
    out_ref, e_ref, heat_ref, sem,
):
    rows, channels, columns = out_ref.shape
    row_group = lax.axis_index("gx")
    col_group = lax.axis_index("gy")
    is_atmos = lax.axis_index("comp") == 0
    copies = [
        pltpu.make_async_copy(out_ref.at[r], out_hbm.at[0, r], sem.at[r]) for r in range(rows)
    ]

    @pl.when(is_atmos)
    def _():
        for r in range(rows):
            for k in range(columns // LANES):
                lanes = slice(k * LANES, (k + 1) * LANES)
                at = k * rows + r
                out_ref[r, :, lanes] = (
                    base_ref[r, :, lanes] + column_ref[...] * sum_ref[at : at + 1, :]
                )
            copies[r].start()

    @pl.when(jnp.logical_not(is_atmos))
    def _():
        levels = channels // 2
        even = row_group % 2 == 0
        below = jnp.where(even, far_ref[...].astype(f32), near_ref[...].astype(f32))
        above = jnp.where(even, near_ref[...].astype(f32), far_ref[...].astype(f32))

        low = from_tiles(below, 8)
        high = from_tiles(above, 8)
        by_low = c_ref[1, 1:2, :] * (c_ref[5, 0:1, :] + c_ref[5, 1:2, :])
        by_high = c_ref[2, rows : rows + 1, :] * (
            c_ref[5, rows : rows + 1, :] + c_ref[5, rows + 1 : rows + 2, :]
        )
        has_before = jnp.where(col_group > 0, 1.0, 0.0)
        has_after = jnp.where(col_group < groups_y - 1, 1.0, 0.0)

        @pl.when(col_group == 0)
        def _():
            span = rows + 2
            e_ref[0:1, :] = low[0:1]
            e_ref[1 : rows + 1, :] = from_tiles(sum_ref[...], rows)
            e_ref[rows + 1 : span, :] = high[0:1]
            e_ref[0:span, :] = c_ref[6, 0:span, :] * e_ref[0:span, :]
            own = slice(1, rows + 1)
            heat = e_ref[own, :]
            second = c_ref[5, own, :] * heat
            first = (c_ref[0, own, :] + 1.0) * heat + second
            first = first + c_ref[1, own, :] * e_ref[0:rows, :]
            first = first + c_ref[2, own, :] * e_ref[2 : rows + 2, :]
            first = first + c_ref[3, own, :] * pltpu.roll(heat, 1, 1)
            first = first + c_ref[4, own, :] * pltpu.roll(heat, columns - 1, 1)
            heat_ref[0] = first
            heat_ref[1] = second

        for r in [1, rows - 2] + list(range(2, rows - 2)) + [0, rows - 1]:
            out_ref[r] = base_ref[r]
            for t in range(2):
                c = t * levels
                for edge, factor, lines in ((0, by_low, low), (rows - 1, by_high, high)):
                    if r == edge:
                        out_ref[r, c : c + 1, :] = out_ref[r, c : c + 1, :] + (
                            has_before * factor * lines[t + 1 : t + 2]
                        )
                        d = c + levels - 1
                        out_ref[r, d : d + 1, :] = out_ref[r, d : d + 1, :] + (
                            has_after * factor * lines[t + 3 : t + 4]
                        )

            @pl.when(col_group == 0)
            def _():
                for t, gain in enumerate((heat_gain, salt_gain)):
                    c = t * levels
                    for k in range(2):
                        out_ref[r, c + k : c + k + 1, :] = (
                            out_ref[r, c + k : c + k + 1, :] + gain * heat_ref[k, r : r + 1, :]
                        )

            copies[r].start()

    for copy in copies:
        copy.wait()


def local(
    fields,
    wet_cells,
    flux_weight,
    variable_sea_response,
    diffusivity,
    a2o_source,
    a2o_target,
    a2o_count,
    a2o_weight,
    marine_air_input_index,
    marine_air_output_index,
    marine_air_piece_tally,
    marine_air_piece_factor,
):
    _, rows, channels, columns = fields.shape
    groups_x = lax.axis_size("gx")
    groups_y = lax.axis_size("gy")
    blocks, points = a2o_source.shape[2:]
    cells = rows * columns // LANES
    forward, inverse = fourier_tables(columns)
    flux_row = flux_weight[None, :]
    gain_row = variable_sea_response[None, :]
    diff_row = diffusivity[None, :]
    paired = groups_x == 4
    params = functools.partial(pltpu.CompilerParams, vmem_limit_bytes=40 * 2**20)
    vmem = pl.BlockSpec(memory_space=pltpu.VMEM)
    smem = pl.BlockSpec(memory_space=pltpu.SMEM)
    hbm = pl.BlockSpec(memory_space=pltpu.HBM)
    anywhere = pl.BlockSpec(memory_space=pl.ANY)

    def shape(dims, dtype):
        return jax.ShapeDtypeStruct(dims, dtype)

    lines = 2 * channels + 16
    shapes = [
        shape((cells, LANES), bf16),
        shape((cells + 16, LANES), bf16),
        shape((lines, columns), bf16),
        shape((lines, columns), bf16),
        shape((4 * rows, columns), bf16),
        shape((4 * rows, columns), bf16),
    ]
    if not paired:
        shapes.append(shape((2, channels, columns), bf16))
    coarse, wide, e1, e3, e2, e4, *sums = pl.pallas_call(
        functools.partial(start_kernel, groups_x, paired),
        out_shape=shapes,
        in_specs=[hbm] * 5,
        out_specs=[hbm] * len(shapes),
        scratch_shapes=[pltpu.VMEM(out.shape, out.dtype) for out in shapes]
        + [
            pltpu.VMEM((rows, channels, columns), f32),
            pltpu.VMEM((rows, columns), jnp.int32),
            pltpu.VMEM(flux_row.shape, f32),
            pltpu.VMEM(diff_row.shape, f32),
            pltpu.VMEM(forward.shape, bf16),
            pltpu.VMEM((rows * channels, columns), bf16),
            pltpu.VMEM((rows, columns), f32),
            pltpu.VMEM((4 * rows, columns), f32),
            pltpu.VMEM((columns // 2 // LANES, 2 * rows + 1, channels, LANES), f32),
            pltpu.SemaphoreType.DMA((rows,)),
            pltpu.SemaphoreType.DMA((4,)),
            pltpu.SemaphoreType.DMA((len(shapes),)),
        ],
        compiler_params=pltpu.CompilerParams(vmem_limit_bytes=58 * 2**20),
        name="surface_and_forward_or_halos",
    )(fields, wet_cells, flux_row, diff_row, forward)

    one_hots = pl.pallas_call(
        functools.partial(one_hot_kernel, rows, columns),
        out_shape=[
            shape((LANES, blocks * points), bf16),
            shape((LANES, blocks * points), bf16),
            shape((blocks, points), jnp.int32),
            shape((blocks, points), jnp.int32),
            shape((blocks, points), jnp.int32),
        ],
        in_specs=[vmem, vmem, smem] * 2,
        out_specs=[vmem] * 5,
        compiler_params=params(),
        name="one_hots",
    )(
        a2o_source, a2o_target, a2o_count,
        marine_air_input_index, marine_air_output_index, marine_air_piece_tally,
    )

    masks = [1 << bit for bit in reversed(range(groups_y.bit_length() - 1))]

    def sum_route(mask):
        return [(j, j ^ mask) for j in range(groups_y)]

    def partner_route(mask):
        return both_ways([(j, groups_y + (j ^ mask)) for j in range(groups_y)])

    surface = lax.ppermute(coarse, ("comp", "gy"), partner_route(0)).astype(f32)
    for mask in masks[:1]:
        far = lax.ppermute(wide, ("comp", "gy"), partner_route(mask))
        surface = surface + far[:cells].astype(f32)
    coarse = surface.astype(bf16)
    *one_hots, used = one_hots
    coarse, used = lax.optimization_barrier((coarse, used))
    for mask in masks[1:-1]:
        surface = surface + lax.ppermute(coarse, "gy", sum_route(mask)).astype(f32)
        coarse = surface.astype(bf16)
    surfaces = [surface] + [
        lax.ppermute(coarse, "gy", sum_route(mask)) for mask in masks[1:][-1:]
    ]

    def ring_pairs(count, odd):
        return [(a, (a + 1) % count) for a in range(odd, count, 2)]

    def flat(comp, i, j):
        return (comp * groups_x + i) * groups_y + j

    def level_route(odd):
        pairs = []
        for i in range(groups_x):
            linked = [(a, a + 1) for a in range(odd, groups_y - 1, 2)]
            alone = set(range(groups_y)) - {j for pair in linked for j in pair}
            pairs += [(flat(1, i, a), flat(1, i, b)) for a, b in linked]
            if i % 2 == 0:
                pairs += [(flat(1, i, j), flat(1, i + 1, j)) for j in sorted(alone)]
                if odd or not paired:
                    pairs += [(flat(0, i, j), flat(0, i + 1, j)) for j in range(groups_y)]
            if paired and not odd and i < i ^ 2:
                pairs += [(flat(0, i, j), flat(0, i ^ 2, j)) for j in range(groups_y)]
        return both_ways(pairs)

    e1 = lax.ppermute(e1, "gx", both_ways(ring_pairs(groups_x, 0)))
    e3 = lax.ppermute(e3, "gx", both_ways(ring_pairs(groups_x, 1)))
    axes = ("comp", "gx", "gy")
    e2 = lax.ppermute(e2, axes, level_route(0))
    e4 = lax.ppermute(e4, axes, level_route(1))

    landing_order = sorted(range(1, groups_y), key=lambda mask: (mask % 2, -mask))
    landing, *sent = pl.pallas_call(
        functools.partial(regrid_kernel, len(surfaces)),
        out_shape=[shape((cells, LANES), f32)]
        + [
            shape((cells + 16 * (groups_y - 2 - landing_order.index(mask)), LANES), bf16)
            for mask in range(1, groups_y)
        ],
        in_specs=[vmem] * (len(surfaces) + 5) + [hbm, hbm] + [anywhere] * 1,
        out_specs=[vmem] * groups_y,
        scratch_shapes=[
            pltpu.VMEM((blocks, points, points), bf16),
            pltpu.VMEM((blocks, points), f32),
            pltpu.VMEM((blocks, points), f32),
            pltpu.SemaphoreType.DMA,
        ],
        compiler_params=params(),
        cost_estimate=pl.CostEstimate(flops=2_200_000_000, bytes_accessed=0, transcendentals=0),
        name="regrid_blocks",
    )(
        *surfaces, *one_hots, used, a2o_weight, marine_air_piece_factor, e3,
    )

    def landing_route(mask):
        pairs = [
            (flat(0, i, j), flat(0, i, j ^ mask))
            for i in range(groups_x)
            for j in range(groups_y)
            if j < j ^ mask
        ]
        pairs += [(flat(1, i, 0), flat(1, i, mask)) for i in range(groups_x)]
        pairs += [
            (flat(1, i, j), flat(1, i + 1, j))
            for i in range(0, groups_x, 2)
            for j in range(groups_y)
            if j not in (0, mask)
        ]
        return both_ways(pairs)

    parts = [
        lax.ppermute(block, axes, landing_route(mask)) for mask, block in enumerate(sent, 1)
    ]

    extra = []
    if not paired:
        p, q = jnp.moveaxis(lax.all_gather(sums[0], "gx").astype(f32), 1, 0)
        viscous = lax.dynamic_slice_in_dim(
            diffusivity, lax.axis_index("gy") * channels, channels
        )[:, None]
        rates = [half_rates(g, 0, columns // 4, columns) for g in (0, 0, 1, 1)]
        _, alpha, _ = decay_terms(viscous, jnp.concatenate(rates, axis=1))
        gap = lax.axis_index("gx") - jnp.arange(groups_x)
        decay = jnp.exp(
            -(rows * jnp.maximum(jnp.abs(gap) - 1, 0))[:, None, None] * alpha[None]
        )
        extra = [
            jnp.sum(jnp.where((gap > 0)[:, None, None], decay * p, 0.0), axis=0),
            jnp.sum(jnp.where((gap < 0)[:, None, None], decay * q, 0.0), axis=0),
        ]
    ring = channels // 2 + 8
    damped, coefs, stepped = pl.pallas_call(
        functools.partial(first_step_kernel, groups_x, groups_y, paired),
        out_shape=[
            shape((rows * channels, columns), bf16),
            shape((7, 16, columns), f32),
            shape((rows + 2, 2, ring, columns), f32),
        ],
        in_specs=[vmem] * (8 + len(extra)),
        out_specs=[vmem] * 3,
        scratch_shapes=[
            pltpu.VMEM((rows, channels, columns), f32),
            pltpu.VMEM((rows * channels, columns), bf16),
            pltpu.VMEM((rows, channels, LANES), f32),
            pltpu.VMEM((rows + 4, 2, ring, columns), f32),
            pltpu.VMEM((16, columns), f32),
        ],
        compiler_params=params(),
        name="damping_or_first_step",
    )(fields, wet_cells, diff_row, forward, e1, e3, e2, e4, *extra)

    surface_sum, near, far = pl.pallas_call(
        functools.partial(heat_kernel, rows),
        out_shape=[
            shape((cells, LANES), f32),
            shape((columns // 16, LANES), bf16),
            shape((columns // 16, LANES), bf16),
        ],
        in_specs=[vmem] * 3 + [anywhere] + [vmem] * len(parts),
        out_specs=[vmem] * 3,
        compiler_params=params(),
        name="surface_sum",
    )(e2, e4, landing, coefs, *parts)

    near = lax.ppermute(near, "gx", both_ways(ring_pairs(groups_x, 0)))
    far = lax.ppermute(far, "gx", both_ways(ring_pairs(groups_x, 1)))
    base, column = pl.pallas_call(
        second_step_kernel,
        out_shape=[shape((rows, channels, columns), f32), shape((channels, LANES), f32)],
        in_specs=[vmem] * 5,
        out_specs=[vmem] * 2,
        compiler_params=params(),
        name="inverse_or_second_step",
    )(gain_row, inverse, damped, coefs, stepped)
    return pl.pallas_call(
        functools.partial(last_kernel, groups_x, groups_y),
        out_shape=shape(fields.shape, f32),
        in_specs=[vmem] * 6,
        out_specs=hbm,
        scratch_shapes=[
            pltpu.VMEM((rows, channels, columns), f32),
            pltpu.VMEM((16, columns), f32),
            pltpu.VMEM((2, rows, columns), f32),
            pltpu.SemaphoreType.DMA((rows,)),
        ],
        compiler_params=params(),
        name="add_surface_terms",
    )(column, base, coefs, surface_sum, near, far)


def solution(mesh):
    in_specs = (
        P("comp", "gx", "gy", None),
        P("gx", None),
        P(),
        P(),
        P(),
        P("gx", "gy", None, None),
        P("gx", "gy", None, None),
        P("gx", "gy"),
        P("gx", "gy", None, None, None),
        P("gx", "gy", None, None),
        P("gx", "gy", None, None),
        P("gx", "gy"),
        P("gx", "gy", None, None, None),
    )
    out_specs = P("comp", "gx", "gy", None)
    return jax.shard_map(local, mesh=mesh, in_specs=in_specs, out_specs=out_specs, check_vma=False)
```

```python
import functools

import jax
import jax.numpy as jnp
import numpy as np
from jax import lax
from jax.experimental import pallas as pl
from jax.experimental.pallas import tpu as pltpu
from jax.sharding import PartitionSpec as P

spread_rate = 0.2
mixing_rate = 0.1
heat_gain = 0.5
salt_gain = -0.25
LANES = 128
f32 = jnp.float32
bf16 = jnp.bfloat16


def fourier_tables(columns):
    half = columns // 2
    forward, inverse = [], []
    for first in (0, 1):
        waves = np.arange(first, half, 2)
        phase = np.arange(half)[:, None] * waves[None, :] % columns
        angles = phase * (2.0 * np.pi / columns)
        table = np.concatenate([np.cos(angles), np.sin(angles)], axis=1)
        weight = np.where(waves == 0, 1.0, 2.0) / columns
        forward.append(table)
        inverse.append(table.T * np.concatenate([weight, weight])[:, None])
    return (
        jnp.asarray(np.concatenate(forward).astype(np.float32), bf16),
        jnp.asarray(np.concatenate(inverse).astype(np.float32), bf16),
    )


def wave_parts(columns):
    quarter = columns // 4
    return [
        (g, n, (g * 2 * quarter + n, (g * 2 + 1) * quarter + n))
        for g in (0, 1)
        for n in range(0, quarter, LANES)
    ]


def half_rates(group, first, count, columns):
    lane = lax.broadcasted_iota(jnp.int32, (1, count), 1) + first
    wave = (2 * lane + group).astype(f32)
    sine = jnp.sin(wave * (np.pi / columns))
    return 2.0 * sine * sine


def both_ways(pairs):
    return [p for a, b in pairs for p in ((a, b), (b, a))]


def channel_column(row, channels, first):
    n = row.shape[1]
    lane = lax.broadcasted_iota(jnp.int32, (channels, n), 1)
    sub = lax.broadcasted_iota(jnp.int32, (channels, n), 0)
    return jnp.sum(jnp.where(lane == sub + first, row, 0.0), axis=1, keepdims=True)


def to_tiles(surface):
    cols = surface.shape[1]
    return jnp.concatenate(
        [surface[:, k : k + LANES] for k in range(0, cols, LANES)], axis=0
    )


def from_tiles(tiles, rows):
    return jnp.concatenate(
        [tiles[k : k + rows] for k in range(0, tiles.shape[0], rows)], axis=1
    )


def lengthen(ref, block):
    rows = block.shape[0]
    ref[0:rows, :] = block
    if ref.shape[0] > rows:
        ref[rows:, :] = block[: ref.shape[0] - rows]


def decay_terms(diff_column, rates):
    half = 0.5 / diff_column + rates
    sinh = jnp.sqrt(half * (half + 2.0))
    grow = 1.0 + half + sinh
    return 1.0 / grow, jnp.log(grow), sinh


def edge_factors(lam, alpha, base, total, rows):
    lam2 = lam * lam
    powers = [
        jnp.exp(-2.0 * base * alpha) * lam2,
        jnp.exp(-2.0 * (total - rows - base) * alpha) * lam2,
    ]
    lows, highs = [], []
    for _ in range(rows):
        lows.append(1.0 - powers[0])
        highs.insert(0, 1.0 - powers[1])
        powers = [power * lam2 for power in powers]
    return lows, highs


def fold(values, flat_ref, r):
    channels, columns = values.shape
    half = columns // 2
    left, right = values[:, :half], values[:, half:]
    flat_ref[r * channels : (r + 1) * channels, :half] = (left + right).astype(bf16)
    flat_ref[r * channels : (r + 1) * channels, half:] = (left - right).astype(bf16)


def start_kernel(
    groups_x, paired, x_hbm, wet_hbm, flux_hbm, diff_hbm, table_hbm, *refs
):
    outs = 6 if paired else 7
    coarse_hbm, wide_hbm, *message_hbm = refs[:outs]
    coarse_ref, wide_ref, *message_ref = refs[outs : 2 * outs]
    e1_ref, e3_ref, e2_ref, e4_ref = message_ref[:4]
    if not paired:
        pq_ref = message_ref[4]
    (
        x_ref, wet_ref, flux_ref, diff_ref, table_ref, flat_ref, row_ref, edge_ref,
        factor_ref, x_sem, sem, out_sem,
    ) = refs[2 * outs :]
    rows, channels, columns = x_ref.shape
    half = columns // 2
    row_group = lax.axis_index("gx")
    col_group = lax.axis_index("gy")
    is_atmos = lax.axis_index("comp") == 0

    x_copies = [
        pltpu.make_async_copy(x_hbm.at[0, r], x_ref.at[r], x_sem.at[r]) for r in range(rows)
    ]
    surface_copies = [
        pltpu.make_async_copy(coarse_ref, coarse_hbm, out_sem.at[0]),
        pltpu.make_async_copy(wide_ref, wide_hbm, out_sem.at[1]),
    ]
    message_copies = [
        pltpu.make_async_copy(ref, hbm, out_sem.at[2 + k])
        for k, (ref, hbm) in enumerate(zip(message_ref, message_hbm))
    ]

    def send_surface():
        coarse = to_tiles(row_ref[...]).astype(bf16)
        coarse_ref[...] = coarse
        lengthen(wide_ref, coarse)
        for copy in surface_copies:
            copy.start()

    @pl.when(is_atmos)
    def _():
        flux_copy = pltpu.make_async_copy(flux_hbm, flux_ref, sem.at[0])
        diff_copy = pltpu.make_async_copy(diff_hbm, diff_ref, sem.at[1])
        table_copies = [
            pltpu.make_async_copy(
                table_hbm.at[pl.ds(k * half, half)], table_ref.at[pl.ds(k * half, half)], sem.at[2 + k]
            )
            for k in range(2)
        ]
        for copy in [flux_copy, diff_copy] + x_copies + table_copies:
            copy.start()
        first = col_group * channels
        flux_copy.wait()
        weight = channel_column(flux_ref[...], channels, first)
        diff_copy.wait()
        diff = channel_column(diff_ref[...], channels, first)
        total = rows * groups_x
        base = (row_group * rows).astype(f32)
        tiles = wave_parts(columns)
        for k, (group, n, _) in enumerate(tiles):
            lam, alpha, _ = decay_terms(diff, half_rates(group, n, LANES, columns))
            factor_ref[k, 0] = lam
            lows, highs = edge_factors(lam, alpha, base, total, rows)
            for r in range(rows):
                factor_ref[k, 1 + r] = lows[r]
                factor_ref[k, 1 + rows + r] = highs[r]
        for r in range(rows):
            x_copies[r].wait()
            row_ref[r : r + 1, :] = jnp.sum(x_ref[r] * weight, axis=0, keepdims=True)
            fold(x_ref[r], flat_ref, r)
        send_surface()
        for k in range(2):
            table_copies[k].wait()
            lanes = slice(k * half, (k + 1) * half)
            part = jnp.dot(
                flat_ref[:, lanes], table_ref[lanes, :], preferred_element_type=f32
            )
            for tile, (group, _, parts) in enumerate(tiles):
                if group != k:
                    continue
                lam = factor_ref[tile, 0]
                for at in parts:
                    lanes = slice(at, at + LANES)
                    here = slice(at - k * half, at - k * half + LANES)
                    p = factor_ref[tile, 1] * part[0:channels, here]
                    q = factor_ref[tile, 2 * rows] * part[(rows - 1) * channels :, here]
                    for r in range(1, rows):
                        up = part[r * channels : (r + 1) * channels, here]
                        down = part[(rows - 1 - r) * channels : (rows - r) * channels, here]
                        p = lam * p + factor_ref[tile, 1 + r] * up
                        q = lam * q + factor_ref[tile, 2 * rows - r] * down
                    if paired:
                        for mask, out in ((1, e1_ref), (2, e2_ref), (3, e3_ref)):
                            upward = row_group < (row_group ^ mask)
                            out[0:channels, lanes] = jnp.where(upward, p, q).astype(bf16)
                    else:
                        pq_ref[0, :, lanes] = p.astype(bf16)
                        pq_ref[1, :, lanes] = q.astype(bf16)
        sums_copies = [
            pltpu.make_async_copy(
                message_ref[k].at[pl.ds(0, channels)],
                message_hbm[k].at[pl.ds(0, channels)],
                out_sem.at[2 + k],
            )
            for k in range(3)
        ]
        if not paired:
            sums_copies = message_copies[4:]
        for copy in sums_copies:
            copy.start()
        for copy in surface_copies + sums_copies:
            copy.wait()

    @pl.when(jnp.logical_not(is_atmos))
    def _():
        wet_copy = pltpu.make_async_copy(wet_hbm, wet_ref, sem.at[0])
        for copy in x_copies + [wet_copy]:
            copy.start()
        gain = jnp.where(col_group == 0, 1.0, 0.0)
        for r in range(rows):
            x_copies[r].wait()
            row_ref[r : r + 1, :] = x_ref[r, 0:1, :] * gain
        send_surface()
        wet_copy.wait()
        levels = channels // 2
        lines = 2 * channels
        even_x = row_group % 2 == 0
        even_y = col_group % 2 == 0
        wet = wet_ref[...].astype(f32)
        wet = jnp.concatenate([wet, wet], axis=0).astype(bf16)

        def put(out, last):
            @pl.when(last)
            def _():
                out[0:lines, :] = x_ref[rows - 2 :].reshape(lines, columns).astype(bf16)

            @pl.when(jnp.logical_not(last))
            def _():
                out[0:lines, :] = x_ref[:2].reshape(lines, columns).astype(bf16)

            out[lines : lines + 16, :] = wet

        put(e1_ref, even_x)
        put(e3_ref, jnp.logical_not(even_x))

        def put_edges(out, level):
            for r in range(rows):
                for t in range(2):
                    at = (r * 2 + t) * 2
                    c = t * levels + level
                    edge_ref[at : at + 2, :] = x_ref[r, c : c + 2, :]
            out[0 : rows * 4, :] = edge_ref[...].astype(bf16)

        @pl.when(even_y)
        def _():
            put_edges(e2_ref, levels - 2)
            put_edges(e4_ref, 0)

        @pl.when(jnp.logical_not(even_y))
        def _():
            put_edges(e2_ref, 0)
            put_edges(e4_ref, levels - 2)

        for copy in message_copies:
            copy.start()
        for copy in surface_copies + message_copies:
            copy.wait()


def one_hot_kernel(
    rows, columns, a_src, a_dst, a_count, m_src, m_dst, m_count, src_hot_ref, dst_hot_ref,
    src_row_ref, dst_row_ref, used_ref,
):
    is_atmos = lax.axis_index("comp") == 0
    blocks, points = src_row_ref.shape
    count = jnp.where(is_atmos, m_count[0, 0], a_count[0, 0])
    block_iota = lax.broadcasted_iota(jnp.int32, (blocks, points), 0)
    used_ref[...] = jnp.where(block_iota < count, 1, 0)
    lane_iota = lax.broadcasted_iota(jnp.int32, (LANES, points), 0)
    for a_ref, m_ref, hot_ref, row_ref in (
        (a_src, m_src, src_hot_ref, src_row_ref),
        (a_dst, m_dst, dst_hot_ref, dst_row_ref),
    ):
        index = jnp.where(is_atmos, m_ref[0, 0], a_ref[0, 0])
        row = index // columns
        tile = (index // LANES) % (columns // LANES)
        row_ref[...] = tile * rows + row
        lane = index % LANES
        for b in range(blocks):
            hot_ref[:, b * points : (b + 1) * points] = jnp.where(
                lane_iota == lane[b : b + 1], 1.0, 0.0
            ).astype(bf16)


def regrid_kernel(n_surfaces, *refs):
    surfaces = refs[:n_surfaces]
    (
        src_hot_ref, dst_hot_ref, src_row_ref, dst_row_ref, used_ref, a_weight, m_weight,
        _,
        *refs,
    ) = refs[n_surfaces:]
    land_ref, *sent_refs = refs[:-4]
    weight_ref, gath_ref, val_ref, sem = refs[-4:]
    is_atmos = lax.axis_index("comp") == 0
    blocks, points = val_ref.shape
    cells = surfaces[0].shape[0]

    @pl.when(is_atmos)
    def _():
        pltpu.make_async_copy(m_weight.at[0, 0], weight_ref, sem).start()

    @pl.when(jnp.logical_not(is_atmos))
    def _():
        pltpu.make_async_copy(a_weight.at[0, 0], weight_ref, sem).start()

    pair = 2 * points
    row_iota = lax.broadcasted_iota(jnp.int32, (cells, points), 0)
    table = sum(surface[...].astype(f32) for surface in surfaces).astype(bf16)
    for b in range(0, blocks, 2):
        picked = jnp.dot(
            table, src_hot_ref[:, b * points : b * points + pair], preferred_element_type=f32
        )
        for k in range(2):
            mine = row_iota == src_row_ref[b + k : b + k + 1, :]
            part = jnp.where(mine, picked[:, k * points : (k + 1) * points], 0.0)
            gath_ref[b + k : b + k + 1, :] = jnp.sum(part, axis=0, keepdims=True)
    gathered = gath_ref[...].astype(bf16)

    @pl.when(is_atmos)
    def _():
        pltpu.make_async_copy(m_weight.at[0, 0], weight_ref, sem).wait()

    @pl.when(jnp.logical_not(is_atmos))
    def _():
        pltpu.make_async_copy(a_weight.at[0, 0], weight_ref, sem).wait()

    block_iota = lax.broadcasted_iota(jnp.int32, (blocks, points), 0)
    values = jnp.zeros((blocks, points), f32)
    for b in range(0, blocks, 2):
        terms = lax.dot_general(
            gathered,
            weight_ref[b : b + 2].reshape(pair, points),
            (((1,), (1,)), ((), ())),
            preferred_element_type=f32,
        )
        for k in range(2):
            values = jnp.where(block_iota == b + k, terms[:, k * points : (k + 1) * points], values)
    val_ref[...] = jnp.where(used_ref[...] > 0, values, 0.0)
    land = jnp.zeros((2 * cells, LANES), f32)
    for b in range(0, blocks, 2):
        spread = []
        for k in range(b, b + 2):
            value = val_ref[k : k + 1, :]
            coarse = value.astype(bf16).astype(f32)
            fine = value - coarse
            mine = row_iota == dst_row_ref[k : k + 1, :]
            spread.append(
                jnp.concatenate(
                    [jnp.where(mine, coarse, 0.0), jnp.where(mine, fine, 0.0)], axis=0
                ).astype(bf16)
            )
        land = land + lax.dot_general(
            jnp.concatenate(spread, axis=1),
            dst_hot_ref[:, b * points : b * points + pair],
            (((1,), (1,)), ((), ())),
            preferred_element_type=f32,
        )
    land = land[:cells] + land[cells:]
    land_ref[...] = land
    for sent_ref in sent_refs:
        lengthen(sent_ref, land.astype(bf16))


def heat_kernel(rows, e2_ref, e4_ref, land_ref, _, *refs):
    parts = refs[:-3]
    sum_ref, near_ref, far_ref = refs[-3:]
    cells = land_ref.shape[0]
    columns = cells // rows * LANES
    even_x = lax.axis_index("gx") % 2 == 0
    even_y = lax.axis_index("gy") % 2 == 0
    total = land_ref[...]
    for part in parts:
        total = total + part[0:cells, :].astype(f32)
    sum_ref[...] = total

    def corners(row):
        start = row * 4 // 16 * 16
        one = e2_ref[start : start + 16, :].astype(f32)
        two = e4_ref[start : start + 16, :].astype(f32)
        low = jnp.where(even_y, two, one)
        high = jnp.where(even_y, one, two)
        at = row * 4 - start
        lines = [low[at + 1 : at + 2], low[at + 3 : at + 4], high[at : at + 1], high[at + 2 : at + 3]]
        heat = from_tiles(total, rows)[row : row + 1]
        blank = jnp.zeros((3, columns), f32)
        return to_tiles(jnp.concatenate([heat] + lines + [blank], axis=0))

    first, last = corners(0), corners(rows - 1)
    near_ref[...] = jnp.where(even_x, last, first).astype(bf16)
    far_ref[...] = jnp.where(even_x, first, last).astype(bf16)


def advance(ref, r, t, coefs, size):
    ring, columns = ref.shape[2:]
    whole = ref[r, t]
    up = pltpu.roll(whole, 1, 0)[:size]
    down = pltpu.roll(whole, ring - 1, 0)[:size]
    mid = whole[:size]
    total = coefs[0] * mid + coefs[5] * (up + down)
    total = total + coefs[1] * ref[r - 1, t, 0:size, :]
    total = total + coefs[2] * ref[r + 1, t, 0:size, :]
    total = total + coefs[3] * pltpu.roll(mid, 1, 1)
    return total + coefs[4] * pltpu.roll(mid, columns - 1, 1)


def first_step_kernel(
    groups_x, groups_y, paired, x_ref, wet_ref, diff_ref, table_ref, e1_ref, e3_ref,
    e2_ref, e4_ref, *refs,
):
    if not paired:
        pin_ref, qin_ref = refs[:2]
    zb_ref, c_ref, t1_ref, y_ref, flat_ref, z_ref, t0_ref, w_ref = refs[-8:]
    _, rows, channels, columns = x_ref.shape
    row_group = lax.axis_index("gx")
    col_group = lax.axis_index("gy")
    is_atmos = lax.axis_index("comp") == 0

    @pl.when(is_atmos)
    def _():
        half = columns // 2
        for r in range(rows):
            fold(x_ref[0, r], flat_ref, r)
        for k in range(2):
            lanes = slice(k * half, (k + 1) * half)
            part = jnp.dot(
                flat_ref[:, lanes], table_ref[lanes, :], preferred_element_type=f32
            )
            y_ref[:, :, lanes] = part.reshape(rows, channels, half)
        diff = channel_column(diff_ref[...], channels, col_group * channels)
        total = rows * groups_x
        base = (row_group * rows).astype(f32)
        for group, n, parts in wave_parts(columns):
            lam, alpha, sinh = decay_terms(diff, half_rates(group, n, LANES, columns))
            scale = 1.0 / (
                2.0 * diff * sinh * (1.0 - jnp.exp(-2.0 * (total + 1) * alpha))
            )
            lows, highs = edge_factors(lam, alpha, base, total, rows)
            for part in parts:
                lanes = slice(part, part + LANES)
                if paired:
                    pin = jnp.zeros((channels, LANES), f32)
                    qin = jnp.zeros((channels, LANES), f32)
                    for mask, msg in ((1, e1_ref), (2, e2_ref), (3, e3_ref)):
                        band = row_group ^ mask
                        gap = (jnp.abs(row_group - band) - 1) * rows
                        term = jnp.exp(-gap.astype(f32) * alpha)
                        term = term * msg[0:channels, lanes].astype(f32)
                        pin = pin + jnp.where(band < row_group, term, 0.0)
                        qin = qin + jnp.where(band > row_group, term, 0.0)
                else:
                    pin = pin_ref[:, lanes]
                    qin = qin_ref[:, lanes]
                f = pin
                for r in range(rows):
                    f = lam * f + lows[r] * y_ref[r, :, lanes]
                    z_ref[r] = highs[r] * f
                g = lam * qin
                for r in reversed(range(rows)):
                    z = scale * (z_ref[r] + lows[r] * g)
                    zb_ref[r * channels : (r + 1) * channels, lanes] = z.astype(bf16)
                    g = lam * (g + highs[r] * y_ref[r, :, lanes])

    @pl.when(jnp.logical_not(is_atmos))
    def _():
        levels = channels // 2
        ring = levels + 8
        lines = 2 * channels
        first_x = row_group == 0
        last_x = row_group == groups_x - 1
        top = col_group == 0
        bottom = col_group == groups_y - 1
        even_x = row_group % 2 == 0
        even_y = col_group % 2 == 0

        one = e1_ref[lines : lines + 16, :].astype(f32)
        three = e3_ref[lines : lines + 16, :].astype(f32)
        below = jnp.where(even_x, three, one)[rows - 2 : rows]
        above = jnp.where(even_x, one, three)[0:2]
        w_ref[0:2, :] = jnp.where(first_x, 0.0, below)
        w_ref[2 : rows + 2, :] = wet_ref[...].astype(f32)
        w_ref[rows + 2 : rows + 4, :] = jnp.where(last_x, 0.0, above)

        span = rows + 2
        north = w_ref[0:span, :]
        here = w_ref[1 : span + 1, :]
        south = w_ref[2 : span + 2, :]
        west = pltpu.roll(here, 1, 1)
        east = pltpu.roll(here, columns - 1, 1)
        c_ref[0, 0:span, :] = here * (
            1.0 - 2.0 * mixing_rate - spread_rate * (north + south + west + east)
        )
        c_ref[1, 0:span, :] = spread_rate * here * north
        c_ref[2, 0:span, :] = spread_rate * here * south
        c_ref[3, 0:span, :] = spread_rate * here * west
        c_ref[4, 0:span, :] = spread_rate * here * east
        c_ref[5, 0:span, :] = mixing_rate * here
        c_ref[6, 0:span, :] = here

        one = e1_ref[0:lines, :].astype(f32)
        three = e3_ref[0:lines, :].astype(f32)
        below = jnp.where(even_x, three, one)
        above = jnp.where(even_x, one, three)
        blank = jnp.zeros((8, columns), f32)
        for k in range(2):
            for t in range(2):
                c = k * channels + t * levels
                t0_ref[k, t, 0:levels, :] = below[c : c + levels]
                t0_ref[rows + 2 + k, t, 0:levels, :] = above[c : c + levels]
                t0_ref[k, t, levels:ring, :] = blank
                t0_ref[rows + 2 + k, t, levels:ring, :] = blank
        one = e2_ref[...].astype(f32)
        two = e4_ref[0 : 4 * rows, :].astype(f32)
        before = jnp.where(even_y, two, one)
        after = jnp.where(even_y, one, two)
        for r in range(rows):
            for t in range(2):
                k = (r * 2 + t) * 2
                t0_ref[r + 2, t, 0:levels, :] = x_ref[0, r, t * levels : (t + 1) * levels, :]
                t0_ref[r + 2, t, levels : levels + 2, :] = after[k : k + 2]
                t0_ref[r + 2, t, ring - 2 : ring, :] = before[k : k + 2]

        def close(ref, r):
            for t in range(2):
                ref[r, t, ring - 1 : ring, :] = jnp.where(
                    top, ref[r, t, 0:1, :], ref[r, t, ring - 1 : ring, :]
                )
                ref[r, t, levels : levels + 1, :] = jnp.where(
                    bottom, ref[r, t, levels - 1 : levels, :], ref[r, t, levels : levels + 1, :]
                )

        def first(r, carry):
            coefs = [c_ref[k, pl.ds(r, 1), :] for k in range(6)]
            close(t0_ref, r + 1)
            for t in range(2):
                t1_ref[r, t] = advance(t0_ref, r + 1, t, coefs, ring)
            close(t1_ref, r)
            return carry

        lax.fori_loop(0, span, first, 0)


def second_step_kernel(gain_ref, table_ref, zb_ref, c_ref, t1_ref, sum_ref, base_ref):
    rows, channels, columns = base_ref.shape
    is_atmos = lax.axis_index("comp") == 0

    @pl.when(is_atmos)
    def _():
        response = channel_column(gain_ref[...], channels, lax.axis_index("gy") * channels)
        forcing = from_tiles(sum_ref[...], rows)
        half = columns // 2
        step = 256
        for n in range(0, half, step):
            even, odd = [
                jnp.dot(
                    zb_ref[:, k * half : (k + 1) * half],
                    table_ref[k * half : (k + 1) * half, n : n + step],
                    preferred_element_type=f32,
                ).reshape(rows, channels, step)
                for k in range(2)
            ]
            for r in range(rows):
                for lane, part in ((n, even[r] + odd[r]), (n + half, even[r] - odd[r])):
                    lanes = slice(lane, lane + step)
                    base_ref[r, :, lanes] = part + response * forcing[r : r + 1, lanes]

    @pl.when(jnp.logical_not(is_atmos))
    def _():
        levels = channels // 2

        def second(r, carry):
            coefs = [c_ref[k, pl.ds(r, 1), :] for k in range(6)]
            for t in range(2):
                c = t * levels
                base_ref[r - 1, c : c + levels, :] = advance(t1_ref, r, t, coefs, levels)
            return carry

        lax.fori_loop(1, rows + 1, second, 0)


def last_kernel(
    groups_x, groups_y, base_ref, c_ref, sum_ref, near_ref, far_ref, out_hbm,
    out_ref, e_ref, heat_ref, sem,
):
    rows, channels, columns = out_ref.shape
    row_group = lax.axis_index("gx")
    col_group = lax.axis_index("gy")
    is_atmos = lax.axis_index("comp") == 0
    copies = [
        pltpu.make_async_copy(out_ref.at[r], out_hbm.at[0, r], sem.at[r]) for r in range(rows)
    ]
    as_they_are = [
        pltpu.make_async_copy(base_ref.at[r], out_hbm.at[0, r], sem.at[r]) for r in range(rows)
    ]

    @pl.when(is_atmos)
    def _():
        for copy in as_they_are:
            copy.start()

    @pl.when(jnp.logical_and(jnp.logical_not(is_atmos), col_group > 0))
    def _():
        for copy in as_they_are[1:-1]:
            copy.start()

    @pl.when(jnp.logical_not(is_atmos))
    def _():
        levels = channels // 2
        even = row_group % 2 == 0
        below = jnp.where(even, far_ref[...].astype(f32), near_ref[...].astype(f32))
        above = jnp.where(even, near_ref[...].astype(f32), far_ref[...].astype(f32))

        low = from_tiles(below, 8)
        high = from_tiles(above, 8)
        by_low = c_ref[1, 1:2, :] * (c_ref[5, 0:1, :] + c_ref[5, 1:2, :])
        by_high = c_ref[2, rows : rows + 1, :] * (
            c_ref[5, rows : rows + 1, :] + c_ref[5, rows + 1 : rows + 2, :]
        )
        has_before = jnp.where(col_group > 0, 1.0, 0.0)
        has_after = jnp.where(col_group < groups_y - 1, 1.0, 0.0)

        @pl.when(col_group == 0)
        def _():
            span = rows + 2
            e_ref[0:1, :] = low[0:1]
            e_ref[1 : rows + 1, :] = from_tiles(sum_ref[...], rows)
            e_ref[rows + 1 : span, :] = high[0:1]
            e_ref[0:span, :] = c_ref[6, 0:span, :] * e_ref[0:span, :]
            own = slice(1, rows + 1)
            heat = e_ref[own, :]
            second = c_ref[5, own, :] * heat
            first = (c_ref[0, own, :] + 1.0) * heat + second
            first = first + c_ref[1, own, :] * e_ref[0:rows, :]
            first = first + c_ref[2, own, :] * e_ref[2 : rows + 2, :]
            first = first + c_ref[3, own, :] * pltpu.roll(heat, 1, 1)
            first = first + c_ref[4, own, :] * pltpu.roll(heat, columns - 1, 1)
            heat_ref[0] = first
            heat_ref[1] = second

        for r in (0, rows - 1):
            out_ref[r] = base_ref[r]
        for t in range(2):
            c = t * levels
            d = c + levels - 1
            for r, factor, lines in ((0, by_low, low), (rows - 1, by_high, high)):
                out_ref[r, c : c + 1, :] = out_ref[r, c : c + 1, :] + (
                    has_before * factor * lines[t + 1 : t + 2]
                )
                out_ref[r, d : d + 1, :] = out_ref[r, d : d + 1, :] + (
                    has_after * factor * lines[t + 3 : t + 4]
                )

        @pl.when(col_group == 0)
        def _():
            for r in range(rows):
                if r not in (0, rows - 1):
                    out_ref[r] = base_ref[r]
                for t, gain in enumerate((heat_gain, salt_gain)):
                    c = t * levels
                    for k in range(2):
                        out_ref[r, c + k : c + k + 1, :] = (
                            out_ref[r, c + k : c + k + 1, :] + gain * heat_ref[k, r : r + 1, :]
                        )
                copies[r].start()

        @pl.when(col_group > 0)
        def _():
            copies[0].start()
            copies[-1].start()

    for copy in copies:
        copy.wait()


def local(
    fields,
    wet_cells,
    flux_weight,
    variable_sea_response,
    diffusivity,
    a2o_source,
    a2o_target,
    a2o_count,
    a2o_weight,
    marine_air_input_index,
    marine_air_output_index,
    marine_air_piece_tally,
    marine_air_piece_factor,
):
    _, rows, channels, columns = fields.shape
    groups_x = lax.axis_size("gx")
    groups_y = lax.axis_size("gy")
    blocks, points = a2o_source.shape[2:]
    cells = rows * columns // LANES
    forward, inverse = fourier_tables(columns)
    flux_row = flux_weight[None, :]
    gain_row = variable_sea_response[None, :]
    diff_row = diffusivity[None, :]
    paired = groups_x == 4
    params = functools.partial(pltpu.CompilerParams, vmem_limit_bytes=40 * 2**20)
    vmem = pl.BlockSpec(memory_space=pltpu.VMEM)
    smem = pl.BlockSpec(memory_space=pltpu.SMEM)
    hbm = pl.BlockSpec(memory_space=pltpu.HBM)
    anywhere = pl.BlockSpec(memory_space=pl.ANY)

    def shape(dims, dtype):
        return jax.ShapeDtypeStruct(dims, dtype)

    lines = 2 * channels + 16
    shapes = [
        shape((cells, LANES), bf16),
        shape((cells + 16, LANES), bf16),
        shape((lines, columns), bf16),
        shape((lines, columns), bf16),
        shape((4 * rows, columns), bf16),
        shape((4 * rows, columns), bf16),
    ]
    if not paired:
        shapes.append(shape((2, channels, columns), bf16))
    coarse, wide, e1, e3, e2, e4, *sums = pl.pallas_call(
        functools.partial(start_kernel, groups_x, paired),
        out_shape=shapes,
        in_specs=[hbm] * 5,
        out_specs=[hbm] * len(shapes),
        scratch_shapes=[pltpu.VMEM(out.shape, out.dtype) for out in shapes]
        + [
            pltpu.VMEM((rows, channels, columns), f32),
            pltpu.VMEM((rows, columns), jnp.int32),
            pltpu.VMEM(flux_row.shape, f32),
            pltpu.VMEM(diff_row.shape, f32),
            pltpu.VMEM(forward.shape, bf16),
            pltpu.VMEM((rows * channels, columns), bf16),
            pltpu.VMEM((rows, columns), f32),
            pltpu.VMEM((4 * rows, columns), f32),
            pltpu.VMEM((columns // 2 // LANES, 2 * rows + 1, channels, LANES), f32),
            pltpu.SemaphoreType.DMA((rows,)),
            pltpu.SemaphoreType.DMA((4,)),
            pltpu.SemaphoreType.DMA((len(shapes),)),
        ],
        compiler_params=pltpu.CompilerParams(vmem_limit_bytes=58 * 2**20),
        name="surface_and_forward_or_halos",
    )(fields, wet_cells, flux_row, diff_row, forward)

    one_hots = pl.pallas_call(
        functools.partial(one_hot_kernel, rows, columns),
        out_shape=[
            shape((LANES, blocks * points), bf16),
            shape((LANES, blocks * points), bf16),
            shape((blocks, points), jnp.int32),
            shape((blocks, points), jnp.int32),
            shape((blocks, points), jnp.int32),
        ],
        in_specs=[vmem, vmem, smem] * 2,
        out_specs=[vmem] * 5,
        compiler_params=params(),
        name="one_hots",
    )(
        a2o_source, a2o_target, a2o_count,
        marine_air_input_index, marine_air_output_index, marine_air_piece_tally,
    )

    masks = [1 << bit for bit in reversed(range(groups_y.bit_length() - 1))]

    def sum_route(mask):
        return [(j, j ^ mask) for j in range(groups_y)]

    def partner_route(mask):
        return both_ways([(j, groups_y + (j ^ mask)) for j in range(groups_y)])

    surface = lax.ppermute(coarse, ("comp", "gy"), partner_route(0)).astype(f32)
    for mask in masks[:1]:
        far = lax.ppermute(wide, ("comp", "gy"), partner_route(mask))
        surface = surface + far[:cells].astype(f32)
    coarse = surface.astype(bf16)
    *one_hots, used = one_hots
    coarse, used = lax.optimization_barrier((coarse, used))
    for mask in masks[1:-1]:
        surface = surface + lax.ppermute(coarse, "gy", sum_route(mask)).astype(f32)
        coarse = surface.astype(bf16)
    surfaces = [surface] + [
        lax.ppermute(coarse, "gy", sum_route(mask)) for mask in masks[1:][-1:]
    ]

    def ring_pairs(count, odd):
        return [(a, (a + 1) % count) for a in range(odd, count, 2)]

    def flat(comp, i, j):
        return (comp * groups_x + i) * groups_y + j

    def level_route(odd):
        pairs = []
        for i in range(groups_x):
            linked = [(a, a + 1) for a in range(odd, groups_y - 1, 2)]
            alone = set(range(groups_y)) - {j for pair in linked for j in pair}
            pairs += [(flat(1, i, a), flat(1, i, b)) for a, b in linked]
            if i % 2 == 0:
                pairs += [(flat(1, i, j), flat(1, i + 1, j)) for j in sorted(alone)]
                if odd or not paired:
                    pairs += [(flat(0, i, j), flat(0, i + 1, j)) for j in range(groups_y)]
            if paired and not odd and i < i ^ 2:
                pairs += [(flat(0, i, j), flat(0, i ^ 2, j)) for j in range(groups_y)]
        return both_ways(pairs)

    e1 = lax.ppermute(e1, "gx", both_ways(ring_pairs(groups_x, 0)))
    e3 = lax.ppermute(e3, "gx", both_ways(ring_pairs(groups_x, 1)))
    axes = ("comp", "gx", "gy")
    e2 = lax.ppermute(e2, axes, level_route(0))
    e4 = lax.ppermute(e4, axes, level_route(1))

    landing_order = sorted(range(1, groups_y), key=lambda mask: (mask % 2, -mask))
    landing, *sent = pl.pallas_call(
        functools.partial(regrid_kernel, len(surfaces)),
        out_shape=[shape((cells, LANES), f32)]
        + [
            shape((cells + 16 * (groups_y - 2 - landing_order.index(mask)), LANES), bf16)
            for mask in range(1, groups_y)
        ],
        in_specs=[vmem] * (len(surfaces) + 5) + [hbm, hbm] + [anywhere] * 1,
        out_specs=[vmem] * groups_y,
        scratch_shapes=[
            pltpu.VMEM((blocks, points, points), bf16),
            pltpu.VMEM((blocks, points), f32),
            pltpu.VMEM((blocks, points), f32),
            pltpu.SemaphoreType.DMA,
        ],
        compiler_params=params(),
        cost_estimate=pl.CostEstimate(flops=2_200_000_000, bytes_accessed=0, transcendentals=0),
        name="regrid_blocks",
    )(
        *surfaces, *one_hots, used, a2o_weight, marine_air_piece_factor, e3,
    )

    def landing_route(mask):
        pairs = [
            (flat(0, i, j), flat(0, i, j ^ mask))
            for i in range(groups_x)
            for j in range(groups_y)
            if j < j ^ mask
        ]
        pairs += [(flat(1, i, 0), flat(1, i, mask)) for i in range(groups_x)]
        pairs += [
            (flat(1, i, j), flat(1, i + 1, j))
            for i in range(0, groups_x, 2)
            for j in range(groups_y)
            if j not in (0, mask)
        ]
        return both_ways(pairs)

    parts = [
        lax.ppermute(block, axes, landing_route(mask)) for mask, block in enumerate(sent, 1)
    ]

    extra = []
    if not paired:
        p, q = jnp.moveaxis(lax.all_gather(sums[0], "gx").astype(f32), 1, 0)
        viscous = lax.dynamic_slice_in_dim(
            diffusivity, lax.axis_index("gy") * channels, channels
        )[:, None]
        rates = [half_rates(g, 0, columns // 4, columns) for g in (0, 0, 1, 1)]
        _, alpha, _ = decay_terms(viscous, jnp.concatenate(rates, axis=1))
        gap = lax.axis_index("gx") - jnp.arange(groups_x)
        decay = jnp.exp(
            -(rows * jnp.maximum(jnp.abs(gap) - 1, 0))[:, None, None] * alpha[None]
        )
        extra = [
            jnp.sum(jnp.where((gap > 0)[:, None, None], decay * p, 0.0), axis=0),
            jnp.sum(jnp.where((gap < 0)[:, None, None], decay * q, 0.0), axis=0),
        ]
    ring = channels // 2 + 8
    damped, coefs, stepped = pl.pallas_call(
        functools.partial(first_step_kernel, groups_x, groups_y, paired),
        out_shape=[
            shape((rows * channels, columns), bf16),
            shape((7, 16, columns), f32),
            shape((rows + 2, 2, ring, columns), f32),
        ],
        in_specs=[vmem] * (8 + len(extra)),
        out_specs=[vmem] * 3,
        scratch_shapes=[
            pltpu.VMEM((rows, channels, columns), f32),
            pltpu.VMEM((rows * channels, columns), bf16),
            pltpu.VMEM((rows, channels, LANES), f32),
            pltpu.VMEM((rows + 4, 2, ring, columns), f32),
            pltpu.VMEM((16, columns), f32),
        ],
        compiler_params=params(),
        name="damping_or_first_step",
    )(fields, wet_cells, diff_row, forward, e1, e3, e2, e4, *extra)

    surface_sum, near, far = pl.pallas_call(
        functools.partial(heat_kernel, rows),
        out_shape=[
            shape((cells, LANES), f32),
            shape((columns // 16, LANES), bf16),
            shape((columns // 16, LANES), bf16),
        ],
        in_specs=[vmem] * 3 + [anywhere] + [vmem] * len(parts),
        out_specs=[vmem] * 3,
        compiler_params=params(),
        name="surface_sum",
    )(e2, e4, landing, coefs, *parts)

    near = lax.ppermute(near, "gx", both_ways(ring_pairs(groups_x, 0)))
    far = lax.ppermute(far, "gx", both_ways(ring_pairs(groups_x, 1)))
    base = pl.pallas_call(
        second_step_kernel,
        out_shape=shape((rows, channels, columns), f32),
        in_specs=[vmem] * 6,
        out_specs=vmem,
        compiler_params=params(),
        name="inverse_or_second_step",
    )(gain_row, inverse, damped, coefs, stepped, surface_sum)
    return pl.pallas_call(
        functools.partial(last_kernel, groups_x, groups_y),
        out_shape=shape(fields.shape, f32),
        in_specs=[vmem] * 5,
        out_specs=hbm,
        scratch_shapes=[
            pltpu.VMEM((rows, channels, columns), f32),
            pltpu.VMEM((16, columns), f32),
            pltpu.VMEM((2, rows, columns), f32),
            pltpu.SemaphoreType.DMA((rows,)),
        ],
        compiler_params=params(),
        name="add_surface_terms",
    )(base, coefs, surface_sum, near, far)


def solution(mesh):
    in_specs = (
        P("comp", "gx", "gy", None),
        P("gx", None),
        P(),
        P(),
        P(),
        P("gx", "gy", None, None),
        P("gx", "gy", None, None),
        P("gx", "gy"),
        P("gx", "gy", None, None, None),
        P("gx", "gy", None, None),
        P("gx", "gy", None, None),
        P("gx", "gy"),
        P("gx", "gy", None, None, None),
    )
    out_specs = P("comp", "gx", "gy", None)
    return jax.shard_map(local, mesh=mesh, in_specs=in_specs, out_specs=out_specs, check_vma=False)
```

```python
import functools

import jax
import jax.numpy as jnp
import numpy as np
from jax import lax
from jax.experimental import pallas as pl
from jax.experimental.pallas import tpu as pltpu
from jax.sharding import PartitionSpec as P

spread_rate = 0.2
mixing_rate = 0.1
heat_gain = 0.5
salt_gain = -0.25
LANES = 128
f32 = jnp.float32
bf16 = jnp.bfloat16


def fourier_tables(columns):
    half = columns // 2
    forward, inverse = [], []
    for first in (0, 1):
        waves = np.arange(first, half, 2)
        phase = np.arange(half)[:, None] * waves[None, :] % columns
        angles = phase * (2.0 * np.pi / columns)
        table = np.concatenate([np.cos(angles), np.sin(angles)], axis=1)
        weight = np.where(waves == 0, 1.0, 2.0) / columns
        forward.append(table)
        inverse.append(table.T * np.concatenate([weight, weight])[:, None])
    return (
        jnp.asarray(np.concatenate(forward).astype(np.float32), bf16),
        jnp.asarray(np.concatenate(inverse).astype(np.float32), bf16),
    )


def wave_parts(columns):
    quarter = columns // 4
    return [
        (g, n, (g * 2 * quarter + n, (g * 2 + 1) * quarter + n))
        for g in (0, 1)
        for n in range(0, quarter, LANES)
    ]


def half_rates(group, first, count, columns):
    lane = lax.broadcasted_iota(jnp.int32, (1, count), 1) + first
    wave = (2 * lane + group).astype(f32)
    sine = jnp.sin(wave * (np.pi / columns))
    return 2.0 * sine * sine


def both_ways(pairs):
    return [p for a, b in pairs for p in ((a, b), (b, a))]


def channel_column(row, channels, first):
    n = row.shape[1]
    lane = lax.broadcasted_iota(jnp.int32, (channels, n), 1)
    sub = lax.broadcasted_iota(jnp.int32, (channels, n), 0)
    return jnp.sum(jnp.where(lane == sub + first, row, 0.0), axis=1, keepdims=True)


def to_tiles(surface):
    cols = surface.shape[1]
    return jnp.concatenate(
        [surface[:, k : k + LANES] for k in range(0, cols, LANES)], axis=0
    )


def from_tiles(tiles, rows):
    return jnp.concatenate(
        [tiles[k : k + rows] for k in range(0, tiles.shape[0], rows)], axis=1
    )


def lengthen(ref, block):
    rows = block.shape[0]
    ref[0:rows, :] = block
    if ref.shape[0] > rows:
        ref[rows:, :] = block[: ref.shape[0] - rows]


def decay_terms(diff_column, rates):
    half = 0.5 / diff_column + rates
    sinh = jnp.sqrt(half * (half + 2.0))
    grow = 1.0 + half + sinh
    return 1.0 / grow, jnp.log(grow), sinh


def edge_factors(lam, alpha, base, total, rows):
    lam2 = lam * lam
    powers = [
        jnp.exp(-2.0 * base * alpha) * lam2,
        jnp.exp(-2.0 * (total - rows - base) * alpha) * lam2,
    ]
    lows, highs = [], []
    for _ in range(rows):
        lows.append(1.0 - powers[0])
        highs.insert(0, 1.0 - powers[1])
        powers = [power * lam2 for power in powers]
    return lows, highs


def fold(values, flat_ref, r):
    channels, columns = values.shape
    half = columns // 2
    left, right = values[:, :half], values[:, half:]
    flat_ref[r * channels : (r + 1) * channels, :half] = (left + right).astype(bf16)
    flat_ref[r * channels : (r + 1) * channels, half:] = (left - right).astype(bf16)


def start_kernel(
    groups_x, paired, x_hbm, wet_hbm, flux_hbm, diff_hbm, table_hbm, *refs
):
    outs = 6 if paired else 7
    coarse_hbm, wide_hbm, *message_hbm = refs[:outs]
    coarse_ref, wide_ref, *message_ref = refs[outs : 2 * outs]
    e1_ref, e3_ref, e2_ref, e4_ref = message_ref[:4]
    if not paired:
        pq_ref = message_ref[4]
    (
        x_ref, wet_ref, flux_ref, diff_ref, table_ref, flat_ref, row_ref, edge_ref,
        factor_ref, x_sem, sem, out_sem,
    ) = refs[2 * outs :]
    rows, channels, columns = x_ref.shape
    half = columns // 2
    row_group = lax.axis_index("gx")
    col_group = lax.axis_index("gy")
    is_atmos = lax.axis_index("comp") == 0

    x_copies = [
        pltpu.make_async_copy(x_hbm.at[0, r], x_ref.at[r], x_sem.at[r]) for r in range(rows)
    ]
    surface_copies = [
        pltpu.make_async_copy(coarse_ref, coarse_hbm, out_sem.at[0]),
        pltpu.make_async_copy(wide_ref, wide_hbm, out_sem.at[1]),
    ]
    message_copies = [
        pltpu.make_async_copy(ref, hbm, out_sem.at[2 + k])
        for k, (ref, hbm) in enumerate(zip(message_ref, message_hbm))
    ]

    def send_surface():
        coarse = to_tiles(row_ref[...]).astype(bf16)
        coarse_ref[...] = coarse
        lengthen(wide_ref, coarse)
        for copy in surface_copies:
            copy.start()

    @pl.when(is_atmos)
    def _():
        flux_copy = pltpu.make_async_copy(flux_hbm, flux_ref, sem.at[0])
        diff_copy = pltpu.make_async_copy(diff_hbm, diff_ref, sem.at[1])
        table_copies = [
            pltpu.make_async_copy(
                table_hbm.at[pl.ds(k * half, half)], table_ref.at[pl.ds(k * half, half)], sem.at[2 + k]
            )
            for k in range(2)
        ]
        for copy in [flux_copy, diff_copy] + x_copies + table_copies:
            copy.start()
        first = col_group * channels
        flux_copy.wait()
        weight = channel_column(flux_ref[...], channels, first)
        diff_copy.wait()
        diff = channel_column(diff_ref[...], channels, first)
        total = rows * groups_x
        base = (row_group * rows).astype(f32)
        tiles = wave_parts(columns)
        for k, (group, n, _) in enumerate(tiles):
            lam, alpha, _ = decay_terms(diff, half_rates(group, n, LANES, columns))
            factor_ref[k, 0] = lam
            lows, highs = edge_factors(lam, alpha, base, total, rows)
            for r in range(rows):
                factor_ref[k, 1 + r] = lows[r]
                factor_ref[k, 1 + rows + r] = highs[r]
        for r in range(rows):
            x_copies[r].wait()
            row_ref[r : r + 1, :] = jnp.sum(x_ref[r] * weight, axis=0, keepdims=True)
            fold(x_ref[r], flat_ref, r)
        send_surface()
        for k in range(2):
            table_copies[k].wait()
            lanes = slice(k * half, (k + 1) * half)
            part = jnp.dot(
                flat_ref[:, lanes], table_ref[lanes, :], preferred_element_type=f32
            )
            for tile, (group, _, parts) in enumerate(tiles):
                if group != k:
                    continue
                lam = factor_ref[tile, 0]
                for at in parts:
                    lanes = slice(at, at + LANES)
                    here = slice(at - k * half, at - k * half + LANES)
                    p = factor_ref[tile, 1] * part[0:channels, here]
                    q = factor_ref[tile, 2 * rows] * part[(rows - 1) * channels :, here]
                    for r in range(1, rows):
                        up = part[r * channels : (r + 1) * channels, here]
                        down = part[(rows - 1 - r) * channels : (rows - r) * channels, here]
                        p = lam * p + factor_ref[tile, 1 + r] * up
                        q = lam * q + factor_ref[tile, 2 * rows - r] * down
                    if paired:
                        for mask, out in ((1, e1_ref), (2, e2_ref), (3, e3_ref)):
                            upward = row_group < (row_group ^ mask)
                            out[0:channels, lanes] = jnp.where(upward, p, q).astype(bf16)
                    else:
                        pq_ref[0, :, lanes] = p.astype(bf16)
                        pq_ref[1, :, lanes] = q.astype(bf16)
        sums_copies = [
            pltpu.make_async_copy(
                message_ref[k].at[pl.ds(0, channels)],
                message_hbm[k].at[pl.ds(0, channels)],
                out_sem.at[2 + k],
            )
            for k in range(3)
        ]
        if not paired:
            sums_copies = message_copies[4:]
        for copy in sums_copies:
            copy.start()
        for copy in surface_copies + sums_copies:
            copy.wait()

    @pl.when(jnp.logical_not(is_atmos))
    def _():
        wet_copy = pltpu.make_async_copy(wet_hbm, wet_ref, sem.at[0])
        for copy in x_copies + [wet_copy]:
            copy.start()
        gain = jnp.where(col_group == 0, 1.0, 0.0)
        for r in range(rows):
            x_copies[r].wait()
            row_ref[r : r + 1, :] = x_ref[r, 0:1, :] * gain
        send_surface()
        wet_copy.wait()
        levels = channels // 2
        lines = 2 * channels
        even_x = row_group % 2 == 0
        even_y = col_group % 2 == 0
        wet = wet_ref[...].astype(f32)
        wet = jnp.concatenate([wet, wet], axis=0).astype(bf16)

        def put(out, last):
            @pl.when(last)
            def _():
                out[0:lines, :] = x_ref[rows - 2 :].reshape(lines, columns).astype(bf16)

            @pl.when(jnp.logical_not(last))
            def _():
                out[0:lines, :] = x_ref[:2].reshape(lines, columns).astype(bf16)

            out[lines : lines + 16, :] = wet

        put(e1_ref, even_x)
        put(e3_ref, jnp.logical_not(even_x))

        def put_edges(out, level):
            for r in range(rows):
                for t in range(2):
                    at = (r * 2 + t) * 2
                    c = t * levels + level
                    edge_ref[at : at + 2, :] = x_ref[r, c : c + 2, :]
            out[0 : rows * 4, :] = edge_ref[...].astype(bf16)

        @pl.when(even_y)
        def _():
            put_edges(e2_ref, levels - 2)
            put_edges(e4_ref, 0)

        @pl.when(jnp.logical_not(even_y))
        def _():
            put_edges(e2_ref, 0)
            put_edges(e4_ref, levels - 2)

        for copy in message_copies:
            copy.start()
        for copy in surface_copies + message_copies:
            copy.wait()


def one_hot_kernel(
    rows, columns, a_src, a_dst, a_count, m_src, m_dst, m_count, src_hot_ref, dst_hot_ref,
    src_row_ref, dst_row_ref, used_ref,
):
    is_atmos = lax.axis_index("comp") == 0
    blocks, points = src_row_ref.shape
    count = jnp.where(is_atmos, m_count[0, 0], a_count[0, 0])
    block_iota = lax.broadcasted_iota(jnp.int32, (blocks, points), 0)
    used_ref[...] = jnp.where(block_iota < count, 1, 0)
    lane_iota = lax.broadcasted_iota(jnp.int32, (LANES, points), 0)
    for a_ref, m_ref, hot_ref, row_ref in (
        (a_src, m_src, src_hot_ref, src_row_ref),
        (a_dst, m_dst, dst_hot_ref, dst_row_ref),
    ):
        index = jnp.where(is_atmos, m_ref[0, 0], a_ref[0, 0])
        row = index // columns
        tile = (index // LANES) % (columns // LANES)
        row_ref[...] = tile * rows + row
        lane = index % LANES
        for b in range(blocks):
            hot_ref[:, b * points : (b + 1) * points] = jnp.where(
                lane_iota == lane[b : b + 1], 1.0, 0.0
            ).astype(bf16)


def regrid_kernel(n_surfaces, *refs):
    surfaces = refs[:n_surfaces]
    (
        src_hot_ref, dst_hot_ref, src_row_ref, dst_row_ref, used_ref, a_weight, m_weight,
        _,
        *refs,
    ) = refs[n_surfaces:]
    land_ref, *sent_refs = refs[:-4]
    weight_ref, gath_ref, val_ref, sem = refs[-4:]
    is_atmos = lax.axis_index("comp") == 0
    blocks, points = val_ref.shape
    cells = surfaces[0].shape[0]

    @pl.when(is_atmos)
    def _():
        pltpu.make_async_copy(m_weight.at[0, 0], weight_ref, sem).start()

    @pl.when(jnp.logical_not(is_atmos))
    def _():
        pltpu.make_async_copy(a_weight.at[0, 0], weight_ref, sem).start()

    pair = 2 * points
    row_iota = lax.broadcasted_iota(jnp.int32, (cells, points), 0)
    table = sum(surface[...].astype(f32) for surface in surfaces).astype(bf16)
    for b in range(0, blocks, 2):
        picked = jnp.dot(
            table, src_hot_ref[:, b * points : b * points + pair], preferred_element_type=f32
        )
        for k in range(2):
            mine = row_iota == src_row_ref[b + k : b + k + 1, :]
            part = jnp.where(mine, picked[:, k * points : (k + 1) * points], 0.0)
            gath_ref[b + k : b + k + 1, :] = jnp.sum(part, axis=0, keepdims=True)
    gathered = gath_ref[...].astype(bf16)

    @pl.when(is_atmos)
    def _():
        pltpu.make_async_copy(m_weight.at[0, 0], weight_ref, sem).wait()

    @pl.when(jnp.logical_not(is_atmos))
    def _():
        pltpu.make_async_copy(a_weight.at[0, 0], weight_ref, sem).wait()

    block_iota = lax.broadcasted_iota(jnp.int32, (blocks, points), 0)
    values = jnp.zeros((blocks, points), f32)
    for b in range(0, blocks, 2):
        terms = lax.dot_general(
            gathered,
            weight_ref[b : b + 2].reshape(pair, points),
            (((1,), (1,)), ((), ())),
            preferred_element_type=f32,
        )
        for k in range(2):
            values = jnp.where(block_iota == b + k, terms[:, k * points : (k + 1) * points], values)
    val_ref[...] = jnp.where(used_ref[...] > 0, values, 0.0)
    land = jnp.zeros((2 * cells, LANES), f32)
    for b in range(0, blocks, 2):
        spread = []
        for k in range(b, b + 2):
            value = val_ref[k : k + 1, :]
            coarse = value.astype(bf16).astype(f32)
            fine = value - coarse
            mine = row_iota == dst_row_ref[k : k + 1, :]
            spread.append(
                jnp.concatenate(
                    [jnp.where(mine, coarse, 0.0), jnp.where(mine, fine, 0.0)], axis=0
                ).astype(bf16)
            )
        land = land + lax.dot_general(
            jnp.concatenate(spread, axis=1),
            dst_hot_ref[:, b * points : b * points + pair],
            (((1,), (1,)), ((), ())),
            preferred_element_type=f32,
        )
    land = land[:cells] + land[cells:]
    land_ref[...] = land
    for sent_ref in sent_refs:
        lengthen(sent_ref, land.astype(bf16))


def heat_kernel(rows, e2_ref, e4_ref, land_ref, _, *refs):
    parts = refs[:-3]
    sum_ref, near_ref, far_ref = refs[-3:]
    cells = land_ref.shape[0]
    columns = cells // rows * LANES
    even_x = lax.axis_index("gx") % 2 == 0
    even_y = lax.axis_index("gy") % 2 == 0
    total = land_ref[...]
    for part in parts:
        total = total + part[0:cells, :].astype(f32)
    sum_ref[...] = total

    def corners(row):
        start = row * 4 // 16 * 16
        one = e2_ref[start : start + 16, :].astype(f32)
        two = e4_ref[start : start + 16, :].astype(f32)
        low = jnp.where(even_y, two, one)
        high = jnp.where(even_y, one, two)
        at = row * 4 - start
        lines = [low[at + 1 : at + 2], low[at + 3 : at + 4], high[at : at + 1], high[at + 2 : at + 3]]
        heat = from_tiles(total, rows)[row : row + 1]
        blank = jnp.zeros((3, columns), f32)
        return to_tiles(jnp.concatenate([heat] + lines + [blank], axis=0))

    first, last = corners(0), corners(rows - 1)
    near_ref[...] = jnp.where(even_x, last, first).astype(bf16)
    far_ref[...] = jnp.where(even_x, first, last).astype(bf16)


def advance(ref, r, t, coefs, size):
    ring, columns = ref.shape[2:]
    whole = ref[r, t]
    up = pltpu.roll(whole, 1, 0)[:size]
    down = pltpu.roll(whole, ring - 1, 0)[:size]
    mid = whole[:size]
    total = coefs[0] * mid + coefs[5] * (up + down)
    total = total + coefs[1] * ref[r - 1, t, 0:size, :]
    total = total + coefs[2] * ref[r + 1, t, 0:size, :]
    total = total + coefs[3] * pltpu.roll(mid, 1, 1)
    return total + coefs[4] * pltpu.roll(mid, columns - 1, 1)


def first_step_kernel(
    groups_x, groups_y, paired, x_ref, wet_ref, diff_ref, table_ref, e1_ref, e3_ref,
    e2_ref, e4_ref, *refs,
):
    if not paired:
        pin_ref, qin_ref = refs[:2]
    zb_ref, c_ref, t1_ref, y_ref, flat_ref, z_ref, t0_ref, w_ref = refs[-8:]
    _, rows, channels, columns = x_ref.shape
    row_group = lax.axis_index("gx")
    col_group = lax.axis_index("gy")
    is_atmos = lax.axis_index("comp") == 0

    @pl.when(is_atmos)
    def _():
        half = columns // 2
        for r in range(rows):
            fold(x_ref[0, r], flat_ref, r)
        for k in range(2):
            lanes = slice(k * half, (k + 1) * half)
            part = jnp.dot(
                flat_ref[:, lanes], table_ref[lanes, :], preferred_element_type=f32
            )
            y_ref[:, :, lanes] = part.reshape(rows, channels, half)
        diff = channel_column(diff_ref[...], channels, col_group * channels)
        total = rows * groups_x
        base = (row_group * rows).astype(f32)
        for group, n, parts in wave_parts(columns):
            lam, alpha, sinh = decay_terms(diff, half_rates(group, n, LANES, columns))
            scale = 1.0 / (
                2.0 * diff * sinh * (1.0 - jnp.exp(-2.0 * (total + 1) * alpha))
            )
            lows, highs = edge_factors(lam, alpha, base, total, rows)
            for part in parts:
                lanes = slice(part, part + LANES)
                if paired:
                    pin = jnp.zeros((channels, LANES), f32)
                    qin = jnp.zeros((channels, LANES), f32)
                    for mask, msg in ((1, e1_ref), (2, e2_ref), (3, e3_ref)):
                        band = row_group ^ mask
                        gap = (jnp.abs(row_group - band) - 1) * rows
                        term = jnp.exp(-gap.astype(f32) * alpha)
                        term = term * msg[0:channels, lanes].astype(f32)
                        pin = pin + jnp.where(band < row_group, term, 0.0)
                        qin = qin + jnp.where(band > row_group, term, 0.0)
                else:
                    pin = pin_ref[:, lanes]
                    qin = qin_ref[:, lanes]
                f = pin
                for r in range(rows):
                    f = lam * f + lows[r] * y_ref[r, :, lanes]
                    z_ref[r] = highs[r] * f
                g = lam * qin
                for r in reversed(range(rows)):
                    z = scale * (z_ref[r] + lows[r] * g)
                    zb_ref[r * channels : (r + 1) * channels, lanes] = z.astype(bf16)
                    g = lam * (g + highs[r] * y_ref[r, :, lanes])

    @pl.when(jnp.logical_not(is_atmos))
    def _():
        levels = channels // 2
        ring = levels + 8
        lines = 2 * channels
        first_x = row_group == 0
        last_x = row_group == groups_x - 1
        top = col_group == 0
        bottom = col_group == groups_y - 1
        even_x = row_group % 2 == 0
        even_y = col_group % 2 == 0

        one = e1_ref[lines : lines + 16, :].astype(f32)
        three = e3_ref[lines : lines + 16, :].astype(f32)
        below = jnp.where(even_x, three, one)[rows - 2 : rows]
        above = jnp.where(even_x, one, three)[0:2]
        w_ref[0:2, :] = jnp.where(first_x, 0.0, below)
        w_ref[2 : rows + 2, :] = wet_ref[...].astype(f32)
        w_ref[rows + 2 : rows + 4, :] = jnp.where(last_x, 0.0, above)

        span = rows + 2
        north = w_ref[0:span, :]
        here = w_ref[1 : span + 1, :]
        south = w_ref[2 : span + 2, :]
        west = pltpu.roll(here, 1, 1)
        east = pltpu.roll(here, columns - 1, 1)
        c_ref[0, 0:span, :] = here * (
            1.0 - 2.0 * mixing_rate - spread_rate * (north + south + west + east)
        )
        c_ref[1, 0:span, :] = spread_rate * here * north
        c_ref[2, 0:span, :] = spread_rate * here * south
        c_ref[3, 0:span, :] = spread_rate * here * west
        c_ref[4, 0:span, :] = spread_rate * here * east
        c_ref[5, 0:span, :] = mixing_rate * here
        c_ref[6, 0:span, :] = here

        one = e1_ref[0:lines, :].astype(f32)
        three = e3_ref[0:lines, :].astype(f32)
        below = jnp.where(even_x, three, one)
        above = jnp.where(even_x, one, three)
        blank = jnp.zeros((8, columns), f32)
        for k in range(2):
            for t in range(2):
                c = k * channels + t * levels
                t0_ref[k, t, 0:levels, :] = below[c : c + levels]
                t0_ref[rows + 2 + k, t, 0:levels, :] = above[c : c + levels]
                t0_ref[k, t, levels:ring, :] = blank
                t0_ref[rows + 2 + k, t, levels:ring, :] = blank
        one = e2_ref[...].astype(f32)
        two = e4_ref[0 : 4 * rows, :].astype(f32)
        before = jnp.where(even_y, two, one)
        after = jnp.where(even_y, one, two)
        for r in range(rows):
            for t in range(2):
                k = (r * 2 + t) * 2
                t0_ref[r + 2, t, 0:levels, :] = x_ref[0, r, t * levels : (t + 1) * levels, :]
                t0_ref[r + 2, t, levels : levels + 2, :] = after[k : k + 2]
                t0_ref[r + 2, t, ring - 2 : ring, :] = before[k : k + 2]

        def close(ref, r):
            for t in range(2):
                ref[r, t, ring - 1 : ring, :] = jnp.where(
                    top, ref[r, t, 0:1, :], ref[r, t, ring - 1 : ring, :]
                )
                ref[r, t, levels : levels + 1, :] = jnp.where(
                    bottom, ref[r, t, levels - 1 : levels, :], ref[r, t, levels : levels + 1, :]
                )

        def first(r, carry):
            coefs = [c_ref[k, pl.ds(r, 1), :] for k in range(6)]
            close(t0_ref, r + 1)
            for t in range(2):
                t1_ref[r, t] = advance(t0_ref, r + 1, t, coefs, ring)
            close(t1_ref, r)
            return carry

        lax.fori_loop(0, span, first, 0)


def second_step_kernel(gain_ref, table_ref, zb_ref, c_ref, t1_ref, sum_ref, base_ref):
    rows, channels, columns = base_ref.shape
    is_atmos = lax.axis_index("comp") == 0

    @pl.when(is_atmos)
    def _():
        response = channel_column(gain_ref[...], channels, lax.axis_index("gy") * channels)
        forcing = from_tiles(sum_ref[...], rows)
        half = columns // 2
        step = 256
        for n in range(0, half, step):
            even, odd = [
                jnp.dot(
                    zb_ref[:, k * half : (k + 1) * half],
                    table_ref[k * half : (k + 1) * half, n : n + step],
                    preferred_element_type=f32,
                ).reshape(rows, channels, step)
                for k in range(2)
            ]
            for r in range(rows):
                for lane, part in ((n, even[r] + odd[r]), (n + half, even[r] - odd[r])):
                    lanes = slice(lane, lane + step)
                    base_ref[r, :, lanes] = part + response * forcing[r : r + 1, lanes]

    @pl.when(jnp.logical_not(is_atmos))
    def _():
        levels = channels // 2

        def second(r, carry):
            coefs = [c_ref[k, pl.ds(r, 1), :] for k in range(6)]
            for t in range(2):
                c = t * levels
                base_ref[r - 1, c : c + levels, :] = advance(t1_ref, r, t, coefs, levels)
            return carry

        lax.fori_loop(1, rows + 1, second, 0)


def last_kernel(
    groups_x, groups_y, base_ref, c_ref, sum_ref, near_ref, far_ref, out_hbm,
    out_ref, e_ref, heat_ref, sem,
):
    rows, channels, columns = out_ref.shape
    row_group = lax.axis_index("gx")
    col_group = lax.axis_index("gy")
    is_atmos = lax.axis_index("comp") == 0
    copies = [
        pltpu.make_async_copy(out_ref.at[r], out_hbm.at[0, r], sem.at[r]) for r in range(rows)
    ]
    as_they_are = [
        pltpu.make_async_copy(base_ref.at[r], out_hbm.at[0, r], sem.at[r]) for r in range(rows)
    ]

    @pl.when(is_atmos)
    def _():
        for copy in as_they_are:
            copy.start()

    @pl.when(jnp.logical_and(jnp.logical_not(is_atmos), col_group > 0))
    def _():
        for copy in as_they_are[1:-1]:
            copy.start()

    @pl.when(jnp.logical_not(is_atmos))
    def _():
        levels = channels // 2
        even = row_group % 2 == 0
        below = jnp.where(even, far_ref[...].astype(f32), near_ref[...].astype(f32))
        above = jnp.where(even, near_ref[...].astype(f32), far_ref[...].astype(f32))

        low = from_tiles(below, 8)
        high = from_tiles(above, 8)
        by_low = c_ref[1, 1:2, :] * (c_ref[5, 0:1, :] + c_ref[5, 1:2, :])
        by_high = c_ref[2, rows : rows + 1, :] * (
            c_ref[5, rows : rows + 1, :] + c_ref[5, rows + 1 : rows + 2, :]
        )
        has_before = jnp.where(col_group > 0, 1.0, 0.0)
        has_after = jnp.where(col_group < groups_y - 1, 1.0, 0.0)

        @pl.when(col_group == 0)
        def _():
            span = rows + 2
            e_ref[0:1, :] = low[0:1]
            e_ref[1 : rows + 1, :] = from_tiles(sum_ref[...], rows)
            e_ref[rows + 1 : span, :] = high[0:1]
            e_ref[0:span, :] = c_ref[6, 0:span, :] * e_ref[0:span, :]
            own = slice(1, rows + 1)
            heat = e_ref[own, :]
            second = c_ref[5, own, :] * heat
            first = (c_ref[0, own, :] + 1.0) * heat + second
            first = first + c_ref[1, own, :] * e_ref[0:rows, :]
            first = first + c_ref[2, own, :] * e_ref[2 : rows + 2, :]
            first = first + c_ref[3, own, :] * pltpu.roll(heat, 1, 1)
            first = first + c_ref[4, own, :] * pltpu.roll(heat, columns - 1, 1)
            heat_ref[0] = first
            heat_ref[1] = second

        for r in (0, rows - 1):
            out_ref[r] = base_ref[r]
        for t in range(2):
            c = t * levels
            d = c + levels - 1
            for r, factor, lines in ((0, by_low, low), (rows - 1, by_high, high)):
                out_ref[r, c : c + 1, :] = out_ref[r, c : c + 1, :] + (
                    has_before * factor * lines[t + 1 : t + 2]
                )
                out_ref[r, d : d + 1, :] = out_ref[r, d : d + 1, :] + (
                    has_after * factor * lines[t + 3 : t + 4]
                )

        @pl.when(col_group == 0)
        def _():
            for r in range(rows):
                if r not in (0, rows - 1):
                    out_ref[r] = base_ref[r]
                for t, gain in enumerate((heat_gain, salt_gain)):
                    c = t * levels
                    for k in range(2):
                        out_ref[r, c + k : c + k + 1, :] = (
                            out_ref[r, c + k : c + k + 1, :] + gain * heat_ref[k, r : r + 1, :]
                        )
                copies[r].start()

        @pl.when(col_group > 0)
        def _():
            copies[0].start()
            copies[-1].start()

    for copy in copies:
        copy.wait()


def local(
    fields,
    wet_cells,
    flux_weight,
    variable_sea_response,
    diffusivity,
    a2o_source,
    a2o_target,
    a2o_count,
    a2o_weight,
    marine_air_input_index,
    marine_air_output_index,
    marine_air_piece_tally,
    marine_air_piece_factor,
):
    _, rows, channels, columns = fields.shape
    groups_x = lax.axis_size("gx")
    groups_y = lax.axis_size("gy")
    blocks, points = a2o_source.shape[2:]
    cells = rows * columns // LANES
    forward, inverse = fourier_tables(columns)
    flux_row = flux_weight[None, :]
    gain_row = variable_sea_response[None, :]
    diff_row = diffusivity[None, :]
    paired = groups_x == 4
    params = functools.partial(pltpu.CompilerParams, vmem_limit_bytes=40 * 2**20)
    vmem = pl.BlockSpec(memory_space=pltpu.VMEM)
    smem = pl.BlockSpec(memory_space=pltpu.SMEM)
    hbm = pl.BlockSpec(memory_space=pltpu.HBM)
    anywhere = pl.BlockSpec(memory_space=pl.ANY)

    def shape(dims, dtype):
        return jax.ShapeDtypeStruct(dims, dtype)

    lines = 2 * channels + 16
    shapes = [
        shape((cells, LANES), bf16),
        shape((cells + 16, LANES), bf16),
        shape((lines, columns), bf16),
        shape((lines, columns), bf16),
        shape((4 * rows, columns), bf16),
        shape((4 * rows, columns), bf16),
    ]
    if not paired:
        shapes.append(shape((2, channels, columns), bf16))
    coarse, wide, e1, e3, e2, e4, *sums = pl.pallas_call(
        functools.partial(start_kernel, groups_x, paired),
        out_shape=shapes,
        in_specs=[hbm] * 5,
        out_specs=[hbm] * len(shapes),
        scratch_shapes=[pltpu.VMEM(out.shape, out.dtype) for out in shapes]
        + [
            pltpu.VMEM((rows, channels, columns), f32),
            pltpu.VMEM((rows, columns), jnp.int32),
            pltpu.VMEM(flux_row.shape, f32),
            pltpu.VMEM(diff_row.shape, f32),
            pltpu.VMEM(forward.shape, bf16),
            pltpu.VMEM((rows * channels, columns), bf16),
            pltpu.VMEM((rows, columns), f32),
            pltpu.VMEM((4 * rows, columns), f32),
            pltpu.VMEM((columns // 2 // LANES, 2 * rows + 1, channels, LANES), f32),
            pltpu.SemaphoreType.DMA((rows,)),
            pltpu.SemaphoreType.DMA((4,)),
            pltpu.SemaphoreType.DMA((len(shapes),)),
        ],
        compiler_params=pltpu.CompilerParams(vmem_limit_bytes=58 * 2**20),
        name="surface_and_forward_or_halos",
    )(fields, wet_cells, flux_row, diff_row, forward)

    one_hots = pl.pallas_call(
        functools.partial(one_hot_kernel, rows, columns),
        out_shape=[
            shape((LANES, blocks * points), bf16),
            shape((LANES, blocks * points), bf16),
            shape((blocks, points), jnp.int32),
            shape((blocks, points), jnp.int32),
            shape((blocks, points), jnp.int32),
        ],
        in_specs=[vmem, vmem, smem] * 2,
        out_specs=[vmem] * 5,
        compiler_params=params(),
        name="one_hots",
    )(
        a2o_source, a2o_target, a2o_count,
        marine_air_input_index, marine_air_output_index, marine_air_piece_tally,
    )

    masks = [1 << bit for bit in range(groups_y.bit_length() - 1)]

    def sum_route(mask):
        return [(j, j ^ mask) for j in range(groups_y)]

    def partner_route(mask):
        return both_ways([(j, groups_y + (j ^ mask)) for j in range(groups_y)])

    surface = lax.ppermute(coarse, ("comp", "gy"), partner_route(0)).astype(f32)
    for mask in masks[:1]:
        far = lax.ppermute(wide, ("comp", "gy"), partner_route(mask))
        surface = surface + far[:cells].astype(f32)
    coarse = surface.astype(bf16)
    *one_hots, used = one_hots
    coarse, used = lax.optimization_barrier((coarse, used))
    for mask in masks[1:-1]:
        surface = surface + lax.ppermute(coarse, "gy", sum_route(mask)).astype(f32)
        coarse = surface.astype(bf16)
    surfaces = [surface] + [
        lax.ppermute(coarse, "gy", sum_route(mask)) for mask in masks[1:][-1:]
    ]

    def ring_pairs(count, odd):
        return [(a, (a + 1) % count) for a in range(odd, count, 2)]

    def flat(comp, i, j):
        return (comp * groups_x + i) * groups_y + j

    def level_route(odd):
        pairs = []
        for i in range(groups_x):
            linked = [(a, a + 1) for a in range(odd, groups_y - 1, 2)]
            alone = set(range(groups_y)) - {j for pair in linked for j in pair}
            pairs += [(flat(1, i, a), flat(1, i, b)) for a, b in linked]
            if i % 2 == 0:
                pairs += [(flat(1, i, j), flat(1, i + 1, j)) for j in sorted(alone)]
                if odd or not paired:
                    pairs += [(flat(0, i, j), flat(0, i + 1, j)) for j in range(groups_y)]
            if paired and not odd and i < i ^ 2:
                pairs += [(flat(0, i, j), flat(0, i ^ 2, j)) for j in range(groups_y)]
        return both_ways(pairs)

    e1 = lax.ppermute(e1, "gx", both_ways(ring_pairs(groups_x, 0)))
    e3 = lax.ppermute(e3, "gx", both_ways(ring_pairs(groups_x, 1)))
    axes = ("comp", "gx", "gy")
    e2 = lax.ppermute(e2, axes, level_route(0))
    e4 = lax.ppermute(e4, axes, level_route(1))

    landing, *sent = pl.pallas_call(
        functools.partial(regrid_kernel, len(surfaces)),
        out_shape=[shape((cells, LANES), f32)]
        + [shape((cells + 16 * (mask - 1), LANES), bf16) for mask in range(1, groups_y)],
        in_specs=[vmem] * (len(surfaces) + 5) + [hbm, hbm] + [anywhere] * 1,
        out_specs=[vmem] * groups_y,
        scratch_shapes=[
            pltpu.VMEM((blocks, points, points), bf16),
            pltpu.VMEM((blocks, points), f32),
            pltpu.VMEM((blocks, points), f32),
            pltpu.SemaphoreType.DMA,
        ],
        compiler_params=params(),
        cost_estimate=pl.CostEstimate(flops=2_200_000_000, bytes_accessed=0, transcendentals=0),
        name="regrid_blocks",
    )(
        *surfaces, *one_hots, used, a2o_weight, marine_air_piece_factor, e3,
    )

    def landing_route(mask):
        pairs = [
            (flat(0, i, j), flat(0, i, j ^ mask))
            for i in range(groups_x)
            for j in range(groups_y)
            if j < j ^ mask
        ]
        pairs += [(flat(1, i, 0), flat(1, i, mask)) for i in range(groups_x)]
        pairs += [
            (flat(1, i, j), flat(1, i + 1, j))
            for i in range(0, groups_x, 2)
            for j in range(groups_y)
            if j not in (0, mask)
        ]
        return both_ways(pairs)

    parts = [
        lax.ppermute(block, axes, landing_route(mask)) for mask, block in enumerate(sent, 1)
    ]

    extra = []
    if not paired:
        p, q = jnp.moveaxis(lax.all_gather(sums[0], "gx").astype(f32), 1, 0)
        viscous = lax.dynamic_slice_in_dim(
            diffusivity, lax.axis_index("gy") * channels, channels
        )[:, None]
        rates = [half_rates(g, 0, columns // 4, columns) for g in (0, 0, 1, 1)]
        _, alpha, _ = decay_terms(viscous, jnp.concatenate(rates, axis=1))
        gap = lax.axis_index("gx") - jnp.arange(groups_x)
        decay = jnp.exp(
            -(rows * jnp.maximum(jnp.abs(gap) - 1, 0))[:, None, None] * alpha[None]
        )
        extra = [
            jnp.sum(jnp.where((gap > 0)[:, None, None], decay * p, 0.0), axis=0),
            jnp.sum(jnp.where((gap < 0)[:, None, None], decay * q, 0.0), axis=0),
        ]
    ring = channels // 2 + 8
    damped, coefs, stepped = pl.pallas_call(
        functools.partial(first_step_kernel, groups_x, groups_y, paired),
        out_shape=[
            shape((rows * channels, columns), bf16),
            shape((7, 16, columns), f32),
            shape((rows + 2, 2, ring, columns), f32),
        ],
        in_specs=[vmem] * (8 + len(extra)),
        out_specs=[vmem] * 3,
        scratch_shapes=[
            pltpu.VMEM((rows, channels, columns), f32),
            pltpu.VMEM((rows * channels, columns), bf16),
            pltpu.VMEM((rows, channels, LANES), f32),
            pltpu.VMEM((rows + 4, 2, ring, columns), f32),
            pltpu.VMEM((16, columns), f32),
        ],
        compiler_params=params(),
        name="damping_or_first_step",
    )(fields, wet_cells, diff_row, forward, e1, e3, e2, e4, *extra)

    surface_sum, near, far = pl.pallas_call(
        functools.partial(heat_kernel, rows),
        out_shape=[
            shape((cells, LANES), f32),
            shape((columns // 16, LANES), bf16),
            shape((columns // 16, LANES), bf16),
        ],
        in_specs=[vmem] * 3 + [anywhere] + [vmem] * len(parts),
        out_specs=[vmem] * 3,
        compiler_params=params(),
        name="surface_sum",
    )(e2, e4, landing, coefs, *parts)

    near = lax.ppermute(near, "gx", both_ways(ring_pairs(groups_x, 0)))
    far = lax.ppermute(far, "gx", both_ways(ring_pairs(groups_x, 1)))
    base = pl.pallas_call(
        second_step_kernel,
        out_shape=shape((rows, channels, columns), f32),
        in_specs=[vmem] * 6,
        out_specs=vmem,
        compiler_params=params(),
        name="inverse_or_second_step",
    )(gain_row, inverse, damped, coefs, stepped, surface_sum)
    return pl.pallas_call(
        functools.partial(last_kernel, groups_x, groups_y),
        out_shape=shape(fields.shape, f32),
        in_specs=[vmem] * 5,
        out_specs=hbm,
        scratch_shapes=[
            pltpu.VMEM((rows, channels, columns), f32),
            pltpu.VMEM((16, columns), f32),
            pltpu.VMEM((2, rows, columns), f32),
            pltpu.SemaphoreType.DMA((rows,)),
        ],
        compiler_params=params(),
        name="add_surface_terms",
    )(base, coefs, surface_sum, near, far)


def solution(mesh):
    in_specs = (
        P("comp", "gx", "gy", None),
        P("gx", None),
        P(),
        P(),
        P(),
        P("gx", "gy", None, None),
        P("gx", "gy", None, None),
        P("gx", "gy"),
        P("gx", "gy", None, None, None),
        P("gx", "gy", None, None),
        P("gx", "gy", None, None),
        P("gx", "gy"),
        P("gx", "gy", None, None, None),
    )
    out_specs = P("comp", "gx", "gy", None)
    return jax.shard_map(local, mesh=mesh, in_specs=in_specs, out_specs=out_specs, check_vma=False)
```

```python
import functools

import jax
import jax.numpy as jnp
import numpy as np
from jax import lax
from jax.experimental import pallas as pl
from jax.experimental.pallas import tpu as pltpu
from jax.sharding import PartitionSpec as P

spread_rate = 0.2
mixing_rate = 0.1
heat_gain = 0.5
salt_gain = -0.25
LANES = 128
f32 = jnp.float32
bf16 = jnp.bfloat16


def fourier_tables(columns):
    half = columns // 2
    forward, inverse = [], []
    for first in (0, 1):
        waves = np.arange(first, half, 2)
        phase = np.arange(half)[:, None] * waves[None, :] % columns
        angles = phase * (2.0 * np.pi / columns)
        table = np.concatenate([np.cos(angles), np.sin(angles)], axis=1)
        weight = np.where(waves == 0, 1.0, 2.0) / columns
        forward.append(table)
        inverse.append(table.T * np.concatenate([weight, weight])[:, None])
    return (
        jnp.asarray(np.concatenate(forward).astype(np.float32), bf16),
        jnp.asarray(np.concatenate(inverse).astype(np.float32), bf16),
    )


def wave_parts(columns):
    quarter = columns // 4
    return [
        (g, n, (g * 2 * quarter + n, (g * 2 + 1) * quarter + n))
        for g in (0, 1)
        for n in range(0, quarter, LANES)
    ]


def half_rates(group, first, count, columns):
    lane = lax.broadcasted_iota(jnp.int32, (1, count), 1) + first
    wave = (2 * lane + group).astype(f32)
    sine = jnp.sin(wave * (np.pi / columns))
    return 2.0 * sine * sine


def both_ways(pairs):
    return [p for a, b in pairs for p in ((a, b), (b, a))]


def channel_column(row, channels, first):
    n = row.shape[1]
    lane = lax.broadcasted_iota(jnp.int32, (channels, n), 1)
    sub = lax.broadcasted_iota(jnp.int32, (channels, n), 0)
    return jnp.sum(jnp.where(lane == sub + first, row, 0.0), axis=1, keepdims=True)


def to_tiles(surface):
    cols = surface.shape[1]
    return jnp.concatenate(
        [surface[:, k : k + LANES] for k in range(0, cols, LANES)], axis=0
    )


def from_tiles(tiles, rows):
    return jnp.concatenate(
        [tiles[k : k + rows] for k in range(0, tiles.shape[0], rows)], axis=1
    )


def lengthen(ref, block):
    rows = block.shape[0]
    ref[0:rows, :] = block
    if ref.shape[0] > rows:
        ref[rows:, :] = block[: ref.shape[0] - rows]


def decay_terms(diff_column, rates):
    half = 0.5 / diff_column + rates
    sinh = jnp.sqrt(half * (half + 2.0))
    grow = 1.0 + half + sinh
    return 1.0 / grow, jnp.log(grow), sinh


def edge_factors(lam, alpha, base, total, rows):
    lam2 = lam * lam
    powers = [
        jnp.exp(-2.0 * base * alpha) * lam2,
        jnp.exp(-2.0 * (total - rows - base) * alpha) * lam2,
    ]
    lows, highs = [], []
    for _ in range(rows):
        lows.append(1.0 - powers[0])
        highs.insert(0, 1.0 - powers[1])
        powers = [power * lam2 for power in powers]
    return lows, highs


def fold(values, flat_ref, r):
    channels, columns = values.shape
    half = columns // 2
    left, right = values[:, :half], values[:, half:]
    flat_ref[r * channels : (r + 1) * channels, :half] = (left + right).astype(bf16)
    flat_ref[r * channels : (r + 1) * channels, half:] = (left - right).astype(bf16)


def start_kernel(
    groups_x, paired, x_hbm, wet_hbm, flux_hbm, diff_hbm, table_hbm, *refs
):
    outs = 6 if paired else 7
    coarse_hbm, wide_hbm, *message_hbm = refs[:outs]
    coarse_ref, wide_ref, *message_ref = refs[outs : 2 * outs]
    e1_ref, e3_ref, e2_ref, e4_ref = message_ref[:4]
    if not paired:
        pq_ref = message_ref[4]
    (
        x_ref, wet_ref, flux_ref, diff_ref, table_ref, flat_ref, row_ref, edge_ref,
        factor_ref, x_sem, sem, out_sem,
    ) = refs[2 * outs :]
    rows, channels, columns = x_ref.shape
    half = columns // 2
    row_group = lax.axis_index("gx")
    col_group = lax.axis_index("gy")
    is_atmos = lax.axis_index("comp") == 0

    x_copies = [
        pltpu.make_async_copy(x_hbm.at[0, r], x_ref.at[r], x_sem.at[r]) for r in range(rows)
    ]
    surface_copies = [
        pltpu.make_async_copy(coarse_ref, coarse_hbm, out_sem.at[0]),
        pltpu.make_async_copy(wide_ref, wide_hbm, out_sem.at[1]),
    ]
    message_copies = [
        pltpu.make_async_copy(ref, hbm, out_sem.at[2 + k])
        for k, (ref, hbm) in enumerate(zip(message_ref, message_hbm))
    ]

    def send_surface():
        coarse = to_tiles(row_ref[...]).astype(bf16)
        coarse_ref[...] = coarse
        lengthen(wide_ref, coarse)
        for copy in surface_copies:
            copy.start()

    @pl.when(is_atmos)
    def _():
        flux_copy = pltpu.make_async_copy(flux_hbm, flux_ref, sem.at[0])
        diff_copy = pltpu.make_async_copy(diff_hbm, diff_ref, sem.at[1])
        table_copies = [
            pltpu.make_async_copy(
                table_hbm.at[pl.ds(k * half, half)], table_ref.at[pl.ds(k * half, half)], sem.at[2 + k]
            )
            for k in range(2)
        ]
        for copy in [flux_copy, diff_copy] + x_copies + table_copies:
            copy.start()
        first = col_group * channels
        flux_copy.wait()
        weight = channel_column(flux_ref[...], channels, first)
        diff_copy.wait()
        diff = channel_column(diff_ref[...], channels, first)
        total = rows * groups_x
        base = (row_group * rows).astype(f32)
        tiles = wave_parts(columns)
        for k, (group, n, _) in enumerate(tiles):
            lam, alpha, _ = decay_terms(diff, half_rates(group, n, LANES, columns))
            factor_ref[k, 0] = lam
            lows, highs = edge_factors(lam, alpha, base, total, rows)
            for r in range(rows):
                factor_ref[k, 1 + r] = lows[r]
                factor_ref[k, 1 + rows + r] = highs[r]
        for r in range(rows):
            x_copies[r].wait()
            row_ref[r : r + 1, :] = jnp.sum(x_ref[r] * weight, axis=0, keepdims=True)
            fold(x_ref[r], flat_ref, r)
        send_surface()
        for k in range(2):
            table_copies[k].wait()
            lanes = slice(k * half, (k + 1) * half)
            part = jnp.dot(
                flat_ref[:, lanes], table_ref[lanes, :], preferred_element_type=f32
            )
            for tile, (group, _, parts) in enumerate(tiles):
                if group != k:
                    continue
                lam = factor_ref[tile, 0]
                for at in parts:
                    lanes = slice(at, at + LANES)
                    here = slice(at - k * half, at - k * half + LANES)
                    p = factor_ref[tile, 1] * part[0:channels, here]
                    q = factor_ref[tile, 2 * rows] * part[(rows - 1) * channels :, here]
                    for r in range(1, rows):
                        up = part[r * channels : (r + 1) * channels, here]
                        down = part[(rows - 1 - r) * channels : (rows - r) * channels, here]
                        p = lam * p + factor_ref[tile, 1 + r] * up
                        q = lam * q + factor_ref[tile, 2 * rows - r] * down
                    if paired:
                        for mask, out in ((1, e1_ref), (2, e2_ref), (3, e3_ref)):
                            upward = row_group < (row_group ^ mask)
                            out[0:channels, lanes] = jnp.where(upward, p, q).astype(bf16)
                    else:
                        pq_ref[0, :, lanes] = p.astype(bf16)
                        pq_ref[1, :, lanes] = q.astype(bf16)
        sums_copies = [
            pltpu.make_async_copy(
                message_ref[k].at[pl.ds(0, channels)],
                message_hbm[k].at[pl.ds(0, channels)],
                out_sem.at[2 + k],
            )
            for k in range(3)
        ]
        if not paired:
            sums_copies = message_copies[4:]
        for copy in sums_copies:
            copy.start()
        for copy in surface_copies + sums_copies:
            copy.wait()

    @pl.when(jnp.logical_not(is_atmos))
    def _():
        wet_copy = pltpu.make_async_copy(wet_hbm, wet_ref, sem.at[0])
        for copy in x_copies + [wet_copy]:
            copy.start()
        gain = jnp.where(col_group == 0, 1.0, 0.0)
        for r in range(rows):
            x_copies[r].wait()
            row_ref[r : r + 1, :] = x_ref[r, 0:1, :] * gain
        send_surface()
        wet_copy.wait()
        levels = channels // 2
        lines = 2 * channels
        even_x = row_group % 2 == 0
        even_y = col_group % 2 == 0
        wet = wet_ref[...].astype(f32)
        wet = jnp.concatenate([wet, wet], axis=0).astype(bf16)

        def put(out, last):
            @pl.when(last)
            def _():
                out[0:lines, :] = x_ref[rows - 2 :].reshape(lines, columns).astype(bf16)

            @pl.when(jnp.logical_not(last))
            def _():
                out[0:lines, :] = x_ref[:2].reshape(lines, columns).astype(bf16)

            out[lines : lines + 16, :] = wet

        put(e1_ref, even_x)
        put(e3_ref, jnp.logical_not(even_x))

        def put_edges(out, level):
            for r in range(rows):
                for t in range(2):
                    at = (r * 2 + t) * 2
                    c = t * levels + level
                    edge_ref[at : at + 2, :] = x_ref[r, c : c + 2, :]
            out[0 : rows * 4, :] = edge_ref[...].astype(bf16)

        @pl.when(even_y)
        def _():
            put_edges(e2_ref, levels - 2)
            put_edges(e4_ref, 0)

        @pl.when(jnp.logical_not(even_y))
        def _():
            put_edges(e2_ref, 0)
            put_edges(e4_ref, levels - 2)

        for copy in message_copies:
            copy.start()
        for copy in surface_copies + message_copies:
            copy.wait()


def one_hot_kernel(
    rows, columns, a_src, a_dst, a_count, m_src, m_dst, m_count, src_hot_ref, dst_hot_ref,
    src_row_ref, dst_mask_ref, used_ref,
):
    is_atmos = lax.axis_index("comp") == 0
    blocks, points = src_row_ref.shape
    count = jnp.where(is_atmos, m_count[0, 0], a_count[0, 0])
    block_iota = lax.broadcasted_iota(jnp.int32, (blocks, points), 0)
    used_ref[...] = jnp.where(block_iota < count, 1, 0)
    lane_iota = lax.broadcasted_iota(jnp.int32, (LANES, points), 0)
    cells = dst_mask_ref.shape[0]
    row_iota = lax.broadcasted_iota(jnp.int32, (cells, points), 0)
    for a_ref, m_ref, hot_ref in ((a_src, m_src, src_hot_ref), (a_dst, m_dst, dst_hot_ref)):
        index = jnp.where(is_atmos, m_ref[0, 0], a_ref[0, 0])
        tile = (index // LANES) % (columns // LANES)
        row = tile * rows + index // columns
        if hot_ref is src_hot_ref:
            src_row_ref[...] = row
        lane = index % LANES
        for b in range(blocks):
            at = slice(b * points, (b + 1) * points)
            hot_ref[:, at] = jnp.where(lane_iota == lane[b : b + 1], 1.0, 0.0).astype(bf16)
            if hot_ref is dst_hot_ref:
                dst_mask_ref[:, at] = jnp.where(row_iota == row[b : b + 1], 1.0, 0.0).astype(bf16)


def regrid_kernel(n_surfaces, *refs):
    surfaces = refs[:n_surfaces]
    (
        src_hot_ref, dst_hot_ref, src_row_ref, dst_mask_ref, used_ref, a_weight, m_weight,
        _,
        *refs,
    ) = refs[n_surfaces:]
    land_ref, *sent_refs = refs[:-4]
    weight_ref, gath_ref, val_ref, sem = refs[-4:]
    is_atmos = lax.axis_index("comp") == 0
    blocks, points = val_ref.shape
    cells = surfaces[0].shape[0]

    @pl.when(is_atmos)
    def _():
        pltpu.make_async_copy(m_weight.at[0, 0], weight_ref, sem).start()

    @pl.when(jnp.logical_not(is_atmos))
    def _():
        pltpu.make_async_copy(a_weight.at[0, 0], weight_ref, sem).start()

    pair = 2 * points
    row_iota = lax.broadcasted_iota(jnp.int32, (cells, points), 0)
    table = sum(surface[...].astype(f32) for surface in surfaces).astype(bf16)
    for b in range(0, blocks, 2):
        picked = jnp.dot(
            table, src_hot_ref[:, b * points : b * points + pair], preferred_element_type=f32
        )
        for k in range(2):
            mine = row_iota == src_row_ref[b + k : b + k + 1, :]
            part = jnp.where(mine, picked[:, k * points : (k + 1) * points], 0.0)
            gath_ref[b + k : b + k + 1, :] = jnp.sum(part, axis=0, keepdims=True)
    gathered = gath_ref[...].astype(bf16)

    @pl.when(is_atmos)
    def _():
        pltpu.make_async_copy(m_weight.at[0, 0], weight_ref, sem).wait()

    @pl.when(jnp.logical_not(is_atmos))
    def _():
        pltpu.make_async_copy(a_weight.at[0, 0], weight_ref, sem).wait()

    block_iota = lax.broadcasted_iota(jnp.int32, (blocks, points), 0)
    values = jnp.zeros((blocks, points), f32)
    for b in range(0, blocks, 2):
        terms = lax.dot_general(
            gathered,
            weight_ref[b : b + 2].reshape(pair, points),
            (((1,), (1,)), ((), ())),
            preferred_element_type=f32,
        )
        for k in range(2):
            values = jnp.where(block_iota == b + k, terms[:, k * points : (k + 1) * points], values)
    val_ref[...] = jnp.where(used_ref[...] > 0, values, 0.0)
    land = jnp.zeros((2 * cells, LANES), f32)
    for b in range(0, blocks, 2):
        spread = []
        for k in range(b, b + 2):
            value = val_ref[k : k + 1, :]
            coarse = value.astype(bf16)
            fine = (value - coarse.astype(f32)).astype(bf16)
            mine = dst_mask_ref[:, k * points : (k + 1) * points]
            spread.append(jnp.concatenate([mine * coarse, mine * fine], axis=0))
        land = land + lax.dot_general(
            jnp.concatenate(spread, axis=1),
            dst_hot_ref[:, b * points : b * points + pair],
            (((1,), (1,)), ((), ())),
            preferred_element_type=f32,
        )
    land = land[:cells] + land[cells:]
    land_ref[...] = land
    for sent_ref in sent_refs:
        lengthen(sent_ref, land.astype(bf16))


def heat_kernel(rows, e2_ref, e4_ref, land_ref, _, *refs):
    parts = refs[:-3]
    sum_ref, near_ref, far_ref = refs[-3:]
    cells = land_ref.shape[0]
    columns = cells // rows * LANES
    even_x = lax.axis_index("gx") % 2 == 0
    even_y = lax.axis_index("gy") % 2 == 0
    total = land_ref[...]
    for part in parts:
        total = total + part[0:cells, :].astype(f32)
    sum_ref[...] = total

    def corners(row):
        start = row * 4 // 16 * 16
        one = e2_ref[start : start + 16, :].astype(f32)
        two = e4_ref[start : start + 16, :].astype(f32)
        low = jnp.where(even_y, two, one)
        high = jnp.where(even_y, one, two)
        at = row * 4 - start
        lines = [low[at + 1 : at + 2], low[at + 3 : at + 4], high[at : at + 1], high[at + 2 : at + 3]]
        heat = from_tiles(total, rows)[row : row + 1]
        blank = jnp.zeros((3, columns), f32)
        return to_tiles(jnp.concatenate([heat] + lines + [blank], axis=0))

    first, last = corners(0), corners(rows - 1)
    near_ref[...] = jnp.where(even_x, last, first).astype(bf16)
    far_ref[...] = jnp.where(even_x, first, last).astype(bf16)


def advance(ref, r, t, coefs, size):
    ring, columns = ref.shape[2:]
    whole = ref[r, t]
    up = pltpu.roll(whole, 1, 0)[:size]
    down = pltpu.roll(whole, ring - 1, 0)[:size]
    mid = whole[:size]
    total = coefs[0] * mid + coefs[5] * (up + down)
    total = total + coefs[1] * ref[r - 1, t, 0:size, :]
    total = total + coefs[2] * ref[r + 1, t, 0:size, :]
    total = total + coefs[3] * pltpu.roll(mid, 1, 1)
    return total + coefs[4] * pltpu.roll(mid, columns - 1, 1)


def first_step_kernel(
    groups_x, groups_y, paired, x_ref, wet_ref, diff_ref, table_ref, e1_ref, e3_ref,
    e2_ref, e4_ref, *refs,
):
    if not paired:
        pin_ref, qin_ref = refs[:2]
    zb_ref, c_ref, t1_ref, y_ref, flat_ref, z_ref, t0_ref, w_ref = refs[-8:]
    _, rows, channels, columns = x_ref.shape
    row_group = lax.axis_index("gx")
    col_group = lax.axis_index("gy")
    is_atmos = lax.axis_index("comp") == 0

    @pl.when(is_atmos)
    def _():
        half = columns // 2
        for r in range(rows):
            fold(x_ref[0, r], flat_ref, r)
        for k in range(2):
            lanes = slice(k * half, (k + 1) * half)
            part = jnp.dot(
                flat_ref[:, lanes], table_ref[lanes, :], preferred_element_type=f32
            )
            y_ref[:, :, lanes] = part.reshape(rows, channels, half)
        diff = channel_column(diff_ref[...], channels, col_group * channels)
        total = rows * groups_x
        base = (row_group * rows).astype(f32)
        for group, n, parts in wave_parts(columns):
            lam, alpha, sinh = decay_terms(diff, half_rates(group, n, LANES, columns))
            scale = 1.0 / (
                2.0 * diff * sinh * (1.0 - jnp.exp(-2.0 * (total + 1) * alpha))
            )
            lows, highs = edge_factors(lam, alpha, base, total, rows)
            for part in parts:
                lanes = slice(part, part + LANES)
                if paired:
                    pin = jnp.zeros((channels, LANES), f32)
                    qin = jnp.zeros((channels, LANES), f32)
                    for mask, msg in ((1, e1_ref), (2, e2_ref), (3, e3_ref)):
                        band = row_group ^ mask
                        gap = (jnp.abs(row_group - band) - 1) * rows
                        term = jnp.exp(-gap.astype(f32) * alpha)
                        term = term * msg[0:channels, lanes].astype(f32)
                        pin = pin + jnp.where(band < row_group, term, 0.0)
                        qin = qin + jnp.where(band > row_group, term, 0.0)
                else:
                    pin = pin_ref[:, lanes]
                    qin = qin_ref[:, lanes]
                f = pin
                for r in range(rows):
                    f = lam * f + lows[r] * y_ref[r, :, lanes]
                    z_ref[r] = highs[r] * f
                g = lam * qin
                for r in reversed(range(rows)):
                    z = scale * (z_ref[r] + lows[r] * g)
                    zb_ref[r * channels : (r + 1) * channels, lanes] = z.astype(bf16)
                    g = lam * (g + highs[r] * y_ref[r, :, lanes])

    @pl.when(jnp.logical_not(is_atmos))
    def _():
        levels = channels // 2
        ring = levels + 8
        lines = 2 * channels
        first_x = row_group == 0
        last_x = row_group == groups_x - 1
        top = col_group == 0
        bottom = col_group == groups_y - 1
        even_x = row_group % 2 == 0
        even_y = col_group % 2 == 0

        one = e1_ref[lines : lines + 16, :].astype(f32)
        three = e3_ref[lines : lines + 16, :].astype(f32)
        below = jnp.where(even_x, three, one)[rows - 2 : rows]
        above = jnp.where(even_x, one, three)[0:2]
        w_ref[0:2, :] = jnp.where(first_x, 0.0, below)
        w_ref[2 : rows + 2, :] = wet_ref[...].astype(f32)
        w_ref[rows + 2 : rows + 4, :] = jnp.where(last_x, 0.0, above)

        span = rows + 2
        north = w_ref[0:span, :]
        here = w_ref[1 : span + 1, :]
        south = w_ref[2 : span + 2, :]
        west = pltpu.roll(here, 1, 1)
        east = pltpu.roll(here, columns - 1, 1)
        c_ref[0, 0:span, :] = here * (
            1.0 - 2.0 * mixing_rate - spread_rate * (north + south + west + east)
        )
        c_ref[1, 0:span, :] = spread_rate * here * north
        c_ref[2, 0:span, :] = spread_rate * here * south
        c_ref[3, 0:span, :] = spread_rate * here * west
        c_ref[4, 0:span, :] = spread_rate * here * east
        c_ref[5, 0:span, :] = mixing_rate * here
        c_ref[6, 0:span, :] = here

        one = e1_ref[0:lines, :].astype(f32)
        three = e3_ref[0:lines, :].astype(f32)
        below = jnp.where(even_x, three, one)
        above = jnp.where(even_x, one, three)
        blank = jnp.zeros((8, columns), f32)
        for k in range(2):
            for t in range(2):
                c = k * channels + t * levels
                t0_ref[k, t, 0:levels, :] = below[c : c + levels]
                t0_ref[rows + 2 + k, t, 0:levels, :] = above[c : c + levels]
                t0_ref[k, t, levels:ring, :] = blank
                t0_ref[rows + 2 + k, t, levels:ring, :] = blank
        one = e2_ref[...].astype(f32)
        two = e4_ref[0 : 4 * rows, :].astype(f32)
        before = jnp.where(even_y, two, one)
        after = jnp.where(even_y, one, two)
        for r in range(rows):
            for t in range(2):
                k = (r * 2 + t) * 2
                t0_ref[r + 2, t, 0:levels, :] = x_ref[0, r, t * levels : (t + 1) * levels, :]
                t0_ref[r + 2, t, levels : levels + 2, :] = after[k : k + 2]
                t0_ref[r + 2, t, ring - 2 : ring, :] = before[k : k + 2]

        def close(ref, r):
            for t in range(2):
                ref[r, t, ring - 1 : ring, :] = jnp.where(
                    top, ref[r, t, 0:1, :], ref[r, t, ring - 1 : ring, :]
                )
                ref[r, t, levels : levels + 1, :] = jnp.where(
                    bottom, ref[r, t, levels - 1 : levels, :], ref[r, t, levels : levels + 1, :]
                )

        def first(r, carry):
            coefs = [c_ref[k, pl.ds(r, 1), :] for k in range(6)]
            close(t0_ref, r + 1)
            for t in range(2):
                t1_ref[r, t] = advance(t0_ref, r + 1, t, coefs, ring)
            close(t1_ref, r)
            return carry

        lax.fori_loop(0, span, first, 0)


def second_step_kernel(gain_ref, table_ref, zb_ref, c_ref, t1_ref, sum_ref, base_ref):
    rows, channels, columns = base_ref.shape
    is_atmos = lax.axis_index("comp") == 0

    @pl.when(is_atmos)
    def _():
        response = channel_column(gain_ref[...], channels, lax.axis_index("gy") * channels)
        forcing = from_tiles(sum_ref[...], rows)
        half = columns // 2
        step = 256
        for n in range(0, half, step):
            even, odd = [
                jnp.dot(
                    zb_ref[:, k * half : (k + 1) * half],
                    table_ref[k * half : (k + 1) * half, n : n + step],
                    preferred_element_type=f32,
                ).reshape(rows, channels, step)
                for k in range(2)
            ]
            for r in range(rows):
                for lane, part in ((n, even[r] + odd[r]), (n + half, even[r] - odd[r])):
                    lanes = slice(lane, lane + step)
                    base_ref[r, :, lanes] = part + response * forcing[r : r + 1, lanes]

    @pl.when(jnp.logical_not(is_atmos))
    def _():
        levels = channels // 2

        def second(r, carry):
            coefs = [c_ref[k, pl.ds(r, 1), :] for k in range(6)]
            for t in range(2):
                c = t * levels
                base_ref[r - 1, c : c + levels, :] = advance(t1_ref, r, t, coefs, levels)
            return carry

        lax.fori_loop(1, rows + 1, second, 0)


def last_kernel(
    groups_x, groups_y, base_ref, c_ref, sum_ref, near_ref, far_ref, out_hbm,
    out_ref, e_ref, heat_ref, sem,
):
    rows, channels, columns = out_ref.shape
    row_group = lax.axis_index("gx")
    col_group = lax.axis_index("gy")
    is_atmos = lax.axis_index("comp") == 0
    copies = [
        pltpu.make_async_copy(out_ref.at[r], out_hbm.at[0, r], sem.at[r]) for r in range(rows)
    ]
    as_they_are = [
        pltpu.make_async_copy(base_ref.at[r], out_hbm.at[0, r], sem.at[r]) for r in range(rows)
    ]

    @pl.when(is_atmos)
    def _():
        for copy in as_they_are:
            copy.start()

    @pl.when(jnp.logical_and(jnp.logical_not(is_atmos), col_group > 0))
    def _():
        for copy in as_they_are[1:-1]:
            copy.start()

    @pl.when(jnp.logical_not(is_atmos))
    def _():
        levels = channels // 2
        even = row_group % 2 == 0
        below = jnp.where(even, far_ref[...].astype(f32), near_ref[...].astype(f32))
        above = jnp.where(even, near_ref[...].astype(f32), far_ref[...].astype(f32))

        low = from_tiles(below, 8)
        high = from_tiles(above, 8)
        by_low = c_ref[1, 1:2, :] * (c_ref[5, 0:1, :] + c_ref[5, 1:2, :])
        by_high = c_ref[2, rows : rows + 1, :] * (
            c_ref[5, rows : rows + 1, :] + c_ref[5, rows + 1 : rows + 2, :]
        )
        has_before = jnp.where(col_group > 0, 1.0, 0.0)
        has_after = jnp.where(col_group < groups_y - 1, 1.0, 0.0)

        @pl.when(col_group == 0)
        def _():
            span = rows + 2
            e_ref[0:1, :] = low[0:1]
            e_ref[1 : rows + 1, :] = from_tiles(sum_ref[...], rows)
            e_ref[rows + 1 : span, :] = high[0:1]
            e_ref[0:span, :] = c_ref[6, 0:span, :] * e_ref[0:span, :]
            own = slice(1, rows + 1)
            heat = e_ref[own, :]
            second = c_ref[5, own, :] * heat
            first = (c_ref[0, own, :] + 1.0) * heat + second
            first = first + c_ref[1, own, :] * e_ref[0:rows, :]
            first = first + c_ref[2, own, :] * e_ref[2 : rows + 2, :]
            first = first + c_ref[3, own, :] * pltpu.roll(heat, 1, 1)
            first = first + c_ref[4, own, :] * pltpu.roll(heat, columns - 1, 1)
            heat_ref[0] = first
            heat_ref[1] = second

        for r in (0, rows - 1):
            out_ref[r] = base_ref[r]
        for t in range(2):
            c = t * levels
            d = c + levels - 1
            for r, factor, lines in ((0, by_low, low), (rows - 1, by_high, high)):
                out_ref[r, c : c + 1, :] = out_ref[r, c : c + 1, :] + (
                    has_before * factor * lines[t + 1 : t + 2]
                )
                out_ref[r, d : d + 1, :] = out_ref[r, d : d + 1, :] + (
                    has_after * factor * lines[t + 3 : t + 4]
                )

        @pl.when(col_group == 0)
        def _():
            for r in range(rows):
                if r not in (0, rows - 1):
                    out_ref[r] = base_ref[r]
                for t, gain in enumerate((heat_gain, salt_gain)):
                    c = t * levels
                    for k in range(2):
                        out_ref[r, c + k : c + k + 1, :] = (
                            out_ref[r, c + k : c + k + 1, :] + gain * heat_ref[k, r : r + 1, :]
                        )
                copies[r].start()

        @pl.when(col_group > 0)
        def _():
            copies[0].start()
            copies[-1].start()

    for copy in copies:
        copy.wait()


def local(
    fields,
    wet_cells,
    flux_weight,
    variable_sea_response,
    diffusivity,
    a2o_source,
    a2o_target,
    a2o_count,
    a2o_weight,
    marine_air_input_index,
    marine_air_output_index,
    marine_air_piece_tally,
    marine_air_piece_factor,
):
    _, rows, channels, columns = fields.shape
    groups_x = lax.axis_size("gx")
    groups_y = lax.axis_size("gy")
    blocks, points = a2o_source.shape[2:]
    cells = rows * columns // LANES
    forward, inverse = fourier_tables(columns)
    flux_row = flux_weight[None, :]
    gain_row = variable_sea_response[None, :]
    diff_row = diffusivity[None, :]
    paired = groups_x == 4
    params = functools.partial(pltpu.CompilerParams, vmem_limit_bytes=40 * 2**20)
    vmem = pl.BlockSpec(memory_space=pltpu.VMEM)
    smem = pl.BlockSpec(memory_space=pltpu.SMEM)
    hbm = pl.BlockSpec(memory_space=pltpu.HBM)
    anywhere = pl.BlockSpec(memory_space=pl.ANY)

    def shape(dims, dtype):
        return jax.ShapeDtypeStruct(dims, dtype)

    lines = 2 * channels + 16
    shapes = [
        shape((cells, LANES), bf16),
        shape((cells + 16, LANES), bf16),
        shape((lines, columns), bf16),
        shape((lines, columns), bf16),
        shape((4 * rows, columns), bf16),
        shape((4 * rows, columns), bf16),
    ]
    if not paired:
        shapes.append(shape((2, channels, columns), bf16))
    coarse, wide, e1, e3, e2, e4, *sums = pl.pallas_call(
        functools.partial(start_kernel, groups_x, paired),
        out_shape=shapes,
        in_specs=[hbm] * 5,
        out_specs=[hbm] * len(shapes),
        scratch_shapes=[pltpu.VMEM(out.shape, out.dtype) for out in shapes]
        + [
            pltpu.VMEM((rows, channels, columns), f32),
            pltpu.VMEM((rows, columns), jnp.int32),
            pltpu.VMEM(flux_row.shape, f32),
            pltpu.VMEM(diff_row.shape, f32),
            pltpu.VMEM(forward.shape, bf16),
            pltpu.VMEM((rows * channels, columns), bf16),
            pltpu.VMEM((rows, columns), f32),
            pltpu.VMEM((4 * rows, columns), f32),
            pltpu.VMEM((columns // 2 // LANES, 2 * rows + 1, channels, LANES), f32),
            pltpu.SemaphoreType.DMA((rows,)),
            pltpu.SemaphoreType.DMA((4,)),
            pltpu.SemaphoreType.DMA((len(shapes),)),
        ],
        compiler_params=pltpu.CompilerParams(vmem_limit_bytes=58 * 2**20),
        name="surface_and_forward_or_halos",
    )(fields, wet_cells, flux_row, diff_row, forward)

    one_hots = pl.pallas_call(
        functools.partial(one_hot_kernel, rows, columns),
        out_shape=[
            shape((LANES, blocks * points), bf16),
            shape((LANES, blocks * points), bf16),
            shape((blocks, points), jnp.int32),
            shape((cells, blocks * points), bf16),
            shape((blocks, points), jnp.int32),
        ],
        in_specs=[vmem, vmem, smem] * 2,
        out_specs=[vmem] * 5,
        compiler_params=params(),
        name="one_hots",
    )(
        a2o_source, a2o_target, a2o_count,
        marine_air_input_index, marine_air_output_index, marine_air_piece_tally,
    )

    masks = [1 << bit for bit in range(groups_y.bit_length() - 1)]

    def sum_route(mask):
        return [(j, j ^ mask) for j in range(groups_y)]

    def partner_route(mask):
        return both_ways([(j, groups_y + (j ^ mask)) for j in range(groups_y)])

    surface = lax.ppermute(coarse, ("comp", "gy"), partner_route(0)).astype(f32)
    for mask in masks[:1]:
        far = lax.ppermute(wide, ("comp", "gy"), partner_route(mask))
        surface = surface + far[:cells].astype(f32)
    coarse = surface.astype(bf16)
    *one_hots, used = one_hots
    coarse, used = lax.optimization_barrier((coarse, used))
    for mask in masks[1:-1]:
        surface = surface + lax.ppermute(coarse, "gy", sum_route(mask)).astype(f32)
        coarse = surface.astype(bf16)
    surfaces = [surface] + [
        lax.ppermute(coarse, "gy", sum_route(mask)) for mask in masks[1:][-1:]
    ]

    def ring_pairs(count, odd):
        return [(a, (a + 1) % count) for a in range(odd, count, 2)]

    def flat(comp, i, j):
        return (comp * groups_x + i) * groups_y + j

    def level_route(odd):
        pairs = []
        for i in range(groups_x):
            linked = [(a, a + 1) for a in range(odd, groups_y - 1, 2)]
            alone = set(range(groups_y)) - {j for pair in linked for j in pair}
            pairs += [(flat(1, i, a), flat(1, i, b)) for a, b in linked]
            if i % 2 == 0:
                pairs += [(flat(1, i, j), flat(1, i + 1, j)) for j in sorted(alone)]
                if odd or not paired:
                    pairs += [(flat(0, i, j), flat(0, i + 1, j)) for j in range(groups_y)]
            if paired and not odd and i < i ^ 2:
                pairs += [(flat(0, i, j), flat(0, i ^ 2, j)) for j in range(groups_y)]
        return both_ways(pairs)

    e1 = lax.ppermute(e1, "gx", both_ways(ring_pairs(groups_x, 0)))
    e3 = lax.ppermute(e3, "gx", both_ways(ring_pairs(groups_x, 1)))
    axes = ("comp", "gx", "gy")
    e2 = lax.ppermute(e2, axes, level_route(0))
    e4 = lax.ppermute(e4, axes, level_route(1))

    landing, *sent = pl.pallas_call(
        functools.partial(regrid_kernel, len(surfaces)),
        out_shape=[shape((cells, LANES), f32)]
        + [shape((cells + 16 * (mask - 1), LANES), bf16) for mask in range(1, groups_y)],
        in_specs=[vmem] * (len(surfaces) + 5) + [hbm, hbm] + [anywhere] * 1,
        out_specs=[vmem] * groups_y,
        scratch_shapes=[
            pltpu.VMEM((blocks, points, points), bf16),
            pltpu.VMEM((blocks, points), f32),
            pltpu.VMEM((blocks, points), f32),
            pltpu.SemaphoreType.DMA,
        ],
        compiler_params=params(),
        cost_estimate=pl.CostEstimate(flops=2_200_000_000, bytes_accessed=0, transcendentals=0),
        name="regrid_blocks",
    )(
        *surfaces, *one_hots, used, a2o_weight, marine_air_piece_factor, e3,
    )

    def landing_route(mask):
        pairs = [
            (flat(0, i, j), flat(0, i, j ^ mask))
            for i in range(groups_x)
            for j in range(groups_y)
            if j < j ^ mask
        ]
        pairs += [(flat(1, i, 0), flat(1, i, mask)) for i in range(groups_x)]
        pairs += [
            (flat(1, i, j), flat(1, i + 1, j))
            for i in range(0, groups_x, 2)
            for j in range(groups_y)
            if j not in (0, mask)
        ]
        return both_ways(pairs)

    parts = [
        lax.ppermute(block, axes, landing_route(mask)) for mask, block in enumerate(sent, 1)
    ]

    extra = []
    if not paired:
        p, q = jnp.moveaxis(lax.all_gather(sums[0], "gx").astype(f32), 1, 0)
        viscous = lax.dynamic_slice_in_dim(
            diffusivity, lax.axis_index("gy") * channels, channels
        )[:, None]
        rates = [half_rates(g, 0, columns // 4, columns) for g in (0, 0, 1, 1)]
        _, alpha, _ = decay_terms(viscous, jnp.concatenate(rates, axis=1))
        gap = lax.axis_index("gx") - jnp.arange(groups_x)
        decay = jnp.exp(
            -(rows * jnp.maximum(jnp.abs(gap) - 1, 0))[:, None, None] * alpha[None]
        )
        extra = [
            jnp.sum(jnp.where((gap > 0)[:, None, None], decay * p, 0.0), axis=0),
            jnp.sum(jnp.where((gap < 0)[:, None, None], decay * q, 0.0), axis=0),
        ]
    ring = channels // 2 + 8
    damped, coefs, stepped = pl.pallas_call(
        functools.partial(first_step_kernel, groups_x, groups_y, paired),
        out_shape=[
            shape((rows * channels, columns), bf16),
            shape((7, 16, columns), f32),
            shape((rows + 2, 2, ring, columns), f32),
        ],
        in_specs=[vmem] * (8 + len(extra)),
        out_specs=[vmem] * 3,
        scratch_shapes=[
            pltpu.VMEM((rows, channels, columns), f32),
            pltpu.VMEM((rows * channels, columns), bf16),
            pltpu.VMEM((rows, channels, LANES), f32),
            pltpu.VMEM((rows + 4, 2, ring, columns), f32),
            pltpu.VMEM((16, columns), f32),
        ],
        compiler_params=params(),
        name="damping_or_first_step",
    )(fields, wet_cells, diff_row, forward, e1, e3, e2, e4, *extra)

    surface_sum, near, far = pl.pallas_call(
        functools.partial(heat_kernel, rows),
        out_shape=[
            shape((cells, LANES), f32),
            shape((columns // 16, LANES), bf16),
            shape((columns // 16, LANES), bf16),
        ],
        in_specs=[vmem] * 3 + [anywhere] + [vmem] * len(parts),
        out_specs=[vmem] * 3,
        compiler_params=params(),
        name="surface_sum",
    )(e2, e4, landing, coefs, *parts)

    near = lax.ppermute(near, "gx", both_ways(ring_pairs(groups_x, 0)))
    far = lax.ppermute(far, "gx", both_ways(ring_pairs(groups_x, 1)))
    base = pl.pallas_call(
        second_step_kernel,
        out_shape=shape((rows, channels, columns), f32),
        in_specs=[vmem] * 6,
        out_specs=vmem,
        compiler_params=params(),
        name="inverse_or_second_step",
    )(gain_row, inverse, damped, coefs, stepped, surface_sum)
    return pl.pallas_call(
        functools.partial(last_kernel, groups_x, groups_y),
        out_shape=shape(fields.shape, f32),
        in_specs=[vmem] * 5,
        out_specs=hbm,
        scratch_shapes=[
            pltpu.VMEM((rows, channels, columns), f32),
            pltpu.VMEM((16, columns), f32),
            pltpu.VMEM((2, rows, columns), f32),
            pltpu.SemaphoreType.DMA((rows,)),
        ],
        compiler_params=params(),
        name="add_surface_terms",
    )(base, coefs, surface_sum, near, far)


def solution(mesh):
    in_specs = (
        P("comp", "gx", "gy", None),
        P("gx", None),
        P(),
        P(),
        P(),
        P("gx", "gy", None, None),
        P("gx", "gy", None, None),
        P("gx", "gy"),
        P("gx", "gy", None, None, None),
        P("gx", "gy", None, None),
        P("gx", "gy", None, None),
        P("gx", "gy"),
        P("gx", "gy", None, None, None),
    )
    out_specs = P("comp", "gx", "gy", None)
    return jax.shard_map(local, mesh=mesh, in_specs=in_specs, out_specs=out_specs, check_vma=False)
```

```python
import functools

import jax
import jax.numpy as jnp
import numpy as np
from jax import lax
from jax.experimental import pallas as pl
from jax.experimental.pallas import tpu as pltpu
from jax.sharding import PartitionSpec as P

spread_rate = 0.2
mixing_rate = 0.1
heat_gain = 0.5
salt_gain = -0.25
LANES = 128
f32 = jnp.float32
bf16 = jnp.bfloat16


def fourier_tables(columns):
    half = columns // 2
    forward, inverse = [], []
    for first in (0, 1):
        waves = np.arange(first, half, 2)
        phase = np.arange(half)[:, None] * waves[None, :] % columns
        angles = phase * (2.0 * np.pi / columns)
        table = np.concatenate([np.cos(angles), np.sin(angles)], axis=1)
        weight = np.where(waves == 0, 1.0, 2.0) / columns
        forward.append(table)
        inverse.append(table.T * np.concatenate([weight, weight])[:, None])
    return (
        jnp.asarray(np.concatenate(forward).astype(np.float32), bf16),
        jnp.asarray(np.concatenate(inverse).astype(np.float32), bf16),
    )


def wave_parts(columns):
    quarter = columns // 4
    return [
        (g, n, (g * 2 * quarter + n, (g * 2 + 1) * quarter + n))
        for g in (0, 1)
        for n in range(0, quarter, LANES)
    ]


def half_rates(group, first, count, columns):
    lane = lax.broadcasted_iota(jnp.int32, (1, count), 1) + first
    wave = (2 * lane + group).astype(f32)
    sine = jnp.sin(wave * (np.pi / columns))
    return 2.0 * sine * sine


def both_ways(pairs):
    return [p for a, b in pairs for p in ((a, b), (b, a))]


def channel_column(row, channels, first):
    n = row.shape[1]
    lane = lax.broadcasted_iota(jnp.int32, (channels, n), 1)
    sub = lax.broadcasted_iota(jnp.int32, (channels, n), 0)
    return jnp.sum(jnp.where(lane == sub + first, row, 0.0), axis=1, keepdims=True)


def to_tiles(surface):
    cols = surface.shape[1]
    return jnp.concatenate(
        [surface[:, k : k + LANES] for k in range(0, cols, LANES)], axis=0
    )


def from_tiles(tiles, rows):
    return jnp.concatenate(
        [tiles[k : k + rows] for k in range(0, tiles.shape[0], rows)], axis=1
    )


def lengthen(ref, block):
    rows = block.shape[0]
    ref[0:rows, :] = block
    if ref.shape[0] > rows:
        ref[rows:, :] = block[: ref.shape[0] - rows]


def decay_terms(diff_column, rates):
    half = 0.5 / diff_column + rates
    sinh = jnp.sqrt(half * (half + 2.0))
    grow = 1.0 + half + sinh
    return 1.0 / grow, jnp.log(grow), sinh


def edge_factors(lam, alpha, base, total, rows):
    lam2 = lam * lam
    powers = [
        jnp.exp(-2.0 * base * alpha) * lam2,
        jnp.exp(-2.0 * (total - rows - base) * alpha) * lam2,
    ]
    lows, highs = [], []
    for _ in range(rows):
        lows.append(1.0 - powers[0])
        highs.insert(0, 1.0 - powers[1])
        powers = [power * lam2 for power in powers]
    return lows, highs


def fold(values, flat_ref, r):
    channels, columns = values.shape
    half = columns // 2
    left, right = values[:, :half], values[:, half:]
    flat_ref[r * channels : (r + 1) * channels, :half] = (left + right).astype(bf16)
    flat_ref[r * channels : (r + 1) * channels, half:] = (left - right).astype(bf16)


def start_kernel(
    groups_x, paired, x_hbm, wet_hbm, flux_hbm, diff_hbm, table_hbm, *refs
):
    outs = 6 if paired else 7
    coarse_hbm, wide_hbm, *message_hbm = refs[:outs]
    coarse_ref, wide_ref, *message_ref = refs[outs : 2 * outs]
    e1_ref, e3_ref, e2_ref, e4_ref = message_ref[:4]
    if not paired:
        pq_ref = message_ref[4]
    (
        x_ref, wet_ref, flux_ref, diff_ref, table_ref, flat_ref, row_ref, edge_ref,
        factor_ref, x_sem, sem, out_sem,
    ) = refs[2 * outs :]
    rows, channels, columns = x_ref.shape
    half = columns // 2
    row_group = lax.axis_index("gx")
    col_group = lax.axis_index("gy")
    is_atmos = lax.axis_index("comp") == 0

    x_copies = [
        pltpu.make_async_copy(x_hbm.at[0, r], x_ref.at[r], x_sem.at[r]) for r in range(rows)
    ]
    surface_copies = [
        pltpu.make_async_copy(coarse_ref, coarse_hbm, out_sem.at[0]),
        pltpu.make_async_copy(wide_ref, wide_hbm, out_sem.at[1]),
    ]
    message_copies = [
        pltpu.make_async_copy(ref, hbm, out_sem.at[2 + k])
        for k, (ref, hbm) in enumerate(zip(message_ref, message_hbm))
    ]

    def send_surface():
        coarse = to_tiles(row_ref[...]).astype(bf16)
        coarse_ref[...] = coarse
        lengthen(wide_ref, coarse)
        for copy in surface_copies:
            copy.start()

    @pl.when(is_atmos)
    def _():
        flux_copy = pltpu.make_async_copy(flux_hbm, flux_ref, sem.at[0])
        diff_copy = pltpu.make_async_copy(diff_hbm, diff_ref, sem.at[1])
        table_copies = [
            pltpu.make_async_copy(
                table_hbm.at[pl.ds(k * half, half)], table_ref.at[pl.ds(k * half, half)], sem.at[2 + k]
            )
            for k in range(2)
        ]
        for copy in [flux_copy, diff_copy] + x_copies + table_copies:
            copy.start()
        first = col_group * channels
        flux_copy.wait()
        weight = channel_column(flux_ref[...], channels, first)
        diff_copy.wait()
        diff = channel_column(diff_ref[...], channels, first)
        total = rows * groups_x
        base = (row_group * rows).astype(f32)
        tiles = wave_parts(columns)
        for k, (group, n, _) in enumerate(tiles):
            lam, alpha, _ = decay_terms(diff, half_rates(group, n, LANES, columns))
            factor_ref[k, 0] = lam
            lows, highs = edge_factors(lam, alpha, base, total, rows)
            for r in range(rows):
                factor_ref[k, 1 + r] = lows[r]
                factor_ref[k, 1 + rows + r] = highs[r]
        for r in range(rows):
            x_copies[r].wait()
            row_ref[r : r + 1, :] = jnp.sum(x_ref[r] * weight, axis=0, keepdims=True)
            fold(x_ref[r], flat_ref, r)
        send_surface()
        for k in range(2):
            table_copies[k].wait()
            lanes = slice(k * half, (k + 1) * half)
            part = jnp.dot(
                flat_ref[:, lanes], table_ref[lanes, :], preferred_element_type=f32
            )
            for tile, (group, _, parts) in enumerate(tiles):
                if group != k:
                    continue
                lam = factor_ref[tile, 0]
                for at in parts:
                    lanes = slice(at, at + LANES)
                    here = slice(at - k * half, at - k * half + LANES)
                    p = factor_ref[tile, 1] * part[0:channels, here]
                    q = factor_ref[tile, 2 * rows] * part[(rows - 1) * channels :, here]
                    for r in range(1, rows):
                        up = part[r * channels : (r + 1) * channels, here]
                        down = part[(rows - 1 - r) * channels : (rows - r) * channels, here]
                        p = lam * p + factor_ref[tile, 1 + r] * up
                        q = lam * q + factor_ref[tile, 2 * rows - r] * down
                    if paired:
                        for mask, out in ((1, e1_ref), (2, e2_ref), (3, e3_ref)):
                            upward = row_group < (row_group ^ mask)
                            out[0:channels, lanes] = jnp.where(upward, p, q).astype(bf16)
                    else:
                        pq_ref[0, :, lanes] = p.astype(bf16)
                        pq_ref[1, :, lanes] = q.astype(bf16)
        sums_copies = [
            pltpu.make_async_copy(
                message_ref[k].at[pl.ds(0, channels)],
                message_hbm[k].at[pl.ds(0, channels)],
                out_sem.at[2 + k],
            )
            for k in range(3)
        ]
        if not paired:
            sums_copies = message_copies[4:]
        for copy in sums_copies:
            copy.start()
        for copy in surface_copies + sums_copies:
            copy.wait()

    @pl.when(jnp.logical_not(is_atmos))
    def _():
        wet_copy = pltpu.make_async_copy(wet_hbm, wet_ref, sem.at[0])
        for copy in x_copies + [wet_copy]:
            copy.start()
        gain = jnp.where(col_group == 0, 1.0, 0.0)
        for r in range(rows):
            x_copies[r].wait()
            row_ref[r : r + 1, :] = x_ref[r, 0:1, :] * gain
        send_surface()
        wet_copy.wait()
        levels = channels // 2
        lines = 2 * channels
        even_x = row_group % 2 == 0
        even_y = col_group % 2 == 0
        wet = wet_ref[...].astype(f32)
        wet = jnp.concatenate([wet, wet], axis=0).astype(bf16)

        def put(out, last):
            @pl.when(last)
            def _():
                out[0:lines, :] = x_ref[rows - 2 :].reshape(lines, columns).astype(bf16)

            @pl.when(jnp.logical_not(last))
            def _():
                out[0:lines, :] = x_ref[:2].reshape(lines, columns).astype(bf16)

            out[lines : lines + 16, :] = wet

        put(e1_ref, even_x)
        put(e3_ref, jnp.logical_not(even_x))

        def put_edges(out, level):
            for r in range(rows):
                for t in range(2):
                    at = (r * 2 + t) * 2
                    c = t * levels + level
                    edge_ref[at : at + 2, :] = x_ref[r, c : c + 2, :]
            out[0 : rows * 4, :] = edge_ref[...].astype(bf16)

        @pl.when(even_y)
        def _():
            put_edges(e2_ref, levels - 2)
            put_edges(e4_ref, 0)

        @pl.when(jnp.logical_not(even_y))
        def _():
            put_edges(e2_ref, 0)
            put_edges(e4_ref, levels - 2)

        for copy in message_copies:
            copy.start()
        for copy in surface_copies + message_copies:
            copy.wait()


def one_hot_kernel(
    rows, columns, a_src, a_dst, a_count, m_src, m_dst, m_count, src_hot_ref, dst_hot_ref,
    src_row_ref, dst_row_ref, used_ref,
):
    is_atmos = lax.axis_index("comp") == 0
    blocks, points = src_row_ref.shape
    count = jnp.where(is_atmos, m_count[0, 0], a_count[0, 0])
    block_iota = lax.broadcasted_iota(jnp.int32, (blocks, points), 0)
    used_ref[...] = jnp.where(block_iota < count, 1, 0)
    lane_iota = lax.broadcasted_iota(jnp.int32, (LANES, points), 0)
    for a_ref, m_ref, hot_ref, row_ref in (
        (a_src, m_src, src_hot_ref, src_row_ref),
        (a_dst, m_dst, dst_hot_ref, dst_row_ref),
    ):
        index = jnp.where(is_atmos, m_ref[0, 0], a_ref[0, 0])
        row = index // columns
        tile = (index // LANES) % (columns // LANES)
        row_ref[...] = tile * rows + row
        lane = index % LANES
        for b in range(blocks):
            hot_ref[:, b * points : (b + 1) * points] = jnp.where(
                lane_iota == lane[b : b + 1], 1.0, 0.0
            ).astype(bf16)


def regrid_kernel(n_surfaces, *refs):
    surfaces = refs[:n_surfaces]
    (
        src_hot_ref, dst_hot_ref, src_row_ref, dst_row_ref, used_ref, a_weight, m_weight,
        _,
        *refs,
    ) = refs[n_surfaces:]
    land_ref, *sent_refs = refs[:-2]
    gath_ref, val_ref = refs[-2:]
    is_atmos = lax.axis_index("comp") == 0
    blocks, points = val_ref.shape
    cells = surfaces[0].shape[0]

    pair = 2 * points
    row_iota = lax.broadcasted_iota(jnp.int32, (cells, points), 0)
    table = sum(surface[...].astype(f32) for surface in surfaces).astype(bf16)
    for b in range(0, blocks, 2):
        picked = jnp.dot(
            table, src_hot_ref[:, b * points : b * points + pair], preferred_element_type=f32
        )
        for k in range(2):
            mine = row_iota == src_row_ref[b + k : b + k + 1, :]
            part = jnp.where(mine, picked[:, k * points : (k + 1) * points], 0.0)
            gath_ref[b + k : b + k + 1, :] = jnp.sum(part, axis=0, keepdims=True)
    gathered = gath_ref[...].astype(bf16)

    def block_products(weight_ref):
        block_iota = lax.broadcasted_iota(jnp.int32, (blocks, points), 0)
        values = jnp.zeros((blocks, points), f32)
        for b in range(0, blocks, 2):
            terms = lax.dot_general(
                gathered,
                weight_ref[0, 0, b : b + 2].reshape(pair, points),
                (((1,), (1,)), ((), ())),
                preferred_element_type=f32,
            )
            for k in range(2):
                values = jnp.where(
                    block_iota == b + k, terms[:, k * points : (k + 1) * points], values
                )
        val_ref[...] = jnp.where(used_ref[...] > 0, values, 0.0)

    @pl.when(is_atmos)
    def _():
        block_products(m_weight)

    @pl.when(jnp.logical_not(is_atmos))
    def _():
        block_products(a_weight)

    land = jnp.zeros((2 * cells, LANES), f32)
    for b in range(0, blocks, 2):
        spread = []
        for k in range(b, b + 2):
            value = val_ref[k : k + 1, :]
            coarse = value.astype(bf16).astype(f32)
            fine = value - coarse
            mine = row_iota == dst_row_ref[k : k + 1, :]
            spread.append(
                jnp.concatenate(
                    [jnp.where(mine, coarse, 0.0), jnp.where(mine, fine, 0.0)], axis=0
                ).astype(bf16)
            )
        land = land + lax.dot_general(
            jnp.concatenate(spread, axis=1),
            dst_hot_ref[:, b * points : b * points + pair],
            (((1,), (1,)), ((), ())),
            preferred_element_type=f32,
        )
    land = land[:cells] + land[cells:]
    land_ref[...] = land
    for sent_ref in sent_refs:
        lengthen(sent_ref, land.astype(bf16))


def heat_kernel(rows, e2_ref, e4_ref, land_ref, _, *refs):
    parts = refs[:-3]
    sum_ref, near_ref, far_ref = refs[-3:]
    cells = land_ref.shape[0]
    columns = cells // rows * LANES
    even_x = lax.axis_index("gx") % 2 == 0
    even_y = lax.axis_index("gy") % 2 == 0
    total = land_ref[...]
    for part in parts:
        total = total + part[0:cells, :].astype(f32)
    sum_ref[...] = total

    def corners(row):
        start = row * 4 // 16 * 16
        one = e2_ref[start : start + 16, :].astype(f32)
        two = e4_ref[start : start + 16, :].astype(f32)
        low = jnp.where(even_y, two, one)
        high = jnp.where(even_y, one, two)
        at = row * 4 - start
        lines = [low[at + 1 : at + 2], low[at + 3 : at + 4], high[at : at + 1], high[at + 2 : at + 3]]
        heat = from_tiles(total, rows)[row : row + 1]
        blank = jnp.zeros((3, columns), f32)
        return to_tiles(jnp.concatenate([heat] + lines + [blank], axis=0))

    first, last = corners(0), corners(rows - 1)
    near_ref[...] = jnp.where(even_x, last, first).astype(bf16)
    far_ref[...] = jnp.where(even_x, first, last).astype(bf16)


def advance(ref, r, t, coefs, size):
    ring, columns = ref.shape[2:]
    whole = ref[r, t]
    up = pltpu.roll(whole, 1, 0)[:size]
    down = pltpu.roll(whole, ring - 1, 0)[:size]
    mid = whole[:size]
    total = coefs[0] * mid + coefs[5] * (up + down)
    total = total + coefs[1] * ref[r - 1, t, 0:size, :]
    total = total + coefs[2] * ref[r + 1, t, 0:size, :]
    total = total + coefs[3] * pltpu.roll(mid, 1, 1)
    return total + coefs[4] * pltpu.roll(mid, columns - 1, 1)


def first_step_kernel(
    groups_x, groups_y, paired, x_ref, wet_ref, diff_ref, table_ref, e1_ref, e3_ref,
    e2_ref, e4_ref, *refs,
):
    if not paired:
        pin_ref, qin_ref = refs[:2]
    zb_ref, c_ref, t1_ref, y_ref, flat_ref, z_ref, t0_ref, w_ref = refs[-8:]
    _, rows, channels, columns = x_ref.shape
    row_group = lax.axis_index("gx")
    col_group = lax.axis_index("gy")
    is_atmos = lax.axis_index("comp") == 0

    @pl.when(is_atmos)
    def _():
        half = columns // 2
        for r in range(rows):
            fold(x_ref[0, r], flat_ref, r)
        for k in range(2):
            lanes = slice(k * half, (k + 1) * half)
            part = jnp.dot(
                flat_ref[:, lanes], table_ref[lanes, :], preferred_element_type=f32
            )
            y_ref[:, :, lanes] = part.reshape(rows, channels, half)
        diff = channel_column(diff_ref[...], channels, col_group * channels)
        total = rows * groups_x
        base = (row_group * rows).astype(f32)
        for group, n, parts in wave_parts(columns):
            lam, alpha, sinh = decay_terms(diff, half_rates(group, n, LANES, columns))
            scale = 1.0 / (
                2.0 * diff * sinh * (1.0 - jnp.exp(-2.0 * (total + 1) * alpha))
            )
            lows, highs = edge_factors(lam, alpha, base, total, rows)
            for part in parts:
                lanes = slice(part, part + LANES)
                if paired:
                    pin = jnp.zeros((channels, LANES), f32)
                    qin = jnp.zeros((channels, LANES), f32)
                    for mask, msg in ((1, e1_ref), (2, e2_ref), (3, e3_ref)):
                        band = row_group ^ mask
                        gap = (jnp.abs(row_group - band) - 1) * rows
                        term = jnp.exp(-gap.astype(f32) * alpha)
                        term = term * msg[0:channels, lanes].astype(f32)
                        pin = pin + jnp.where(band < row_group, term, 0.0)
                        qin = qin + jnp.where(band > row_group, term, 0.0)
                else:
                    pin = pin_ref[:, lanes]
                    qin = qin_ref[:, lanes]
                f = pin
                for r in range(rows):
                    f = lam * f + lows[r] * y_ref[r, :, lanes]
                    z_ref[r] = highs[r] * f
                g = lam * qin
                for r in reversed(range(rows)):
                    z = scale * (z_ref[r] + lows[r] * g)
                    zb_ref[r * channels : (r + 1) * channels, lanes] = z.astype(bf16)
                    g = lam * (g + highs[r] * y_ref[r, :, lanes])

    @pl.when(jnp.logical_not(is_atmos))
    def _():
        levels = channels // 2
        ring = levels + 8
        lines = 2 * channels
        first_x = row_group == 0
        last_x = row_group == groups_x - 1
        top = col_group == 0
        bottom = col_group == groups_y - 1
        even_x = row_group % 2 == 0
        even_y = col_group % 2 == 0

        one = e1_ref[lines : lines + 16, :].astype(f32)
        three = e3_ref[lines : lines + 16, :].astype(f32)
        below = jnp.where(even_x, three, one)[rows - 2 : rows]
        above = jnp.where(even_x, one, three)[0:2]
        w_ref[0:2, :] = jnp.where(first_x, 0.0, below)
        w_ref[2 : rows + 2, :] = wet_ref[...].astype(f32)
        w_ref[rows + 2 : rows + 4, :] = jnp.where(last_x, 0.0, above)

        span = rows + 2
        north = w_ref[0:span, :]
        here = w_ref[1 : span + 1, :]
        south = w_ref[2 : span + 2, :]
        west = pltpu.roll(here, 1, 1)
        east = pltpu.roll(here, columns - 1, 1)
        c_ref[0, 0:span, :] = here * (
            1.0 - 2.0 * mixing_rate - spread_rate * (north + south + west + east)
        )
        c_ref[1, 0:span, :] = spread_rate * here * north
        c_ref[2, 0:span, :] = spread_rate * here * south
        c_ref[3, 0:span, :] = spread_rate * here * west
        c_ref[4, 0:span, :] = spread_rate * here * east
        c_ref[5, 0:span, :] = mixing_rate * here
        c_ref[6, 0:span, :] = here

        one = e1_ref[0:lines, :].astype(f32)
        three = e3_ref[0:lines, :].astype(f32)
        below = jnp.where(even_x, three, one)
        above = jnp.where(even_x, one, three)
        blank = jnp.zeros((8, columns), f32)
        for k in range(2):
            for t in range(2):
                c = k * channels + t * levels
                t0_ref[k, t, 0:levels, :] = below[c : c + levels]
                t0_ref[rows + 2 + k, t, 0:levels, :] = above[c : c + levels]
                t0_ref[k, t, levels:ring, :] = blank
                t0_ref[rows + 2 + k, t, levels:ring, :] = blank
        one = e2_ref[...].astype(f32)
        two = e4_ref[0 : 4 * rows, :].astype(f32)
        before = jnp.where(even_y, two, one)
        after = jnp.where(even_y, one, two)
        for r in range(rows):
            for t in range(2):
                k = (r * 2 + t) * 2
                t0_ref[r + 2, t, 0:levels, :] = x_ref[0, r, t * levels : (t + 1) * levels, :]
                t0_ref[r + 2, t, levels : levels + 2, :] = after[k : k + 2]
                t0_ref[r + 2, t, ring - 2 : ring, :] = before[k : k + 2]

        def close(ref, r):
            for t in range(2):
                ref[r, t, ring - 1 : ring, :] = jnp.where(
                    top, ref[r, t, 0:1, :], ref[r, t, ring - 1 : ring, :]
                )
                ref[r, t, levels : levels + 1, :] = jnp.where(
                    bottom, ref[r, t, levels - 1 : levels, :], ref[r, t, levels : levels + 1, :]
                )

        def first(r, carry):
            coefs = [c_ref[k, pl.ds(r, 1), :] for k in range(6)]
            close(t0_ref, r + 1)
            for t in range(2):
                t1_ref[r, t] = advance(t0_ref, r + 1, t, coefs, ring)
            close(t1_ref, r)
            return carry

        lax.fori_loop(0, span, first, 0)


def second_step_kernel(gain_ref, table_ref, zb_ref, c_ref, t1_ref, sum_ref, base_ref):
    rows, channels, columns = base_ref.shape
    is_atmos = lax.axis_index("comp") == 0

    @pl.when(is_atmos)
    def _():
        response = channel_column(gain_ref[...], channels, lax.axis_index("gy") * channels)
        forcing = from_tiles(sum_ref[...], rows)
        half = columns // 2
        step = 256
        for n in range(0, half, step):
            even, odd = [
                jnp.dot(
                    zb_ref[:, k * half : (k + 1) * half],
                    table_ref[k * half : (k + 1) * half, n : n + step],
                    preferred_element_type=f32,
                ).reshape(rows, channels, step)
                for k in range(2)
            ]
            for r in range(rows):
                for lane, part in ((n, even[r] + odd[r]), (n + half, even[r] - odd[r])):
                    lanes = slice(lane, lane + step)
                    base_ref[r, :, lanes] = part + response * forcing[r : r + 1, lanes]

    @pl.when(jnp.logical_not(is_atmos))
    def _():
        levels = channels // 2

        def second(r, carry):
            coefs = [c_ref[k, pl.ds(r, 1), :] for k in range(6)]
            for t in range(2):
                c = t * levels
                base_ref[r - 1, c : c + levels, :] = advance(t1_ref, r, t, coefs, levels)
            return carry

        lax.fori_loop(1, rows + 1, second, 0)


def last_kernel(
    groups_x, groups_y, base_ref, c_ref, sum_ref, near_ref, far_ref, out_hbm,
    out_ref, e_ref, heat_ref, sem,
):
    rows, channels, columns = out_ref.shape
    row_group = lax.axis_index("gx")
    col_group = lax.axis_index("gy")
    is_atmos = lax.axis_index("comp") == 0
    copies = [
        pltpu.make_async_copy(out_ref.at[r], out_hbm.at[0, r], sem.at[r]) for r in range(rows)
    ]
    as_they_are = [
        pltpu.make_async_copy(base_ref.at[r], out_hbm.at[0, r], sem.at[r]) for r in range(rows)
    ]

    @pl.when(is_atmos)
    def _():
        for copy in as_they_are:
            copy.start()

    @pl.when(jnp.logical_and(jnp.logical_not(is_atmos), col_group > 0))
    def _():
        for copy in as_they_are[1:-1]:
            copy.start()

    @pl.when(jnp.logical_not(is_atmos))
    def _():
        levels = channels // 2
        even = row_group % 2 == 0
        below = jnp.where(even, far_ref[...].astype(f32), near_ref[...].astype(f32))
        above = jnp.where(even, near_ref[...].astype(f32), far_ref[...].astype(f32))

        low = from_tiles(below, 8)
        high = from_tiles(above, 8)
        by_low = c_ref[1, 1:2, :] * (c_ref[5, 0:1, :] + c_ref[5, 1:2, :])
        by_high = c_ref[2, rows : rows + 1, :] * (
            c_ref[5, rows : rows + 1, :] + c_ref[5, rows + 1 : rows + 2, :]
        )
        has_before = jnp.where(col_group > 0, 1.0, 0.0)
        has_after = jnp.where(col_group < groups_y - 1, 1.0, 0.0)

        @pl.when(col_group == 0)
        def _():
            span = rows + 2
            e_ref[0:1, :] = low[0:1]
            e_ref[1 : rows + 1, :] = from_tiles(sum_ref[...], rows)
            e_ref[rows + 1 : span, :] = high[0:1]
            e_ref[0:span, :] = c_ref[6, 0:span, :] * e_ref[0:span, :]
            own = slice(1, rows + 1)
            heat = e_ref[own, :]
            second = c_ref[5, own, :] * heat
            first = (c_ref[0, own, :] + 1.0) * heat + second
            first = first + c_ref[1, own, :] * e_ref[0:rows, :]
            first = first + c_ref[2, own, :] * e_ref[2 : rows + 2, :]
            first = first + c_ref[3, own, :] * pltpu.roll(heat, 1, 1)
            first = first + c_ref[4, own, :] * pltpu.roll(heat, columns - 1, 1)
            heat_ref[0] = first
            heat_ref[1] = second

        for r in (0, rows - 1):
            out_ref[r] = base_ref[r]
        for t in range(2):
            c = t * levels
            d = c + levels - 1
            for r, factor, lines in ((0, by_low, low), (rows - 1, by_high, high)):
                out_ref[r, c : c + 1, :] = out_ref[r, c : c + 1, :] + (
                    has_before * factor * lines[t + 1 : t + 2]
                )
                out_ref[r, d : d + 1, :] = out_ref[r, d : d + 1, :] + (
                    has_after * factor * lines[t + 3 : t + 4]
                )

        @pl.when(col_group == 0)
        def _():
            for r in range(rows):
                if r not in (0, rows - 1):
                    out_ref[r] = base_ref[r]
                for t, gain in enumerate((heat_gain, salt_gain)):
                    c = t * levels
                    for k in range(2):
                        out_ref[r, c + k : c + k + 1, :] = (
                            out_ref[r, c + k : c + k + 1, :] + gain * heat_ref[k, r : r + 1, :]
                        )
                copies[r].start()

        @pl.when(col_group > 0)
        def _():
            copies[0].start()
            copies[-1].start()

    for copy in copies:
        copy.wait()


def local(
    fields,
    wet_cells,
    flux_weight,
    variable_sea_response,
    diffusivity,
    a2o_source,
    a2o_target,
    a2o_count,
    a2o_weight,
    marine_air_input_index,
    marine_air_output_index,
    marine_air_piece_tally,
    marine_air_piece_factor,
):
    _, rows, channels, columns = fields.shape
    groups_x = lax.axis_size("gx")
    groups_y = lax.axis_size("gy")
    blocks, points = a2o_source.shape[2:]
    cells = rows * columns // LANES
    forward, inverse = fourier_tables(columns)
    flux_row = flux_weight[None, :]
    gain_row = variable_sea_response[None, :]
    diff_row = diffusivity[None, :]
    paired = groups_x == 4
    params = functools.partial(pltpu.CompilerParams, vmem_limit_bytes=40 * 2**20)
    vmem = pl.BlockSpec(memory_space=pltpu.VMEM)
    smem = pl.BlockSpec(memory_space=pltpu.SMEM)
    hbm = pl.BlockSpec(memory_space=pltpu.HBM)
    anywhere = pl.BlockSpec(memory_space=pl.ANY)

    def shape(dims, dtype):
        return jax.ShapeDtypeStruct(dims, dtype)

    lines = 2 * channels + 16
    shapes = [
        shape((cells, LANES), bf16),
        shape((cells + 16, LANES), bf16),
        shape((lines, columns), bf16),
        shape((lines, columns), bf16),
        shape((4 * rows, columns), bf16),
        shape((4 * rows, columns), bf16),
    ]
    if not paired:
        shapes.append(shape((2, channels, columns), bf16))
    coarse, wide, e1, e3, e2, e4, *sums = pl.pallas_call(
        functools.partial(start_kernel, groups_x, paired),
        out_shape=shapes,
        in_specs=[hbm] * 5,
        out_specs=[hbm] * len(shapes),
        scratch_shapes=[pltpu.VMEM(out.shape, out.dtype) for out in shapes]
        + [
            pltpu.VMEM((rows, channels, columns), f32),
            pltpu.VMEM((rows, columns), jnp.int32),
            pltpu.VMEM(flux_row.shape, f32),
            pltpu.VMEM(diff_row.shape, f32),
            pltpu.VMEM(forward.shape, bf16),
            pltpu.VMEM((rows * channels, columns), bf16),
            pltpu.VMEM((rows, columns), f32),
            pltpu.VMEM((4 * rows, columns), f32),
            pltpu.VMEM((columns // 2 // LANES, 2 * rows + 1, channels, LANES), f32),
            pltpu.SemaphoreType.DMA((rows,)),
            pltpu.SemaphoreType.DMA((4,)),
            pltpu.SemaphoreType.DMA((len(shapes),)),
        ],
        compiler_params=pltpu.CompilerParams(vmem_limit_bytes=58 * 2**20),
        name="surface_and_forward_or_halos",
    )(fields, wet_cells, flux_row, diff_row, forward)

    one_hots = pl.pallas_call(
        functools.partial(one_hot_kernel, rows, columns),
        out_shape=[
            shape((LANES, blocks * points), bf16),
            shape((LANES, blocks * points), bf16),
            shape((blocks, points), jnp.int32),
            shape((blocks, points), jnp.int32),
            shape((blocks, points), jnp.int32),
        ],
        in_specs=[vmem, vmem, smem] * 2,
        out_specs=[vmem] * 5,
        compiler_params=params(),
        name="one_hots",
    )(
        a2o_source, a2o_target, a2o_count,
        marine_air_input_index, marine_air_output_index, marine_air_piece_tally,
    )

    masks = [1 << bit for bit in range(groups_y.bit_length() - 1)]

    def sum_route(mask):
        return [(j, j ^ mask) for j in range(groups_y)]

    def partner_route(mask):
        return both_ways([(j, groups_y + (j ^ mask)) for j in range(groups_y)])

    surface = lax.ppermute(coarse, ("comp", "gy"), partner_route(0)).astype(f32)
    for mask in masks[:1]:
        far = lax.ppermute(wide, ("comp", "gy"), partner_route(mask))
        surface = surface + far[:cells].astype(f32)
    coarse = surface.astype(bf16)
    *one_hots, used = one_hots
    coarse, used = lax.optimization_barrier((coarse, used))
    for mask in masks[1:-1]:
        surface = surface + lax.ppermute(coarse, "gy", sum_route(mask)).astype(f32)
        coarse = surface.astype(bf16)
    surfaces = [surface] + [
        lax.ppermute(coarse, "gy", sum_route(mask)) for mask in masks[1:][-1:]
    ]

    def ring_pairs(count, odd):
        return [(a, (a + 1) % count) for a in range(odd, count, 2)]

    def flat(comp, i, j):
        return (comp * groups_x + i) * groups_y + j

    def level_route(odd):
        pairs = []
        for i in range(groups_x):
            linked = [(a, a + 1) for a in range(odd, groups_y - 1, 2)]
            alone = set(range(groups_y)) - {j for pair in linked for j in pair}
            pairs += [(flat(1, i, a), flat(1, i, b)) for a, b in linked]
            if i % 2 == 0:
                pairs += [(flat(1, i, j), flat(1, i + 1, j)) for j in sorted(alone)]
                if odd or not paired:
                    pairs += [(flat(0, i, j), flat(0, i + 1, j)) for j in range(groups_y)]
            if paired and not odd and i < i ^ 2:
                pairs += [(flat(0, i, j), flat(0, i ^ 2, j)) for j in range(groups_y)]
        return both_ways(pairs)

    e1 = lax.ppermute(e1, "gx", both_ways(ring_pairs(groups_x, 0)))
    e3 = lax.ppermute(e3, "gx", both_ways(ring_pairs(groups_x, 1)))
    axes = ("comp", "gx", "gy")
    e2 = lax.ppermute(e2, axes, level_route(0))
    e4 = lax.ppermute(e4, axes, level_route(1))

    landing, *sent = pl.pallas_call(
        functools.partial(regrid_kernel, len(surfaces)),
        out_shape=[shape((cells, LANES), f32)]
        + [shape((cells + 16 * (mask - 1), LANES), bf16) for mask in range(1, groups_y)],
        in_specs=[vmem] * (len(surfaces) + 7) + [anywhere] * 1,
        out_specs=[vmem] * groups_y,
        scratch_shapes=[
            pltpu.VMEM((blocks, points), f32),
            pltpu.VMEM((blocks, points), f32),
        ],
        compiler_params=params(),
        cost_estimate=pl.CostEstimate(flops=2_200_000_000, bytes_accessed=0, transcendentals=0),
        name="regrid_blocks",
    )(
        *surfaces, *one_hots, used, a2o_weight, marine_air_piece_factor, e3,
    )

    def landing_route(mask):
        pairs = [
            (flat(0, i, j), flat(0, i, j ^ mask))
            for i in range(groups_x)
            for j in range(groups_y)
            if j < j ^ mask
        ]
        pairs += [(flat(1, i, 0), flat(1, i, mask)) for i in range(groups_x)]
        pairs += [
            (flat(1, i, j), flat(1, i + 1, j))
            for i in range(0, groups_x, 2)
            for j in range(groups_y)
            if j not in (0, mask)
        ]
        return both_ways(pairs)

    parts = [
        lax.ppermute(block, axes, landing_route(mask)) for mask, block in enumerate(sent, 1)
    ]

    extra = []
    if not paired:
        p, q = jnp.moveaxis(lax.all_gather(sums[0], "gx").astype(f32), 1, 0)
        viscous = lax.dynamic_slice_in_dim(
            diffusivity, lax.axis_index("gy") * channels, channels
        )[:, None]
        rates = [half_rates(g, 0, columns // 4, columns) for g in (0, 0, 1, 1)]
        _, alpha, _ = decay_terms(viscous, jnp.concatenate(rates, axis=1))
        gap = lax.axis_index("gx") - jnp.arange(groups_x)
        decay = jnp.exp(
            -(rows * jnp.maximum(jnp.abs(gap) - 1, 0))[:, None, None] * alpha[None]
        )
        extra = [
            jnp.sum(jnp.where((gap > 0)[:, None, None], decay * p, 0.0), axis=0),
            jnp.sum(jnp.where((gap < 0)[:, None, None], decay * q, 0.0), axis=0),
        ]
    ring = channels // 2 + 8
    damped, coefs, stepped = pl.pallas_call(
        functools.partial(first_step_kernel, groups_x, groups_y, paired),
        out_shape=[
            shape((rows * channels, columns), bf16),
            shape((7, 16, columns), f32),
            shape((rows + 2, 2, ring, columns), f32),
        ],
        in_specs=[vmem] * (8 + len(extra)),
        out_specs=[vmem] * 3,
        scratch_shapes=[
            pltpu.VMEM((rows, channels, columns), f32),
            pltpu.VMEM((rows * channels, columns), bf16),
            pltpu.VMEM((rows, channels, LANES), f32),
            pltpu.VMEM((rows + 4, 2, ring, columns), f32),
            pltpu.VMEM((16, columns), f32),
        ],
        compiler_params=params(),
        name="damping_or_first_step",
    )(fields, wet_cells, diff_row, forward, e1, e3, e2, e4, *extra)

    surface_sum, near, far = pl.pallas_call(
        functools.partial(heat_kernel, rows),
        out_shape=[
            shape((cells, LANES), f32),
            shape((columns // 16, LANES), bf16),
            shape((columns // 16, LANES), bf16),
        ],
        in_specs=[vmem] * 3 + [anywhere] + [vmem] * len(parts),
        out_specs=[vmem] * 3,
        compiler_params=params(),
        name="surface_sum",
    )(e2, e4, landing, coefs, *parts)

    near = lax.ppermute(near, "gx", both_ways(ring_pairs(groups_x, 0)))
    far = lax.ppermute(far, "gx", both_ways(ring_pairs(groups_x, 1)))
    base = pl.pallas_call(
        second_step_kernel,
        out_shape=shape((rows, channels, columns), f32),
        in_specs=[vmem] * 6,
        out_specs=vmem,
        compiler_params=params(),
        name="inverse_or_second_step",
    )(gain_row, inverse, damped, coefs, stepped, surface_sum)
    return pl.pallas_call(
        functools.partial(last_kernel, groups_x, groups_y),
        out_shape=shape(fields.shape, f32),
        in_specs=[vmem] * 5,
        out_specs=hbm,
        scratch_shapes=[
            pltpu.VMEM((rows, channels, columns), f32),
            pltpu.VMEM((16, columns), f32),
            pltpu.VMEM((2, rows, columns), f32),
            pltpu.SemaphoreType.DMA((rows,)),
        ],
        compiler_params=params(),
        name="add_surface_terms",
    )(base, coefs, surface_sum, near, far)


def solution(mesh):
    in_specs = (
        P("comp", "gx", "gy", None),
        P("gx", None),
        P(),
        P(),
        P(),
        P("gx", "gy", None, None),
        P("gx", "gy", None, None),
        P("gx", "gy"),
        P("gx", "gy", None, None, None),
        P("gx", "gy", None, None),
        P("gx", "gy", None, None),
        P("gx", "gy"),
        P("gx", "gy", None, None, None),
    )
    out_specs = P("comp", "gx", "gy", None)
    return jax.shard_map(local, mesh=mesh, in_specs=in_specs, out_specs=out_specs, check_vma=False)
```
